32 devices in a mesh: wide: 2 (over core), narrow: 16 (over z, y, x).
Axes of the slice: x: 2, y: 2, z: 4, core: 2. Of those that a mesh axis runs over, the one named last changes fastest.
Arguments:
- tokens: bfloat16 [16384, 1024], P(('wide', 'narrow')), may hold values from -6 to 6
- cotangent: bfloat16 [16384, 1024], P(('wide', 'narrow')), may hold values from -6 to 6
- loss_mask: int32 [16384], P(('wide', 'narrow')), may hold values 0 or 1
- seq_lengths: int32 [32, 3], P(('wide', 'narrow')), may hold values from 1 to 384, 512 in all within a row
- norm_gain: float32 [1024], P('narrow'), may hold values from 0.5 to 1.5
- in_proj: float32 [1024, 4096], P('narrow'), may hold values from -0.1875 to 0.1875
- conv_weight: float32 [4, 2048], P(None, 'narrow'), may hold values from -3 to 3
- conv_bias: float32 [2048], P('narrow'), may hold values from -3 to 3
- select_proj: float32 [96, 2048], P(None, 'narrow'), may hold values from -0.125 to 0.125
- step_proj: float32 [64, 2048], P(None, 'narrow'), may hold values from -0.75 to 0.75
- step_bias: float32 [2048], P('narrow'), may hold values from -5 to -2
- decay_log: float32 [16, 2048], P(None, 'narrow'), may hold values from 0 to 2.8
- skip_scale: float32 [2048], P('narrow'), may hold values from 0.5 to 1.5
- out_proj: float32 [2048, 1024], P('narrow'), may hold values from -0.125 to 0.125
Outputs:
- output: bfloat16 [16384, 1024], P(('wide', 'narrow'))
- grad_tokens: bfloat16 [16384, 1024], P(('wide', 'narrow'))
- grad_norm_gain: float32 [1024], P('narrow')
- grad_in_proj: float32 [1024, 4096], P('narrow')
- grad_conv_weight: float32 [4, 2048], P(None, 'narrow')
- grad_conv_bias: float32 [2048], P('narrow')
- grad_select_proj: float32 [96, 2048], P(None, 'narrow')
- grad_step_proj: float32 [64, 2048], P(None, 'narrow')
- grad_step_bias: float32 [2048], P('narrow')
- grad_decay_log: float32 [16, 2048], P(None, 'narrow')
- grad_skip_scale: float32 [2048], P('narrow')
- grad_out_proj: float32 [2048, 1024], P('narrow')
- decay_sq: float32 [], replicated
- plain_sq: float32 [], replicated
The draws below stay inside these ranges and needn't reach their ends.
Inputs may be any that keep to these rules, and one draw needn't show every extreme that they name: `seq_lengths`: each row holds 3 lengths that sum to 512; the longest of each row is exactly 384.
All inputs are finite; a program needn't handle non-finite values. No bound on the sum of `loss_mask` on one device may be relied on, other than what follows from the above.
Results may differ from the reference program's by a relative error of at most 0.0055.
The reference program's roundings to bfloat16 on the way count: a program that leaves them out, or rounds other values in their place, can miss the bound.
Values may be sent and summed in bfloat16 or wider, within the bound.
A program may use at most 192 MiB of HBM per device.

```python
import math
import jax
import jax.numpy as jnp
import numpy as np
from jax import lax

MODEL = 1024
INNER = 2048
STATE = 16
RANK = 64
CONV = 4
TOK_DEV = 512
SEQ_DEV = 3
MAXLEN = 384
TOKENS = 16384
N_WIDE = 2
N_NARROW = 16


def with_ends(entries, rng, least, high):
    longest = entries.shape.index(max(entries.shape))
    spots = []
    for shift in (0, 1):
        where = [jax.random.randint(jax.random.fold_in(rng, axis), (), 0, length) for axis, length in enumerate(entries.shape)]
        where[longest] = (where[longest] + shift) % entries.shape[longest]
        spots.append(tuple(where))
    return entries.at[spots[0]].set(least).at[spots[1]].set(high)


def level_of(own_key, shape, cuts, smallest, largest):
    level, own = 1.0, jax.random.fold_in(own_key, 6)
    for position, blocks in cuts:
        steps = jnp.exp(jax.random.uniform(jax.random.fold_in(own, position), (blocks,), jnp.float32, smallest / len(cuts), largest / len(cuts)))
        level = level * jnp.repeat(steps, shape[position] // blocks).reshape([-1 if axis == position else 1 for axis in range(len(shape))])
    return level


def length_profile(amount, total, limit, skew):
    loads = [(1 << 20) // math.isqrt(rank ** skew) + 1 for rank in range(2, amount + 1)]
    spare, counts = total - limit - (amount - 1), [1] * (amount - 1)
    while spare > 0:
        free = [i for i in range(amount - 1) if counts[i] < limit]
        mass, budget = sum([loads[i] for i in free]), spare
        for i in free:
            more = min(limit - counts[i], max(1, budget * loads[i] // mass), spare)
            counts[i] = counts[i] + more
            spare = spare - more
    return np.array([limit] + counts)


def uneven_parts(own_key, number_of, total, reach, lean):
    if number_of == 2:
        one = jax.random.randint(own_key, (), max(1, total - reach), min(reach, total - 1) + 1)
        return jnp.stack([one, total - one])
    sizes = jnp.asarray(length_profile(number_of, total, reach, lean), jnp.int32)
    twos = (number_of - 1) // 2
    donor, taker = sizes[1:1 + 2 * twos:2], sizes[2:2 + 2 * twos:2]
    slack = jnp.minimum(donor - 1, reach - taker)
    moved = jax.random.randint(jax.random.fold_in(own_key, 1), (twos,), 0, 1 << 20) % (slack + 1)
    sizes = sizes.at[1:1 + 2 * twos:2].set(donor - moved).at[2:2 + 2 * twos:2].set(taker + moved)
    return sizes[jax.random.permutation(jax.random.fold_in(own_key, 2), number_of)]


def centred(rng, shape, spread, bound, split=(), kind=jnp.bfloat16):
    factor_of = level_of(rng, shape, split, -0.22, 0.18) if split else 1.0
    array = jax.random.normal(rng, shape, jnp.float32) * spread * factor_of
    return jnp.minimum(jnp.maximum(array, -bound), bound).astype(kind)


def setup_inputs(seed: int = 0) -> dict:
    splits = jax.random.split(jax.random.key(seed), 15)
    return {
        "tokens": centred(splits[0], (TOKENS, MODEL), 1.0, 6.0, ((0, 32),)),
        "cotangent": centred(splits[1], (TOKENS, MODEL), 1.0, 6.0, ((0, 32),)),
        "loss_mask": with_ends((jax.random.randint(splits[2], (TOKENS,), 0, 4) < 3).astype(jnp.int32), jax.random.fold_in(splits[2], 1), 0, 1),
        "seq_lengths": jax.vmap(lambda own: uneven_parts(own, SEQ_DEV, TOK_DEV, MAXLEN, 2))(jax.random.split(splits[3], (N_WIDE * N_NARROW))).reshape((N_WIDE * N_NARROW, SEQ_DEV)).astype(jnp.int32),
        "norm_gain": jnp.clip(1.0 + 0.1 * jax.random.normal(splits[4], (MODEL,), jnp.float32), 0.5, 1.5),
        "in_proj": centred(splits[5], (MODEL, 2 * INNER), MODEL ** -0.5, 0.1875, ((0, 16),), jnp.float32),
        "conv_weight": centred(splits[6], (CONV, INNER), CONV ** -0.5, 3.0, ((1, 16),), jnp.float32),
        "conv_bias": centred(splits[7], (INNER,), 0.5, 3.0, ((0, 16),), jnp.float32),
        "select_proj": centred(splits[8], (RANK + 2 * STATE, INNER), INNER ** -0.5, 0.125, ((1, 16),), jnp.float32),
        "step_proj": centred(splits[9], (RANK, INNER), RANK ** -0.5, 0.75, ((1, 16),), jnp.float32),
        "step_bias": jnp.clip(-5.0 + 3.0 * jax.random.uniform(splits[10], (INNER,), jnp.float32) ** level_of(splits[10], (INNER,), ((0, 16),), -0.2, 0.2), -5.0, -2.0),
        "decay_log": jnp.clip(2.8 * jax.random.uniform(splits[11], (STATE, INNER), jnp.float32) ** level_of(splits[11], (STATE, INNER), ((1, 16),), -0.2, 0.2), 0.0, 2.8),
        "skip_scale": jnp.clip(0.5 + 1.0 * jax.random.uniform(splits[12], (INNER,), jnp.float32) ** level_of(splits[12], (INNER,), ((0, 16),), -0.2, 0.2), 0.5, 1.5),
        "out_proj": centred(splits[13], (INNER, MODEL), INNER ** -0.5, 0.125, ((0, 16),), jnp.float32),
    }


epsilon = 1e-05
span_length = 16

@jax.custom_vjp
def low(v):
    return lax.optimization_barrier(v.astype(jnp.bfloat16)).astype(jnp.float32)

@jax.custom_vjp
def low_back(v):
    return v

def low_keep(v):
    return (low(v), None)

def low_pass(kept, grad):
    return (grad,)

def back_keep(v):
    return (v, None)

def back_low(kept, grad):
    return (low(grad),)
low.defvjp(low_keep, low_pass)
low_back.defvjp(back_keep, back_low)

def layout(lengths_row, total_rows):
    finish = jnp.cumsum(lengths_row, dtype=jnp.int32)
    starts = (finish - lengths_row).astype(jnp.int32)
    places = jnp.arange(total_rows, dtype=jnp.int32)
    before = starts[None, :] <= places[:, None]
    begin_at = lax.optimization_barrier(jnp.max(jnp.where(before, starts[None, :], 0), axis=1)).astype(jnp.int32)
    offset_in = (places - begin_at).astype(jnp.int32)
    return offset_in

def shifted(value_entries, lagged):
    return jnp.pad(value_entries[:value_entries.shape[0] - lagged], ((lagged, 0), (0, 0)))

def convolve(branch, taps, conv_shift, offset_in):
    tap_count = taps.shape[0]
    summed = conv_shift[None, :] + taps[tap_count - 1][None, :] * branch
    for tap_index in range(tap_count - 1):
        lagged = tap_count - 1 - tap_index
        allowed = (offset_in >= lagged).astype(branch.dtype)[:, None]
        summed = summed + taps[tap_index][None, :] * shifted(branch, lagged) * allowed
    return summed

def selective(step_size, write_rows, read_rows, signal, keeping, decay_rate):
    span_count = step_size.shape[0] // span_length

    def token_step(carried, pieces):
        step_row, write_row, read_row, signal_row, keep_row = pieces
        factor = jnp.exp(step_row[None, :] * decay_rate) * keep_row
        carried = factor * carried + write_row[:, None] * (step_row * signal_row)[None, :]
        return (carried, lax.optimization_barrier(jnp.sum(carried * read_row[:, None], axis=0)))

    @jax.checkpoint
    def span_step(carried, pieces):
        return lax.scan(token_step, carried, pieces)

    def blocked(value_entries):
        return value_entries.reshape((span_count, span_length) + value_entries.shape[1:])
    initial = jnp.zeros(decay_rate.shape, step_size.dtype)
    _, scan_results = lax.scan(span_step, initial, (blocked(step_size), blocked(write_rows), blocked(read_rows), blocked(signal), blocked(keeping)))
    return scan_results.reshape(step_size.shape)

def layer(residual, norm_gain, in_proj, conv_weight, conv_bias, select_proj, step_proj, step_bias, decay_log, skip_scale, out_proj, keeping, offset_in):
    highest = lax.Precision.HIGHEST
    norm_gain = low(norm_gain)
    in_proj = low(in_proj)
    conv_weight = low(conv_weight)
    conv_bias = low(conv_bias)
    select_proj = low(select_proj)
    step_proj = low(step_proj)
    step_bias = low(step_bias)
    decay_log = low(decay_log)
    skip_scale = low(skip_scale)
    out_proj = low(out_proj)
    inv_rms = lax.rsqrt(lax.optimization_barrier(jnp.mean(residual * residual, axis=1, keepdims=True)) + epsilon)
    normed = low(residual * inv_rms * norm_gain)
    mixed_rows = low_back(jnp.dot(normed, in_proj, precision=highest))
    inner_width = skip_scale.shape[0]
    branch = mixed_rows[:, :inner_width]
    gate_pre = mixed_rows[:, inner_width:]
    signal = low(jax.nn.silu(convolve(branch, conv_weight, conv_bias, offset_in)))
    projected = low_back(jnp.dot(signal, select_proj.T, precision=highest))
    rank_width = step_proj.shape[0]
    state_size = decay_log.shape[0]
    step_low = low(projected[:, :rank_width])
    write_rows = projected[:, rank_width:rank_width + state_size]
    read_rows = projected[:, rank_width + state_size:]
    step_size = jax.nn.softplus(low_back(jnp.dot(step_low, step_proj, precision=highest)) + step_bias)
    decay_rate = -jnp.exp(decay_log)
    core_out = selective(step_size, write_rows, read_rows, signal, keeping, decay_rate) + skip_scale * signal
    gated_rows = low(core_out * jax.nn.silu(gate_pre))
    return residual + jnp.dot(gated_rows, out_proj, precision=highest)

def reference(tokens, cotangent, loss_mask, seq_lengths, norm_gain, in_proj, conv_weight, conv_bias, select_proj, step_proj, step_bias, decay_log, skip_scale, out_proj):
    weights = (norm_gain, in_proj, conv_weight, conv_bias, select_proj, step_proj, step_bias, decay_log, skip_scale, out_proj)
    groups = N_WIDE * N_NARROW
    blocks = (tokens.reshape(groups, TOK_DEV, MODEL), cotangent.reshape(groups, TOK_DEV, MODEL), loss_mask.reshape(groups, TOK_DEV), seq_lengths)

    def one_block(running, pieces):
        block_tokens, block_cot, block_mask, block_lengths = pieces
        offset_in = layout(block_lengths, TOK_DEV)
        keeping = (offset_in > 0).astype(jnp.float32)

        def closed(residual, *params):
            return layer(residual, *params, keeping, offset_in)
        result, pullback = jax.vjp(closed, block_tokens.astype(jnp.float32), *weights)
        row_cotangent = block_cot.astype(jnp.float32) * block_mask.astype(jnp.float32)[:, None]
        grads = pullback(row_cotangent.astype(result.dtype))
        running = tuple((total_grad + grad_piece for total_grad, grad_piece in zip(running, grads[1:])))
        return (running, (result.astype(jnp.bfloat16), grads[0].astype(jnp.bfloat16)))
    initial = tuple((jnp.zeros_like(weight_now) for weight_now in weights))
    running, (scan_results, grad_rows) = lax.scan(one_block, initial, blocks)
    squares = [jnp.sum(grad_now * grad_now) for grad_now in running]
    decay_sq = squares[0] + squares[1] + squares[2] + squares[3] + squares[4] + squares[5] + squares[9]
    plain_sq = squares[6] + squares[7] + squares[8]
    return (scan_results.reshape(TOKENS, MODEL), grad_rows.reshape(TOKENS, MODEL), running[0], running[1], running[2], running[3], running[4], running[5], running[6], running[7], running[8], running[9], decay_sq, plain_sq)
```

```python
import functools
import math

import jax
import jax.numpy as jnp
from jax import lax
from jax.experimental import pallas as pl
from jax.experimental.pallas import tpu as pltpu
from jax.sharding import PartitionSpec as P

epsilon = 1e-05
chunk = 8
lanes = 128
log2e = math.log2(math.e)
ln2 = math.log(2.0)
far = 1e30


def layout(lengths_row, total_rows):
    finish = jnp.cumsum(lengths_row, dtype=jnp.int32)
    starts = finish - lengths_row
    places = jnp.arange(total_rows, dtype=jnp.int32)
    before = starts[None, :] <= places[:, None]
    begin_at = jnp.max(jnp.where(before, starts[None, :], 0), axis=1)
    return places - begin_at


def shifted(value_entries, lagged):
    return jnp.pad(value_entries[: value_entries.shape[0] - lagged], ((lagged, 0), (0, 0)))


def unshifted(value_entries, lagged):
    return jnp.pad(value_entries[lagged:], ((0, lagged), (0, 0)))


def convolve(branch, taps, conv_shift, offset_in):
    tap_count = taps.shape[0]
    summed = conv_shift[None, :] + taps[tap_count - 1][None, :] * branch
    for tap_index in range(tap_count - 1):
        lagged = tap_count - 1 - tap_index
        allowed = (offset_in >= lagged).astype(jnp.float32)[:, None]
        summed = summed + taps[tap_index][None, :] * shifted(branch, lagged) * allowed
    return summed


def convolve_back(grad_conv, branch, taps, offset_in):
    tap_count = taps.shape[0]
    grad_branch = grad_conv * taps[tap_count - 1][None, :]
    tap_grads = [None] * tap_count
    tap_grads[tap_count - 1] = jnp.sum(grad_conv * branch, axis=0)
    for tap_index in range(tap_count - 1):
        lagged = tap_count - 1 - tap_index
        allowed = (offset_in >= lagged).astype(jnp.float32)[:, None]
        masked = grad_conv * allowed
        grad_branch = grad_branch + taps[tap_index][None, :] * unshifted(masked, lagged)
        tap_grads[tap_index] = jnp.sum(masked * shifted(branch, lagged), axis=0)
    return (grad_branch, jnp.stack(tap_grads, axis=0), jnp.sum(grad_conv, axis=0))


def silu_grad(value_entries):
    sigma = jax.nn.sigmoid(value_entries)
    return sigma * (1.0 + value_entries * (1.0 - sigma))


def contract(left, right, left_dim, right_dim):
    return lax.dot_general(
        left, right, (((left_dim,), (right_dim,)), ((), ())), preferred_element_type=jnp.float32
    )


def scan_kernel(
    step_ref,
    signal_ref,
    grad_ref,
    offset_ref,
    write_ref,
    read_ref,
    rate_ref,
    core_ref,
    grad_step_ref,
    grad_signal_ref,
    grad_write_ref,
    grad_read_ref,
    grad_decay_ref,
    states,
    decay_step,
    inflow,
    first_buf,
    second_buf,
):
    chunks, _, width = step_ref.shape
    size = rate_ref.shape[0]
    half = size // 2
    tiles = width // lanes
    block = pl.program_id(0)

    def cut(tile):
        return pl.ds(tile * lanes, lanes)

    def prepare(index, carry):
        inside = offset_ref[index] > 0
        for tile in range(tiles):
            decay_step[index, :, cut(tile)] = jnp.where(inside, step_ref[index, :, cut(tile)], far)
        inflow[index] = step_ref[index] * signal_ref[index]
        return carry

    lax.fori_loop(0, chunks, prepare, 0)

    states[0] = jnp.zeros((size, width), jnp.float32)

    def folded(buffer, tile):
        total = buffer[tile, pl.ds(0, chunk, stride=chunk), :]
        for row in range(1, chunk):
            total = total + buffer[tile, pl.ds(row, chunk, stride=chunk), :]
        return total

    def forward(index, held):
        base = index * chunk
        held = list(held)
        for place in range(chunk):
            now = base + place
            write_now = write_ref[now]
            read_now = read_ref[now]
            for tile in range(tiles):
                rate = rate_ref[:, cut(tile)]
                decay = jnp.exp2(rate * decay_step[index, pl.ds(place, 1), cut(tile)])
                fresh = decay * held[tile] + write_now * inflow[index, pl.ds(place, 1), cut(tile)]
                held[tile] = fresh
                states[now + 1, :, cut(tile)] = fresh
                product = read_now * fresh
                first_buf[tile, pl.ds(place * chunk, chunk), :] = product[:half] + product[half:]
        for tile in range(tiles):
            core_ref[index, :, cut(tile)] = folded(first_buf, tile)
        return tuple(held)

    zero_tile = jnp.zeros((size, lanes), jnp.float32)
    lax.fori_loop(0, chunks, forward, (zero_tile,) * tiles)

    @pl.when(block == 0)
    def _():
        grad_write_ref[...] = jnp.zeros_like(grad_write_ref)
        grad_read_ref[...] = jnp.zeros_like(grad_read_ref)

    def backward(position, carried):
        index = chunks - 1 - position
        base = index * chunk
        incoming, decay_sums = list(carried[0]), list(carried[1])
        for place in range(chunk - 1, -1, -1):
            now = base + place
            write_now = write_ref[now]
            read_now = read_ref[now]
            read_sum = None
            write_sum = None
            for tile in range(tiles):
                rate = rate_ref[:, cut(tile)]
                step_now = decay_step[index, pl.ds(place, 1), cut(tile)]
                grad_now = grad_ref[index, pl.ds(place, 1), cut(tile)]
                grad_state = incoming[tile] + read_now * grad_now
                through_read = states[now + 1, :, cut(tile)] * grad_now
                through_write = grad_state * inflow[index, pl.ds(place, 1), cut(tile)]
                read_sum = through_read if read_sum is None else read_sum + through_read
                write_sum = through_write if write_sum is None else write_sum + through_write
                passed = grad_state * write_now
                first_buf[tile, pl.ds(place * chunk, chunk), :] = passed[:half] + passed[half:]
                leaving = jnp.exp2(rate * step_now) * grad_state
                incoming[tile] = leaving
                weighted = leaving * states[now, :, cut(tile)]
                scaled = weighted * rate
                second_buf[tile, pl.ds(place * chunk, chunk), :] = scaled[:half] + scaled[half:]
                decay_sums[tile] = decay_sums[tile] + weighted * step_now
            grad_read_ref[now] += read_sum
            grad_write_ref[now] += write_sum
        for tile in range(tiles):
            through = folded(first_buf, tile)
            grad_step_ref[index, :, cut(tile)] = through * signal_ref[
                index, :, cut(tile)
            ] + ln2 * folded(second_buf, tile)
            grad_signal_ref[index, :, cut(tile)] = through * step_ref[index, :, cut(tile)]
        return (tuple(incoming), tuple(decay_sums))

    _, decay_sums = lax.fori_loop(0, chunks, backward, ((zero_tile,) * tiles, (zero_tile,) * tiles))
    for tile in range(tiles):
        grad_decay_ref[:, cut(tile)] = decay_sums[tile] * rate_ref[:, cut(tile)] * ln2


def scan_both(step_size, signal_f, grad_core, offset_in, write_rows, read_rows, decay_rate):
    rows, inner = step_size.shape
    size = decay_rate.shape[0]
    width = 512
    blocks = inner // width
    chunks = rows // chunk
    tall = pl.BlockSpec((chunks, chunk, width), lambda b: (0, 0, b))
    thin = pl.BlockSpec((size, width), lambda b: (0, b))
    whole = pl.BlockSpec(memory_space=pltpu.VMEM)
    held = pl.BlockSpec((rows, size, lanes), lambda b: (0, 0, 0))
    wide_offsets = jnp.broadcast_to(offset_in[:, None], (rows, lanes)).reshape(chunks, chunk, lanes)
    wide_write = jnp.broadcast_to(write_rows[:, :, None], (rows, size, lanes))
    wide_read = jnp.broadcast_to(read_rows[:, :, None], (rows, size, lanes))
    full = jax.ShapeDtypeStruct((chunks, chunk, inner), jnp.float32)
    spread = jax.ShapeDtypeStruct((rows, size, lanes), jnp.float32)
    core, grad_step, grad_signal, grad_write, grad_read, grad_decay = pl.pallas_call(
        scan_kernel,
        grid=(blocks,),
        in_specs=[tall, tall, tall, whole, whole, whole, thin],
        out_specs=[tall, tall, tall, held, held, thin],
        out_shape=[full, full, full, spread, spread, jax.ShapeDtypeStruct((size, inner), jnp.float32)],
        scratch_shapes=[
            pltpu.VMEM((rows + 1, size, width), jnp.float32),
            pltpu.VMEM((chunks, chunk, width), jnp.float32),
            pltpu.VMEM((chunks, chunk, width), jnp.float32),
            pltpu.VMEM((width // lanes, chunk * chunk, lanes), jnp.float32),
            pltpu.VMEM((width // lanes, chunk * chunk, lanes), jnp.float32),
        ],
        compiler_params=pltpu.CompilerParams(
            dimension_semantics=("arbitrary",), vmem_limit_bytes=60 * 1024 * 1024
        ),
        cost_estimate=pl.CostEstimate(
            flops=60 * rows * inner * size,
            bytes_accessed=40 * rows * inner,
            transcendentals=2 * rows * inner * size,
        ),
        name="scan_both",
    )(
        step_size.reshape(full.shape),
        signal_f.reshape(full.shape),
        grad_core.reshape(full.shape),
        wide_offsets,
        wide_write,
        wide_read,
        decay_rate * log2e,
    )
    core, grad_step, grad_signal = (
        piece.reshape(rows, inner) for piece in (core, grad_step, grad_signal)
    )
    return (
        core,
        grad_step,
        grad_signal,
        jnp.sum(grad_write, axis=2),
        jnp.sum(grad_read, axis=2),
        grad_decay,
    )


def per_device(
    tokens,
    cotangent,
    loss_mask,
    seq_lengths,
    norm_gain,
    in_proj,
    conv_weight,
    conv_bias,
    select_proj,
    step_proj,
    step_bias,
    decay_log,
    skip_scale,
    out_proj,
):
    half = jnp.bfloat16
    in_whole = lax.all_gather(in_proj.astype(half), "narrow", axis=0, tiled=True)
    out_whole = lax.all_gather(out_proj.astype(half), "narrow", axis=0, tiled=True)
    piece = skip_scale.shape[0]
    gain_piece = norm_gain.shape[0]
    taps_n, select_n, step_n, state_size = (
        conv_weight.shape[0],
        select_proj.shape[0],
        step_proj.shape[0],
        decay_log.shape[0],
    )
    heights = (select_n, step_n, state_size, taps_n, 1, 1, 1, 1)
    packed = jnp.concatenate(
        [
            select_proj,
            step_proj,
            decay_log,
            conv_weight,
            conv_bias[None],
            step_bias[None],
            skip_scale[None],
            jnp.pad(norm_gain, (0, piece - gain_piece))[None],
        ],
        axis=0,
    ).astype(half)
    packed_whole = lax.all_gather(packed, "narrow", axis=1, tiled=True)
    cuts = [sum(heights[:index]) for index in range(len(heights) + 1)]
    parts = [packed_whole[cuts[i] : cuts[i + 1]] for i in range(len(heights))]
    select_whole, step_whole = parts[0], parts[1]
    decay_value, taps_value = parts[2].astype(jnp.float32), parts[3].astype(jnp.float32)
    shift_value, bias_value, skip_value = (parts[i][0].astype(jnp.float32) for i in (4, 5, 6))
    gain_value = parts[7].reshape(-1, piece)[:, :gain_piece].reshape(-1).astype(jnp.float32)

    total_rows = tokens.shape[0]
    inner_width = skip_value.shape[0]
    rank_width = step_whole.shape[0]
    offset_in = layout(seq_lengths[0], total_rows)
    residual = tokens.astype(jnp.float32)
    inv_rms = lax.rsqrt(jnp.mean(residual * residual, axis=1, keepdims=True) + epsilon)
    normed = (residual * inv_rms * gain_value).astype(half)
    mixed_rows = jnp.dot(normed, in_whole, preferred_element_type=jnp.float32)
    branch = mixed_rows[:, :inner_width]
    gate_pre = mixed_rows[:, inner_width:]
    conv_pre = convolve(branch, taps_value, shift_value, offset_in)
    signal = jax.nn.silu(conv_pre).astype(half)
    signal_f = signal.astype(jnp.float32)
    projected = contract(signal, select_whole, 1, 1)
    step_low = projected[:, :rank_width].astype(half)
    write_rows = projected[:, rank_width : rank_width + state_size]
    read_rows = projected[:, rank_width + state_size :]
    step_pre = jnp.dot(step_low, step_whole, preferred_element_type=jnp.float32) + bias_value
    step_size = jax.nn.softplus(step_pre)
    decay_rate = -jnp.exp(decay_value)
    grad_y = cotangent.astype(jnp.float32) * loss_mask.astype(jnp.float32)[:, None]
    grad_low = grad_y.astype(half)
    grad_gated = contract(grad_low, out_whole, 1, 1)
    gate_act = jax.nn.silu(gate_pre)
    grad_core = grad_gated * gate_act
    scanned, timestep_gradient, signal_gradient, writein_gradient, readout_gradient, grad_decaylog = (
        scan_both(step_size, signal_f, grad_core, offset_in, write_rows, read_rows, decay_rate)
    )
    core_out = scanned + skip_value * signal_f
    gated_rows = (core_out * gate_act).astype(half)
    output = (residual + jnp.dot(gated_rows, out_whole, preferred_element_type=jnp.float32)).astype(
        half
    )
    grad_outw = contract(gated_rows, grad_low, 0, 0)
    grad_gate = grad_gated * core_out * silu_grad(gate_pre)
    grad_skip = jnp.sum(grad_core * signal_f, axis=0)
    signal_gradient = signal_gradient + grad_core * skip_value
    grad_step_pre = timestep_gradient * jax.nn.sigmoid(step_pre)
    grad_bias = jnp.sum(grad_step_pre, axis=0)
    grad_step_low = grad_step_pre.astype(half)
    grad_stepw = contract(step_low, grad_step_low, 0, 0)
    grad_rank = contract(grad_step_low, step_whole, 1, 1)
    grad_projected = jnp.concatenate(
        [grad_rank, writein_gradient, readout_gradient], axis=1
    ).astype(half)
    grad_select = contract(grad_projected, signal, 0, 0)
    signal_gradient = signal_gradient + jnp.dot(
        grad_projected, select_whole, preferred_element_type=jnp.float32
    )
    grad_conv = signal_gradient * silu_grad(conv_pre)
    grad_branch, grad_taps, grad_shift = convolve_back(grad_conv, branch, taps_value, offset_in)
    grad_mixed = jnp.concatenate([grad_branch, grad_gate], axis=1).astype(half)
    grad_inw = contract(normed, grad_mixed, 0, 0)
    grad_normed = contract(grad_mixed, in_whole, 1, 1)
    grad_gain = jnp.sum(grad_normed * residual * inv_rms, axis=0)
    weighted = grad_normed * gain_value
    grad_resid = inv_rms * weighted - residual * (inv_rms * inv_rms * inv_rms) * jnp.mean(
        weighted * residual, axis=1, keepdims=True
    )
    grad_tokens = (grad_y + grad_resid).astype(half)

    gain_row = jnp.pad(
        grad_gain.reshape(-1, gain_piece), ((0, 0), (0, piece - gain_piece))
    ).reshape(1, -1)
    grads_packed = jnp.concatenate(
        [
            grad_select,
            grad_stepw,
            grad_decaylog,
            grad_taps,
            grad_shift[None],
            grad_bias[None],
            grad_skip[None],
            gain_row,
        ],
        axis=0,
    )
    out_sum = lax.psum_scatter(grad_outw, "narrow", scatter_dimension=0, tiled=True)
    packed_sum = lax.psum_scatter(grads_packed, "narrow", scatter_dimension=1, tiled=True)
    in_sum = lax.psum_scatter(grad_inw, "narrow", scatter_dimension=0, tiled=True)
    out_sum, packed_sum, in_sum = lax.psum((out_sum, packed_sum, in_sum), "wide")
    small = [packed_sum[cuts[i] : cuts[i + 1]] for i in range(len(heights))]
    gain_sum = small[7][0, :gain_piece]

    def square(values):
        return jnp.sum(values * values)

    decay_part = (
        square(gain_sum)
        + square(in_sum)
        + square(small[3])
        + square(small[4])
        + square(small[0])
        + square(small[1])
        + square(out_sum)
    )
    plain_part = square(small[5]) + square(small[2]) + square(small[6])
    norms = lax.psum(jnp.stack([decay_part, plain_part]), "narrow")
    return (
        output,
        grad_tokens,
        gain_sum,
        in_sum,
        small[3],
        small[4][0],
        small[0],
        small[1],
        small[5][0],
        small[2],
        small[6][0],
        out_sum,
        norms[0],
        norms[1],
    )


def solution(mesh):
    placed = (
        P(("wide", "narrow"), None),
        P(("wide", "narrow"), None),
        P(("wide", "narrow")),
        P(("wide", "narrow"), None),
        P("narrow"),
        P("narrow", None),
        P(None, "narrow"),
        P("narrow"),
        P(None, "narrow"),
        P(None, "narrow"),
        P("narrow"),
        P(None, "narrow"),
        P("narrow"),
        P("narrow", None),
    )
    return jax.shard_map(
        per_device,
        mesh=mesh,
        in_specs=placed,
        out_specs=(
            P(("wide", "narrow"), None),
            P(("wide", "narrow"), None),
            P("narrow"),
            P("narrow", None),
            P(None, "narrow"),
            P("narrow"),
            P(None, "narrow"),
            P(None, "narrow"),
            P("narrow"),
            P(None, "narrow"),
            P("narrow"),
            P("narrow", None),
            P(),
            P(),
        ),
        check_vma=False,
    )
```

```python
import functools
import math

import jax
import jax.numpy as jnp
from jax import lax
from jax.experimental import pallas as pl
from jax.experimental.pallas import tpu as pltpu
from jax.sharding import PartitionSpec as P

epsilon = 1e-05
chunk = 8
lanes = 128
log2e = math.log2(math.e)
ln2 = math.log(2.0)
far = 1e30


def layout(lengths_row, total_rows):
    finish = jnp.cumsum(lengths_row, dtype=jnp.int32)
    starts = finish - lengths_row
    places = jnp.arange(total_rows, dtype=jnp.int32)
    before = starts[None, :] <= places[:, None]
    begin_at = jnp.max(jnp.where(before, starts[None, :], 0), axis=1)
    return places - begin_at


def shifted(value_entries, lagged):
    return jnp.pad(value_entries[: value_entries.shape[0] - lagged], ((lagged, 0), (0, 0)))


def unshifted(value_entries, lagged):
    return jnp.pad(value_entries[lagged:], ((0, lagged), (0, 0)))


def convolve(branch, taps, conv_shift, offset_in):
    tap_count = taps.shape[0]
    summed = conv_shift[None, :] + taps[tap_count - 1][None, :] * branch
    for tap_index in range(tap_count - 1):
        lagged = tap_count - 1 - tap_index
        allowed = (offset_in >= lagged).astype(jnp.float32)[:, None]
        summed = summed + taps[tap_index][None, :] * shifted(branch, lagged) * allowed
    return summed


def convolve_back(grad_conv, branch, taps, offset_in):
    tap_count = taps.shape[0]
    grad_branch = grad_conv * taps[tap_count - 1][None, :]
    tap_grads = [None] * tap_count
    tap_grads[tap_count - 1] = jnp.sum(grad_conv * branch, axis=0)
    for tap_index in range(tap_count - 1):
        lagged = tap_count - 1 - tap_index
        allowed = (offset_in >= lagged).astype(jnp.float32)[:, None]
        masked = grad_conv * allowed
        grad_branch = grad_branch + taps[tap_index][None, :] * unshifted(masked, lagged)
        tap_grads[tap_index] = jnp.sum(masked * shifted(branch, lagged), axis=0)
    return (grad_branch, jnp.stack(tap_grads, axis=0), jnp.sum(grad_conv, axis=0))


def silu_grad(value_entries):
    sigma = jax.nn.sigmoid(value_entries)
    return sigma * (1.0 + value_entries * (1.0 - sigma))


def contract(left, right, left_dim, right_dim):
    return lax.dot_general(
        left, right, (((left_dim,), (right_dim,)), ((), ())), preferred_element_type=jnp.float32
    )


def scan_kernel(
    step_ref,
    signal_ref,
    grad_ref,
    offset_ref,
    write_ref,
    read_ref,
    rate_ref,
    core_ref,
    grad_step_ref,
    grad_signal_ref,
    grad_write_ref,
    grad_read_ref,
    grad_decay_ref,
    states,
    decay_step,
    inflow,
    first_buf,
    second_buf,
):
    chunks, _, width = step_ref.shape
    size = rate_ref.shape[0]
    half = size // 2
    tiles = width // lanes
    block = pl.program_id(0)

    def cut(tile):
        return pl.ds(tile * lanes, lanes)

    def prepare(index, carry):
        inside = offset_ref[index] > 0
        for tile in range(tiles):
            decay_step[index, :, cut(tile)] = jnp.where(inside, step_ref[index, :, cut(tile)], far)
        inflow[index] = step_ref[index] * signal_ref[index]
        return carry

    lax.fori_loop(0, chunks, prepare, 0)

    states[0] = jnp.zeros((size, width), jnp.float32)

    def folded(buffer, tile):
        total = buffer[tile, pl.ds(0, chunk, stride=chunk), :]
        for row in range(1, chunk):
            total = total + buffer[tile, pl.ds(row, chunk, stride=chunk), :]
        return total

    def forward(index, held):
        base = index * chunk
        held = list(held)
        for place in range(chunk):
            now = base + place
            write_now = write_ref[now]
            read_now = read_ref[now]
            for tile in range(tiles):
                rate = rate_ref[:, cut(tile)]
                decay = jnp.exp2(rate * decay_step[index, pl.ds(place, 1), cut(tile)])
                fresh = decay * held[tile] + write_now * inflow[index, pl.ds(place, 1), cut(tile)]
                held[tile] = fresh
                states[now + 1, :, cut(tile)] = fresh
                product = read_now * fresh
                first_buf[tile, pl.ds(place * chunk, chunk), :] = product[:half] + product[half:]
        for tile in range(tiles):
            core_ref[index, :, cut(tile)] = folded(first_buf, tile)
        return tuple(held)

    zero_tile = jnp.zeros((size, lanes), jnp.float32)
    lax.fori_loop(0, chunks, forward, (zero_tile,) * tiles)

    @pl.when(block == 0)
    def _():
        grad_write_ref[...] = jnp.zeros_like(grad_write_ref)
        grad_read_ref[...] = jnp.zeros_like(grad_read_ref)

    def backward(position, carried):
        index = chunks - 1 - position
        base = index * chunk
        incoming, decay_sums = list(carried[0]), list(carried[1])
        for place in range(chunk - 1, -1, -1):
            now = base + place
            write_now = write_ref[now]
            read_now = read_ref[now]
            read_sum = None
            write_sum = None
            for tile in range(tiles):
                rate = rate_ref[:, cut(tile)]
                step_now = decay_step[index, pl.ds(place, 1), cut(tile)]
                grad_now = grad_ref[index, pl.ds(place, 1), cut(tile)]
                grad_state = incoming[tile] + read_now * grad_now
                through_read = states[now + 1, :, cut(tile)] * grad_now
                through_write = grad_state * inflow[index, pl.ds(place, 1), cut(tile)]
                read_sum = through_read if read_sum is None else read_sum + through_read
                write_sum = through_write if write_sum is None else write_sum + through_write
                passed = grad_state * write_now
                first_buf[tile, pl.ds(place * chunk, chunk), :] = passed[:half] + passed[half:]
                leaving = jnp.exp2(rate * step_now) * grad_state
                incoming[tile] = leaving
                weighted = leaving * states[now, :, cut(tile)]
                scaled = weighted * rate
                second_buf[tile, pl.ds(place * chunk, chunk), :] = scaled[:half] + scaled[half:]
                decay_sums[tile] = decay_sums[tile] + weighted * step_now
            grad_read_ref[now] += read_sum
            grad_write_ref[now] += write_sum
        for tile in range(tiles):
            through = folded(first_buf, tile)
            grad_step_ref[index, :, cut(tile)] = through * signal_ref[
                index, :, cut(tile)
            ] + ln2 * folded(second_buf, tile)
            grad_signal_ref[index, :, cut(tile)] = through * step_ref[index, :, cut(tile)]
        return (tuple(incoming), tuple(decay_sums))

    _, decay_sums = lax.fori_loop(0, chunks, backward, ((zero_tile,) * tiles, (zero_tile,) * tiles))
    for tile in range(tiles):
        grad_decay_ref[:, cut(tile)] = decay_sums[tile] * rate_ref[:, cut(tile)] * ln2


def scan_both(step_size, signal_f, grad_core, offset_in, write_rows, read_rows, decay_rate):
    rows, inner = step_size.shape
    size = decay_rate.shape[0]
    width = 512
    blocks = inner // width
    chunks = rows // chunk
    tall = pl.BlockSpec((chunks, chunk, width), lambda b: (0, 0, b))
    thin = pl.BlockSpec((size, width), lambda b: (0, b))
    whole = pl.BlockSpec(memory_space=pltpu.VMEM)
    held = pl.BlockSpec((rows, size, lanes), lambda b: (0, 0, 0))
    wide_offsets = jnp.broadcast_to(offset_in[:, None], (rows, lanes)).reshape(chunks, chunk, lanes)
    wide_write = jnp.broadcast_to(write_rows[:, :, None], (rows, size, lanes))
    wide_read = jnp.broadcast_to(read_rows[:, :, None], (rows, size, lanes))
    full = jax.ShapeDtypeStruct((chunks, chunk, inner), jnp.float32)
    spread = jax.ShapeDtypeStruct((rows, size, lanes), jnp.float32)
    core, grad_step, grad_signal, grad_write, grad_read, grad_decay = pl.pallas_call(
        scan_kernel,
        grid=(blocks,),
        in_specs=[tall, tall, tall, whole, whole, whole, thin],
        out_specs=[tall, tall, tall, held, held, thin],
        out_shape=[full, full, full, spread, spread, jax.ShapeDtypeStruct((size, inner), jnp.float32)],
        scratch_shapes=[
            pltpu.VMEM((rows + 1, size, width), jnp.float32),
            pltpu.VMEM((chunks, chunk, width), jnp.float32),
            pltpu.VMEM((chunks, chunk, width), jnp.float32),
            pltpu.VMEM((width // lanes, chunk * chunk, lanes), jnp.float32),
            pltpu.VMEM((width // lanes, chunk * chunk, lanes), jnp.float32),
        ],
        compiler_params=pltpu.CompilerParams(
            dimension_semantics=("arbitrary",), vmem_limit_bytes=60 * 1024 * 1024
        ),
        cost_estimate=pl.CostEstimate(
            flops=60 * rows * inner * size,
            bytes_accessed=40 * rows * inner,
            transcendentals=2 * rows * inner * size,
        ),
        name="scan_both",
    )(
        step_size.reshape(full.shape),
        signal_f.reshape(full.shape),
        grad_core.reshape(full.shape),
        wide_offsets,
        wide_write,
        wide_read,
        decay_rate * log2e,
    )
    core, grad_step, grad_signal = (
        piece.reshape(rows, inner) for piece in (core, grad_step, grad_signal)
    )
    return (
        core,
        grad_step,
        grad_signal,
        jnp.sum(grad_write, axis=2),
        jnp.sum(grad_read, axis=2),
        grad_decay,
    )


def place_of(dims):
    depth, tall, wide = dims
    core = lax.axis_index("wide")
    me = lax.axis_index("narrow")
    across = lax.rem(me, wide)
    up = lax.rem(lax.div(me, wide), tall)
    deep = lax.div(me, wide * tall)
    turn = core if tall == wide else 0
    second = (1 + turn * (wide - 1), across + turn * (up - across), wide)
    third = (wide - turn * (wide - 1), up + turn * (across - up), tall)
    return core, deep, second, third


def block_at(dims, deep, second, third, d, e, f):
    depth, tall, wide = dims
    return (
        lax.rem(deep + d, depth) * (tall * wide)
        + lax.rem(second[1] + e, second[2]) * second[0]
        + lax.rem(third[1] + f, third[2]) * third[0]
    )


def greet(dims, deep, second, third, core):
    barrier = pltpu.get_barrier_semaphore()
    peers = 1
    pl.semaphore_signal(barrier, inc=1, device_id={"wide": 1 - core}, device_id_type=pl.DeviceIdType.MESH)
    for axis, size in enumerate((dims[0], second[2], third[2])):
        for hop in range(1, size):
            moves = [0, 0, 0]
            moves[axis] = hop
            target = block_at(dims, deep, second, third, *moves)
            pl.semaphore_signal(
                barrier, inc=1, device_id={"narrow": target}, device_id_type=pl.DeviceIdType.MESH
            )
            peers += 1
    pl.semaphore_wait(barrier, peers)


def half_of(width, core):
    return pl.ds(pl.multiple_of(core * (width // 2), lanes), width // 2)


def remote(source, target, send_sem, recv_sem, device):
    return pltpu.make_async_remote_copy(
        src_ref=source,
        dst_ref=target,
        send_sem=send_sem,
        recv_sem=recv_sem,
        device_id=device,
        device_id_type=pl.DeviceIdType.MESH,
    )


def gather_kernel(dims, count, *refs):
    own, whole = refs[:count], refs[count : 2 * count]
    local_sem, send_sem, recv_sem, core_send, core_recv = refs[2 * count :]
    core, deep, second, third = place_of(dims)
    greet(dims, deep, second, third, core)
    depth, span_e, span_f = dims[0], second[2], third[2]
    other = {"wide": 1 - core}
    pending = []

    def at(d, e, f):
        return block_at(dims, deep, second, third, d, e, f)

    def slot(d, e, f):
        return (d * span_e + e) * span_f + f

    def back(size, hop):
        return (size - hop) % size

    def piece(which, number, side):
        return whole[which].at[number, :, half_of(whole[which].shape[2], side)]

    def onward(which, d, e, f):
        number = at(back(depth, d), back(span_e, e), back(span_f, f))
        first = d == 0 and e == 0 and f == 0
        source = own[which].at[:, half_of(own[which].shape[1], core)] if first else piece(which, number, core)
        target = piece(which, number, core)

        def push(moved, index):
            copy = remote(
                source, target, send_sem.at[which, index], recv_sem.at[which, index], {"narrow": at(*moved)}
            )
            copy.start()
            pending.append(copy)

        if e == 0 and f == 0 and d == 0:
            for hop in range(1, depth):
                push((hop, 0, 0), slot(hop, 0, 0))
        if f == 0 and e == 0:
            for hop in range(1, span_e):
                push((0, hop, 0), slot(d, hop, 0))
        if f == 0:
            for hop in range(1, span_f):
                push((0, 0, hop), slot(d, e, hop))
        if not first:
            index = slot(d, e, f)
            copy = remote(source, target, core_send.at[which, index], core_recv.at[which, index], other)
            copy.start()
            pending.append(copy)

    def arrived(which, d, e, f):
        target = piece(which, at(back(depth, d), back(span_e, e), back(span_f, f)), core)
        index = slot(d, e, f)
        remote(
            target, target, send_sem.at[which, index], recv_sem.at[which, index], {"narrow": at(0, 0, 1)}
        ).wait_recv()

    locals_ = []
    for which in range(count):
        onward(which, 0, 0, 0)
    for which in range(count):
        copy = pltpu.make_async_copy(own[which], whole[which].at[at(0, 0, 0)], local_sem.at[which])
        copy.start()
        locals_.append(copy)
    for which in range(count):
        for d in range(1, depth):
            arrived(which, d, 0, 0)
            onward(which, d, 0, 0)
        for d in range(depth):
            for e in range(1, span_e):
                arrived(which, d, e, 0)
                onward(which, d, e, 0)
        for d in range(depth):
            for e in range(span_e):
                for f in range(1, span_f):
                    arrived(which, d, e, f)
                    onward(which, d, e, f)
    mirror = place_of_other(dims)
    for which in range(count):
        for d in range(depth):
            for e in range(span_e):
                for f in range(span_f):
                    if d == 0 and e == 0 and f == 0:
                        continue
                    number = block_at(
                        dims, deep, *mirror, back(depth, d), back(span_e, e), back(span_f, f)
                    )
                    target = piece(which, number, 1 - core)
                    index = slot(d, e, f)
                    remote(
                        target, target, core_send.at[which, index], core_recv.at[which, index], other
                    ).wait_recv()
    for copy in pending:
        copy.wait_send()
    for copy in locals_:
        copy.wait()


def place_of_other(dims):
    core, deep, second, third = place_of(dims)
    if dims[1] != dims[2]:
        return second, third
    return third, second


def gather_weights(dims, shards):
    number = dims[0] * dims[1] * dims[2]
    count = len(shards)
    anywhere = pl.BlockSpec(memory_space=pl.ANY)
    return pl.pallas_call(
        functools.partial(gather_kernel, dims, count),
        in_specs=[anywhere] * count,
        out_specs=[anywhere] * count,
        out_shape=[jax.ShapeDtypeStruct((number,) + shard.shape, shard.dtype) for shard in shards],
        scratch_shapes=[
            pltpu.SemaphoreType.DMA((count,)),
            pltpu.SemaphoreType.DMA((count, number)),
            pltpu.SemaphoreType.DMA((count, number)),
            pltpu.SemaphoreType.DMA((count, number)),
            pltpu.SemaphoreType.DMA((count, number)),
        ],
        compiler_params=pltpu.CompilerParams(collective_id=0, has_side_effects=True),
        name="gather_weights",
    )(*shards)


def reduce_kernel(dims, count, plain_at, *refs):
    grads, plain_ref = refs[:count], refs[count]
    sums, norms = refs[count + 1 : 2 * count + 1], refs[2 * count + 1]
    held = refs[2 * count + 2 :]
    mine, swapped, third_in, second_in, first_in = (
        held[index * count : (index + 1) * count] for index in range(5)
    )
    (norm_core, norm_deep, norm_wide, norm_tall) = held[5 * count : 5 * count + 4]
    (
        local_sem,
        core_send,
        core_recv,
        leg_send,
        leg_recv,
        last_send,
        last_recv,
        norm_send,
        norm_recv,
    ) = held[5 * count + 4 :]
    core, deep, second, third = place_of(dims)
    greet(dims, deep, second, third, core)
    depth, span_e, span_f = dims[0], second[2], third[2]
    other = {"wide": 1 - core}
    mirror = place_of_other(dims)
    pending = []

    def at(d, e, f):
        return block_at(dims, deep, second, third, d, e, f)

    def slot(d, e, f):
        return (d * span_e + e) * span_f + f

    far_first = sorted(
        ((d, e, f) for d in range(depth) for e in range(span_e) for f in range(span_f)),
        key=lambda item: (item[2] == 0, item[1] == 0, item[0] == 0),
    )
    loads = {}
    for move in far_first:
        for which in range(count):
            width = grads[which].shape[2]
            number = block_at(dims, deep, *mirror, *move)
            copy = remote(
                grads[which].at[number, :, half_of(width, 1 - core)],
                swapped[which].at[slot(*move)],
                core_send.at[which, slot(*move)],
                core_recv.at[which, slot(*move)],
                other,
            )
            copy.start()
            pending.append(copy)
            load = pltpu.make_async_copy(
                grads[which].at[at(*move), :, half_of(width, core)],
                mine[which].at[slot(*move)],
                local_sem.at[which, slot(*move)],
            )
            load.start()
            loads[which, move] = load

    def added(which, place, parts, store):
        rows = mine[which].shape[1]
        group = min(rows, 16)

        def some(index, carry):
            at_rows = pl.ds(pl.multiple_of(index * group, group), group)
            total = mine[which][place, at_rows, :].astype(jnp.float32)
            for ref, spot in parts:
                total = total + ref[spot, at_rows, :].astype(jnp.float32)
            return store(at_rows, total, carry)

        return functools.partial(lax.fori_loop, 0, rows // group, some)

    def wait_leg(which, index, ref, spot):
        remote(
            ref.at[spot], ref.at[spot], leg_send.at[which, index], leg_recv.at[which, index], other
        ).wait_recv()

    def collect(which, move):
        d, e, f = move
        place = slot(*move)
        loads[which, move].wait()
        remote(
            swapped[which].at[place],
            swapped[which].at[place],
            core_send.at[which, place],
            core_recv.at[which, place],
            other,
        ).wait_recv()
        parts = [(swapped[which], place)]
        if f == 0:
            for hop in range(1, span_f):
                spot = (d * span_e + e) * (span_f - 1) + hop - 1
                wait_leg(which, slot(d, e, hop), third_in[which], spot)
                parts.append((third_in[which], spot))
        if f == 0 and e == 0:
            for hop in range(1, span_e):
                spot = d * (span_e - 1) + hop - 1
                wait_leg(which, slot(d, hop, 0), second_in[which], spot)
                parts.append((second_in[which], spot))
        if f == 0 and e == 0 and d == 0:
            for hop in range(1, depth):
                wait_leg(which, slot(hop, 0, 0), first_in[which], hop - 1)
                parts.append((first_in[which], hop - 1))
        return place, parts

    for move in far_first[:-1]:
        d, e, f = move
        for which in range(count):
            place, parts = collect(which, move)

            def keep(at_rows, total, carry, which=which, place=place):
                mine[which][place, at_rows, :] = total.astype(mine[which].dtype)
                return carry

            added(which, place, parts, keep)(0)
            if f > 0:
                target, spot, moved = third_in[which], (d * span_e + e) * (span_f - 1) + f - 1, (0, 0, f)
            elif e > 0:
                target, spot, moved = second_in[which], d * (span_e - 1) + e - 1, (0, e, 0)
            else:
                target, spot, moved = first_in[which], d - 1, (d, 0, 0)
            copy = remote(
                mine[which].at[place],
                target.at[spot],
                leg_send.at[which, place],
                leg_recv.at[which, place],
                {"narrow": at(*moved)},
            )
            copy.start()
            pending.append(copy)

    squares = [jnp.zeros((8, lanes), jnp.float32), jnp.zeros((8, lanes), jnp.float32)]
    for which in range(count):
        place, parts = collect(which, (0, 0, 0))
        width = sums[which].shape[1]
        side = half_of(width, core)

        def finish(at_rows, total, carry, which=which, side=side):
            sums[which][at_rows, side] = total
            kept, plain = carry
            squared = total * total
            if which == plain_at:
                marked = squared * plain_ref[at_rows, side]
                plain = plain + folded_squares(marked)
                squared = squared - marked
            return (kept + folded_squares(squared), plain)

        squares = added(which, place, parts, finish)(tuple(squares))
        copy = remote(
            sums[which].at[:, side], sums[which].at[:, side], last_send.at[which], last_recv.at[which], other
        )
        copy.start()
        pending.append(copy)

    running = jnp.stack(list(squares))
    me = lax.axis_index("narrow")
    tall, wide = dims[1], dims[2]
    my_wide = lax.rem(me, wide)
    my_tall = lax.rem(lax.div(me, wide), tall)
    plane = tall * wide
    index = 0
    stages = (
        (norm_core, 2, core, lambda spot: {"wide": spot}),
        (norm_deep, depth, deep, lambda spot: {"narrow": spot * plane + lax.rem(me, plane)}),
        (norm_wide, wide, my_wide, lambda spot: {"narrow": me - my_wide + spot}),
        (norm_tall, tall, my_tall, lambda spot: {"narrow": me + (spot - my_tall) * wide}),
    )
    for buffer, size, mine_at, device in stages:
        buffer[mine_at] = running
        for hop in range(1, size):
            copy = remote(
                buffer.at[mine_at],
                buffer.at[mine_at],
                norm_send.at[index],
                norm_recv.at[index],
                device(lax.rem(mine_at + hop, size)),
            )
            copy.start()
            pending.append(copy)
            index += 1
        index -= size - 1
        for hop in range(1, size):
            came = lax.rem(mine_at + size - hop, size)
            remote(
                buffer.at[came], buffer.at[came], norm_send.at[index], norm_recv.at[index], device(came)
            ).wait_recv()
            index += 1
        running = buffer[0]
        for spot in range(1, size):
            running = running + buffer[spot]
    norms[...] = running
    for which in range(count):
        side = half_of(sums[which].shape[1], 1 - core)
        remote(
            sums[which].at[:, side], sums[which].at[:, side], last_send.at[which], last_recv.at[which], other
        ).wait_recv()
    for copy in pending:
        copy.wait_send()


def folded_squares(values):
    total = None
    for row in range(0, values.shape[0], 8):
        for column in range(0, values.shape[1], lanes):
            piece = values[row : row + 8, column : column + lanes]
            total = piece if total is None else total + piece
    return total


def reduce_grads(dims, grads, plain_mask, plain_at):
    number = dims[0] * dims[1] * dims[2]
    depth, tall, wide = dims
    count = len(grads)
    anywhere = pl.BlockSpec(memory_space=pl.ANY)
    inside = pl.BlockSpec(memory_space=pltpu.VMEM)

    def room(places):
        return [
            pltpu.VMEM((places, grad.shape[1], grad.shape[2] // 2), grad.dtype) for grad in grads
        ]

    third, second = (tall, wide)
    result = pl.pallas_call(
        functools.partial(reduce_kernel, dims, count, plain_at),
        in_specs=[anywhere] * count + [inside],
        out_specs=[inside] * (count + 1),
        out_shape=[jax.ShapeDtypeStruct(grad.shape[1:], jnp.float32) for grad in grads]
        + [jax.ShapeDtypeStruct((2, 8, lanes), jnp.float32)],
        scratch_shapes=room(number)
        + room(number)
        + room(depth * second * (third - 1))
        + room(depth * (second - 1))
        + room(depth - 1)
        + [pltpu.VMEM((size, 2, 8, lanes), jnp.float32) for size in (2, depth, wide, tall)]
        + [
            pltpu.SemaphoreType.DMA((count, number)),
            pltpu.SemaphoreType.DMA((count, number)),
            pltpu.SemaphoreType.DMA((count, number)),
            pltpu.SemaphoreType.DMA((count, number)),
            pltpu.SemaphoreType.DMA((count, number)),
            pltpu.SemaphoreType.DMA((count,)),
            pltpu.SemaphoreType.DMA((count,)),
            pltpu.SemaphoreType.DMA((depth + tall + wide,)),
            pltpu.SemaphoreType.DMA((depth + tall + wide,)),
        ],
        compiler_params=pltpu.CompilerParams(
            collective_id=1, has_side_effects=True, vmem_limit_bytes=56 * 1024 * 1024
        ),
        name="reduce_grads",
    )(*grads, plain_mask)
    return result[:count], jnp.sum(result[count], axis=(1, 2))


def grid_of(mesh):
    number = mesh.shape["narrow"]
    places = [getattr(device, "coords", None) for device in mesh.devices[0]]
    if all(place is not None for place in places):
        sizes = [len({place[axis] for place in places}) for axis in (2, 1, 0)]
        if sizes[0] * sizes[1] * sizes[2] == number:
            return tuple(sizes)
    side = round((number / 2) ** (1 / 3))
    return (2 * side, side, side) if 2 * side**3 == number else (number, 1, 1)


def folded_small(values):
    flat = values.reshape(-1)
    rows = -(-flat.shape[0] // (32 * lanes)) * 16
    flat = jnp.pad(flat, (0, 2 * rows * lanes - flat.shape[0])).reshape(2, rows, lanes)
    return jnp.concatenate([flat[0], flat[1]], axis=1)


def per_device(
    dims,
    tokens,
    cotangent,
    loss_mask,
    seq_lengths,
    norm_gain,
    in_proj,
    conv_weight,
    conv_bias,
    select_proj,
    step_proj,
    step_bias,
    decay_log,
    skip_scale,
    out_proj,
):
    half = jnp.bfloat16
    piece = skip_scale.shape[0]
    gain_piece = norm_gain.shape[0]
    taps_n, select_n, step_n, state_size = (
        conv_weight.shape[0],
        select_proj.shape[0],
        step_proj.shape[0],
        decay_log.shape[0],
    )
    heights = (select_n, step_n, state_size, taps_n, 1, 1, 1, 1)
    packed = jnp.concatenate(
        [
            select_proj,
            step_proj,
            decay_log,
            conv_weight,
            conv_bias[None],
            step_bias[None],
            skip_scale[None],
            jnp.pad(norm_gain, (0, piece - gain_piece))[None],
        ],
        axis=0,
    ).astype(half)
    in_blocks, out_blocks, packed_blocks = gather_weights(
        dims, [in_proj.astype(half), out_proj.astype(half), folded_small(packed)]
    )
    in_whole = in_blocks.reshape(-1, in_blocks.shape[2])
    out_whole = out_blocks.reshape(-1, out_blocks.shape[2])
    packed_whole = jnp.concatenate(
        [
            packed_blocks[:, :, :lanes].reshape(packed_blocks.shape[0], -1),
            packed_blocks[:, :, lanes:].reshape(packed_blocks.shape[0], -1),
        ],
        axis=1,
    )[:, : packed.size].reshape((-1,) + packed.shape)
    packed_whole = jnp.swapaxes(packed_whole, 0, 1).reshape(packed.shape[0], -1)
    cuts = [sum(heights[:index]) for index in range(len(heights) + 1)]
    parts = [packed_whole[cuts[i] : cuts[i + 1]] for i in range(len(heights))]
    select_whole, step_whole = parts[0], parts[1]
    decay_value, taps_value = parts[2].astype(jnp.float32), parts[3].astype(jnp.float32)
    shift_value, bias_value, skip_value = (parts[i][0].astype(jnp.float32) for i in (4, 5, 6))
    gain_value = parts[7].reshape(-1, piece)[:, :gain_piece].reshape(-1).astype(jnp.float32)

    total_rows = tokens.shape[0]
    inner_width = skip_value.shape[0]
    rank_width = step_whole.shape[0]
    offset_in = layout(seq_lengths[0], total_rows)
    residual = tokens.astype(jnp.float32)
    inv_rms = lax.rsqrt(jnp.mean(residual * residual, axis=1, keepdims=True) + epsilon)
    normed = (residual * inv_rms * gain_value).astype(half)
    mixed_rows = jnp.dot(normed, in_whole, preferred_element_type=jnp.float32)
    branch = mixed_rows[:, :inner_width]
    gate_pre = mixed_rows[:, inner_width:]
    conv_pre = convolve(branch, taps_value, shift_value, offset_in)
    signal = jax.nn.silu(conv_pre).astype(half)
    signal_f = signal.astype(jnp.float32)
    projected = contract(signal, select_whole, 1, 1)
    step_low = projected[:, :rank_width].astype(half)
    write_rows = projected[:, rank_width : rank_width + state_size]
    read_rows = projected[:, rank_width + state_size :]
    step_pre = jnp.dot(step_low, step_whole, preferred_element_type=jnp.float32) + bias_value
    step_size = jax.nn.softplus(step_pre)
    decay_rate = -jnp.exp(decay_value)
    grad_y = cotangent.astype(jnp.float32) * loss_mask.astype(jnp.float32)[:, None]
    grad_low = grad_y.astype(half)
    grad_gated = contract(grad_low, out_whole, 1, 1)
    gate_act = jax.nn.silu(gate_pre)
    grad_core = grad_gated * gate_act
    scanned, timestep_gradient, signal_gradient, writein_gradient, readout_gradient, grad_decaylog = (
        scan_both(step_size, signal_f, grad_core, offset_in, write_rows, read_rows, decay_rate)
    )
    core_out = scanned + skip_value * signal_f
    gated_rows = (core_out * gate_act).astype(half)
    output = (residual + jnp.dot(gated_rows, out_whole, preferred_element_type=jnp.float32)).astype(
        half
    )
    grad_outw = contract(gated_rows, grad_low, 0, 0)
    grad_gate = grad_gated * core_out * silu_grad(gate_pre)
    grad_skip = jnp.sum(grad_core * signal_f, axis=0)
    signal_gradient = signal_gradient + grad_core * skip_value
    grad_step_pre = timestep_gradient * jax.nn.sigmoid(step_pre)
    grad_bias = jnp.sum(grad_step_pre, axis=0)
    grad_step_low = grad_step_pre.astype(half)
    grad_stepw = contract(step_low, grad_step_low, 0, 0)
    grad_rank = contract(grad_step_low, step_whole, 1, 1)
    grad_projected = jnp.concatenate(
        [grad_rank, writein_gradient, readout_gradient], axis=1
    ).astype(half)
    grad_select = contract(grad_projected, signal, 0, 0)
    signal_gradient = signal_gradient + jnp.dot(
        grad_projected, select_whole, preferred_element_type=jnp.float32
    )
    grad_conv = signal_gradient * silu_grad(conv_pre)
    grad_branch, grad_taps, grad_shift = convolve_back(grad_conv, branch, taps_value, offset_in)
    grad_mixed = jnp.concatenate([grad_branch, grad_gate], axis=1).astype(half)
    grad_inw = contract(normed, grad_mixed, 0, 0)
    grad_normed = contract(grad_mixed, in_whole, 1, 1)
    grad_gain = jnp.sum(grad_normed * residual * inv_rms, axis=0)
    weighted = grad_normed * gain_value
    grad_resid = inv_rms * weighted - residual * (inv_rms * inv_rms * inv_rms) * jnp.mean(
        weighted * residual, axis=1, keepdims=True
    )
    grad_tokens = (grad_y + grad_resid).astype(half)

    gain_row = jnp.pad(
        grad_gain.reshape(-1, gain_piece), ((0, 0), (0, piece - gain_piece))
    ).reshape(1, -1)
    grads_packed = jnp.concatenate(
        [
            grad_select,
            grad_stepw,
            grad_decaylog,
            grad_taps,
            grad_shift[None],
            grad_bias[None],
            grad_skip[None],
            gain_row,
        ],
        axis=0,
    )
    blocks = in_blocks.shape[0]
    packed_grads = jax.vmap(folded_small)(
        jnp.swapaxes(grads_packed.reshape(packed.shape[0], blocks, piece), 0, 1)
    )
    rows_of = jnp.concatenate(
        [jnp.full((height, piece), index in (2, 5, 6), jnp.float32) for index, height in enumerate(heights)]
    )
    (in_sum, out_sum, packed_sum), norms = reduce_grads(
        dims,
        [
            grad_inw.astype(half).reshape(in_blocks.shape),
            grad_outw.astype(half).reshape(out_blocks.shape),
            packed_grads.astype(half),
        ],
        folded_small(rows_of),
        2,
    )
    packed_sum = jnp.concatenate(
        [packed_sum[:, :lanes].reshape(-1), packed_sum[:, lanes:].reshape(-1)]
    )[: packed.size].reshape(packed.shape)
    small = [packed_sum[cuts[i] : cuts[i + 1]] for i in range(len(heights))]
    gain_sum = small[7][0, :gain_piece]

    return (
        output,
        grad_tokens,
        gain_sum,
        in_sum,
        small[3],
        small[4][0],
        small[0],
        small[1],
        small[5][0],
        small[2],
        small[6][0],
        out_sum,
        norms[0],
        norms[1],
    )


def solution(mesh):
    placed = (
        P(("wide", "narrow"), None),
        P(("wide", "narrow"), None),
        P(("wide", "narrow")),
        P(("wide", "narrow"), None),
        P("narrow"),
        P("narrow", None),
        P(None, "narrow"),
        P("narrow"),
        P(None, "narrow"),
        P(None, "narrow"),
        P("narrow"),
        P(None, "narrow"),
        P("narrow"),
        P("narrow", None),
    )
    return jax.shard_map(
        functools.partial(per_device, grid_of(mesh)),
        mesh=mesh,
        in_specs=placed,
        out_specs=(
            P(("wide", "narrow"), None),
            P(("wide", "narrow"), None),
            P("narrow"),
            P("narrow", None),
            P(None, "narrow"),
            P("narrow"),
            P(None, "narrow"),
            P(None, "narrow"),
            P("narrow"),
            P(None, "narrow"),
            P("narrow"),
            P("narrow", None),
            P(),
            P(),
        ),
        check_vma=False,
    )
```

```python
import functools
import math

import jax
import jax.numpy as jnp
from jax import lax
from jax.experimental import pallas as pl
from jax.experimental.pallas import tpu as pltpu
from jax.sharding import PartitionSpec as P

epsilon = 1e-05
chunk = 8
lanes = 128
log2e = math.log2(math.e)
ln2 = math.log(2.0)
far = 1e30


def layout(lengths_row, total_rows):
    finish = jnp.cumsum(lengths_row, dtype=jnp.int32)
    starts = finish - lengths_row
    places = jnp.arange(total_rows, dtype=jnp.int32)
    before = starts[None, :] <= places[:, None]
    begin_at = jnp.max(jnp.where(before, starts[None, :], 0), axis=1)
    return places - begin_at


def contract(left, right, left_dim, right_dim):
    return lax.dot_general(
        left, right, (((left_dim,), (right_dim,)), ((), ())), preferred_element_type=jnp.float32
    )


def row_loop(rows, group, body, initial):
    def some(index, carry):
        return body(index, pl.ds(pl.multiple_of(index * group, group), group), carry)

    return lax.fori_loop(0, rows // group, some, initial)


def tiled(values, width):
    return jnp.concatenate([values] * (width // lanes), axis=1)


def sigmoid(values):
    return 1.0 / (1.0 + jnp.exp(-values))


def conv_rows(index, at, group, branch_ref, offset_ref, taps_ref, shift_ref):
    width = branch_ref.shape[1]
    taps = taps_ref.shape[0]
    current = branch_ref[at, :]
    before = branch_ref[pl.ds(pl.multiple_of(jnp.maximum(index * group - 8, 0), 8), 8), :]
    both = jnp.concatenate([before, current], axis=0)
    offsets = tiled(offset_ref[at, :], width)
    summed = shift_ref[...] + taps_ref[taps - 1 : taps, :] * current
    reads = [None] * taps
    reads[taps - 1] = current
    for tap in range(taps - 1):
        lag = taps - 1 - tap
        moved = pltpu.roll(both, lag, 0)[8:]
        reads[tap] = jnp.where(offsets >= lag, moved, 0.0)
        summed = summed + taps_ref[tap : tap + 1, :] * reads[tap]
    return summed, reads


def front_kernel(
    tokens_ref,
    gain_ref,
    offset_ref,
    taps_ref,
    shift_ref,
    select_ref,
    branch_w,
    gate_w,
    branch_ref,
    gate_ref,
    signal_ref,
    projected_ref,
    flipped_ref,
    normed_ref,
):
    rows = tokens_ref.shape[0]
    block = pl.program_id(0)

    @pl.when(block == 0)
    def _():
        def norm(index, at, carry):
            residual = tokens_ref[at, :].astype(jnp.float32)
            scale = lax.rsqrt(jnp.mean(residual * residual, axis=1, keepdims=True) + epsilon)
            normed_ref[at, :] = (residual * scale * gain_ref[...]).astype(normed_ref.dtype)
            return carry

        row_loop(rows, 32, norm, 0)
        flipped_ref[...] = normed_ref[...].T
        projected_ref[...] = jnp.zeros_like(projected_ref)

    branch_ref[...] = jnp.dot(normed_ref[...], branch_w[...], preferred_element_type=jnp.float32)
    gate_ref[...] = jnp.dot(normed_ref[...], gate_w[...], preferred_element_type=jnp.float32)

    def some(index, at, carry):
        summed, _ = conv_rows(index, at, 32, branch_ref, offset_ref, taps_ref, shift_ref)
        signal_ref[at, :] = (summed * sigmoid(summed)).astype(signal_ref.dtype)
        return carry

    row_loop(rows, 32, some, 0)
    projected_ref[...] += contract(signal_ref[...], select_ref[...], 1, 1)


def prepare_steps(projected_ref, step_w, bias_ref, offset_ref, signal_ref, pre_buf, decay_step, inflow, extra):
    rows = projected_ref.shape[0]
    rank = step_w.shape[0]
    width = step_w.shape[1]
    pre_buf[...] = (
        jnp.dot(
            projected_ref[:, :rank].astype(step_w.dtype), step_w[...], preferred_element_type=jnp.float32
        )
        + bias_ref[...]
    )

    def some(index, at, carry):
        pre = pre_buf[at, :]
        step = jnp.maximum(pre, 0.0) + jnp.log1p(jnp.exp(-jnp.abs(pre)))
        spot = pl.ds(pl.multiple_of(index * 4, 4), 4)
        inside = tiled(offset_ref[at, :], width) > 0
        decay_step[spot] = jnp.where(inside, step, far).reshape(4, chunk, width)
        flow = step * signal_ref[at, :].astype(jnp.float32)
        inflow[spot] = flow.reshape(4, chunk, width)
        extra(index, at, spot, step, flow)
        return carry

    row_loop(rows, 4 * chunk, some, 0)


def folded(buffer, tile):
    total = buffer[tile, pl.ds(0, chunk, stride=chunk), :]
    for row in range(1, chunk):
        total = total + buffer[tile, pl.ds(row, chunk, stride=chunk), :]
    return total


def cut(tile):
    return pl.ds(tile * lanes, lanes)


def forward_kernel(
    projected_ref,
    step_w,
    bias_ref,
    offset_ref,
    signal_ref,
    write_ref,
    read_ref,
    rate_ref,
    skip_ref,
    gate_ref,
    low_ref,
    out_w,
    flipped_ref,
    tokens_ref,
    states_ref,
    core_grad_ref,
    gate_grad_ref,
    skip_grad_ref,
    out_grad_ref,
    in_grad_ref,
    output_ref,
    pre_buf,
    decay_step,
    inflow,
    core_buf,
    fold_buf,
    gated_buf,
    total,
):
    rows = projected_ref.shape[0]
    width = step_w.shape[1]
    size = rate_ref.shape[0]
    half = size // 2
    tiles = width // lanes
    block = pl.program_id(0)
    prepare_steps(
        projected_ref,
        step_w,
        bias_ref,
        offset_ref,
        signal_ref,
        pre_buf,
        decay_step,
        inflow,
        lambda *_: None,
    )

    def forward(index, held):
        held = list(held)
        for place in range(chunk):
            now = index * chunk + place
            write_now = write_ref[now]
            read_now = read_ref[now]
            for tile in range(tiles):
                decay = jnp.exp2(rate_ref[:, cut(tile)] * decay_step[index, pl.ds(place, 1), cut(tile)])
                fresh = decay * held[tile] + write_now * inflow[index, pl.ds(place, 1), cut(tile)]
                held[tile] = fresh
                states_ref[now, :, cut(tile)] = fresh.astype(states_ref.dtype)
                product = read_now * fresh
                fold_buf[tile, pl.ds(place * chunk, chunk), :] = product[:half] + product[half:]
        for tile in range(tiles):
            core_buf[index, :, cut(tile)] = folded(fold_buf, tile)
        return tuple(held)

    zero_tile = jnp.zeros((size, lanes), jnp.float32)
    lax.fori_loop(0, rows // chunk, forward, (zero_tile,) * tiles)

    pre_buf[...] = contract(low_ref[...], out_w[...], 1, 1)

    def after(index, at, carry):
        spot = pl.ds(pl.multiple_of(index * 4, 4), 4)
        signal = signal_ref[at, :].astype(jnp.float32)
        core = core_buf[spot].reshape(4 * chunk, width) + skip_ref[...] * signal
        gate = gate_ref[at, :]
        sigma = sigmoid(gate)
        active = gate * sigma
        gated_buf[at, :] = (core * active).astype(gated_buf.dtype)
        grad_gated = pre_buf[at, :]
        grad_core = grad_gated * active
        core_grad_ref[spot] = grad_core.reshape(4, chunk, width)
        slope = sigma * (1.0 + gate * (1.0 - sigma))
        gate_grad_ref[at, :] = (grad_gated * core * slope).astype(gate_grad_ref.dtype)
        return carry + grad_core * signal

    skips = row_loop(rows, 4 * chunk, after, jnp.zeros((4 * chunk, width), jnp.float32))
    skip_grad_ref[...] = jnp.sum(skips, axis=0, keepdims=True)
    out_grad_ref[...] = contract(gated_buf[...], low_ref[...], 0, 0).astype(out_grad_ref.dtype)
    in_grad_ref[...] = jnp.dot(
        flipped_ref[...], gate_grad_ref[...], preferred_element_type=jnp.float32
    ).astype(in_grad_ref.dtype)
    piece = jnp.dot(gated_buf[...], out_w[...], preferred_element_type=jnp.float32)

    @pl.when(block == 0)
    def _():
        total[...] = piece

    @pl.when(block > 0)
    def _():
        total[...] += piece

    @pl.when(block == pl.num_programs(0) - 1)
    def _():
        output_ref[...] = (tokens_ref[...].astype(jnp.float32) + total[...]).astype(output_ref.dtype)


def backward_kernel(
    projected_ref,
    step_w,
    bias_ref,
    offset_ref,
    signal_ref,
    write_ref,
    read_ref,
    rate_ref,
    skip_ref,
    core_grad_ref,
    states_ref,
    signal_grad_ref,
    step_w_grad_ref,
    bias_grad_ref,
    decay_grad_ref,
    rank_ref,
    write_grad_ref,
    read_grad_ref,
    pre_buf,
    decay_step,
    inflow,
    flow_pair,
    grad_pair,
    first_buf,
    second_buf,
    grad_rows,
    through_buf,
    scaled_buf,
    low_buf,
):
    rows = projected_ref.shape[0]
    rank = step_w.shape[0]
    width = step_w.shape[1]
    size = rate_ref.shape[0]
    half = size // 2
    tiles = width // lanes
    chunks = rows // chunk
    block = pl.program_id(0)

    def paired(values):
        high = values.astype(jnp.bfloat16).astype(jnp.float32)
        return jnp.concatenate([high, values - high], axis=0).astype(jnp.bfloat16)

    def extra(index, at, spot, step, flow):
        for part in range(4):
            here = index * 4 + part
            flow_pair[here] = paired(flow[part * chunk : (part + 1) * chunk])
            grad_pair[here] = paired(core_grad_ref[here])

    prepare_steps(
        projected_ref, step_w, bias_ref, offset_ref, signal_ref, pre_buf, decay_step, inflow, extra
    )
    flow_pair[chunks] = jnp.zeros_like(flow_pair[chunks])
    grad_rows[...] = jnp.zeros_like(grad_rows)
    first_buf[...] = jnp.zeros_like(first_buf)
    second_buf[...] = jnp.zeros_like(second_buf)

    @pl.when(block == 0)
    def _():
        write_grad_ref[...] = jnp.zeros_like(write_grad_ref)
        read_grad_ref[...] = jnp.zeros_like(read_grad_ref)
        rank_ref[...] = jnp.zeros_like(rank_ref)

    token_of = lax.rem(lax.broadcasted_iota(jnp.int32, (size, 2 * chunk), 1), chunk)

    def own_token(products):
        kept = None
        for place in range(chunk):
            piece = products[place * size : (place + 1) * size]
            kept = piece if kept is None else jnp.where(token_of == place, piece, kept)
        return kept

    def settle(index, slot):
        for tile in range(tiles):
            through_buf[index, :, cut(tile)] = folded(first_buf.at[slot], tile)
            scaled_buf[index, :, cut(tile)] = folded(second_buf.at[slot], tile)
        write_grad_ref[index] += own_token(contract(grad_rows[slot], flow_pair[index], 1, 1))

    def backward(position, carried):
        index = chunks - 1 - position
        slot = lax.rem(position, 2)
        settle(index + 1, 1 - slot)
        base = index * chunk
        here = states_ref[pl.ds(base, chunk)].reshape(chunk * size, width)
        read_grad_ref[index] += own_token(contract(here, grad_pair[index], 1, 1))
        incoming, decay_sums = list(carried[0]), list(carried[1])
        for place in range(chunk - 1, -1, -1):
            now = base + place
            earlier = jnp.maximum(now - 1, 0) if place == 0 else now - 1
            write_now = write_ref[now]
            read_now = read_ref[now]
            for tile in range(tiles):
                rate = rate_ref[:, cut(tile)]
                step_now = decay_step[index, pl.ds(place, 1), cut(tile)]
                grad_state = incoming[tile] + read_now * core_grad_ref[index, pl.ds(place, 1), cut(tile)]
                grad_rows[slot, pl.ds(place * size, size), cut(tile)] = grad_state.astype(grad_rows.dtype)
                passed = grad_state * write_now
                first_buf[slot, tile, pl.ds(place * chunk, chunk), :] = passed[:half] + passed[half:]
                leaving = jnp.exp2(rate * step_now) * grad_state
                incoming[tile] = leaving
                weighted = leaving * states_ref[earlier, :, cut(tile)].astype(jnp.float32)
                scaled = weighted * rate
                second_buf[slot, tile, pl.ds(place * chunk, chunk), :] = scaled[:half] + scaled[half:]
                decay_sums[tile] = decay_sums[tile] + weighted * step_now
        return (tuple(incoming), tuple(decay_sums))

    zero_tile = jnp.zeros((size, lanes), jnp.float32)
    _, decay_sums = lax.fori_loop(0, chunks, backward, ((zero_tile,) * tiles, (zero_tile,) * tiles))
    settle(0, (chunks - 1) % 2)
    for tile in range(tiles):
        decay_grad_ref[:, cut(tile)] = decay_sums[tile] * rate_ref[:, cut(tile)] * ln2

    def after(index, at, carry):
        spot = pl.ds(pl.multiple_of(index * 4, 4), 4)
        pre = pre_buf[at, :]
        signal = signal_ref[at, :].astype(jnp.float32)
        through = through_buf[spot].reshape(4 * chunk, width)
        grad_step = through * signal + ln2 * scaled_buf[spot].reshape(4 * chunk, width)
        grad_pre = grad_step * sigmoid(pre)
        low_buf[at, :] = grad_pre.astype(low_buf.dtype)
        step = jnp.maximum(pre, 0.0) + jnp.log1p(jnp.exp(-jnp.abs(pre)))
        signal_grad_ref[at, :] = through * step + skip_ref[...] * core_grad_ref[spot].reshape(
            4 * chunk, width
        )
        return carry + grad_pre

    sums = row_loop(rows, 4 * chunk, after, jnp.zeros((4 * chunk, width), jnp.float32))
    bias_grad_ref[...] = jnp.sum(sums, axis=0, keepdims=True)
    step_w_grad_ref[...] = contract(
        projected_ref[:, :rank].astype(low_buf.dtype), low_buf[...], 0, 0
    )
    rank_ref[...] += contract(low_buf[...], step_w[...], 1, 1)


def back_kernel(
    tokens_ref,
    cotangent_ref,
    mask_ref,
    gain_ref,
    offset_ref,
    taps_ref,
    shift_ref,
    select_ref,
    flat_ref,
    branch_ref,
    signal_ref,
    signal_grad_ref,
    gate_grad_ref,
    flipped_ref,
    branch_w,
    gate_w,
    select_grad_ref,
    taps_grad_ref,
    shift_grad_ref,
    in_grad_ref,
    gain_grad_ref,
    tokens_grad_ref,
    conv_buf,
    mixed_buf,
    total,
):
    rows = tokens_ref.shape[0]
    width = branch_ref.shape[1]
    taps = taps_ref.shape[0]
    block = pl.program_id(0)
    select_grad_ref[...] = contract(flat_ref[...], signal_ref[...], 0, 0)
    conv_buf[pl.ds(0, rows), :] = signal_grad_ref[...] + jnp.dot(
        flat_ref[...], select_ref[...], preferred_element_type=jnp.float32
    )
    conv_buf[pl.ds(rows, 8), :] = jnp.zeros((8, width), jnp.float32)

    def through_conv(index, at, carry):
        summed, reads = conv_rows(index, at, 32, branch_ref, offset_ref, taps_ref, shift_ref)
        sigma = sigmoid(summed)
        grad_conv = conv_buf[at, :] * (sigma * (1.0 + summed * (1.0 - sigma)))
        conv_buf[at, :] = grad_conv
        adds = [grad_conv] + [grad_conv * read for read in reads]
        return tuple(
            kept + (add[:8] + add[8:16] + add[16:24] + add[24:]) for kept, add in zip(carry, adds)
        )

    zeros = jnp.zeros((8, width), jnp.float32)
    sums = row_loop(rows, 32, through_conv, (zeros,) * (taps + 1))
    shift_grad_ref[...] = jnp.sum(sums[0], axis=0, keepdims=True)
    for tap in range(taps):
        taps_grad_ref[tap : tap + 1, :] = jnp.sum(sums[tap + 1], axis=0, keepdims=True)

    def to_branch(index, at, carry):
        longer = pl.ds(pl.multiple_of(index * 32, 32), 40)
        grads = conv_buf[longer, :]
        offsets = tiled(offset_ref[longer, :], width)
        summed = taps_ref[taps - 1 : taps, :] * grads[:32]
        for tap in range(taps - 1):
            lag = taps - 1 - tap
            kept = jnp.where(offsets >= lag, grads, 0.0)
            summed = summed + taps_ref[tap : tap + 1, :] * pltpu.roll(kept, 40 - lag, 0)[:32]
        mixed_buf[at, :] = summed.astype(mixed_buf.dtype)
        return carry

    row_loop(rows, 32, to_branch, 0)
    in_grad_ref[...] = jnp.dot(
        flipped_ref[...], mixed_buf[...], preferred_element_type=jnp.float32
    ).astype(in_grad_ref.dtype)
    piece = contract(mixed_buf[...], branch_w[...], 1, 1) + contract(gate_grad_ref[...], gate_w[...], 1, 1)

    @pl.when(block == 0)
    def _():
        total[...] = piece

    @pl.when(block > 0)
    def _():
        total[...] += piece

    @pl.when(block == pl.num_programs(0) - 1)
    def _():
        def finish(index, at, carry):
            residual = tokens_ref[at, :].astype(jnp.float32)
            scale = lax.rsqrt(jnp.mean(residual * residual, axis=1, keepdims=True) + epsilon)
            grad_normed = total[at, :]
            weighted = grad_normed * gain_ref[...]
            inner = jnp.mean(weighted * residual, axis=1, keepdims=True)
            grad_y = cotangent_ref[at, :].astype(jnp.float32) * tiled(mask_ref[at, :], residual.shape[1])
            result = grad_y + (scale * weighted - residual * (scale * scale * scale) * inner)
            tokens_grad_ref[at, :] = result.astype(tokens_grad_ref.dtype)
            add = grad_normed * residual * scale
            return carry + (add[:8] + add[8:16] + add[16:24] + add[24:])

        gains = row_loop(rows, 32, finish, jnp.zeros((8, total.shape[1]), jnp.float32))
        gain_grad_ref[...] = jnp.sum(gains, axis=0, keepdims=True)


def shape(dims, kind=jnp.float32):
    return jax.ShapeDtypeStruct(dims, kind)


def compute_call(kernel, name, blocks, in_specs, out_specs, out_shape, scratch, flops, operands):
    return pl.pallas_call(
        kernel,
        grid=(blocks,),
        in_specs=in_specs,
        out_specs=out_specs,
        out_shape=out_shape,
        scratch_shapes=scratch,
        compiler_params=pltpu.CompilerParams(
            dimension_semantics=("arbitrary",), vmem_limit_bytes=58 * 1024 * 1024
        ),
        cost_estimate=pl.CostEstimate(flops=flops, bytes_accessed=40 << 20, transcendentals=0),
        name=name,
    )(*operands)


def place_of(dims):
    depth, tall, wide = dims
    core = lax.axis_index("wide")
    me = lax.axis_index("narrow")
    across = lax.rem(me, wide)
    up = lax.rem(lax.div(me, wide), tall)
    deep = lax.div(me, wide * tall)
    turn = core if tall == wide else 0
    second = (1 + turn * (wide - 1), across + turn * (up - across), wide)
    third = (wide - turn * (wide - 1), up + turn * (across - up), tall)
    return core, deep, second, third


def block_at(dims, deep, second, third, d, e, f):
    depth, tall, wide = dims
    return (
        lax.rem(deep + d, depth) * (tall * wide)
        + lax.rem(second[1] + e, second[2]) * second[0]
        + lax.rem(third[1] + f, third[2]) * third[0]
    )


def greet(dims, deep, second, third, core):
    barrier = pltpu.get_barrier_semaphore()
    peers = 1
    pl.semaphore_signal(barrier, inc=1, device_id={"wide": 1 - core}, device_id_type=pl.DeviceIdType.MESH)
    for axis, size in enumerate((dims[0], second[2], third[2])):
        for hop in range(1, size):
            moves = [0, 0, 0]
            moves[axis] = hop
            target = block_at(dims, deep, second, third, *moves)
            pl.semaphore_signal(
                barrier, inc=1, device_id={"narrow": target}, device_id_type=pl.DeviceIdType.MESH
            )
            peers += 1
    pl.semaphore_wait(barrier, peers)


def half_of(width, core):
    return pl.ds(pl.multiple_of(core * (width // 2), lanes), width // 2)


def remote(source, target, send_sem, recv_sem, device):
    return pltpu.make_async_remote_copy(
        src_ref=source,
        dst_ref=target,
        send_sem=send_sem,
        recv_sem=recv_sem,
        device_id=device,
        device_id_type=pl.DeviceIdType.MESH,
    )


def gather_kernel(dims, count, *refs):
    own, whole = refs[:count], refs[count : 2 * count]
    local_sem, send_sem, recv_sem, core_send, core_recv = refs[2 * count :]
    core, deep, second, third = place_of(dims)
    greet(dims, deep, second, third, core)
    depth, span_e, span_f = dims[0], second[2], third[2]
    other = {"wide": 1 - core}
    pending = []

    def at(d, e, f):
        return block_at(dims, deep, second, third, d, e, f)

    def slot(d, e, f):
        return (d * span_e + e) * span_f + f

    def back(size, hop):
        return (size - hop) % size

    def piece(which, number, side):
        return whole[which].at[number, :, half_of(whole[which].shape[2], side)]

    def onward(which, d, e, f):
        number = at(back(depth, d), back(span_e, e), back(span_f, f))
        first = d == 0 and e == 0 and f == 0
        source = own[which].at[:, half_of(own[which].shape[1], core)] if first else piece(which, number, core)
        target = piece(which, number, core)

        def push(moved, index):
            copy = remote(
                source, target, send_sem.at[which, index], recv_sem.at[which, index], {"narrow": at(*moved)}
            )
            copy.start()
            pending.append(copy)

        if e == 0 and f == 0 and d == 0:
            for hop in range(1, depth):
                push((hop, 0, 0), slot(hop, 0, 0))
        if f == 0 and e == 0:
            for hop in range(1, span_e):
                push((0, hop, 0), slot(d, hop, 0))
        if f == 0:
            for hop in range(1, span_f):
                push((0, 0, hop), slot(d, e, hop))
        if not first:
            index = slot(d, e, f)
            copy = remote(source, target, core_send.at[which, index], core_recv.at[which, index], other)
            copy.start()
            pending.append(copy)

    def arrived(which, d, e, f):
        target = piece(which, at(back(depth, d), back(span_e, e), back(span_f, f)), core)
        index = slot(d, e, f)
        remote(
            target, target, send_sem.at[which, index], recv_sem.at[which, index], {"narrow": at(0, 0, 1)}
        ).wait_recv()

    locals_ = []
    for which in range(count):
        onward(which, 0, 0, 0)
    for which in range(count):
        copy = pltpu.make_async_copy(own[which], whole[which].at[at(0, 0, 0)], local_sem.at[which])
        copy.start()
        locals_.append(copy)
    for which in range(count):
        for d in range(1, depth):
            arrived(which, d, 0, 0)
            onward(which, d, 0, 0)
        for d in range(depth):
            for e in range(1, span_e):
                arrived(which, d, e, 0)
                onward(which, d, e, 0)
        for d in range(depth):
            for e in range(span_e):
                for f in range(1, span_f):
                    arrived(which, d, e, f)
                    onward(which, d, e, f)
    mirror = place_of_other(dims)
    for which in range(count):
        for d in range(depth):
            for e in range(span_e):
                for f in range(span_f):
                    if d == 0 and e == 0 and f == 0:
                        continue
                    number = block_at(
                        dims, deep, *mirror, back(depth, d), back(span_e, e), back(span_f, f)
                    )
                    target = piece(which, number, 1 - core)
                    index = slot(d, e, f)
                    remote(
                        target, target, core_send.at[which, index], core_recv.at[which, index], other
                    ).wait_recv()
    for copy in pending:
        copy.wait_send()
    for copy in locals_:
        copy.wait()


def place_of_other(dims):
    core, deep, second, third = place_of(dims)
    if dims[1] != dims[2]:
        return second, third
    return third, second


def gather_weights(dims, shards):
    number = dims[0] * dims[1] * dims[2]
    count = len(shards)
    anywhere = pl.BlockSpec(memory_space=pl.ANY)
    return pl.pallas_call(
        functools.partial(gather_kernel, dims, count),
        in_specs=[anywhere] * count,
        out_specs=[anywhere] * count,
        out_shape=[jax.ShapeDtypeStruct((number,) + shard.shape, shard.dtype) for shard in shards],
        scratch_shapes=[
            pltpu.SemaphoreType.DMA((count,)),
            pltpu.SemaphoreType.DMA((count, number)),
            pltpu.SemaphoreType.DMA((count, number)),
            pltpu.SemaphoreType.DMA((count, number)),
            pltpu.SemaphoreType.DMA((count, number)),
        ],
        compiler_params=pltpu.CompilerParams(collective_id=0, has_side_effects=True),
        name="gather_weights",
    )(*shards)


def reduce_kernel(dims, count, places, plain_at, *refs):
    grads, plain_ref = refs[:count], refs[count]
    results = 1 + max(place[0] for place in places)
    sums, norms = refs[count + 1 : count + 1 + results], refs[count + 1 + results]
    held = refs[count + 2 + results :]
    mine, swapped, third_in, second_in, first_in = (
        held[index * count : (index + 1) * count] for index in range(5)
    )
    (norm_core, norm_deep, norm_wide, norm_tall) = held[5 * count : 5 * count + 4]
    (
        local_sem,
        core_send,
        core_recv,
        leg_send,
        leg_recv,
        last_send,
        last_recv,
        norm_send,
        norm_recv,
    ) = held[5 * count + 4 :]
    core, deep, second, third = place_of(dims)
    greet(dims, deep, second, third, core)
    depth, span_e, span_f = dims[0], second[2], third[2]
    other = {"wide": 1 - core}
    mirror = place_of_other(dims)
    pending = []

    def at(d, e, f):
        return block_at(dims, deep, second, third, d, e, f)

    def slot(d, e, f):
        return (d * span_e + e) * span_f + f

    def share(which, side):
        width = grads[which].shape[2]
        result, first = places[which]
        columns = pl.ds(pl.multiple_of(first + side * (width // 2), lanes), width // 2)
        return sums[result], columns

    far_first = sorted(
        ((d, e, f) for d in range(depth) for e in range(span_e) for f in range(span_f)),
        key=lambda item: (item[2] == 0, item[1] == 0, item[0] == 0),
    )
    loads = {}
    for move in far_first:
        for which in range(count):
            width = grads[which].shape[2]
            number = block_at(dims, deep, *mirror, *move)
            copy = remote(
                grads[which].at[number, :, half_of(width, 1 - core)],
                swapped[which].at[slot(*move)],
                core_send.at[which, slot(*move)],
                core_recv.at[which, slot(*move)],
                other,
            )
            copy.start()
            pending.append(copy)
            load = pltpu.make_async_copy(
                grads[which].at[at(*move), :, half_of(width, core)],
                mine[which].at[slot(*move)],
                local_sem.at[which, slot(*move)],
            )
            load.start()
            loads[which, move] = load

    def added(which, place, parts, store):
        rows = mine[which].shape[1]
        group = min(rows, 16)

        def some(index, carry):
            at_rows = pl.ds(pl.multiple_of(index * group, group), group)
            total = mine[which][place, at_rows, :].astype(jnp.float32)
            for ref, spot in parts:
                total = total + ref[spot, at_rows, :].astype(jnp.float32)
            return store(at_rows, total, carry)

        return functools.partial(lax.fori_loop, 0, rows // group, some)

    def wait_leg(which, index, ref, spot):
        remote(
            ref.at[spot], ref.at[spot], leg_send.at[which, index], leg_recv.at[which, index], other
        ).wait_recv()

    def collect(which, move):
        d, e, f = move
        place = slot(*move)
        loads[which, move].wait()
        remote(
            swapped[which].at[place],
            swapped[which].at[place],
            core_send.at[which, place],
            core_recv.at[which, place],
            other,
        ).wait_recv()
        parts = [(swapped[which], place)]
        if f == 0:
            for hop in range(1, span_f):
                spot = (d * span_e + e) * (span_f - 1) + hop - 1
                wait_leg(which, slot(d, e, hop), third_in[which], spot)
                parts.append((third_in[which], spot))
        if f == 0 and e == 0:
            for hop in range(1, span_e):
                spot = d * (span_e - 1) + hop - 1
                wait_leg(which, slot(d, hop, 0), second_in[which], spot)
                parts.append((second_in[which], spot))
        if f == 0 and e == 0 and d == 0:
            for hop in range(1, depth):
                wait_leg(which, slot(hop, 0, 0), first_in[which], hop - 1)
                parts.append((first_in[which], hop - 1))
        return place, parts

    for move in far_first[:-1]:
        d, e, f = move
        for which in range(count):
            place, parts = collect(which, move)

            def keep(at_rows, total, carry, which=which, place=place):
                mine[which][place, at_rows, :] = total.astype(mine[which].dtype)
                return carry

            added(which, place, parts, keep)(0)
            if f > 0:
                target, spot, moved = third_in[which], (d * span_e + e) * (span_f - 1) + f - 1, (0, 0, f)
            elif e > 0:
                target, spot, moved = second_in[which], d * (span_e - 1) + e - 1, (0, e, 0)
            else:
                target, spot, moved = first_in[which], d - 1, (d, 0, 0)
            copy = remote(
                mine[which].at[place],
                target.at[spot],
                leg_send.at[which, place],
                leg_recv.at[which, place],
                {"narrow": at(*moved)},
            )
            copy.start()
            pending.append(copy)

    squares = [jnp.zeros((8, lanes), jnp.float32), jnp.zeros((8, lanes), jnp.float32)]
    for which in range(count):
        place, parts = collect(which, (0, 0, 0))
        result, side = share(which, core)

        def finish(at_rows, total, carry, which=which, result=result, side=side):
            result[at_rows, side] = total
            kept, plain = carry
            squared = total * total
            if which == plain_at:
                marked = squared * plain_ref[at_rows, half_of(plain_ref.shape[1], core)]
                plain = plain + folded_squares(marked)
                squared = squared - marked
            return (kept + folded_squares(squared), plain)

        squares = added(which, place, parts, finish)(tuple(squares))
        copy = remote(
            result.at[:, side], result.at[:, side], last_send.at[which], last_recv.at[which], other
        )
        copy.start()
        pending.append(copy)

    running = jnp.stack(list(squares))
    me = lax.axis_index("narrow")
    tall, wide = dims[1], dims[2]
    my_wide = lax.rem(me, wide)
    my_tall = lax.rem(lax.div(me, wide), tall)
    plane = tall * wide
    index = 0
    stages = (
        (norm_core, 2, core, lambda spot: {"wide": spot}),
        (norm_deep, depth, deep, lambda spot: {"narrow": spot * plane + lax.rem(me, plane)}),
        (norm_wide, wide, my_wide, lambda spot: {"narrow": me - my_wide + spot}),
        (norm_tall, tall, my_tall, lambda spot: {"narrow": me + (spot - my_tall) * wide}),
    )
    for buffer, size, mine_at, device in stages:
        buffer[mine_at] = running
        for hop in range(1, size):
            copy = remote(
                buffer.at[mine_at],
                buffer.at[mine_at],
                norm_send.at[index],
                norm_recv.at[index],
                device(lax.rem(mine_at + hop, size)),
            )
            copy.start()
            pending.append(copy)
            index += 1
        index -= size - 1
        for hop in range(1, size):
            came = lax.rem(mine_at + size - hop, size)
            remote(
                buffer.at[came], buffer.at[came], norm_send.at[index], norm_recv.at[index], device(came)
            ).wait_recv()
            index += 1
        running = buffer[0]
        for spot in range(1, size):
            running = running + buffer[spot]
    norms[...] = running
    for which in range(count):
        result, side = share(which, 1 - core)
        remote(
            result.at[:, side], result.at[:, side], last_send.at[which], last_recv.at[which], other
        ).wait_recv()
    for copy in pending:
        copy.wait_send()


def folded_squares(values):
    total = None
    for row in range(0, values.shape[0], 8):
        for column in range(0, values.shape[1], lanes):
            piece = values[row : row + 8, column : column + lanes]
            total = piece if total is None else total + piece
    return total


def reduce_grads(dims, grads, places, plain_mask, plain_at):
    number = dims[0] * dims[1] * dims[2]
    depth, tall, wide = dims
    count = len(grads)
    anywhere = pl.BlockSpec(memory_space=pl.ANY)
    inside = pl.BlockSpec(memory_space=pltpu.VMEM)

    def room(places):
        return [
            pltpu.VMEM((places, grad.shape[1], grad.shape[2] // 2), grad.dtype) for grad in grads
        ]

    third, second = (tall, wide)
    results = 1 + max(place[0] for place in places)
    sums = []
    for index in range(results):
        members = [grad for grad, place in zip(grads, places) if place[0] == index]
        sums.append(shape((members[0].shape[1], sum(grad.shape[2] for grad in members))))
    result = pl.pallas_call(
        functools.partial(reduce_kernel, dims, count, places, plain_at),
        in_specs=[anywhere] * count + [inside],
        out_specs=[inside] * (results + 1),
        out_shape=sums + [shape((2, 8, lanes))],
        scratch_shapes=room(number)
        + room(number)
        + room(depth * second * (third - 1))
        + room(depth * (second - 1))
        + room(depth - 1)
        + [pltpu.VMEM((size, 2, 8, lanes), jnp.float32) for size in (2, depth, wide, tall)]
        + [
            pltpu.SemaphoreType.DMA((count, number)),
            pltpu.SemaphoreType.DMA((count, number)),
            pltpu.SemaphoreType.DMA((count, number)),
            pltpu.SemaphoreType.DMA((count, number)),
            pltpu.SemaphoreType.DMA((count, number)),
            pltpu.SemaphoreType.DMA((count,)),
            pltpu.SemaphoreType.DMA((count,)),
            pltpu.SemaphoreType.DMA((depth + tall + wide,)),
            pltpu.SemaphoreType.DMA((depth + tall + wide,)),
        ],
        compiler_params=pltpu.CompilerParams(
            collective_id=1, has_side_effects=True, vmem_limit_bytes=56 * 1024 * 1024
        ),
        name="reduce_grads",
    )(*grads, plain_mask)
    return result[:results], jnp.sum(result[results], axis=(1, 2))


def grid_of(mesh):
    number = mesh.shape["narrow"]
    places = [getattr(device, "coords", None) for device in mesh.devices[0]]
    if all(place is not None for place in places):
        sizes = [len({place[axis] for place in places}) for axis in (2, 1, 0)]
        if sizes[0] * sizes[1] * sizes[2] == number:
            return tuple(sizes)
    side = round((number / 2) ** (1 / 3))
    return (2 * side, side, side) if 2 * side**3 == number else (number, 1, 1)


def folded_small(values):
    flat = values.reshape(-1)
    rows = -(-flat.shape[0] // (32 * lanes)) * 16
    flat = jnp.pad(flat, (0, 2 * rows * lanes - flat.shape[0])).reshape(2, rows, lanes)
    return jnp.concatenate([flat[0], flat[1]], axis=1)


def per_device(
    dims,
    tokens,
    cotangent,
    loss_mask,
    seq_lengths,
    norm_gain,
    in_proj,
    conv_weight,
    conv_bias,
    select_proj,
    step_proj,
    step_bias,
    decay_log,
    skip_scale,
    out_proj,
):
    half = jnp.bfloat16
    piece = skip_scale.shape[0]
    gain_piece = norm_gain.shape[0]
    taps_n, select_n, step_n, state_size = (
        conv_weight.shape[0],
        select_proj.shape[0],
        step_proj.shape[0],
        decay_log.shape[0],
    )
    heights = (select_n, step_n, state_size, taps_n, 1, 1, 1, 1)
    packed = jnp.concatenate(
        [
            select_proj,
            step_proj,
            decay_log,
            conv_weight,
            conv_bias[None],
            step_bias[None],
            skip_scale[None],
            jnp.pad(norm_gain, (0, piece - gain_piece))[None],
        ],
        axis=0,
    ).astype(half)
    in_blocks, out_blocks, packed_blocks = gather_weights(
        dims, [in_proj.astype(half), out_proj.astype(half), folded_small(packed)]
    )
    in_whole = in_blocks.reshape(-1, in_blocks.shape[2])
    out_whole = out_blocks.reshape(-1, out_blocks.shape[2])
    packed_whole = jnp.concatenate(
        [
            packed_blocks[:, :, :lanes].reshape(packed_blocks.shape[0], -1),
            packed_blocks[:, :, lanes:].reshape(packed_blocks.shape[0], -1),
        ],
        axis=1,
    )[:, : packed.size].reshape((-1,) + packed.shape)
    packed_whole = jnp.swapaxes(packed_whole, 0, 1).reshape(packed.shape[0], -1)
    cuts = [sum(heights[:index]) for index in range(len(heights) + 1)]
    parts = [packed_whole[cuts[i] : cuts[i + 1]] for i in range(len(heights))]
    step_whole = parts[1]
    select_whole = jnp.pad(parts[0], ((0, lanes - select_n), (0, 0)))
    decay_value, taps_value = parts[2].astype(jnp.float32), parts[3].astype(jnp.float32)
    shift_value, bias_value, skip_value = (parts[i].astype(jnp.float32) for i in (4, 5, 6))
    gain_value = parts[7].reshape(-1, piece)[:, :gain_piece].reshape(1, -1).astype(jnp.float32)

    rows, model = tokens.shape
    inner = skip_value.shape[1]
    rank, size = step_n, state_size
    width = 4 * lanes
    blocks = inner // width
    chunks = rows // chunk
    offset_in = layout(seq_lengths[0], rows)
    offsets = jnp.broadcast_to(jnp.pad(offset_in, (0, 8))[:, None], (rows + 8, lanes))
    grad_low = cotangent * loss_mask.astype(half)[:, None]
    rate = -jnp.exp(decay_value) * log2e

    whole = pl.BlockSpec(memory_space=pltpu.VMEM)
    tall = pl.BlockSpec((rows, width), lambda b: (0, b))
    deep = pl.BlockSpec((chunks, chunk, width), lambda b: (0, 0, b))
    lead = pl.BlockSpec((rows, size, width), lambda b: (0, 0, b))
    first_w = pl.BlockSpec((model, width), lambda b: (0, b))
    second_w = pl.BlockSpec((model, width), lambda b: (0, b + blocks))
    out_w = pl.BlockSpec((width, model), lambda b: (b, 0))

    def thin(height):
        return pl.BlockSpec((height, width), lambda b: (0, b))

    def fixed(*dims_of):
        return pl.BlockSpec(dims_of, lambda b: (0,) * len(dims_of))

    branch, gate_pre, signal, projected, flipped = compute_call(
        front_kernel,
        "front",
        blocks,
        [whole, whole, whole, thin(taps_n), thin(1), thin(lanes), first_w, second_w],
        [tall, tall, tall, fixed(rows, lanes), fixed(model, rows)],
        [
            shape((rows, inner)),
            shape((rows, inner)),
            shape((rows, inner), half),
            shape((rows, lanes)),
            shape((model, rows), half),
        ],
        [pltpu.VMEM((rows, model), half)],
        4 * rows * model * inner,
        (tokens, gain_value, offsets, taps_value, shift_value, select_whole, in_whole, in_whole),
    )
    write_rows = projected[:, rank : rank + size]
    read_rows = projected[:, rank + size : rank + 2 * size]
    wide_write = jnp.broadcast_to(write_rows[:, :, None], (rows, size, lanes))
    wide_read = jnp.broadcast_to(read_rows[:, :, None], (rows, size, lanes))
    states, core_grad, gate_grad, grad_skip, grad_outw, grad_in_gate, output = compute_call(
        forward_kernel,
        "forward",
        blocks,
        [whole, thin(rank), thin(1), whole, tall, whole, whole, thin(size), thin(1), tall]
        + [whole, out_w, whole, whole],
        [lead, deep, tall, thin(1), out_w, first_w, fixed(rows, model)],
        [
            shape((rows, size, inner), half),
            shape((chunks, chunk, inner)),
            shape((rows, inner), half),
            shape((1, inner)),
            shape((inner, model), half),
            shape((model, inner), half),
            shape((rows, model), half),
        ],
        [
            pltpu.VMEM((rows, width), jnp.float32),
            pltpu.VMEM((chunks, chunk, width), jnp.float32),
            pltpu.VMEM((chunks, chunk, width), jnp.float32),
            pltpu.VMEM((chunks, chunk, width), jnp.float32),
            pltpu.VMEM((width // lanes, chunk * chunk, lanes), jnp.float32),
            pltpu.VMEM((rows, width), half),
            pltpu.VMEM((rows, model), jnp.float32),
        ],
        15 * rows * inner * size,
        (
            projected,
            step_whole,
            bias_value,
            offsets,
            signal,
            wide_write,
            wide_read,
            rate,
            skip_value,
            gate_pre,
            grad_low,
            out_whole,
            flipped,
            tokens,
        ),
    )
    signal_grad, grad_stepw, grad_bias, grad_decaylog, grad_rank, grad_write, grad_read = compute_call(
        backward_kernel,
        "backward",
        blocks,
        [whole, thin(rank), thin(1), whole, tall, whole, whole, thin(size), thin(1), deep, lead],
        [
            tall,
            thin(rank),
            thin(1),
            thin(size),
            fixed(rows, rank),
            fixed(chunks + 1, size, 2 * chunk),
            fixed(chunks + 1, size, 2 * chunk),
        ],
        [
            shape((rows, inner)),
            shape((rank, inner)),
            shape((1, inner)),
            shape((size, inner)),
            shape((rows, rank)),
            shape((chunks + 1, size, 2 * chunk)),
            shape((chunks + 1, size, 2 * chunk)),
        ],
        [
            pltpu.VMEM((rows, width), jnp.float32),
            pltpu.VMEM((chunks, chunk, width), jnp.float32),
            pltpu.VMEM((chunks, chunk, width), jnp.float32),
            pltpu.VMEM((chunks + 1, 2 * chunk, width), half),
            pltpu.VMEM((chunks, 2 * chunk, width), half),
            pltpu.VMEM((2, width // lanes, chunk * chunk, lanes), jnp.float32),
            pltpu.VMEM((2, width // lanes, chunk * chunk, lanes), jnp.float32),
            pltpu.VMEM((2, chunk * size, width), half),
            pltpu.VMEM((chunks + 1, chunk, width), jnp.float32),
            pltpu.VMEM((chunks + 1, chunk, width), jnp.float32),
            pltpu.VMEM((rows, width), half),
        ],
        40 * rows * inner * size,
        (
            projected,
            step_whole,
            bias_value,
            offsets,
            signal,
            wide_write,
            wide_read,
            rate,
            skip_value,
            core_grad,
            states,
        ),
    )

    def by_token(pairs):
        summed = pairs[:chunks, :, :chunk] + pairs[:chunks, :, chunk:]
        return jnp.swapaxes(summed, 1, 2).reshape(rows, size)

    flat = jnp.concatenate(
        [
            grad_rank,
            by_token(grad_write),
            by_token(grad_read),
            jnp.zeros((rows, lanes - rank - 2 * size), jnp.float32),
        ],
        axis=1,
    ).astype(half)
    wide_mask = jnp.broadcast_to(loss_mask.astype(jnp.float32)[:, None], (rows, lanes))
    grad_select, grad_taps, grad_shift, grad_in_branch, grad_gain, grad_tokens = compute_call(
        back_kernel,
        "back",
        blocks,
        [whole, whole, whole, whole, whole, thin(taps_n), thin(1), thin(lanes), whole]
        + [tall, tall, tall, tall, whole, first_w, second_w],
        [thin(lanes), thin(taps_n), thin(1), first_w, fixed(1, model), fixed(rows, model)],
        [
            shape((lanes, inner)),
            shape((taps_n, inner)),
            shape((1, inner)),
            shape((model, inner), half),
            shape((1, model)),
            shape((rows, model), half),
        ],
        [
            pltpu.VMEM((rows + 8, width), jnp.float32),
            pltpu.VMEM((rows, width), half),
            pltpu.VMEM((rows, model), jnp.float32),
        ],
        8 * rows * model * inner,
        (
            tokens,
            cotangent,
            wide_mask,
            gain_value,
            offsets,
            taps_value,
            shift_value,
            select_whole,
            flat,
            branch,
            signal,
            signal_grad,
            gate_grad,
            flipped,
            in_whole,
            in_whole,
        ),
    )

    gain_row = jnp.pad(
        grad_gain.reshape(-1, gain_piece), ((0, 0), (0, piece - gain_piece))
    ).reshape(1, -1)
    grads_packed = jnp.concatenate(
        [
            grad_select[:select_n],
            grad_stepw,
            grad_decaylog,
            grad_taps,
            grad_shift,
            grad_bias,
            grad_skip,
            gain_row,
        ],
        axis=0,
    )
    blocks = in_blocks.shape[0]
    packed_grads = jax.vmap(folded_small)(
        jnp.swapaxes(grads_packed.reshape(packed.shape[0], blocks, piece), 0, 1)
    )
    rows_of = jnp.concatenate(
        [jnp.full((height, piece), index in (2, 5, 6), jnp.float32) for index, height in enumerate(heights)]
    )
    split = in_blocks.shape[:2] + (inner,)
    (in_sum, out_sum, packed_sum), norms = reduce_grads(
        dims,
        [
            grad_in_branch.reshape(split),
            grad_in_gate.reshape(split),
            grad_outw.reshape(out_blocks.shape),
            packed_grads.astype(half),
        ],
        [(0, 0), (0, inner), (1, 0), (2, 0)],
        folded_small(rows_of),
        3,
    )
    packed_sum = jnp.concatenate(
        [packed_sum[:, :lanes].reshape(-1), packed_sum[:, lanes:].reshape(-1)]
    )[: packed.size].reshape(packed.shape)
    small = [packed_sum[cuts[i] : cuts[i + 1]] for i in range(len(heights))]
    gain_sum = small[7][0, :gain_piece]

    return (
        output,
        grad_tokens,
        gain_sum,
        in_sum,
        small[3],
        small[4][0],
        small[0],
        small[1],
        small[5][0],
        small[2],
        small[6][0],
        out_sum,
        norms[0],
        norms[1],
    )


def solution(mesh):
    placed = (
        P(("wide", "narrow"), None),
        P(("wide", "narrow"), None),
        P(("wide", "narrow")),
        P(("wide", "narrow"), None),
        P("narrow"),
        P("narrow", None),
        P(None, "narrow"),
        P("narrow"),
        P(None, "narrow"),
        P(None, "narrow"),
        P("narrow"),
        P(None, "narrow"),
        P("narrow"),
        P("narrow", None),
    )
    return jax.shard_map(
        functools.partial(per_device, grid_of(mesh)),
        mesh=mesh,
        in_specs=placed,
        out_specs=(
            P(("wide", "narrow"), None),
            P(("wide", "narrow"), None),
            P("narrow"),
            P("narrow", None),
            P(None, "narrow"),
            P("narrow"),
            P(None, "narrow"),
            P(None, "narrow"),
            P("narrow"),
            P(None, "narrow"),
            P("narrow"),
            P("narrow", None),
            P(),
            P(),
        ),
        check_vma=False,
    )
```

```python
import functools
import math

import jax
import jax.numpy as jnp
import numpy as np
from jax import lax
from jax.experimental import pallas as pl
from jax.experimental.pallas import tpu as pltpu
from jax.sharding import PartitionSpec as P

epsilon = 1e-05
chunk = 8
lanes = 128
log2e = math.log2(math.e)
ln2 = math.log(2.0)
far = 1e30


def contract(left, right, left_dim, right_dim):
    return lax.dot_general(
        left, right, (((left_dim,), (right_dim,)), ((), ())), preferred_element_type=jnp.float32
    )


def row_loop(rows, group, body, initial):
    def some(index, carry):
        return body(index, pl.ds(pl.multiple_of(index * group, group), group), carry)

    return lax.fori_loop(0, rows // group, some, initial)


def cut(tile):
    return pl.ds(tile * lanes, lanes)


def sigmoid(values):
    return 0.5 * jnp.tanh(0.5 * values) + 0.5


def softplus(values):
    small = jnp.exp(-jnp.abs(values))
    series = small * (1.0 - small * (0.5 - small * (1.0 / 3.0 - 0.25 * small)))
    return jnp.maximum(values, 0.0) + jnp.where(small < 0.03, series, jnp.log(1.0 + small))


def slope_of(step):
    series = step * (1.0 - step * (0.5 - step * (1.0 / 6.0 - step * (1.0 / 24.0))))
    return jnp.where(step < 0.03, series, 1.0 - jnp.exp(-step))


def fill_offsets(lengths_ref, offset_buf, rows):
    place = lax.broadcasted_iota(jnp.int32, offset_buf.shape, 0)
    start = jnp.zeros(offset_buf.shape, jnp.int32)
    ahead = jnp.int32(0)
    for index in range(lengths_ref.shape[1] - 1):
        ahead = ahead + lengths_ref[0, index]
        start = jnp.where(place >= ahead, ahead, start)
    offset_buf[...] = jnp.where(place < rows, place - start, 0)


def small_rows(small_ref, first, count):
    base = first // 16 * 16
    tall = -(-(first + count - base) // 16) * 16
    return small_ref[base : base + tall, :].astype(jnp.float32)[first - base : first - base + count]


def eight(values):
    total = values[:8]
    for row in range(8, values.shape[0], 8):
        total = total + values[row : row + 8]
    return total


def conv_rows(index, at, group, tile, branch_ref, offset_buf, taps, shift):
    count = taps.shape[0]
    here = slice(tile * lanes, (tile + 1) * lanes)
    current = branch_ref[at, cut(tile)]
    before = branch_ref[pl.ds(pl.multiple_of(jnp.maximum(index * group - 8, 0), 8), 8), cut(tile)]
    both = jnp.concatenate([before, current], axis=0)
    offsets = offset_buf[at, :]
    summed = shift[:, here] + taps[count - 1 : count, here] * current
    reads = [None] * count
    reads[count - 1] = current
    for tap in range(count - 1):
        lag = count - 1 - tap
        reads[tap] = jnp.where(offsets >= lag, pltpu.roll(both, lag, 0)[8:], 0.0)
        summed = summed + taps[tap : tap + 1, here] * reads[tap]
    return summed, reads


def front_kernel(
    plan,
    lengths_ref,
    tokens_ref,
    cotangent_ref,
    mask_ref,
    gain_ref,
    small_ref,
    branch_w,
    gate_w,
    branch_ref,
    gate_ref,
    signal_ref,
    projected_ref,
    flipped_ref,
    low_ref,
    normed_buf,
    offset_buf,
):
    rows = tokens_ref.shape[0]
    width = branch_ref.shape[1]
    block = pl.program_id(0)

    @pl.when(block == 0)
    def _():
        fill_offsets(lengths_ref, offset_buf, rows)

        def norm(index, at, carry):
            residual = tokens_ref[at, :].astype(jnp.float32)
            scale = lax.rsqrt(jnp.mean(residual * residual, axis=1, keepdims=True) + epsilon)
            normed_buf[at, :] = (residual * scale * gain_ref[...]).astype(normed_buf.dtype)
            return carry

        row_loop(rows, 16, norm, 0)
        flipped_ref[...] = normed_buf[...].T
        projected_ref[...] = jnp.zeros_like(projected_ref)
        down = lax.broadcasted_iota(jnp.int32, (rows, rows), 0)
        along = lax.broadcasted_iota(jnp.int32, (rows, rows), 1)
        diagonal = jnp.where(down == along, mask_ref[...].astype(jnp.float32), 0.0).astype(low_ref.dtype)
        low_ref[...] = jnp.dot(
            diagonal, cotangent_ref[...], preferred_element_type=jnp.float32
        ).astype(low_ref.dtype)

    branch_ref[...] = jnp.dot(normed_buf[...], branch_w[...], preferred_element_type=jnp.float32)
    gate_ref[...] = jnp.dot(normed_buf[...], gate_w[...], preferred_element_type=jnp.float32)
    taps = small_rows(small_ref, *plan["taps"])
    shift = small_rows(small_ref, *plan["shift"])

    def some(index, at, carry):
        for tile in range(width // lanes):
            summed, _ = conv_rows(index, at, 32, tile, branch_ref, offset_buf, taps, shift)
            signal_ref[at, cut(tile)] = (summed * sigmoid(summed)).astype(signal_ref.dtype)
        return carry

    row_loop(rows, 32, some, 0)
    projected_ref[...] += contract(signal_ref[...], small_ref[:lanes, :], 1, 1)


def folded(buffer, tile):
    total = buffer[tile, pl.ds(0, chunk, stride=chunk), :]
    for row in range(1, chunk):
        total = total + buffer[tile, pl.ds(row, chunk, stride=chunk), :]
    return total


def forward_kernel(
    plan,
    lengths_ref,
    projected_ref,
    small_ref,
    signal_ref,
    write_ref,
    read_ref,
    gate_ref,
    low_ref,
    out_w,
    flipped_ref,
    tokens_ref,
    states_ref,
    step_ref,
    core_grad_ref,
    gate_grad_ref,
    skip_grad_ref,
    out_grad_ref,
    in_grad_ref,
    output_ref,
    offset_buf,
    pre_buf,
    decay_step,
    inflow,
    core_buf,
    fold_buf,
    gated_buf,
    total,
):
    rows, width = pre_buf.shape
    size = write_ref.shape[1]
    half = size // 2
    tiles = width // lanes
    rank = plan["step"][1]
    block = pl.program_id(0)

    @pl.when(block == 0)
    def _():
        fill_offsets(lengths_ref, offset_buf, rows)

    pre_buf[...] = jnp.dot(
        projected_ref[:, :rank].astype(small_ref.dtype),
        small_ref[pl.ds(plan["step"][0], rank), :],
        preferred_element_type=jnp.float32,
    )
    bias = small_rows(small_ref, *plan["bias"])

    def before(index, at, carry):
        spot = pl.ds(pl.multiple_of(index * 4, 4), 4)
        inside = offset_buf[at, :] > 0
        for tile in range(tiles):
            step = softplus(pre_buf[at, cut(tile)] + bias[:, tile * lanes : (tile + 1) * lanes])
            step_ref[spot, :, cut(tile)] = step.reshape(4, chunk, lanes)
            decay_step[spot, :, cut(tile)] = jnp.where(inside, step, far).reshape(4, chunk, lanes)
            flow = step * signal_ref[at, cut(tile)].astype(jnp.float32)
            inflow[spot, :, cut(tile)] = flow.reshape(4, chunk, lanes)
        return carry

    row_loop(rows, 4 * chunk, before, 0)
    rates = -jnp.exp(small_rows(small_ref, *plan["decay"])) * log2e
    rates = [rates[:, tile * lanes : (tile + 1) * lanes] for tile in range(tiles)]

    def forward(index, held):
        held = list(held)
        for place in range(chunk):
            now = index * chunk + place
            write_now = write_ref[now]
            read_now = read_ref[now]
            for tile in range(tiles):
                decay = jnp.exp2(rates[tile] * decay_step[index, pl.ds(place, 1), cut(tile)])
                fresh = decay * held[tile] + write_now * inflow[index, pl.ds(place, 1), cut(tile)]
                held[tile] = fresh
                states_ref[now, :, cut(tile)] = fresh.astype(states_ref.dtype)
                product = read_now * fresh
                fold_buf[tile, pl.ds(place * chunk, chunk), :] = product[:half] + product[half:]
        for tile in range(tiles):
            core_buf[index, :, cut(tile)] = folded(fold_buf, tile)
        return tuple(held)

    zero_tile = jnp.zeros((size, lanes), jnp.float32)
    lax.fori_loop(0, rows // chunk, forward, (zero_tile,) * tiles)

    pre_buf[...] = contract(low_ref[...], out_w[...], 1, 1)
    skip = small_rows(small_ref, *plan["skip"])

    def after(index, at, carry):
        spot = pl.ds(pl.multiple_of(index * 4, 4), 4)
        sums = []
        for tile in range(tiles):
            signal = signal_ref[at, cut(tile)].astype(jnp.float32)
            core = core_buf[spot, :, cut(tile)].reshape(4 * chunk, lanes)
            core = core + skip[:, tile * lanes : (tile + 1) * lanes] * signal
            gate = gate_ref[at, cut(tile)]
            sigma = sigmoid(gate)
            active = gate * sigma
            gated_buf[at, cut(tile)] = (core * active).astype(gated_buf.dtype)
            grad_gated = pre_buf[at, cut(tile)]
            grad_core = grad_gated * active
            core_grad_ref[spot, :, cut(tile)] = grad_core.reshape(4, chunk, lanes)
            slope = sigma + active * (1.0 - sigma)
            gate_grad_ref[at, cut(tile)] = (grad_gated * core * slope).astype(gate_grad_ref.dtype)
            sums.append(carry[tile] + eight(grad_core * signal))
        return tuple(sums)

    zero_rows = jnp.zeros((8, lanes), jnp.float32)
    skips = row_loop(rows, 4 * chunk, after, (zero_rows,) * tiles)
    for tile in range(tiles):
        skip_grad_ref[:, cut(tile)] = jnp.sum(skips[tile], axis=0, keepdims=True)
    out_grad_ref[...] = contract(gated_buf[...], low_ref[...], 0, 0).astype(out_grad_ref.dtype)
    in_grad_ref[...] = jnp.dot(
        flipped_ref[...], gate_grad_ref[...], preferred_element_type=jnp.float32
    ).astype(in_grad_ref.dtype)
    piece = jnp.dot(gated_buf[...], out_w[...], preferred_element_type=jnp.float32)

    @pl.when(block == 0)
    def _():
        total[...] = piece

    @pl.when(block > 0)
    def _():
        total[...] += piece

    @pl.when(block == pl.num_programs(0) - 1)
    def _():
        output_ref[...] = (tokens_ref[...].astype(jnp.float32) + total[...]).astype(output_ref.dtype)


def backward_kernel(
    plan,
    lengths_ref,
    projected_ref,
    small_ref,
    signal_ref,
    write_ref,
    read_ref,
    step_ref,
    core_grad_ref,
    states_ref,
    signal_grad_ref,
    step_w_grad_ref,
    bias_grad_ref,
    decay_grad_ref,
    rank_ref,
    write_grad_ref,
    read_grad_ref,
    offset_buf,
    decay_step,
    inflow,
    flow_pair,
    grad_pair,
    first_buf,
    second_buf,
    grad_rows,
    through_buf,
    scaled_buf,
    low_buf,
):
    rows, width = low_buf.shape
    rank = plan["step"][1]
    size = write_ref.shape[1]
    half = size // 2
    tiles = width // lanes
    chunks = rows // chunk
    block = pl.program_id(0)

    def paired(values):
        high = values.astype(jnp.bfloat16).astype(jnp.float32)
        return jnp.concatenate([high, values - high], axis=0).astype(jnp.bfloat16)

    @pl.when(block == 0)
    def _():
        fill_offsets(lengths_ref, offset_buf, rows)
        write_grad_ref[...] = jnp.zeros_like(write_grad_ref)
        read_grad_ref[...] = jnp.zeros_like(read_grad_ref)
        rank_ref[...] = jnp.zeros_like(rank_ref)

    def before(index, at, carry):
        spot = pl.ds(pl.multiple_of(index * 4, 4), 4)
        inside = (offset_buf[at, :] > 0).reshape(4, chunk, lanes)
        for tile in range(tiles):
            step = step_ref[spot, :, cut(tile)]
            decay_step[spot, :, cut(tile)] = jnp.where(inside, step, far)
            signal = signal_ref[at, cut(tile)].astype(jnp.float32).reshape(4, chunk, lanes)
            flow = step * signal
            inflow[spot, :, cut(tile)] = flow
            for part in range(4):
                here = index * 4 + part
                flow_pair[here, :, cut(tile)] = paired(flow[part])
                grad_pair[here, :, cut(tile)] = paired(core_grad_ref[here, :, cut(tile)])
        return carry

    row_loop(rows, 4 * chunk, before, 0)
    flow_pair[chunks] = jnp.zeros_like(flow_pair[chunks])
    grad_rows[...] = jnp.zeros_like(grad_rows)
    first_buf[...] = jnp.zeros_like(first_buf)
    second_buf[...] = jnp.zeros_like(second_buf)
    rates = -jnp.exp(small_rows(small_ref, *plan["decay"])) * log2e
    rates = [rates[:, tile * lanes : (tile + 1) * lanes] for tile in range(tiles)]

    token_of = lax.rem(lax.broadcasted_iota(jnp.int32, (size, 2 * chunk), 1), chunk)

    def own_token(products):
        kept = None
        for place in range(chunk):
            piece = products[place * size : (place + 1) * size]
            kept = piece if kept is None else jnp.where(token_of == place, piece, kept)
        return kept

    def settle(index, slot):
        for tile in range(tiles):
            through_buf[index, :, cut(tile)] = folded(first_buf.at[slot], tile)
            scaled_buf[index, :, cut(tile)] = folded(second_buf.at[slot], tile)
        write_grad_ref[index] += own_token(contract(grad_rows[slot], flow_pair[index], 1, 1))

    def backward(position, carried):
        index = chunks - 1 - position
        slot = lax.rem(position, 2)
        settle(index + 1, 1 - slot)
        base = index * chunk
        here = states_ref[pl.ds(base, chunk)].reshape(chunk * size, width)
        read_grad_ref[index] += own_token(contract(here, grad_pair[index], 1, 1))
        incoming, decay_sums = list(carried[0]), list(carried[1])
        for place in range(chunk - 1, -1, -1):
            now = base + place
            earlier = jnp.maximum(now - 1, 0) if place == 0 else now - 1
            write_now = write_ref[now]
            read_now = read_ref[now]
            for tile in range(tiles):
                step_now = decay_step[index, pl.ds(place, 1), cut(tile)]
                grad_state = incoming[tile] + read_now * core_grad_ref[index, pl.ds(place, 1), cut(tile)]
                grad_rows[slot, pl.ds(place * size, size), cut(tile)] = grad_state.astype(grad_rows.dtype)
                passed = grad_state * write_now
                first_buf[slot, tile, pl.ds(place * chunk, chunk), :] = passed[:half] + passed[half:]
                leaving = jnp.exp2(rates[tile] * step_now) * grad_state
                incoming[tile] = leaving
                weighted = leaving * states_ref[earlier, :, cut(tile)].astype(jnp.float32)
                scaled = weighted * rates[tile]
                second_buf[slot, tile, pl.ds(place * chunk, chunk), :] = scaled[:half] + scaled[half:]
                decay_sums[tile] = decay_sums[tile] + weighted * step_now
        return (tuple(incoming), tuple(decay_sums))

    zero_tile = jnp.zeros((size, lanes), jnp.float32)
    _, decay_sums = lax.fori_loop(0, chunks, backward, ((zero_tile,) * tiles, (zero_tile,) * tiles))
    settle(0, (chunks - 1) % 2)
    for tile in range(tiles):
        decay_grad_ref[:, cut(tile)] = decay_sums[tile] * rates[tile] * ln2
    skip = small_rows(small_ref, *plan["skip"])

    def after(index, at, carry):
        spot = pl.ds(pl.multiple_of(index * 4, 4), 4)
        sums = []
        for tile in range(tiles):
            signal = signal_ref[at, cut(tile)].astype(jnp.float32)
            step = step_ref[spot, :, cut(tile)].reshape(4 * chunk, lanes)
            through = through_buf[spot, :, cut(tile)].reshape(4 * chunk, lanes)
            scaled = scaled_buf[spot, :, cut(tile)].reshape(4 * chunk, lanes)
            core_grad = core_grad_ref[spot, :, cut(tile)].reshape(4 * chunk, lanes)
            grad_pre = (through * signal + ln2 * scaled) * slope_of(step)
            low_buf[at, cut(tile)] = grad_pre.astype(low_buf.dtype)
            signal_grad_ref[at, cut(tile)] = (
                through * step + skip[:, tile * lanes : (tile + 1) * lanes] * core_grad
            )
            sums.append(carry[tile] + eight(grad_pre))
        return tuple(sums)

    zero_rows = jnp.zeros((8, lanes), jnp.float32)
    sums = row_loop(rows, 4 * chunk, after, (zero_rows,) * tiles)
    for tile in range(tiles):
        bias_grad_ref[:, cut(tile)] = jnp.sum(sums[tile], axis=0, keepdims=True)
    step_w_grad_ref[...] = contract(
        projected_ref[:, :rank].astype(low_buf.dtype), low_buf[...], 0, 0
    )
    rank_ref[...] += contract(low_buf[...], small_ref[pl.ds(plan["step"][0], rank), :], 1, 1)


def back_kernel(
    plan,
    lengths_ref,
    tokens_ref,
    low_ref,
    gain_ref,
    small_ref,
    flat_ref,
    branch_ref,
    signal_ref,
    signal_grad_ref,
    gate_grad_ref,
    flipped_ref,
    branch_w,
    gate_w,
    step_w_grad_ref,
    bias_grad_ref,
    decay_grad_ref,
    skip_grad_ref,
    small_grad_ref,
    in_grad_ref,
    gain_grad_ref,
    tokens_grad_ref,
    offset_buf,
    conv_buf,
    mixed_buf,
    total,
):
    rows = tokens_ref.shape[0]
    width = branch_ref.shape[1]
    tiles = width // lanes
    block = pl.program_id(0)

    @pl.when(block == 0)
    def _():
        fill_offsets(lengths_ref, offset_buf, rows)

    taps = small_rows(small_ref, *plan["taps"])
    shift = small_rows(small_ref, *plan["shift"])
    count = taps.shape[0]
    small_grad_ref[:lanes, :] = contract(flat_ref[...], signal_ref[...], 0, 0)

    def place_rows(name, values):
        first, tall = plan[name]
        small_grad_ref[first : first + tall, :] = values

    place_rows("step", step_w_grad_ref[...])
    place_rows("decay", decay_grad_ref[...])
    place_rows("bias", bias_grad_ref[...])
    place_rows("skip", skip_grad_ref[...])
    conv_buf[pl.ds(0, rows), :] = signal_grad_ref[...] + jnp.dot(
        flat_ref[...], small_ref[:lanes, :], preferred_element_type=jnp.float32
    )
    conv_buf[pl.ds(rows, 8), :] = jnp.zeros((8, width), jnp.float32)

    def through_conv(index, at, carry):
        sums = []
        for tile in range(tiles):
            summed, reads = conv_rows(index, at, 32, tile, branch_ref, offset_buf, taps, shift)
            sigma = sigmoid(summed)
            grad_conv = conv_buf[at, cut(tile)] * (sigma + summed * sigma * (1.0 - sigma))
            conv_buf[at, cut(tile)] = grad_conv
            adds = [grad_conv] + [grad_conv * read for read in reads]
            sums.append(tuple(kept + eight(add) for kept, add in zip(carry[tile], adds)))
        return tuple(sums)

    zero_rows = jnp.zeros((8, lanes), jnp.float32)
    sums = row_loop(rows, 32, through_conv, ((zero_rows,) * (count + 1),) * tiles)
    for tile in range(tiles):
        first = plan["shift"][0]
        small_grad_ref[first : first + 1, cut(tile)] = jnp.sum(sums[tile][0], axis=0, keepdims=True)
        for tap in range(count):
            first = plan["taps"][0] + tap
            small_grad_ref[first : first + 1, cut(tile)] = jnp.sum(
                sums[tile][tap + 1], axis=0, keepdims=True
            )

    def to_branch(index, at, carry):
        longer = pl.ds(pl.multiple_of(index * 32, 32), 40)
        offsets = offset_buf[longer, :]
        for tile in range(tiles):
            here = slice(tile * lanes, (tile + 1) * lanes)
            grads = conv_buf[longer, cut(tile)]
            summed = taps[count - 1 : count, here] * grads[:32]
            for tap in range(count - 1):
                lag = count - 1 - tap
                kept = jnp.where(offsets >= lag, grads, 0.0)
                summed = summed + taps[tap : tap + 1, here] * pltpu.roll(kept, 40 - lag, 0)[:32]
            mixed_buf[at, cut(tile)] = summed.astype(mixed_buf.dtype)
        return carry

    row_loop(rows, 32, to_branch, 0)
    in_grad_ref[...] = jnp.dot(
        flipped_ref[...], mixed_buf[...], preferred_element_type=jnp.float32
    ).astype(in_grad_ref.dtype)
    piece = contract(mixed_buf[...], branch_w[...], 1, 1) + contract(gate_grad_ref[...], gate_w[...], 1, 1)

    @pl.when(block == 0)
    def _():
        total[...] = piece

    @pl.when(block > 0)
    def _():
        total[...] += piece

    @pl.when(block == pl.num_programs(0) - 1)
    def _():
        def finish(index, at, carry):
            residual = tokens_ref[at, :].astype(jnp.float32)
            scale = lax.rsqrt(jnp.mean(residual * residual, axis=1, keepdims=True) + epsilon)
            grad_normed = total[at, :]
            weighted = grad_normed * gain_ref[...]
            inner = jnp.mean(weighted * residual, axis=1, keepdims=True)
            grad_y = low_ref[at, :].astype(jnp.float32)
            result = grad_y + (scale * weighted - residual * (scale * scale * scale) * inner)
            tokens_grad_ref[at, :] = result.astype(tokens_grad_ref.dtype)
            return carry + eight(grad_normed * residual * scale)

        gains = row_loop(rows, 16, finish, jnp.zeros((8, total.shape[1]), jnp.float32))
        gain_grad_ref[...] = jnp.sum(gains, axis=0, keepdims=True)


def finish_kernel(plan, names, in_ref, out_ref, small_ref, norm_ref, *outs):
    outs[0][...] = in_ref[...]
    outs[1][...] = out_ref[...]
    for name, target in zip(names, outs[2 : 2 + len(names)]):
        first, count = plan[name]
        if len(target.shape) == 1:
            target[...] = small_ref[first, : target.shape[0]]
        else:
            target[...] = small_ref[first : first + count, :]
    for index in range(2):
        outs[2 + len(names) + index][0, 0] = jnp.sum(norm_ref[index])


def shape(dims, kind=jnp.float32):
    return jax.ShapeDtypeStruct(dims, kind)


def compute_call(kernel, name, blocks, in_specs, out_specs, out_shape, scratch, flops, operands):
    return pl.pallas_call(
        kernel,
        grid=(blocks,),
        in_specs=in_specs,
        out_specs=out_specs,
        out_shape=out_shape,
        scratch_shapes=scratch,
        compiler_params=pltpu.CompilerParams(
            dimension_semantics=("arbitrary",), vmem_limit_bytes=58 * 1024 * 1024
        ),
        cost_estimate=pl.CostEstimate(flops=flops, bytes_accessed=40 << 20, transcendentals=0),
        name=name,
    )(*operands)


def place_of(dims):
    depth, tall, wide = dims
    core = lax.axis_index("wide")
    me = lax.axis_index("narrow")
    across = lax.rem(me, wide)
    up = lax.rem(lax.div(me, wide), tall)
    deep = lax.div(me, wide * tall)
    turn = core if tall == wide else 0
    second = (1 + turn * (wide - 1), across + turn * (up - across), wide)
    third = (wide - turn * (wide - 1), up + turn * (across - up), tall)
    return core, deep, second, third


def block_at(dims, deep, second, third, d, e, f):
    depth, tall, wide = dims
    return (
        lax.rem(deep + d, depth) * (tall * wide)
        + lax.rem(second[1] + e, second[2]) * second[0]
        + lax.rem(third[1] + f, third[2]) * third[0]
    )


def greet(dims, deep, second, third, core):
    barrier = pltpu.get_barrier_semaphore()
    peers = 1
    pl.semaphore_signal(barrier, inc=1, device_id={"wide": 1 - core}, device_id_type=pl.DeviceIdType.MESH)
    for axis, size in enumerate((dims[0], second[2], third[2])):
        for hop in range(1, size):
            moves = [0, 0, 0]
            moves[axis] = hop
            target = block_at(dims, deep, second, third, *moves)
            pl.semaphore_signal(
                barrier, inc=1, device_id={"narrow": target}, device_id_type=pl.DeviceIdType.MESH
            )
            peers += 1
    pl.semaphore_wait(barrier, peers)


def half_of(width, core):
    return pl.ds(pl.multiple_of(core * (width // 2), lanes), width // 2)


def remote(source, target, send_sem, recv_sem, device):
    return pltpu.make_async_remote_copy(
        src_ref=source,
        dst_ref=target,
        send_sem=send_sem,
        recv_sem=recv_sem,
        device_id=device,
        device_id_type=pl.DeviceIdType.MESH,
    )


def side_of(block, side):
    if len(block.shape) == 3:
        return block.at[side]
    return block.at[:, half_of(block.shape[1], side)]


def gather_kernel(dims, plan, names, *refs):
    count = 3
    smalls, bigs = refs[: len(names)], refs[len(names) : len(names) + 2]
    whole = refs[len(names) + 2 : len(names) + 5]
    own = refs[len(names) + 5 : len(names) + 8]
    pack_buf, local_sem, send_sem, recv_sem, core_send, core_recv = refs[len(names) + 8 :]
    core, deep, second, third = place_of(dims)
    pack_buf[...] = jnp.zeros_like(pack_buf)
    for name, ref in zip(names, smalls):
        first, tall = plan[name]
        pack_buf[first : first + tall, : ref.shape[1]] = ref[...]
    tall = pack_buf.shape[0] // 2
    for side in range(2):
        own[0][side] = pack_buf[side * tall : (side + 1) * tall, :].astype(own[0].dtype)
    own[1][...] = bigs[0][...].astype(own[1].dtype)
    own[2][...] = bigs[1][...].astype(own[2].dtype)
    greet(dims, deep, second, third, core)
    depth, span_e, span_f = dims[0], second[2], third[2]
    other = {"wide": 1 - core}
    pending = []

    def at(d, e, f):
        return block_at(dims, deep, second, third, d, e, f)

    def slot(d, e, f):
        return (d * span_e + e) * span_f + f

    def back(size, hop):
        return (size - hop) % size

    def piece(which, number, side):
        return side_of(whole[which].at[number], side)

    def onward(which, d, e, f):
        number = at(back(depth, d), back(span_e, e), back(span_f, f))
        first = d == 0 and e == 0 and f == 0
        source = side_of(own[which], core) if first else piece(which, number, core)
        target = piece(which, number, core)

        def push(moved, index):
            copy = remote(
                source, target, send_sem.at[which, index], recv_sem.at[which, index], {"narrow": at(*moved)}
            )
            copy.start()
            pending.append(copy)

        if e == 0 and f == 0 and d == 0:
            for hop in range(1, depth):
                push((hop, 0, 0), slot(hop, 0, 0))
        if f == 0 and e == 0:
            for hop in range(1, span_e):
                push((0, hop, 0), slot(d, hop, 0))
        if f == 0:
            for hop in range(1, span_f):
                push((0, 0, hop), slot(d, e, hop))
        if not first:
            index = slot(d, e, f)
            copy = remote(source, target, core_send.at[which, index], core_recv.at[which, index], other)
            copy.start()
            pending.append(copy)

    def arrived(which, d, e, f):
        target = piece(which, at(back(depth, d), back(span_e, e), back(span_f, f)), core)
        index = slot(d, e, f)
        remote(
            target, target, send_sem.at[which, index], recv_sem.at[which, index], {"narrow": at(0, 0, 1)}
        ).wait_recv()

    locals_ = []
    for which in range(count):
        onward(which, 0, 0, 0)
    for which in range(count):
        copy = pltpu.make_async_copy(own[which], whole[which].at[at(0, 0, 0)], local_sem.at[which])
        copy.start()
        locals_.append(copy)
    for which in range(count):
        for d in range(1, depth):
            arrived(which, d, 0, 0)
            onward(which, d, 0, 0)
        for d in range(depth):
            for e in range(1, span_e):
                arrived(which, d, e, 0)
                onward(which, d, e, 0)
        for d in range(depth):
            for e in range(span_e):
                for f in range(1, span_f):
                    arrived(which, d, e, f)
                    onward(which, d, e, f)
    mirror = place_of_other(dims)
    for which in range(count):
        for d in range(depth):
            for e in range(span_e):
                for f in range(span_f):
                    if d == 0 and e == 0 and f == 0:
                        continue
                    number = block_at(
                        dims, deep, *mirror, back(depth, d), back(span_e, e), back(span_f, f)
                    )
                    target = piece(which, number, 1 - core)
                    index = slot(d, e, f)
                    remote(
                        target, target, core_send.at[which, index], core_recv.at[which, index], other
                    ).wait_recv()
    for copy in pending:
        copy.wait_send()
    for copy in locals_:
        copy.wait()


def place_of_other(dims):
    core, deep, second, third = place_of(dims)
    if dims[1] != dims[2]:
        return second, third
    return third, second


def gather_weights(dims, plan, smalls, bigs):
    number = dims[0] * dims[1] * dims[2]
    names = list(smalls)
    width = smalls["select"].shape[1]
    owned = [shape((2, plan["rows"] // 2, width), jnp.bfloat16)]
    owned += [shape(big.shape, jnp.bfloat16) for big in bigs]
    inside = pl.BlockSpec(memory_space=pltpu.VMEM)
    return pl.pallas_call(
        functools.partial(gather_kernel, dims, plan, names),
        in_specs=[inside] * (len(names) + 2),
        out_specs=[pl.BlockSpec(memory_space=pl.ANY)] * 3,
        out_shape=[shape((number,) + kind.shape, kind.dtype) for kind in owned],
        scratch_shapes=[pltpu.VMEM(kind.shape, kind.dtype) for kind in owned]
        + [
            pltpu.VMEM((plan["rows"], width), jnp.float32),
            pltpu.SemaphoreType.DMA((3,)),
            pltpu.SemaphoreType.DMA((3, number)),
            pltpu.SemaphoreType.DMA((3, number)),
            pltpu.SemaphoreType.DMA((3, number)),
            pltpu.SemaphoreType.DMA((3, number)),
        ],
        compiler_params=pltpu.CompilerParams(
            collective_id=0, has_side_effects=True, vmem_limit_bytes=60 * 1024 * 1024
        ),
        name="gather_weights",
    )(*smalls.values(), *bigs)


def reduce_kernel(dims, count, places, plain_at, *refs):
    grads, plain_ref = refs[:count], refs[count]
    results = 1 + max(place[0] for place in places)
    sums, norms = refs[count + 1 : count + 1 + results], refs[count + 1 + results]
    held = refs[count + 2 + results :]
    mine, swapped, third_in, second_in, first_in = (
        held[index * count : (index + 1) * count] for index in range(5)
    )
    (norm_core, norm_deep, norm_wide, norm_tall) = held[5 * count : 5 * count + 4]
    (
        local_sem,
        core_send,
        core_recv,
        leg_send,
        leg_recv,
        last_send,
        last_recv,
        norm_send,
        norm_recv,
    ) = held[5 * count + 4 :]
    core, deep, second, third = place_of(dims)
    greet(dims, deep, second, third, core)
    depth, span_e, span_f = dims[0], second[2], third[2]
    other = {"wide": 1 - core}
    mirror = place_of_other(dims)
    pending = []

    def at(d, e, f):
        return block_at(dims, deep, second, third, d, e, f)

    def slot(d, e, f):
        return (d * span_e + e) * span_f + f

    def share(which, side):
        result, first = places[which]
        if len(grads[which].shape) == 4:
            return sums[result].at[side]
        width = grads[which].shape[2]
        columns = pl.ds(pl.multiple_of(first + side * (width // 2), lanes), width // 2)
        return sums[result].at[:, columns]

    far_first = sorted(
        ((d, e, f) for d in range(depth) for e in range(span_e) for f in range(span_f)),
        key=lambda item: (item[2] == 0, item[1] == 0, item[0] == 0),
    )
    loads = {}
    for move in far_first:
        for which in range(count):
            number = block_at(dims, deep, *mirror, *move)
            copy = remote(
                side_of(grads[which].at[number], 1 - core),
                swapped[which].at[slot(*move)],
                core_send.at[which, slot(*move)],
                core_recv.at[which, slot(*move)],
                other,
            )
            copy.start()
            pending.append(copy)
            load = pltpu.make_async_copy(
                side_of(grads[which].at[at(*move)], core),
                mine[which].at[slot(*move)],
                local_sem.at[which, slot(*move)],
            )
            load.start()
            loads[which, move] = load

    def added(which, place, parts, store):
        rows = mine[which].shape[1]
        group = min(rows, 16)

        def some(index, carry):
            at_rows = pl.ds(pl.multiple_of(index * group, group), group)
            total = mine[which][place, at_rows, :].astype(jnp.float32)
            for ref, spot in parts:
                total = total + ref[spot, at_rows, :].astype(jnp.float32)
            return store(at_rows, total, carry)

        return functools.partial(lax.fori_loop, 0, rows // group, some)

    def wait_leg(which, index, ref, spot):
        remote(
            ref.at[spot], ref.at[spot], leg_send.at[which, index], leg_recv.at[which, index], other
        ).wait_recv()

    def collect(which, move):
        d, e, f = move
        place = slot(*move)
        loads[which, move].wait()
        remote(
            swapped[which].at[place],
            swapped[which].at[place],
            core_send.at[which, place],
            core_recv.at[which, place],
            other,
        ).wait_recv()
        parts = [(swapped[which], place)]
        if f == 0:
            for hop in range(1, span_f):
                spot = (d * span_e + e) * (span_f - 1) + hop - 1
                wait_leg(which, slot(d, e, hop), third_in[which], spot)
                parts.append((third_in[which], spot))
        if f == 0 and e == 0:
            for hop in range(1, span_e):
                spot = d * (span_e - 1) + hop - 1
                wait_leg(which, slot(d, hop, 0), second_in[which], spot)
                parts.append((second_in[which], spot))
        if f == 0 and e == 0 and d == 0:
            for hop in range(1, depth):
                wait_leg(which, slot(hop, 0, 0), first_in[which], hop - 1)
                parts.append((first_in[which], hop - 1))
        return place, parts

    for move in far_first[:-1]:
        d, e, f = move
        for which in range(count):
            place, parts = collect(which, move)

            def keep(at_rows, total, carry, which=which, place=place):
                mine[which][place, at_rows, :] = total.astype(mine[which].dtype)
                return carry

            added(which, place, parts, keep)(0)
            if f > 0:
                target, spot, moved = third_in[which], (d * span_e + e) * (span_f - 1) + f - 1, (0, 0, f)
            elif e > 0:
                target, spot, moved = second_in[which], d * (span_e - 1) + e - 1, (0, e, 0)
            else:
                target, spot, moved = first_in[which], d - 1, (d, 0, 0)
            copy = remote(
                mine[which].at[place],
                target.at[spot],
                leg_send.at[which, place],
                leg_recv.at[which, place],
                {"narrow": at(*moved)},
            )
            copy.start()
            pending.append(copy)

    squares = [jnp.zeros((8, lanes), jnp.float32), jnp.zeros((8, lanes), jnp.float32)]
    for which in range(count):
        place, parts = collect(which, (0, 0, 0))
        result = share(which, core)

        def finish(at_rows, total, carry, which=which, result=result):
            result[at_rows, :] = total
            kept, plain = carry
            squared = total * total
            if which == plain_at:
                marked = squared * plain_ref[core, at_rows, :]
                plain = plain + folded_squares(marked)
                squared = squared - marked
            return (kept + folded_squares(squared), plain)

        squares = added(which, place, parts, finish)(tuple(squares))
        copy = remote(result, result, last_send.at[which], last_recv.at[which], other)
        copy.start()
        pending.append(copy)

    running = jnp.stack(list(squares))
    me = lax.axis_index("narrow")
    tall, wide = dims[1], dims[2]
    my_wide = lax.rem(me, wide)
    my_tall = lax.rem(lax.div(me, wide), tall)
    plane = tall * wide
    index = 0
    stages = (
        (norm_core, 2, core, lambda spot: {"wide": spot}),
        (norm_deep, depth, deep, lambda spot: {"narrow": spot * plane + lax.rem(me, plane)}),
        (norm_wide, wide, my_wide, lambda spot: {"narrow": me - my_wide + spot}),
        (norm_tall, tall, my_tall, lambda spot: {"narrow": me + (spot - my_tall) * wide}),
    )
    for buffer, size, mine_at, device in stages:
        buffer[mine_at] = running
        for hop in range(1, size):
            copy = remote(
                buffer.at[mine_at],
                buffer.at[mine_at],
                norm_send.at[index],
                norm_recv.at[index],
                device(lax.rem(mine_at + hop, size)),
            )
            copy.start()
            pending.append(copy)
            index += 1
        index -= size - 1
        for hop in range(1, size):
            came = lax.rem(mine_at + size - hop, size)
            remote(
                buffer.at[came], buffer.at[came], norm_send.at[index], norm_recv.at[index], device(came)
            ).wait_recv()
            index += 1
        running = buffer[0]
        for spot in range(1, size):
            running = running + buffer[spot]
    norms[...] = running
    for which in range(count):
        result = share(which, 1 - core)
        remote(result, result, last_send.at[which], last_recv.at[which], other).wait_recv()
    for copy in pending:
        copy.wait_send()


def folded_squares(values):
    total = None
    if values.shape[1] < lanes:
        first = lax.broadcasted_iota(jnp.int32, (values.shape[0], lanes), 1) == 0
        values = jnp.where(first, jnp.sum(values, axis=1, keepdims=True), 0.0)
    for row in range(0, values.shape[0], 8):
        for column in range(0, values.shape[1], lanes):
            piece = values[row : row + 8, column : column + lanes]
            total = piece if total is None else total + piece
    return total


def reduce_grads(dims, grads, places, plain_mask, plain_at):
    number = dims[0] * dims[1] * dims[2]
    depth, tall, wide = dims
    count = len(grads)
    anywhere = pl.BlockSpec(memory_space=pl.ANY)
    inside = pl.BlockSpec(memory_space=pltpu.VMEM)

    def room(places):
        return [
            pltpu.VMEM(
                (places,) + (grad.shape[2:] if grad.ndim == 4 else (grad.shape[1], grad.shape[2] // 2)),
                grad.dtype,
            )
            for grad in grads
        ]

    third, second = (tall, wide)
    results = 1 + max(place[0] for place in places)
    sums = []
    for index in range(results):
        members = [grad for grad, place in zip(grads, places) if place[0] == index]
        if members[0].ndim == 4:
            sums.append(shape(members[0].shape[1:]))
        else:
            sums.append(shape((members[0].shape[1], sum(grad.shape[2] for grad in members))))
    result = pl.pallas_call(
        functools.partial(reduce_kernel, dims, count, places, plain_at),
        in_specs=[anywhere] * count + [inside],
        out_specs=[inside] * (results + 1),
        out_shape=sums + [shape((2, 8, lanes))],
        scratch_shapes=room(number)
        + room(number)
        + room(depth * second * (third - 1))
        + room(depth * (second - 1))
        + room(depth - 1)
        + [pltpu.VMEM((size, 2, 8, lanes), jnp.float32) for size in (2, depth, wide, tall)]
        + [
            pltpu.SemaphoreType.DMA((count, number)),
            pltpu.SemaphoreType.DMA((count, number)),
            pltpu.SemaphoreType.DMA((count, number)),
            pltpu.SemaphoreType.DMA((count, number)),
            pltpu.SemaphoreType.DMA((count, number)),
            pltpu.SemaphoreType.DMA((count,)),
            pltpu.SemaphoreType.DMA((count,)),
            pltpu.SemaphoreType.DMA((depth + tall + wide,)),
            pltpu.SemaphoreType.DMA((depth + tall + wide,)),
        ],
        compiler_params=pltpu.CompilerParams(
            collective_id=1, has_side_effects=True, vmem_limit_bytes=56 * 1024 * 1024
        ),
        name="reduce_grads",
    )(*grads, plain_mask)
    return result[:results], result[results]


def grid_of(mesh):
    number = mesh.shape["narrow"]
    places = [getattr(device, "coords", None) for device in mesh.devices[0]]
    if all(place is not None for place in places):
        sizes = [len({place[axis] for place in places}) for axis in (2, 1, 0)]
        if sizes[0] * sizes[1] * sizes[2] == number:
            return tuple(sizes)
    side = round((number / 2) ** (1 / 3))
    return (2 * side, side, side) if 2 * side**3 == number else (number, 1, 1)


def plan_of(select_rows, state_size, tap_count, step_rows):
    plan, first = {}, 0
    for name, tall in (
        ("select", select_rows),
        ("decay", state_size),
        ("taps", tap_count),
        ("shift", 1),
        ("bias", 1),
        ("skip", 1),
        ("gain", 1),
    ):
        plan[name] = (first, tall)
        first += tall
    plan["step"] = (lanes, step_rows)
    plan["rows"] = -(-(lanes + step_rows) // 32) * 32
    return plan


def per_device(
    dims,
    tokens,
    cotangent,
    loss_mask,
    seq_lengths,
    norm_gain,
    in_proj,
    conv_weight,
    conv_bias,
    select_proj,
    step_proj,
    step_bias,
    decay_log,
    skip_scale,
    out_proj,
):
    half = jnp.bfloat16
    piece = skip_scale.shape[0]
    gain_piece = norm_gain.shape[0]
    rank, size = step_proj.shape[0], decay_log.shape[0]
    plan = plan_of(select_proj.shape[0], size, conv_weight.shape[0], rank)
    small_blocks, in_blocks, out_blocks = gather_weights(
        dims,
        plan,
        {
            "select": select_proj,
            "decay": decay_log,
            "taps": conv_weight,
            "shift": conv_bias[None],
            "bias": step_bias[None],
            "skip": skip_scale[None],
            "gain": norm_gain[None],
            "step": step_proj,
        },
        [in_proj, out_proj],
    )
    in_whole = in_blocks.reshape(-1, in_blocks.shape[2])
    out_whole = out_blocks.reshape(-1, out_blocks.shape[2])
    small_blocks = small_blocks.reshape(-1, plan["rows"], piece)
    small = jnp.swapaxes(small_blocks, 0, 1).reshape(plan["rows"], -1)
    gain_value = small_blocks[:, plan["gain"][0], :gain_piece].reshape(1, -1).astype(jnp.float32)

    rows, model = tokens.shape
    inner = small.shape[1]
    width = 4 * lanes
    blocks = inner // width
    chunks = rows // chunk
    mask_row = loss_mask[None]

    whole = pl.BlockSpec(memory_space=pltpu.VMEM)
    tall = pl.BlockSpec((rows, width), lambda b: (0, b))
    deep = pl.BlockSpec((chunks, chunk, width), lambda b: (0, 0, b))
    lead = pl.BlockSpec((rows, size, width), lambda b: (0, 0, b))
    first_w = pl.BlockSpec((model, width), lambda b: (0, b))
    second_w = pl.BlockSpec((model, width), lambda b: (0, b + blocks))
    out_w = pl.BlockSpec((width, model), lambda b: (b, 0))

    def thin(height):
        return pl.BlockSpec((height, width), lambda b: (0, b))

    def fixed(*dims_of):
        return pl.BlockSpec(dims_of, lambda b: (0,) * len(dims_of))

    scalars = pl.BlockSpec(memory_space=pltpu.SMEM)
    offset_buf = pltpu.VMEM((rows + 8, lanes), jnp.int32)
    packed = thin(plan["rows"])

    branch, gate_pre, signal, projected, flipped, grad_low = compute_call(
        functools.partial(front_kernel, plan),
        "front",
        blocks,
        [scalars, whole, whole, whole, whole, packed, first_w, second_w],
        [tall, tall, tall, fixed(rows, lanes), fixed(model, rows), fixed(rows, model)],
        [
            shape((rows, inner)),
            shape((rows, inner)),
            shape((rows, inner), half),
            shape((rows, lanes)),
            shape((model, rows), half),
            shape((rows, model), half),
        ],
        [pltpu.VMEM((rows, model), half), offset_buf],
        4 * rows * model * inner,
        (seq_lengths, tokens, cotangent, mask_row, gain_value, small, in_whole, in_whole),
    )
    write_rows = projected[:, rank : rank + size]
    read_rows = projected[:, rank + size : rank + 2 * size]
    wide_write = jnp.broadcast_to(write_rows[:, :, None], (rows, size, lanes))
    wide_read = jnp.broadcast_to(read_rows[:, :, None], (rows, size, lanes))
    row_block = pltpu.VMEM((chunks, chunk, width), jnp.float32)
    spare_block = pltpu.VMEM((chunks + 1, chunk, width), jnp.float32)
    states, step, core_grad, gate_grad, grad_skip, grad_outw, grad_in_gate, output = compute_call(
        functools.partial(forward_kernel, plan),
        "forward",
        blocks,
        [scalars, whole, packed, tall, whole, whole, tall, whole, out_w, whole, whole],
        [lead, deep, deep, tall, thin(1), out_w, first_w, fixed(rows, model)],
        [
            shape((rows, size, inner), half),
            shape((chunks, chunk, inner)),
            shape((chunks, chunk, inner)),
            shape((rows, inner), half),
            shape((1, inner)),
            shape((inner, model), half),
            shape((model, inner), half),
            shape((rows, model), half),
        ],
        [
            offset_buf,
            pltpu.VMEM((rows, width), jnp.float32),
            row_block,
            row_block,
            row_block,
            pltpu.VMEM((width // lanes, chunk * chunk, lanes), jnp.float32),
            pltpu.VMEM((rows, width), half),
            pltpu.VMEM((rows, model), jnp.float32),
        ],
        15 * rows * inner * size,
        (
            seq_lengths,
            projected,
            small,
            signal,
            wide_write,
            wide_read,
            gate_pre,
            grad_low,
            out_whole,
            flipped,
            tokens,
        ),
    )
    pairs = (chunks + 1, size, 2 * chunk)
    fold_buf = pltpu.VMEM((2, width // lanes, chunk * chunk, lanes), jnp.float32)
    signal_grad, grad_stepw, grad_bias, grad_decaylog, grad_rank, grad_write, grad_read = compute_call(
        functools.partial(backward_kernel, plan),
        "backward",
        blocks,
        [scalars, whole, packed, tall, whole, whole, deep, deep, lead],
        [tall, thin(rank), thin(1), thin(size), fixed(rows, rank), fixed(*pairs), fixed(*pairs)],
        [
            shape((rows, inner)),
            shape((rank, inner)),
            shape((1, inner)),
            shape((size, inner)),
            shape((rows, rank)),
            shape(pairs),
            shape(pairs),
        ],
        [
            offset_buf,
            row_block,
            row_block,
            pltpu.VMEM((chunks + 1, 2 * chunk, width), half),
            pltpu.VMEM((chunks, 2 * chunk, width), half),
            fold_buf,
            fold_buf,
            pltpu.VMEM((2, chunk * size, width), half),
            spare_block,
            spare_block,
            pltpu.VMEM((rows, width), half),
        ],
        40 * rows * inner * size,
        (seq_lengths, projected, small, signal, wide_write, wide_read, step, core_grad, states),
    )

    def by_token(pairs):
        summed = pairs[:chunks, :, :chunk] + pairs[:chunks, :, chunk:]
        return jnp.swapaxes(summed, 1, 2).reshape(rows, size)

    flat = jnp.concatenate(
        [
            grad_rank,
            by_token(grad_write),
            by_token(grad_read),
            jnp.zeros((rows, lanes - rank - 2 * size), jnp.float32),
        ],
        axis=1,
    ).astype(half)
    small_grad, grad_in_branch, grad_gain, grad_tokens = compute_call(
        functools.partial(back_kernel, plan),
        "back",
        blocks,
        [scalars, whole, whole, whole, packed, whole, tall, tall, tall, tall, whole, first_w, second_w]
        + [thin(rank), thin(1), thin(size), thin(1)],
        [packed, first_w, fixed(1, model), fixed(rows, model)],
        [
            shape((plan["rows"], inner)),
            shape((model, inner), half),
            shape((1, model)),
            shape((rows, model), half),
        ],
        [
            offset_buf,
            pltpu.VMEM((rows + 8, width), jnp.float32),
            pltpu.VMEM((rows, width), half),
            pltpu.VMEM((rows, model), jnp.float32),
        ],
        8 * rows * model * inner,
        (
            seq_lengths,
            tokens,
            grad_low,
            gain_value,
            small,
            flat,
            branch,
            signal,
            signal_grad,
            gate_grad,
            flipped,
            in_whole,
            in_whole,
            grad_stepw,
            grad_bias,
            grad_decaylog,
            grad_skip,
        ),
    )

    number = small_blocks.shape[0]
    gain_rows = jnp.pad(grad_gain.reshape(number, 1, gain_piece), ((0, 0), (0, 0), (0, piece - gain_piece)))
    place = plan["gain"][0]
    small_grad = jnp.swapaxes(small_grad.reshape(plan["rows"], number, piece), 0, 1) + jnp.pad(
        gain_rows, ((0, 0), (place, plan["rows"] - place - 1), (0, 0))
    )
    split = in_blocks.shape[:2] + (inner,)
    plain_rows = np.zeros((plan["rows"], piece), np.float32)
    for name in ("bias", "decay", "skip"):
        first, count = plan[name]
        plain_rows[first : first + count] = 1.0
    halves = (2, plan["rows"] // 2, piece)
    (in_sum, out_sum, small_sum), norms = reduce_grads(
        dims,
        [
            grad_in_branch.reshape(split),
            grad_in_gate.reshape(split),
            grad_outw.reshape(out_blocks.shape),
            small_grad.astype(half).reshape((number,) + halves),
        ],
        [(0, 0), (0, inner), (1, 0), (2, 0)],
        jnp.asarray(plain_rows.reshape(halves)),
        3,
    )
    names = ("gain", "taps", "shift", "select", "step", "bias", "decay", "skip")
    own = (norm_gain, conv_weight, conv_bias, select_proj, step_proj, step_bias, decay_log, skip_scale)
    in_grad, out_grad, gain_grad, *small_grads, decay_sq, plain_sq = pl.pallas_call(
        functools.partial(finish_kernel, plan, names),
        in_specs=[whole] * 4,
        out_specs=[whole] * (2 + len(names)) + [scalars] * 2,
        out_shape=[shape(in_sum.shape), shape(out_sum.shape)]
        + [shape(array.shape) for array in own]
        + [shape((1, 1))] * 2,
        name="finish",
    )(in_sum, out_sum, small_sum.reshape(plan["rows"], piece), norms)
    return (
        output,
        grad_tokens,
        gain_grad,
        in_grad,
        *small_grads,
        out_grad,
        decay_sq[0, 0],
        plain_sq[0, 0],
    )


def solution(mesh):
    placed = (
        P(("wide", "narrow"), None),
        P(("wide", "narrow"), None),
        P(("wide", "narrow")),
        P(("wide", "narrow"), None),
        P("narrow"),
        P("narrow", None),
        P(None, "narrow"),
        P("narrow"),
        P(None, "narrow"),
        P(None, "narrow"),
        P("narrow"),
        P(None, "narrow"),
        P("narrow"),
        P("narrow", None),
    )
    return jax.shard_map(
        functools.partial(per_device, grid_of(mesh)),
        mesh=mesh,
        in_specs=placed,
        out_specs=(
            P(("wide", "narrow"), None),
            P(("wide", "narrow"), None),
            P("narrow"),
            P("narrow", None),
            P(None, "narrow"),
            P("narrow"),
            P(None, "narrow"),
            P(None, "narrow"),
            P("narrow"),
            P(None, "narrow"),
            P("narrow"),
            P("narrow", None),
            P(),
            P(),
        ),
        check_vma=False,
    )
```

```python
import functools
import math

import jax
import jax.numpy as jnp
import numpy as np
from jax import lax
from jax.experimental import pallas as pl
from jax.experimental.pallas import tpu as pltpu
from jax.sharding import PartitionSpec as P

epsilon = 1e-05
chunk = 8
lanes = 128
log2e = math.log2(math.e)
ln2 = math.log(2.0)
far = 1e30


def contract(left, right, left_dim, right_dim):
    return lax.dot_general(
        left, right, (((left_dim,), (right_dim,)), ((), ())), preferred_element_type=jnp.float32
    )


def row_loop(rows, group, body, initial):
    def some(index, carry):
        return body(index, pl.ds(pl.multiple_of(index * group, group), group), carry)

    return lax.fori_loop(0, rows // group, some, initial)


def cut(tile):
    return pl.ds(tile * lanes, lanes)


def sigmoid(values):
    return 0.5 * jnp.tanh(0.5 * values) + 0.5


def softplus(values):
    small = jnp.exp(-jnp.abs(values))
    series = small * (1.0 - small * (0.5 - small * (1.0 / 3.0 - 0.25 * small)))
    return jnp.maximum(values, 0.0) + jnp.where(small < 0.03, series, jnp.log(1.0 + small))


def slope_of(step):
    series = step * (1.0 - step * (0.5 - step * (1.0 / 6.0 - step * (1.0 / 24.0))))
    return jnp.where(step < 0.03, series, 1.0 - jnp.exp(-step))


def fill_offsets(lengths_ref, offset_buf, rows):
    place = lax.broadcasted_iota(jnp.int32, offset_buf.shape, 0)
    start = jnp.zeros(offset_buf.shape, jnp.int32)
    ahead = jnp.int32(0)
    for index in range(lengths_ref.shape[1] - 1):
        ahead = ahead + lengths_ref[0, index]
        start = jnp.where(place >= ahead, ahead, start)
    offset_buf[...] = jnp.where(place < rows, place - start, 0)


def small_rows(small_ref, first, count):
    base = first // 16 * 16
    tall = -(-(first + count - base) // 16) * 16
    return small_ref[base : base + tall, :].astype(jnp.float32)[first - base : first - base + count]


def eight(values):
    total = values[:8]
    for row in range(8, values.shape[0], 8):
        total = total + values[row : row + 8]
    return total


def conv_rows(index, at, group, tile, branch_ref, offset_buf, taps, shift):
    count = taps.shape[0]
    here = slice(tile * lanes, (tile + 1) * lanes)
    current = branch_ref[at, cut(tile)]
    before = branch_ref[pl.ds(pl.multiple_of(jnp.maximum(index * group - 8, 0), 8), 8), cut(tile)]
    both = jnp.concatenate([before, current], axis=0)
    offsets = offset_buf[at, :]
    summed = shift[:, here] + taps[count - 1 : count, here] * current
    reads = [None] * count
    reads[count - 1] = current
    for tap in range(count - 1):
        lag = count - 1 - tap
        reads[tap] = jnp.where(offsets >= lag, pltpu.roll(both, lag, 0)[8:], 0.0)
        summed = summed + taps[tap : tap + 1, here] * reads[tap]
    return summed, reads


def front_kernel(
    plan,
    lengths_ref,
    tokens_ref,
    cotangent_ref,
    mask_ref,
    gain_ref,
    small_ref,
    branch_w,
    gate_w,
    branch_ref,
    gate_ref,
    signal_ref,
    projected_ref,
    flipped_ref,
    low_ref,
    normed_buf,
    offset_buf,
):
    rows = tokens_ref.shape[0]
    width = branch_ref.shape[1]
    block = pl.program_id(0)

    @pl.when(block == 0)
    def _():
        fill_offsets(lengths_ref, offset_buf, rows)

        def norm(index, at, carry):
            residual = tokens_ref[at, :].astype(jnp.float32)
            scale = lax.rsqrt(jnp.mean(residual * residual, axis=1, keepdims=True) + epsilon)
            normed_buf[at, :] = (residual * scale * gain_ref[...]).astype(normed_buf.dtype)
            return carry

        row_loop(rows, 16, norm, 0)
        flipped_ref[...] = normed_buf[...].T
        projected_ref[...] = jnp.zeros_like(projected_ref)
        down = lax.broadcasted_iota(jnp.int32, (rows, rows), 0)
        along = lax.broadcasted_iota(jnp.int32, (rows, rows), 1)
        diagonal = jnp.where(down == along, mask_ref[...].astype(jnp.float32), 0.0).astype(low_ref.dtype)
        low_ref[...] = jnp.dot(
            diagonal, cotangent_ref[...], preferred_element_type=jnp.float32
        ).astype(low_ref.dtype)

    branch_ref[...] = jnp.dot(normed_buf[...], branch_w[...], preferred_element_type=jnp.float32)
    gate_ref[...] = jnp.dot(normed_buf[...], gate_w[...], preferred_element_type=jnp.float32)
    taps = small_rows(small_ref, *plan["taps"])
    shift = small_rows(small_ref, *plan["shift"])

    def some(index, at, carry):
        for tile in range(width // lanes):
            summed, _ = conv_rows(index, at, 32, tile, branch_ref, offset_buf, taps, shift)
            signal_ref[at, cut(tile)] = (summed * sigmoid(summed)).astype(signal_ref.dtype)
        return carry

    row_loop(rows, 32, some, 0)
    projected_ref[...] += contract(signal_ref[...], small_ref[:lanes, :], 1, 1)


def folded(buffer, tile):
    total = buffer[tile, pl.ds(0, chunk, stride=chunk), :]
    for row in range(1, chunk):
        total = total + buffer[tile, pl.ds(row, chunk, stride=chunk), :]
    return total


def forward_kernel(
    plan,
    dims,
    lengths_ref,
    projected_ref,
    small_ref,
    signal_ref,
    write_ref,
    read_ref,
    own_ref,
    states_ref,
    step_ref,
    core_ref,
    whole_ref,
    offset_buf,
    pre_buf,
    decay_step,
    inflow,
    fold_buf,
    low_buf,
    *sems,
):
    rows, width = pre_buf.shape
    size = write_ref.shape[1]
    half = size // 2
    tiles = width // lanes
    rank = plan["step"][1]
    block = pl.program_id(0)
    gather = Gather(dims, [low_buf], [whole_ref], sems)

    @pl.when(block == 0)
    def _():
        low_buf[...] = own_ref[...].astype(low_buf.dtype)
        gather.start()
        fill_offsets(lengths_ref, offset_buf, rows)

    for number in (1, 2, 3):

        @pl.when(block == number)
        def _(number=number):
            gather.leg(number)

    pre_buf[...] = jnp.dot(
        projected_ref[:, :rank].astype(small_ref.dtype),
        small_ref[pl.ds(plan["step"][0], rank), :],
        preferred_element_type=jnp.float32,
    )
    bias = small_rows(small_ref, *plan["bias"])

    def before(index, at, carry):
        spot = pl.ds(pl.multiple_of(index * 4, 4), 4)
        inside = offset_buf[at, :] > 0
        for tile in range(tiles):
            step = softplus(pre_buf[at, cut(tile)] + bias[:, tile * lanes : (tile + 1) * lanes])
            step_ref[spot, :, cut(tile)] = step.reshape(4, chunk, lanes)
            decay_step[spot, :, cut(tile)] = jnp.where(inside, step, far).reshape(4, chunk, lanes)
            flow = step * signal_ref[at, cut(tile)].astype(jnp.float32)
            inflow[spot, :, cut(tile)] = flow.reshape(4, chunk, lanes)
        return carry

    row_loop(rows, 4 * chunk, before, 0)
    rates = -jnp.exp(small_rows(small_ref, *plan["decay"])) * log2e
    rates = [rates[:, tile * lanes : (tile + 1) * lanes] for tile in range(tiles)]

    def forward(index, held):
        held = list(held)
        for place in range(chunk):
            now = index * chunk + place
            write_now = write_ref[now]
            read_now = read_ref[now]
            for tile in range(tiles):
                decay = jnp.exp2(rates[tile] * decay_step[index, pl.ds(place, 1), cut(tile)])
                fresh = decay * held[tile] + write_now * inflow[index, pl.ds(place, 1), cut(tile)]
                held[tile] = fresh
                states_ref[now, :, cut(tile)] = fresh.astype(states_ref.dtype)
                product = read_now * fresh
                fold_buf[tile, pl.ds(place * chunk, chunk), :] = product[:half] + product[half:]
        for tile in range(tiles):
            core_ref[index, :, cut(tile)] = folded(fold_buf, tile)
        return tuple(held)

    zero_tile = jnp.zeros((size, lanes), jnp.float32)
    lax.fori_loop(0, rows // chunk, forward, (zero_tile,) * tiles)

    @pl.when(block == pl.num_programs(0) - 1)
    def _():
        gather.finish()


def middle_kernel(
    plan,
    core_ref,
    small_ref,
    signal_ref,
    gate_ref,
    low_ref,
    out_w,
    flipped_ref,
    tokens_ref,
    core_grad_ref,
    gate_grad_ref,
    skip_grad_ref,
    out_grad_ref,
    in_grad_ref,
    output_ref,
    pre_buf,
    gated_buf,
    total,
):
    rows, width = pre_buf.shape
    tiles = width // lanes
    block = pl.program_id(0)
    pre_buf[...] = contract(low_ref[...], out_w[...], 1, 1)
    skip = small_rows(small_ref, *plan["skip"])

    def after(index, at, carry):
        spot = pl.ds(pl.multiple_of(index * 4, 4), 4)
        sums = []
        for tile in range(tiles):
            signal = signal_ref[at, cut(tile)].astype(jnp.float32)
            core = core_ref[spot, :, cut(tile)].reshape(4 * chunk, lanes)
            core = core + skip[:, tile * lanes : (tile + 1) * lanes] * signal
            gate = gate_ref[at, cut(tile)]
            sigma = sigmoid(gate)
            active = gate * sigma
            gated_buf[at, cut(tile)] = (core * active).astype(gated_buf.dtype)
            grad_gated = pre_buf[at, cut(tile)]
            grad_core = grad_gated * active
            core_grad_ref[spot, :, cut(tile)] = grad_core.reshape(4, chunk, lanes)
            slope = sigma + active * (1.0 - sigma)
            gate_grad_ref[at, cut(tile)] = (grad_gated * core * slope).astype(gate_grad_ref.dtype)
            sums.append(carry[tile] + eight(grad_core * signal))
        return tuple(sums)

    zero_rows = jnp.zeros((8, lanes), jnp.float32)
    skips = row_loop(rows, 4 * chunk, after, (zero_rows,) * tiles)
    for tile in range(tiles):
        skip_grad_ref[:, cut(tile)] = jnp.sum(skips[tile], axis=0, keepdims=True)
    out_grad_ref[...] = contract(gated_buf[...], low_ref[...], 0, 0).astype(out_grad_ref.dtype)
    in_grad_ref[...] = jnp.dot(
        flipped_ref[...], gate_grad_ref[...], preferred_element_type=jnp.float32
    ).astype(in_grad_ref.dtype)
    piece = jnp.dot(gated_buf[...], out_w[...], preferred_element_type=jnp.float32)

    @pl.when(block == 0)
    def _():
        total[...] = piece

    @pl.when(block > 0)
    def _():
        total[...] += piece

    @pl.when(block == pl.num_programs(0) - 1)
    def _():
        output_ref[...] = (tokens_ref[...].astype(jnp.float32) + total[...]).astype(output_ref.dtype)


def backward_kernel(
    plan,
    dims,
    lengths_ref,
    projected_ref,
    small_ref,
    signal_ref,
    write_ref,
    read_ref,
    step_ref,
    core_grad_ref,
    states_ref,
    out_grad_ref,
    in_grad_ref,
    signal_grad_ref,
    step_w_grad_ref,
    bias_grad_ref,
    decay_grad_ref,
    rank_ref,
    write_grad_ref,
    read_grad_ref,
    out_sum_ref,
    in_sum_ref,
    square_ref,
    offset_buf,
    decay_step,
    inflow,
    flow_pair,
    grad_pair,
    first_buf,
    second_buf,
    grad_rows,
    through_buf,
    scaled_buf,
    low_buf,
    *parts,
):
    rows, width = low_buf.shape
    rank = plan["step"][1]
    size = write_ref.shape[1]
    half = size // 2
    tiles = width // lanes
    chunks = rows // chunk
    block = pl.program_id(0)

    def paired(values):
        high = values.astype(jnp.bfloat16).astype(jnp.float32)
        return jnp.concatenate([high, values - high], axis=0).astype(jnp.bfloat16)

    reduce = Reduce(
        dims,
        [out_grad_ref, in_grad_ref],
        parts[2:12],
        parts[12:],
        parts[:2],
        [(0, 0), (1, 0)],
    )

    @pl.when(block == 0)
    def _():
        reduce.start()
        fill_offsets(lengths_ref, offset_buf, rows)
        write_grad_ref[...] = jnp.zeros_like(write_grad_ref)
        read_grad_ref[...] = jnp.zeros_like(read_grad_ref)
        rank_ref[...] = jnp.zeros_like(rank_ref)

    def before(index, at, carry):
        spot = pl.ds(pl.multiple_of(index * 4, 4), 4)
        inside = (offset_buf[at, :] > 0).reshape(4, chunk, lanes)
        for tile in range(tiles):
            step = step_ref[spot, :, cut(tile)]
            decay_step[spot, :, cut(tile)] = jnp.where(inside, step, far)
            signal = signal_ref[at, cut(tile)].astype(jnp.float32).reshape(4, chunk, lanes)
            flow = step * signal
            inflow[spot, :, cut(tile)] = flow
            for part in range(4):
                here = index * 4 + part
                flow_pair[here, :, cut(tile)] = paired(flow[part])
                grad_pair[here, :, cut(tile)] = paired(core_grad_ref[here, :, cut(tile)])
        return carry

    row_loop(rows, 4 * chunk, before, 0)
    flow_pair[chunks] = jnp.zeros_like(flow_pair[chunks])
    grad_rows[...] = jnp.zeros_like(grad_rows)
    first_buf[...] = jnp.zeros_like(first_buf)
    second_buf[...] = jnp.zeros_like(second_buf)
    rates = -jnp.exp(small_rows(small_ref, *plan["decay"])) * log2e
    rates = [rates[:, tile * lanes : (tile + 1) * lanes] for tile in range(tiles)]

    token_of = lax.rem(lax.broadcasted_iota(jnp.int32, (size, 2 * chunk), 1), chunk)

    def own_token(products):
        kept = None
        for place in range(chunk):
            piece = products[place * size : (place + 1) * size]
            kept = piece if kept is None else jnp.where(token_of == place, piece, kept)
        return kept

    def settle(index, slot):
        for tile in range(tiles):
            through_buf[index, :, cut(tile)] = folded(first_buf.at[slot], tile)
            scaled_buf[index, :, cut(tile)] = folded(second_buf.at[slot], tile)
        write_grad_ref[index] += own_token(contract(grad_rows[slot], flow_pair[index], 1, 1))

    def backward(position, carried):
        index = chunks - 1 - position
        slot = lax.rem(position, 2)
        settle(index + 1, 1 - slot)
        base = index * chunk
        here = states_ref[pl.ds(base, chunk)].reshape(chunk * size, width)
        read_grad_ref[index] += own_token(contract(here, grad_pair[index], 1, 1))
        incoming, decay_sums = list(carried[0]), list(carried[1])
        for place in range(chunk - 1, -1, -1):
            now = base + place
            earlier = jnp.maximum(now - 1, 0) if place == 0 else now - 1
            write_now = write_ref[now]
            read_now = read_ref[now]
            for tile in range(tiles):
                step_now = decay_step[index, pl.ds(place, 1), cut(tile)]
                grad_state = incoming[tile] + read_now * core_grad_ref[index, pl.ds(place, 1), cut(tile)]
                grad_rows[slot, pl.ds(place * size, size), cut(tile)] = grad_state.astype(grad_rows.dtype)
                passed = grad_state * write_now
                first_buf[slot, tile, pl.ds(place * chunk, chunk), :] = passed[:half] + passed[half:]
                leaving = jnp.exp2(rates[tile] * step_now) * grad_state
                incoming[tile] = leaving
                weighted = leaving * states_ref[earlier, :, cut(tile)].astype(jnp.float32)
                scaled = weighted * rates[tile]
                second_buf[slot, tile, pl.ds(place * chunk, chunk), :] = scaled[:half] + scaled[half:]
                decay_sums[tile] = decay_sums[tile] + weighted * step_now
        return (tuple(incoming), tuple(decay_sums))

    zero_tile = jnp.zeros((size, lanes), jnp.float32)
    zero_tiles = ((zero_tile,) * tiles, (zero_tile,) * tiles)
    early = chunks // 2
    carried = lax.fori_loop(0, early, backward, zero_tiles)

    @pl.when(block == 0)
    def _():
        reduce.leg(1)

    @pl.when(block == 2)
    def _():
        reduce.leg(2)

    @pl.when(block == pl.num_programs(0) - 1)
    def _():
        reduce.leg(3)

    _, decay_sums = lax.fori_loop(early, chunks, backward, carried)
    settle(0, (chunks - 1) % 2)
    for tile in range(tiles):
        decay_grad_ref[:, cut(tile)] = decay_sums[tile] * rates[tile] * ln2
    skip = small_rows(small_ref, *plan["skip"])

    def after(index, at, carry):
        spot = pl.ds(pl.multiple_of(index * 4, 4), 4)
        sums = []
        for tile in range(tiles):
            signal = signal_ref[at, cut(tile)].astype(jnp.float32)
            step = step_ref[spot, :, cut(tile)].reshape(4 * chunk, lanes)
            through = through_buf[spot, :, cut(tile)].reshape(4 * chunk, lanes)
            scaled = scaled_buf[spot, :, cut(tile)].reshape(4 * chunk, lanes)
            core_grad = core_grad_ref[spot, :, cut(tile)].reshape(4 * chunk, lanes)
            grad_pre = (through * signal + ln2 * scaled) * slope_of(step)
            low_buf[at, cut(tile)] = grad_pre.astype(low_buf.dtype)
            signal_grad_ref[at, cut(tile)] = (
                through * step + skip[:, tile * lanes : (tile + 1) * lanes] * core_grad
            )
            sums.append(carry[tile] + eight(grad_pre))
        return tuple(sums)

    zero_rows = jnp.zeros((8, lanes), jnp.float32)
    sums = row_loop(rows, 4 * chunk, after, (zero_rows,) * tiles)
    for tile in range(tiles):
        bias_grad_ref[:, cut(tile)] = jnp.sum(sums[tile], axis=0, keepdims=True)
    step_w_grad_ref[...] = contract(
        projected_ref[:, :rank].astype(low_buf.dtype), low_buf[...], 0, 0
    )
    rank_ref[...] += contract(low_buf[...], small_ref[pl.ds(plan["step"][0], rank), :], 1, 1)

    @pl.when(block == pl.num_programs(0) - 1)
    def _():
        square_ref[...] = reduce.finish(None, None)[0]
        reduce.settle()
        out_sum_ref[...] = parts[0][...]
        in_sum_ref[...] = parts[1][...]


def back_kernel(
    plan,
    lengths_ref,
    tokens_ref,
    low_ref,
    gain_ref,
    small_ref,
    flat_ref,
    branch_ref,
    signal_ref,
    signal_grad_ref,
    gate_grad_ref,
    flipped_ref,
    branch_w,
    gate_w,
    step_w_grad_ref,
    bias_grad_ref,
    decay_grad_ref,
    skip_grad_ref,
    small_grad_ref,
    in_grad_ref,
    gain_grad_ref,
    tokens_grad_ref,
    offset_buf,
    conv_buf,
    mixed_buf,
    total,
):
    rows = tokens_ref.shape[0]
    width = branch_ref.shape[1]
    tiles = width // lanes
    block = pl.program_id(0)

    @pl.when(block == 0)
    def _():
        fill_offsets(lengths_ref, offset_buf, rows)

    taps = small_rows(small_ref, *plan["taps"])
    shift = small_rows(small_ref, *plan["shift"])
    count = taps.shape[0]
    small_grad_ref[:lanes, :] = contract(flat_ref[...], signal_ref[...], 0, 0)

    def place_rows(name, values):
        first, tall = plan[name]
        small_grad_ref[first : first + tall, :] = values

    place_rows("step", step_w_grad_ref[...])
    place_rows("decay", decay_grad_ref[...])
    place_rows("bias", bias_grad_ref[...])
    place_rows("skip", skip_grad_ref[...])
    conv_buf[pl.ds(0, rows), :] = signal_grad_ref[...] + jnp.dot(
        flat_ref[...], small_ref[:lanes, :], preferred_element_type=jnp.float32
    )
    conv_buf[pl.ds(rows, 8), :] = jnp.zeros((8, width), jnp.float32)

    def through_conv(index, at, carry):
        sums = []
        for tile in range(tiles):
            summed, reads = conv_rows(index, at, 32, tile, branch_ref, offset_buf, taps, shift)
            sigma = sigmoid(summed)
            grad_conv = conv_buf[at, cut(tile)] * (sigma + summed * sigma * (1.0 - sigma))
            conv_buf[at, cut(tile)] = grad_conv
            adds = [grad_conv] + [grad_conv * read for read in reads]
            sums.append(tuple(kept + eight(add) for kept, add in zip(carry[tile], adds)))
        return tuple(sums)

    zero_rows = jnp.zeros((8, lanes), jnp.float32)
    sums = row_loop(rows, 32, through_conv, ((zero_rows,) * (count + 1),) * tiles)
    for tile in range(tiles):
        first = plan["shift"][0]
        small_grad_ref[first : first + 1, cut(tile)] = jnp.sum(sums[tile][0], axis=0, keepdims=True)
        for tap in range(count):
            first = plan["taps"][0] + tap
            small_grad_ref[first : first + 1, cut(tile)] = jnp.sum(
                sums[tile][tap + 1], axis=0, keepdims=True
            )

    def to_branch(index, at, carry):
        longer = pl.ds(pl.multiple_of(index * 32, 32), 40)
        offsets = offset_buf[longer, :]
        for tile in range(tiles):
            here = slice(tile * lanes, (tile + 1) * lanes)
            grads = conv_buf[longer, cut(tile)]
            summed = taps[count - 1 : count, here] * grads[:32]
            for tap in range(count - 1):
                lag = count - 1 - tap
                kept = jnp.where(offsets >= lag, grads, 0.0)
                summed = summed + taps[tap : tap + 1, here] * pltpu.roll(kept, 40 - lag, 0)[:32]
            mixed_buf[at, cut(tile)] = summed.astype(mixed_buf.dtype)
        return carry

    row_loop(rows, 32, to_branch, 0)
    in_grad_ref[...] = jnp.dot(
        flipped_ref[...], mixed_buf[...], preferred_element_type=jnp.float32
    ).astype(in_grad_ref.dtype)
    piece = contract(mixed_buf[...], branch_w[...], 1, 1) + contract(gate_grad_ref[...], gate_w[...], 1, 1)

    @pl.when(block == 0)
    def _():
        total[...] = piece

    @pl.when(block > 0)
    def _():
        total[...] += piece

    @pl.when(block == pl.num_programs(0) - 1)
    def _():
        def finish(index, at, carry):
            residual = tokens_ref[at, :].astype(jnp.float32)
            scale = lax.rsqrt(jnp.mean(residual * residual, axis=1, keepdims=True) + epsilon)
            grad_normed = total[at, :]
            weighted = grad_normed * gain_ref[...]
            inner = jnp.mean(weighted * residual, axis=1, keepdims=True)
            grad_y = low_ref[at, :].astype(jnp.float32)
            result = grad_y + (scale * weighted - residual * (scale * scale * scale) * inner)
            tokens_grad_ref[at, :] = result.astype(tokens_grad_ref.dtype)
            return carry + eight(grad_normed * residual * scale)

        gains = row_loop(rows, 16, finish, jnp.zeros((8, total.shape[1]), jnp.float32))
        gain_grad_ref[...] = jnp.sum(gains, axis=0, keepdims=True)


def finish_kernel(plan, names, branch_ref, gate_ref, out_ref, small_ref, norm_ref, *outs):
    middle = branch_ref.shape[1]
    outs[0][:, :middle] = branch_ref[...]
    outs[0][:, middle:] = gate_ref[...]
    outs[1][...] = out_ref[...]
    for name, target in zip(names, outs[2 : 2 + len(names)]):
        first, count = plan[name]
        if len(target.shape) == 1:
            target[...] = small_ref[first, : target.shape[0]]
        else:
            target[...] = small_ref[first : first + count, :]
    for index in range(2):
        outs[2 + len(names) + index][0, 0] = jnp.sum(norm_ref[index])


def shape(dims, kind=jnp.float32):
    return jax.ShapeDtypeStruct(dims, kind)


def compute_call(
    kernel, name, blocks, in_specs, out_specs, out_shape, scratch, flops, operands, collective_id=None
):
    return pl.pallas_call(
        kernel,
        grid=(blocks,),
        in_specs=in_specs,
        out_specs=out_specs,
        out_shape=out_shape,
        scratch_shapes=scratch,
        compiler_params=pltpu.CompilerParams(
            dimension_semantics=("arbitrary",),
            vmem_limit_bytes=62 * 1024 * 1024,
            collective_id=collective_id,
            has_side_effects=collective_id is not None,
        ),
        cost_estimate=pl.CostEstimate(flops=flops, bytes_accessed=40 << 20, transcendentals=0),
        name=name,
    )(*operands)


class Place:
    def __init__(self, dims, swapped=False):
        depth, tall, wide = dims
        self.dims = dims
        self.core = lax.axis_index("wide")
        self.me = lax.axis_index("narrow")
        self.across = lax.rem(self.me, wide)
        self.up = lax.rem(lax.div(self.me, wide), tall)
        self.deep = lax.div(self.me, wide * tall)
        side = 1 - self.core if swapped else self.core
        turn = side if tall == wide else 0
        self.second = (1 + turn * (wide - 1), self.across + turn * (self.up - self.across), wide)
        self.third = (wide - turn * (wide - 1), self.up + turn * (self.across - self.up), tall)
        self.spans = (depth, wide, tall)
        self.other = {"wide": 1 - self.core}

    def at(self, d, e, f):
        depth, tall, wide = self.dims
        return (
            lax.rem(self.deep + d, depth) * (tall * wide)
            + lax.rem(self.second[1] + e, self.second[2]) * self.second[0]
            + lax.rem(self.third[1] + f, self.third[2]) * self.third[0]
        )

    def behind(self, d, e, f):
        return self.at(*((size - hop) % size for size, hop in zip(self.spans, (d, e, f))))

    def slot(self, d, e, f):
        return (d * self.spans[1] + e) * self.spans[2] + f

    def moves(self):
        return [
            (d, e, f)
            for d in range(self.spans[0])
            for e in range(self.spans[1])
            for f in range(self.spans[2])
        ]

    def greet(self):
        barrier = pltpu.get_barrier_semaphore()
        pl.semaphore_signal(barrier, inc=1, device_id=self.other, device_id_type=pl.DeviceIdType.MESH)
        peers = 1
        for axis, size in enumerate(self.spans):
            for hop in range(1, size):
                move = [0, 0, 0]
                move[axis] = hop
                pl.semaphore_signal(
                    barrier,
                    inc=1,
                    device_id={"narrow": self.at(*move)},
                    device_id_type=pl.DeviceIdType.MESH,
                )
                peers += 1
        pl.semaphore_wait(barrier, peers)


def half_of(width, core):
    return pl.ds(pl.multiple_of(core * (width // 2), lanes), width // 2)


def side_of(block, side):
    if len(block.shape) == 3:
        return block.at[side]
    return block.at[:, half_of(block.shape[1], side)]


def half_shape(array):
    return array.shape[2:] if len(array.shape) == 4 else (array.shape[1], array.shape[2] // 2)


def remote(source, target, send_sem, recv_sem, device):
    return pltpu.make_async_remote_copy(
        src_ref=source,
        dst_ref=target,
        send_sem=send_sem,
        recv_sem=recv_sem,
        device_id=device,
        device_id_type=pl.DeviceIdType.MESH,
    )


class Gather:
    def __init__(self, dims, own, whole, sems):
        self.dims, self.own, self.whole = dims, own, whole
        self.local_sem, self.send_sem, self.recv_sem, self.core_send, self.core_recv = sems

    @staticmethod
    def scratch(count, dims):
        number = dims[0] * dims[1] * dims[2]
        return [pltpu.SemaphoreType.DMA((count,))] + [pltpu.SemaphoreType.DMA((count, number))] * 4

    def onward(self, place, which, move):
        d, e, f = move
        number = place.behind(*move)
        target = side_of(self.whole[which].at[number], place.core)
        source = side_of(self.own[which], place.core) if move == (0, 0, 0) else target
        hops = []
        if f == 0:
            hops += [((0, 0, hop), (d, e, hop)) for hop in range(1, place.spans[2])]
        if f == 0 and e == 0:
            hops += [((0, hop, 0), (d, hop, 0)) for hop in range(1, place.spans[1])]
        if move == (0, 0, 0):
            hops += [((hop, 0, 0), (hop, 0, 0)) for hop in range(1, place.spans[0])]
        for step, landing in reversed(hops):
            index = place.slot(*landing)
            remote(
                source,
                target,
                self.send_sem.at[which, index],
                self.recv_sem.at[which, index],
                {"narrow": place.at(*step)},
            ).start()
        if move != (0, 0, 0):
            index = place.slot(*move)
            remote(
                source,
                target,
                self.core_send.at[which, index],
                self.core_recv.at[which, index],
                place.other,
            ).start()

    def local(self, place, which):
        return pltpu.make_async_copy(
            self.own[which], self.whole[which].at[place.at(0, 0, 0)], self.local_sem.at[which]
        )

    def start(self):
        place = Place(self.dims)
        place.greet()
        for which in range(len(self.own)):
            self.onward(place, which, (0, 0, 0))
        for which in range(len(self.own)):
            self.local(place, which).start()

    def leg(self, number):
        place = Place(self.dims)
        for which in range(len(self.own)):
            for move in place.moves():
                d, e, f = move
                if (number == 3) != (f > 0):
                    continue
                if number < 3 and (number == 2) != (e > 0):
                    continue
                if move == (0, 0, 0):
                    continue
                index = place.slot(*move)
                landed = side_of(self.whole[which].at[place.behind(*move)], place.core)
                remote(
                    landed,
                    landed,
                    self.send_sem.at[which, index],
                    self.recv_sem.at[which, index],
                    place.other,
                ).wait_recv()
                self.onward(place, which, move)

    def finish(self):
        place = Place(self.dims)
        mirror = Place(self.dims, swapped=True)
        for which in range(len(self.own)):
            for move in place.moves():
                if move == (0, 0, 0):
                    continue
                index = place.slot(*move)
                landed = side_of(self.whole[which].at[mirror.behind(*move)], 1 - place.core)
                handed = remote(
                    landed,
                    landed,
                    self.core_send.at[which, index],
                    self.core_recv.at[which, index],
                    place.other,
                )
                handed.wait_recv()
                handed.wait_send()
                remote(
                    landed,
                    landed,
                    self.send_sem.at[which, index],
                    self.recv_sem.at[which, index],
                    place.other,
                ).wait_send()
            self.local(place, which).wait()


class Reduce:
    def __init__(self, dims, grads, held, sems, results, targets):
        self.dims, self.grads = dims, grads
        count = len(grads)
        self.mine, self.swapped, self.third, self.second, self.first = (
            held[index * count : (index + 1) * count] for index in range(5)
        )
        (
            self.local_sem,
            self.core_send,
            self.core_recv,
            self.leg_send,
            self.leg_recv,
            self.last_send,
            self.last_recv,
        ) = sems
        self.results, self.targets = results, targets

    @staticmethod
    def rooms(dims, grads):
        depth, tall, wide = dims
        number = depth * tall * wide
        places = (number, number, depth * wide * (tall - 1), depth * (wide - 1), depth - 1)
        return [
            pltpu.VMEM((room,) + tuple(half_shape(grad)), grad.dtype) for room in places for grad in grads
        ]

    @staticmethod
    def sems(dims, count):
        number = dims[0] * dims[1] * dims[2]
        return [pltpu.SemaphoreType.DMA((count, number))] * 5 + [pltpu.SemaphoreType.DMA((count,))] * 2

    def order(self, place):
        return sorted(place.moves(), key=lambda item: (item[2] == 0, item[1] == 0, item[0] == 0))

    def share(self, which, side):
        result, first = self.targets[which]
        if len(self.grads[which].shape) == 4:
            return self.results[result].at[side]
        width = self.grads[which].shape[2]
        columns = pl.ds(pl.multiple_of(first + side * (width // 2), lanes), width // 2)
        return self.results[result].at[:, columns]

    def load(self, place, which, move):
        return pltpu.make_async_copy(
            side_of(self.grads[which].at[place.at(*move)], place.core),
            self.mine[which].at[place.slot(*move)],
            self.local_sem.at[which, place.slot(*move)],
        )

    def swap(self, place, which, move, mirror):
        index = place.slot(*move)
        return remote(
            side_of(self.grads[which].at[mirror.at(*move)], 1 - place.core),
            self.swapped[which].at[index],
            self.core_send.at[which, index],
            self.core_recv.at[which, index],
            place.other,
        )

    def start(self):
        place, mirror = Place(self.dims), Place(self.dims, swapped=True)
        place.greet()
        for move in self.order(place):
            for which in range(len(self.grads)):
                self.swap(place, which, move, mirror).start()
                self.load(place, which, move).start()

    def landing(self, place, which, move):
        d, e, f = move
        if f > 0:
            return self.third[which].at[(d * place.spans[1] + e) * (place.spans[2] - 1) + f - 1], (0, 0, f)
        if e > 0:
            return self.second[which].at[d * (place.spans[1] - 1) + e - 1], (0, e, 0)
        return self.first[which].at[d - 1], (d, 0, 0)

    def hop(self, place, which, move):
        landing, step = self.landing(place, which, move)
        index = place.slot(*move)
        return remote(
            self.mine[which].at[index],
            landing,
            self.leg_send.at[which, index],
            self.leg_recv.at[which, index],
            {"narrow": place.at(*step)},
        )

    def collect(self, place, which, move):
        d, e, f = move
        index = place.slot(*move)
        self.load(place, which, move).wait()
        handed = self.swapped[which].at[index]
        remote(
            handed, handed, self.core_send.at[which, index], self.core_recv.at[which, index], place.other
        ).wait_recv()
        parts = [handed]
        coming = []
        if f == 0:
            coming += [(d, e, hop) for hop in range(1, place.spans[2])]
        if f == 0 and e == 0:
            coming += [(d, hop, 0) for hop in range(1, place.spans[1])]
        if move == (0, 0, 0):
            coming += [(hop, 0, 0) for hop in range(1, place.spans[0])]
        for source in coming:
            self.hop(place, which, source).wait_recv()
            parts.append(self.landing(place, which, source)[0])
        return parts

    def added(self, place, which, move, parts, store, carry):
        block = self.mine[which].at[place.slot(*move)]
        rows = block.shape[0]
        group = min(rows, 16)

        def some(index, carry):
            at_rows = pl.ds(pl.multiple_of(index * group, group), group)
            total = block[at_rows, :].astype(jnp.float32)
            for part in parts:
                total = total + part[at_rows, :].astype(jnp.float32)
            return store(block, at_rows, total, carry)

        return lax.fori_loop(0, rows // group, some, carry)

    def leg(self, number):
        place = Place(self.dims)

        def keep(block, at_rows, total, carry):
            block[at_rows, :] = total.astype(block.dtype)
            return carry

        for move in self.order(place)[:-1]:
            d, e, f = move
            if number != (1 if f > 0 else 2 if e > 0 else 3):
                continue
            for which in range(len(self.grads)):
                parts = self.collect(place, which, move)
                self.added(place, which, move, parts, keep, 0)
                self.hop(place, which, move).start()

    def finish(self, plain_at, plain_ref):
        place, mirror = Place(self.dims), Place(self.dims, swapped=True)
        squares = (jnp.zeros((8, lanes), jnp.float32),) * 2
        for which in range(len(self.grads)):
            parts = self.collect(place, which, (0, 0, 0))
            result = self.share(which, place.core)

            def store(block, at_rows, total, carry, which=which, result=result):
                result[at_rows, :] = total
                kept, plain = carry
                squared = total * total
                if which == plain_at:
                    marked = squared * plain_ref[place.core, at_rows, :]
                    plain = plain + folded_squares(marked)
                    squared = squared - marked
                return (kept + folded_squares(squared), plain)

            squares = self.added(place, which, (0, 0, 0), parts, store, squares)
            remote(result, result, self.last_send.at[which], self.last_recv.at[which], place.other).start()
        return squares

    def settle(self):
        place, mirror = Place(self.dims), Place(self.dims, swapped=True)
        for which in range(len(self.grads)):
            result = self.share(which, 1 - place.core)
            last = remote(result, result, self.last_send.at[which], self.last_recv.at[which], place.other)
            last.wait_recv()
            last.wait_send()
            for move in place.moves():
                self.swap(place, which, move, mirror).wait_send()
                if move != (0, 0, 0):
                    self.hop(place, which, move).wait_send()


def folded_squares(values):
    total = None
    if values.shape[1] < lanes:
        first = lax.broadcasted_iota(jnp.int32, (values.shape[0], lanes), 1) == 0
        values = jnp.where(first, jnp.sum(values, axis=1, keepdims=True), 0.0)
    for row in range(0, values.shape[0], 8):
        for column in range(0, values.shape[1], lanes):
            piece = values[row : row + 8, column : column + lanes]
            total = piece if total is None else total + piece
    return total


def gather_kernel(dims, plan, names, *refs):
    smalls, bigs = refs[: len(names)], refs[len(names) : len(names) + 1]
    refs = refs[len(names) + 1 :]
    whole, own, pack_buf, sems = refs[:2], refs[2:4], refs[4], refs[5:]
    pack_buf[...] = jnp.zeros_like(pack_buf)
    for name, ref in zip(names, smalls):
        first, tall = plan[name]
        pack_buf[first : first + tall, : ref.shape[1]] = ref[...]
    tall = pack_buf.shape[0] // 2
    for side in range(2):
        own[0][side] = pack_buf[side * tall : (side + 1) * tall, :].astype(own[0].dtype)
    own[1][...] = bigs[0][...].astype(own[1].dtype)
    gather = Gather(dims, own, whole, sems)
    gather.start()
    for number in (1, 2, 3):
        gather.leg(number)
    gather.finish()


def gather_weights(dims, plan, smalls, big):
    number = dims[0] * dims[1] * dims[2]
    names = list(smalls)
    width = smalls["select"].shape[1]
    owned = [shape((2, plan["rows"] // 2, width), jnp.bfloat16), shape(big.shape, jnp.bfloat16)]
    inside = pl.BlockSpec(memory_space=pltpu.VMEM)
    return pl.pallas_call(
        functools.partial(gather_kernel, dims, plan, names),
        in_specs=[inside] * (len(names) + 1),
        out_specs=[pl.BlockSpec(memory_space=pl.ANY)] * 2,
        out_shape=[shape((number,) + kind.shape, kind.dtype) for kind in owned],
        scratch_shapes=[pltpu.VMEM(kind.shape, kind.dtype) for kind in owned]
        + [pltpu.VMEM((plan["rows"], width), jnp.float32)]
        + Gather.scratch(2, dims),
        compiler_params=pltpu.CompilerParams(
            collective_id=0, has_side_effects=True, vmem_limit_bytes=60 * 1024 * 1024
        ),
        name="gather_weights",
    )(*smalls.values(), big)


def reduce_kernel(dims, count, results, targets, plain_at, *refs):
    grads, plain_ref, earlier_ref = refs[:count], refs[count], refs[count + 1]
    refs = refs[count + 2 :]
    sums, norms = refs[:results], refs[results]
    refs = refs[results + 1 :]
    held, buffers = refs[: 5 * count], refs[5 * count : 5 * count + 4]
    refs = refs[5 * count + 4 :]
    sems, (norm_send, norm_recv) = refs[:7], refs[7:]
    reduce = Reduce(dims, grads, held, sems, sums, targets)
    reduce.start()
    for number in (1, 2, 3):
        reduce.leg(number)
    kept, plain = reduce.finish(plain_at, plain_ref)
    running = jnp.stack([kept + earlier_ref[...], plain])

    place = Place(dims)
    depth, tall, wide = dims
    plane = tall * wide
    me = place.me
    stages = (
        (buffers[0], 2, place.core, lambda spot: {"wide": spot}),
        (buffers[1], depth, place.deep, lambda spot: {"narrow": spot * plane + lax.rem(me, plane)}),
        (buffers[2], wide, place.across, lambda spot: {"narrow": me - place.across + spot}),
        (buffers[3], tall, place.up, lambda spot: {"narrow": me + (spot - place.up) * wide}),
    )
    pending = []
    first = 0
    for buffer, size, mine_at, device in stages:
        buffer[mine_at] = running
        for hop in range(1, size):
            copy = remote(
                buffer.at[mine_at],
                buffer.at[mine_at],
                norm_send.at[first + hop - 1],
                norm_recv.at[first + hop - 1],
                device(lax.rem(mine_at + hop, size)),
            )
            copy.start()
            pending.append(copy)
        for hop in range(1, size):
            came = lax.rem(mine_at + size - hop, size)
            remote(
                buffer.at[came],
                buffer.at[came],
                norm_send.at[first + hop - 1],
                norm_recv.at[first + hop - 1],
                device(came),
            ).wait_recv()
        first += size - 1
        running = buffer[0]
        for spot in range(1, size):
            running = running + buffer[spot]
    norms[...] = running
    reduce.settle()
    for copy in pending:
        copy.wait_send()


def sum_shapes(grads, targets):
    sums = []
    for index in range(1 + max(target[0] for target in targets)):
        members = [grad for grad, target in zip(grads, targets) if target[0] == index]
        if len(members[0].shape) == 4:
            sums.append(shape(members[0].shape[1:]))
        else:
            sums.append(shape((members[0].shape[1], sum(grad.shape[2] for grad in members))))
    return sums


def reduce_grads(dims, grads, targets, plain_mask, plain_at, earlier):
    depth, tall, wide = dims
    count = len(grads)
    anywhere = pl.BlockSpec(memory_space=pl.ANY)
    inside = pl.BlockSpec(memory_space=pltpu.VMEM)
    sums = sum_shapes(grads, targets)
    result = pl.pallas_call(
        functools.partial(reduce_kernel, dims, count, len(sums), targets, plain_at),
        in_specs=[anywhere] * count + [inside] * 2,
        out_specs=[inside] * (len(sums) + 1),
        out_shape=sums + [shape((2, 8, lanes))],
        scratch_shapes=Reduce.rooms(dims, grads)
        + [pltpu.VMEM((size, 2, 8, lanes), jnp.float32) for size in (2, depth, wide, tall)]
        + Reduce.sems(dims, count)
        + [pltpu.SemaphoreType.DMA((depth + tall + wide,))] * 2,
        compiler_params=pltpu.CompilerParams(
            collective_id=1, has_side_effects=True, vmem_limit_bytes=56 * 1024 * 1024
        ),
        name="reduce_grads",
    )(*grads, plain_mask, earlier)
    return result[: len(sums)], result[len(sums)]


def grid_of(mesh):
    number = mesh.shape["narrow"]
    places = [getattr(device, "coords", None) for device in mesh.devices[0]]
    if all(place is not None for place in places):
        sizes = [len({place[axis] for place in places}) for axis in (2, 1, 0)]
        if sizes[0] * sizes[1] * sizes[2] == number:
            return tuple(sizes)
    side = round((number / 2) ** (1 / 3))
    return (2 * side, side, side) if 2 * side**3 == number else (number, 1, 1)


def plan_of(select_rows, state_size, tap_count, step_rows):
    plan, first = {}, 0
    for name, tall in (
        ("select", select_rows),
        ("decay", state_size),
        ("taps", tap_count),
        ("shift", 1),
        ("bias", 1),
        ("skip", 1),
        ("gain", 1),
    ):
        plan[name] = (first, tall)
        first += tall
    plan["step"] = (lanes, step_rows)
    plan["rows"] = -(-(lanes + step_rows) // 32) * 32
    return plan


def per_device(
    dims,
    tokens,
    cotangent,
    loss_mask,
    seq_lengths,
    norm_gain,
    in_proj,
    conv_weight,
    conv_bias,
    select_proj,
    step_proj,
    step_bias,
    decay_log,
    skip_scale,
    out_proj,
):
    half = jnp.bfloat16
    piece = skip_scale.shape[0]
    gain_piece = norm_gain.shape[0]
    rank, size = step_proj.shape[0], decay_log.shape[0]
    plan = plan_of(select_proj.shape[0], size, conv_weight.shape[0], rank)
    small_blocks, in_blocks = gather_weights(
        dims,
        plan,
        {
            "select": select_proj,
            "decay": decay_log,
            "taps": conv_weight,
            "shift": conv_bias[None],
            "bias": step_bias[None],
            "skip": skip_scale[None],
            "gain": norm_gain[None],
            "step": step_proj,
        },
        in_proj,
    )
    in_whole = in_blocks.reshape(-1, in_blocks.shape[2])
    small_blocks = small_blocks.reshape(-1, plan["rows"], piece)
    small = jnp.swapaxes(small_blocks, 0, 1).reshape(plan["rows"], -1)
    gain_value = small_blocks[:, plan["gain"][0], :gain_piece].reshape(1, -1).astype(jnp.float32)

    rows, model = tokens.shape
    inner = small.shape[1]
    width = 4 * lanes
    blocks = inner // width
    chunks = rows // chunk
    mask_row = loss_mask[None]

    whole = pl.BlockSpec(memory_space=pltpu.VMEM)
    tall = pl.BlockSpec((rows, width), lambda b: (0, b))
    deep = pl.BlockSpec((chunks, chunk, width), lambda b: (0, 0, b))
    lead = pl.BlockSpec((rows, size, width), lambda b: (0, 0, b))
    first_w = pl.BlockSpec((model, width), lambda b: (0, b))
    second_w = pl.BlockSpec((model, width), lambda b: (0, b + blocks))
    out_w = pl.BlockSpec((width, model), lambda b: (b, 0))

    def thin(height):
        return pl.BlockSpec((height, width), lambda b: (0, b))

    def fixed(*dims_of):
        return pl.BlockSpec(dims_of, lambda b: (0,) * len(dims_of))

    scalars = pl.BlockSpec(memory_space=pltpu.SMEM)
    offset_buf = pltpu.VMEM((rows + 8, lanes), jnp.int32)
    packed = thin(plan["rows"])

    branch, gate_pre, signal, projected, flipped, grad_low = compute_call(
        functools.partial(front_kernel, plan),
        "front",
        blocks,
        [scalars, whole, whole, whole, whole, packed, first_w, second_w],
        [tall, tall, tall, fixed(rows, lanes), fixed(model, rows), fixed(rows, model)],
        [
            shape((rows, inner)),
            shape((rows, inner)),
            shape((rows, inner), half),
            shape((rows, lanes)),
            shape((model, rows), half),
            shape((rows, model), half),
        ],
        [pltpu.VMEM((rows, model), half), offset_buf],
        4 * rows * model * inner,
        (seq_lengths, tokens, cotangent, mask_row, gain_value, small, in_whole, in_whole),
    )
    write_rows = projected[:, rank : rank + size]
    read_rows = projected[:, rank + size : rank + 2 * size]
    wide_write = jnp.broadcast_to(write_rows[:, :, None], (rows, size, lanes))
    wide_read = jnp.broadcast_to(read_rows[:, :, None], (rows, size, lanes))
    row_block = pltpu.VMEM((chunks, chunk, width), jnp.float32)
    spare_block = pltpu.VMEM((chunks + 1, chunk, width), jnp.float32)
    number = small_blocks.shape[0]
    anywhere = pl.BlockSpec(memory_space=pl.ANY)
    states, step, core, out_blocks = compute_call(
        functools.partial(forward_kernel, plan, dims),
        "forward",
        blocks,
        [scalars, whole, packed, tall, whole, whole, whole],
        [lead, deep, deep, anywhere],
        [
            shape((rows, size, inner), half),
            shape((chunks, chunk, inner)),
            shape((chunks, chunk, inner)),
            shape((number,) + out_proj.shape, half),
        ],
        [
            offset_buf,
            pltpu.VMEM((rows, width), jnp.float32),
            row_block,
            row_block,
            pltpu.VMEM((width // lanes, chunk * chunk, lanes), jnp.float32),
            pltpu.VMEM(out_proj.shape, half),
        ]
        + Gather.scratch(1, dims),
        15 * rows * inner * size,
        (seq_lengths, projected, small, signal, wide_write, wide_read, out_proj),
        collective_id=2,
    )
    core_grad, gate_grad, grad_skip, grad_outw, grad_in_gate, output = compute_call(
        functools.partial(middle_kernel, plan),
        "middle",
        blocks,
        [deep, packed, tall, tall, whole, out_w, whole, whole],
        [deep, tall, thin(1), out_w, first_w, fixed(rows, model)],
        [
            shape((chunks, chunk, inner)),
            shape((rows, inner), half),
            shape((1, inner)),
            shape((inner, model), half),
            shape((model, inner), half),
            shape((rows, model), half),
        ],
        [
            pltpu.VMEM((rows, width), jnp.float32),
            pltpu.VMEM((rows, width), half),
            pltpu.VMEM((rows, model), jnp.float32),
        ],
        8 * rows * model * inner,
        (core, small, signal, gate_pre, grad_low, out_blocks.reshape(inner, model), flipped, tokens),
    )
    split = in_blocks.shape[:2] + (inner,)
    early_grads = [grad_outw.reshape(out_blocks.shape), grad_in_gate.reshape(split)]
    early_sums = sum_shapes(early_grads, [(0, 0), (1, 0)])
    pairs = (chunks + 1, size, 2 * chunk)
    fold_buf = pltpu.VMEM((2, width // lanes, chunk * chunk, lanes), jnp.float32)
    (
        signal_grad,
        grad_stepw,
        grad_bias,
        grad_decaylog,
        grad_rank,
        grad_write,
        grad_read,
        out_sum,
        in_gate_sum,
        early_squares,
    ) = compute_call(
        functools.partial(backward_kernel, plan, dims),
        "backward",
        blocks,
        [scalars, whole, packed, tall, whole, whole, deep, deep, lead, anywhere, anywhere],
        [tall, thin(rank), thin(1), thin(size), fixed(rows, rank), fixed(*pairs), fixed(*pairs)]
        + [whole] * 3,
        [
            shape((rows, inner)),
            shape((rank, inner)),
            shape((1, inner)),
            shape((size, inner)),
            shape((rows, rank)),
            shape(pairs),
            shape(pairs),
            *early_sums,
            shape((8, lanes)),
        ],
        [
            offset_buf,
            row_block,
            row_block,
            pltpu.VMEM((chunks + 1, 2 * chunk, width), half),
            pltpu.VMEM((chunks, 2 * chunk, width), half),
            fold_buf,
            fold_buf,
            pltpu.VMEM((2, chunk * size, width), half),
            spare_block,
            spare_block,
            pltpu.VMEM((rows, width), half),
        ]
        + [pltpu.VMEM(early.shape, early.dtype) for early in early_sums]
        + Reduce.rooms(dims, early_grads)
        + Reduce.sems(dims, 2),
        40 * rows * inner * size,
        (seq_lengths, projected, small, signal, wide_write, wide_read, step, core_grad, states, *early_grads),
        collective_id=3,
    )

    def by_token(pairs):
        summed = pairs[:chunks, :, :chunk] + pairs[:chunks, :, chunk:]
        return jnp.swapaxes(summed, 1, 2).reshape(rows, size)

    flat = jnp.concatenate(
        [
            grad_rank,
            by_token(grad_write),
            by_token(grad_read),
            jnp.zeros((rows, lanes - rank - 2 * size), jnp.float32),
        ],
        axis=1,
    ).astype(half)
    small_grad, grad_in_branch, grad_gain, grad_tokens = compute_call(
        functools.partial(back_kernel, plan),
        "back",
        blocks,
        [scalars, whole, whole, whole, packed, whole, tall, tall, tall, tall, whole, first_w, second_w]
        + [thin(rank), thin(1), thin(size), thin(1)],
        [packed, first_w, fixed(1, model), fixed(rows, model)],
        [
            shape((plan["rows"], inner)),
            shape((model, inner), half),
            shape((1, model)),
            shape((rows, model), half),
        ],
        [
            offset_buf,
            pltpu.VMEM((rows + 8, width), jnp.float32),
            pltpu.VMEM((rows, width), half),
            pltpu.VMEM((rows, model), jnp.float32),
        ],
        8 * rows * model * inner,
        (
            seq_lengths,
            tokens,
            grad_low,
            gain_value,
            small,
            flat,
            branch,
            signal,
            signal_grad,
            gate_grad,
            flipped,
            in_whole,
            in_whole,
            grad_stepw,
            grad_bias,
            grad_decaylog,
            grad_skip,
        ),
    )

    gain_rows = jnp.pad(grad_gain.reshape(number, 1, gain_piece), ((0, 0), (0, 0), (0, piece - gain_piece)))
    place = plan["gain"][0]
    small_grad = jnp.swapaxes(small_grad.reshape(plan["rows"], number, piece), 0, 1) + jnp.pad(
        gain_rows, ((0, 0), (place, plan["rows"] - place - 1), (0, 0))
    )
    plain_rows = np.zeros((plan["rows"], piece), np.float32)
    for name in ("bias", "decay", "skip"):
        first, count = plan[name]
        plain_rows[first : first + count] = 1.0
    halves = (2, plan["rows"] // 2, piece)
    (in_branch_sum, small_sum), norms = reduce_grads(
        dims,
        [grad_in_branch.reshape(split), small_grad.astype(half).reshape((number,) + halves)],
        [(0, 0), (1, 0)],
        jnp.asarray(plain_rows.reshape(halves)),
        1,
        early_squares,
    )
    names = ("gain", "taps", "shift", "select", "step", "bias", "decay", "skip")
    own = (norm_gain, conv_weight, conv_bias, select_proj, step_proj, step_bias, decay_log, skip_scale)
    in_grad, out_grad, gain_grad, *small_grads, decay_sq, plain_sq = pl.pallas_call(
        functools.partial(finish_kernel, plan, names),
        in_specs=[whole] * 5,
        out_specs=[whole] * (2 + len(names)) + [scalars] * 2,
        out_shape=[shape(in_proj.shape), shape(out_proj.shape)]
        + [shape(array.shape) for array in own]
        + [shape((1, 1))] * 2,
        name="finish",
    )(in_branch_sum, in_gate_sum, out_sum, small_sum.reshape(plan["rows"], piece), norms)
    return (
        output,
        grad_tokens,
        gain_grad,
        in_grad,
        *small_grads,
        out_grad,
        decay_sq[0, 0],
        plain_sq[0, 0],
    )


def solution(mesh):
    placed = (
        P(("wide", "narrow"), None),
        P(("wide", "narrow"), None),
        P(("wide", "narrow")),
        P(("wide", "narrow"), None),
        P("narrow"),
        P("narrow", None),
        P(None, "narrow"),
        P("narrow"),
        P(None, "narrow"),
        P(None, "narrow"),
        P("narrow"),
        P(None, "narrow"),
        P("narrow"),
        P("narrow", None),
    )
    return jax.shard_map(
        functools.partial(per_device, grid_of(mesh)),
        mesh=mesh,
        in_specs=placed,
        out_specs=(
            P(("wide", "narrow"), None),
            P(("wide", "narrow"), None),
            P("narrow"),
            P("narrow", None),
            P(None, "narrow"),
            P("narrow"),
            P(None, "narrow"),
            P(None, "narrow"),
            P("narrow"),
            P(None, "narrow"),
            P("narrow"),
            P("narrow", None),
            P(),
            P(),
        ),
        check_vma=False,
    )
```

```python
import functools
import math

import jax
import jax.numpy as jnp
import numpy as np
from jax import lax
from jax.experimental import pallas as pl
from jax.experimental.pallas import tpu as pltpu
from jax.sharding import PartitionSpec as P

epsilon = 1e-05
chunk = 8
lanes = 128
log2e = math.log2(math.e)
ln2 = math.log(2.0)
far = 1e30


def contract(left, right, left_dim, right_dim):
    return lax.dot_general(
        left, right, (((left_dim,), (right_dim,)), ((), ())), preferred_element_type=jnp.float32
    )


def row_loop(rows, group, body, initial):
    def some(index, carry):
        return body(index, pl.ds(pl.multiple_of(index * group, group), group), carry)

    return lax.fori_loop(0, rows // group, some, initial)


def cut(tile):
    return pl.ds(tile * lanes, lanes)


def sigmoid(values):
    return 0.5 * jnp.tanh(0.5 * values) + 0.5


def softplus(values):
    small = jnp.exp(-jnp.abs(values))
    series = small * (1.0 - small * (0.5 - small * (1.0 / 3.0 - 0.25 * small)))
    return jnp.maximum(values, 0.0) + jnp.where(small < 0.03, series, jnp.log(1.0 + small))


def slope_of(step):
    series = step * (1.0 - step * (0.5 - step * (1.0 / 6.0 - step * (1.0 / 24.0))))
    return jnp.where(step < 0.03, series, 1.0 - jnp.exp(-step))


def fill_offsets(lengths_ref, offset_buf, rows):
    place = lax.broadcasted_iota(jnp.int32, offset_buf.shape, 0)
    start = jnp.zeros(offset_buf.shape, jnp.int32)
    ahead = jnp.int32(0)
    for index in range(lengths_ref.shape[1] - 1):
        ahead = ahead + lengths_ref[0, index]
        start = jnp.where(place >= ahead, ahead, start)
    offset_buf[...] = jnp.where(place < rows, place - start, 0)


def small_rows(small_ref, first, count):
    base = first // 16 * 16
    tall = -(-(first + count - base) // 16) * 16
    return small_ref[base : base + tall, :].astype(jnp.float32)[first - base : first - base + count]


def eight(values):
    total = values[:8]
    for row in range(8, values.shape[0], 8):
        total = total + values[row : row + 8]
    return total


def conv_rows(index, at, group, tile, branch_ref, offset_buf, taps, shift):
    count = taps.shape[0]
    here = slice(tile * lanes, (tile + 1) * lanes)
    current = branch_ref[at, cut(tile)]
    before = branch_ref[pl.ds(pl.multiple_of(jnp.maximum(index * group - 8, 0), 8), 8), cut(tile)]
    both = jnp.concatenate([before, current], axis=0)
    offsets = offset_buf[at, :]
    summed = shift[:, here] + taps[count - 1 : count, here] * current
    for tap in range(count - 1):
        lag = count - 1 - tap
        read = jnp.where(offsets >= lag, pltpu.roll(both, lag, 0)[8:], 0.0)
        summed = summed + taps[tap : tap + 1, here] * read
    return summed


def front_kernel(
    plan,
    lengths_ref,
    tokens_ref,
    cotangent_ref,
    mask_ref,
    gain_ref,
    small_ref,
    branch_w,
    gate_w,
    branch_ref,
    gate_ref,
    signal_ref,
    slope_ref,
    projected_ref,
    flipped_ref,
    low_ref,
    write_pair,
    write_triple,
    read_pair,
    read_triple,
    normed_buf,
    offset_buf,
):
    rows = tokens_ref.shape[0]
    width = branch_ref.shape[1]
    block = pl.program_id(0)

    @pl.when(block == 0)
    def _():
        fill_offsets(lengths_ref, offset_buf, rows)

        def norm(index, at, carry):
            residual = tokens_ref[at, :].astype(jnp.float32)
            scale = lax.rsqrt(jnp.mean(residual * residual, axis=1, keepdims=True) + epsilon)
            normed_buf[at, :] = (residual * scale * gain_ref[...]).astype(normed_buf.dtype)
            return carry

        row_loop(rows, 16, norm, 0)
        flipped_ref[...] = normed_buf[...].T
        projected_ref[...] = jnp.zeros_like(projected_ref)
        down = lax.broadcasted_iota(jnp.int32, (rows, rows), 0)
        along = lax.broadcasted_iota(jnp.int32, (rows, rows), 1)
        diagonal = jnp.where(down == along, mask_ref[...].astype(jnp.float32), 0.0).astype(low_ref.dtype)
        low_ref[...] = jnp.dot(
            diagonal, cotangent_ref[...], preferred_element_type=jnp.float32
        ).astype(low_ref.dtype)

    branch_ref[...] = jnp.dot(normed_buf[...], branch_w[...], preferred_element_type=jnp.float32)
    gate_ref[...] = jnp.dot(normed_buf[...], gate_w[...], preferred_element_type=jnp.float32)
    taps = small_rows(small_ref, *plan["taps"])
    shift = small_rows(small_ref, *plan["shift"])

    def some(index, at, carry):
        for tile in range(width // lanes):
            summed = conv_rows(index, at, 32, tile, branch_ref, offset_buf, taps, shift)
            sigma = sigmoid(summed)
            active = summed * sigma
            signal_ref[at, cut(tile)] = active.astype(signal_ref.dtype)
            slope_ref[at, cut(tile)] = sigma + active * (1.0 - sigma)
        return carry

    row_loop(rows, 32, some, 0)
    projected_ref[...] += contract(signal_ref[...], small_ref[:lanes, :], 1, 1)

    @pl.when(block == pl.num_programs(0) - 1)
    def _():
        high, low = high_low(projected_ref[...])
        own = own_tokens(rows)
        rank = plan["step"][1]
        size = plan["decay"][1]
        entry = lax.broadcasted_iota(jnp.int32, (lanes, lanes), 0)
        lane = lax.rem(lax.broadcasted_iota(jnp.int32, (lanes, lanes), 1), size)
        for first, pair, triple in ((rank, write_pair, write_triple), (rank + size, read_pair, read_triple)):
            spread = (entry == lane + first).astype(jnp.bfloat16)
            parts = [
                (jnp.dot(part.astype(jnp.bfloat16), spread, preferred_element_type=jnp.float32) * own).reshape(
                    rows // chunk, chunk, lanes
                )
                for part in (high, low)
            ]
            pair[...] = jnp.concatenate(parts, axis=1).astype(pair.dtype)
            triple[...] = jnp.concatenate(
                [parts[0], parts[0], parts[1], jnp.zeros_like(parts[0])], axis=1
            ).astype(triple.dtype)


def high_low(values):
    high = values.astype(jnp.bfloat16).astype(jnp.float32)
    return high, values - high


def own_tokens(rows):
    token = lax.rem(lax.broadcasted_iota(jnp.int32, (rows, lanes), 0), chunk)
    return (token == lax.div(lax.broadcasted_iota(jnp.int32, (rows, lanes), 1), lanes // chunk)).astype(
        jnp.float32
    )


def tripled(values):
    high, low = high_low(values)
    return jnp.concatenate([high, low, high, jnp.zeros_like(high)], axis=1).astype(jnp.bfloat16)


def forward_kernel(
    plan,
    dims,
    lengths_ref,
    projected_ref,
    small_ref,
    signal_ref,
    write_triple,
    read_pair,
    own_ref,
    states_ref,
    step_ref,
    core_ref,
    whole_ref,
    offset_buf,
    pre_buf,
    decay_step,
    flows,
    entering,
    low_buf,
    *sems,
):
    rows, width = pre_buf.shape
    size = plan["decay"][1]
    tiles = width // lanes
    chunks = rows // chunk
    rank = plan["step"][1]
    block = pl.program_id(0)
    gather = Gather(dims, [low_buf], [whole_ref], sems)

    @pl.when(block == 0)
    def _():
        low_buf[...] = own_ref[...].astype(low_buf.dtype)
        gather.start()
        fill_offsets(lengths_ref, offset_buf, rows)

    pre_buf[...] = jnp.dot(
        projected_ref[:, :rank].astype(small_ref.dtype),
        small_ref[pl.ds(plan["step"][0], rank), :],
        preferred_element_type=jnp.float32,
    )
    bias = small_rows(small_ref, *plan["bias"])

    def before(index, at, carry):
        spot = pl.ds(pl.multiple_of(index * 4, 4), 4)
        inside = offset_buf[at, :] > 0
        for tile in range(tiles):
            step = softplus(pre_buf[at, cut(tile)] + bias[:, tile * lanes : (tile + 1) * lanes])
            step_ref[spot, :, cut(tile)] = step.reshape(4, chunk, lanes)
            decay_step[spot, :, cut(tile)] = jnp.where(inside, step, far).reshape(4, chunk, lanes)
            flow = (step * signal_ref[at, cut(tile)].astype(jnp.float32)).reshape(4, chunk, lanes)
            flows[spot, :, cut(tile)] = tripled(flow)
        return carry

    row_loop(rows, 4 * chunk, before, 0)
    flows[chunks] = jnp.zeros_like(flows[chunks])
    rates = -jnp.exp(small_rows(small_ref, *plan["decay"])) * log2e
    rates = [rates[:, tile * lanes : (tile + 1) * lanes] for tile in range(tiles)]

    def enter(index):
        return contract(write_triple[jnp.minimum(index, chunks - 1)], flows[index], 0, 0)

    def leave(index):
        read = jnp.dot(
            read_pair[index],
            states_ref[pl.ds(index * chunk, chunk)].reshape(chunk * size, width),
            preferred_element_type=jnp.float32,
        )
        core_ref[index] = read[:chunk] + read[chunk:]

    def forward(index, held):
        slot = lax.rem(index, 2)
        entering[1 - slot] = enter(index + 1)
        leave(jnp.maximum(index - 1, 0))
        held = list(held)
        for place in range(chunk):
            for tile in range(tiles):
                decay = jnp.exp2(rates[tile] * decay_step[index, pl.ds(place, 1), cut(tile)])
                added = entering[slot, pl.ds(place * size, size), cut(tile)]
                fresh = decay * held[tile] + added
                held[tile] = fresh
                states_ref[index * chunk + place, :, cut(tile)] = fresh.astype(states_ref.dtype)
        return tuple(held)

    entering[0] = enter(0)
    held = (jnp.zeros((size, lanes), jnp.float32),) * tiles
    for part in range(2):
        for number, moment in ((1, 3), (2, 5), (3, 7)):
            if moment % 2 == part:

                @pl.when(block == moment // 2)
                def _(number=number):
                    gather.leg(number)

        held = lax.fori_loop(part * chunks // 2, (part + 1) * chunks // 2, forward, held)
    leave(chunks - 1)

    @pl.when(block == pl.num_programs(0) - 1)
    def _():
        gather.finish()


def middle_kernel(
    plan,
    core_ref,
    small_ref,
    signal_ref,
    gate_ref,
    low_ref,
    out_w,
    flipped_ref,
    tokens_ref,
    core_grad_ref,
    gate_grad_ref,
    skip_grad_ref,
    out_grad_ref,
    in_grad_ref,
    output_ref,
    pre_buf,
    gated_buf,
    total,
):
    rows, width = pre_buf.shape
    tiles = width // lanes
    block = pl.program_id(0)
    pre_buf[...] = contract(low_ref[...], out_w[...], 1, 1)
    skip = small_rows(small_ref, *plan["skip"])

    def after(index, at, carry):
        spot = pl.ds(pl.multiple_of(index * 4, 4), 4)
        sums = []
        for tile in range(tiles):
            signal = signal_ref[at, cut(tile)].astype(jnp.float32)
            core = core_ref[spot, :, cut(tile)].reshape(4 * chunk, lanes)
            core = core + skip[:, tile * lanes : (tile + 1) * lanes] * signal
            gate = gate_ref[at, cut(tile)]
            sigma = sigmoid(gate)
            active = gate * sigma
            gated_buf[at, cut(tile)] = (core * active).astype(gated_buf.dtype)
            grad_gated = pre_buf[at, cut(tile)]
            grad_core = grad_gated * active
            core_grad_ref[spot, :, cut(tile)] = grad_core.reshape(4, chunk, lanes)
            slope = sigma + active * (1.0 - sigma)
            gate_grad_ref[at, cut(tile)] = (grad_gated * core * slope).astype(gate_grad_ref.dtype)
            sums.append(carry[tile] + eight(grad_core * signal))
        return tuple(sums)

    zero_rows = jnp.zeros((8, lanes), jnp.float32)
    skips = row_loop(rows, 4 * chunk, after, (zero_rows,) * tiles)
    for tile in range(tiles):
        skip_grad_ref[:, cut(tile)] = jnp.sum(skips[tile], axis=0, keepdims=True)
    out_grad_ref[...] = contract(gated_buf[...], low_ref[...], 0, 0).astype(out_grad_ref.dtype)
    in_grad_ref[...] = jnp.dot(
        flipped_ref[...], gate_grad_ref[...], preferred_element_type=jnp.float32
    ).astype(in_grad_ref.dtype)
    piece = jnp.dot(gated_buf[...], out_w[...], preferred_element_type=jnp.float32)

    @pl.when(block == 0)
    def _():
        total[...] = piece

    @pl.when(block > 0)
    def _():
        total[...] += piece

    @pl.when(block == pl.num_programs(0) - 1)
    def _():
        output_ref[...] = (tokens_ref[...].astype(jnp.float32) + total[...]).astype(output_ref.dtype)


def backward_kernel(
    plan,
    dims,
    lengths_ref,
    projected_ref,
    small_ref,
    signal_ref,
    write_pair,
    read_triple,
    step_ref,
    core_grad_ref,
    states_ref,
    out_grad_ref,
    in_grad_ref,
    signal_grad_ref,
    step_w_grad_ref,
    bias_grad_ref,
    decay_grad_ref,
    flat_ref,
    out_sum_ref,
    in_sum_ref,
    square_ref,
    offset_buf,
    decay_step,
    flows,
    grads,
    entering,
    grad_rows,
    scaled_rows,
    through_buf,
    scaled_buf,
    low_buf,
    rank_buf,
    write_buf,
    read_buf,
    *parts,
):
    rows, width = low_buf.shape
    rank = plan["step"][1]
    size = plan["decay"][1]
    tiles = width // lanes
    chunks = rows // chunk
    block = pl.program_id(0)
    reduce = Reduce(
        dims,
        [out_grad_ref, in_grad_ref],
        parts[2:12],
        parts[12:],
        parts[:2],
        [(0, 0), (1, 0)],
    )

    @pl.when(block == 0)
    def _():
        reduce.start()
        fill_offsets(lengths_ref, offset_buf, rows)
        write_buf[...] = jnp.zeros_like(write_buf)
        read_buf[...] = jnp.zeros_like(read_buf)
        rank_buf[...] = jnp.zeros_like(rank_buf)

    def before(index, at, carry):
        spot = pl.ds(pl.multiple_of(index * 4, 4), 4)
        inside = (offset_buf[at, :] > 0).reshape(4, chunk, lanes)
        for tile in range(tiles):
            step = step_ref[spot, :, cut(tile)]
            decay_step[spot, :, cut(tile)] = jnp.where(inside, step, far)
            signal = signal_ref[at, cut(tile)].astype(jnp.float32).reshape(4, chunk, lanes)
            high, low = high_low(step * signal)
            flows[spot, :, cut(tile)] = jnp.concatenate([high, low], axis=1).astype(flows.dtype)
            grads[spot, :, cut(tile)] = tripled(core_grad_ref[spot, :, cut(tile)])
        return carry

    row_loop(rows, 4 * chunk, before, 0)
    flows[chunks] = jnp.zeros_like(flows[chunks])
    grad_rows[...] = jnp.zeros_like(grad_rows)
    scaled_rows[...] = jnp.zeros_like(scaled_rows)
    rates = -jnp.exp(small_rows(small_ref, *plan["decay"])) * log2e
    rates = [rates[:, tile * lanes : (tile + 1) * lanes] for tile in range(tiles)]
    own = own_tokens(2 * chunk)
    ones = (own * (lax.broadcasted_iota(jnp.int32, own.shape, 0) < chunk)).astype(jnp.bfloat16)

    def enter(index):
        return contract(read_triple[index], grads[index], 0, 0)

    def kept(products):
        products = products * own
        return products[:chunk] + products[chunk:]

    def settle(index, slot):
        gone = grad_rows[slot]
        through = jnp.dot(
            write_pair[jnp.minimum(index, chunks - 1)], gone, preferred_element_type=jnp.float32
        )
        through_buf[index] = through[:chunk] + through[chunk:]
        scaled = jnp.dot(ones, scaled_rows[slot], preferred_element_type=jnp.float32)
        scaled_buf[index] = scaled[:chunk]
        write_buf[index] += kept(contract(flows[index], gone, 1, 1))

    def backward(position, carried):
        index = chunks - 1 - position
        slot = lax.rem(position, 2)
        entering[1 - slot] = enter(jnp.maximum(index - 1, 0))
        settle(index + 1, 1 - slot)
        base = index * chunk
        here = states_ref[pl.ds(base, chunk)].reshape(chunk * size, width)
        read_buf[index] += kept(contract(grads[index, : 2 * chunk], here, 1, 1))
        incoming, decay_sums = list(carried[0]), list(carried[1])
        for place in range(chunk - 1, -1, -1):
            now = base + place
            earlier = jnp.maximum(now - 1, 0) if place == 0 else now - 1
            lot = pl.ds(place * size, size)
            for tile in range(tiles):
                step_now = decay_step[index, pl.ds(place, 1), cut(tile)]
                grad_state = incoming[tile] + entering[slot, lot, cut(tile)]
                grad_rows[slot, lot, cut(tile)] = grad_state.astype(grad_rows.dtype)
                leaving = jnp.exp2(rates[tile] * step_now) * grad_state
                incoming[tile] = leaving
                weighted = leaving * states_ref[earlier, :, cut(tile)].astype(jnp.float32)
                scaled_rows[slot, lot, cut(tile)] = (weighted * rates[tile]).astype(scaled_rows.dtype)
                decay_sums[tile] = decay_sums[tile] + weighted * step_now
        return (tuple(incoming), tuple(decay_sums))

    entering[0] = enter(chunks - 1)
    carried = ((jnp.zeros((size, lanes), jnp.float32),) * tiles,) * 2
    for part in range(2):
        for number, moment in ((1, 1), (2, 4), (3, 6)):
            if moment % 2 == part:

                @pl.when(block == moment // 2)
                def _(number=number):
                    reduce.leg(number)

        carried = lax.fori_loop(part * chunks // 2, (part + 1) * chunks // 2, backward, carried)
    settle(0, (chunks - 1) % 2)
    for tile in range(tiles):
        decay_grad_ref[:, cut(tile)] = carried[1][tile] * rates[tile] * ln2
    skip = small_rows(small_ref, *plan["skip"])

    def after(index, at, carry):
        spot = pl.ds(pl.multiple_of(index * 4, 4), 4)
        sums = []
        for tile in range(tiles):
            signal = signal_ref[at, cut(tile)].astype(jnp.float32)
            step = step_ref[spot, :, cut(tile)].reshape(4 * chunk, lanes)
            through = through_buf[spot, :, cut(tile)].reshape(4 * chunk, lanes)
            scaled = scaled_buf[spot, :, cut(tile)].reshape(4 * chunk, lanes)
            core_grad = core_grad_ref[spot, :, cut(tile)].reshape(4 * chunk, lanes)
            grad_pre = (through * signal + ln2 * scaled) * slope_of(step)
            low_buf[at, cut(tile)] = grad_pre.astype(low_buf.dtype)
            signal_grad_ref[at, cut(tile)] = (
                through * step + skip[:, tile * lanes : (tile + 1) * lanes] * core_grad
            )
            sums.append(carry[tile] + eight(grad_pre))
        return tuple(sums)

    zero_rows = jnp.zeros((8, lanes), jnp.float32)
    sums = row_loop(rows, 4 * chunk, after, (zero_rows,) * tiles)
    for tile in range(tiles):
        bias_grad_ref[:, cut(tile)] = jnp.sum(sums[tile], axis=0, keepdims=True)
    step_w_grad_ref[...] = contract(
        projected_ref[:, :rank].astype(low_buf.dtype), low_buf[...], 0, 0
    )
    step_w = small_ref[pl.ds(plan["step"][0], rank), :]
    step_w = jnp.concatenate([step_w, jnp.zeros((lanes - rank, width), step_w.dtype)], axis=0)
    rank_buf[...] += contract(low_buf[...], step_w, 1, 1).reshape(chunks, chunk, lanes)

    @pl.when(block == pl.num_programs(0) - 1)
    def _():
        square_ref[...] = reduce.finish(None, None)[0]
        lane = lax.broadcasted_iota(jnp.int32, (lanes, lanes), 0)
        target = lax.broadcasted_iota(jnp.int32, (lanes, lanes), 1)
        sums = [jnp.sum(buffer[:chunks], axis=1).astype(jnp.bfloat16) for buffer in (write_buf, read_buf)]
        for token in range(chunk):
            total = None
            for number, summed in enumerate(sums):
                first = rank + number * size
                entry = target - first
                take = (entry >= 0) & (entry < size) & (lane == token * size + entry)
                piece = jnp.dot(summed, take.astype(jnp.bfloat16), preferred_element_type=jnp.float32)
                total = piece if total is None else total + piece
            rank_buf[:, token, :] += total
        flat_ref[...] = rank_buf[...].reshape(rows, lanes).astype(flat_ref.dtype)
        reduce.settle()
        out_sum_ref[...] = parts[0][...]
        in_sum_ref[...] = parts[1][...]


def back_kernel(
    plan,
    lengths_ref,
    tokens_ref,
    low_ref,
    gain_ref,
    small_ref,
    flat_ref,
    branch_ref,
    signal_ref,
    slope_ref,
    signal_grad_ref,
    gate_grad_ref,
    flipped_ref,
    branch_w,
    gate_w,
    step_w_grad_ref,
    bias_grad_ref,
    decay_grad_ref,
    skip_grad_ref,
    small_grad_ref,
    in_grad_ref,
    gain_grad_ref,
    tokens_grad_ref,
    offset_buf,
    conv_buf,
    mixed_buf,
    total,
):
    rows = tokens_ref.shape[0]
    width = branch_ref.shape[1]
    tiles = width // lanes
    block = pl.program_id(0)

    @pl.when(block == 0)
    def _():
        fill_offsets(lengths_ref, offset_buf, rows)

    taps = small_rows(small_ref, *plan["taps"])
    count = taps.shape[0]
    small_grad_ref[:lanes, :] = contract(flat_ref[...], signal_ref[...], 0, 0)

    def place_rows(name, values):
        first, tall = plan[name]
        small_grad_ref[first : first + tall, :] = values

    place_rows("step", step_w_grad_ref[...])
    place_rows("decay", decay_grad_ref[...])
    place_rows("bias", bias_grad_ref[...])
    place_rows("skip", skip_grad_ref[...])
    conv_buf[pl.ds(0, rows), :] = signal_grad_ref[...] + jnp.dot(
        flat_ref[...], small_ref[:lanes, :], preferred_element_type=jnp.float32
    )
    conv_buf[pl.ds(rows, 8), :] = jnp.zeros((8, width), jnp.float32)

    def through_conv(index, at, carry):
        sums = []
        for tile in range(tiles):
            grad_conv = conv_buf[at, cut(tile)] * slope_ref[at, cut(tile)]
            conv_buf[at, cut(tile)] = grad_conv
            sums.append(carry[tile] + eight(grad_conv))
        return tuple(sums)

    zero_rows = jnp.zeros((8, lanes), jnp.float32)
    sums = row_loop(rows, 32, through_conv, (zero_rows,) * tiles)
    for tile in range(tiles):
        first = plan["shift"][0]
        small_grad_ref[first : first + 1, cut(tile)] = jnp.sum(sums[tile], axis=0, keepdims=True)

    def to_branch(index, at, carry):
        longer = pl.ds(pl.multiple_of(index * 32, 32), 40)
        offsets = offset_buf[longer, :]
        result = []
        for tile in range(tiles):
            here = slice(tile * lanes, (tile + 1) * lanes)
            grads = conv_buf[longer, cut(tile)]
            branch = branch_ref[at, cut(tile)]
            summed = taps[count - 1 : count, here] * grads[:32]
            sums = [None] * count
            sums[count - 1] = carry[tile][count - 1] + eight(branch * grads[:32])
            for tap in range(count - 1):
                lag = count - 1 - tap
                moved = pltpu.roll(jnp.where(offsets >= lag, grads, 0.0), 40 - lag, 0)[:32]
                summed = summed + taps[tap : tap + 1, here] * moved
                sums[tap] = carry[tile][tap] + eight(branch * moved)
            mixed_buf[at, cut(tile)] = summed.astype(mixed_buf.dtype)
            result.append(tuple(sums))
        return tuple(result)

    sums = row_loop(rows, 32, to_branch, ((zero_rows,) * count,) * tiles)
    for tile in range(tiles):
        for tap in range(count):
            first = plan["taps"][0] + tap
            small_grad_ref[first : first + 1, cut(tile)] = jnp.sum(sums[tile][tap], axis=0, keepdims=True)
    in_grad_ref[...] = jnp.dot(
        flipped_ref[...], mixed_buf[...], preferred_element_type=jnp.float32
    ).astype(in_grad_ref.dtype)
    piece = contract(mixed_buf[...], branch_w[...], 1, 1) + contract(gate_grad_ref[...], gate_w[...], 1, 1)

    @pl.when(block == 0)
    def _():
        total[...] = piece

    @pl.when(block > 0)
    def _():
        total[...] += piece

    @pl.when(block == pl.num_programs(0) - 1)
    def _():
        def finish(index, at, carry):
            residual = tokens_ref[at, :].astype(jnp.float32)
            scale = lax.rsqrt(jnp.mean(residual * residual, axis=1, keepdims=True) + epsilon)
            grad_normed = total[at, :]
            weighted = grad_normed * gain_ref[...]
            inner = jnp.mean(weighted * residual, axis=1, keepdims=True)
            grad_y = low_ref[at, :].astype(jnp.float32)
            result = grad_y + (scale * weighted - residual * (scale * scale * scale) * inner)
            tokens_grad_ref[at, :] = result.astype(tokens_grad_ref.dtype)
            return carry + eight(grad_normed * residual * scale)

        gains = row_loop(rows, 16, finish, jnp.zeros((8, total.shape[1]), jnp.float32))
        gain_grad_ref[...] = jnp.sum(gains, axis=0, keepdims=True)


def finish_kernel(plan, names, branch_ref, gate_ref, out_ref, small_ref, norm_ref, *outs):
    middle = branch_ref.shape[1]
    outs[0][:, :middle] = branch_ref[...]
    outs[0][:, middle:] = gate_ref[...]
    outs[1][...] = out_ref[...]
    for name, target in zip(names, outs[2 : 2 + len(names)]):
        first, count = plan[name]
        if len(target.shape) == 1:
            target[...] = small_ref[first, : target.shape[0]]
        else:
            target[...] = small_ref[first : first + count, :]
    for index in range(2):
        outs[2 + len(names) + index][0, 0] = jnp.sum(norm_ref[index])


def shape(dims, kind=jnp.float32):
    return jax.ShapeDtypeStruct(dims, kind)


def compute_call(
    kernel, name, blocks, in_specs, out_specs, out_shape, scratch, flops, operands, collective_id=None
):
    return pl.pallas_call(
        kernel,
        grid=(blocks,),
        in_specs=in_specs,
        out_specs=out_specs,
        out_shape=out_shape,
        scratch_shapes=scratch,
        compiler_params=pltpu.CompilerParams(
            dimension_semantics=("arbitrary",),
            vmem_limit_bytes=62 * 1024 * 1024,
            collective_id=collective_id,
            has_side_effects=collective_id is not None,
        ),
        cost_estimate=pl.CostEstimate(flops=flops, bytes_accessed=40 << 20, transcendentals=0),
        name=name,
    )(*operands)


class Place:
    def __init__(self, dims, swapped=False):
        depth, tall, wide = dims
        self.dims = dims
        self.core = lax.axis_index("wide")
        self.me = lax.axis_index("narrow")
        self.across = lax.rem(self.me, wide)
        self.up = lax.rem(lax.div(self.me, wide), tall)
        self.deep = lax.div(self.me, wide * tall)
        side = 1 - self.core if swapped else self.core
        turn = side if tall == wide else 0
        self.second = (1 + turn * (wide - 1), self.across + turn * (self.up - self.across), wide)
        self.third = (wide - turn * (wide - 1), self.up + turn * (self.across - self.up), tall)
        self.spans = (depth, wide, tall)
        self.other = {"wide": 1 - self.core}

    def at(self, d, e, f):
        depth, tall, wide = self.dims
        return (
            lax.rem(self.deep + d, depth) * (tall * wide)
            + lax.rem(self.second[1] + e, self.second[2]) * self.second[0]
            + lax.rem(self.third[1] + f, self.third[2]) * self.third[0]
        )

    def behind(self, d, e, f):
        return self.at(*((size - hop) % size for size, hop in zip(self.spans, (d, e, f))))

    def slot(self, d, e, f):
        return (d * self.spans[1] + e) * self.spans[2] + f

    def moves(self):
        return [
            (d, e, f)
            for d in range(self.spans[0])
            for e in range(self.spans[1])
            for f in range(self.spans[2])
        ]

    def greet(self):
        barrier = pltpu.get_barrier_semaphore()
        pl.semaphore_signal(barrier, inc=1, device_id=self.other, device_id_type=pl.DeviceIdType.MESH)
        peers = 1
        for axis, size in enumerate(self.spans):
            for hop in range(1, size):
                move = [0, 0, 0]
                move[axis] = hop
                pl.semaphore_signal(
                    barrier,
                    inc=1,
                    device_id={"narrow": self.at(*move)},
                    device_id_type=pl.DeviceIdType.MESH,
                )
                peers += 1
        pl.semaphore_wait(barrier, peers)


def half_of(width, core):
    return pl.ds(pl.multiple_of(core * (width // 2), lanes), width // 2)


def side_of(block, side):
    if len(block.shape) == 3:
        return block.at[side]
    return block.at[:, half_of(block.shape[1], side)]


def half_shape(array):
    return array.shape[2:] if len(array.shape) == 4 else (array.shape[1], array.shape[2] // 2)


def remote(source, target, send_sem, recv_sem, device):
    return pltpu.make_async_remote_copy(
        src_ref=source,
        dst_ref=target,
        send_sem=send_sem,
        recv_sem=recv_sem,
        device_id=device,
        device_id_type=pl.DeviceIdType.MESH,
    )


class Gather:
    def __init__(self, dims, own, whole, sems):
        self.dims, self.own, self.whole = dims, own, whole
        self.local_sem, self.send_sem, self.recv_sem, self.core_send, self.core_recv = sems

    @staticmethod
    def scratch(count, dims):
        number = dims[0] * dims[1] * dims[2]
        return [pltpu.SemaphoreType.DMA((count,))] + [pltpu.SemaphoreType.DMA((count, number))] * 4

    def onward(self, place, which, move):
        d, e, f = move
        number = place.behind(*move)
        target = side_of(self.whole[which].at[number], place.core)
        source = side_of(self.own[which], place.core) if move == (0, 0, 0) else target
        hops = []
        if f == 0:
            hops += [((0, 0, hop), (d, e, hop)) for hop in range(1, place.spans[2])]
        if f == 0 and e == 0:
            hops += [((0, hop, 0), (d, hop, 0)) for hop in range(1, place.spans[1])]
        if move == (0, 0, 0):
            hops += [((hop, 0, 0), (hop, 0, 0)) for hop in range(1, place.spans[0])]
        for step, landing in reversed(hops):
            index = place.slot(*landing)
            remote(
                source,
                target,
                self.send_sem.at[which, index],
                self.recv_sem.at[which, index],
                {"narrow": place.at(*step)},
            ).start()
        if move != (0, 0, 0):
            index = place.slot(*move)
            remote(
                source,
                target,
                self.core_send.at[which, index],
                self.core_recv.at[which, index],
                place.other,
            ).start()

    def local(self, place, which):
        return pltpu.make_async_copy(
            self.own[which], self.whole[which].at[place.at(0, 0, 0)], self.local_sem.at[which]
        )

    def start(self):
        place = Place(self.dims)
        place.greet()
        for which in range(len(self.own)):
            self.onward(place, which, (0, 0, 0))
        for which in range(len(self.own)):
            self.local(place, which).start()

    def leg(self, number):
        place = Place(self.dims)
        for which in range(len(self.own)):
            for move in place.moves():
                d, e, f = move
                if (number == 3) != (f > 0):
                    continue
                if number < 3 and (number == 2) != (e > 0):
                    continue
                if move == (0, 0, 0):
                    continue
                index = place.slot(*move)
                landed = side_of(self.whole[which].at[place.behind(*move)], place.core)
                remote(
                    landed,
                    landed,
                    self.send_sem.at[which, index],
                    self.recv_sem.at[which, index],
                    place.other,
                ).wait_recv()
                self.onward(place, which, move)

    def finish(self):
        place = Place(self.dims)
        mirror = Place(self.dims, swapped=True)
        for which in range(len(self.own)):
            for move in place.moves():
                if move == (0, 0, 0):
                    continue
                index = place.slot(*move)
                landed = side_of(self.whole[which].at[mirror.behind(*move)], 1 - place.core)
                handed = remote(
                    landed,
                    landed,
                    self.core_send.at[which, index],
                    self.core_recv.at[which, index],
                    place.other,
                )
                handed.wait_recv()
                handed.wait_send()
                remote(
                    landed,
                    landed,
                    self.send_sem.at[which, index],
                    self.recv_sem.at[which, index],
                    place.other,
                ).wait_send()
            self.local(place, which).wait()


class Reduce:
    def __init__(self, dims, grads, held, sems, results, targets):
        self.dims, self.grads = dims, grads
        count = len(grads)
        self.mine, self.swapped, self.third, self.second, self.first = (
            held[index * count : (index + 1) * count] for index in range(5)
        )
        (
            self.local_sem,
            self.core_send,
            self.core_recv,
            self.leg_send,
            self.leg_recv,
            self.last_send,
            self.last_recv,
        ) = sems
        self.results, self.targets = results, targets

    @staticmethod
    def rooms(dims, grads):
        depth, tall, wide = dims
        number = depth * tall * wide
        places = (number, number, depth * wide * (tall - 1), depth * (wide - 1), depth - 1)
        return [
            pltpu.VMEM((room,) + tuple(half_shape(grad)), grad.dtype) for room in places for grad in grads
        ]

    @staticmethod
    def sems(dims, count):
        number = dims[0] * dims[1] * dims[2]
        return [pltpu.SemaphoreType.DMA((count, number))] * 5 + [pltpu.SemaphoreType.DMA((count,))] * 2

    def order(self, place):
        return sorted(place.moves(), key=lambda item: (item[2] == 0, item[1] == 0, item[0] == 0))

    def share(self, which, side):
        result, first = self.targets[which]
        if len(self.grads[which].shape) == 4:
            return self.results[result].at[side]
        width = self.grads[which].shape[2]
        columns = pl.ds(pl.multiple_of(first + side * (width // 2), lanes), width // 2)
        return self.results[result].at[:, columns]

    def load(self, place, which, move):
        return pltpu.make_async_copy(
            side_of(self.grads[which].at[place.at(*move)], place.core),
            self.mine[which].at[place.slot(*move)],
            self.local_sem.at[which, place.slot(*move)],
        )

    def swap(self, place, which, move, mirror):
        index = place.slot(*move)
        return remote(
            side_of(self.grads[which].at[mirror.at(*move)], 1 - place.core),
            self.swapped[which].at[index],
            self.core_send.at[which, index],
            self.core_recv.at[which, index],
            place.other,
        )

    def start(self):
        place, mirror = Place(self.dims), Place(self.dims, swapped=True)
        place.greet()
        for move in self.order(place):
            for which in range(len(self.grads)):
                self.swap(place, which, move, mirror).start()
                self.load(place, which, move).start()

    def landing(self, place, which, move):
        d, e, f = move
        if f > 0:
            return self.third[which].at[(d * place.spans[1] + e) * (place.spans[2] - 1) + f - 1], (0, 0, f)
        if e > 0:
            return self.second[which].at[d * (place.spans[1] - 1) + e - 1], (0, e, 0)
        return self.first[which].at[d - 1], (d, 0, 0)

    def hop(self, place, which, move):
        landing, step = self.landing(place, which, move)
        index = place.slot(*move)
        return remote(
            self.mine[which].at[index],
            landing,
            self.leg_send.at[which, index],
            self.leg_recv.at[which, index],
            {"narrow": place.at(*step)},
        )

    def collect(self, place, which, move):
        d, e, f = move
        index = place.slot(*move)
        self.load(place, which, move).wait()
        handed = self.swapped[which].at[index]
        remote(
            handed, handed, self.core_send.at[which, index], self.core_recv.at[which, index], place.other
        ).wait_recv()
        parts = [handed]
        coming = []
        if f == 0:
            coming += [(d, e, hop) for hop in range(1, place.spans[2])]
        if f == 0 and e == 0:
            coming += [(d, hop, 0) for hop in range(1, place.spans[1])]
        if move == (0, 0, 0):
            coming += [(hop, 0, 0) for hop in range(1, place.spans[0])]
        for source in coming:
            self.hop(place, which, source).wait_recv()
            parts.append(self.landing(place, which, source)[0])
        return parts

    def added(self, place, which, move, parts, store, carry):
        block = self.mine[which].at[place.slot(*move)]
        rows = block.shape[0]
        group = min(rows, 16)

        def some(index, carry):
            at_rows = pl.ds(pl.multiple_of(index * group, group), group)
            total = block[at_rows, :].astype(jnp.float32)
            for part in parts:
                total = total + part[at_rows, :].astype(jnp.float32)
            return store(block, at_rows, total, carry)

        return lax.fori_loop(0, rows // group, some, carry)

    def leg(self, number):
        place = Place(self.dims)

        def keep(block, at_rows, total, carry):
            block[at_rows, :] = total.astype(block.dtype)
            return carry

        for move in self.order(place)[:-1]:
            d, e, f = move
            if number != (1 if f > 0 else 2 if e > 0 else 3):
                continue
            for which in range(len(self.grads)):
                parts = self.collect(place, which, move)
                self.added(place, which, move, parts, keep, 0)
                self.hop(place, which, move).start()

    def finish(self, plain_at, plain_ref):
        place, mirror = Place(self.dims), Place(self.dims, swapped=True)
        squares = (jnp.zeros((8, lanes), jnp.float32),) * 2
        for which in range(len(self.grads)):
            parts = self.collect(place, which, (0, 0, 0))
            result = self.share(which, place.core)

            def store(block, at_rows, total, carry, which=which, result=result):
                result[at_rows, :] = total
                kept, plain = carry
                squared = total * total
                if which == plain_at:
                    marked = squared * plain_ref[place.core, at_rows, :]
                    plain = plain + folded_squares(marked)
                    squared = squared - marked
                return (kept + folded_squares(squared), plain)

            squares = self.added(place, which, (0, 0, 0), parts, store, squares)
            remote(result, result, self.last_send.at[which], self.last_recv.at[which], place.other).start()
        return squares

    def settle(self):
        place, mirror = Place(self.dims), Place(self.dims, swapped=True)
        for which in range(len(self.grads)):
            result = self.share(which, 1 - place.core)
            last = remote(result, result, self.last_send.at[which], self.last_recv.at[which], place.other)
            last.wait_recv()
            last.wait_send()
            for move in place.moves():
                self.swap(place, which, move, mirror).wait_send()
                if move != (0, 0, 0):
                    self.hop(place, which, move).wait_send()


def folded_squares(values):
    total = None
    if values.shape[1] < lanes:
        first = lax.broadcasted_iota(jnp.int32, (values.shape[0], lanes), 1) == 0
        values = jnp.where(first, jnp.sum(values, axis=1, keepdims=True), 0.0)
    for row in range(0, values.shape[0], 8):
        for column in range(0, values.shape[1], lanes):
            piece = values[row : row + 8, column : column + lanes]
            total = piece if total is None else total + piece
    return total


def gather_kernel(dims, plan, names, *refs):
    smalls, bigs = refs[: len(names)], refs[len(names) : len(names) + 1]
    refs = refs[len(names) + 1 :]
    whole, own, pack_buf, sems = refs[:2], refs[2:4], refs[4], refs[5:]
    pack_buf[...] = jnp.zeros_like(pack_buf)
    for name, ref in zip(names, smalls):
        first, tall = plan[name]
        pack_buf[first : first + tall, : ref.shape[1]] = ref[...]
    tall = pack_buf.shape[0] // 2
    for side in range(2):
        own[0][side] = pack_buf[side * tall : (side + 1) * tall, :].astype(own[0].dtype)
    own[1][...] = bigs[0][...].astype(own[1].dtype)
    gather = Gather(dims, own, whole, sems)
    gather.start()
    for number in (1, 2, 3):
        gather.leg(number)
    gather.finish()


def gather_weights(dims, plan, smalls, big):
    number = dims[0] * dims[1] * dims[2]
    names = list(smalls)
    width = smalls["select"].shape[1]
    owned = [shape((2, plan["rows"] // 2, width), jnp.bfloat16), shape(big.shape, jnp.bfloat16)]
    inside = pl.BlockSpec(memory_space=pltpu.VMEM)
    return pl.pallas_call(
        functools.partial(gather_kernel, dims, plan, names),
        in_specs=[inside] * (len(names) + 1),
        out_specs=[pl.BlockSpec(memory_space=pl.ANY)] * 2,
        out_shape=[shape((number,) + kind.shape, kind.dtype) for kind in owned],
        scratch_shapes=[pltpu.VMEM(kind.shape, kind.dtype) for kind in owned]
        + [pltpu.VMEM((plan["rows"], width), jnp.float32)]
        + Gather.scratch(2, dims),
        compiler_params=pltpu.CompilerParams(
            collective_id=0, has_side_effects=True, vmem_limit_bytes=60 * 1024 * 1024
        ),
        name="gather_weights",
    )(*smalls.values(), big)


def reduce_kernel(dims, count, results, targets, plain_at, *refs):
    grads, plain_ref, earlier_ref = refs[:count], refs[count], refs[count + 1]
    refs = refs[count + 2 :]
    sums, norms = refs[:results], refs[results]
    refs = refs[results + 1 :]
    held, buffers = refs[: 5 * count], refs[5 * count : 5 * count + 4]
    refs = refs[5 * count + 4 :]
    sems, (norm_send, norm_recv) = refs[:7], refs[7:]
    reduce = Reduce(dims, grads, held, sems, sums, targets)
    reduce.start()
    for number in (1, 2, 3):
        reduce.leg(number)
    kept, plain = reduce.finish(plain_at, plain_ref)
    running = jnp.stack([kept + earlier_ref[...], plain])

    place = Place(dims)
    depth, tall, wide = dims
    plane = tall * wide
    me = place.me
    stages = (
        (buffers[0], 2, place.core, lambda spot: {"wide": spot}),
        (buffers[1], depth, place.deep, lambda spot: {"narrow": spot * plane + lax.rem(me, plane)}),
        (buffers[2], wide, place.across, lambda spot: {"narrow": me - place.across + spot}),
        (buffers[3], tall, place.up, lambda spot: {"narrow": me + (spot - place.up) * wide}),
    )
    pending = []
    first = 0
    for buffer, size, mine_at, device in stages:
        buffer[mine_at] = running
        for hop in range(1, size):
            copy = remote(
                buffer.at[mine_at],
                buffer.at[mine_at],
                norm_send.at[first + hop - 1],
                norm_recv.at[first + hop - 1],
                device(lax.rem(mine_at + hop, size)),
            )
            copy.start()
            pending.append(copy)
        for hop in range(1, size):
            came = lax.rem(mine_at + size - hop, size)
            remote(
                buffer.at[came],
                buffer.at[came],
                norm_send.at[first + hop - 1],
                norm_recv.at[first + hop - 1],
                device(came),
            ).wait_recv()
        first += size - 1
        running = buffer[0]
        for spot in range(1, size):
            running = running + buffer[spot]
    norms[...] = running
    reduce.settle()
    for copy in pending:
        copy.wait_send()


def sum_shapes(grads, targets):
    sums = []
    for index in range(1 + max(target[0] for target in targets)):
        members = [grad for grad, target in zip(grads, targets) if target[0] == index]
        if len(members[0].shape) == 4:
            sums.append(shape(members[0].shape[1:]))
        else:
            sums.append(shape((members[0].shape[1], sum(grad.shape[2] for grad in members))))
    return sums


def reduce_grads(dims, grads, targets, plain_mask, plain_at, earlier):
    depth, tall, wide = dims
    count = len(grads)
    anywhere = pl.BlockSpec(memory_space=pl.ANY)
    inside = pl.BlockSpec(memory_space=pltpu.VMEM)
    sums = sum_shapes(grads, targets)
    result = pl.pallas_call(
        functools.partial(reduce_kernel, dims, count, len(sums), targets, plain_at),
        in_specs=[anywhere] * count + [inside] * 2,
        out_specs=[inside] * (len(sums) + 1),
        out_shape=sums + [shape((2, 8, lanes))],
        scratch_shapes=Reduce.rooms(dims, grads)
        + [pltpu.VMEM((size, 2, 8, lanes), jnp.float32) for size in (2, depth, wide, tall)]
        + Reduce.sems(dims, count)
        + [pltpu.SemaphoreType.DMA((depth + tall + wide,))] * 2,
        compiler_params=pltpu.CompilerParams(
            collective_id=1, has_side_effects=True, vmem_limit_bytes=56 * 1024 * 1024
        ),
        name="reduce_grads",
    )(*grads, plain_mask, earlier)
    return result[: len(sums)], result[len(sums)]


def grid_of(mesh):
    number = mesh.shape["narrow"]
    places = [getattr(device, "coords", None) for device in mesh.devices[0]]
    if all(place is not None for place in places):
        sizes = [len({place[axis] for place in places}) for axis in (2, 1, 0)]
        if sizes[0] * sizes[1] * sizes[2] == number:
            return tuple(sizes)
    side = round((number / 2) ** (1 / 3))
    return (2 * side, side, side) if 2 * side**3 == number else (number, 1, 1)


def plan_of(select_rows, state_size, tap_count, step_rows):
    plan, first = {}, 0
    for name, tall in (
        ("select", select_rows),
        ("decay", state_size),
        ("taps", tap_count),
        ("shift", 1),
        ("bias", 1),
        ("skip", 1),
        ("gain", 1),
    ):
        plan[name] = (first, tall)
        first += tall
    plan["step"] = (lanes, step_rows)
    plan["rows"] = -(-(lanes + step_rows) // 32) * 32
    return plan


def per_device(
    dims,
    tokens,
    cotangent,
    loss_mask,
    seq_lengths,
    norm_gain,
    in_proj,
    conv_weight,
    conv_bias,
    select_proj,
    step_proj,
    step_bias,
    decay_log,
    skip_scale,
    out_proj,
):
    half = jnp.bfloat16
    piece = skip_scale.shape[0]
    gain_piece = norm_gain.shape[0]
    rank, size = step_proj.shape[0], decay_log.shape[0]
    plan = plan_of(select_proj.shape[0], size, conv_weight.shape[0], rank)
    small_blocks, in_blocks = gather_weights(
        dims,
        plan,
        {
            "select": select_proj,
            "decay": decay_log,
            "taps": conv_weight,
            "shift": conv_bias[None],
            "bias": step_bias[None],
            "skip": skip_scale[None],
            "gain": norm_gain[None],
            "step": step_proj,
        },
        in_proj,
    )
    in_whole = in_blocks.reshape(-1, in_blocks.shape[2])
    small_blocks = small_blocks.reshape(-1, plan["rows"], piece)
    small = jnp.swapaxes(small_blocks, 0, 1).reshape(plan["rows"], -1)
    gain_value = small_blocks[:, plan["gain"][0], :gain_piece].reshape(1, -1).astype(jnp.float32)

    rows, model = tokens.shape
    inner = small.shape[1]
    width = 4 * lanes
    blocks = inner // width
    chunks = rows // chunk
    mask_row = loss_mask[None]

    whole = pl.BlockSpec(memory_space=pltpu.VMEM)
    tall = pl.BlockSpec((rows, width), lambda b: (0, b))
    deep = pl.BlockSpec((chunks, chunk, width), lambda b: (0, 0, b))
    lead = pl.BlockSpec((rows, size, width), lambda b: (0, 0, b))
    first_w = pl.BlockSpec((model, width), lambda b: (0, b))
    second_w = pl.BlockSpec((model, width), lambda b: (0, b + blocks))
    out_w = pl.BlockSpec((width, model), lambda b: (b, 0))

    def thin(height):
        return pl.BlockSpec((height, width), lambda b: (0, b))

    def fixed(*dims_of):
        return pl.BlockSpec(dims_of, lambda b: (0,) * len(dims_of))

    scalars = pl.BlockSpec(memory_space=pltpu.SMEM)
    offset_buf = pltpu.VMEM((rows + 8, lanes), jnp.int32)
    packed = thin(plan["rows"])

    pair, triple = (chunks, 2 * chunk, lanes), (chunks, 4 * chunk, lanes)
    (
        branch,
        gate_pre,
        signal,
        slope,
        projected,
        flipped,
        grad_low,
        write_pair,
        write_triple,
        read_pair,
        read_triple,
    ) = compute_call(
        functools.partial(front_kernel, plan),
        "front",
        blocks,
        [scalars, whole, whole, whole, whole, packed, first_w, second_w],
        [tall, tall, tall, tall, fixed(rows, lanes), fixed(model, rows), fixed(rows, model)]
        + [fixed(*pair), fixed(*triple)] * 2,
        [
            shape((rows, inner)),
            shape((rows, inner)),
            shape((rows, inner), half),
            shape((rows, inner)),
            shape((rows, lanes)),
            shape((model, rows), half),
            shape((rows, model), half),
        ]
        + [shape(pair, half), shape(triple, half)] * 2,
        [pltpu.VMEM((rows, model), half), offset_buf],
        4 * rows * model * inner,
        (seq_lengths, tokens, cotangent, mask_row, gain_value, small, in_whole, in_whole),
    )
    row_block = pltpu.VMEM((chunks, chunk, width), jnp.float32)
    spare_block = pltpu.VMEM((chunks + 1, chunk, width), jnp.float32)
    number = small_blocks.shape[0]
    anywhere = pl.BlockSpec(memory_space=pl.ANY)
    states, step, core, out_blocks = compute_call(
        functools.partial(forward_kernel, plan, dims),
        "forward",
        blocks,
        [scalars, whole, packed, tall, whole, whole, whole],
        [lead, deep, deep, anywhere],
        [
            shape((rows, size, inner), half),
            shape((chunks, chunk, inner)),
            shape((chunks, chunk, inner)),
            shape((number,) + out_proj.shape, half),
        ],
        [
            offset_buf,
            pltpu.VMEM((rows, width), jnp.float32),
            row_block,
            pltpu.VMEM((chunks + 1, 4 * chunk, width), half),
            pltpu.VMEM((2, chunk * size, width), jnp.float32),
            pltpu.VMEM(out_proj.shape, half),
        ]
        + Gather.scratch(1, dims),
        15 * rows * inner * size,
        (seq_lengths, projected, small, signal, write_triple, read_pair, out_proj),
        collective_id=2,
    )
    core_grad, gate_grad, grad_skip, grad_outw, grad_in_gate, output = compute_call(
        functools.partial(middle_kernel, plan),
        "middle",
        blocks,
        [deep, packed, tall, tall, whole, out_w, whole, whole],
        [deep, tall, thin(1), out_w, first_w, fixed(rows, model)],
        [
            shape((chunks, chunk, inner)),
            shape((rows, inner), half),
            shape((1, inner)),
            shape((inner, model), half),
            shape((model, inner), half),
            shape((rows, model), half),
        ],
        [
            pltpu.VMEM((rows, width), jnp.float32),
            pltpu.VMEM((rows, width), half),
            pltpu.VMEM((rows, model), jnp.float32),
        ],
        8 * rows * model * inner,
        (core, small, signal, gate_pre, grad_low, out_blocks.reshape(inner, model), flipped, tokens),
    )
    split = in_blocks.shape[:2] + (inner,)
    early_grads = [grad_outw.reshape(out_blocks.shape), grad_in_gate.reshape(split)]
    early_sums = sum_shapes(early_grads, [(0, 0), (1, 0)])
    (
        signal_grad,
        grad_stepw,
        grad_bias,
        grad_decaylog,
        flat,
        out_sum,
        in_gate_sum,
        early_squares,
    ) = compute_call(
        functools.partial(backward_kernel, plan, dims),
        "backward",
        blocks,
        [scalars, whole, packed, tall, whole, whole, deep, deep, lead, anywhere, anywhere],
        [tall, thin(rank), thin(1), thin(size), fixed(rows, lanes)]
        + [whole] * 3,
        [
            shape((rows, inner)),
            shape((rank, inner)),
            shape((1, inner)),
            shape((size, inner)),
            shape((rows, lanes), half),
            *early_sums,
            shape((8, lanes)),
        ],
        [
            offset_buf,
            row_block,
            pltpu.VMEM((chunks + 1, 2 * chunk, width), half),
            pltpu.VMEM((chunks, 4 * chunk, width), half),
            pltpu.VMEM((2, chunk * size, width), jnp.float32),
            pltpu.VMEM((2, chunk * size, width), half),
            pltpu.VMEM((2, chunk * size, width), half),
            spare_block,
            spare_block,
            pltpu.VMEM((rows, width), half),
            pltpu.VMEM((chunks, chunk, lanes), jnp.float32),
            pltpu.VMEM((chunks + 1, chunk, lanes), jnp.float32),
            pltpu.VMEM((chunks, chunk, lanes), jnp.float32),
        ]
        + [pltpu.VMEM(early.shape, early.dtype) for early in early_sums]
        + Reduce.rooms(dims, early_grads)
        + Reduce.sems(dims, 2),
        40 * rows * inner * size,
        (seq_lengths, projected, small, signal, write_pair, read_triple, step, core_grad, states, *early_grads),
        collective_id=3,
    )

    small_grad, grad_in_branch, grad_gain, grad_tokens = compute_call(
        functools.partial(back_kernel, plan),
        "back",
        blocks,
        [scalars, whole, whole, whole, packed, whole, tall, tall, tall, tall, tall, whole, first_w, second_w]
        + [thin(rank), thin(1), thin(size), thin(1)],
        [packed, first_w, fixed(1, model), fixed(rows, model)],
        [
            shape((plan["rows"], inner)),
            shape((model, inner), half),
            shape((1, model)),
            shape((rows, model), half),
        ],
        [
            offset_buf,
            pltpu.VMEM((rows + 8, width), jnp.float32),
            pltpu.VMEM((rows, width), half),
            pltpu.VMEM((rows, model), jnp.float32),
        ],
        8 * rows * model * inner,
        (
            seq_lengths,
            tokens,
            grad_low,
            gain_value,
            small,
            flat,
            branch,
            signal,
            slope,
            signal_grad,
            gate_grad,
            flipped,
            in_whole,
            in_whole,
            grad_stepw,
            grad_bias,
            grad_decaylog,
            grad_skip,
        ),
    )

    gain_rows = jnp.pad(grad_gain.reshape(number, 1, gain_piece), ((0, 0), (0, 0), (0, piece - gain_piece)))
    place = plan["gain"][0]
    small_grad = jnp.swapaxes(small_grad.reshape(plan["rows"], number, piece), 0, 1) + jnp.pad(
        gain_rows, ((0, 0), (place, plan["rows"] - place - 1), (0, 0))
    )
    plain_rows = np.zeros((plan["rows"], piece), np.float32)
    for name in ("bias", "decay", "skip"):
        first, count = plan[name]
        plain_rows[first : first + count] = 1.0
    halves = (2, plan["rows"] // 2, piece)
    (in_branch_sum, small_sum), norms = reduce_grads(
        dims,
        [grad_in_branch.reshape(split), small_grad.reshape((number,) + halves)],
        [(0, 0), (1, 0)],
        jnp.asarray(plain_rows.reshape(halves)),
        1,
        early_squares,
    )
    names = ("gain", "taps", "shift", "select", "step", "bias", "decay", "skip")
    own = (norm_gain, conv_weight, conv_bias, select_proj, step_proj, step_bias, decay_log, skip_scale)
    in_grad, out_grad, gain_grad, *small_grads, decay_sq, plain_sq = pl.pallas_call(
        functools.partial(finish_kernel, plan, names),
        in_specs=[whole] * 5,
        out_specs=[whole] * (2 + len(names)) + [scalars] * 2,
        out_shape=[shape(in_proj.shape), shape(out_proj.shape)]
        + [shape(array.shape) for array in own]
        + [shape((1, 1))] * 2,
        name="finish",
    )(in_branch_sum, in_gate_sum, out_sum, small_sum.reshape(plan["rows"], piece), norms)
    return (
        output,
        grad_tokens,
        gain_grad,
        in_grad,
        *small_grads,
        out_grad,
        decay_sq[0, 0],
        plain_sq[0, 0],
    )


def solution(mesh):
    placed = (
        P(("wide", "narrow"), None),
        P(("wide", "narrow"), None),
        P(("wide", "narrow")),
        P(("wide", "narrow"), None),
        P("narrow"),
        P("narrow", None),
        P(None, "narrow"),
        P("narrow"),
        P(None, "narrow"),
        P(None, "narrow"),
        P("narrow"),
        P(None, "narrow"),
        P("narrow"),
        P("narrow", None),
    )
    return jax.shard_map(
        functools.partial(per_device, grid_of(mesh)),
        mesh=mesh,
        in_specs=placed,
        out_specs=(
            P(("wide", "narrow"), None),
            P(("wide", "narrow"), None),
            P("narrow"),
            P("narrow", None),
            P(None, "narrow"),
            P("narrow"),
            P(None, "narrow"),
            P(None, "narrow"),
            P("narrow"),
            P(None, "narrow"),
            P("narrow"),
            P("narrow", None),
            P(),
            P(),
        ),
        check_vma=False,
    )
```

```python
import functools
import math

import jax
import jax.numpy as jnp
import numpy as np
from jax import lax
from jax.experimental import pallas as pl
from jax.experimental.pallas import tpu as pltpu
from jax.sharding import PartitionSpec as P

epsilon = 1e-05
chunk = 8
lanes = 128
log2e = math.log2(math.e)
ln2 = math.log(2.0)
far = 1e30


def contract(left, right, left_dim, right_dim):
    return lax.dot_general(
        left, right, (((left_dim,), (right_dim,)), ((), ())), preferred_element_type=jnp.float32
    )


def row_loop(rows, group, body, initial):
    def some(index, carry):
        return body(index, pl.ds(pl.multiple_of(index * group, group), group), carry)

    return lax.fori_loop(0, rows // group, some, initial)


def cut(tile):
    return pl.ds(tile * lanes, lanes)


def sigmoid(values):
    return 0.5 * jnp.tanh(0.5 * values) + 0.5


def softplus(values):
    small = jnp.exp(-jnp.abs(values))
    series = small * (1.0 - small * (0.5 - small * (1.0 / 3.0 - 0.25 * small)))
    return jnp.maximum(values, 0.0) + jnp.where(small < 0.03, series, jnp.log(1.0 + small))


def slope_of(step):
    series = step * (1.0 - step * (0.5 - step * (1.0 / 6.0 - step * (1.0 / 24.0))))
    return jnp.where(step < 0.03, series, 1.0 - jnp.exp(-step))


def fill_offsets(lengths_ref, offset_buf, rows):
    place = lax.broadcasted_iota(jnp.int32, offset_buf.shape, 0)
    start = jnp.zeros(offset_buf.shape, jnp.int32)
    ahead = jnp.int32(0)
    for index in range(lengths_ref.shape[1] - 1):
        ahead = ahead + lengths_ref[0, index]
        start = jnp.where(place >= ahead, ahead, start)
    offset_buf[...] = jnp.where(place < rows, place - start, 0)


def small_rows(small_ref, first, count):
    base = first // 16 * 16
    tall = -(-(first + count - base) // 16) * 16
    return small_ref[base : base + tall, :].astype(jnp.float32)[first - base : first - base + count]


def eight(values):
    total = values[:8]
    for row in range(8, values.shape[0], 8):
        total = total + values[row : row + 8]
    return total


def conv_rows(index, at, group, tile, branch_ref, offset_buf, taps, shift):
    count = taps.shape[0]
    here = slice(tile * lanes, (tile + 1) * lanes)
    current = branch_ref[at, cut(tile)]
    before = branch_ref[pl.ds(pl.multiple_of(jnp.maximum(index * group - 8, 0), 8), 8), cut(tile)]
    both = jnp.concatenate([before, current], axis=0)
    offsets = offset_buf[at, :]
    summed = shift[:, here] + taps[count - 1 : count, here] * current
    for tap in range(count - 1):
        lag = count - 1 - tap
        read = jnp.where(offsets >= lag, pltpu.roll(both, lag, 0)[8:], 0.0)
        summed = summed + taps[tap : tap + 1, here] * read
    return summed


def front_kernel(
    plan,
    lengths_ref,
    tokens_ref,
    cotangent_ref,
    mask_ref,
    gain_ref,
    small_ref,
    branch_w,
    gate_w,
    branch_ref,
    gate_ref,
    signal_ref,
    slope_ref,
    projected_ref,
    flipped_ref,
    low_ref,
    write_pair,
    write_triple,
    read_pair,
    read_triple,
    normed_buf,
    offset_buf,
):
    rows = tokens_ref.shape[0]
    width = branch_ref.shape[1]
    block = pl.program_id(0)

    @pl.when(block == 0)
    def _():
        fill_offsets(lengths_ref, offset_buf, rows)

        def norm(index, at, carry):
            residual = tokens_ref[at, :].astype(jnp.float32)
            scale = lax.rsqrt(jnp.mean(residual * residual, axis=1, keepdims=True) + epsilon)
            normed_buf[at, :] = (residual * scale * gain_ref[...]).astype(normed_buf.dtype)
            return carry

        row_loop(rows, 16, norm, 0)
        flipped_ref[...] = normed_buf[...].T
        projected_ref[...] = jnp.zeros_like(projected_ref)
        down = lax.broadcasted_iota(jnp.int32, (rows, rows), 0)
        along = lax.broadcasted_iota(jnp.int32, (rows, rows), 1)
        diagonal = jnp.where(down == along, mask_ref[...].astype(jnp.float32), 0.0).astype(low_ref.dtype)
        low_ref[...] = jnp.dot(
            diagonal, cotangent_ref[...], preferred_element_type=jnp.float32
        ).astype(low_ref.dtype)

    branch_ref[...] = jnp.dot(normed_buf[...], branch_w[...], preferred_element_type=jnp.float32)
    gate_ref[...] = jnp.dot(normed_buf[...], gate_w[...], preferred_element_type=jnp.float32)
    taps = small_rows(small_ref, *plan["taps"])
    shift = small_rows(small_ref, *plan["shift"])

    def some(index, at, carry):
        for tile in range(width // lanes):
            summed = conv_rows(index, at, 32, tile, branch_ref, offset_buf, taps, shift)
            sigma = sigmoid(summed)
            active = summed * sigma
            signal_ref[at, cut(tile)] = active.astype(signal_ref.dtype)
            slope_ref[at, cut(tile)] = sigma + active * (1.0 - sigma)
        return carry

    row_loop(rows, 32, some, 0)
    projected_ref[...] += contract(signal_ref[...], small_ref[:lanes, :], 1, 1)

    @pl.when(block == pl.num_programs(0) - 1)
    def _():
        high, low = high_low(projected_ref[...])
        own = own_tokens(rows)
        rank = plan["step"][1]
        size = plan["decay"][1]
        entry = lax.broadcasted_iota(jnp.int32, (lanes, lanes), 0)
        lane = lax.rem(lax.broadcasted_iota(jnp.int32, (lanes, lanes), 1), size)
        for first, pair, triple in ((rank, write_pair, write_triple), (rank + size, read_pair, read_triple)):
            spread = (entry == lane + first).astype(jnp.bfloat16)
            parts = [
                (jnp.dot(part.astype(jnp.bfloat16), spread, preferred_element_type=jnp.float32) * own).reshape(
                    rows // chunk, chunk, lanes
                )
                for part in (high, low)
            ]
            pair[...] = jnp.concatenate(parts, axis=1).astype(pair.dtype)
            triple[...] = jnp.concatenate(
                [parts[0], parts[0], parts[1], jnp.zeros_like(parts[0])], axis=1
            ).astype(triple.dtype)


def high_low(values):
    high = values.astype(jnp.bfloat16).astype(jnp.float32)
    return high, values - high


def own_tokens(rows):
    token = lax.rem(lax.broadcasted_iota(jnp.int32, (rows, lanes), 0), chunk)
    return (token == lax.div(lax.broadcasted_iota(jnp.int32, (rows, lanes), 1), lanes // chunk)).astype(
        jnp.float32
    )


def tripled(values):
    high, low = high_low(values)
    return jnp.concatenate([high, low, high, jnp.zeros_like(high)], axis=1).astype(jnp.bfloat16)


def forward_kernel(
    plan,
    dims,
    lengths_ref,
    projected_ref,
    small_ref,
    signal_ref,
    write_triple,
    read_pair,
    own_ref,
    states_ref,
    step_ref,
    core_ref,
    whole_ref,
    offset_buf,
    pre_buf,
    decay_step,
    flows,
    entering_a,
    entering_b,
    low_buf,
    *sems,
):
    rows, width = pre_buf.shape
    size = plan["decay"][1]
    tiles = width // lanes
    chunks = rows // chunk
    rank = plan["step"][1]
    block = pl.program_id(0)
    gather = Gather(dims, [low_buf], [whole_ref], sems)

    @pl.when(block == 0)
    def _():
        low_buf[...] = own_ref[...].astype(low_buf.dtype)
        gather.start()
        fill_offsets(lengths_ref, offset_buf, rows)

    pre_buf[...] = jnp.dot(
        projected_ref[:, :rank].astype(small_ref.dtype),
        small_ref[pl.ds(plan["step"][0], rank), :],
        preferred_element_type=jnp.float32,
    )
    bias = small_rows(small_ref, *plan["bias"])

    def before(index, at, carry):
        spot = pl.ds(pl.multiple_of(index * 4, 4), 4)
        inside = offset_buf[at, :] > 0
        for tile in range(tiles):
            step = softplus(pre_buf[at, cut(tile)] + bias[:, tile * lanes : (tile + 1) * lanes])
            step_ref[spot, :, cut(tile)] = step.reshape(4, chunk, lanes)
            decay_step[spot, :, cut(tile)] = jnp.where(inside, step, far).reshape(4, chunk, lanes)
            flow = (step * signal_ref[at, cut(tile)].astype(jnp.float32)).reshape(4, chunk, lanes)
            flows[spot, :, cut(tile)] = tripled(flow)
        return carry

    row_loop(rows, 4 * chunk, before, 0)
    flows[chunks] = jnp.zeros_like(flows[chunks])
    rates = -jnp.exp(small_rows(small_ref, *plan["decay"])) * log2e
    rates = [rates[:, tile * lanes : (tile + 1) * lanes] for tile in range(tiles)]

    def enter(index):
        return contract(write_triple[jnp.minimum(index, chunks - 1)], flows[index], 0, 0)

    def leave(index):
        read = jnp.dot(
            read_pair[index],
            states_ref[pl.ds(index * chunk, chunk)].reshape(chunk * size, width),
            preferred_element_type=jnp.float32,
        )
        core_ref[index] = read[:chunk] + read[chunk:]

    def advance(index, held, entering):
        held = list(held)
        for place in range(chunk):
            for tile in range(tiles):
                decay = jnp.exp2(rates[tile] * decay_step[index, pl.ds(place, 1), cut(tile)])
                fresh = decay * held[tile] + entering[pl.ds(place * size, size), cut(tile)]
                held[tile] = fresh
                states_ref[index * chunk + place, :, cut(tile)] = fresh.astype(states_ref.dtype)
        return tuple(held)

    def forward(pair, held):
        index = 2 * pair
        entering_b[...] = enter(index + 1)
        leave(jnp.maximum(index - 1, 0))
        held = advance(index, held, entering_a)
        entering_a[...] = enter(index + 2)
        leave(index)
        return advance(index + 1, held, entering_b)

    entering_a[...] = enter(0)
    held = (jnp.zeros((size, lanes), jnp.float32),) * tiles
    for part in range(2):
        for number, moment in ((1, 3), (2, 5), (3, 7)):
            if moment % 2 == part:

                @pl.when(block == moment // 2)
                def _(number=number):
                    gather.leg(number)

        held = lax.fori_loop(part * chunks // 4, (part + 1) * chunks // 4, forward, held)
    leave(chunks - 1)

    @pl.when(block == pl.num_programs(0) - 1)
    def _():
        gather.finish()


def middle_kernel(
    plan,
    core_ref,
    small_ref,
    signal_ref,
    gate_ref,
    low_ref,
    out_w,
    flipped_ref,
    tokens_ref,
    core_grad_ref,
    gate_grad_ref,
    skip_grad_ref,
    out_grad_ref,
    in_grad_ref,
    output_ref,
    pre_buf,
    gated_buf,
    total,
):
    rows, width = pre_buf.shape
    tiles = width // lanes
    block = pl.program_id(0)
    pre_buf[...] = contract(low_ref[...], out_w[...], 1, 1)
    skip = small_rows(small_ref, *plan["skip"])

    def after(index, at, carry):
        spot = pl.ds(pl.multiple_of(index * 4, 4), 4)
        sums = []
        for tile in range(tiles):
            signal = signal_ref[at, cut(tile)].astype(jnp.float32)
            core = core_ref[spot, :, cut(tile)].reshape(4 * chunk, lanes)
            core = core + skip[:, tile * lanes : (tile + 1) * lanes] * signal
            gate = gate_ref[at, cut(tile)]
            sigma = sigmoid(gate)
            active = gate * sigma
            gated_buf[at, cut(tile)] = (core * active).astype(gated_buf.dtype)
            grad_gated = pre_buf[at, cut(tile)]
            grad_core = grad_gated * active
            core_grad_ref[spot, :, cut(tile)] = grad_core.reshape(4, chunk, lanes)
            slope = sigma + active * (1.0 - sigma)
            gate_grad_ref[at, cut(tile)] = (grad_gated * core * slope).astype(gate_grad_ref.dtype)
            sums.append(carry[tile] + eight(grad_core * signal))
        return tuple(sums)

    zero_rows = jnp.zeros((8, lanes), jnp.float32)
    skips = row_loop(rows, 4 * chunk, after, (zero_rows,) * tiles)
    for tile in range(tiles):
        skip_grad_ref[:, cut(tile)] = jnp.sum(skips[tile], axis=0, keepdims=True)
    out_grad_ref[...] = contract(gated_buf[...], low_ref[...], 0, 0).astype(out_grad_ref.dtype)
    in_grad_ref[...] = jnp.dot(
        flipped_ref[...], gate_grad_ref[...], preferred_element_type=jnp.float32
    ).astype(in_grad_ref.dtype)
    piece = jnp.dot(gated_buf[...], out_w[...], preferred_element_type=jnp.float32)

    @pl.when(block == 0)
    def _():
        total[...] = piece

    @pl.when(block > 0)
    def _():
        total[...] += piece

    @pl.when(block == pl.num_programs(0) - 1)
    def _():
        output_ref[...] = (tokens_ref[...].astype(jnp.float32) + total[...]).astype(output_ref.dtype)


def backward_kernel(
    plan,
    dims,
    lengths_ref,
    projected_ref,
    small_ref,
    signal_ref,
    write_pair,
    read_triple,
    step_ref,
    core_grad_ref,
    states_ref,
    out_grad_ref,
    in_grad_ref,
    signal_grad_ref,
    step_w_grad_ref,
    bias_grad_ref,
    decay_grad_ref,
    flat_ref,
    out_sum_ref,
    in_sum_ref,
    square_ref,
    offset_buf,
    decay_step,
    flows,
    grads,
    entering_a,
    entering_b,
    gone_a,
    gone_b,
    scaled_a,
    scaled_b,
    through_buf,
    scaled_buf,
    low_buf,
    rank_buf,
    write_buf,
    read_buf,
    *parts,
):
    rows, width = low_buf.shape
    rank = plan["step"][1]
    size = plan["decay"][1]
    tiles = width // lanes
    chunks = rows // chunk
    block = pl.program_id(0)
    reduce = Reduce(
        dims,
        [out_grad_ref, in_grad_ref],
        parts[2:12],
        parts[12:],
        parts[:2],
        [(0, 0), (1, 0)],
    )

    @pl.when(block == 0)
    def _():
        reduce.start()
        fill_offsets(lengths_ref, offset_buf, rows)
        write_buf[...] = jnp.zeros_like(write_buf)
        read_buf[...] = jnp.zeros_like(read_buf)
        rank_buf[...] = jnp.zeros_like(rank_buf)

    def before(index, at, carry):
        spot = pl.ds(pl.multiple_of(index * 4, 4), 4)
        inside = (offset_buf[at, :] > 0).reshape(4, chunk, lanes)
        for tile in range(tiles):
            step = step_ref[spot, :, cut(tile)]
            decay_step[spot, :, cut(tile)] = jnp.where(inside, step, far)
            signal = signal_ref[at, cut(tile)].astype(jnp.float32).reshape(4, chunk, lanes)
            high, low = high_low(step * signal)
            flows[spot, :, cut(tile)] = jnp.concatenate([high, low], axis=1).astype(flows.dtype)
            grads[spot, :, cut(tile)] = tripled(core_grad_ref[spot, :, cut(tile)])
        return carry

    row_loop(rows, 4 * chunk, before, 0)
    flows[chunks] = jnp.zeros_like(flows[chunks])
    gone_b[...] = jnp.zeros_like(gone_b)
    scaled_b[...] = jnp.zeros_like(scaled_b)
    rates = -jnp.exp(small_rows(small_ref, *plan["decay"])) * log2e
    rates = [rates[:, tile * lanes : (tile + 1) * lanes] for tile in range(tiles)]
    own = own_tokens(2 * chunk)
    ones = (own * (lax.broadcasted_iota(jnp.int32, own.shape, 0) < chunk)).astype(jnp.bfloat16)

    def enter(index):
        return contract(read_triple[index], grads[index], 0, 0)

    def kept(products):
        products = products * own
        return products[:chunk] + products[chunk:]

    def settle(index, gone_rows, scaled_rows):
        gone = gone_rows[...]
        through = jnp.dot(
            write_pair[jnp.minimum(index, chunks - 1)], gone, preferred_element_type=jnp.float32
        )
        through_buf[index] = through[:chunk] + through[chunk:]
        scaled = jnp.dot(ones, scaled_rows[...], preferred_element_type=jnp.float32)
        scaled_buf[index] = scaled[:chunk]
        write_buf[index] += kept(contract(flows[index], gone, 1, 1))

    def retreat(index, carried, entering, gone_rows, scaled_rows):
        base = index * chunk
        here = states_ref[pl.ds(base, chunk)].reshape(chunk * size, width)
        read_buf[index] += kept(contract(grads[index, : 2 * chunk], here, 1, 1))
        incoming, decay_sums = list(carried[0]), list(carried[1])
        for place in range(chunk - 1, -1, -1):
            now = base + place
            earlier = jnp.maximum(now - 1, 0) if place == 0 else now - 1
            lot = pl.ds(place * size, size)
            for tile in range(tiles):
                step_now = decay_step[index, pl.ds(place, 1), cut(tile)]
                grad_state = incoming[tile] + entering[lot, cut(tile)]
                gone_rows[lot, cut(tile)] = grad_state.astype(gone_rows.dtype)
                leaving = jnp.exp2(rates[tile] * step_now) * grad_state
                incoming[tile] = leaving
                weighted = leaving * states_ref[earlier, :, cut(tile)].astype(jnp.float32)
                scaled_rows[lot, cut(tile)] = (weighted * rates[tile]).astype(scaled_rows.dtype)
                decay_sums[tile] = decay_sums[tile] + weighted * step_now
        return (tuple(incoming), tuple(decay_sums))

    def backward(pair, carried):
        index = chunks - 1 - 2 * pair
        entering_b[...] = enter(index - 1)
        settle(index + 1, gone_b, scaled_b)
        carried = retreat(index, carried, entering_a, gone_a, scaled_a)
        entering_a[...] = enter(jnp.maximum(index - 2, 0))
        settle(index, gone_a, scaled_a)
        return retreat(index - 1, carried, entering_b, gone_b, scaled_b)

    entering_a[...] = enter(chunks - 1)
    carried = ((jnp.zeros((size, lanes), jnp.float32),) * tiles,) * 2
    for part in range(2):
        for number, moment in ((1, 1), (2, 4), (3, 6)):
            if moment % 2 == part:

                @pl.when(block == moment // 2)
                def _(number=number):
                    reduce.leg(number)

        carried = lax.fori_loop(part * chunks // 4, (part + 1) * chunks // 4, backward, carried)
    settle(0, gone_b, scaled_b)
    for tile in range(tiles):
        decay_grad_ref[:, cut(tile)] = carried[1][tile] * rates[tile] * ln2
    skip = small_rows(small_ref, *plan["skip"])

    def after(index, at, carry):
        spot = pl.ds(pl.multiple_of(index * 4, 4), 4)
        sums = []
        for tile in range(tiles):
            signal = signal_ref[at, cut(tile)].astype(jnp.float32)
            step = step_ref[spot, :, cut(tile)].reshape(4 * chunk, lanes)
            through = through_buf[spot, :, cut(tile)].reshape(4 * chunk, lanes)
            scaled = scaled_buf[spot, :, cut(tile)].reshape(4 * chunk, lanes)
            core_grad = core_grad_ref[spot, :, cut(tile)].reshape(4 * chunk, lanes)
            grad_pre = (through * signal + ln2 * scaled) * slope_of(step)
            low_buf[at, cut(tile)] = grad_pre.astype(low_buf.dtype)
            signal_grad_ref[at, cut(tile)] = (
                through * step + skip[:, tile * lanes : (tile + 1) * lanes] * core_grad
            )
            sums.append(carry[tile] + eight(grad_pre))
        return tuple(sums)

    zero_rows = jnp.zeros((8, lanes), jnp.float32)
    sums = row_loop(rows, 4 * chunk, after, (zero_rows,) * tiles)
    for tile in range(tiles):
        bias_grad_ref[:, cut(tile)] = jnp.sum(sums[tile], axis=0, keepdims=True)
    step_w_grad_ref[...] = contract(
        projected_ref[:, :rank].astype(low_buf.dtype), low_buf[...], 0, 0
    )
    step_w = small_ref[pl.ds(plan["step"][0], rank), :]
    step_w = jnp.concatenate([step_w, jnp.zeros((lanes - rank, width), step_w.dtype)], axis=0)
    rank_buf[...] += contract(low_buf[...], step_w, 1, 1).reshape(chunks, chunk, lanes)

    @pl.when(block == pl.num_programs(0) - 1)
    def _():
        square_ref[...] = reduce.finish(None, None)[0]
        lane = lax.broadcasted_iota(jnp.int32, (lanes, lanes), 0)
        target = lax.broadcasted_iota(jnp.int32, (lanes, lanes), 1)
        sums = [jnp.sum(buffer[:chunks], axis=1).astype(jnp.bfloat16) for buffer in (write_buf, read_buf)]
        for token in range(chunk):
            total = None
            for number, summed in enumerate(sums):
                first = rank + number * size
                entry = target - first
                take = (entry >= 0) & (entry < size) & (lane == token * size + entry)
                piece = jnp.dot(summed, take.astype(jnp.bfloat16), preferred_element_type=jnp.float32)
                total = piece if total is None else total + piece
            rank_buf[:, token, :] += total
        flat_ref[...] = rank_buf[...].reshape(rows, lanes).astype(flat_ref.dtype)
        reduce.settle()
        out_sum_ref[...] = parts[0][...]
        in_sum_ref[...] = parts[1][...]


def back_kernel(
    plan,
    lengths_ref,
    tokens_ref,
    low_ref,
    gain_ref,
    small_ref,
    flat_ref,
    branch_ref,
    signal_ref,
    slope_ref,
    signal_grad_ref,
    gate_grad_ref,
    flipped_ref,
    branch_w,
    gate_w,
    step_w_grad_ref,
    bias_grad_ref,
    decay_grad_ref,
    skip_grad_ref,
    small_grad_ref,
    in_grad_ref,
    gain_grad_ref,
    tokens_grad_ref,
    offset_buf,
    conv_buf,
    mixed_buf,
    total,
):
    rows = tokens_ref.shape[0]
    width = branch_ref.shape[1]
    tiles = width // lanes
    block = pl.program_id(0)

    @pl.when(block == 0)
    def _():
        fill_offsets(lengths_ref, offset_buf, rows)

    taps = small_rows(small_ref, *plan["taps"])
    count = taps.shape[0]
    small_grad_ref[:lanes, :] = contract(flat_ref[...], signal_ref[...], 0, 0)

    def place_rows(name, values):
        first, tall = plan[name]
        small_grad_ref[first : first + tall, :] = values

    place_rows("step", step_w_grad_ref[...])
    place_rows("decay", decay_grad_ref[...])
    place_rows("bias", bias_grad_ref[...])
    place_rows("skip", skip_grad_ref[...])
    conv_buf[pl.ds(0, rows), :] = signal_grad_ref[...] + jnp.dot(
        flat_ref[...], small_ref[:lanes, :], preferred_element_type=jnp.float32
    )
    conv_buf[pl.ds(rows, 8), :] = jnp.zeros((8, width), jnp.float32)

    def through_conv(index, at, carry):
        sums = []
        for tile in range(tiles):
            grad_conv = conv_buf[at, cut(tile)] * slope_ref[at, cut(tile)]
            conv_buf[at, cut(tile)] = grad_conv
            sums.append(carry[tile] + eight(grad_conv))
        return tuple(sums)

    zero_rows = jnp.zeros((8, lanes), jnp.float32)
    sums = row_loop(rows, 32, through_conv, (zero_rows,) * tiles)
    for tile in range(tiles):
        first = plan["shift"][0]
        small_grad_ref[first : first + 1, cut(tile)] = jnp.sum(sums[tile], axis=0, keepdims=True)

    def to_branch(index, at, carry):
        longer = pl.ds(pl.multiple_of(index * 32, 32), 40)
        offsets = offset_buf[longer, :]
        result = []
        for tile in range(tiles):
            here = slice(tile * lanes, (tile + 1) * lanes)
            grads = conv_buf[longer, cut(tile)]
            branch = branch_ref[at, cut(tile)]
            summed = taps[count - 1 : count, here] * grads[:32]
            sums = [None] * count
            sums[count - 1] = carry[tile][count - 1] + eight(branch * grads[:32])
            for tap in range(count - 1):
                lag = count - 1 - tap
                moved = pltpu.roll(jnp.where(offsets >= lag, grads, 0.0), 40 - lag, 0)[:32]
                summed = summed + taps[tap : tap + 1, here] * moved
                sums[tap] = carry[tile][tap] + eight(branch * moved)
            mixed_buf[at, cut(tile)] = summed.astype(mixed_buf.dtype)
            result.append(tuple(sums))
        return tuple(result)

    sums = row_loop(rows, 32, to_branch, ((zero_rows,) * count,) * tiles)
    for tile in range(tiles):
        for tap in range(count):
            first = plan["taps"][0] + tap
            small_grad_ref[first : first + 1, cut(tile)] = jnp.sum(sums[tile][tap], axis=0, keepdims=True)
    in_grad_ref[...] = jnp.dot(
        flipped_ref[...], mixed_buf[...], preferred_element_type=jnp.float32
    ).astype(in_grad_ref.dtype)
    piece = contract(mixed_buf[...], branch_w[...], 1, 1) + contract(gate_grad_ref[...], gate_w[...], 1, 1)

    @pl.when(block == 0)
    def _():
        total[...] = piece

    @pl.when(block > 0)
    def _():
        total[...] += piece

    @pl.when(block == pl.num_programs(0) - 1)
    def _():
        def finish(index, at, carry):
            residual = tokens_ref[at, :].astype(jnp.float32)
            scale = lax.rsqrt(jnp.mean(residual * residual, axis=1, keepdims=True) + epsilon)
            grad_normed = total[at, :]
            weighted = grad_normed * gain_ref[...]
            inner = jnp.mean(weighted * residual, axis=1, keepdims=True)
            grad_y = low_ref[at, :].astype(jnp.float32)
            result = grad_y + (scale * weighted - residual * (scale * scale * scale) * inner)
            tokens_grad_ref[at, :] = result.astype(tokens_grad_ref.dtype)
            return carry + eight(grad_normed * residual * scale)

        gains = row_loop(rows, 16, finish, jnp.zeros((8, total.shape[1]), jnp.float32))
        gain_grad_ref[...] = jnp.sum(gains, axis=0, keepdims=True)


def finish_kernel(plan, names, branch_ref, gate_ref, out_ref, small_ref, norm_ref, *outs):
    middle = branch_ref.shape[1]
    outs[0][:, :middle] = branch_ref[...]
    outs[0][:, middle:] = gate_ref[...]
    outs[1][...] = out_ref[...]
    for name, target in zip(names, outs[2 : 2 + len(names)]):
        first, count = plan[name]
        if len(target.shape) == 1:
            target[...] = small_ref[first, : target.shape[0]]
        else:
            target[...] = small_ref[first : first + count, :]
    for index in range(2):
        outs[2 + len(names) + index][0, 0] = jnp.sum(norm_ref[index])


def shape(dims, kind=jnp.float32):
    return jax.ShapeDtypeStruct(dims, kind)


def compute_call(
    kernel, name, blocks, in_specs, out_specs, out_shape, scratch, flops, operands, collective_id=None
):
    return pl.pallas_call(
        kernel,
        grid=(blocks,),
        in_specs=in_specs,
        out_specs=out_specs,
        out_shape=out_shape,
        scratch_shapes=scratch,
        compiler_params=pltpu.CompilerParams(
            dimension_semantics=("arbitrary",),
            vmem_limit_bytes=62 * 1024 * 1024,
            collective_id=collective_id,
            has_side_effects=collective_id is not None,
        ),
        cost_estimate=pl.CostEstimate(flops=flops, bytes_accessed=40 << 20, transcendentals=0),
        name=name,
    )(*operands)


class Place:
    def __init__(self, dims, swapped=False):
        depth, tall, wide = dims
        self.dims = dims
        self.core = lax.axis_index("wide")
        self.me = lax.axis_index("narrow")
        self.across = lax.rem(self.me, wide)
        self.up = lax.rem(lax.div(self.me, wide), tall)
        self.deep = lax.div(self.me, wide * tall)
        side = 1 - self.core if swapped else self.core
        turn = side if tall == wide else 0
        self.second = (1 + turn * (wide - 1), self.across + turn * (self.up - self.across), wide)
        self.third = (wide - turn * (wide - 1), self.up + turn * (self.across - self.up), tall)
        self.spans = (depth, wide, tall)
        self.other = {"wide": 1 - self.core}

    def at(self, d, e, f):
        depth, tall, wide = self.dims
        return (
            lax.rem(self.deep + d, depth) * (tall * wide)
            + lax.rem(self.second[1] + e, self.second[2]) * self.second[0]
            + lax.rem(self.third[1] + f, self.third[2]) * self.third[0]
        )

    def behind(self, d, e, f):
        return self.at(*((size - hop) % size for size, hop in zip(self.spans, (d, e, f))))

    def slot(self, d, e, f):
        return (d * self.spans[1] + e) * self.spans[2] + f

    def moves(self):
        return [
            (d, e, f)
            for d in range(self.spans[0])
            for e in range(self.spans[1])
            for f in range(self.spans[2])
        ]

    def greet(self):
        barrier = pltpu.get_barrier_semaphore()
        pl.semaphore_signal(barrier, inc=1, device_id=self.other, device_id_type=pl.DeviceIdType.MESH)
        peers = 1
        for axis, size in enumerate(self.spans):
            for hop in range(1, size):
                move = [0, 0, 0]
                move[axis] = hop
                pl.semaphore_signal(
                    barrier,
                    inc=1,
                    device_id={"narrow": self.at(*move)},
                    device_id_type=pl.DeviceIdType.MESH,
                )
                peers += 1
        pl.semaphore_wait(barrier, peers)


def half_of(width, core):
    return pl.ds(pl.multiple_of(core * (width // 2), lanes), width // 2)


def side_of(block, side):
    if len(block.shape) == 3:
        return block.at[side]
    return block.at[:, half_of(block.shape[1], side)]


def half_shape(array):
    return array.shape[2:] if len(array.shape) == 4 else (array.shape[1], array.shape[2] // 2)


def remote(source, target, send_sem, recv_sem, device):
    return pltpu.make_async_remote_copy(
        src_ref=source,
        dst_ref=target,
        send_sem=send_sem,
        recv_sem=recv_sem,
        device_id=device,
        device_id_type=pl.DeviceIdType.MESH,
    )


class Gather:
    def __init__(self, dims, own, whole, sems):
        self.dims, self.own, self.whole = dims, own, whole
        self.local_sem, self.send_sem, self.recv_sem, self.core_send, self.core_recv = sems

    @staticmethod
    def scratch(count, dims):
        number = dims[0] * dims[1] * dims[2]
        return [pltpu.SemaphoreType.DMA((count,))] + [pltpu.SemaphoreType.DMA((count, number))] * 4

    def onward(self, place, which, move):
        d, e, f = move
        number = place.behind(*move)
        target = side_of(self.whole[which].at[number], place.core)
        source = side_of(self.own[which], place.core) if move == (0, 0, 0) else target
        hops = []
        if f == 0:
            hops += [((0, 0, hop), (d, e, hop)) for hop in range(1, place.spans[2])]
        if f == 0 and e == 0:
            hops += [((0, hop, 0), (d, hop, 0)) for hop in range(1, place.spans[1])]
        if move == (0, 0, 0):
            hops += [((hop, 0, 0), (hop, 0, 0)) for hop in range(1, place.spans[0])]
        for step, landing in reversed(hops):
            index = place.slot(*landing)
            remote(
                source,
                target,
                self.send_sem.at[which, index],
                self.recv_sem.at[which, index],
                {"narrow": place.at(*step)},
            ).start()
        if move != (0, 0, 0):
            index = place.slot(*move)
            remote(
                source,
                target,
                self.core_send.at[which, index],
                self.core_recv.at[which, index],
                place.other,
            ).start()

    def local(self, place, which):
        return pltpu.make_async_copy(
            self.own[which], self.whole[which].at[place.at(0, 0, 0)], self.local_sem.at[which]
        )

    def start(self):
        place = Place(self.dims)
        place.greet()
        for which in range(len(self.own)):
            self.onward(place, which, (0, 0, 0))
        for which in range(len(self.own)):
            self.local(place, which).start()

    def leg(self, number):
        place = Place(self.dims)
        for which in range(len(self.own)):
            for move in place.moves():
                d, e, f = move
                if (number == 3) != (f > 0):
                    continue
                if number < 3 and (number == 2) != (e > 0):
                    continue
                if move == (0, 0, 0):
                    continue
                index = place.slot(*move)
                landed = side_of(self.whole[which].at[place.behind(*move)], place.core)
                remote(
                    landed,
                    landed,
                    self.send_sem.at[which, index],
                    self.recv_sem.at[which, index],
                    place.other,
                ).wait_recv()
                self.onward(place, which, move)

    def finish(self):
        place = Place(self.dims)
        mirror = Place(self.dims, swapped=True)
        for which in range(len(self.own)):
            for move in place.moves():
                if move == (0, 0, 0):
                    continue
                index = place.slot(*move)
                landed = side_of(self.whole[which].at[mirror.behind(*move)], 1 - place.core)
                handed = remote(
                    landed,
                    landed,
                    self.core_send.at[which, index],
                    self.core_recv.at[which, index],
                    place.other,
                )
                handed.wait_recv()
                handed.wait_send()
                remote(
                    landed,
                    landed,
                    self.send_sem.at[which, index],
                    self.recv_sem.at[which, index],
                    place.other,
                ).wait_send()
            self.local(place, which).wait()


class Reduce:
    def __init__(self, dims, grads, held, sems, results, targets):
        self.dims, self.grads = dims, grads
        count = len(grads)
        self.mine, self.swapped, self.third, self.second, self.first = (
            held[index * count : (index + 1) * count] for index in range(5)
        )
        (
            self.local_sem,
            self.core_send,
            self.core_recv,
            self.leg_send,
            self.leg_recv,
            self.last_send,
            self.last_recv,
        ) = sems
        self.results, self.targets = results, targets

    @staticmethod
    def rooms(dims, grads):
        depth, tall, wide = dims
        number = depth * tall * wide
        places = (number, number, depth * wide * (tall - 1), depth * (wide - 1), depth - 1)
        return [
            pltpu.VMEM((room,) + tuple(half_shape(grad)), grad.dtype) for room in places for grad in grads
        ]

    @staticmethod
    def sems(dims, count):
        number = dims[0] * dims[1] * dims[2]
        return [pltpu.SemaphoreType.DMA((count, number))] * 5 + [pltpu.SemaphoreType.DMA((count,))] * 2

    def order(self, place):
        return sorted(place.moves(), key=lambda item: (item[2] == 0, item[1] == 0, item[0] == 0))

    def share(self, which, side):
        result, first = self.targets[which]
        if len(self.grads[which].shape) == 4:
            return self.results[result].at[side]
        width = self.grads[which].shape[2]
        columns = pl.ds(pl.multiple_of(first + side * (width // 2), lanes), width // 2)
        return self.results[result].at[:, columns]

    def load(self, place, which, move):
        return pltpu.make_async_copy(
            side_of(self.grads[which].at[place.at(*move)], place.core),
            self.mine[which].at[place.slot(*move)],
            self.local_sem.at[which, place.slot(*move)],
        )

    def swap(self, place, which, move, mirror):
        index = place.slot(*move)
        return remote(
            side_of(self.grads[which].at[mirror.at(*move)], 1 - place.core),
            self.swapped[which].at[index],
            self.core_send.at[which, index],
            self.core_recv.at[which, index],
            place.other,
        )

    def start(self):
        place, mirror = Place(self.dims), Place(self.dims, swapped=True)
        place.greet()
        for move in self.order(place):
            for which in range(len(self.grads)):
                self.swap(place, which, move, mirror).start()
                self.load(place, which, move).start()

    def landing(self, place, which, move):
        d, e, f = move
        if f > 0:
            return self.third[which].at[(d * place.spans[1] + e) * (place.spans[2] - 1) + f - 1], (0, 0, f)
        if e > 0:
            return self.second[which].at[d * (place.spans[1] - 1) + e - 1], (0, e, 0)
        return self.first[which].at[d - 1], (d, 0, 0)

    def hop(self, place, which, move):
        landing, step = self.landing(place, which, move)
        index = place.slot(*move)
        return remote(
            self.mine[which].at[index],
            landing,
            self.leg_send.at[which, index],
            self.leg_recv.at[which, index],
            {"narrow": place.at(*step)},
        )

    def collect(self, place, which, move):
        d, e, f = move
        index = place.slot(*move)
        self.load(place, which, move).wait()
        handed = self.swapped[which].at[index]
        remote(
            handed, handed, self.core_send.at[which, index], self.core_recv.at[which, index], place.other
        ).wait_recv()
        parts = [handed]
        coming = []
        if f == 0:
            coming += [(d, e, hop) for hop in range(1, place.spans[2])]
        if f == 0 and e == 0:
            coming += [(d, hop, 0) for hop in range(1, place.spans[1])]
        if move == (0, 0, 0):
            coming += [(hop, 0, 0) for hop in range(1, place.spans[0])]
        for source in coming:
            self.hop(place, which, source).wait_recv()
            parts.append(self.landing(place, which, source)[0])
        return parts

    def added(self, place, which, move, parts, store, carry):
        block = self.mine[which].at[place.slot(*move)]
        rows = block.shape[0]
        group = min(rows, 16)

        def some(index, carry):
            at_rows = pl.ds(pl.multiple_of(index * group, group), group)
            total = block[at_rows, :].astype(jnp.float32)
            for part in parts:
                total = total + part[at_rows, :].astype(jnp.float32)
            return store(block, at_rows, total, carry)

        return lax.fori_loop(0, rows // group, some, carry)

    def leg(self, number):
        place = Place(self.dims)

        def keep(block, at_rows, total, carry):
            block[at_rows, :] = total.astype(block.dtype)
            return carry

        for move in self.order(place)[:-1]:
            d, e, f = move
            if number != (1 if f > 0 else 2 if e > 0 else 3):
                continue
            for which in range(len(self.grads)):
                parts = self.collect(place, which, move)
                self.added(place, which, move, parts, keep, 0)
                self.hop(place, which, move).start()

    def finish(self, plain_at, plain_ref):
        place, mirror = Place(self.dims), Place(self.dims, swapped=True)
        squares = (jnp.zeros((8, lanes), jnp.float32),) * 2
        for which in range(len(self.grads)):
            parts = self.collect(place, which, (0, 0, 0))
            result = self.share(which, place.core)

            def store(block, at_rows, total, carry, which=which, result=result):
                result[at_rows, :] = total
                kept, plain = carry
                squared = total * total
                if which == plain_at:
                    marked = squared * plain_ref[place.core, at_rows, :]
                    plain = plain + folded_squares(marked)
                    squared = squared - marked
                return (kept + folded_squares(squared), plain)

            squares = self.added(place, which, (0, 0, 0), parts, store, squares)
            remote(result, result, self.last_send.at[which], self.last_recv.at[which], place.other).start()
        return squares

    def settle(self):
        place, mirror = Place(self.dims), Place(self.dims, swapped=True)
        for which in range(len(self.grads)):
            result = self.share(which, 1 - place.core)
            last = remote(result, result, self.last_send.at[which], self.last_recv.at[which], place.other)
            last.wait_recv()
            last.wait_send()
            for move in place.moves():
                self.swap(place, which, move, mirror).wait_send()
                if move != (0, 0, 0):
                    self.hop(place, which, move).wait_send()


def folded_squares(values):
    total = None
    if values.shape[1] < lanes:
        first = lax.broadcasted_iota(jnp.int32, (values.shape[0], lanes), 1) == 0
        values = jnp.where(first, jnp.sum(values, axis=1, keepdims=True), 0.0)
    for row in range(0, values.shape[0], 8):
        for column in range(0, values.shape[1], lanes):
            piece = values[row : row + 8, column : column + lanes]
            total = piece if total is None else total + piece
    return total


def gather_kernel(dims, plan, names, *refs):
    smalls, bigs = refs[: len(names)], refs[len(names) : len(names) + 1]
    refs = refs[len(names) + 1 :]
    whole, own, pack_buf, sems = refs[:2], refs[2:4], refs[4], refs[5:]
    pack_buf[...] = jnp.zeros_like(pack_buf)
    for name, ref in zip(names, smalls):
        first, tall = plan[name]
        pack_buf[first : first + tall, : ref.shape[1]] = ref[...]
    tall = pack_buf.shape[0] // 2
    for side in range(2):
        own[0][side] = pack_buf[side * tall : (side + 1) * tall, :].astype(own[0].dtype)
    own[1][...] = bigs[0][...].astype(own[1].dtype)
    gather = Gather(dims, own, whole, sems)
    gather.start()
    for number in (1, 2, 3):
        gather.leg(number)
    gather.finish()


def gather_weights(dims, plan, smalls, big):
    number = dims[0] * dims[1] * dims[2]
    names = list(smalls)
    width = smalls["select"].shape[1]
    owned = [shape((2, plan["rows"] // 2, width), jnp.bfloat16), shape(big.shape, jnp.bfloat16)]
    inside = pl.BlockSpec(memory_space=pltpu.VMEM)
    return pl.pallas_call(
        functools.partial(gather_kernel, dims, plan, names),
        in_specs=[inside] * (len(names) + 1),
        out_specs=[pl.BlockSpec(memory_space=pl.ANY)] * 2,
        out_shape=[shape((number,) + kind.shape, kind.dtype) for kind in owned],
        scratch_shapes=[pltpu.VMEM(kind.shape, kind.dtype) for kind in owned]
        + [pltpu.VMEM((plan["rows"], width), jnp.float32)]
        + Gather.scratch(2, dims),
        compiler_params=pltpu.CompilerParams(
            collective_id=0, has_side_effects=True, vmem_limit_bytes=60 * 1024 * 1024
        ),
        name="gather_weights",
    )(*smalls.values(), big)


def reduce_kernel(dims, count, results, targets, plain_at, *refs):
    grads, plain_ref, earlier_ref = refs[:count], refs[count], refs[count + 1]
    refs = refs[count + 2 :]
    sums, norms = refs[:results], refs[results]
    refs = refs[results + 1 :]
    held, buffers = refs[: 5 * count], refs[5 * count : 5 * count + 4]
    refs = refs[5 * count + 4 :]
    sems, (norm_send, norm_recv) = refs[:7], refs[7:]
    reduce = Reduce(dims, grads, held, sems, sums, targets)
    reduce.start()
    for number in (1, 2, 3):
        reduce.leg(number)
    kept, plain = reduce.finish(plain_at, plain_ref)
    running = jnp.stack([kept + earlier_ref[...], plain])

    place = Place(dims)
    depth, tall, wide = dims
    plane = tall * wide
    me = place.me
    stages = (
        (buffers[0], 2, place.core, lambda spot: {"wide": spot}),
        (buffers[1], depth, place.deep, lambda spot: {"narrow": spot * plane + lax.rem(me, plane)}),
        (buffers[2], wide, place.across, lambda spot: {"narrow": me - place.across + spot}),
        (buffers[3], tall, place.up, lambda spot: {"narrow": me + (spot - place.up) * wide}),
    )
    pending = []
    first = 0
    for buffer, size, mine_at, device in stages:
        buffer[mine_at] = running
        for hop in range(1, size):
            copy = remote(
                buffer.at[mine_at],
                buffer.at[mine_at],
                norm_send.at[first + hop - 1],
                norm_recv.at[first + hop - 1],
                device(lax.rem(mine_at + hop, size)),
            )
            copy.start()
            pending.append(copy)
        for hop in range(1, size):
            came = lax.rem(mine_at + size - hop, size)
            remote(
                buffer.at[came],
                buffer.at[came],
                norm_send.at[first + hop - 1],
                norm_recv.at[first + hop - 1],
                device(came),
            ).wait_recv()
        first += size - 1
        running = buffer[0]
        for spot in range(1, size):
            running = running + buffer[spot]
    norms[...] = running
    reduce.settle()
    for copy in pending:
        copy.wait_send()


def sum_shapes(grads, targets):
    sums = []
    for index in range(1 + max(target[0] for target in targets)):
        members = [grad for grad, target in zip(grads, targets) if target[0] == index]
        if len(members[0].shape) == 4:
            sums.append(shape(members[0].shape[1:]))
        else:
            sums.append(shape((members[0].shape[1], sum(grad.shape[2] for grad in members))))
    return sums


def reduce_grads(dims, grads, targets, plain_mask, plain_at, earlier):
    depth, tall, wide = dims
    count = len(grads)
    anywhere = pl.BlockSpec(memory_space=pl.ANY)
    inside = pl.BlockSpec(memory_space=pltpu.VMEM)
    sums = sum_shapes(grads, targets)
    result = pl.pallas_call(
        functools.partial(reduce_kernel, dims, count, len(sums), targets, plain_at),
        in_specs=[anywhere] * count + [inside] * 2,
        out_specs=[inside] * (len(sums) + 1),
        out_shape=sums + [shape((2, 8, lanes))],
        scratch_shapes=Reduce.rooms(dims, grads)
        + [pltpu.VMEM((size, 2, 8, lanes), jnp.float32) for size in (2, depth, wide, tall)]
        + Reduce.sems(dims, count)
        + [pltpu.SemaphoreType.DMA((depth + tall + wide,))] * 2,
        compiler_params=pltpu.CompilerParams(
            collective_id=1, has_side_effects=True, vmem_limit_bytes=56 * 1024 * 1024
        ),
        name="reduce_grads",
    )(*grads, plain_mask, earlier)
    return result[: len(sums)], result[len(sums)]


def grid_of(mesh):
    number = mesh.shape["narrow"]
    places = [getattr(device, "coords", None) for device in mesh.devices[0]]
    if all(place is not None for place in places):
        sizes = [len({place[axis] for place in places}) for axis in (2, 1, 0)]
        if sizes[0] * sizes[1] * sizes[2] == number:
            return tuple(sizes)
    side = round((number / 2) ** (1 / 3))
    return (2 * side, side, side) if 2 * side**3 == number else (number, 1, 1)


def plan_of(select_rows, state_size, tap_count, step_rows):
    plan, first = {}, 0
    for name, tall in (
        ("select", select_rows),
        ("decay", state_size),
        ("taps", tap_count),
        ("shift", 1),
        ("bias", 1),
        ("skip", 1),
        ("gain", 1),
    ):
        plan[name] = (first, tall)
        first += tall
    plan["step"] = (lanes, step_rows)
    plan["rows"] = -(-(lanes + step_rows) // 32) * 32
    return plan


def per_device(
    dims,
    tokens,
    cotangent,
    loss_mask,
    seq_lengths,
    norm_gain,
    in_proj,
    conv_weight,
    conv_bias,
    select_proj,
    step_proj,
    step_bias,
    decay_log,
    skip_scale,
    out_proj,
):
    half = jnp.bfloat16
    piece = skip_scale.shape[0]
    gain_piece = norm_gain.shape[0]
    rank, size = step_proj.shape[0], decay_log.shape[0]
    plan = plan_of(select_proj.shape[0], size, conv_weight.shape[0], rank)
    small_blocks, in_blocks = gather_weights(
        dims,
        plan,
        {
            "select": select_proj,
            "decay": decay_log,
            "taps": conv_weight,
            "shift": conv_bias[None],
            "bias": step_bias[None],
            "skip": skip_scale[None],
            "gain": norm_gain[None],
            "step": step_proj,
        },
        in_proj,
    )
    in_whole = in_blocks.reshape(-1, in_blocks.shape[2])
    small_blocks = small_blocks.reshape(-1, plan["rows"], piece)
    small = jnp.swapaxes(small_blocks, 0, 1).reshape(plan["rows"], -1)
    gain_value = small_blocks[:, plan["gain"][0], :gain_piece].reshape(1, -1).astype(jnp.float32)

    rows, model = tokens.shape
    inner = small.shape[1]
    width = 4 * lanes
    blocks = inner // width
    chunks = rows // chunk
    mask_row = loss_mask[None]

    whole = pl.BlockSpec(memory_space=pltpu.VMEM)
    tall = pl.BlockSpec((rows, width), lambda b: (0, b))
    deep = pl.BlockSpec((chunks, chunk, width), lambda b: (0, 0, b))
    lead = pl.BlockSpec((rows, size, width), lambda b: (0, 0, b))
    first_w = pl.BlockSpec((model, width), lambda b: (0, b))
    second_w = pl.BlockSpec((model, width), lambda b: (0, b + blocks))
    out_w = pl.BlockSpec((width, model), lambda b: (b, 0))

    def thin(height):
        return pl.BlockSpec((height, width), lambda b: (0, b))

    def fixed(*dims_of):
        return pl.BlockSpec(dims_of, lambda b: (0,) * len(dims_of))

    scalars = pl.BlockSpec(memory_space=pltpu.SMEM)
    offset_buf = pltpu.VMEM((rows + 8, lanes), jnp.int32)
    packed = thin(plan["rows"])

    pair, triple = (chunks, 2 * chunk, lanes), (chunks, 4 * chunk, lanes)
    (
        branch,
        gate_pre,
        signal,
        slope,
        projected,
        flipped,
        grad_low,
        write_pair,
        write_triple,
        read_pair,
        read_triple,
    ) = compute_call(
        functools.partial(front_kernel, plan),
        "front",
        blocks,
        [scalars, whole, whole, whole, whole, packed, first_w, second_w],
        [tall, tall, tall, tall, fixed(rows, lanes), fixed(model, rows), fixed(rows, model)]
        + [fixed(*pair), fixed(*triple)] * 2,
        [
            shape((rows, inner)),
            shape((rows, inner)),
            shape((rows, inner), half),
            shape((rows, inner)),
            shape((rows, lanes)),
            shape((model, rows), half),
            shape((rows, model), half),
        ]
        + [shape(pair, half), shape(triple, half)] * 2,
        [pltpu.VMEM((rows, model), half), offset_buf],
        4 * rows * model * inner,
        (seq_lengths, tokens, cotangent, mask_row, gain_value, small, in_whole, in_whole),
    )
    row_block = pltpu.VMEM((chunks, chunk, width), jnp.float32)
    spare_block = pltpu.VMEM((chunks + 1, chunk, width), jnp.float32)
    number = small_blocks.shape[0]
    anywhere = pl.BlockSpec(memory_space=pl.ANY)
    states, step, core, out_blocks = compute_call(
        functools.partial(forward_kernel, plan, dims),
        "forward",
        blocks,
        [scalars, whole, packed, tall, whole, whole, whole],
        [lead, deep, deep, anywhere],
        [
            shape((rows, size, inner), half),
            shape((chunks, chunk, inner)),
            shape((chunks, chunk, inner)),
            shape((number,) + out_proj.shape, half),
        ],
        [
            offset_buf,
            pltpu.VMEM((rows, width), jnp.float32),
            row_block,
            pltpu.VMEM((chunks + 1, 4 * chunk, width), half),
            pltpu.VMEM((chunk * size, width), jnp.float32),
            pltpu.VMEM((chunk * size, width), jnp.float32),
            pltpu.VMEM(out_proj.shape, half),
        ]
        + Gather.scratch(1, dims),
        15 * rows * inner * size,
        (seq_lengths, projected, small, signal, write_triple, read_pair, out_proj),
        collective_id=2,
    )
    core_grad, gate_grad, grad_skip, grad_outw, grad_in_gate, output = compute_call(
        functools.partial(middle_kernel, plan),
        "middle",
        blocks,
        [deep, packed, tall, tall, whole, out_w, whole, whole],
        [deep, tall, thin(1), out_w, first_w, fixed(rows, model)],
        [
            shape((chunks, chunk, inner)),
            shape((rows, inner), half),
            shape((1, inner)),
            shape((inner, model), half),
            shape((model, inner), half),
            shape((rows, model), half),
        ],
        [
            pltpu.VMEM((rows, width), jnp.float32),
            pltpu.VMEM((rows, width), half),
            pltpu.VMEM((rows, model), jnp.float32),
        ],
        8 * rows * model * inner,
        (core, small, signal, gate_pre, grad_low, out_blocks.reshape(inner, model), flipped, tokens),
    )
    split = in_blocks.shape[:2] + (inner,)
    early_grads = [grad_outw.reshape(out_blocks.shape), grad_in_gate.reshape(split)]
    early_sums = sum_shapes(early_grads, [(0, 0), (1, 0)])
    (
        signal_grad,
        grad_stepw,
        grad_bias,
        grad_decaylog,
        flat,
        out_sum,
        in_gate_sum,
        early_squares,
    ) = compute_call(
        functools.partial(backward_kernel, plan, dims),
        "backward",
        blocks,
        [scalars, whole, packed, tall, whole, whole, deep, deep, lead, anywhere, anywhere],
        [tall, thin(rank), thin(1), thin(size), fixed(rows, lanes)]
        + [whole] * 3,
        [
            shape((rows, inner)),
            shape((rank, inner)),
            shape((1, inner)),
            shape((size, inner)),
            shape((rows, lanes), half),
            *early_sums,
            shape((8, lanes)),
        ],
        [
            offset_buf,
            row_block,
            pltpu.VMEM((chunks + 1, 2 * chunk, width), half),
            pltpu.VMEM((chunks, 4 * chunk, width), half),
            pltpu.VMEM((chunk * size, width), jnp.float32),
            pltpu.VMEM((chunk * size, width), jnp.float32),
            pltpu.VMEM((chunk * size, width), half),
            pltpu.VMEM((chunk * size, width), half),
            pltpu.VMEM((chunk * size, width), half),
            pltpu.VMEM((chunk * size, width), half),
            spare_block,
            spare_block,
            pltpu.VMEM((rows, width), half),
            pltpu.VMEM((chunks, chunk, lanes), jnp.float32),
            pltpu.VMEM((chunks + 1, chunk, lanes), jnp.float32),
            pltpu.VMEM((chunks, chunk, lanes), jnp.float32),
        ]
        + [pltpu.VMEM(early.shape, early.dtype) for early in early_sums]
        + Reduce.rooms(dims, early_grads)
        + Reduce.sems(dims, 2),
        40 * rows * inner * size,
        (seq_lengths, projected, small, signal, write_pair, read_triple, step, core_grad, states, *early_grads),
        collective_id=3,
    )

    small_grad, grad_in_branch, grad_gain, grad_tokens = compute_call(
        functools.partial(back_kernel, plan),
        "back",
        blocks,
        [scalars, whole, whole, whole, packed, whole, tall, tall, tall, tall, tall, whole, first_w, second_w]
        + [thin(rank), thin(1), thin(size), thin(1)],
        [packed, first_w, fixed(1, model), fixed(rows, model)],
        [
            shape((plan["rows"], inner)),
            shape((model, inner), half),
            shape((1, model)),
            shape((rows, model), half),
        ],
        [
            offset_buf,
            pltpu.VMEM((rows + 8, width), jnp.float32),
            pltpu.VMEM((rows, width), half),
            pltpu.VMEM((rows, model), jnp.float32),
        ],
        8 * rows * model * inner,
        (
            seq_lengths,
            tokens,
            grad_low,
            gain_value,
            small,
            flat,
            branch,
            signal,
            slope,
            signal_grad,
            gate_grad,
            flipped,
            in_whole,
            in_whole,
            grad_stepw,
            grad_bias,
            grad_decaylog,
            grad_skip,
        ),
    )

    gain_rows = jnp.pad(grad_gain.reshape(number, 1, gain_piece), ((0, 0), (0, 0), (0, piece - gain_piece)))
    place = plan["gain"][0]
    small_grad = jnp.swapaxes(small_grad.reshape(plan["rows"], number, piece), 0, 1) + jnp.pad(
        gain_rows, ((0, 0), (place, plan["rows"] - place - 1), (0, 0))
    )
    plain_rows = np.zeros((plan["rows"], piece), np.float32)
    for name in ("bias", "decay", "skip"):
        first, count = plan[name]
        plain_rows[first : first + count] = 1.0
    halves = (2, plan["rows"] // 2, piece)
    (in_branch_sum, small_sum), norms = reduce_grads(
        dims,
        [grad_in_branch.reshape(split), small_grad.reshape((number,) + halves)],
        [(0, 0), (1, 0)],
        jnp.asarray(plain_rows.reshape(halves)),
        1,
        early_squares,
    )
    names = ("gain", "taps", "shift", "select", "step", "bias", "decay", "skip")
    own = (norm_gain, conv_weight, conv_bias, select_proj, step_proj, step_bias, decay_log, skip_scale)
    in_grad, out_grad, gain_grad, *small_grads, decay_sq, plain_sq = pl.pallas_call(
        functools.partial(finish_kernel, plan, names),
        in_specs=[whole] * 5,
        out_specs=[whole] * (2 + len(names)) + [scalars] * 2,
        out_shape=[shape(in_proj.shape), shape(out_proj.shape)]
        + [shape(array.shape) for array in own]
        + [shape((1, 1))] * 2,
        name="finish",
    )(in_branch_sum, in_gate_sum, out_sum, small_sum.reshape(plan["rows"], piece), norms)
    return (
        output,
        grad_tokens,
        gain_grad,
        in_grad,
        *small_grads,
        out_grad,
        decay_sq[0, 0],
        plain_sq[0, 0],
    )


def solution(mesh):
    placed = (
        P(("wide", "narrow"), None),
        P(("wide", "narrow"), None),
        P(("wide", "narrow")),
        P(("wide", "narrow"), None),
        P("narrow"),
        P("narrow", None),
        P(None, "narrow"),
        P("narrow"),
        P(None, "narrow"),
        P(None, "narrow"),
        P("narrow"),
        P(None, "narrow"),
        P("narrow"),
        P("narrow", None),
    )
    return jax.shard_map(
        functools.partial(per_device, grid_of(mesh)),
        mesh=mesh,
        in_specs=placed,
        out_specs=(
            P(("wide", "narrow"), None),
            P(("wide", "narrow"), None),
            P("narrow"),
            P("narrow", None),
            P(None, "narrow"),
            P("narrow"),
            P(None, "narrow"),
            P(None, "narrow"),
            P("narrow"),
            P(None, "narrow"),
            P("narrow"),
            P("narrow", None),
            P(),
            P(),
        ),
        check_vma=False,
    )
```

```python
import functools
import math

import jax
import jax.numpy as jnp
import numpy as np
from jax import lax
from jax.experimental import pallas as pl
from jax.experimental.pallas import tpu as pltpu
from jax.sharding import PartitionSpec as P

epsilon = 1e-05
chunk = 8
lanes = 128
log2e = math.log2(math.e)
ln2 = math.log(2.0)
far = 1e30


def contract(left, right, left_dim, right_dim):
    return lax.dot_general(
        left, right, (((left_dim,), (right_dim,)), ((), ())), preferred_element_type=jnp.float32
    )


def row_loop(rows, group, body, initial):
    def some(index, carry):
        return body(index, pl.ds(pl.multiple_of(index * group, group), group), carry)

    return lax.fori_loop(0, rows // group, some, initial)


def cut(tile):
    return pl.ds(tile * lanes, lanes)


def sigmoid(values):
    return 0.5 * jnp.tanh(0.5 * values) + 0.5


def softplus(values):
    small = jnp.exp(-jnp.abs(values))
    series = small * (1.0 - small * (0.5 - small * (1.0 / 3.0 - 0.25 * small)))
    return jnp.maximum(values, 0.0) + jnp.where(small < 0.03, series, jnp.log(1.0 + small))


def slope_of(step):
    series = step * (1.0 - step * (0.5 - step * (1.0 / 6.0 - step * (1.0 / 24.0))))
    return jnp.where(step < 0.03, series, 1.0 - jnp.exp(-step))


def fill_offsets(lengths_ref, offset_buf, rows):
    place = lax.broadcasted_iota(jnp.int32, offset_buf.shape, 0)
    start = jnp.zeros(offset_buf.shape, jnp.int32)
    ahead = jnp.int32(0)
    for index in range(lengths_ref.shape[1] - 1):
        ahead = ahead + lengths_ref[0, index]
        start = jnp.where(place >= ahead, ahead, start)
    offset_buf[...] = jnp.where(place < rows, place - start, 0)


def small_rows(small_ref, first, count):
    base = first // 16 * 16
    tall = -(-(first + count - base) // 16) * 16
    return small_ref[base : base + tall, :].astype(jnp.float32)[first - base : first - base + count]


def eight(values):
    total = values[:8]
    for row in range(8, values.shape[0], 8):
        total = total + values[row : row + 8]
    return total


def conv_rows(index, at, group, tile, branch_ref, offset_buf, taps, shift):
    count = taps.shape[0]
    here = slice(tile * lanes, (tile + 1) * lanes)
    current = branch_ref[at, cut(tile)]
    before = branch_ref[pl.ds(pl.multiple_of(jnp.maximum(index * group - 8, 0), 8), 8), cut(tile)]
    both = jnp.concatenate([before, current], axis=0)
    offsets = offset_buf[at, :]
    summed = shift[:, here] + taps[count - 1 : count, here] * current
    for tap in range(count - 1):
        lag = count - 1 - tap
        read = jnp.where(offsets >= lag, pltpu.roll(both, lag, 0)[8:], 0.0)
        summed = summed + taps[tap : tap + 1, here] * read
    return summed


def front_kernel(
    plan,
    lengths_ref,
    tokens_ref,
    cotangent_ref,
    mask_ref,
    gain_ref,
    small_ref,
    branch_w,
    gate_w,
    branch_ref,
    gate_ref,
    signal_ref,
    slope_ref,
    projected_ref,
    flipped_ref,
    low_ref,
    write_pair,
    read_pair,
    normed_buf,
    offset_buf,
):
    rows = tokens_ref.shape[0]
    width = branch_ref.shape[1]
    block = pl.program_id(0)

    @pl.when(block == 0)
    def _():
        fill_offsets(lengths_ref, offset_buf, rows)

        def norm(index, at, carry):
            residual = tokens_ref[at, :].astype(jnp.float32)
            scale = lax.rsqrt(jnp.mean(residual * residual, axis=1, keepdims=True) + epsilon)
            normed_buf[at, :] = (residual * scale * gain_ref[...]).astype(normed_buf.dtype)
            return carry

        row_loop(rows, 16, norm, 0)
        flipped_ref[...] = normed_buf[...].T
        projected_ref[...] = jnp.zeros_like(projected_ref)
        down = lax.broadcasted_iota(jnp.int32, (rows, rows), 0)
        along = lax.broadcasted_iota(jnp.int32, (rows, rows), 1)
        diagonal = jnp.where(down == along, mask_ref[...].astype(jnp.float32), 0.0).astype(low_ref.dtype)
        low_ref[...] = jnp.dot(
            diagonal, cotangent_ref[...], preferred_element_type=jnp.float32
        ).astype(low_ref.dtype)

    branch_ref[...] = jnp.dot(normed_buf[...], branch_w[...], preferred_element_type=jnp.float32)
    gate_ref[...] = jnp.dot(normed_buf[...], gate_w[...], preferred_element_type=jnp.float32)
    taps = small_rows(small_ref, *plan["taps"])
    shift = small_rows(small_ref, *plan["shift"])

    def some(index, at, carry):
        for tile in range(width // lanes):
            summed = conv_rows(index, at, 32, tile, branch_ref, offset_buf, taps, shift)
            sigma = sigmoid(summed)
            active = summed * sigma
            signal_ref[at, cut(tile)] = active.astype(signal_ref.dtype)
            slope_ref[at, cut(tile)] = sigma + active * (1.0 - sigma)
        return carry

    row_loop(rows, 32, some, 0)
    projected_ref[...] += contract(signal_ref[...], small_ref[:lanes, :], 1, 1)

    @pl.when(block == pl.num_programs(0) - 1)
    def _():
        high, low = high_low(projected_ref[...])
        own = own_tokens(rows)
        rank = plan["step"][1]
        size = plan["decay"][1]
        entry = lax.broadcasted_iota(jnp.int32, (lanes, lanes), 0)
        lane = lax.rem(lax.broadcasted_iota(jnp.int32, (lanes, lanes), 1), size)
        for first, pair in ((rank, write_pair), (rank + size, read_pair)):
            spread = (entry == lane + first).astype(jnp.bfloat16)
            parts = [
                (jnp.dot(part.astype(jnp.bfloat16), spread, preferred_element_type=jnp.float32) * own).reshape(
                    rows // chunk, chunk, lanes
                )
                for part in (high, low)
            ]
            pair[...] = jnp.concatenate(parts, axis=1).astype(pair.dtype)


def high_low(values):
    high = values.astype(jnp.bfloat16).astype(jnp.float32)
    return high, values - high


def own_tokens(rows):
    token = lax.rem(lax.broadcasted_iota(jnp.int32, (rows, lanes), 0), chunk)
    return (token == lax.div(lax.broadcasted_iota(jnp.int32, (rows, lanes), 1), lanes // chunk)).astype(
        jnp.float32
    )


def spread_rows(pair):
    return contract(pair, jnp.ones((pair.shape[0], lanes), pair.dtype), 0, 0)


def forward_kernel(
    plan,
    dims,
    lengths_ref,
    projected_ref,
    small_ref,
    signal_ref,
    write_pair,
    read_pair,
    own_ref,
    states_ref,
    step_ref,
    core_ref,
    whole_ref,
    offset_buf,
    pre_buf,
    decay_step,
    flows,
    entering_a,
    entering_b,
    low_buf,
    *sems,
):
    rows, width = pre_buf.shape
    size = plan["decay"][1]
    tiles = width // lanes
    chunks = rows // chunk
    rank = plan["step"][1]
    block = pl.program_id(0)
    gather = Gather(dims, [low_buf], [whole_ref], sems)

    @pl.when(block == 0)
    def _():
        low_buf[...] = own_ref[...].astype(low_buf.dtype)
        gather.start()
        fill_offsets(lengths_ref, offset_buf, rows)

    pre_buf[...] = jnp.dot(
        projected_ref[:, :rank].astype(small_ref.dtype),
        small_ref[pl.ds(plan["step"][0], rank), :],
        preferred_element_type=jnp.float32,
    )
    bias = small_rows(small_ref, *plan["bias"])

    def before(index, at, carry):
        spot = pl.ds(pl.multiple_of(index * 4, 4), 4)
        inside = offset_buf[at, :] > 0
        for tile in range(tiles):
            step = softplus(pre_buf[at, cut(tile)] + bias[:, tile * lanes : (tile + 1) * lanes])
            step_ref[spot, :, cut(tile)] = step.reshape(4, chunk, lanes)
            decay_step[spot, :, cut(tile)] = jnp.where(inside, step, far).reshape(4, chunk, lanes)
            flow = step * signal_ref[at, cut(tile)].astype(jnp.float32)
            flows[spot, :, cut(tile)] = flow.reshape(4, chunk, lanes)
        return carry

    row_loop(rows, 4 * chunk, before, 0)
    rates = -jnp.exp(small_rows(small_ref, *plan["decay"])) * log2e
    rates = [rates[:, tile * lanes : (tile + 1) * lanes] for tile in range(tiles)]

    def enter(index):
        return spread_rows(write_pair[jnp.minimum(index, chunks - 1)])

    def leave(index):
        read = jnp.dot(
            read_pair[index],
            states_ref[pl.ds(index * chunk, chunk)].reshape(chunk * size, width),
            preferred_element_type=jnp.float32,
        )
        core_ref[index] = read[:chunk] + read[chunk:]

    def advance(index, held, entering):
        held = list(held)
        for place in range(chunk):
            write_now = entering[pl.ds(place * size, size), :]
            for tile in range(tiles):
                decay = jnp.exp2(rates[tile] * decay_step[index, pl.ds(place, 1), cut(tile)])
                fresh = decay * held[tile] + write_now * flows[index, pl.ds(place, 1), cut(tile)]
                held[tile] = fresh
                states_ref[index * chunk + place, :, cut(tile)] = fresh.astype(states_ref.dtype)
        return tuple(held)

    def forward(pair, held):
        index = 2 * pair
        entering_b[...] = enter(index + 1)
        leave(jnp.maximum(index - 1, 0))
        held = advance(index, held, entering_a)
        entering_a[...] = enter(index + 2)
        leave(index)
        return advance(index + 1, held, entering_b)

    entering_a[...] = enter(0)
    held = (jnp.zeros((size, lanes), jnp.float32),) * tiles
    for part in range(2):
        for number, moment in ((1, 3), (2, 5), (3, 7)):
            if moment % 2 == part:

                @pl.when(block == moment // 2)
                def _(number=number):
                    gather.leg(number)

        held = lax.fori_loop(part * chunks // 4, (part + 1) * chunks // 4, forward, held)
    leave(chunks - 1)

    @pl.when(block == pl.num_programs(0) - 1)
    def _():
        gather.finish()


def middle_kernel(
    plan,
    core_ref,
    small_ref,
    signal_ref,
    gate_ref,
    low_ref,
    out_w,
    flipped_ref,
    tokens_ref,
    core_grad_ref,
    gate_grad_ref,
    skip_grad_ref,
    out_grad_ref,
    in_grad_ref,
    output_ref,
    pre_buf,
    gated_buf,
    total,
):
    rows, width = pre_buf.shape
    tiles = width // lanes
    block = pl.program_id(0)
    pre_buf[...] = contract(low_ref[...], out_w[...], 1, 1)
    skip = small_rows(small_ref, *plan["skip"])

    def after(index, at, carry):
        spot = pl.ds(pl.multiple_of(index * 4, 4), 4)
        sums = []
        for tile in range(tiles):
            signal = signal_ref[at, cut(tile)].astype(jnp.float32)
            core = core_ref[spot, :, cut(tile)].reshape(4 * chunk, lanes)
            core = core + skip[:, tile * lanes : (tile + 1) * lanes] * signal
            gate = gate_ref[at, cut(tile)]
            sigma = sigmoid(gate)
            active = gate * sigma
            gated_buf[at, cut(tile)] = (core * active).astype(gated_buf.dtype)
            grad_gated = pre_buf[at, cut(tile)]
            grad_core = grad_gated * active
            core_grad_ref[spot, :, cut(tile)] = grad_core.reshape(4, chunk, lanes)
            slope = sigma + active * (1.0 - sigma)
            gate_grad_ref[at, cut(tile)] = (grad_gated * core * slope).astype(gate_grad_ref.dtype)
            sums.append(carry[tile] + eight(grad_core * signal))
        return tuple(sums)

    zero_rows = jnp.zeros((8, lanes), jnp.float32)
    skips = row_loop(rows, 4 * chunk, after, (zero_rows,) * tiles)
    for tile in range(tiles):
        skip_grad_ref[:, cut(tile)] = jnp.sum(skips[tile], axis=0, keepdims=True)
    out_grad_ref[...] = contract(gated_buf[...], low_ref[...], 0, 0).astype(out_grad_ref.dtype)
    in_grad_ref[...] = jnp.dot(
        flipped_ref[...], gate_grad_ref[...], preferred_element_type=jnp.float32
    ).astype(in_grad_ref.dtype)
    piece = jnp.dot(gated_buf[...], out_w[...], preferred_element_type=jnp.float32)

    @pl.when(block == 0)
    def _():
        total[...] = piece

    @pl.when(block > 0)
    def _():
        total[...] += piece

    @pl.when(block == pl.num_programs(0) - 1)
    def _():
        output_ref[...] = (tokens_ref[...].astype(jnp.float32) + total[...]).astype(output_ref.dtype)


def backward_kernel(
    plan,
    dims,
    lengths_ref,
    projected_ref,
    small_ref,
    signal_ref,
    write_pair,
    read_pair,
    step_ref,
    core_grad_ref,
    states_ref,
    out_grad_ref,
    in_grad_ref,
    signal_grad_ref,
    step_w_grad_ref,
    bias_grad_ref,
    decay_grad_ref,
    flat_ref,
    out_sum_ref,
    in_sum_ref,
    square_ref,
    offset_buf,
    decay_step,
    flows,
    grads,
    entering_a,
    entering_b,
    gone_a,
    gone_b,
    scaled_a,
    scaled_b,
    through_buf,
    scaled_buf,
    low_buf,
    rank_buf,
    write_buf,
    read_buf,
    *parts,
):
    rows, width = low_buf.shape
    rank = plan["step"][1]
    size = plan["decay"][1]
    tiles = width // lanes
    chunks = rows // chunk
    block = pl.program_id(0)
    reduce = Reduce(
        dims,
        [out_grad_ref, in_grad_ref],
        parts[2:12],
        parts[12:],
        parts[:2],
        [(0, 0), (1, 0)],
    )

    @pl.when(block == 0)
    def _():
        reduce.start()
        fill_offsets(lengths_ref, offset_buf, rows)
        write_buf[...] = jnp.zeros_like(write_buf)
        read_buf[...] = jnp.zeros_like(read_buf)
        rank_buf[...] = jnp.zeros_like(rank_buf)

    def before(index, at, carry):
        spot = pl.ds(pl.multiple_of(index * 4, 4), 4)
        inside = (offset_buf[at, :] > 0).reshape(4, chunk, lanes)
        for tile in range(tiles):
            step = step_ref[spot, :, cut(tile)]
            decay_step[spot, :, cut(tile)] = jnp.where(inside, step, far)
            signal = signal_ref[at, cut(tile)].astype(jnp.float32).reshape(4, chunk, lanes)
            high, low = high_low(step * signal)
            flows[spot, :, cut(tile)] = jnp.concatenate([high, low], axis=1).astype(flows.dtype)
            high, low = high_low(core_grad_ref[spot, :, cut(tile)])
            grads[spot, :, cut(tile)] = jnp.concatenate([high, low], axis=1).astype(grads.dtype)
        return carry

    row_loop(rows, 4 * chunk, before, 0)
    flows[chunks] = jnp.zeros_like(flows[chunks])
    gone_b[...] = jnp.zeros_like(gone_b)
    scaled_b[...] = jnp.zeros_like(scaled_b)
    rates = -jnp.exp(small_rows(small_ref, *plan["decay"])) * log2e
    rates = [rates[:, tile * lanes : (tile + 1) * lanes] for tile in range(tiles)]
    own = own_tokens(2 * chunk)
    ones = (own * (lax.broadcasted_iota(jnp.int32, own.shape, 0) < chunk)).astype(jnp.bfloat16)

    token_of = lax.rem(lax.broadcasted_iota(jnp.int32, (size, 2 * chunk), 1), chunk)

    def enter(index):
        return spread_rows(read_pair[index])

    def kept(products):
        result = products[:size]
        for place in range(1, chunk):
            result = jnp.where(token_of == place, products[place * size : (place + 1) * size], result)
        return result

    def settle(index, gone_rows, scaled_rows):
        gone = gone_rows[...]
        through = jnp.dot(
            write_pair[jnp.minimum(index, chunks - 1)], gone, preferred_element_type=jnp.float32
        )
        through_buf[index] = through[:chunk] + through[chunk:]
        scaled = jnp.dot(ones, scaled_rows[...], preferred_element_type=jnp.float32)
        scaled_buf[index] = scaled[:chunk]
        write_buf[index] += kept(contract(gone, flows[index], 1, 1))

    def retreat(index, carried, entering, gone_rows, scaled_rows):
        base = index * chunk
        here = states_ref[pl.ds(base, chunk)].reshape(chunk * size, width)
        read_buf[index] += kept(contract(here, grads[index], 1, 1))
        incoming, decay_sums = list(carried[0]), list(carried[1])
        for place in range(chunk - 1, -1, -1):
            now = base + place
            earlier = jnp.maximum(now - 1, 0) if place == 0 else now - 1
            lot = pl.ds(place * size, size)
            read_now = entering[lot, :]
            for tile in range(tiles):
                step_now = decay_step[index, pl.ds(place, 1), cut(tile)]
                grad_state = incoming[tile] + read_now * core_grad_ref[index, pl.ds(place, 1), cut(tile)]
                gone_rows[lot, cut(tile)] = grad_state.astype(gone_rows.dtype)
                leaving = jnp.exp2(rates[tile] * step_now) * grad_state
                incoming[tile] = leaving
                weighted = leaving * states_ref[earlier, :, cut(tile)].astype(jnp.float32)
                scaled_rows[lot, cut(tile)] = (weighted * rates[tile]).astype(scaled_rows.dtype)
                decay_sums[tile] = decay_sums[tile] + weighted * step_now
        return (tuple(incoming), tuple(decay_sums))

    def backward(pair, carried):
        index = chunks - 1 - 2 * pair
        entering_b[...] = enter(index - 1)
        settle(index + 1, gone_b, scaled_b)
        carried = retreat(index, carried, entering_a, gone_a, scaled_a)
        entering_a[...] = enter(jnp.maximum(index - 2, 0))
        settle(index, gone_a, scaled_a)
        return retreat(index - 1, carried, entering_b, gone_b, scaled_b)

    entering_a[...] = enter(chunks - 1)
    carried = ((jnp.zeros((size, lanes), jnp.float32),) * tiles,) * 2
    for part in range(2):
        for number, moment in ((1, 1), (2, 4), (3, 6)):
            if moment % 2 == part:

                @pl.when(block == moment // 2)
                def _(number=number):
                    reduce.leg(number)

        carried = lax.fori_loop(part * chunks // 4, (part + 1) * chunks // 4, backward, carried)
    settle(0, gone_b, scaled_b)
    for tile in range(tiles):
        decay_grad_ref[:, cut(tile)] = carried[1][tile] * rates[tile] * ln2
    skip = small_rows(small_ref, *plan["skip"])

    def after(index, at, carry):
        spot = pl.ds(pl.multiple_of(index * 4, 4), 4)
        sums = []
        for tile in range(tiles):
            signal = signal_ref[at, cut(tile)].astype(jnp.float32)
            step = step_ref[spot, :, cut(tile)].reshape(4 * chunk, lanes)
            through = through_buf[spot, :, cut(tile)].reshape(4 * chunk, lanes)
            scaled = scaled_buf[spot, :, cut(tile)].reshape(4 * chunk, lanes)
            core_grad = core_grad_ref[spot, :, cut(tile)].reshape(4 * chunk, lanes)
            grad_pre = (through * signal + ln2 * scaled) * slope_of(step)
            low_buf[at, cut(tile)] = grad_pre.astype(low_buf.dtype)
            signal_grad_ref[at, cut(tile)] = (
                through * step + skip[:, tile * lanes : (tile + 1) * lanes] * core_grad
            )
            sums.append(carry[tile] + eight(grad_pre))
        return tuple(sums)

    zero_rows = jnp.zeros((8, lanes), jnp.float32)
    sums = row_loop(rows, 4 * chunk, after, (zero_rows,) * tiles)
    for tile in range(tiles):
        bias_grad_ref[:, cut(tile)] = jnp.sum(sums[tile], axis=0, keepdims=True)
    step_w_grad_ref[...] = contract(
        projected_ref[:, :rank].astype(low_buf.dtype), low_buf[...], 0, 0
    )
    step_w = small_ref[pl.ds(plan["step"][0], rank), :]
    step_w = jnp.concatenate([step_w, jnp.zeros((lanes - rank, width), step_w.dtype)], axis=0)
    rank_buf[...] += contract(low_buf[...], step_w, 1, 1).reshape(chunks, chunk, lanes)

    @pl.when(block == pl.num_programs(0) - 1)
    def _():
        square_ref[...] = reduce.finish(None, None)[0]
        entry = lax.broadcasted_iota(jnp.int32, (size, lanes), 0)
        target = lax.broadcasted_iota(jnp.int32, (size, lanes), 1)
        places = [(target == entry + rank + number * size).astype(jnp.bfloat16) for number in range(2)]

        def lay(index, carry):
            for buffer, place in zip((write_buf, read_buf), places):
                summed = buffer[index][:, :chunk] + buffer[index][:, chunk:]
                rank_buf[index] += contract(summed.astype(jnp.bfloat16), place, 0, 0)
            return carry

        lax.fori_loop(0, chunks, lay, 0, unroll=8)
        flat_ref[...] = rank_buf[...].reshape(rows, lanes).astype(flat_ref.dtype)
        reduce.settle()
        out_sum_ref[...] = parts[0][...]
        in_sum_ref[...] = parts[1][...]


def back_kernel(
    plan,
    lengths_ref,
    tokens_ref,
    low_ref,
    gain_ref,
    small_ref,
    flat_ref,
    branch_ref,
    signal_ref,
    slope_ref,
    signal_grad_ref,
    gate_grad_ref,
    flipped_ref,
    branch_w,
    gate_w,
    step_w_grad_ref,
    bias_grad_ref,
    decay_grad_ref,
    skip_grad_ref,
    small_grad_ref,
    in_grad_ref,
    gain_grad_ref,
    tokens_grad_ref,
    offset_buf,
    conv_buf,
    mixed_buf,
    total,
):
    rows = tokens_ref.shape[0]
    width = branch_ref.shape[1]
    tiles = width // lanes
    block = pl.program_id(0)

    @pl.when(block == 0)
    def _():
        fill_offsets(lengths_ref, offset_buf, rows)

    taps = small_rows(small_ref, *plan["taps"])
    count = taps.shape[0]
    small_grad_ref[:lanes, :] = contract(flat_ref[...], signal_ref[...], 0, 0)

    def place_rows(name, values):
        first, tall = plan[name]
        small_grad_ref[first : first + tall, :] = values

    place_rows("step", step_w_grad_ref[...])
    place_rows("decay", decay_grad_ref[...])
    place_rows("bias", bias_grad_ref[...])
    place_rows("skip", skip_grad_ref[...])
    conv_buf[pl.ds(0, rows), :] = signal_grad_ref[...] + jnp.dot(
        flat_ref[...], small_ref[:lanes, :], preferred_element_type=jnp.float32
    )
    conv_buf[pl.ds(rows, 8), :] = jnp.zeros((8, width), jnp.float32)

    def through_conv(index, at, carry):
        sums = []
        for tile in range(tiles):
            grad_conv = conv_buf[at, cut(tile)] * slope_ref[at, cut(tile)]
            conv_buf[at, cut(tile)] = grad_conv
            sums.append(carry[tile] + eight(grad_conv))
        return tuple(sums)

    zero_rows = jnp.zeros((8, lanes), jnp.float32)
    sums = row_loop(rows, 32, through_conv, (zero_rows,) * tiles)
    for tile in range(tiles):
        first = plan["shift"][0]
        small_grad_ref[first : first + 1, cut(tile)] = jnp.sum(sums[tile], axis=0, keepdims=True)

    def to_branch(index, at, carry):
        longer = pl.ds(pl.multiple_of(index * 32, 32), 40)
        offsets = offset_buf[longer, :]
        result = []
        for tile in range(tiles):
            here = slice(tile * lanes, (tile + 1) * lanes)
            grads = conv_buf[longer, cut(tile)]
            branch = branch_ref[at, cut(tile)]
            summed = taps[count - 1 : count, here] * grads[:32]
            sums = [None] * count
            sums[count - 1] = carry[tile][count - 1] + eight(branch * grads[:32])
            for tap in range(count - 1):
                lag = count - 1 - tap
                moved = pltpu.roll(jnp.where(offsets >= lag, grads, 0.0), 40 - lag, 0)[:32]
                summed = summed + taps[tap : tap + 1, here] * moved
                sums[tap] = carry[tile][tap] + eight(branch * moved)
            mixed_buf[at, cut(tile)] = summed.astype(mixed_buf.dtype)
            result.append(tuple(sums))
        return tuple(result)

    sums = row_loop(rows, 32, to_branch, ((zero_rows,) * count,) * tiles)
    for tile in range(tiles):
        for tap in range(count):
            first = plan["taps"][0] + tap
            small_grad_ref[first : first + 1, cut(tile)] = jnp.sum(sums[tile][tap], axis=0, keepdims=True)
    in_grad_ref[...] = jnp.dot(
        flipped_ref[...], mixed_buf[...], preferred_element_type=jnp.float32
    ).astype(in_grad_ref.dtype)
    piece = contract(mixed_buf[...], branch_w[...], 1, 1) + contract(gate_grad_ref[...], gate_w[...], 1, 1)

    @pl.when(block == 0)
    def _():
        total[...] = piece

    @pl.when(block > 0)
    def _():
        total[...] += piece

    @pl.when(block == pl.num_programs(0) - 1)
    def _():
        def finish(index, at, carry):
            residual = tokens_ref[at, :].astype(jnp.float32)
            scale = lax.rsqrt(jnp.mean(residual * residual, axis=1, keepdims=True) + epsilon)
            grad_normed = total[at, :]
            weighted = grad_normed * gain_ref[...]
            inner = jnp.mean(weighted * residual, axis=1, keepdims=True)
            grad_y = low_ref[at, :].astype(jnp.float32)
            result = grad_y + (scale * weighted - residual * (scale * scale * scale) * inner)
            tokens_grad_ref[at, :] = result.astype(tokens_grad_ref.dtype)
            return carry + eight(grad_normed * residual * scale)

        gains = row_loop(rows, 16, finish, jnp.zeros((8, total.shape[1]), jnp.float32))
        gain_grad_ref[...] = jnp.sum(gains, axis=0, keepdims=True)


def finish_kernel(plan, names, branch_ref, gate_ref, out_ref, small_ref, norm_ref, *outs):
    middle = branch_ref.shape[1]
    outs[0][:, :middle] = branch_ref[...]
    outs[0][:, middle:] = gate_ref[...]
    outs[1][...] = out_ref[...]
    for name, target in zip(names, outs[2 : 2 + len(names)]):
        first, count = plan[name]
        if len(target.shape) == 1:
            target[...] = small_ref[first, : target.shape[0]]
        else:
            target[...] = small_ref[first : first + count, :]
    for index in range(2):
        outs[2 + len(names) + index][0, 0] = jnp.sum(norm_ref[index])


def shape(dims, kind=jnp.float32):
    return jax.ShapeDtypeStruct(dims, kind)


def compute_call(
    kernel, name, blocks, in_specs, out_specs, out_shape, scratch, flops, operands, collective_id=None
):
    return pl.pallas_call(
        kernel,
        grid=(blocks,),
        in_specs=in_specs,
        out_specs=out_specs,
        out_shape=out_shape,
        scratch_shapes=scratch,
        compiler_params=pltpu.CompilerParams(
            dimension_semantics=("arbitrary",),
            vmem_limit_bytes=62 * 1024 * 1024,
            collective_id=collective_id,
            has_side_effects=collective_id is not None,
        ),
        cost_estimate=pl.CostEstimate(flops=flops, bytes_accessed=40 << 20, transcendentals=0),
        name=name,
    )(*operands)


class Place:
    def __init__(self, dims, swapped=False):
        depth, tall, wide = dims
        self.dims = dims
        self.core = lax.axis_index("wide")
        self.me = lax.axis_index("narrow")
        self.across = lax.rem(self.me, wide)
        self.up = lax.rem(lax.div(self.me, wide), tall)
        self.deep = lax.div(self.me, wide * tall)
        side = 1 - self.core if swapped else self.core
        turn = side if tall == wide else 0
        self.second = (1 + turn * (wide - 1), self.across + turn * (self.up - self.across), wide)
        self.third = (wide - turn * (wide - 1), self.up + turn * (self.across - self.up), tall)
        self.spans = (depth, wide, tall)
        self.other = {"wide": 1 - self.core}

    def at(self, d, e, f):
        depth, tall, wide = self.dims
        return (
            lax.rem(self.deep + d, depth) * (tall * wide)
            + lax.rem(self.second[1] + e, self.second[2]) * self.second[0]
            + lax.rem(self.third[1] + f, self.third[2]) * self.third[0]
        )

    def behind(self, d, e, f):
        return self.at(*((size - hop) % size for size, hop in zip(self.spans, (d, e, f))))

    def slot(self, d, e, f):
        return (d * self.spans[1] + e) * self.spans[2] + f

    def moves(self):
        return [
            (d, e, f)
            for d in range(self.spans[0])
            for e in range(self.spans[1])
            for f in range(self.spans[2])
        ]

    def greet(self):
        barrier = pltpu.get_barrier_semaphore()
        pl.semaphore_signal(barrier, inc=1, device_id=self.other, device_id_type=pl.DeviceIdType.MESH)
        peers = 1
        for axis, size in enumerate(self.spans):
            for hop in range(1, size):
                move = [0, 0, 0]
                move[axis] = hop
                pl.semaphore_signal(
                    barrier,
                    inc=1,
                    device_id={"narrow": self.at(*move)},
                    device_id_type=pl.DeviceIdType.MESH,
                )
                peers += 1
        pl.semaphore_wait(barrier, peers)


def half_of(width, core):
    return pl.ds(pl.multiple_of(core * (width // 2), lanes), width // 2)


def side_of(block, side):
    if len(block.shape) == 3:
        return block.at[side]
    return block.at[:, half_of(block.shape[1], side)]


def half_shape(array):
    return array.shape[2:] if len(array.shape) == 4 else (array.shape[1], array.shape[2] // 2)


def remote(source, target, send_sem, recv_sem, device):
    return pltpu.make_async_remote_copy(
        src_ref=source,
        dst_ref=target,
        send_sem=send_sem,
        recv_sem=recv_sem,
        device_id=device,
        device_id_type=pl.DeviceIdType.MESH,
    )


class Gather:
    def __init__(self, dims, own, whole, sems):
        self.dims, self.own, self.whole = dims, own, whole
        self.local_sem, self.send_sem, self.recv_sem, self.core_send, self.core_recv = sems

    @staticmethod
    def scratch(count, dims):
        number = dims[0] * dims[1] * dims[2]
        return [pltpu.SemaphoreType.DMA((count,))] + [pltpu.SemaphoreType.DMA((count, number))] * 4

    def onward(self, place, which, move):
        d, e, f = move
        number = place.behind(*move)
        target = side_of(self.whole[which].at[number], place.core)
        source = side_of(self.own[which], place.core) if move == (0, 0, 0) else target
        hops = []
        if f == 0:
            hops += [((0, 0, hop), (d, e, hop)) for hop in range(1, place.spans[2])]
        if f == 0 and e == 0:
            hops += [((0, hop, 0), (d, hop, 0)) for hop in range(1, place.spans[1])]
        if move == (0, 0, 0):
            hops += [((hop, 0, 0), (hop, 0, 0)) for hop in range(1, place.spans[0])]
        for step, landing in reversed(hops):
            index = place.slot(*landing)
            remote(
                source,
                target,
                self.send_sem.at[which, index],
                self.recv_sem.at[which, index],
                {"narrow": place.at(*step)},
            ).start()
        if move != (0, 0, 0):
            index = place.slot(*move)
            remote(
                source,
                target,
                self.core_send.at[which, index],
                self.core_recv.at[which, index],
                place.other,
            ).start()

    def local(self, place, which):
        return pltpu.make_async_copy(
            self.own[which], self.whole[which].at[place.at(0, 0, 0)], self.local_sem.at[which]
        )

    def start(self):
        place = Place(self.dims)
        place.greet()
        for which in range(len(self.own)):
            self.onward(place, which, (0, 0, 0))
        for which in range(len(self.own)):
            self.local(place, which).start()

    def leg(self, number):
        place = Place(self.dims)
        for which in range(len(self.own)):
            for move in place.moves():
                d, e, f = move
                if (number == 3) != (f > 0):
                    continue
                if number < 3 and (number == 2) != (e > 0):
                    continue
                if move == (0, 0, 0):
                    continue
                index = place.slot(*move)
                landed = side_of(self.whole[which].at[place.behind(*move)], place.core)
                remote(
                    landed,
                    landed,
                    self.send_sem.at[which, index],
                    self.recv_sem.at[which, index],
                    place.other,
                ).wait_recv()
                self.onward(place, which, move)

    def finish(self):
        place = Place(self.dims)
        mirror = Place(self.dims, swapped=True)
        for which in range(len(self.own)):
            for move in place.moves():
                if move == (0, 0, 0):
                    continue
                index = place.slot(*move)
                landed = side_of(self.whole[which].at[mirror.behind(*move)], 1 - place.core)
                handed = remote(
                    landed,
                    landed,
                    self.core_send.at[which, index],
                    self.core_recv.at[which, index],
                    place.other,
                )
                handed.wait_recv()
                handed.wait_send()
                remote(
                    landed,
                    landed,
                    self.send_sem.at[which, index],
                    self.recv_sem.at[which, index],
                    place.other,
                ).wait_send()
            self.local(place, which).wait()


class Reduce:
    def __init__(self, dims, grads, held, sems, results, targets):
        self.dims, self.grads = dims, grads
        count = len(grads)
        self.mine, self.swapped, self.third, self.second, self.first = (
            held[index * count : (index + 1) * count] for index in range(5)
        )
        (
            self.local_sem,
            self.core_send,
            self.core_recv,
            self.leg_send,
            self.leg_recv,
            self.last_send,
            self.last_recv,
        ) = sems
        self.results, self.targets = results, targets

    @staticmethod
    def rooms(dims, grads):
        depth, tall, wide = dims
        number = depth * tall * wide
        places = (number, number, depth * wide * (tall - 1), depth * (wide - 1), depth - 1)
        return [
            pltpu.VMEM((room,) + tuple(half_shape(grad)), grad.dtype) for room in places for grad in grads
        ]

    @staticmethod
    def sems(dims, count):
        number = dims[0] * dims[1] * dims[2]
        return [pltpu.SemaphoreType.DMA((count, number))] * 5 + [pltpu.SemaphoreType.DMA((count,))] * 2

    def order(self, place):
        return sorted(place.moves(), key=lambda item: (item[2] == 0, item[1] == 0, item[0] == 0))

    def share(self, which, side):
        result, first = self.targets[which]
        if len(self.grads[which].shape) == 4:
            return self.results[result].at[side]
        width = self.grads[which].shape[2]
        columns = pl.ds(pl.multiple_of(first + side * (width // 2), lanes), width // 2)
        return self.results[result].at[:, columns]

    def load(self, place, which, move):
        return pltpu.make_async_copy(
            side_of(self.grads[which].at[place.at(*move)], place.core),
            self.mine[which].at[place.slot(*move)],
            self.local_sem.at[which, place.slot(*move)],
        )

    def swap(self, place, which, move, mirror):
        index = place.slot(*move)
        return remote(
            side_of(self.grads[which].at[mirror.at(*move)], 1 - place.core),
            self.swapped[which].at[index],
            self.core_send.at[which, index],
            self.core_recv.at[which, index],
            place.other,
        )

    def start(self):
        place, mirror = Place(self.dims), Place(self.dims, swapped=True)
        place.greet()
        for move in self.order(place):
            for which in range(len(self.grads)):
                self.swap(place, which, move, mirror).start()
                self.load(place, which, move).start()

    def landing(self, place, which, move):
        d, e, f = move
        if f > 0:
            return self.third[which].at[(d * place.spans[1] + e) * (place.spans[2] - 1) + f - 1], (0, 0, f)
        if e > 0:
            return self.second[which].at[d * (place.spans[1] - 1) + e - 1], (0, e, 0)
        return self.first[which].at[d - 1], (d, 0, 0)

    def hop(self, place, which, move):
        landing, step = self.landing(place, which, move)
        index = place.slot(*move)
        return remote(
            self.mine[which].at[index],
            landing,
            self.leg_send.at[which, index],
            self.leg_recv.at[which, index],
            {"narrow": place.at(*step)},
        )

    def collect(self, place, which, move):
        d, e, f = move
        index = place.slot(*move)
        self.load(place, which, move).wait()
        handed = self.swapped[which].at[index]
        remote(
            handed, handed, self.core_send.at[which, index], self.core_recv.at[which, index], place.other
        ).wait_recv()
        parts = [handed]
        coming = []
        if f == 0:
            coming += [(d, e, hop) for hop in range(1, place.spans[2])]
        if f == 0 and e == 0:
            coming += [(d, hop, 0) for hop in range(1, place.spans[1])]
        if move == (0, 0, 0):
            coming += [(hop, 0, 0) for hop in range(1, place.spans[0])]
        for source in coming:
            self.hop(place, which, source).wait_recv()
            parts.append(self.landing(place, which, source)[0])
        return parts

    def added(self, place, which, move, parts, store, carry):
        block = self.mine[which].at[place.slot(*move)]
        rows = block.shape[0]
        group = min(rows, 16)

        def some(index, carry):
            at_rows = pl.ds(pl.multiple_of(index * group, group), group)
            total = block[at_rows, :].astype(jnp.float32)
            for part in parts:
                total = total + part[at_rows, :].astype(jnp.float32)
            return store(block, at_rows, total, carry)

        return lax.fori_loop(0, rows // group, some, carry)

    def leg(self, number):
        place = Place(self.dims)

        def keep(block, at_rows, total, carry):
            block[at_rows, :] = total.astype(block.dtype)
            return carry

        for move in self.order(place)[:-1]:
            d, e, f = move
            if number != (1 if f > 0 else 2 if e > 0 else 3):
                continue
            for which in range(len(self.grads)):
                parts = self.collect(place, which, move)
                self.added(place, which, move, parts, keep, 0)
                self.hop(place, which, move).start()

    def finish(self, plain_at, plain_ref):
        place, mirror = Place(self.dims), Place(self.dims, swapped=True)
        squares = (jnp.zeros((8, lanes), jnp.float32),) * 2
        for which in range(len(self.grads)):
            parts = self.collect(place, which, (0, 0, 0))
            result = self.share(which, place.core)

            def store(block, at_rows, total, carry, which=which, result=result):
                result[at_rows, :] = total
                kept, plain = carry
                squared = total * total
                if which == plain_at:
                    marked = squared * plain_ref[place.core, at_rows, :]
                    plain = plain + folded_squares(marked)
                    squared = squared - marked
                return (kept + folded_squares(squared), plain)

            squares = self.added(place, which, (0, 0, 0), parts, store, squares)
            remote(result, result, self.last_send.at[which], self.last_recv.at[which], place.other).start()
        return squares

    def settle(self):
        place, mirror = Place(self.dims), Place(self.dims, swapped=True)
        for which in range(len(self.grads)):
            result = self.share(which, 1 - place.core)
            last = remote(result, result, self.last_send.at[which], self.last_recv.at[which], place.other)
            last.wait_recv()
            last.wait_send()
            for move in place.moves():
                self.swap(place, which, move, mirror).wait_send()
                if move != (0, 0, 0):
                    self.hop(place, which, move).wait_send()


def folded_squares(values):
    total = None
    if values.shape[1] < lanes:
        first = lax.broadcasted_iota(jnp.int32, (values.shape[0], lanes), 1) == 0
        values = jnp.where(first, jnp.sum(values, axis=1, keepdims=True), 0.0)
    for row in range(0, values.shape[0], 8):
        for column in range(0, values.shape[1], lanes):
            piece = values[row : row + 8, column : column + lanes]
            total = piece if total is None else total + piece
    return total


def gather_kernel(dims, plan, names, *refs):
    smalls, bigs = refs[: len(names)], refs[len(names) : len(names) + 1]
    refs = refs[len(names) + 1 :]
    whole, own, pack_buf, sems = refs[:2], refs[2:4], refs[4], refs[5:]
    pack_buf[...] = jnp.zeros_like(pack_buf)
    for name, ref in zip(names, smalls):
        first, tall = plan[name]
        pack_buf[first : first + tall, : ref.shape[1]] = ref[...]
    tall = pack_buf.shape[0] // 2
    for side in range(2):
        own[0][side] = pack_buf[side * tall : (side + 1) * tall, :].astype(own[0].dtype)
    own[1][...] = bigs[0][...].astype(own[1].dtype)
    gather = Gather(dims, own, whole, sems)
    gather.start()
    for number in (1, 2, 3):
        gather.leg(number)
    gather.finish()


def gather_weights(dims, plan, smalls, big):
    number = dims[0] * dims[1] * dims[2]
    names = list(smalls)
    width = smalls["select"].shape[1]
    owned = [shape((2, plan["rows"] // 2, width), jnp.bfloat16), shape(big.shape, jnp.bfloat16)]
    inside = pl.BlockSpec(memory_space=pltpu.VMEM)
    return pl.pallas_call(
        functools.partial(gather_kernel, dims, plan, names),
        in_specs=[inside] * (len(names) + 1),
        out_specs=[pl.BlockSpec(memory_space=pl.ANY)] * 2,
        out_shape=[shape((number,) + kind.shape, kind.dtype) for kind in owned],
        scratch_shapes=[pltpu.VMEM(kind.shape, kind.dtype) for kind in owned]
        + [pltpu.VMEM((plan["rows"], width), jnp.float32)]
        + Gather.scratch(2, dims),
        compiler_params=pltpu.CompilerParams(
            collective_id=0, has_side_effects=True, vmem_limit_bytes=60 * 1024 * 1024
        ),
        name="gather_weights",
    )(*smalls.values(), big)


def reduce_kernel(dims, count, results, targets, plain_at, *refs):
    grads, plain_ref, earlier_ref = refs[:count], refs[count], refs[count + 1]
    refs = refs[count + 2 :]
    sums, norms = refs[:results], refs[results]
    refs = refs[results + 1 :]
    held, buffers = refs[: 5 * count], refs[5 * count : 5 * count + 4]
    refs = refs[5 * count + 4 :]
    sems, (norm_send, norm_recv) = refs[:7], refs[7:]
    reduce = Reduce(dims, grads, held, sems, sums, targets)
    reduce.start()
    for number in (1, 2, 3):
        reduce.leg(number)
    kept, plain = reduce.finish(plain_at, plain_ref)
    running = jnp.stack([kept + earlier_ref[...], plain])

    place = Place(dims)
    depth, tall, wide = dims
    plane = tall * wide
    me = place.me
    stages = (
        (buffers[0], 2, place.core, lambda spot: {"wide": spot}),
        (buffers[1], depth, place.deep, lambda spot: {"narrow": spot * plane + lax.rem(me, plane)}),
        (buffers[2], wide, place.across, lambda spot: {"narrow": me - place.across + spot}),
        (buffers[3], tall, place.up, lambda spot: {"narrow": me + (spot - place.up) * wide}),
    )
    pending = []
    first = 0
    for buffer, size, mine_at, device in stages:
        buffer[mine_at] = running
        for hop in range(1, size):
            copy = remote(
                buffer.at[mine_at],
                buffer.at[mine_at],
                norm_send.at[first + hop - 1],
                norm_recv.at[first + hop - 1],
                device(lax.rem(mine_at + hop, size)),
            )
            copy.start()
            pending.append(copy)
        for hop in range(1, size):
            came = lax.rem(mine_at + size - hop, size)
            remote(
                buffer.at[came],
                buffer.at[came],
                norm_send.at[first + hop - 1],
                norm_recv.at[first + hop - 1],
                device(came),
            ).wait_recv()
        first += size - 1
        running = buffer[0]
        for spot in range(1, size):
            running = running + buffer[spot]
    norms[...] = running
    reduce.settle()
    for copy in pending:
        copy.wait_send()


def sum_shapes(grads, targets):
    sums = []
    for index in range(1 + max(target[0] for target in targets)):
        members = [grad for grad, target in zip(grads, targets) if target[0] == index]
        if len(members[0].shape) == 4:
            sums.append(shape(members[0].shape[1:]))
        else:
            sums.append(shape((members[0].shape[1], sum(grad.shape[2] for grad in members))))
    return sums


def reduce_grads(dims, grads, targets, plain_mask, plain_at, earlier):
    depth, tall, wide = dims
    count = len(grads)
    anywhere = pl.BlockSpec(memory_space=pl.ANY)
    inside = pl.BlockSpec(memory_space=pltpu.VMEM)
    sums = sum_shapes(grads, targets)
    result = pl.pallas_call(
        functools.partial(reduce_kernel, dims, count, len(sums), targets, plain_at),
        in_specs=[anywhere] * count + [inside] * 2,
        out_specs=[inside] * (len(sums) + 1),
        out_shape=sums + [shape((2, 8, lanes))],
        scratch_shapes=Reduce.rooms(dims, grads)
        + [pltpu.VMEM((size, 2, 8, lanes), jnp.float32) for size in (2, depth, wide, tall)]
        + Reduce.sems(dims, count)
        + [pltpu.SemaphoreType.DMA((depth + tall + wide,))] * 2,
        compiler_params=pltpu.CompilerParams(
            collective_id=1, has_side_effects=True, vmem_limit_bytes=56 * 1024 * 1024
        ),
        name="reduce_grads",
    )(*grads, plain_mask, earlier)
    return result[: len(sums)], result[len(sums)]


def grid_of(mesh):
    number = mesh.shape["narrow"]
    places = [getattr(device, "coords", None) for device in mesh.devices[0]]
    if all(place is not None for place in places):
        sizes = [len({place[axis] for place in places}) for axis in (2, 1, 0)]
        if sizes[0] * sizes[1] * sizes[2] == number:
            return tuple(sizes)
    side = round((number / 2) ** (1 / 3))
    return (2 * side, side, side) if 2 * side**3 == number else (number, 1, 1)


def plan_of(select_rows, state_size, tap_count, step_rows):
    plan, first = {}, 0
    for name, tall in (
        ("select", select_rows),
        ("decay", state_size),
        ("taps", tap_count),
        ("shift", 1),
        ("bias", 1),
        ("skip", 1),
        ("gain", 1),
    ):
        plan[name] = (first, tall)
        first += tall
    plan["step"] = (lanes, step_rows)
    plan["rows"] = -(-(lanes + step_rows) // 32) * 32
    return plan


def per_device(
    dims,
    tokens,
    cotangent,
    loss_mask,
    seq_lengths,
    norm_gain,
    in_proj,
    conv_weight,
    conv_bias,
    select_proj,
    step_proj,
    step_bias,
    decay_log,
    skip_scale,
    out_proj,
):
    half = jnp.bfloat16
    piece = skip_scale.shape[0]
    gain_piece = norm_gain.shape[0]
    rank, size = step_proj.shape[0], decay_log.shape[0]
    plan = plan_of(select_proj.shape[0], size, conv_weight.shape[0], rank)
    small_blocks, in_blocks = gather_weights(
        dims,
        plan,
        {
            "select": select_proj,
            "decay": decay_log,
            "taps": conv_weight,
            "shift": conv_bias[None],
            "bias": step_bias[None],
            "skip": skip_scale[None],
            "gain": norm_gain[None],
            "step": step_proj,
        },
        in_proj,
    )
    in_whole = in_blocks.reshape(-1, in_blocks.shape[2])
    small_blocks = small_blocks.reshape(-1, plan["rows"], piece)
    small = jnp.swapaxes(small_blocks, 0, 1).reshape(plan["rows"], -1)
    gain_value = small_blocks[:, plan["gain"][0], :gain_piece].reshape(1, -1).astype(jnp.float32)

    rows, model = tokens.shape
    inner = small.shape[1]
    width = 4 * lanes
    blocks = inner // width
    chunks = rows // chunk
    mask_row = loss_mask[None]

    whole = pl.BlockSpec(memory_space=pltpu.VMEM)
    tall = pl.BlockSpec((rows, width), lambda b: (0, b))
    deep = pl.BlockSpec((chunks, chunk, width), lambda b: (0, 0, b))
    lead = pl.BlockSpec((rows, size, width), lambda b: (0, 0, b))
    first_w = pl.BlockSpec((model, width), lambda b: (0, b))
    second_w = pl.BlockSpec((model, width), lambda b: (0, b + blocks))
    out_w = pl.BlockSpec((width, model), lambda b: (b, 0))

    def thin(height):
        return pl.BlockSpec((height, width), lambda b: (0, b))

    def fixed(*dims_of):
        return pl.BlockSpec(dims_of, lambda b: (0,) * len(dims_of))

    scalars = pl.BlockSpec(memory_space=pltpu.SMEM)
    offset_buf = pltpu.VMEM((rows + 8, lanes), jnp.int32)
    packed = thin(plan["rows"])

    pair = (chunks, 2 * chunk, lanes)
    (
        branch,
        gate_pre,
        signal,
        slope,
        projected,
        flipped,
        grad_low,
        write_pair,
        read_pair,
    ) = compute_call(
        functools.partial(front_kernel, plan),
        "front",
        blocks,
        [scalars, whole, whole, whole, whole, packed, first_w, second_w],
        [tall, tall, tall, tall, fixed(rows, lanes), fixed(model, rows), fixed(rows, model)]
        + [fixed(*pair)] * 2,
        [
            shape((rows, inner)),
            shape((rows, inner)),
            shape((rows, inner), half),
            shape((rows, inner)),
            shape((rows, lanes)),
            shape((model, rows), half),
            shape((rows, model), half),
        ]
        + [shape(pair, half)] * 2,
        [pltpu.VMEM((rows, model), half), offset_buf],
        4 * rows * model * inner,
        (seq_lengths, tokens, cotangent, mask_row, gain_value, small, in_whole, in_whole),
    )
    row_block = pltpu.VMEM((chunks, chunk, width), jnp.float32)
    spare_block = pltpu.VMEM((chunks + 1, chunk, width), jnp.float32)
    number = small_blocks.shape[0]
    anywhere = pl.BlockSpec(memory_space=pl.ANY)
    states, step, core, out_blocks = compute_call(
        functools.partial(forward_kernel, plan, dims),
        "forward",
        blocks,
        [scalars, whole, packed, tall, whole, whole, whole],
        [lead, deep, deep, anywhere],
        [
            shape((rows, size, inner), half),
            shape((chunks, chunk, inner)),
            shape((chunks, chunk, inner)),
            shape((number,) + out_proj.shape, half),
        ],
        [
            offset_buf,
            pltpu.VMEM((rows, width), jnp.float32),
            row_block,
            row_block,
            pltpu.VMEM((chunk * size, lanes), jnp.float32),
            pltpu.VMEM((chunk * size, lanes), jnp.float32),
            pltpu.VMEM(out_proj.shape, half),
        ]
        + Gather.scratch(1, dims),
        15 * rows * inner * size,
        (seq_lengths, projected, small, signal, write_pair, read_pair, out_proj),
        collective_id=2,
    )
    core_grad, gate_grad, grad_skip, grad_outw, grad_in_gate, output = compute_call(
        functools.partial(middle_kernel, plan),
        "middle",
        blocks,
        [deep, packed, tall, tall, whole, out_w, whole, whole],
        [deep, tall, thin(1), out_w, first_w, fixed(rows, model)],
        [
            shape((chunks, chunk, inner)),
            shape((rows, inner), half),
            shape((1, inner)),
            shape((inner, model), half),
            shape((model, inner), half),
            shape((rows, model), half),
        ],
        [
            pltpu.VMEM((rows, width), jnp.float32),
            pltpu.VMEM((rows, width), half),
            pltpu.VMEM((rows, model), jnp.float32),
        ],
        8 * rows * model * inner,
        (core, small, signal, gate_pre, grad_low, out_blocks.reshape(inner, model), flipped, tokens),
    )
    split = in_blocks.shape[:2] + (inner,)
    early_grads = [grad_outw.reshape(out_blocks.shape), grad_in_gate.reshape(split)]
    early_sums = sum_shapes(early_grads, [(0, 0), (1, 0)])
    (
        signal_grad,
        grad_stepw,
        grad_bias,
        grad_decaylog,
        flat,
        out_sum,
        in_gate_sum,
        early_squares,
    ) = compute_call(
        functools.partial(backward_kernel, plan, dims),
        "backward",
        blocks,
        [scalars, whole, packed, tall, whole, whole, deep, deep, lead, anywhere, anywhere],
        [tall, thin(rank), thin(1), thin(size), fixed(rows, lanes)]
        + [whole] * 3,
        [
            shape((rows, inner)),
            shape((rank, inner)),
            shape((1, inner)),
            shape((size, inner)),
            shape((rows, lanes), half),
            *early_sums,
            shape((8, lanes)),
        ],
        [
            offset_buf,
            row_block,
            pltpu.VMEM((chunks + 1, 2 * chunk, width), half),
            pltpu.VMEM((chunks, 2 * chunk, width), half),
            pltpu.VMEM((chunk * size, lanes), jnp.float32),
            pltpu.VMEM((chunk * size, lanes), jnp.float32),
            pltpu.VMEM((chunk * size, width), half),
            pltpu.VMEM((chunk * size, width), half),
            pltpu.VMEM((chunk * size, width), half),
            pltpu.VMEM((chunk * size, width), half),
            spare_block,
            spare_block,
            pltpu.VMEM((rows, width), half),
            pltpu.VMEM((chunks, chunk, lanes), jnp.float32),
            pltpu.VMEM((chunks + 1, size, 2 * chunk), jnp.float32),
            pltpu.VMEM((chunks, size, 2 * chunk), jnp.float32),
        ]
        + [pltpu.VMEM(early.shape, early.dtype) for early in early_sums]
        + Reduce.rooms(dims, early_grads)
        + Reduce.sems(dims, 2),
        40 * rows * inner * size,
        (seq_lengths, projected, small, signal, write_pair, read_pair, step, core_grad, states, *early_grads),
        collective_id=3,
    )

    small_grad, grad_in_branch, grad_gain, grad_tokens = compute_call(
        functools.partial(back_kernel, plan),
        "back",
        blocks,
        [scalars, whole, whole, whole, packed, whole, tall, tall, tall, tall, tall, whole, first_w, second_w]
        + [thin(rank), thin(1), thin(size), thin(1)],
        [packed, first_w, fixed(1, model), fixed(rows, model)],
        [
            shape((plan["rows"], inner)),
            shape((model, inner), half),
            shape((1, model)),
            shape((rows, model), half),
        ],
        [
            offset_buf,
            pltpu.VMEM((rows + 8, width), jnp.float32),
            pltpu.VMEM((rows, width), half),
            pltpu.VMEM((rows, model), jnp.float32),
        ],
        8 * rows * model * inner,
        (
            seq_lengths,
            tokens,
            grad_low,
            gain_value,
            small,
            flat,
            branch,
            signal,
            slope,
            signal_grad,
            gate_grad,
            flipped,
            in_whole,
            in_whole,
            grad_stepw,
            grad_bias,
            grad_decaylog,
            grad_skip,
        ),
    )

    gain_rows = jnp.pad(grad_gain.reshape(number, 1, gain_piece), ((0, 0), (0, 0), (0, piece - gain_piece)))
    place = plan["gain"][0]
    small_grad = jnp.swapaxes(small_grad.reshape(plan["rows"], number, piece), 0, 1) + jnp.pad(
        gain_rows, ((0, 0), (place, plan["rows"] - place - 1), (0, 0))
    )
    plain_rows = np.zeros((plan["rows"], piece), np.float32)
    for name in ("bias", "decay", "skip"):
        first, count = plan[name]
        plain_rows[first : first + count] = 1.0
    halves = (2, plan["rows"] // 2, piece)
    (in_branch_sum, small_sum), norms = reduce_grads(
        dims,
        [grad_in_branch.reshape(split), small_grad.reshape((number,) + halves)],
        [(0, 0), (1, 0)],
        jnp.asarray(plain_rows.reshape(halves)),
        1,
        early_squares,
    )
    names = ("gain", "taps", "shift", "select", "step", "bias", "decay", "skip")
    own = (norm_gain, conv_weight, conv_bias, select_proj, step_proj, step_bias, decay_log, skip_scale)
    in_grad, out_grad, gain_grad, *small_grads, decay_sq, plain_sq = pl.pallas_call(
        functools.partial(finish_kernel, plan, names),
        in_specs=[whole] * 5,
        out_specs=[whole] * (2 + len(names)) + [scalars] * 2,
        out_shape=[shape(in_proj.shape), shape(out_proj.shape)]
        + [shape(array.shape) for array in own]
        + [shape((1, 1))] * 2,
        name="finish",
    )(in_branch_sum, in_gate_sum, out_sum, small_sum.reshape(plan["rows"], piece), norms)
    return (
        output,
        grad_tokens,
        gain_grad,
        in_grad,
        *small_grads,
        out_grad,
        decay_sq[0, 0],
        plain_sq[0, 0],
    )


def solution(mesh):
    placed = (
        P(("wide", "narrow"), None),
        P(("wide", "narrow"), None),
        P(("wide", "narrow")),
        P(("wide", "narrow"), None),
        P("narrow"),
        P("narrow", None),
        P(None, "narrow"),
        P("narrow"),
        P(None, "narrow"),
        P(None, "narrow"),
        P("narrow"),
        P(None, "narrow"),
        P("narrow"),
        P("narrow", None),
    )
    return jax.shard_map(
        functools.partial(per_device, grid_of(mesh)),
        mesh=mesh,
        in_specs=placed,
        out_specs=(
            P(("wide", "narrow"), None),
            P(("wide", "narrow"), None),
            P("narrow"),
            P("narrow", None),
            P(None, "narrow"),
            P("narrow"),
            P(None, "narrow"),
            P(None, "narrow"),
            P("narrow"),
            P(None, "narrow"),
            P("narrow"),
            P("narrow", None),
            P(),
            P(),
        ),
        check_vma=False,
    )
```

```python
import functools
import math

import jax
import jax.numpy as jnp
import numpy as np
from jax import lax
from jax.experimental import pallas as pl
from jax.experimental.pallas import tpu as pltpu
from jax.sharding import PartitionSpec as P

epsilon = 1e-05
chunk = 8
lanes = 128
log2e = math.log2(math.e)
ln2 = math.log(2.0)
far = 1e30


def contract(left, right, left_dim, right_dim):
    return lax.dot_general(
        left, right, (((left_dim,), (right_dim,)), ((), ())), preferred_element_type=jnp.float32
    )


def row_loop(rows, group, body, initial):
    def some(index, carry):
        return body(index, pl.ds(pl.multiple_of(index * group, group), group), carry)

    return lax.fori_loop(0, rows // group, some, initial)


def cut(tile):
    return pl.ds(tile * lanes, lanes)


def sigmoid(values):
    return 0.5 * jnp.tanh(0.5 * values) + 0.5


def softplus(values):
    small = jnp.exp(-jnp.abs(values))
    series = small * (1.0 - small * (0.5 - small * (1.0 / 3.0 - 0.25 * small)))
    return jnp.maximum(values, 0.0) + jnp.where(small < 0.03, series, jnp.log(1.0 + small))


def slope_of(step):
    series = step * (1.0 - step * (0.5 - step * (1.0 / 6.0 - step * (1.0 / 24.0))))
    return jnp.where(step < 0.03, series, 1.0 - jnp.exp(-step))


def fill_offsets(lengths_ref, offset_buf, rows):
    place = lax.broadcasted_iota(jnp.int32, offset_buf.shape, 0)
    start = jnp.zeros(offset_buf.shape, jnp.int32)
    ahead = jnp.int32(0)
    for index in range(lengths_ref.shape[1] - 1):
        ahead = ahead + lengths_ref[0, index]
        start = jnp.where(place >= ahead, ahead, start)
    offset_buf[...] = jnp.where(place < rows, place - start, 0)


def small_rows(small_ref, first, count):
    base = first // 16 * 16
    tall = -(-(first + count - base) // 16) * 16
    return small_ref[base : base + tall, :].astype(jnp.float32)[first - base : first - base + count]


def eight(values):
    total = values[:8]
    for row in range(8, values.shape[0], 8):
        total = total + values[row : row + 8]
    return total


def conv_rows(index, at, group, tile, branch_ref, offset_buf, taps, shift):
    count = taps.shape[0]
    here = slice(tile * lanes, (tile + 1) * lanes)
    current = branch_ref[at, cut(tile)]
    before = branch_ref[pl.ds(pl.multiple_of(jnp.maximum(index * group - 8, 0), 8), 8), cut(tile)]
    both = jnp.concatenate([before, current], axis=0)
    offsets = offset_buf[at, :]
    summed = shift[:, here] + taps[count - 1 : count, here] * current
    for tap in range(count - 1):
        lag = count - 1 - tap
        read = jnp.where(offsets >= lag, pltpu.roll(both, lag, 0)[8:], 0.0)
        summed = summed + taps[tap : tap + 1, here] * read
    return summed


def front_kernel(
    plan,
    lengths_ref,
    tokens_ref,
    cotangent_ref,
    mask_ref,
    gain_ref,
    small_ref,
    branch_w,
    gate_w,
    branch_ref,
    gate_ref,
    signal_ref,
    slope_ref,
    projected_ref,
    flipped_ref,
    low_ref,
    write_pair,
    read_pair,
    normed_buf,
    offset_buf,
):
    rows = tokens_ref.shape[0]
    width = branch_ref.shape[1]
    block = pl.program_id(0)

    @pl.when(block == 0)
    def _():
        fill_offsets(lengths_ref, offset_buf, rows)

        def norm(index, at, carry):
            residual = tokens_ref[at, :].astype(jnp.float32)
            scale = lax.rsqrt(jnp.mean(residual * residual, axis=1, keepdims=True) + epsilon)
            normed_buf[at, :] = (residual * scale * gain_ref[...]).astype(normed_buf.dtype)
            return carry

        row_loop(rows, 16, norm, 0)
        flipped_ref[...] = normed_buf[...].T
        projected_ref[...] = jnp.zeros_like(projected_ref)
        down = lax.broadcasted_iota(jnp.int32, (rows, rows), 0)
        along = lax.broadcasted_iota(jnp.int32, (rows, rows), 1)
        diagonal = jnp.where(down == along, mask_ref[...].astype(jnp.float32), 0.0).astype(low_ref.dtype)
        low_ref[...] = jnp.dot(
            diagonal, cotangent_ref[...], preferred_element_type=jnp.float32
        ).astype(low_ref.dtype)

    branch_ref[...] = jnp.dot(normed_buf[...], branch_w[...], preferred_element_type=jnp.float32)
    gate_ref[...] = jnp.dot(normed_buf[...], gate_w[...], preferred_element_type=jnp.float32)
    taps = small_rows(small_ref, *plan["taps"])
    shift = small_rows(small_ref, *plan["shift"])

    def some(index, at, carry):
        for tile in range(width // lanes):
            summed = conv_rows(index, at, 32, tile, branch_ref, offset_buf, taps, shift)
            sigma = sigmoid(summed)
            active = summed * sigma
            signal_ref[at, cut(tile)] = active.astype(signal_ref.dtype)
            slope_ref[at, cut(tile)] = sigma + active * (1.0 - sigma)
        return carry

    row_loop(rows, 32, some, 0)
    projected_ref[...] += contract(signal_ref[...], small_ref[:lanes, :], 1, 1)

    @pl.when(block == pl.num_programs(0) - 1)
    def _():
        high, low = high_low(projected_ref[...])
        own = own_tokens(rows)
        rank = plan["step"][1]
        size = plan["decay"][1]
        entry = lax.broadcasted_iota(jnp.int32, (lanes, lanes), 0)
        lane = lax.rem(lax.broadcasted_iota(jnp.int32, (lanes, lanes), 1), size)
        for first, pair in ((rank, write_pair), (rank + size, read_pair)):
            spread = (entry == lane + first).astype(jnp.bfloat16)
            parts = [
                (jnp.dot(part.astype(jnp.bfloat16), spread, preferred_element_type=jnp.float32) * own).reshape(
                    rows // chunk, chunk, lanes
                )
                for part in (high, low)
            ]
            pair[...] = jnp.concatenate(parts, axis=1).astype(pair.dtype)


def high_low(values):
    high = values.astype(jnp.bfloat16).astype(jnp.float32)
    return high, values - high


def own_tokens(rows):
    token = lax.rem(lax.broadcasted_iota(jnp.int32, (rows, lanes), 0), chunk)
    return (token == lax.div(lax.broadcasted_iota(jnp.int32, (rows, lanes), 1), lanes // chunk)).astype(
        jnp.float32
    )


def spread_rows(pair):
    return contract(pair, jnp.ones((pair.shape[0], lanes), pair.dtype), 0, 0)


def folded(buffer, tile):
    total = buffer[tile, pl.ds(0, chunk, stride=chunk), :]
    for row in range(1, chunk):
        total = total + buffer[tile, pl.ds(row, chunk, stride=chunk), :]
    return total


def forward_kernel(
    plan,
    dims,
    lengths_ref,
    projected_ref,
    small_ref,
    signal_ref,
    write_pair,
    read_pair,
    own_ref,
    states_ref,
    step_ref,
    core_ref,
    begin_ref,
    whole_ref,
    offset_buf,
    pre_buf,
    decay_step,
    flows,
    write_a,
    write_b,
    read_a,
    read_b,
    fold_a,
    fold_b,
    held_buf,
    low_buf,
    *sems,
):
    rows, width = pre_buf.shape
    size = plan["decay"][1]
    half = size // 2
    tiles = width // lanes
    chunks = rows // chunk
    rank = plan["step"][1]
    group = pl.program_id(1)
    groups = pl.num_programs(1)
    moment = pl.program_id(0) * groups + group
    moments = pl.num_programs(0) * groups
    gather = Gather(dims, [low_buf], [whole_ref], sems)

    @pl.when(moment == 0)
    def _():
        low_buf[...] = own_ref[...].astype(low_buf.dtype)
        gather.start()
        fill_offsets(lengths_ref, offset_buf, offset_buf.shape[0] - 8)

    for number, when in ((1, 5), (2, 9), (3, 13)):

        @pl.when(moment == when)
        def _(number=number):
            gather.leg(number)

    @pl.when(group == 0)
    def _():
        held_buf[...] = jnp.zeros_like(held_buf)

    begin_ref[0] = held_buf[...]
    pre_buf[...] = jnp.dot(
        projected_ref[:, :rank].astype(small_ref.dtype),
        small_ref[pl.ds(plan["step"][0], rank), :],
        preferred_element_type=jnp.float32,
    )
    bias = small_rows(small_ref, *plan["bias"])

    def before(index, at, carry):
        spot = pl.ds(pl.multiple_of(index * 4, 4), 4)
        inside = offset_buf[pl.ds(pl.multiple_of(group * rows + index * 32, 32), 32), :] > 0
        for tile in range(tiles):
            step = softplus(pre_buf[at, cut(tile)] + bias[:, tile * lanes : (tile + 1) * lanes])
            step_ref[spot, :, cut(tile)] = step.reshape(4, chunk, lanes)
            decay_step[spot, :, cut(tile)] = jnp.where(inside, step, far).reshape(4, chunk, lanes)
            flow = step * signal_ref[at, cut(tile)].astype(jnp.float32)
            flows[spot, :, cut(tile)] = flow.reshape(4, chunk, lanes)
        return carry

    row_loop(rows, 4 * chunk, before, 0)
    rates = -jnp.exp(small_rows(small_ref, *plan["decay"])) * log2e
    rates = [rates[:, tile * lanes : (tile + 1) * lanes] for tile in range(tiles)]

    def enter(index, write_rows, read_rows):
        write_rows[...] = spread_rows(write_pair[index])
        read_rows[...] = spread_rows(read_pair[index])

    def leave(index, fold_buf):
        for tile in range(tiles):
            core_ref[index, :, cut(tile)] = folded(fold_buf, tile)

    def advance(index, held, write_rows, read_rows, fold_buf):
        held = list(held)
        for place in range(chunk):
            lot = pl.ds(place * size, size)
            write_now = write_rows[lot, :]
            read_now = read_rows[lot, :]
            for tile in range(tiles):
                decay = jnp.exp2(rates[tile] * decay_step[index, pl.ds(place, 1), cut(tile)])
                fresh = decay * held[tile] + write_now * flows[index, pl.ds(place, 1), cut(tile)]
                held[tile] = fresh
                states_ref[index * chunk + place, :, cut(tile)] = fresh
                product = read_now * fresh
                fold_buf[tile, pl.ds(place * chunk, chunk), :] = product[:half] + product[half:]
        return tuple(held)

    def forward(pair, held):
        index = 2 * pair
        enter(index + 1, write_b, read_b)
        leave(jnp.maximum(index - 1, 0), fold_b)
        held = advance(index, held, write_a, read_a, fold_a)
        enter(jnp.minimum(index + 2, chunks - 1), write_a, read_a)
        leave(index, fold_a)
        return advance(index + 1, held, write_b, read_b, fold_b)

    enter(0, write_a, read_a)
    held = tuple(held_buf[:, cut(tile)] for tile in range(tiles))
    held = lax.fori_loop(0, chunks // 2, forward, held)
    leave(chunks - 1, fold_b)
    for tile in range(tiles):
        held_buf[:, cut(tile)] = held[tile]

    @pl.when(moment == moments - 1)
    def _():
        gather.finish()


def middle_kernel(
    plan,
    core_ref,
    small_ref,
    signal_ref,
    gate_ref,
    low_ref,
    out_w,
    flipped_ref,
    tokens_ref,
    core_grad_ref,
    gate_grad_ref,
    skip_grad_ref,
    out_grad_ref,
    in_grad_ref,
    output_ref,
    pre_buf,
    gated_buf,
    total,
):
    rows, width = pre_buf.shape
    tiles = width // lanes
    block = pl.program_id(0)
    pre_buf[...] = contract(low_ref[...], out_w[...], 1, 1)
    skip = small_rows(small_ref, *plan["skip"])

    def after(index, at, carry):
        spot = pl.ds(pl.multiple_of(index * 4, 4), 4)
        sums = []
        for tile in range(tiles):
            signal = signal_ref[at, cut(tile)].astype(jnp.float32)
            core = core_ref[spot, :, cut(tile)].reshape(4 * chunk, lanes)
            core = core + skip[:, tile * lanes : (tile + 1) * lanes] * signal
            gate = gate_ref[at, cut(tile)]
            sigma = sigmoid(gate)
            active = gate * sigma
            gated_buf[at, cut(tile)] = (core * active).astype(gated_buf.dtype)
            grad_gated = pre_buf[at, cut(tile)]
            grad_core = grad_gated * active
            core_grad_ref[spot, :, cut(tile)] = grad_core.reshape(4, chunk, lanes)
            slope = sigma + active * (1.0 - sigma)
            gate_grad_ref[at, cut(tile)] = (grad_gated * core * slope).astype(gate_grad_ref.dtype)
            sums.append(carry[tile] + eight(grad_core * signal))
        return tuple(sums)

    zero_rows = jnp.zeros((8, lanes), jnp.float32)
    skips = row_loop(rows, 4 * chunk, after, (zero_rows,) * tiles)
    for tile in range(tiles):
        skip_grad_ref[:, cut(tile)] = jnp.sum(skips[tile], axis=0, keepdims=True)
    out_grad_ref[...] = contract(gated_buf[...], low_ref[...], 0, 0).astype(out_grad_ref.dtype)
    in_grad_ref[...] = jnp.dot(
        flipped_ref[...], gate_grad_ref[...], preferred_element_type=jnp.float32
    ).astype(in_grad_ref.dtype)
    piece = jnp.dot(gated_buf[...], out_w[...], preferred_element_type=jnp.float32)

    @pl.when(block == 0)
    def _():
        total[...] = piece

    @pl.when(block > 0)
    def _():
        total[...] += piece

    @pl.when(block == pl.num_programs(0) - 1)
    def _():
        output_ref[...] = (tokens_ref[...].astype(jnp.float32) + total[...]).astype(output_ref.dtype)


def backward_kernel(
    plan,
    dims,
    lengths_ref,
    projected_ref,
    small_ref,
    signal_ref,
    write_pair,
    read_pair,
    step_ref,
    core_grad_ref,
    states_ref,
    begin_ref,
    out_grad_ref,
    in_grad_ref,
    signal_grad_ref,
    step_w_grad_ref,
    bias_grad_ref,
    decay_grad_ref,
    flat_ref,
    out_sum_ref,
    in_sum_ref,
    square_ref,
    offset_buf,
    decay_step,
    inflow,
    flows,
    grads,
    write_a,
    write_b,
    read_a,
    read_b,
    gone_a,
    gone_b,
    first_a,
    first_b,
    second_a,
    second_b,
    through_buf,
    scaled_buf,
    low_buf,
    incoming_buf,
    rank_buf,
    write_buf,
    read_buf,
    *parts,
):
    rows, width = low_buf.shape
    rank = plan["step"][1]
    size = plan["decay"][1]
    half = size // 2
    tiles = width // lanes
    chunks = rows // chunk
    block = pl.program_id(0)
    turn = pl.program_id(1)
    groups = pl.num_programs(1)
    group = groups - 1 - turn
    moment = block * groups + turn
    moments = pl.num_programs(0) * groups
    reduce = Reduce(
        dims,
        [out_grad_ref, in_grad_ref],
        parts[2:12],
        parts[12:],
        parts[:2],
        [(0, 0), (1, 0)],
    )

    @pl.when(moment == 0)
    def _():
        reduce.start()
        fill_offsets(lengths_ref, offset_buf, offset_buf.shape[0] - 8)
        write_buf[...] = jnp.zeros_like(write_buf)
        read_buf[...] = jnp.zeros_like(read_buf)
        rank_buf[...] = jnp.zeros_like(rank_buf)

    for number, when in ((1, 2), (2, 7), (3, 11)):

        @pl.when(moment == when)
        def _(number=number):
            reduce.leg(number)

    @pl.when(turn == 0)
    def _():
        incoming_buf[...] = jnp.zeros_like(incoming_buf)
        decay_grad_ref[...] = jnp.zeros_like(decay_grad_ref)
        bias_grad_ref[...] = jnp.zeros_like(bias_grad_ref)
        step_w_grad_ref[...] = jnp.zeros_like(step_w_grad_ref)

    def before(index, at, carry):
        spot = pl.ds(pl.multiple_of(index * 4, 4), 4)
        offsets = offset_buf[pl.ds(pl.multiple_of(group * rows + index * 32, 32), 32), :]
        inside = (offsets > 0).reshape(4, chunk, lanes)
        for tile in range(tiles):
            step = step_ref[spot, :, cut(tile)]
            decay_step[spot, :, cut(tile)] = jnp.where(inside, step, far)
            signal = signal_ref[at, cut(tile)].astype(jnp.float32).reshape(4, chunk, lanes)
            flow = step * signal
            flows[spot, :, cut(tile)] = jnp.concatenate(high_low(flow), axis=1)
            grads[spot, :, cut(tile)] = jnp.concatenate(high_low(core_grad_ref[spot, :, cut(tile)]), axis=1)
        return carry

    row_loop(rows, 4 * chunk, before, 0)
    flows[chunks] = jnp.zeros_like(flows[chunks])
    for buffer in (gone_b, first_b, second_b):
        buffer[...] = jnp.zeros_like(buffer)
    rates = -jnp.exp(small_rows(small_ref, *plan["decay"])) * log2e
    rates = [rates[:, tile * lanes : (tile + 1) * lanes] for tile in range(tiles)]
    token_of = lax.rem(lax.broadcasted_iota(jnp.int32, (size, 2 * chunk), 1), chunk)

    def enter(index, write_rows, read_rows):
        write_rows[...] = spread_rows(write_pair[index])
        read_rows[...] = spread_rows(read_pair[index])

    def kept(products):
        result = products[:size]
        for place in range(1, chunk):
            result = jnp.where(token_of == place, products[place * size : (place + 1) * size], result)
        return result

    def settle(index, gone_rows, first, second):
        for tile in range(tiles):
            through_buf[index, :, cut(tile)] = folded(first, tile)
            scaled_buf[index, :, cut(tile)] = folded(second, tile)
        products = contract(gone_rows[...].astype(jnp.bfloat16), flows[index].astype(jnp.bfloat16), 1, 1)
        write_buf[jnp.minimum(group * chunks + index, write_buf.shape[0] - 1)] += kept(products)

    def retreat(index, carried, write_rows, read_rows, gone_rows, first, second):
        base = index * chunk
        here = states_ref[pl.ds(base, chunk)].reshape(chunk * size, width).astype(jnp.bfloat16)
        read_buf[group * chunks + index] += kept(contract(here, grads[index].astype(jnp.bfloat16), 1, 1))
        incoming, decay_sums = list(carried[0]), list(carried[1])
        for place in range(chunk - 1, -1, -1):
            now = base + place
            lot = pl.ds(place * size, size)
            write_now = write_rows[lot, :]
            read_now = read_rows[lot, :]
            for tile in range(tiles):
                step_now = decay_step[index, pl.ds(place, 1), cut(tile)]
                if place > 0:
                    earlier = states_ref[now - 1, :, cut(tile)]
                else:
                    earlier = jnp.where(
                        index > 0, states_ref[jnp.maximum(now - 1, 0), :, cut(tile)], begin_ref[0, :, cut(tile)]
                    )
                grad_state = incoming[tile] + read_now * core_grad_ref[index, pl.ds(place, 1), cut(tile)]
                gone_rows[lot, cut(tile)] = grad_state
                passed = grad_state * write_now
                first[tile, pl.ds(place * chunk, chunk), :] = passed[:half] + passed[half:]
                leaving = jnp.exp2(rates[tile] * step_now) * grad_state
                incoming[tile] = leaving
                weighted = leaving * earlier
                scaled = weighted * rates[tile]
                second[tile, pl.ds(place * chunk, chunk), :] = scaled[:half] + scaled[half:]
                decay_sums[tile] = decay_sums[tile] + weighted * step_now
        return (tuple(incoming), tuple(decay_sums))

    def backward(pair, carried):
        index = chunks - 1 - 2 * pair
        enter(index - 1, write_b, read_b)
        settle(index + 1, gone_b, first_b, second_b)
        carried = retreat(index, carried, write_a, read_a, gone_a, first_a, second_a)
        enter(jnp.maximum(index - 2, 0), write_a, read_a)
        settle(index, gone_a, first_a, second_a)
        return retreat(index - 1, carried, write_b, read_b, gone_b, first_b, second_b)

    enter(chunks - 1, write_a, read_a)
    incoming = tuple(incoming_buf[:, cut(tile)] for tile in range(tiles))
    nothing = (jnp.zeros((size, lanes), jnp.float32),) * tiles
    incoming, decay_sums = lax.fori_loop(0, chunks // 2, backward, (incoming, nothing))
    settle(0, gone_b, first_b, second_b)
    for tile in range(tiles):
        incoming_buf[:, cut(tile)] = incoming[tile]
        decay_grad_ref[:, cut(tile)] += decay_sums[tile] * rates[tile] * ln2
    skip = small_rows(small_ref, *plan["skip"])

    def after(index, at, carry):
        spot = pl.ds(pl.multiple_of(index * 4, 4), 4)
        sums = []
        for tile in range(tiles):
            signal = signal_ref[at, cut(tile)].astype(jnp.float32)
            step = step_ref[spot, :, cut(tile)].reshape(4 * chunk, lanes)
            through = through_buf[spot, :, cut(tile)].reshape(4 * chunk, lanes)
            scaled = scaled_buf[spot, :, cut(tile)].reshape(4 * chunk, lanes)
            core_grad = core_grad_ref[spot, :, cut(tile)].reshape(4 * chunk, lanes)
            grad_pre = (through * signal + ln2 * scaled) * slope_of(step)
            low_buf[at, cut(tile)] = grad_pre.astype(low_buf.dtype)
            signal_grad_ref[at, cut(tile)] = (
                through * step + skip[:, tile * lanes : (tile + 1) * lanes] * core_grad
            )
            sums.append(carry[tile] + eight(grad_pre))
        return tuple(sums)

    zero_rows = jnp.zeros((8, lanes), jnp.float32)
    sums = row_loop(rows, 4 * chunk, after, (zero_rows,) * tiles)
    for tile in range(tiles):
        bias_grad_ref[:, cut(tile)] += jnp.sum(sums[tile], axis=0, keepdims=True)
    step_w_grad_ref[...] += contract(
        projected_ref[:, :rank].astype(low_buf.dtype), low_buf[...], 0, 0
    )
    step_w = small_ref[pl.ds(plan["step"][0], rank), :]
    step_w = jnp.concatenate([step_w, jnp.zeros((lanes - rank, width), step_w.dtype)], axis=0)
    rank_buf[pl.ds(group * chunks, chunks)] += contract(low_buf[...], step_w, 1, 1).reshape(
        chunks, chunk, lanes
    )

    @pl.when(moment == moments - 1)
    def _():
        square_ref[...] = reduce.finish(None, None)[0]
        entry = lax.broadcasted_iota(jnp.int32, (size, lanes), 0)
        target = lax.broadcasted_iota(jnp.int32, (size, lanes), 1)
        places = [(target == entry + rank + number * size).astype(jnp.bfloat16) for number in range(2)]

        def lay(index, carry):
            for buffer, place in zip((write_buf, read_buf), places):
                summed = buffer[index][:, :chunk] + buffer[index][:, chunk:]
                rank_buf[index] += contract(summed.astype(jnp.bfloat16), place, 0, 0)
            return carry

        lax.fori_loop(0, rank_buf.shape[0], lay, 0, unroll=8)
        flat_ref[...] = rank_buf[...].reshape(flat_ref.shape).astype(flat_ref.dtype)
        reduce.settle()
        out_sum_ref[...] = parts[0][...]
        in_sum_ref[...] = parts[1][...]


def back_kernel(
    plan,
    lengths_ref,
    tokens_ref,
    low_ref,
    gain_ref,
    small_ref,
    flat_ref,
    branch_ref,
    signal_ref,
    slope_ref,
    signal_grad_ref,
    gate_grad_ref,
    flipped_ref,
    branch_w,
    gate_w,
    step_w_grad_ref,
    bias_grad_ref,
    decay_grad_ref,
    skip_grad_ref,
    small_grad_ref,
    in_grad_ref,
    gain_grad_ref,
    tokens_grad_ref,
    offset_buf,
    conv_buf,
    mixed_buf,
    total,
):
    rows = tokens_ref.shape[0]
    width = branch_ref.shape[1]
    tiles = width // lanes
    block = pl.program_id(0)

    @pl.when(block == 0)
    def _():
        fill_offsets(lengths_ref, offset_buf, rows)

    taps = small_rows(small_ref, *plan["taps"])
    count = taps.shape[0]
    small_grad_ref[:lanes, :] = contract(flat_ref[...], signal_ref[...], 0, 0)

    def place_rows(name, values):
        first, tall = plan[name]
        small_grad_ref[first : first + tall, :] = values

    place_rows("step", step_w_grad_ref[...])
    place_rows("decay", decay_grad_ref[...])
    place_rows("bias", bias_grad_ref[...])
    place_rows("skip", skip_grad_ref[...])
    conv_buf[pl.ds(0, rows), :] = signal_grad_ref[...] + jnp.dot(
        flat_ref[...], small_ref[:lanes, :], preferred_element_type=jnp.float32
    )
    conv_buf[pl.ds(rows, 8), :] = jnp.zeros((8, width), jnp.float32)

    def through_conv(index, at, carry):
        sums = []
        for tile in range(tiles):
            grad_conv = conv_buf[at, cut(tile)] * slope_ref[at, cut(tile)]
            conv_buf[at, cut(tile)] = grad_conv
            sums.append(carry[tile] + eight(grad_conv))
        return tuple(sums)

    zero_rows = jnp.zeros((8, lanes), jnp.float32)
    sums = row_loop(rows, 32, through_conv, (zero_rows,) * tiles)
    for tile in range(tiles):
        first = plan["shift"][0]
        small_grad_ref[first : first + 1, cut(tile)] = jnp.sum(sums[tile], axis=0, keepdims=True)

    def to_branch(index, at, carry):
        longer = pl.ds(pl.multiple_of(index * 32, 32), 40)
        offsets = offset_buf[longer, :]
        result = []
        for tile in range(tiles):
            here = slice(tile * lanes, (tile + 1) * lanes)
            grads = conv_buf[longer, cut(tile)]
            branch = branch_ref[at, cut(tile)]
            summed = taps[count - 1 : count, here] * grads[:32]
            sums = [None] * count
            sums[count - 1] = carry[tile][count - 1] + eight(branch * grads[:32])
            for tap in range(count - 1):
                lag = count - 1 - tap
                moved = pltpu.roll(jnp.where(offsets >= lag, grads, 0.0), 40 - lag, 0)[:32]
                summed = summed + taps[tap : tap + 1, here] * moved
                sums[tap] = carry[tile][tap] + eight(branch * moved)
            mixed_buf[at, cut(tile)] = summed.astype(mixed_buf.dtype)
            result.append(tuple(sums))
        return tuple(result)

    sums = row_loop(rows, 32, to_branch, ((zero_rows,) * count,) * tiles)
    for tile in range(tiles):
        for tap in range(count):
            first = plan["taps"][0] + tap
            small_grad_ref[first : first + 1, cut(tile)] = jnp.sum(sums[tile][tap], axis=0, keepdims=True)
    in_grad_ref[...] = jnp.dot(
        flipped_ref[...], mixed_buf[...], preferred_element_type=jnp.float32
    ).astype(in_grad_ref.dtype)
    piece = contract(mixed_buf[...], branch_w[...], 1, 1) + contract(gate_grad_ref[...], gate_w[...], 1, 1)

    @pl.when(block == 0)
    def _():
        total[...] = piece

    @pl.when(block > 0)
    def _():
        total[...] += piece

    @pl.when(block == pl.num_programs(0) - 1)
    def _():
        def finish(index, at, carry):
            residual = tokens_ref[at, :].astype(jnp.float32)
            scale = lax.rsqrt(jnp.mean(residual * residual, axis=1, keepdims=True) + epsilon)
            grad_normed = total[at, :]
            weighted = grad_normed * gain_ref[...]
            inner = jnp.mean(weighted * residual, axis=1, keepdims=True)
            grad_y = low_ref[at, :].astype(jnp.float32)
            result = grad_y + (scale * weighted - residual * (scale * scale * scale) * inner)
            tokens_grad_ref[at, :] = result.astype(tokens_grad_ref.dtype)
            return carry + eight(grad_normed * residual * scale)

        gains = row_loop(rows, 16, finish, jnp.zeros((8, total.shape[1]), jnp.float32))
        gain_grad_ref[...] = jnp.sum(gains, axis=0, keepdims=True)


def finish_kernel(plan, names, branch_ref, gate_ref, out_ref, small_ref, norm_ref, *outs):
    middle = branch_ref.shape[1]
    outs[0][:, :middle] = branch_ref[...]
    outs[0][:, middle:] = gate_ref[...]
    outs[1][...] = out_ref[...]
    for name, target in zip(names, outs[2 : 2 + len(names)]):
        first, count = plan[name]
        if len(target.shape) == 1:
            target[...] = small_ref[first, : target.shape[0]]
        else:
            target[...] = small_ref[first : first + count, :]
    for index in range(2):
        outs[2 + len(names) + index][0, 0] = jnp.sum(norm_ref[index])


def shape(dims, kind=jnp.float32):
    return jax.ShapeDtypeStruct(dims, kind)


def compute_call(
    kernel, name, blocks, in_specs, out_specs, out_shape, scratch, flops, operands, collective_id=None
):
    return pl.pallas_call(
        kernel,
        grid=blocks if isinstance(blocks, tuple) else (blocks,),
        in_specs=in_specs,
        out_specs=out_specs,
        out_shape=out_shape,
        scratch_shapes=scratch,
        compiler_params=pltpu.CompilerParams(
            dimension_semantics=("arbitrary",) * (len(blocks) if isinstance(blocks, tuple) else 1),
            vmem_limit_bytes=62 * 1024 * 1024,
            collective_id=collective_id,
            has_side_effects=collective_id is not None,
        ),
        cost_estimate=pl.CostEstimate(flops=flops, bytes_accessed=40 << 20, transcendentals=0),
        name=name,
    )(*operands)


class Place:
    def __init__(self, dims, swapped=False):
        depth, tall, wide = dims
        self.dims = dims
        self.core = lax.axis_index("wide")
        self.me = lax.axis_index("narrow")
        self.across = lax.rem(self.me, wide)
        self.up = lax.rem(lax.div(self.me, wide), tall)
        self.deep = lax.div(self.me, wide * tall)
        side = 1 - self.core if swapped else self.core
        turn = side if tall == wide else 0
        self.second = (1 + turn * (wide - 1), self.across + turn * (self.up - self.across), wide)
        self.third = (wide - turn * (wide - 1), self.up + turn * (self.across - self.up), tall)
        self.spans = (depth, wide, tall)
        self.other = {"wide": 1 - self.core}

    def at(self, d, e, f):
        depth, tall, wide = self.dims
        return (
            lax.rem(self.deep + d, depth) * (tall * wide)
            + lax.rem(self.second[1] + e, self.second[2]) * self.second[0]
            + lax.rem(self.third[1] + f, self.third[2]) * self.third[0]
        )

    def behind(self, d, e, f):
        return self.at(*((size - hop) % size for size, hop in zip(self.spans, (d, e, f))))

    def slot(self, d, e, f):
        return (d * self.spans[1] + e) * self.spans[2] + f

    def moves(self):
        return [
            (d, e, f)
            for d in range(self.spans[0])
            for e in range(self.spans[1])
            for f in range(self.spans[2])
        ]

    def greet(self):
        barrier = pltpu.get_barrier_semaphore()
        pl.semaphore_signal(barrier, inc=1, device_id=self.other, device_id_type=pl.DeviceIdType.MESH)
        peers = 1
        for axis, size in enumerate(self.spans):
            for hop in range(1, size):
                move = [0, 0, 0]
                move[axis] = hop
                pl.semaphore_signal(
                    barrier,
                    inc=1,
                    device_id={"narrow": self.at(*move)},
                    device_id_type=pl.DeviceIdType.MESH,
                )
                peers += 1
        pl.semaphore_wait(barrier, peers)


def half_of(width, core):
    return pl.ds(pl.multiple_of(core * (width // 2), lanes), width // 2)


def side_of(block, side):
    if len(block.shape) == 3:
        return block.at[side]
    return block.at[:, half_of(block.shape[1], side)]


def half_shape(array):
    return array.shape[2:] if len(array.shape) == 4 else (array.shape[1], array.shape[2] // 2)


def remote(source, target, send_sem, recv_sem, device):
    return pltpu.make_async_remote_copy(
        src_ref=source,
        dst_ref=target,
        send_sem=send_sem,
        recv_sem=recv_sem,
        device_id=device,
        device_id_type=pl.DeviceIdType.MESH,
    )


class Gather:
    def __init__(self, dims, own, whole, sems):
        self.dims, self.own, self.whole = dims, own, whole
        self.local_sem, self.send_sem, self.recv_sem, self.core_send, self.core_recv = sems

    @staticmethod
    def scratch(count, dims):
        number = dims[0] * dims[1] * dims[2]
        return [pltpu.SemaphoreType.DMA((count,))] + [pltpu.SemaphoreType.DMA((count, number))] * 4

    def onward(self, place, which, move):
        d, e, f = move
        number = place.behind(*move)
        target = side_of(self.whole[which].at[number], place.core)
        source = side_of(self.own[which], place.core) if move == (0, 0, 0) else target
        hops = []
        if f == 0:
            hops += [((0, 0, hop), (d, e, hop)) for hop in range(1, place.spans[2])]
        if f == 0 and e == 0:
            hops += [((0, hop, 0), (d, hop, 0)) for hop in range(1, place.spans[1])]
        if move == (0, 0, 0):
            hops += [((hop, 0, 0), (hop, 0, 0)) for hop in range(1, place.spans[0])]
        for step, landing in reversed(hops):
            index = place.slot(*landing)
            remote(
                source,
                target,
                self.send_sem.at[which, index],
                self.recv_sem.at[which, index],
                {"narrow": place.at(*step)},
            ).start()
        if move != (0, 0, 0):
            index = place.slot(*move)
            remote(
                source,
                target,
                self.core_send.at[which, index],
                self.core_recv.at[which, index],
                place.other,
            ).start()

    def local(self, place, which):
        return pltpu.make_async_copy(
            self.own[which], self.whole[which].at[place.at(0, 0, 0)], self.local_sem.at[which]
        )

    def start(self):
        place = Place(self.dims)
        place.greet()
        for which in range(len(self.own)):
            self.onward(place, which, (0, 0, 0))
        for which in range(len(self.own)):
            self.local(place, which).start()

    def leg(self, number):
        place = Place(self.dims)
        for which in range(len(self.own)):
            for move in place.moves():
                d, e, f = move
                if (number == 3) != (f > 0):
                    continue
                if number < 3 and (number == 2) != (e > 0):
                    continue
                if move == (0, 0, 0):
                    continue
                index = place.slot(*move)
                landed = side_of(self.whole[which].at[place.behind(*move)], place.core)
                remote(
                    landed,
                    landed,
                    self.send_sem.at[which, index],
                    self.recv_sem.at[which, index],
                    place.other,
                ).wait_recv()
                self.onward(place, which, move)

    def finish(self):
        place = Place(self.dims)
        mirror = Place(self.dims, swapped=True)
        for which in range(len(self.own)):
            for move in place.moves():
                if move == (0, 0, 0):
                    continue
                index = place.slot(*move)
                landed = side_of(self.whole[which].at[mirror.behind(*move)], 1 - place.core)
                handed = remote(
                    landed,
                    landed,
                    self.core_send.at[which, index],
                    self.core_recv.at[which, index],
                    place.other,
                )
                handed.wait_recv()
                handed.wait_send()
                remote(
                    landed,
                    landed,
                    self.send_sem.at[which, index],
                    self.recv_sem.at[which, index],
                    place.other,
                ).wait_send()
            self.local(place, which).wait()


class Reduce:
    def __init__(self, dims, grads, held, sems, results, targets):
        self.dims, self.grads = dims, grads
        count = len(grads)
        self.mine, self.swapped, self.third, self.second, self.first = (
            held[index * count : (index + 1) * count] for index in range(5)
        )
        (
            self.local_sem,
            self.core_send,
            self.core_recv,
            self.leg_send,
            self.leg_recv,
            self.last_send,
            self.last_recv,
        ) = sems
        self.results, self.targets = results, targets

    @staticmethod
    def rooms(dims, grads):
        depth, tall, wide = dims
        number = depth * tall * wide
        places = (number, number, depth * wide * (tall - 1), depth * (wide - 1), depth - 1)
        return [
            pltpu.VMEM((room,) + tuple(half_shape(grad)), grad.dtype) for room in places for grad in grads
        ]

    @staticmethod
    def sems(dims, count):
        number = dims[0] * dims[1] * dims[2]
        return [pltpu.SemaphoreType.DMA((count, number))] * 5 + [pltpu.SemaphoreType.DMA((count,))] * 2

    def order(self, place):
        return sorted(place.moves(), key=lambda item: (item[2] == 0, item[1] == 0, item[0] == 0))

    def share(self, which, side):
        result, first = self.targets[which]
        if len(self.grads[which].shape) == 4:
            return self.results[result].at[side]
        width = self.grads[which].shape[2]
        columns = pl.ds(pl.multiple_of(first + side * (width // 2), lanes), width // 2)
        return self.results[result].at[:, columns]

    def load(self, place, which, move):
        return pltpu.make_async_copy(
            side_of(self.grads[which].at[place.at(*move)], place.core),
            self.mine[which].at[place.slot(*move)],
            self.local_sem.at[which, place.slot(*move)],
        )

    def swap(self, place, which, move, mirror):
        index = place.slot(*move)
        return remote(
            side_of(self.grads[which].at[mirror.at(*move)], 1 - place.core),
            self.swapped[which].at[index],
            self.core_send.at[which, index],
            self.core_recv.at[which, index],
            place.other,
        )

    def start(self):
        place, mirror = Place(self.dims), Place(self.dims, swapped=True)
        place.greet()
        for move in self.order(place):
            for which in range(len(self.grads)):
                self.swap(place, which, move, mirror).start()
                self.load(place, which, move).start()

    def landing(self, place, which, move):
        d, e, f = move
        if f > 0:
            return self.third[which].at[(d * place.spans[1] + e) * (place.spans[2] - 1) + f - 1], (0, 0, f)
        if e > 0:
            return self.second[which].at[d * (place.spans[1] - 1) + e - 1], (0, e, 0)
        return self.first[which].at[d - 1], (d, 0, 0)

    def hop(self, place, which, move):
        landing, step = self.landing(place, which, move)
        index = place.slot(*move)
        return remote(
            self.mine[which].at[index],
            landing,
            self.leg_send.at[which, index],
            self.leg_recv.at[which, index],
            {"narrow": place.at(*step)},
        )

    def collect(self, place, which, move):
        d, e, f = move
        index = place.slot(*move)
        self.load(place, which, move).wait()
        handed = self.swapped[which].at[index]
        remote(
            handed, handed, self.core_send.at[which, index], self.core_recv.at[which, index], place.other
        ).wait_recv()
        parts = [handed]
        coming = []
        if f == 0:
            coming += [(d, e, hop) for hop in range(1, place.spans[2])]
        if f == 0 and e == 0:
            coming += [(d, hop, 0) for hop in range(1, place.spans[1])]
        if move == (0, 0, 0):
            coming += [(hop, 0, 0) for hop in range(1, place.spans[0])]
        for source in coming:
            self.hop(place, which, source).wait_recv()
            parts.append(self.landing(place, which, source)[0])
        return parts

    def added(self, place, which, move, parts, store, carry):
        block = self.mine[which].at[place.slot(*move)]
        rows = block.shape[0]
        group = min(rows, 16)

        def some(index, carry):
            at_rows = pl.ds(pl.multiple_of(index * group, group), group)
            total = block[at_rows, :].astype(jnp.float32)
            for part in parts:
                total = total + part[at_rows, :].astype(jnp.float32)
            return store(block, at_rows, total, carry)

        return lax.fori_loop(0, rows // group, some, carry)

    def leg(self, number):
        place = Place(self.dims)

        def keep(block, at_rows, total, carry):
            block[at_rows, :] = total.astype(block.dtype)
            return carry

        for move in self.order(place)[:-1]:
            d, e, f = move
            if number != (1 if f > 0 else 2 if e > 0 else 3):
                continue
            for which in range(len(self.grads)):
                parts = self.collect(place, which, move)
                self.added(place, which, move, parts, keep, 0)
                self.hop(place, which, move).start()

    def finish(self, plain_at, plain_ref):
        place, mirror = Place(self.dims), Place(self.dims, swapped=True)
        squares = (jnp.zeros((8, lanes), jnp.float32),) * 2
        for which in range(len(self.grads)):
            parts = self.collect(place, which, (0, 0, 0))
            result = self.share(which, place.core)

            def store(block, at_rows, total, carry, which=which, result=result):
                result[at_rows, :] = total
                kept, plain = carry
                squared = total * total
                if which == plain_at:
                    marked = squared * plain_ref[place.core, at_rows, :]
                    plain = plain + folded_squares(marked)
                    squared = squared - marked
                return (kept + folded_squares(squared), plain)

            squares = self.added(place, which, (0, 0, 0), parts, store, squares)
            remote(result, result, self.last_send.at[which], self.last_recv.at[which], place.other).start()
        return squares

    def settle(self):
        place, mirror = Place(self.dims), Place(self.dims, swapped=True)
        for which in range(len(self.grads)):
            result = self.share(which, 1 - place.core)
            last = remote(result, result, self.last_send.at[which], self.last_recv.at[which], place.other)
            last.wait_recv()
            last.wait_send()
            for move in place.moves():
                self.swap(place, which, move, mirror).wait_send()
                if move != (0, 0, 0):
                    self.hop(place, which, move).wait_send()


def folded_squares(values):
    total = None
    if values.shape[1] < lanes:
        first = lax.broadcasted_iota(jnp.int32, (values.shape[0], lanes), 1) == 0
        values = jnp.where(first, jnp.sum(values, axis=1, keepdims=True), 0.0)
    for row in range(0, values.shape[0], 8):
        for column in range(0, values.shape[1], lanes):
            piece = values[row : row + 8, column : column + lanes]
            total = piece if total is None else total + piece
    return total


def gather_kernel(dims, plan, names, *refs):
    smalls, bigs = refs[: len(names)], refs[len(names) : len(names) + 1]
    refs = refs[len(names) + 1 :]
    whole, own, pack_buf, sems = refs[:2], refs[2:4], refs[4], refs[5:]
    pack_buf[...] = jnp.zeros_like(pack_buf)
    for name, ref in zip(names, smalls):
        first, tall = plan[name]
        pack_buf[first : first + tall, : ref.shape[1]] = ref[...]
    tall = pack_buf.shape[0] // 2
    for side in range(2):
        own[0][side] = pack_buf[side * tall : (side + 1) * tall, :].astype(own[0].dtype)
    own[1][...] = bigs[0][...].astype(own[1].dtype)
    gather = Gather(dims, own, whole, sems)
    gather.start()
    for number in (1, 2, 3):
        gather.leg(number)
    gather.finish()


def gather_weights(dims, plan, smalls, big):
    number = dims[0] * dims[1] * dims[2]
    names = list(smalls)
    width = smalls["select"].shape[1]
    owned = [shape((2, plan["rows"] // 2, width), jnp.bfloat16), shape(big.shape, jnp.bfloat16)]
    inside = pl.BlockSpec(memory_space=pltpu.VMEM)
    return pl.pallas_call(
        functools.partial(gather_kernel, dims, plan, names),
        in_specs=[inside] * (len(names) + 1),
        out_specs=[pl.BlockSpec(memory_space=pl.ANY)] * 2,
        out_shape=[shape((number,) + kind.shape, kind.dtype) for kind in owned],
        scratch_shapes=[pltpu.VMEM(kind.shape, kind.dtype) for kind in owned]
        + [pltpu.VMEM((plan["rows"], width), jnp.float32)]
        + Gather.scratch(2, dims),
        compiler_params=pltpu.CompilerParams(
            collective_id=0, has_side_effects=True, vmem_limit_bytes=60 * 1024 * 1024
        ),
        name="gather_weights",
    )(*smalls.values(), big)


def reduce_kernel(dims, count, results, targets, plain_at, *refs):
    grads, plain_ref, earlier_ref = refs[:count], refs[count], refs[count + 1]
    refs = refs[count + 2 :]
    sums, norms = refs[:results], refs[results]
    refs = refs[results + 1 :]
    held, buffers = refs[: 5 * count], refs[5 * count : 5 * count + 4]
    refs = refs[5 * count + 4 :]
    sems, (norm_send, norm_recv) = refs[:7], refs[7:]
    reduce = Reduce(dims, grads, held, sems, sums, targets)
    reduce.start()
    for number in (1, 2, 3):
        reduce.leg(number)
    kept, plain = reduce.finish(plain_at, plain_ref)
    running = jnp.stack([kept + earlier_ref[...], plain])

    place = Place(dims)
    depth, tall, wide = dims
    plane = tall * wide
    me = place.me
    stages = (
        (buffers[0], 2, place.core, lambda spot: {"wide": spot}),
        (buffers[1], depth, place.deep, lambda spot: {"narrow": spot * plane + lax.rem(me, plane)}),
        (buffers[2], wide, place.across, lambda spot: {"narrow": me - place.across + spot}),
        (buffers[3], tall, place.up, lambda spot: {"narrow": me + (spot - place.up) * wide}),
    )
    pending = []
    first = 0
    for buffer, size, mine_at, device in stages:
        buffer[mine_at] = running
        for hop in range(1, size):
            copy = remote(
                buffer.at[mine_at],
                buffer.at[mine_at],
                norm_send.at[first + hop - 1],
                norm_recv.at[first + hop - 1],
                device(lax.rem(mine_at + hop, size)),
            )
            copy.start()
            pending.append(copy)
        for hop in range(1, size):
            came = lax.rem(mine_at + size - hop, size)
            remote(
                buffer.at[came],
                buffer.at[came],
                norm_send.at[first + hop - 1],
                norm_recv.at[first + hop - 1],
                device(came),
            ).wait_recv()
        first += size - 1
        running = buffer[0]
        for spot in range(1, size):
            running = running + buffer[spot]
    norms[...] = running
    reduce.settle()
    for copy in pending:
        copy.wait_send()


def sum_shapes(grads, targets):
    sums = []
    for index in range(1 + max(target[0] for target in targets)):
        members = [grad for grad, target in zip(grads, targets) if target[0] == index]
        if len(members[0].shape) == 4:
            sums.append(shape(members[0].shape[1:]))
        else:
            sums.append(shape((members[0].shape[1], sum(grad.shape[2] for grad in members))))
    return sums


def reduce_grads(dims, grads, targets, plain_mask, plain_at, earlier):
    depth, tall, wide = dims
    count = len(grads)
    anywhere = pl.BlockSpec(memory_space=pl.ANY)
    inside = pl.BlockSpec(memory_space=pltpu.VMEM)
    sums = sum_shapes(grads, targets)
    result = pl.pallas_call(
        functools.partial(reduce_kernel, dims, count, len(sums), targets, plain_at),
        in_specs=[anywhere] * count + [inside] * 2,
        out_specs=[inside] * (len(sums) + 1),
        out_shape=sums + [shape((2, 8, lanes))],
        scratch_shapes=Reduce.rooms(dims, grads)
        + [pltpu.VMEM((size, 2, 8, lanes), jnp.float32) for size in (2, depth, wide, tall)]
        + Reduce.sems(dims, count)
        + [pltpu.SemaphoreType.DMA((depth + tall + wide,))] * 2,
        compiler_params=pltpu.CompilerParams(
            collective_id=1, has_side_effects=True, vmem_limit_bytes=56 * 1024 * 1024
        ),
        name="reduce_grads",
    )(*grads, plain_mask, earlier)
    return result[: len(sums)], result[len(sums)]


def grid_of(mesh):
    number = mesh.shape["narrow"]
    places = [getattr(device, "coords", None) for device in mesh.devices[0]]
    if all(place is not None for place in places):
        sizes = [len({place[axis] for place in places}) for axis in (2, 1, 0)]
        if sizes[0] * sizes[1] * sizes[2] == number:
            return tuple(sizes)
    side = round((number / 2) ** (1 / 3))
    return (2 * side, side, side) if 2 * side**3 == number else (number, 1, 1)


def plan_of(select_rows, state_size, tap_count, step_rows):
    plan, first = {}, 0
    for name, tall in (
        ("select", select_rows),
        ("decay", state_size),
        ("taps", tap_count),
        ("shift", 1),
        ("bias", 1),
        ("skip", 1),
        ("gain", 1),
    ):
        plan[name] = (first, tall)
        first += tall
    plan["step"] = (lanes, step_rows)
    plan["rows"] = -(-(lanes + step_rows) // 32) * 32
    return plan


def per_device(
    dims,
    tokens,
    cotangent,
    loss_mask,
    seq_lengths,
    norm_gain,
    in_proj,
    conv_weight,
    conv_bias,
    select_proj,
    step_proj,
    step_bias,
    decay_log,
    skip_scale,
    out_proj,
):
    half = jnp.bfloat16
    piece = skip_scale.shape[0]
    gain_piece = norm_gain.shape[0]
    rank, size = step_proj.shape[0], decay_log.shape[0]
    plan = plan_of(select_proj.shape[0], size, conv_weight.shape[0], rank)
    small_blocks, in_blocks = gather_weights(
        dims,
        plan,
        {
            "select": select_proj,
            "decay": decay_log,
            "taps": conv_weight,
            "shift": conv_bias[None],
            "bias": step_bias[None],
            "skip": skip_scale[None],
            "gain": norm_gain[None],
            "step": step_proj,
        },
        in_proj,
    )
    in_whole = in_blocks.reshape(-1, in_blocks.shape[2])
    small_blocks = small_blocks.reshape(-1, plan["rows"], piece)
    small = jnp.swapaxes(small_blocks, 0, 1).reshape(plan["rows"], -1)
    gain_value = small_blocks[:, plan["gain"][0], :gain_piece].reshape(1, -1).astype(jnp.float32)

    rows, model = tokens.shape
    inner = small.shape[1]
    width = 4 * lanes
    blocks = inner // width
    chunks = rows // chunk
    mask_row = loss_mask[None]

    whole = pl.BlockSpec(memory_space=pltpu.VMEM)
    tall = pl.BlockSpec((rows, width), lambda b: (0, b))
    deep = pl.BlockSpec((chunks, chunk, width), lambda b: (0, 0, b))
    lead = pl.BlockSpec((rows, size, width), lambda b: (0, 0, b))
    first_w = pl.BlockSpec((model, width), lambda b: (0, b))
    second_w = pl.BlockSpec((model, width), lambda b: (0, b + blocks))
    out_w = pl.BlockSpec((width, model), lambda b: (b, 0))

    def thin(height):
        return pl.BlockSpec((height, width), lambda b: (0, b))

    def fixed(*dims_of):
        return pl.BlockSpec(dims_of, lambda b: (0,) * len(dims_of))

    scalars = pl.BlockSpec(memory_space=pltpu.SMEM)
    offset_buf = pltpu.VMEM((rows + 8, lanes), jnp.int32)
    packed = thin(plan["rows"])

    pair = (chunks, 2 * chunk, lanes)
    (
        branch,
        gate_pre,
        signal,
        slope,
        projected,
        flipped,
        grad_low,
        write_pair,
        read_pair,
    ) = compute_call(
        functools.partial(front_kernel, plan),
        "front",
        blocks,
        [scalars, whole, whole, whole, whole, packed, first_w, second_w],
        [tall, tall, tall, tall, fixed(rows, lanes), fixed(model, rows), fixed(rows, model)]
        + [fixed(*pair)] * 2,
        [
            shape((rows, inner)),
            shape((rows, inner)),
            shape((rows, inner), half),
            shape((rows, inner)),
            shape((rows, lanes)),
            shape((model, rows), half),
            shape((rows, model), half),
        ]
        + [shape(pair, half)] * 2,
        [pltpu.VMEM((rows, model), half), offset_buf],
        4 * rows * model * inner,
        (seq_lengths, tokens, cotangent, mask_row, gain_value, small, in_whole, in_whole),
    )
    groups = 4
    part, pieces = rows // groups, chunks // groups
    row_block = pltpu.VMEM((pieces, chunk, width), jnp.float32)
    spare_block = pltpu.VMEM((pieces + 1, chunk, width), jnp.float32)
    spread_block = pltpu.VMEM((chunk * size, lanes), jnp.float32)
    fold_block = pltpu.VMEM((width // lanes, chunk * chunk, lanes), jnp.float32)
    number = small_blocks.shape[0]
    anywhere = pl.BlockSpec(memory_space=pl.ANY)

    def by_group(order, *dims_of):
        middle = (0,) * (len(dims_of) - 2)
        return pl.BlockSpec(dims_of, lambda b, g: (order(g),) + middle + (b,))

    def by_token(order, *dims_of):
        return pl.BlockSpec(dims_of, lambda b, g: (order(g),) + (0,) * (len(dims_of) - 1))

    def by_channel(height):
        return pl.BlockSpec((height, width), lambda b, g: (0, b))

    def onward(g):
        return g

    def backward(g):
        return groups - 1 - g

    states, step, core, begins, out_blocks = compute_call(
        functools.partial(forward_kernel, plan, dims),
        "forward",
        (blocks, groups),
        [
            scalars,
            by_token(onward, part, lanes),
            by_channel(plan["rows"]),
            by_group(onward, part, width),
            by_token(onward, pieces, 2 * chunk, lanes),
            by_token(onward, pieces, 2 * chunk, lanes),
            whole,
        ],
        [
            by_group(onward, part, size, width),
            by_group(onward, pieces, chunk, width),
            by_group(onward, pieces, chunk, width),
            by_group(onward, 1, size, width),
            anywhere,
        ],
        [
            shape((rows, size, inner)),
            shape((chunks, chunk, inner)),
            shape((chunks, chunk, inner)),
            shape((groups, size, inner)),
            shape((number,) + out_proj.shape, half),
        ],
        [
            offset_buf,
            pltpu.VMEM((part, width), jnp.float32),
            row_block,
            row_block,
            spread_block,
            spread_block,
            spread_block,
            spread_block,
            fold_block,
            fold_block,
            pltpu.VMEM((size, width), jnp.float32),
            pltpu.VMEM(out_proj.shape, half),
        ]
        + Gather.scratch(1, dims),
        15 * rows * inner * size,
        (seq_lengths, projected, small, signal, write_pair, read_pair, out_proj),
        collective_id=2,
    )
    core_grad, gate_grad, grad_skip, grad_outw, grad_in_gate, output = compute_call(
        functools.partial(middle_kernel, plan),
        "middle",
        blocks,
        [deep, packed, tall, tall, whole, out_w, whole, whole],
        [deep, tall, thin(1), out_w, first_w, fixed(rows, model)],
        [
            shape((chunks, chunk, inner)),
            shape((rows, inner), half),
            shape((1, inner)),
            shape((inner, model), half),
            shape((model, inner), half),
            shape((rows, model), half),
        ],
        [
            pltpu.VMEM((rows, width), jnp.float32),
            pltpu.VMEM((rows, width), half),
            pltpu.VMEM((rows, model), jnp.float32),
        ],
        8 * rows * model * inner,
        (core, small, signal, gate_pre, grad_low, out_blocks.reshape(inner, model), flipped, tokens),
    )
    split = in_blocks.shape[:2] + (inner,)
    early_grads = [grad_outw.reshape(out_blocks.shape), grad_in_gate.reshape(split)]
    early_sums = sum_shapes(early_grads, [(0, 0), (1, 0)])
    (
        signal_grad,
        grad_stepw,
        grad_bias,
        grad_decaylog,
        flat,
        out_sum,
        in_gate_sum,
        early_squares,
    ) = compute_call(
        functools.partial(backward_kernel, plan, dims),
        "backward",
        (blocks, groups),
        [
            scalars,
            by_token(backward, part, lanes),
            by_channel(plan["rows"]),
            by_group(backward, part, width),
            by_token(backward, pieces, 2 * chunk, lanes),
            by_token(backward, pieces, 2 * chunk, lanes),
            by_group(backward, pieces, chunk, width),
            by_group(backward, pieces, chunk, width),
            by_group(backward, part, size, width),
            by_group(backward, 1, size, width),
            anywhere,
            anywhere,
        ],
        [
            by_group(backward, part, width),
            by_channel(rank),
            by_channel(1),
            by_channel(size),
            whole,
        ]
        + [whole] * 3,
        [
            shape((rows, inner)),
            shape((rank, inner)),
            shape((1, inner)),
            shape((size, inner)),
            shape((rows, lanes), half),
            *early_sums,
            shape((8, lanes)),
        ],
        [
            offset_buf,
            row_block,
            row_block,
            pltpu.VMEM((pieces + 1, 2 * chunk, width), jnp.float32),
            pltpu.VMEM((pieces, 2 * chunk, width), jnp.float32),
            spread_block,
            spread_block,
            spread_block,
            spread_block,
            pltpu.VMEM((chunk * size, width), jnp.float32),
            pltpu.VMEM((chunk * size, width), jnp.float32),
            fold_block,
            fold_block,
            fold_block,
            fold_block,
            spare_block,
            spare_block,
            pltpu.VMEM((part, width), half),
            pltpu.VMEM((size, width), jnp.float32),
            pltpu.VMEM((chunks, chunk, lanes), jnp.float32),
            pltpu.VMEM((chunks, size, 2 * chunk), jnp.float32),
            pltpu.VMEM((chunks, size, 2 * chunk), jnp.float32),
        ]
        + [pltpu.VMEM(early.shape, early.dtype) for early in early_sums]
        + Reduce.rooms(dims, early_grads)
        + Reduce.sems(dims, 2),
        40 * rows * inner * size,
        (
            seq_lengths,
            projected,
            small,
            signal,
            write_pair,
            read_pair,
            step,
            core_grad,
            states,
            begins,
            *early_grads,
        ),
        collective_id=3,
    )

    small_grad, grad_in_branch, grad_gain, grad_tokens = compute_call(
        functools.partial(back_kernel, plan),
        "back",
        blocks,
        [scalars, whole, whole, whole, packed, whole, tall, tall, tall, tall, tall, whole, first_w, second_w]
        + [thin(rank), thin(1), thin(size), thin(1)],
        [packed, first_w, fixed(1, model), fixed(rows, model)],
        [
            shape((plan["rows"], inner)),
            shape((model, inner), half),
            shape((1, model)),
            shape((rows, model), half),
        ],
        [
            offset_buf,
            pltpu.VMEM((rows + 8, width), jnp.float32),
            pltpu.VMEM((rows, width), half),
            pltpu.VMEM((rows, model), jnp.float32),
        ],
        8 * rows * model * inner,
        (
            seq_lengths,
            tokens,
            grad_low,
            gain_value,
            small,
            flat,
            branch,
            signal,
            slope,
            signal_grad,
            gate_grad,
            flipped,
            in_whole,
            in_whole,
            grad_stepw,
            grad_bias,
            grad_decaylog,
            grad_skip,
        ),
    )

    gain_rows = jnp.pad(grad_gain.reshape(number, 1, gain_piece), ((0, 0), (0, 0), (0, piece - gain_piece)))
    place = plan["gain"][0]
    small_grad = jnp.swapaxes(small_grad.reshape(plan["rows"], number, piece), 0, 1) + jnp.pad(
        gain_rows, ((0, 0), (place, plan["rows"] - place - 1), (0, 0))
    )
    plain_rows = np.zeros((plan["rows"], piece), np.float32)
    for name in ("bias", "decay", "skip"):
        first, count = plan[name]
        plain_rows[first : first + count] = 1.0
    halves = (2, plan["rows"] // 2, piece)
    (in_branch_sum, small_sum), norms = reduce_grads(
        dims,
        [grad_in_branch.reshape(split), small_grad.reshape((number,) + halves)],
        [(0, 0), (1, 0)],
        jnp.asarray(plain_rows.reshape(halves)),
        1,
        early_squares,
    )
    names = ("gain", "taps", "shift", "select", "step", "bias", "decay", "skip")
    own = (norm_gain, conv_weight, conv_bias, select_proj, step_proj, step_bias, decay_log, skip_scale)
    in_grad, out_grad, gain_grad, *small_grads, decay_sq, plain_sq = pl.pallas_call(
        functools.partial(finish_kernel, plan, names),
        in_specs=[whole] * 5,
        out_specs=[whole] * (2 + len(names)) + [scalars] * 2,
        out_shape=[shape(in_proj.shape), shape(out_proj.shape)]
        + [shape(array.shape) for array in own]
        + [shape((1, 1))] * 2,
        name="finish",
    )(in_branch_sum, in_gate_sum, out_sum, small_sum.reshape(plan["rows"], piece), norms)
    return (
        output,
        grad_tokens,
        gain_grad,
        in_grad,
        *small_grads,
        out_grad,
        decay_sq[0, 0],
        plain_sq[0, 0],
    )


def solution(mesh):
    placed = (
        P(("wide", "narrow"), None),
        P(("wide", "narrow"), None),
        P(("wide", "narrow")),
        P(("wide", "narrow"), None),
        P("narrow"),
        P("narrow", None),
        P(None, "narrow"),
        P("narrow"),
        P(None, "narrow"),
        P(None, "narrow"),
        P("narrow"),
        P(None, "narrow"),
        P("narrow"),
        P("narrow", None),
    )
    return jax.shard_map(
        functools.partial(per_device, grid_of(mesh)),
        mesh=mesh,
        in_specs=placed,
        out_specs=(
            P(("wide", "narrow"), None),
            P(("wide", "narrow"), None),
            P("narrow"),
            P("narrow", None),
            P(None, "narrow"),
            P("narrow"),
            P(None, "narrow"),
            P(None, "narrow"),
            P("narrow"),
            P(None, "narrow"),
            P("narrow"),
            P("narrow", None),
            P(),
            P(),
        ),
        check_vma=False,
    )
```

```python
import functools
import math

import jax
import jax.numpy as jnp
import numpy as np
from jax import lax
from jax.experimental import pallas as pl
from jax.experimental.pallas import tpu as pltpu
from jax.sharding import PartitionSpec as P

epsilon = 1e-05
chunk = 8
lanes = 128
log2e = math.log2(math.e)
ln2 = math.log(2.0)
far = 1e30


def contract(left, right, left_dim, right_dim):
    return lax.dot_general(
        left, right, (((left_dim,), (right_dim,)), ((), ())), preferred_element_type=jnp.float32
    )


def row_loop(rows, group, body, initial):
    def some(index, carry):
        return body(index, pl.ds(pl.multiple_of(index * group, group), group), carry)

    return lax.fori_loop(0, rows // group, some, initial)


def cut(tile):
    return pl.ds(tile * lanes, lanes)


def sigmoid(values):
    return 0.5 * jnp.tanh(0.5 * values) + 0.5


def softplus(values):
    small = jnp.exp(-jnp.abs(values))
    series = small * (1.0 - small * (0.5 - small * (1.0 / 3.0 - 0.25 * small)))
    return jnp.maximum(values, 0.0) + jnp.where(small < 0.03, series, jnp.log(1.0 + small))


def slope_of(step):
    series = step * (1.0 - step * (0.5 - step * (1.0 / 6.0 - step * (1.0 / 24.0))))
    return jnp.where(step < 0.03, series, 1.0 - jnp.exp(-step))


def fill_offsets(lengths_ref, offset_buf, rows):
    place = lax.broadcasted_iota(jnp.int32, offset_buf.shape, 0)
    start = jnp.zeros(offset_buf.shape, jnp.int32)
    ahead = jnp.int32(0)
    for index in range(lengths_ref.shape[1] - 1):
        ahead = ahead + lengths_ref[0, index]
        start = jnp.where(place >= ahead, ahead, start)
    offset_buf[...] = jnp.where(place < rows, place - start, 0)


def small_rows(small_ref, first, count):
    base = first // 16 * 16
    tall = -(-(first + count - base) // 16) * 16
    return small_ref[base : base + tall, :].astype(jnp.float32)[first - base : first - base + count]


def eight(values):
    total = values[:8]
    for row in range(8, values.shape[0], 8):
        total = total + values[row : row + 8]
    return total


def conv_rows(index, at, group, tile, branch_ref, offset_buf, taps, shift):
    count = taps.shape[0]
    here = slice(tile * lanes, (tile + 1) * lanes)
    current = branch_ref[at, cut(tile)]
    before = branch_ref[pl.ds(pl.multiple_of(jnp.maximum(index * group - 8, 0), 8), 8), cut(tile)]
    both = jnp.concatenate([before, current], axis=0)
    offsets = offset_buf[at, :]
    summed = shift[:, here] + taps[count - 1 : count, here] * current
    for tap in range(count - 1):
        lag = count - 1 - tap
        read = jnp.where(offsets >= lag, pltpu.roll(both, lag, 0)[8:], 0.0)
        summed = summed + taps[tap : tap + 1, here] * read
    return summed


def rows_of(blocks):
    return as_matrix(blocks[...][None])


def as_matrix(blocks):
    columns = blocks.shape[3]
    if blocks.shape[2] % 16:
        return blocks.astype(jnp.float32).reshape(-1, columns).astype(blocks.dtype)
    return blocks.reshape(-1, columns)


def front_kernel(
    plan,
    dims,
    names,
    lengths_ref,
    tokens_ref,
    cotangent_ref,
    mask_ref,
    *refs,
):
    smalls, in_ref, refs = refs[: len(names)], refs[len(names)], refs[len(names) + 1 :]
    branch_ref, gate_ref, signal_ref, slope_ref, projected_ref, flipped_ref, low_ref = refs[:7]
    write_pair, read_pair, small_out, gain_ref, whole_ref = refs[7:12]
    normed_buf, offset_buf, pack_buf, own_small, own_in, land_small, land_in, store_sem = refs[12:20]
    rows = tokens_ref.shape[0]
    width = branch_ref.shape[1]
    block = pl.program_id(0)
    last = whole_ref.shape[0]
    gather = Gather(
        dims,
        [own_small] + [own_in.at[index] for index in range(last)],
        [land_small] + [land_in.at[index] for index in range(last)],
        refs[20:],
    )

    def stored(index):
        return pltpu.make_async_copy(land_in.at[index], whole_ref.at[index], store_sem.at[index])

    @pl.when(block == 0)
    def _():
        pack_buf[...] = jnp.zeros_like(pack_buf)
        for name, ref in zip(names, smalls):
            first, tall = plan[name]
            pack_buf[first : first + tall, : ref.shape[1]] = ref[...]
        tall = pack_buf.shape[0] // 2
        for side in range(2):
            own_small[side] = pack_buf[side * tall : (side + 1) * tall, :].astype(own_small.dtype)
            for index in range(last):
                first = (side * last + index) * width
                own_in[index, side] = in_ref[:, first : first + width].astype(own_in.dtype)
        Place(dims).greet()
        for index in range(last + 1):
            gather.start(index)
        fill_offsets(lengths_ref, offset_buf, rows)
        down = lax.broadcasted_iota(jnp.int32, (rows, rows), 0)
        along = lax.broadcasted_iota(jnp.int32, (rows, rows), 1)
        diagonal = jnp.where(down == along, mask_ref[...].astype(jnp.float32), 0.0).astype(low_ref.dtype)
        low_ref[...] = jnp.dot(
            diagonal, cotangent_ref[...], preferred_element_type=jnp.float32
        ).astype(low_ref.dtype)
        projected_ref[...] = jnp.zeros_like(projected_ref)
        for which, number in ((0, 1), (1, 1), (0, 2), (1, 2), (2, 1), (0, 3)):
            gather.leg(which, number)
        gather.arrive(0)
        share = land_small.shape[4]
        gains = gain_ref.shape[1] // (land_small.shape[0] * land_small.shape[1])
        gain_row = plan["gain"][0]
        for z in range(land_small.shape[0]):
            for plane in range(land_small.shape[1]):
                owner = z * land_small.shape[1] + plane
                for side in range(2):
                    small_out[side * tall : (side + 1) * tall, owner * share : (owner + 1) * share] = land_small[
                        z, plane, side
                    ]
                side, row = gain_row // tall, gain_row % tall
                base = row // 16 * 16
                some = land_small[z, plane, side, base : base + 16, :].astype(jnp.float32)
                gain_ref[:, owner * gains : (owner + 1) * gains] = some[row - base : row - base + 1, :gains]

        def norm(index, at, carry):
            residual = tokens_ref[at, :].astype(jnp.float32)
            scale = lax.rsqrt(jnp.mean(residual * residual, axis=1, keepdims=True) + epsilon)
            normed_buf[at, :] = (residual * scale * gain_ref[...]).astype(normed_buf.dtype)
            return carry

        row_loop(rows, 16, norm, 0)
        flipped_ref[...] = normed_buf[...].T
        for which, number in ((3, 1), (2, 2), (1, 3)):
            gather.leg(which, number)

    for moment, legs in ((1, ((4, 1), (3, 2), (2, 3))), (2, ((4, 2), (3, 3))), (3, ((4, 3),))):

        @pl.when(block == moment)
        def _(legs=legs):
            for which, number in legs:
                gather.leg(which, number)

    for index in range(last):

        @pl.when(block == index)
        def _(index=index):
            gather.arrive(index + 1)
            stored(index).start()

    branch_w = as_matrix(land_in[block, :, :, 0])
    branch_ref[...] = jnp.dot(normed_buf[...], branch_w, preferred_element_type=jnp.float32)
    gate_w = as_matrix(land_in[block, :, :, 1])
    gate_ref[...] = jnp.dot(normed_buf[...], gate_w, preferred_element_type=jnp.float32)
    small_ref = small_out.at[:, pl.ds(pl.multiple_of(block * width, width), width)]
    taps = small_rows(small_ref, *plan["taps"])
    shift = small_rows(small_ref, *plan["shift"])

    def some(index, at, carry):
        for tile in range(width // lanes):
            summed = conv_rows(index, at, 32, tile, branch_ref, offset_buf, taps, shift)
            sigma = sigmoid(summed)
            active = summed * sigma
            signal_ref[at, cut(tile)] = active.astype(signal_ref.dtype)
            slope_ref[at, cut(tile)] = sigma + active * (1.0 - sigma)
        return carry

    row_loop(rows, 32, some, 0)
    projected_ref[...] += contract(signal_ref[...], small_ref[:lanes, :], 1, 1)

    @pl.when(block == pl.num_programs(0) - 1)
    def _():
        high, low = high_low(projected_ref[...])
        own = own_tokens(rows)
        rank = plan["step"][1]
        size = plan["decay"][1]
        entry = lax.broadcasted_iota(jnp.int32, (lanes, lanes), 0)
        lane = lax.rem(lax.broadcasted_iota(jnp.int32, (lanes, lanes), 1), size)
        for first, pair in ((rank, write_pair), (rank + size, read_pair)):
            spread = (entry == lane + first).astype(jnp.bfloat16)
            parts = [
                (jnp.dot(part.astype(jnp.bfloat16), spread, preferred_element_type=jnp.float32) * own).reshape(
                    rows // chunk, chunk, lanes
                )
                for part in (high, low)
            ]
            pair[...] = jnp.concatenate(parts, axis=1).astype(pair.dtype)
        for index in range(last + 1):
            gather.drain(index)
        for index in range(last):
            stored(index).wait()


def high_low(values):
    high = values.astype(jnp.bfloat16).astype(jnp.float32)
    return high, values - high


def own_tokens(rows):
    token = lax.rem(lax.broadcasted_iota(jnp.int32, (rows, lanes), 0), chunk)
    return (token == lax.div(lax.broadcasted_iota(jnp.int32, (rows, lanes), 1), lanes // chunk)).astype(
        jnp.float32
    )


def spread_rows(pair):
    return contract(pair, jnp.ones((pair.shape[0], lanes), pair.dtype), 0, 0)


def spread_all(pairs, target):
    def some(index, carry):
        spread = spread_rows(pairs[index])
        target[pl.ds(index * chunk, chunk)] = spread.reshape(chunk, -1, lanes)
        return carry

    lax.fori_loop(0, pairs.shape[0], some, 0, unroll=8)


def folded(buffer, tile):
    total = buffer[tile, pl.ds(0, chunk, stride=chunk), :]
    for row in range(1, chunk):
        total = total + buffer[tile, pl.ds(row, chunk, stride=chunk), :]
    return total


def forward_kernel(
    plan,
    dims,
    lengths_ref,
    projected_ref,
    small_ref,
    signal_ref,
    write_pair,
    read_pair,
    own_ref,
    states_ref,
    step_ref,
    core_ref,
    begin_ref,
    whole_ref,
    offset_buf,
    pre_buf,
    decay_step,
    flows,
    write_wide,
    read_wide,
    fold_buf,
    held_buf,
    low_buf,
    *sems,
):
    rows, width = pre_buf.shape
    size = plan["decay"][1]
    half_size = size // 2
    tiles = width // lanes
    chunks = rows // chunk
    rank = plan["step"][1]
    group = pl.program_id(1)
    groups = pl.num_programs(1)
    moment = pl.program_id(0) * groups + group
    moments = pl.num_programs(0) * groups
    gather = Gather(dims, [low_buf], [whole_ref], sems)

    @pl.when(moment == 0)
    def _():
        low_buf[...] = own_ref[...].astype(low_buf.dtype)
        Place(dims).greet()
        gather.start(0)
        fill_offsets(lengths_ref, offset_buf, offset_buf.shape[0] - 8)
        spread_all(write_pair, write_wide)
        spread_all(read_pair, read_wide)

    for number, when in ((1, 5), (2, 9), (3, 13)):

        @pl.when(moment == when)
        def _(number=number):
            gather.leg(0, number)

    @pl.when(group == 0)
    def _():
        held_buf[...] = jnp.zeros_like(held_buf)

    begin_ref[0] = held_buf[...]
    pre_buf[...] = jnp.dot(
        projected_ref[:, :rank].astype(small_ref.dtype),
        small_ref[pl.ds(plan["step"][0], rank), :],
        preferred_element_type=jnp.float32,
    )
    bias = small_rows(small_ref, *plan["bias"])

    def before(index, at, carry):
        spot = pl.ds(pl.multiple_of(index * 4, 4), 4)
        inside = offset_buf[pl.ds(pl.multiple_of(group * rows + index * 32, 32), 32), :] > 0
        for tile in range(tiles):
            step = softplus(pre_buf[at, cut(tile)] + bias[:, tile * lanes : (tile + 1) * lanes])
            step_ref[spot, :, cut(tile)] = step.reshape(4, chunk, lanes)
            decay_step[spot, :, cut(tile)] = jnp.where(inside, step, far).reshape(4, chunk, lanes)
            flow = step * signal_ref[at, cut(tile)].astype(jnp.float32)
            flows[spot, :, cut(tile)] = flow.reshape(4, chunk, lanes)
        return carry

    row_loop(rows, 4 * chunk, before, 0)
    rates = -jnp.exp(small_rows(small_ref, *plan["decay"])) * log2e
    rates = [rates[:, tile * lanes : (tile + 1) * lanes] for tile in range(tiles)]

    def forward(index, held):
        held = list(held)
        for place in range(chunk):
            now = index * chunk + place
            write_now = write_wide[group * rows + now]
            read_now = read_wide[group * rows + now]
            for tile in range(tiles):
                decay = jnp.exp2(rates[tile] * decay_step[index, pl.ds(place, 1), cut(tile)])
                fresh = decay * held[tile] + write_now * flows[index, pl.ds(place, 1), cut(tile)]
                held[tile] = fresh
                states_ref[now, :, cut(tile)] = fresh
                product = read_now * fresh
                fold_buf[tile, pl.ds(place * chunk, chunk), :] = product[:half_size] + product[half_size:]
        for tile in range(tiles):
            core_ref[index, :, cut(tile)] = folded(fold_buf, tile)
        return tuple(held)

    held = tuple(held_buf[:, cut(tile)] for tile in range(tiles))
    held = lax.fori_loop(0, chunks, forward, held)
    for tile in range(tiles):
        held_buf[:, cut(tile)] = held[tile]

    @pl.when(moment == moments - 1)
    def _():
        gather.arrive(0)
        gather.drain(0)


def middle_kernel(
    plan,
    core_ref,
    small_ref,
    signal_ref,
    gate_ref,
    low_ref,
    out_w,
    flipped_ref,
    tokens_ref,
    core_grad_ref,
    gate_grad_ref,
    skip_grad_ref,
    out_grad_ref,
    in_grad_ref,
    output_ref,
    pre_buf,
    gated_buf,
    total,
):
    rows, width = pre_buf.shape
    tiles = width // lanes
    block = pl.program_id(0)
    pre_buf[...] = contract(low_ref[...], out_w[...], 1, 1)
    skip = small_rows(small_ref, *plan["skip"])

    def after(index, at, carry):
        spot = pl.ds(pl.multiple_of(index * 4, 4), 4)
        sums = []
        for tile in range(tiles):
            signal = signal_ref[at, cut(tile)].astype(jnp.float32)
            core = core_ref[spot, :, cut(tile)].reshape(4 * chunk, lanes)
            core = core + skip[:, tile * lanes : (tile + 1) * lanes] * signal
            gate = gate_ref[at, cut(tile)]
            sigma = sigmoid(gate)
            active = gate * sigma
            gated_buf[at, cut(tile)] = (core * active).astype(gated_buf.dtype)
            grad_gated = pre_buf[at, cut(tile)]
            grad_core = grad_gated * active
            core_grad_ref[spot, :, cut(tile)] = grad_core.reshape(4, chunk, lanes)
            slope = sigma + active * (1.0 - sigma)
            gate_grad_ref[at, cut(tile)] = (grad_gated * core * slope).astype(gate_grad_ref.dtype)
            sums.append(carry[tile] + eight(grad_core * signal))
        return tuple(sums)

    zero_rows = jnp.zeros((8, lanes), jnp.float32)
    skips = row_loop(rows, 4 * chunk, after, (zero_rows,) * tiles)
    for tile in range(tiles):
        skip_grad_ref[:, cut(tile)] = jnp.sum(skips[tile], axis=0, keepdims=True)
    out_grad_ref[...] = contract(gated_buf[...], low_ref[...], 0, 0).astype(out_grad_ref.dtype)
    in_grad_ref[...] = jnp.dot(
        flipped_ref[...], gate_grad_ref[...], preferred_element_type=jnp.float32
    ).astype(in_grad_ref.dtype)
    piece = jnp.dot(gated_buf[...], out_w[...], preferred_element_type=jnp.float32)

    @pl.when(block == 0)
    def _():
        total[...] = piece

    @pl.when(block > 0)
    def _():
        total[...] += piece

    @pl.when(block == pl.num_programs(0) - 1)
    def _():
        output_ref[...] = (tokens_ref[...].astype(jnp.float32) + total[...]).astype(output_ref.dtype)


def backward_kernel(
    plan,
    dims,
    lengths_ref,
    projected_ref,
    small_ref,
    signal_ref,
    write_pair,
    read_pair,
    step_ref,
    core_grad_ref,
    states_ref,
    begin_ref,
    out_grad_ref,
    in_grad_ref,
    signal_grad_ref,
    step_w_grad_ref,
    bias_grad_ref,
    decay_grad_ref,
    flat_ref,
    out_sum_ref,
    in_sum_ref,
    square_ref,
    offset_buf,
    decay_step,
    flows,
    write_wide,
    read_wide,
    first_buf,
    second_buf,
    through_buf,
    scaled_buf,
    low_buf,
    incoming_buf,
    rank_buf,
    write_buf,
    read_buf,
    *parts,
):
    rows, width = low_buf.shape
    rank = plan["step"][1]
    size = plan["decay"][1]
    half_size = size // 2
    tiles = width // lanes
    chunks = rows // chunk
    block = pl.program_id(0)
    turn = pl.program_id(1)
    groups = pl.num_programs(1)
    group = groups - 1 - turn
    moment = block * groups + turn
    moments = pl.num_programs(0) * groups
    reduce = Reduce(
        dims,
        [out_grad_ref, in_grad_ref],
        parts[2:12],
        parts[12:],
        parts[:2],
        False,
    )

    @pl.when(moment == 0)
    def _():
        Place(dims).greet()
        for which in range(2):
            reduce.start(which)
        fill_offsets(lengths_ref, offset_buf, offset_buf.shape[0] - 8)
        spread_all(write_pair, write_wide)
        spread_all(read_pair, read_wide)
        write_buf[...] = jnp.zeros_like(write_buf)
        read_buf[...] = jnp.zeros_like(read_buf)
        rank_buf[...] = jnp.zeros_like(rank_buf)

    for number, when in ((1, 2), (2, 7), (3, 11)):

        @pl.when(moment == when)
        def _(number=number):
            for which in range(2):
                reduce.leg(which, number)

    @pl.when(turn == 0)
    def _():
        incoming_buf[...] = jnp.zeros_like(incoming_buf)
        decay_grad_ref[...] = jnp.zeros_like(decay_grad_ref)
        bias_grad_ref[...] = jnp.zeros_like(bias_grad_ref)
        step_w_grad_ref[...] = jnp.zeros_like(step_w_grad_ref)

    def before(index, at, carry):
        spot = pl.ds(pl.multiple_of(index * 4, 4), 4)
        offsets = offset_buf[pl.ds(pl.multiple_of(group * rows + index * 32, 32), 32), :]
        inside = (offsets > 0).reshape(4, chunk, lanes)
        for tile in range(tiles):
            step = step_ref[spot, :, cut(tile)]
            decay_step[spot, :, cut(tile)] = jnp.where(inside, step, far)
            signal = signal_ref[at, cut(tile)].astype(jnp.float32).reshape(4, chunk, lanes)
            flows[spot, :, cut(tile)] = step * signal
        return carry

    row_loop(rows, 4 * chunk, before, 0)
    rates = -jnp.exp(small_rows(small_ref, *plan["decay"])) * log2e
    rates = [rates[:, tile * lanes : (tile + 1) * lanes] for tile in range(tiles)]

    def backward(position, carried):
        index = chunks - 1 - position
        incoming, decay_sums = list(carried[0]), list(carried[1])
        for place in range(chunk - 1, -1, -1):
            now = index * chunk + place
            token = group * rows + now
            write_now = write_wide[token]
            read_now = read_wide[token]
            read_sum = None
            write_sum = None
            for tile in range(tiles):
                step_now = decay_step[index, pl.ds(place, 1), cut(tile)]
                grad_now = core_grad_ref[index, pl.ds(place, 1), cut(tile)]
                if place > 0:
                    earlier = states_ref[now - 1, :, cut(tile)]
                else:
                    earlier = jnp.where(
                        index > 0, states_ref[jnp.maximum(now - 1, 0), :, cut(tile)], begin_ref[0, :, cut(tile)]
                    )
                grad_state = incoming[tile] + read_now * grad_now
                through_read = states_ref[now, :, cut(tile)] * grad_now
                through_write = grad_state * flows[index, pl.ds(place, 1), cut(tile)]
                read_sum = through_read if read_sum is None else read_sum + through_read
                write_sum = through_write if write_sum is None else write_sum + through_write
                passed = grad_state * write_now
                first_buf[tile, pl.ds(place * chunk, chunk), :] = passed[:half_size] + passed[half_size:]
                leaving = jnp.exp2(rates[tile] * step_now) * grad_state
                incoming[tile] = leaving
                weighted = leaving * earlier
                scaled = weighted * rates[tile]
                second_buf[tile, pl.ds(place * chunk, chunk), :] = scaled[:half_size] + scaled[half_size:]
                decay_sums[tile] = decay_sums[tile] + weighted * step_now
            read_buf[token] += read_sum
            write_buf[token] += write_sum
        for tile in range(tiles):
            through_buf[index, :, cut(tile)] = folded(first_buf, tile)
            scaled_buf[index, :, cut(tile)] = folded(second_buf, tile)
        return (tuple(incoming), tuple(decay_sums))

    incoming = tuple(incoming_buf[:, cut(tile)] for tile in range(tiles))
    nothing = (jnp.zeros((size, lanes), jnp.float32),) * tiles
    incoming, decay_sums = lax.fori_loop(0, chunks, backward, (incoming, nothing))
    for tile in range(tiles):
        incoming_buf[:, cut(tile)] = incoming[tile]
        decay_grad_ref[:, cut(tile)] += decay_sums[tile] * rates[tile] * ln2
    skip = small_rows(small_ref, *plan["skip"])

    def after(index, at, carry):
        spot = pl.ds(pl.multiple_of(index * 4, 4), 4)
        sums = []
        for tile in range(tiles):
            signal = signal_ref[at, cut(tile)].astype(jnp.float32)
            step = step_ref[spot, :, cut(tile)].reshape(4 * chunk, lanes)
            through = through_buf[spot, :, cut(tile)].reshape(4 * chunk, lanes)
            scaled = scaled_buf[spot, :, cut(tile)].reshape(4 * chunk, lanes)
            core_grad = core_grad_ref[spot, :, cut(tile)].reshape(4 * chunk, lanes)
            grad_pre = (through * signal + ln2 * scaled) * slope_of(step)
            low_buf[at, cut(tile)] = grad_pre.astype(low_buf.dtype)
            signal_grad_ref[at, cut(tile)] = (
                through * step + skip[:, tile * lanes : (tile + 1) * lanes] * core_grad
            )
            sums.append(carry[tile] + eight(grad_pre))
        return tuple(sums)

    zero_rows = jnp.zeros((8, lanes), jnp.float32)
    sums = row_loop(rows, 4 * chunk, after, (zero_rows,) * tiles)
    for tile in range(tiles):
        bias_grad_ref[:, cut(tile)] += jnp.sum(sums[tile], axis=0, keepdims=True)
    step_w_grad_ref[...] += contract(
        projected_ref[:, :rank].astype(low_buf.dtype), low_buf[...], 0, 0
    )
    step_w = small_ref[pl.ds(plan["step"][0], rank), :]
    step_w = jnp.concatenate([step_w, jnp.zeros((lanes - rank, width), step_w.dtype)], axis=0)
    rank_buf[pl.ds(group * chunks, chunks)] += contract(low_buf[...], step_w, 1, 1).reshape(
        chunks, chunk, lanes
    )

    @pl.when(moment == moments - 1)
    def _():
        square_ref[...] = reduce.finish(0)[0] + reduce.finish(1)[0]
        entry = lax.rem(lax.broadcasted_iota(jnp.int32, (chunk * size, lanes), 0), size)
        target = lax.broadcasted_iota(jnp.int32, (chunk * size, lanes), 1)
        ones = jnp.ones((lanes, lanes), jnp.bfloat16)
        places = [(target == entry + rank + number * size).astype(jnp.float32) for number in range(2)]

        def lay(index, carry):
            lot = pl.ds(index * chunk, chunk)
            for buffer, place in zip((write_buf, read_buf), places):
                high, low = high_low(buffer[lot].reshape(chunk * size, lanes))
                summed = jnp.dot(high.astype(jnp.bfloat16), ones, preferred_element_type=jnp.float32)
                summed += jnp.dot(low.astype(jnp.bfloat16), ones, preferred_element_type=jnp.float32)
                rank_buf[index] += jnp.sum((summed * place).reshape(chunk, size, lanes), axis=1)
            return carry

        lax.fori_loop(0, rank_buf.shape[0], lay, 0, unroll=4)
        flat_ref[...] = rank_buf[...].reshape(flat_ref.shape).astype(flat_ref.dtype)
        for which in range(2):
            reduce.settle(which)
        out_sum_ref[...] = parts[0][...]
        in_sum_ref[...] = parts[1][...]


def back_kernel(
    plan,
    dims,
    lengths_ref,
    tokens_ref,
    low_ref,
    gain_ref,
    small_ref,
    flat_ref,
    branch_ref,
    signal_ref,
    slope_ref,
    signal_grad_ref,
    gate_grad_ref,
    flipped_ref,
    branch_w,
    gate_w,
    step_w_grad_ref,
    bias_grad_ref,
    decay_grad_ref,
    skip_grad_ref,
    plain_ref,
    earlier_ref,
    tokens_grad_ref,
    in_sum_ref,
    small_sum_ref,
    norm_ref,
    offset_buf,
    conv_buf,
    mixed_buf,
    total,
    small_buf,
    in_stage,
    small_stage,
    in_result,
    small_result,
    *parts,
):
    rows = tokens_ref.shape[0]
    width = branch_ref.shape[1]
    tiles = width // lanes
    block = pl.program_id(0)
    last = in_stage.shape[0]
    count = last + 1
    reduce = Reduce(
        dims,
        [in_stage.at[index] for index in range(last)] + [small_stage],
        parts[: 5 * count],
        parts[5 * count : 5 * count + 7],
        [in_result.at[index] for index in range(last)] + [small_result],
        True,
    )
    norm_parts = parts[5 * count + 7 :]

    @pl.when(block == 0)
    def _():
        Place(dims).greet()
        fill_offsets(lengths_ref, offset_buf, rows)

    taps = small_rows(small_ref, *plan["taps"])
    taps_count = taps.shape[0]
    small_buf[:lanes, :] = contract(flat_ref[...], signal_ref[...], 0, 0)

    def place_rows(name, values):
        first, tall = plan[name]
        small_buf[first : first + tall, :] = values

    place_rows("step", step_w_grad_ref[...])
    place_rows("decay", decay_grad_ref[...])
    place_rows("bias", bias_grad_ref[...])
    place_rows("skip", skip_grad_ref[...])
    conv_buf[pl.ds(0, rows), :] = signal_grad_ref[...] + jnp.dot(
        flat_ref[...], small_ref[:lanes, :], preferred_element_type=jnp.float32
    )
    conv_buf[pl.ds(rows, 8), :] = jnp.zeros((8, width), jnp.float32)

    def through_conv(index, at, carry):
        sums = []
        for tile in range(tiles):
            grad_conv = conv_buf[at, cut(tile)] * slope_ref[at, cut(tile)]
            conv_buf[at, cut(tile)] = grad_conv
            sums.append(carry[tile] + eight(grad_conv))
        return tuple(sums)

    zero_rows = jnp.zeros((8, lanes), jnp.float32)
    sums = row_loop(rows, 32, through_conv, (zero_rows,) * tiles)
    for tile in range(tiles):
        first = plan["shift"][0]
        small_buf[first : first + 1, cut(tile)] = jnp.sum(sums[tile], axis=0, keepdims=True)

    def to_branch(index, at, carry):
        longer = pl.ds(pl.multiple_of(index * 32, 32), 40)
        offsets = offset_buf[longer, :]
        result = []
        for tile in range(tiles):
            here = slice(tile * lanes, (tile + 1) * lanes)
            grads = conv_buf[longer, cut(tile)]
            branch = branch_ref[at, cut(tile)]
            summed = taps[taps_count - 1 : taps_count, here] * grads[:32]
            sums = [None] * taps_count
            sums[taps_count - 1] = carry[tile][taps_count - 1] + eight(branch * grads[:32])
            for tap in range(taps_count - 1):
                lag = taps_count - 1 - tap
                moved = pltpu.roll(jnp.where(offsets >= lag, grads, 0.0), 40 - lag, 0)[:32]
                summed = summed + taps[tap : tap + 1, here] * moved
                sums[tap] = carry[tile][tap] + eight(branch * moved)
            mixed_buf[at, cut(tile)] = summed.astype(mixed_buf.dtype)
            result.append(tuple(sums))
        return tuple(result)

    sums = row_loop(rows, 32, to_branch, ((zero_rows,) * taps_count,) * tiles)
    for tile in range(tiles):
        for tap in range(taps_count):
            first = plan["taps"][0] + tap
            small_buf[first : first + 1, cut(tile)] = jnp.sum(sums[tile][tap], axis=0, keepdims=True)
    in_grad = jnp.dot(flipped_ref[...], mixed_buf[...], preferred_element_type=jnp.float32)
    in_stage[block] = in_grad.reshape(in_stage.shape[1:]).astype(in_stage.dtype)
    share = small_stage.shape[4]
    half_rows = small_stage.shape[3]
    for piece in range(width // share):
        owner = block * (width // share) + piece
        z, plane = lax.div(owner, small_stage.shape[1]), lax.rem(owner, small_stage.shape[1])
        for side in range(2):
            small_stage[z, plane, side] = small_buf[
                side * half_rows : (side + 1) * half_rows, piece * share : (piece + 1) * share
            ].astype(small_stage.dtype)
    for index in range(last):

        @pl.when(block == index)
        def _(index=index):
            reduce.start(index)

    piece = contract(mixed_buf[...], rows_of(branch_w), 1, 1)
    piece += contract(gate_grad_ref[...], rows_of(gate_w), 1, 1)

    @pl.when(block == 0)
    def _():
        total[...] = piece

    @pl.when(block > 0)
    def _():
        total[...] += piece

    for moment, legs in ((1, ((0, 1),)), (2, ((0, 2), (1, 1))), (3, ((0, 3), (1, 2), (2, 1)))):

        @pl.when(block == moment)
        def _(legs=legs):
            for which, number in legs:
                reduce.leg(which, number)

    @pl.when(block == pl.num_programs(0) - 1)
    def _():
        def finish(index, at, carry):
            residual = tokens_ref[at, :].astype(jnp.float32)
            scale = lax.rsqrt(jnp.mean(residual * residual, axis=1, keepdims=True) + epsilon)
            grad_normed = total[at, :]
            weighted = grad_normed * gain_ref[...]
            inner = jnp.mean(weighted * residual, axis=1, keepdims=True)
            grad_y = low_ref[at, :].astype(jnp.float32)
            result = grad_y + (scale * weighted - residual * (scale * scale * scale) * inner)
            tokens_grad_ref[at, :] = result.astype(tokens_grad_ref.dtype)
            return carry + eight(grad_normed * residual * scale)

        gains = row_loop(rows, 16, finish, jnp.zeros((8, total.shape[1]), jnp.float32))
        gains = jnp.sum(gains, axis=0, keepdims=True)
        planes = small_stage.shape[1]
        each = gains.shape[1] // (small_stage.shape[0] * planes)
        side, row = plan["gain"][0] // half_rows, plan["gain"][0] % half_rows
        for owner in range(small_stage.shape[0] * planes):
            small_stage[owner // planes, owner % planes, side, row : row + 1, :each] = gains[
                :, owner * each : (owner + 1) * each
            ].astype(small_stage.dtype)
        reduce.start(last)
        for which, number in ((3, 1), (2, 2), (1, 3), (4, 1), (3, 2), (2, 3), (4, 2), (3, 3), (4, 3)):
            reduce.leg(which, number)
        kept = earlier_ref[...]
        for index in range(last):
            kept = kept + reduce.finish(index)[0]
        more, plain = reduce.finish(last, plain_ref)
        norm_ref[...] = sum_norms(dims, jnp.stack([kept + more, plain]), norm_parts[:4], *norm_parts[4:])
        for index in range(count):
            reduce.settle(index)
        for index in range(last):
            in_sum_ref[:, index * width : (index + 1) * width] = in_result[index]
        small_sum_ref[...] = small_result[...]


def finish_kernel(plan, names, branch_ref, gate_ref, out_ref, small_ref, norm_ref, *outs):
    middle = branch_ref.shape[1]
    outs[0][:, :middle] = branch_ref[...]
    outs[0][:, middle:] = gate_ref[...]
    outs[1][...] = out_ref[...]
    for name, target in zip(names, outs[2 : 2 + len(names)]):
        first, count = plan[name]
        if len(target.shape) == 1:
            target[...] = small_ref[first, : target.shape[0]]
        else:
            target[...] = small_ref[first : first + count, :]
    for index in range(2):
        outs[2 + len(names) + index][0, 0] = jnp.sum(norm_ref[index])


def shape(dims, kind=jnp.float32):
    return jax.ShapeDtypeStruct(dims, kind)


def compute_call(
    kernel, name, blocks, in_specs, out_specs, out_shape, scratch, flops, operands, collective_id=None
):
    return pl.pallas_call(
        kernel,
        grid=blocks if isinstance(blocks, tuple) else (blocks,),
        in_specs=in_specs,
        out_specs=out_specs,
        out_shape=out_shape,
        scratch_shapes=scratch,
        compiler_params=pltpu.CompilerParams(
            dimension_semantics=("arbitrary",) * (len(blocks) if isinstance(blocks, tuple) else 1),
            vmem_limit_bytes=62 * 1024 * 1024,
            collective_id=collective_id,
            has_side_effects=collective_id is not None,
        ),
        cost_estimate=pl.CostEstimate(flops=flops, bytes_accessed=40 << 20, transcendentals=0),
        name=name,
    )(*operands)


class Place:
    def __init__(self, dims, swapped=False):
        depth, tall, wide = dims
        self.dims = dims
        self.core = lax.axis_index("wide")
        self.me = lax.axis_index("narrow")
        self.across = lax.rem(self.me, wide)
        self.up = lax.rem(lax.div(self.me, wide), tall)
        self.deep = lax.div(self.me, wide * tall)
        side = 1 - self.core if swapped else self.core
        turn = side if tall == wide else 0
        self.second = (1 + turn * (wide - 1), self.across + turn * (self.up - self.across), wide)
        self.third = (wide - turn * (wide - 1), self.up + turn * (self.across - self.up), tall)
        self.spans = (depth, wide, tall)
        self.other = {"wide": 1 - self.core}

    def level(self, d):
        return lax.rem(self.deep + d, self.spans[0])

    def plane(self, e, f):
        return (
            lax.rem(self.second[1] + e, self.second[2]) * self.second[0]
            + lax.rem(self.third[1] + f, self.third[2]) * self.third[0]
        )

    def plane_behind(self, e, f):
        return self.plane((self.spans[1] - e) % self.spans[1], (self.spans[2] - f) % self.spans[2])

    def at(self, d, e, f):
        return {"narrow": self.level(d) * (self.dims[1] * self.dims[2]) + self.plane(e, f)}

    def greet(self):
        barrier = pltpu.get_barrier_semaphore()
        peers = [self.other]
        for axis, size in enumerate(self.spans):
            for hop in range(1, size):
                move = [0, 0, 0]
                move[axis] = hop
                peers.append(self.at(*move))
        for peer in peers:
            pl.semaphore_signal(barrier, inc=1, device_id=peer, device_id_type=pl.DeviceIdType.MESH)
        pl.semaphore_wait(barrier, len(peers))


def columns_of(width, side):
    return pl.ds(pl.multiple_of(side * (width // 2), lanes), width // 2)


def half_shape(block):
    return tuple(block[1:]) if len(block) == 3 else (block[0], block[1] // 2)


def half(view, block, side, lead=0):
    if len(block) == 3:
        return view.at[(slice(None),) * lead + (side,)]
    return view.at[(slice(None),) * (lead + 1) + (columns_of(block[1], side),)]


def remote(source, target, send_sem, recv_sem, device):
    return pltpu.make_async_remote_copy(
        src_ref=source,
        dst_ref=target,
        send_sem=send_sem,
        recv_sem=recv_sem,
        device_id=device,
        device_id_type=pl.DeviceIdType.MESH,
    )


class Gather:
    def __init__(self, dims, own, whole, sems):
        self.dims, self.own, self.whole = dims, own, whole
        self.local_sem, self.send_sem, self.recv_sem = sems

    @staticmethod
    def sems(count, dims):
        copies = dims[0] + 2 * dims[1] * dims[2]
        return [pltpu.SemaphoreType.DMA((count,))] + [pltpu.SemaphoreType.DMA((count, copies))] * 2

    def line(self, which, plane, side):
        return half(self.whole[which].at[:, plane], self.own[which].shape, side, 1)

    def local(self, place, which):
        block = self.own[which].shape
        return pltpu.make_async_copy(
            half(self.own[which], block, place.core),
            half(self.whole[which].at[place.deep, place.plane(0, 0)], block, place.core),
            self.local_sem.at[which],
        )

    def copy(self, which, source, target, index, device):
        return remote(
            source, target, self.send_sem.at[which, index], self.recv_sem.at[which, index], device
        )

    def rise(self, place, which, hop):
        block = self.own[which].shape
        return self.copy(
            which,
            half(self.own[which], block, place.core),
            half(self.whole[which].at[place.deep, place.plane(0, 0)], block, place.core),
            hop,
            place.at(hop, 0, 0),
        )

    def leg_index(self, e, f):
        return self.dims[0] + e * self.dims[1] + f

    def hand_index(self, e, f):
        return self.leg_index(e, f) + self.dims[1] * self.dims[2]

    def onward(self, place, which, e, f):
        line = self.line(which, place.plane_behind(e, f), place.core)
        if f == 0:
            for hop in range(1, place.spans[2]):
                self.copy(which, line, line, self.leg_index(e, hop), place.at(0, 0, hop)).start()
        if f == 0 and e == 0:
            for hop in range(1, place.spans[1]):
                self.copy(which, line, line, self.leg_index(hop, 0), place.at(0, hop, 0)).start()
        self.copy(which, line, line, self.hand_index(e, f), place.other).start()

    def start(self, which):
        place = Place(self.dims)
        for hop in range(1, place.spans[0]):
            self.rise(place, which, hop).start()
        self.local(place, which).start()

    def leg(self, which, number):
        place = Place(self.dims)
        if number == 1:
            self.local(place, which).wait()
            for hop in range(1, place.spans[0]):
                self.rise(place, which, hop).wait_recv()
            self.onward(place, which, 0, 0)
            return
        for e in range(place.spans[1]):
            for f in range(place.spans[2]):
                if (number == 2 and f == 0 and e > 0) or (number == 3 and f > 0):
                    line = self.line(which, place.plane_behind(e, f), place.core)
                    self.copy(which, line, line, self.leg_index(e, f), place.other).wait_recv()
                    self.onward(place, which, e, f)

    def arrive(self, which):
        place, mirror = Place(self.dims), Place(self.dims, swapped=True)
        for e in range(place.spans[1]):
            for f in range(place.spans[2]):
                line = self.line(which, mirror.plane_behind(e, f), 1 - place.core)
                self.copy(which, line, line, self.hand_index(e, f), place.other).wait_recv()

    def drain(self, which):
        place = Place(self.dims)
        for hop in range(1, place.spans[0]):
            self.rise(place, which, hop).wait_send()
        for e in range(place.spans[1]):
            for f in range(place.spans[2]):
                line = self.line(which, place.plane_behind(e, f), place.core)
                if e > 0 or f > 0:
                    self.copy(which, line, line, self.leg_index(e, f), place.other).wait_send()
                self.copy(which, line, line, self.hand_index(e, f), place.other).wait_send()


class Reduce:
    def __init__(self, dims, grads, rooms, sems, results, resident):
        self.dims, self.grads, self.resident = dims, grads, resident
        count = len(grads)
        self.mine, self.swapped, self.third, self.second, self.first = (
            rooms[index * count : (index + 1) * count] for index in range(5)
        )
        self.load_sem, self.swap_send, self.swap_recv, self.send_sem, self.recv_sem = sems[:5]
        self.last_send, self.last_recv = sems[5:]
        self.results = results

    @staticmethod
    def rooms(dims, grads):
        depth, tall, wide = dims
        leads = (
            (tall, wide, depth),
            (depth, tall * wide),
            (tall - 1, wide, depth),
            (wide - 1, depth),
            (depth - 1,),
        )
        return [
            pltpu.VMEM(lead + half_shape(grad.shape[2:]), grad.dtype) for lead in leads for grad in grads
        ]

    @staticmethod
    def sems(count, dims):
        groups = dims[1] * dims[2]
        return (
            [pltpu.SemaphoreType.DMA((count, groups))] * 3
            + [pltpu.SemaphoreType.DMA((count, dims[0] + dims[1] + dims[2]))] * 2
            + [pltpu.SemaphoreType.DMA((count,))] * 2
        )

    def groups(self, place):
        return [
            (e, f)
            for f in range(place.spans[2] - 1, -1, -1)
            for e in range(place.spans[1] - 1, -1, -1)
        ]

    def number(self, e, f):
        return e * self.dims[1] + f

    def block(self, which):
        return self.grads[which].shape[2:]

    def load(self, place, which, e, f):
        return pltpu.make_async_copy(
            half(self.grads[which].at[:, place.plane(e, f)], self.block(which), place.core, 1),
            self.mine[which].at[f, e],
            self.load_sem.at[which, self.number(e, f)],
        )

    def swap(self, place, which, e, f, plane):
        return remote(
            half(self.grads[which].at[:, plane], self.block(which), 1 - place.core, 1),
            self.swapped[which].at[:, plane],
            self.swap_send.at[which, self.number(e, f)],
            self.swap_recv.at[which, self.number(e, f)],
            place.other,
        )

    def hop(self, which, source, target, index, device):
        return remote(
            source, target, self.send_sem.at[which, index], self.recv_sem.at[which, index], device
        )

    def third_hop(self, place, which, f):
        return self.hop(which, self.mine[which].at[f], self.third[which].at[f - 1], f, place.at(0, 0, f))

    def second_hop(self, place, which, e):
        return self.hop(
            which,
            self.mine[which].at[0, e],
            self.second[which].at[e - 1],
            self.dims[1] + e,
            place.at(0, e, 0),
        )

    def first_hop(self, place, which, d):
        return self.hop(
            which,
            self.mine[which].at[0, 0, place.level(d)],
            self.first[which].at[d - 1],
            self.dims[1] + self.dims[2] + d,
            place.at(d, 0, 0),
        )

    def start(self, which):
        place, mirror = Place(self.dims), Place(self.dims, swapped=True)
        for e, f in self.groups(place):
            self.swap(place, which, e, f, mirror.plane(e, f)).start()
            if not self.resident:
                self.load(place, which, e, f).start()

    def parts(self, place, which, e, f, z):
        plane = place.plane(e, f)
        if self.resident:
            found = [half(self.grads[which].at[z, plane], self.block(which), place.core)]
        else:
            found = [self.mine[which].at[f, e, z]]
        found.append(self.swapped[which].at[z, plane])
        if f == 0:
            found += [self.third[which].at[hop - 1, e, z] for hop in range(1, place.spans[2])]
        if f == 0 and e == 0:
            found += [self.second[which].at[hop - 1, z] for hop in range(1, place.spans[1])]
        return found

    def ready(self, place, which, e, f):
        if not self.resident:
            self.load(place, which, e, f).wait()
        self.swap(place, which, e, f, place.plane(e, f)).wait_recv()

    def added(self, parts, store, carry):
        rows = parts[0].shape[0]
        group = min(rows, 16)

        def some(index, carry):
            at_rows = pl.ds(pl.multiple_of(index * group, group), group)
            total = parts[0][at_rows, :].astype(jnp.float32)
            for part in parts[1:]:
                total = total + part[at_rows, :].astype(jnp.float32)
            return store(at_rows, total, carry)

        return lax.fori_loop(0, rows // group, some, carry)

    def sum_into(self, place, which, e, f, z):
        target = self.mine[which].at[f, e, z]

        def keep(at_rows, total, carry):
            target[at_rows, :] = total.astype(target.dtype)
            return carry

        self.added(self.parts(place, which, e, f, z), keep, 0)

    def leg(self, which, number):
        place = Place(self.dims)
        depth, span_e, span_f = place.spans
        if number == 1:
            for f in range(span_f - 1, 0, -1):
                for e in range(span_e - 1, -1, -1):
                    self.ready(place, which, e, f)
                    for z in range(depth):
                        self.sum_into(place, which, e, f, z)
                self.third_hop(place, which, f).start()
        elif number == 2:
            for f in range(1, span_f):
                self.third_hop(place, which, f).wait_recv()
            for e in range(span_e - 1, 0, -1):
                self.ready(place, which, e, 0)
                for z in range(depth):
                    self.sum_into(place, which, e, 0, z)
                self.second_hop(place, which, e).start()
        else:
            self.ready(place, which, 0, 0)
            if span_e == 1:
                for f in range(1, span_f):
                    self.third_hop(place, which, f).wait_recv()
            for e in range(1, span_e):
                self.second_hop(place, which, e).wait_recv()
            for d in range(1, depth):
                self.sum_into(place, which, 0, 0, place.level(d))
                self.first_hop(place, which, d).start()

    def result(self, which, side):
        return half(self.results[which], self.block(which), side)

    def last(self, place, which, side):
        share = self.result(which, side)
        return remote(share, share, self.last_send.at[which], self.last_recv.at[which], place.other)

    def finish(self, which, marks=None):
        place = Place(self.dims)
        parts = self.parts(place, which, 0, 0, place.deep)
        for d in range(1, place.spans[0]):
            self.first_hop(place, which, d).wait_recv()
            parts.append(self.first[which].at[d - 1])
        share = self.result(which, place.core)

        def store(at_rows, total, carry):
            share[at_rows, :] = total
            kept, plain = carry
            squared = total * total
            if marks is not None:
                marked = squared * marks[place.core, at_rows, :]
                plain = plain + folded_squares(marked)
                squared = squared - marked
            return (kept + folded_squares(squared), plain)

        squares = self.added(parts, store, (jnp.zeros((8, lanes), jnp.float32),) * 2)
        self.last(place, which, place.core).start()
        return squares

    def settle(self, which):
        place, mirror = Place(self.dims), Place(self.dims, swapped=True)
        last = self.last(place, which, 1 - place.core)
        last.wait_recv()
        last.wait_send()
        for e, f in self.groups(place):
            self.swap(place, which, e, f, mirror.plane(e, f)).wait_send()
        for f in range(1, place.spans[2]):
            self.third_hop(place, which, f).wait_send()
        for e in range(1, place.spans[1]):
            self.second_hop(place, which, e).wait_send()
        for d in range(1, place.spans[0]):
            self.first_hop(place, which, d).wait_send()


def folded_squares(values):
    total = None
    if values.shape[1] < lanes:
        first = lax.broadcasted_iota(jnp.int32, (values.shape[0], lanes), 1) == 0
        values = jnp.where(first, jnp.sum(values, axis=1, keepdims=True), 0.0)
    for row in range(0, values.shape[0], 8):
        for column in range(0, values.shape[1], lanes):
            piece = values[row : row + 8, column : column + lanes]
            total = piece if total is None else total + piece
    return total


def sum_norms(dims, running, buffers, send_sem, recv_sem):
    place = Place(dims)
    depth, tall, wide = dims
    plane = tall * wide
    me = place.me
    stages = (
        (buffers[0], 2, place.core, lambda spot: {"wide": spot}),
        (buffers[1], depth, place.deep, lambda spot: {"narrow": spot * plane + lax.rem(me, plane)}),
        (buffers[2], wide, place.across, lambda spot: {"narrow": me - place.across + spot}),
        (buffers[3], tall, place.up, lambda spot: {"narrow": me + (spot - place.up) * wide}),
    )
    pending = []
    first = 0
    for buffer, size, mine_at, device in stages:
        buffer[mine_at] = running
        for hop in range(1, size):
            copy = remote(
                buffer.at[mine_at],
                buffer.at[mine_at],
                send_sem.at[first + hop - 1],
                recv_sem.at[first + hop - 1],
                device(lax.rem(mine_at + hop, size)),
            )
            copy.start()
            pending.append(copy)
        for hop in range(1, size):
            came = lax.rem(mine_at + size - hop, size)
            remote(
                buffer.at[came],
                buffer.at[came],
                send_sem.at[first + hop - 1],
                recv_sem.at[first + hop - 1],
                device(came),
            ).wait_recv()
        first += size - 1
        running = buffer[0]
        for spot in range(1, size):
            running = running + buffer[spot]
    for copy in pending:
        copy.wait_send()
    return running


def norm_rooms(dims):
    depth, tall, wide = dims
    return [pltpu.VMEM((size, 2, 8, lanes), jnp.float32) for size in (2, depth, wide, tall)] + [
        pltpu.SemaphoreType.DMA((depth + tall + wide,))
    ] * 2


def grid_of(mesh):
    number = mesh.shape["narrow"]
    places = [getattr(device, "coords", None) for device in mesh.devices[0]]
    if all(place is not None for place in places):
        sizes = [len({place[axis] for place in places}) for axis in (2, 1, 0)]
        if sizes[0] * sizes[1] * sizes[2] == number:
            return tuple(sizes)
    side = round((number / 2) ** (1 / 3))
    return (2 * side, side, side) if 2 * side**3 == number else (number, 1, 1)


def plan_of(select_rows, state_size, tap_count, step_rows):
    plan, first = {}, 0
    for name, tall in (
        ("select", select_rows),
        ("decay", state_size),
        ("taps", tap_count),
        ("shift", 1),
        ("bias", 1),
        ("skip", 1),
        ("gain", 1),
    ):
        plan[name] = (first, tall)
        first += tall
    plan["step"] = (lanes, step_rows)
    plan["rows"] = -(-(lanes + step_rows) // 32) * 32
    return plan


def per_device(
    dims,
    tokens,
    cotangent,
    loss_mask,
    seq_lengths,
    norm_gain,
    in_proj,
    conv_weight,
    conv_bias,
    select_proj,
    step_proj,
    step_bias,
    decay_log,
    skip_scale,
    out_proj,
):
    half = jnp.bfloat16
    piece = skip_scale.shape[0]
    gain_piece = norm_gain.shape[0]
    rank, size = step_proj.shape[0], decay_log.shape[0]
    plan = plan_of(select_proj.shape[0], size, conv_weight.shape[0], rank)
    smalls = {
        "select": select_proj,
        "decay": decay_log,
        "taps": conv_weight,
        "shift": conv_bias[None],
        "bias": step_bias[None],
        "skip": skip_scale[None],
        "gain": norm_gain[None],
        "step": step_proj,
    }
    depth, planes = dims[0], dims[1] * dims[2]
    number = depth * planes
    in_rows = in_proj.shape[0]
    rows, model = tokens.shape
    inner = piece * number
    width = 4 * lanes
    blocks = inner // width
    chunks = rows // chunk
    mask_row = loss_mask[None]

    whole = pl.BlockSpec(memory_space=pltpu.VMEM)
    tall = pl.BlockSpec((rows, width), lambda b: (0, b))
    deep = pl.BlockSpec((chunks, chunk, width), lambda b: (0, 0, b))
    lead = pl.BlockSpec((rows, size, width), lambda b: (0, 0, b))
    first_w = pl.BlockSpec((model, width), lambda b: (0, b))
    second_w = pl.BlockSpec((model, width), lambda b: (0, b + blocks))
    out_w = pl.BlockSpec((width, model), lambda b: (b, 0))

    def thin(height):
        return pl.BlockSpec((height, width), lambda b: (0, b))

    def fixed(*dims_of):
        return pl.BlockSpec(dims_of, lambda b: (0,) * len(dims_of))

    scalars = pl.BlockSpec(memory_space=pltpu.SMEM)
    offset_buf = pltpu.VMEM((rows + 8, lanes), jnp.int32)
    packed = thin(plan["rows"])

    pair = (chunks, 2 * chunk, lanes)
    pair = (chunks, 2 * chunk, lanes)
    anywhere = pl.BlockSpec(memory_space=pl.ANY)
    small_half = (2, plan["rows"] // 2, piece)
    in_half = (2, in_rows, width)
    (
        branch,
        gate_pre,
        signal,
        slope,
        projected,
        flipped,
        grad_low,
        write_pair,
        read_pair,
        small,
        gain_value,
        in_blocks,
    ) = compute_call(
        functools.partial(front_kernel, plan, dims, tuple(smalls)),
        "front",
        blocks,
        [scalars, whole, whole, whole] + [whole] * (len(smalls) + 1),
        [tall, tall, tall, tall] + [whole] * 7 + [anywhere],
        [
            shape((rows, inner)),
            shape((rows, inner)),
            shape((rows, inner), half),
            shape((rows, inner)),
            shape((rows, lanes)),
            shape((model, rows), half),
            shape((rows, model), half),
            shape(pair, half),
            shape(pair, half),
            shape((plan["rows"], inner), half),
            shape((1, model)),
            shape((blocks, depth, planes) + in_half, half),
        ],
        [
            pltpu.VMEM((rows, model), half),
            offset_buf,
            pltpu.VMEM((plan["rows"], piece), jnp.float32),
            pltpu.VMEM(small_half, half),
            pltpu.VMEM((blocks,) + in_half, half),
            pltpu.VMEM((depth, planes) + small_half, half),
            pltpu.VMEM((blocks, depth, planes) + in_half, half),
            pltpu.SemaphoreType.DMA((blocks,)),
        ]
        + Gather.sems(blocks + 1, dims),
        4 * rows * model * inner,
        (seq_lengths, tokens, cotangent, mask_row, *smalls.values(), in_proj),
        collective_id=0,
    )
    groups = 4
    part, pieces = rows // groups, chunks // groups
    row_block = pltpu.VMEM((pieces, chunk, width), jnp.float32)
    spread_block = pltpu.VMEM((rows, size, lanes), jnp.float32)
    fold_block = pltpu.VMEM((width // lanes, chunk * chunk, lanes), jnp.float32)

    def by_group(order, *dims_of):
        middle = (0,) * (len(dims_of) - 2)
        return pl.BlockSpec(dims_of, lambda b, g: (order(g),) + middle + (b,))

    def by_token(order, *dims_of):
        return pl.BlockSpec(dims_of, lambda b, g: (order(g),) + (0,) * (len(dims_of) - 1))

    def by_channel(height):
        return pl.BlockSpec((height, width), lambda b, g: (0, b))

    def onward(g):
        return g

    def backward(g):
        return groups - 1 - g

    states, step, core, begins, out_blocks = compute_call(
        functools.partial(forward_kernel, plan, dims),
        "forward",
        (blocks, groups),
        [
            scalars,
            by_token(onward, part, lanes),
            by_channel(plan["rows"]),
            by_group(onward, part, width),
            whole,
            whole,
            whole,
        ],
        [
            by_group(onward, part, size, width),
            by_group(onward, pieces, chunk, width),
            by_group(onward, pieces, chunk, width),
            by_group(onward, 1, size, width),
            anywhere,
        ],
        [
            shape((rows, size, inner)),
            shape((chunks, chunk, inner)),
            shape((chunks, chunk, inner)),
            shape((groups, size, inner)),
            shape((depth, planes) + out_proj.shape, half),
        ],
        [
            offset_buf,
            pltpu.VMEM((part, width), jnp.float32),
            row_block,
            row_block,
            spread_block,
            spread_block,
            fold_block,
            pltpu.VMEM((size, width), jnp.float32),
            pltpu.VMEM(out_proj.shape, half),
        ]
        + Gather.sems(1, dims),
        15 * rows * inner * size,
        (seq_lengths, projected, small, signal, write_pair, read_pair, out_proj),
        collective_id=2,
    )
    core_grad, gate_grad, grad_skip, grad_outw, grad_in_gate, output = compute_call(
        functools.partial(middle_kernel, plan),
        "middle",
        blocks,
        [deep, packed, tall, tall, whole, out_w, whole, whole],
        [deep, tall, thin(1), out_w, first_w, fixed(rows, model)],
        [
            shape((chunks, chunk, inner)),
            shape((rows, inner), half),
            shape((1, inner)),
            shape((inner, model), half),
            shape((model, inner), half),
            shape((rows, model), half),
        ],
        [
            pltpu.VMEM((rows, width), jnp.float32),
            pltpu.VMEM((rows, width), half),
            pltpu.VMEM((rows, model), jnp.float32),
        ],
        8 * rows * model * inner,
        (core, small, signal, gate_pre, grad_low, out_blocks.reshape(inner, model), flipped, tokens),
    )
    early_grads = [
        grad_outw.reshape((depth, planes) + out_proj.shape),
        grad_in_gate.reshape(depth, planes, in_rows, inner),
    ]
    early_sums = [shape(grad.shape[2:]) for grad in early_grads]
    (
        signal_grad,
        grad_stepw,
        grad_bias,
        grad_decaylog,
        flat,
        out_sum,
        in_gate_sum,
        early_squares,
    ) = compute_call(
        functools.partial(backward_kernel, plan, dims),
        "backward",
        (blocks, groups),
        [
            scalars,
            by_token(backward, part, lanes),
            by_channel(plan["rows"]),
            by_group(backward, part, width),
            whole,
            whole,
            by_group(backward, pieces, chunk, width),
            by_group(backward, pieces, chunk, width),
            by_group(backward, part, size, width),
            by_group(backward, 1, size, width),
            anywhere,
            anywhere,
        ],
        [
            by_group(backward, part, width),
            by_channel(rank),
            by_channel(1),
            by_channel(size),
            whole,
        ]
        + [whole] * 3,
        [
            shape((rows, inner)),
            shape((rank, inner)),
            shape((1, inner)),
            shape((size, inner)),
            shape((rows, lanes), half),
            *early_sums,
            shape((8, lanes)),
        ],
        [
            offset_buf,
            row_block,
            row_block,
            spread_block,
            spread_block,
            fold_block,
            fold_block,
            row_block,
            row_block,
            pltpu.VMEM((part, width), half),
            pltpu.VMEM((size, width), jnp.float32),
            pltpu.VMEM((chunks, chunk, lanes), jnp.float32),
            spread_block,
            spread_block,
        ]
        + [pltpu.VMEM(early.shape, early.dtype) for early in early_sums]
        + Reduce.rooms(dims, early_grads)
        + Reduce.sems(2, dims),
        40 * rows * inner * size,
        (
            seq_lengths,
            projected,
            small,
            signal,
            write_pair,
            read_pair,
            step,
            core_grad,
            states,
            begins,
            *early_grads,
        ),
        collective_id=3,
    )

    plain_rows = np.zeros((plan["rows"], piece), np.float32)
    for name in ("bias", "decay", "skip"):
        first, count = plan[name]
        plain_rows[first : first + count] = 1.0
    late_grads = [shape((depth, planes, in_rows, width), half)] * blocks
    late_grads.append(shape((depth, planes) + small_half, jnp.float32 if piece >= lanes else half))

    def weights(side):
        return pl.BlockSpec((None, depth * planes, None, in_rows, width), lambda b: (b, 0, side, 0, 0))

    in_whole = in_blocks.reshape(blocks, number, *in_half)
    grad_tokens, in_branch_sum, small_sum, norms = compute_call(
        functools.partial(back_kernel, plan, dims),
        "back",
        blocks,
        [scalars, whole, whole, whole, packed, whole, tall, tall, tall, tall, tall, whole]
        + [weights(0), weights(1), thin(rank), thin(1), thin(size), thin(1), whole, whole],
        [whole] * 4,
        [
            shape((rows, model), half),
            shape((in_rows, inner)),
            shape(small_half),
            shape((2, 8, lanes)),
        ],
        [
            offset_buf,
            pltpu.VMEM((rows + 8, width), jnp.float32),
            pltpu.VMEM((rows, width), half),
            pltpu.VMEM((rows, model), jnp.float32),
            pltpu.VMEM((plan["rows"], width), jnp.float32),
            pltpu.VMEM((blocks,) + late_grads[0].shape, half),
            pltpu.VMEM(late_grads[-1].shape, late_grads[-1].dtype),
            pltpu.VMEM((blocks, in_rows, width), jnp.float32),
            pltpu.VMEM(small_half, jnp.float32),
        ]
        + Reduce.rooms(dims, late_grads)
        + Reduce.sems(blocks + 1, dims)
        + norm_rooms(dims),
        8 * rows * model * inner,
        (
            seq_lengths,
            tokens,
            grad_low,
            gain_value,
            small,
            flat,
            branch,
            signal,
            slope,
            signal_grad,
            gate_grad,
            flipped,
            in_whole,
            in_whole,
            grad_stepw,
            grad_bias,
            grad_decaylog,
            grad_skip,
            jnp.asarray(plain_rows.reshape(small_half)),
            early_squares,
        ),
        collective_id=1,
    )

    names = ("gain", "taps", "shift", "select", "step", "bias", "decay", "skip")
    own = (norm_gain, conv_weight, conv_bias, select_proj, step_proj, step_bias, decay_log, skip_scale)
    in_grad, out_grad, gain_grad, *small_grads, decay_sq, plain_sq = pl.pallas_call(
        functools.partial(finish_kernel, plan, names),
        in_specs=[whole] * 5,
        out_specs=[whole] * (2 + len(names)) + [scalars] * 2,
        out_shape=[shape(in_proj.shape), shape(out_proj.shape)]
        + [shape(array.shape) for array in own]
        + [shape((1, 1))] * 2,
        name="finish",
    )(in_branch_sum, in_gate_sum, out_sum, small_sum.reshape(plan["rows"], piece), norms)
    return (
        output,
        grad_tokens,
        gain_grad,
        in_grad,
        *small_grads,
        out_grad,
        decay_sq[0, 0],
        plain_sq[0, 0],
    )


def solution(mesh):
    placed = (
        P(("wide", "narrow"), None),
        P(("wide", "narrow"), None),
        P(("wide", "narrow")),
        P(("wide", "narrow"), None),
        P("narrow"),
        P("narrow", None),
        P(None, "narrow"),
        P("narrow"),
        P(None, "narrow"),
        P(None, "narrow"),
        P("narrow"),
        P(None, "narrow"),
        P("narrow"),
        P("narrow", None),
    )
    return jax.shard_map(
        functools.partial(per_device, grid_of(mesh)),
        mesh=mesh,
        in_specs=placed,
        out_specs=(
            P(("wide", "narrow"), None),
            P(("wide", "narrow"), None),
            P("narrow"),
            P("narrow", None),
            P(None, "narrow"),
            P("narrow"),
            P(None, "narrow"),
            P(None, "narrow"),
            P("narrow"),
            P(None, "narrow"),
            P("narrow"),
            P("narrow", None),
            P(),
            P(),
        ),
        check_vma=False,
    )
```

```python
import functools
import math

import jax
import jax.numpy as jnp
import numpy as np
from jax import lax
from jax.experimental import pallas as pl
from jax.experimental.pallas import tpu as pltpu
from jax.sharding import PartitionSpec as P

epsilon = 1e-05
chunk = 8
lanes = 128
log2e = math.log2(math.e)
ln2 = math.log(2.0)
far = 1e30


def contract(left, right, left_dim, right_dim):
    return lax.dot_general(
        left, right, (((left_dim,), (right_dim,)), ((), ())), preferred_element_type=jnp.float32
    )


def row_loop(rows, group, body, initial):
    def some(index, carry):
        return body(index, pl.ds(pl.multiple_of(index * group, group), group), carry)

    return lax.fori_loop(0, rows // group, some, initial)


def cut(tile):
    return pl.ds(tile * lanes, lanes)


def sigmoid(values):
    return 0.5 * jnp.tanh(0.5 * values) + 0.5


def softplus(values):
    small = jnp.exp(-jnp.abs(values))
    series = small * (1.0 - small * (0.5 - small * (1.0 / 3.0 - 0.25 * small)))
    return jnp.maximum(values, 0.0) + jnp.where(small < 0.03, series, jnp.log(1.0 + small))


def slope_of(step):
    series = step * (1.0 - step * (0.5 - step * (1.0 / 6.0 - step * (1.0 / 24.0))))
    return jnp.where(step < 0.03, series, 1.0 - jnp.exp(-step))


def fill_offsets(lengths_ref, offset_buf, rows):
    place = lax.broadcasted_iota(jnp.int32, offset_buf.shape, 0)
    start = jnp.zeros(offset_buf.shape, jnp.int32)
    ahead = jnp.int32(0)
    for index in range(lengths_ref.shape[1] - 1):
        ahead = ahead + lengths_ref[0, index]
        start = jnp.where(place >= ahead, ahead, start)
    offset_buf[...] = jnp.where(place < rows, place - start, 0)


def small_rows(small_ref, first, count):
    base = first // 16 * 16
    tall = -(-(first + count - base) // 16) * 16
    return small_ref[base : base + tall, :].astype(jnp.float32)[first - base : first - base + count]


def eight(values):
    total = values[:8]
    for row in range(8, values.shape[0], 8):
        total = total + values[row : row + 8]
    return total


def conv_rows(index, at, group, tile, branch_ref, offset_buf, taps, shift):
    count = taps.shape[0]
    here = slice(tile * lanes, (tile + 1) * lanes)
    current = branch_ref[at, cut(tile)]
    before = branch_ref[pl.ds(pl.multiple_of(jnp.maximum(index * group - 8, 0), 8), 8), cut(tile)]
    both = jnp.concatenate([before, current], axis=0)
    offsets = offset_buf[at, :]
    summed = shift[:, here] + taps[count - 1 : count, here] * current
    for tap in range(count - 1):
        lag = count - 1 - tap
        read = jnp.where(offsets >= lag, pltpu.roll(both, lag, 0)[8:], 0.0)
        summed = summed + taps[tap : tap + 1, here] * read
    return summed


def rows_of(blocks):
    return as_matrix(blocks[...][None])


def as_matrix(blocks):
    columns = blocks.shape[3]
    if blocks.shape[2] % 16:
        return blocks.astype(jnp.float32).reshape(-1, columns).astype(blocks.dtype)
    return blocks.reshape(-1, columns)


def front_kernel(
    plan,
    dims,
    names,
    lengths_ref,
    tokens_ref,
    cotangent_ref,
    mask_ref,
    *refs,
):
    smalls, in_ref, refs = refs[: len(names)], refs[len(names)], refs[len(names) + 1 :]
    branch_ref, gate_ref, signal_ref, slope_ref, projected_ref, flipped_ref, low_ref = refs[:7]
    write_pair, read_pair, small_out, gain_ref, whole_ref = refs[7:12]
    normed_buf, offset_buf, pack_buf, own_small, own_in, land_small, land_in, store_sem = refs[12:20]
    rows = tokens_ref.shape[0]
    width = branch_ref.shape[1]
    block = pl.program_id(0)
    last = whole_ref.shape[0]
    gather = Gather(
        dims,
        [own_small] + [own_in.at[index] for index in range(last)],
        [land_small] + [land_in.at[index] for index in range(last)],
        refs[20:],
    )

    def stored(index):
        return pltpu.make_async_copy(land_in.at[index], whole_ref.at[index], store_sem.at[index])

    @pl.when(block == 0)
    def _():
        pack_buf[...] = jnp.zeros_like(pack_buf)
        for name, ref in zip(names, smalls):
            first, tall = plan[name]
            pack_buf[first : first + tall, : ref.shape[1]] = ref[...]
        tall = pack_buf.shape[0] // 2
        for side in range(2):
            own_small[side] = pack_buf[side * tall : (side + 1) * tall, :].astype(own_small.dtype)
            for index in range(last):
                first = (side * last + index) * width
                own_in[index, side] = in_ref[:, first : first + width].astype(own_in.dtype)
        Place(dims).greet()
        for index in range(last + 1):
            gather.start(index)
        fill_offsets(lengths_ref, offset_buf, rows)
        down = lax.broadcasted_iota(jnp.int32, (rows, rows), 0)
        along = lax.broadcasted_iota(jnp.int32, (rows, rows), 1)
        diagonal = jnp.where(down == along, mask_ref[...].astype(jnp.float32), 0.0).astype(low_ref.dtype)
        low_ref[...] = jnp.dot(
            diagonal, cotangent_ref[...], preferred_element_type=jnp.float32
        ).astype(low_ref.dtype)
        projected_ref[...] = jnp.zeros_like(projected_ref)
        for which, number in ((0, 1), (1, 1), (0, 2), (1, 2), (2, 1), (0, 3)):
            gather.leg(which, number)
        gather.arrive(0)
        share = land_small.shape[4]
        gains = gain_ref.shape[1] // (land_small.shape[0] * land_small.shape[1])
        gain_row = plan["gain"][0]
        for z in range(land_small.shape[0]):
            for plane in range(land_small.shape[1]):
                owner = z * land_small.shape[1] + plane
                for side in range(2):
                    small_out[side * tall : (side + 1) * tall, owner * share : (owner + 1) * share] = land_small[
                        z, plane, side
                    ]
                side, row = gain_row // tall, gain_row % tall
                base = row // 16 * 16
                some = land_small[z, plane, side, base : base + 16, :].astype(jnp.float32)
                gain_ref[:, owner * gains : (owner + 1) * gains] = some[row - base : row - base + 1, :gains]

        def norm(index, at, carry):
            residual = tokens_ref[at, :].astype(jnp.float32)
            scale = lax.rsqrt(jnp.mean(residual * residual, axis=1, keepdims=True) + epsilon)
            normed_buf[at, :] = (residual * scale * gain_ref[...]).astype(normed_buf.dtype)
            return carry

        row_loop(rows, 16, norm, 0)
        flipped_ref[...] = normed_buf[...].T
        for which, number in ((2, 2), (1, 3), (3, 1)):
            gather.leg(which, number)

    def move_on(plan_of_moves):
        for moment, legs in plan_of_moves:

            @pl.when(block == moment)
            def _(legs=legs):
                for which, number in legs:
                    gather.leg(which, number)

    for index in range(last):

        @pl.when(block == index)
        def _(index=index):
            gather.arrive(index + 1)
            stored(index).start()

    branch_w = as_matrix(land_in[block, :, :, 0])
    branch_ref[...] = jnp.dot(normed_buf[...], branch_w, preferred_element_type=jnp.float32)
    gate_w = as_matrix(land_in[block, :, :, 1])
    move_on(((0, ((4, 1), (2, 3))), (1, ((4, 2), (3, 3))), (2, ((4, 3),))))
    gate_ref[...] = jnp.dot(normed_buf[...], gate_w, preferred_element_type=jnp.float32)
    small_ref = small_out.at[:, pl.ds(pl.multiple_of(block * width, width), width)]
    taps = small_rows(small_ref, *plan["taps"])
    shift = small_rows(small_ref, *plan["shift"])

    def some(index, at, carry):
        for tile in range(width // lanes):
            summed = conv_rows(index, at, 32, tile, branch_ref, offset_buf, taps, shift)
            sigma = sigmoid(summed)
            active = summed * sigma
            signal_ref[at, cut(tile)] = active.astype(signal_ref.dtype)
            slope_ref[at, cut(tile)] = sigma + active * (1.0 - sigma)
        return carry

    row_loop(rows, 32, some, 0)
    move_on(((0, ((3, 2),)),))
    projected_ref[...] += contract(signal_ref[...], small_ref[:lanes, :], 1, 1)

    @pl.when(block == pl.num_programs(0) - 1)
    def _():
        high, low = high_low(projected_ref[...])
        own = own_tokens(rows)
        rank = plan["step"][1]
        size = plan["decay"][1]
        entry = lax.broadcasted_iota(jnp.int32, (lanes, lanes), 0)
        lane = lax.rem(lax.broadcasted_iota(jnp.int32, (lanes, lanes), 1), size)
        for first, pair in ((rank, write_pair), (rank + size, read_pair)):
            spread = (entry == lane + first).astype(jnp.bfloat16)
            parts = [
                (jnp.dot(part.astype(jnp.bfloat16), spread, preferred_element_type=jnp.float32) * own).reshape(
                    rows // chunk, chunk, lanes
                )
                for part in (high, low)
            ]
            pair[...] = jnp.concatenate(parts, axis=1).astype(pair.dtype)
        for index in range(last + 1):
            gather.drain(index)
        for index in range(last):
            stored(index).wait()


def high_low(values):
    high = values.astype(jnp.bfloat16).astype(jnp.float32)
    return high, values - high


def own_tokens(rows):
    token = lax.rem(lax.broadcasted_iota(jnp.int32, (rows, lanes), 0), chunk)
    return (token == lax.div(lax.broadcasted_iota(jnp.int32, (rows, lanes), 1), lanes // chunk)).astype(
        jnp.float32
    )


def spread_all(pairs, target):
    some = 8

    def spread(index, carry):
        rows = jnp.concatenate([pairs[index * some + number] for number in range(some)], axis=1)
        wide = contract(rows, jnp.ones((rows.shape[0], lanes), rows.dtype), 0, 0)
        target[pl.ds(index * some * chunk, some * chunk)] = wide.reshape(some * chunk, -1, lanes)
        return carry

    lax.fori_loop(0, pairs.shape[0] // some, spread, 0)


def folded(buffer, tile):
    total = buffer[tile, pl.ds(0, chunk, stride=chunk), :]
    for row in range(1, chunk):
        total = total + buffer[tile, pl.ds(row, chunk, stride=chunk), :]
    return total


def forward_kernel(
    plan,
    dims,
    lengths_ref,
    projected_ref,
    small_ref,
    signal_ref,
    write_pair,
    read_pair,
    own_ref,
    states_ref,
    step_ref,
    core_ref,
    begin_ref,
    whole_ref,
    offset_buf,
    pre_buf,
    decay_step,
    flows,
    write_wide,
    read_wide,
    fold_buf,
    held_buf,
    low_buf,
    *sems,
):
    rows, width = pre_buf.shape
    size = plan["decay"][1]
    half_size = size // 2
    tiles = width // lanes
    chunks = rows // chunk
    rank = plan["step"][1]
    group = pl.program_id(1)
    groups = pl.num_programs(1)
    moment = pl.program_id(0) * groups + group
    moments = pl.num_programs(0) * groups
    gather = Gather(dims, [low_buf], [whole_ref], sems)

    @pl.when(moment == 0)
    def _():
        low_buf[...] = own_ref[...].astype(low_buf.dtype)
        Place(dims).greet()
        gather.start(0)
        fill_offsets(lengths_ref, offset_buf, offset_buf.shape[0] - 8)
        spread_all(write_pair, write_wide)
        spread_all(read_pair, read_wide)

    for number, when in ((1, 2), (2, 4), (3, 6)):

        @pl.when(moment == when)
        def _(number=number):
            gather.leg(0, number)

    @pl.when(group == 0)
    def _():
        held_buf[...] = jnp.zeros_like(held_buf)

    begin_ref[0] = held_buf[...]
    pre_buf[...] = jnp.dot(
        projected_ref[:, :rank].astype(small_ref.dtype),
        small_ref[pl.ds(plan["step"][0], rank), :],
        preferred_element_type=jnp.float32,
    )
    bias = small_rows(small_ref, *plan["bias"])

    def before(index, at, carry):
        spot = pl.ds(pl.multiple_of(index * 4, 4), 4)
        inside = offset_buf[pl.ds(pl.multiple_of(group * rows + index * 32, 32), 32), :] > 0
        for tile in range(tiles):
            step = softplus(pre_buf[at, cut(tile)] + bias[:, tile * lanes : (tile + 1) * lanes])
            step_ref[spot, :, cut(tile)] = step.reshape(4, chunk, lanes)
            decay_step[spot, :, cut(tile)] = jnp.where(inside, step, far).reshape(4, chunk, lanes)
            flow = step * signal_ref[at, cut(tile)].astype(jnp.float32)
            flows[spot, :, cut(tile)] = flow.reshape(4, chunk, lanes)
        return carry

    row_loop(rows, 4 * chunk, before, 0)
    rates = -jnp.exp(small_rows(small_ref, *plan["decay"])) * log2e
    rates = [rates[:, tile * lanes : (tile + 1) * lanes] for tile in range(tiles)]

    def forward(index, held):
        held = list(held)
        for place in range(chunk):
            now = index * chunk + place
            write_now = write_wide[group * rows + now]
            read_now = read_wide[group * rows + now]
            for tile in range(tiles):
                decay = jnp.exp2(rates[tile] * decay_step[index, pl.ds(place, 1), cut(tile)])
                fresh = decay * held[tile] + write_now * flows[index, pl.ds(place, 1), cut(tile)]
                held[tile] = fresh
                states_ref[now, :, cut(tile)] = fresh
                product = read_now * fresh
                fold_buf[tile, pl.ds(place * chunk, chunk), :] = product[:half_size] + product[half_size:]
        for tile in range(tiles):
            core_ref[index, :, cut(tile)] = folded(fold_buf, tile)
        return tuple(held)

    held = tuple(held_buf[:, cut(tile)] for tile in range(tiles))
    held = lax.fori_loop(0, chunks, forward, held)
    for tile in range(tiles):
        held_buf[:, cut(tile)] = held[tile]

    @pl.when(moment == moments - 1)
    def _():
        gather.arrive(0)
        gather.drain(0)


def middle_kernel(
    plan,
    core_ref,
    small_ref,
    signal_ref,
    gate_ref,
    low_ref,
    out_w,
    flipped_ref,
    tokens_ref,
    core_grad_ref,
    gate_grad_ref,
    skip_grad_ref,
    out_grad_ref,
    in_grad_ref,
    output_ref,
    pre_buf,
    gated_buf,
    total,
):
    rows, width = pre_buf.shape
    tiles = width // lanes
    block = pl.program_id(0)
    pre_buf[...] = contract(low_ref[...], out_w[...], 1, 1)
    skip = small_rows(small_ref, *plan["skip"])

    def after(index, at, carry):
        spot = pl.ds(pl.multiple_of(index * 4, 4), 4)
        sums = []
        for tile in range(tiles):
            signal = signal_ref[at, cut(tile)].astype(jnp.float32)
            core = core_ref[spot, :, cut(tile)].reshape(4 * chunk, lanes)
            core = core + skip[:, tile * lanes : (tile + 1) * lanes] * signal
            gate = gate_ref[at, cut(tile)]
            sigma = sigmoid(gate)
            active = gate * sigma
            gated_buf[at, cut(tile)] = (core * active).astype(gated_buf.dtype)
            grad_gated = pre_buf[at, cut(tile)]
            grad_core = grad_gated * active
            core_grad_ref[spot, :, cut(tile)] = grad_core.reshape(4, chunk, lanes)
            slope = sigma + active * (1.0 - sigma)
            gate_grad_ref[at, cut(tile)] = (grad_gated * core * slope).astype(gate_grad_ref.dtype)
            sums.append(carry[tile] + eight(grad_core * signal))
        return tuple(sums)

    zero_rows = jnp.zeros((8, lanes), jnp.float32)
    skips = row_loop(rows, 4 * chunk, after, (zero_rows,) * tiles)
    for tile in range(tiles):
        skip_grad_ref[:, cut(tile)] = jnp.sum(skips[tile], axis=0, keepdims=True)
    out_grad_ref[...] = contract(gated_buf[...], low_ref[...], 0, 0).astype(out_grad_ref.dtype)
    in_grad_ref[...] = jnp.dot(
        flipped_ref[...], gate_grad_ref[...], preferred_element_type=jnp.float32
    ).astype(in_grad_ref.dtype)
    piece = jnp.dot(gated_buf[...], out_w[...], preferred_element_type=jnp.float32)

    @pl.when(block == 0)
    def _():
        total[...] = piece

    @pl.when(block > 0)
    def _():
        total[...] += piece

    @pl.when(block == pl.num_programs(0) - 1)
    def _():
        output_ref[...] = (tokens_ref[...].astype(jnp.float32) + total[...]).astype(output_ref.dtype)


def backward_kernel(
    plan,
    dims,
    lengths_ref,
    projected_ref,
    small_ref,
    signal_ref,
    write_pair,
    read_pair,
    step_ref,
    core_grad_ref,
    states_ref,
    begin_ref,
    out_grad_ref,
    in_grad_ref,
    signal_grad_ref,
    step_w_grad_ref,
    bias_grad_ref,
    decay_grad_ref,
    flat_ref,
    out_sum_ref,
    in_sum_ref,
    square_ref,
    offset_buf,
    decay_step,
    flows,
    write_wide,
    read_wide,
    first_buf,
    second_buf,
    through_buf,
    scaled_buf,
    low_buf,
    incoming_buf,
    rank_buf,
    write_buf,
    read_buf,
    *parts,
):
    rows, width = low_buf.shape
    rank = plan["step"][1]
    size = plan["decay"][1]
    half_size = size // 2
    tiles = width // lanes
    chunks = rows // chunk
    block = pl.program_id(0)
    turn = pl.program_id(1)
    groups = pl.num_programs(1)
    group = groups - 1 - turn
    moment = block * groups + turn
    moments = pl.num_programs(0) * groups
    reduce = Reduce(
        dims,
        [out_grad_ref, in_grad_ref],
        parts[2:12],
        parts[12:],
        parts[:2],
        False,
    )

    @pl.when(moment == 0)
    def _():
        Place(dims).greet()
        for which in range(2):
            reduce.start(which)
        fill_offsets(lengths_ref, offset_buf, offset_buf.shape[0] - 8)
        spread_all(write_pair, write_wide)
        spread_all(read_pair, read_wide)
        write_buf[...] = jnp.zeros_like(write_buf)
        read_buf[...] = jnp.zeros_like(read_buf)
        rank_buf[...] = jnp.zeros_like(rank_buf)

    for number, when in ((1, 1), (2, 4), (3, 6)):

        @pl.when(moment == when)
        def _(number=number):
            for which in range(2):
                reduce.leg(which, number)

    @pl.when(turn == 0)
    def _():
        incoming_buf[...] = jnp.zeros_like(incoming_buf)
        decay_grad_ref[...] = jnp.zeros_like(decay_grad_ref)
        bias_grad_ref[...] = jnp.zeros_like(bias_grad_ref)
        step_w_grad_ref[...] = jnp.zeros_like(step_w_grad_ref)

    def before(index, at, carry):
        spot = pl.ds(pl.multiple_of(index * 4, 4), 4)
        offsets = offset_buf[pl.ds(pl.multiple_of(group * rows + index * 32, 32), 32), :]
        inside = (offsets > 0).reshape(4, chunk, lanes)
        for tile in range(tiles):
            step = step_ref[spot, :, cut(tile)]
            decay_step[spot, :, cut(tile)] = jnp.where(inside, step, far)
            signal = signal_ref[at, cut(tile)].astype(jnp.float32).reshape(4, chunk, lanes)
            flows[spot, :, cut(tile)] = step * signal
        return carry

    row_loop(rows, 4 * chunk, before, 0)
    rates = -jnp.exp(small_rows(small_ref, *plan["decay"])) * log2e
    rates = [rates[:, tile * lanes : (tile + 1) * lanes] for tile in range(tiles)]

    def backward(position, carried):
        index = chunks - 1 - position
        incoming, decay_sums = list(carried[0]), list(carried[1])
        for place in range(chunk - 1, -1, -1):
            now = index * chunk + place
            token = group * rows + now
            write_now = write_wide[token]
            read_now = read_wide[token]
            read_sum = None
            write_sum = None
            for tile in range(tiles):
                step_now = decay_step[index, pl.ds(place, 1), cut(tile)]
                grad_now = core_grad_ref[index, pl.ds(place, 1), cut(tile)]
                if place > 0:
                    earlier = states_ref[now - 1, :, cut(tile)]
                else:
                    earlier = jnp.where(
                        index > 0, states_ref[jnp.maximum(now - 1, 0), :, cut(tile)], begin_ref[0, :, cut(tile)]
                    )
                grad_state = incoming[tile] + read_now * grad_now
                through_read = states_ref[now, :, cut(tile)] * grad_now
                through_write = grad_state * flows[index, pl.ds(place, 1), cut(tile)]
                read_sum = through_read if read_sum is None else read_sum + through_read
                write_sum = through_write if write_sum is None else write_sum + through_write
                passed = grad_state * write_now
                first_buf[tile, pl.ds(place * chunk, chunk), :] = passed[:half_size] + passed[half_size:]
                leaving = jnp.exp2(rates[tile] * step_now) * grad_state
                incoming[tile] = leaving
                weighted = leaving * earlier
                scaled = weighted * rates[tile]
                second_buf[tile, pl.ds(place * chunk, chunk), :] = scaled[:half_size] + scaled[half_size:]
                decay_sums[tile] = decay_sums[tile] + weighted * step_now
            read_buf[token] += read_sum
            write_buf[token] += write_sum
        for tile in range(tiles):
            through_buf[index, :, cut(tile)] = folded(first_buf, tile)
            scaled_buf[index, :, cut(tile)] = folded(second_buf, tile)
        return (tuple(incoming), tuple(decay_sums))

    incoming = tuple(incoming_buf[:, cut(tile)] for tile in range(tiles))
    nothing = (jnp.zeros((size, lanes), jnp.float32),) * tiles
    incoming, decay_sums = lax.fori_loop(0, chunks, backward, (incoming, nothing))
    for tile in range(tiles):
        incoming_buf[:, cut(tile)] = incoming[tile]
        decay_grad_ref[:, cut(tile)] += decay_sums[tile] * rates[tile] * ln2
    skip = small_rows(small_ref, *plan["skip"])

    def after(index, at, carry):
        spot = pl.ds(pl.multiple_of(index * 4, 4), 4)
        sums = []
        for tile in range(tiles):
            signal = signal_ref[at, cut(tile)].astype(jnp.float32)
            step = step_ref[spot, :, cut(tile)].reshape(4 * chunk, lanes)
            through = through_buf[spot, :, cut(tile)].reshape(4 * chunk, lanes)
            scaled = scaled_buf[spot, :, cut(tile)].reshape(4 * chunk, lanes)
            core_grad = core_grad_ref[spot, :, cut(tile)].reshape(4 * chunk, lanes)
            grad_pre = (through * signal + ln2 * scaled) * slope_of(step)
            low_buf[at, cut(tile)] = grad_pre.astype(low_buf.dtype)
            signal_grad_ref[at, cut(tile)] = (
                through * step + skip[:, tile * lanes : (tile + 1) * lanes] * core_grad
            )
            sums.append(carry[tile] + eight(grad_pre))
        return tuple(sums)

    zero_rows = jnp.zeros((8, lanes), jnp.float32)
    sums = row_loop(rows, 4 * chunk, after, (zero_rows,) * tiles)
    for tile in range(tiles):
        bias_grad_ref[:, cut(tile)] += jnp.sum(sums[tile], axis=0, keepdims=True)
    step_w_grad_ref[...] += contract(
        projected_ref[:, :rank].astype(low_buf.dtype), low_buf[...], 0, 0
    )
    step_w = small_ref[pl.ds(plan["step"][0], rank), :]
    step_w = jnp.concatenate([step_w, jnp.zeros((lanes - rank, width), step_w.dtype)], axis=0)
    rank_buf[pl.ds(group * chunks, chunks)] += contract(low_buf[...], step_w, 1, 1).reshape(
        chunks, chunk, lanes
    )

    @pl.when(moment == moments - 1)
    def _():
        square_ref[...] = reduce.finish(0)[0] + reduce.finish(1)[0]
        some = 8
        entry = lax.rem(lax.broadcasted_iota(jnp.int32, (some * chunk * size, lanes), 0), size)
        target = lax.broadcasted_iota(jnp.int32, (some * chunk * size, lanes), 1)
        ones = jnp.ones((lanes, lanes), jnp.bfloat16)

        def lay(index, carry):
            lot = pl.ds(index * some * chunk, some * chunk)
            for number, buffer in enumerate((write_buf, read_buf)):
                high, low = high_low(buffer[lot].reshape(some * chunk * size, lanes))
                summed = jnp.dot(high.astype(jnp.bfloat16), ones, preferred_element_type=jnp.float32)
                summed += jnp.dot(low.astype(jnp.bfloat16), ones, preferred_element_type=jnp.float32)
                summed = jnp.where(target == entry + rank + number * size, summed, 0.0)
                summed = jnp.sum(summed.reshape(some * chunk, size, lanes), axis=1)
                rank_buf[pl.ds(index * some, some)] += summed.reshape(some, chunk, lanes)
            return carry

        lax.fori_loop(0, rank_buf.shape[0] // some, lay, 0)
        flat_ref[...] = rank_buf[...].reshape(flat_ref.shape).astype(flat_ref.dtype)
        for which in range(2):
            reduce.settle(which)
        out_sum_ref[...] = parts[0][...]
        in_sum_ref[...] = parts[1][...]


def back_kernel(
    plan,
    dims,
    lengths_ref,
    tokens_ref,
    low_ref,
    gain_ref,
    small_ref,
    flat_ref,
    branch_ref,
    signal_ref,
    slope_ref,
    signal_grad_ref,
    gate_grad_ref,
    flipped_ref,
    branch_w,
    gate_w,
    step_w_grad_ref,
    bias_grad_ref,
    decay_grad_ref,
    skip_grad_ref,
    plain_ref,
    earlier_ref,
    tokens_grad_ref,
    in_sum_ref,
    small_sum_ref,
    late_sum_ref,
    norm_ref,
    offset_buf,
    conv_buf,
    mixed_buf,
    total,
    in_stage,
    small_stage,
    late_stage,
    late_land,
    late_cores,
    norm_own,
    norm_land,
    norm_cores,
    in_result,
    small_result,
    direct_send,
    direct_recv,
    *parts,
):
    rows = tokens_ref.shape[0]
    width = branch_ref.shape[1]
    tiles = width // lanes
    block = pl.program_id(0)
    last = in_stage.shape[0]
    count = last + 1
    reduce = Reduce(
        dims,
        [small_stage] + [in_stage.at[index] for index in range(last)],
        parts[: 5 * count],
        parts[5 * count :],
        [small_result] + [in_result.at[index] for index in range(last)],
        True,
    )
    share = small_stage.shape[4]
    half_rows = small_stage.shape[3]
    planes = small_stage.shape[1]
    owners = small_stage.shape[0] * planes

    @pl.when(block == 0)
    def _():
        Place(dims).greet(everyone=True)
        select_grad = contract(flat_ref[...], signal_ref[...], 0, 0)
        step_first, step_tall = plan["step"]
        filler = jnp.zeros((2 * half_rows - step_first - step_tall, select_grad.shape[1]), jnp.float32)
        pieces = {
            "decay": decay_grad_ref[...],
            "bias": bias_grad_ref[...],
            "skip": skip_grad_ref[...],
            "step": step_w_grad_ref[...],
        }
        first = plan["select"][1]
        rows_now = [select_grad[:first]]
        for name in ("decay", "taps", "shift", "bias", "skip", "gain"):
            tall = plan[name][1]
            rows_now.append(
                pieces[name] if name in pieces else jnp.zeros((tall, select_grad.shape[1]), jnp.float32)
            )
            first += tall
        rows_now.append(jnp.zeros((step_first - first, select_grad.shape[1]), jnp.float32))
        rows_now.append(pieces["step"])
        if filler.shape[0]:
            rows_now.append(filler)
        everything = jnp.concatenate(rows_now, axis=0)
        for owner in range(owners):
            for side in range(2):
                small_stage[owner // planes, owner % planes, side] = everything[
                    side * half_rows : (side + 1) * half_rows, owner * share : (owner + 1) * share
                ].astype(small_stage.dtype)
        reduce.start(0)
        fill_offsets(lengths_ref, offset_buf, rows)

    taps = small_rows(small_ref, *plan["taps"])
    taps_count = taps.shape[0]
    conv_buf[pl.ds(0, rows), :] = signal_grad_ref[...] + jnp.dot(
        flat_ref[...], small_ref[:lanes, :], preferred_element_type=jnp.float32
    )
    conv_buf[pl.ds(rows, 8), :] = jnp.zeros((8, width), jnp.float32)

    def through_conv(index, at, carry):
        sums = []
        for tile in range(tiles):
            grad_conv = conv_buf[at, cut(tile)] * slope_ref[at, cut(tile)]
            conv_buf[at, cut(tile)] = grad_conv
            sums.append(carry[tile] + eight(grad_conv))
        return tuple(sums)

    zero_rows = jnp.zeros((8, lanes), jnp.float32)
    shift_sums = row_loop(rows, 32, through_conv, (zero_rows,) * tiles)

    def to_branch(index, at, carry):
        longer = pl.ds(pl.multiple_of(index * 32, 32), 40)
        offsets = offset_buf[longer, :]
        result = []
        for tile in range(tiles):
            here = slice(tile * lanes, (tile + 1) * lanes)
            grads = conv_buf[longer, cut(tile)]
            branch = branch_ref[at, cut(tile)]
            summed = taps[taps_count - 1 : taps_count, here] * grads[:32]
            sums = [None] * taps_count
            sums[taps_count - 1] = carry[tile][taps_count - 1] + eight(branch * grads[:32])
            for tap in range(taps_count - 1):
                lag = taps_count - 1 - tap
                moved = pltpu.roll(jnp.where(offsets >= lag, grads, 0.0), 40 - lag, 0)[:32]
                summed = summed + taps[tap : tap + 1, here] * moved
                sums[tap] = carry[tile][tap] + eight(branch * moved)
            mixed_buf[at, cut(tile)] = summed.astype(mixed_buf.dtype)
            result.append(tuple(sums))
        return tuple(result)

    sums = row_loop(rows, 32, to_branch, ((zero_rows,) * taps_count,) * tiles)
    late = [
        jnp.concatenate(
            [jnp.sum(sums[tile][tap], axis=0, keepdims=True) for tap in range(taps_count)]
            + [jnp.sum(shift_sums[tile], axis=0, keepdims=True)]
            + [jnp.zeros((8 - taps_count - 1, lanes), jnp.float32)],
            axis=0,
        )
        for tile in range(tiles)
    ]
    late = jnp.concatenate(late, axis=1)
    for piece in range(width // share):
        late_stage[block * (width // share) + piece] = late[:, piece * share : (piece + 1) * share]
    in_grad = jnp.dot(flipped_ref[...], mixed_buf[...], preferred_element_type=jnp.float32)
    in_stage[block] = in_grad.reshape(in_stage.shape[1:]).astype(in_stage.dtype)
    for index in range(last):

        @pl.when(block == index)
        def _(index=index):
            reduce.start(index + 1)

    grad_normed_piece = contract(mixed_buf[...], rows_of(branch_w), 1, 1)
    grad_normed_piece += contract(gate_grad_ref[...], rows_of(gate_w), 1, 1)

    @pl.when(block == 0)
    def _():
        total[...] = grad_normed_piece

    @pl.when(block > 0)
    def _():
        total[...] += grad_normed_piece

    for moment, legs in (
        (0, ((0, 1),)),
        (1, ((0, 2), (1, 1))),
        (2, ((0, 3), (1, 2), (2, 1))),
        (3, ((1, 3), (2, 2), (3, 1))),
    ):

        @pl.when(block == moment)
        def _(legs=legs):
            for which, number in legs:
                reduce.leg(which, number)

    @pl.when(block == pl.num_programs(0) - 1)
    def _():
        def finish(index, at, carry):
            residual = tokens_ref[at, :].astype(jnp.float32)
            scale = lax.rsqrt(jnp.mean(residual * residual, axis=1, keepdims=True) + epsilon)
            grad_normed = total[at, :]
            weighted = grad_normed * gain_ref[...]
            inner = jnp.mean(weighted * residual, axis=1, keepdims=True)
            grad_y = low_ref[at, :].astype(jnp.float32)
            result = grad_y + (scale * weighted - residual * (scale * scale * scale) * inner)
            tokens_grad_ref[at, :] = result.astype(tokens_grad_ref.dtype)
            return carry + eight(grad_normed * residual * scale)

        gains = row_loop(rows, 16, finish, jnp.zeros((8, total.shape[1]), jnp.float32))
        gains = jnp.sum(gains, axis=0, keepdims=True)
        place = Place(dims)
        each = gains.shape[1] // owners
        for owner in range(owners):
            late_stage[owner, taps_count + 1 : taps_count + 2, :each] = gains[
                :, owner * each : (owner + 1) * each
            ]
        late_sems = direct_send.at[0], direct_recv.at[0]
        norm_sems = direct_send.at[1], direct_recv.at[1]
        send_to_all(place, lambda target: late_stage.at[target], late_land, *late_sems)
        for which, number in ((4, 1), (3, 2), (2, 3), (4, 2), (3, 3)):
            reduce.leg(which, number)
        late_sum = sum_of_all(place, late_stage[place.me], late_land, *late_sems)
        late_sum = sum_of_cores(place, late_sum, late_cores, direct_send.at[0, 0], direct_recv.at[0, 0])
        late_sum_ref[...] = late_sum
        reduce.leg(4, 3)
        kept = earlier_ref[...] + folded_squares(late_sum * late_sum) * (1 - place.core).astype(jnp.float32)
        more, plain = reduce.finish(0, plain_ref)
        kept = kept + more
        for index in range(1, count):
            kept = kept + reduce.finish(index)[0]
        norm_own[...] = jnp.stack([kept, plain])
        send_to_all(place, lambda target: norm_own, norm_land, *norm_sems)
        norms = sum_of_all(place, norm_own[...], norm_land, *norm_sems)
        norm_ref[...] = sum_of_cores(place, norms, norm_cores, direct_send.at[1, 0], direct_recv.at[1, 0])
        for index in range(count):
            reduce.settle(index)
        for index in range(last):
            in_sum_ref[:, index * width : (index + 1) * width] = in_result[index]
        small_sum_ref[...] = small_result[...]


def finish_kernel(
    plan, names, late, tokens_ref, branch_ref, gate_ref, out_ref, small_ref, late_ref, norm_ref, *outs
):
    middle = branch_ref.shape[1]
    outs[0][:, :middle] = branch_ref[...]
    outs[0][:, middle:] = gate_ref[...]
    outs[1][...] = out_ref[...]
    outs[2][...] = tokens_ref[...]
    for name, target in zip(names, outs[3 : 3 + len(names)]):
        source, (first, count) = (late_ref, late[name]) if name in late else (small_ref, plan[name])
        if len(target.shape) == 1:
            target[...] = source[first, : target.shape[0]]
        else:
            target[...] = source[first : first + count, :]
    for index in range(2):
        outs[3 + len(names) + index][0, 0] = jnp.sum(norm_ref[index])


def shape(dims, kind=jnp.float32):
    return jax.ShapeDtypeStruct(dims, kind)


def compute_call(
    kernel, name, blocks, in_specs, out_specs, out_shape, scratch, flops, operands, collective_id=None
):
    return pl.pallas_call(
        kernel,
        grid=blocks if isinstance(blocks, tuple) else (blocks,),
        in_specs=in_specs,
        out_specs=out_specs,
        out_shape=out_shape,
        scratch_shapes=scratch,
        compiler_params=pltpu.CompilerParams(
            dimension_semantics=("arbitrary",) * (len(blocks) if isinstance(blocks, tuple) else 1),
            vmem_limit_bytes=62 * 1024 * 1024,
            collective_id=collective_id,
            has_side_effects=collective_id is not None,
        ),
        cost_estimate=pl.CostEstimate(flops=flops, bytes_accessed=40 << 20, transcendentals=0),
        name=name,
    )(*operands)


class Place:
    def __init__(self, dims, swapped=False):
        depth, tall, wide = dims
        self.dims = dims
        self.core = lax.axis_index("wide")
        self.me = lax.axis_index("narrow")
        self.across = lax.rem(self.me, wide)
        self.up = lax.rem(lax.div(self.me, wide), tall)
        self.deep = lax.div(self.me, wide * tall)
        side = 1 - self.core if swapped else self.core
        turn = side if tall == wide else 0
        self.second = (1 + turn * (wide - 1), self.across + turn * (self.up - self.across), wide)
        self.third = (wide - turn * (wide - 1), self.up + turn * (self.across - self.up), tall)
        self.spans = (depth, wide, tall)
        self.other = {"wide": 1 - self.core}

    def level(self, d):
        return lax.rem(self.deep + d, self.spans[0])

    def plane(self, e, f):
        return (
            lax.rem(self.second[1] + e, self.second[2]) * self.second[0]
            + lax.rem(self.third[1] + f, self.third[2]) * self.third[0]
        )

    def plane_behind(self, e, f):
        return self.plane((self.spans[1] - e) % self.spans[1], (self.spans[2] - f) % self.spans[2])

    def at(self, d, e, f):
        return {"narrow": self.level(d) * (self.dims[1] * self.dims[2]) + self.plane(e, f)}

    def greet(self, everyone=False):
        barrier = pltpu.get_barrier_semaphore()
        peers = [self.other]
        if everyone:
            number = self.spans[0] * self.spans[1] * self.spans[2]
            peers += [{"narrow": lax.rem(self.me + hop, number)} for hop in range(1, number)]
        else:
            for axis, size in enumerate(self.spans):
                for hop in range(1, size):
                    move = [0, 0, 0]
                    move[axis] = hop
                    peers.append(self.at(*move))
        for peer in peers:
            pl.semaphore_signal(barrier, inc=1, device_id=peer, device_id_type=pl.DeviceIdType.MESH)
        pl.semaphore_wait(barrier, len(peers))


def columns_of(width, side):
    return pl.ds(pl.multiple_of(side * (width // 2), lanes), width // 2)


def half_shape(block):
    return tuple(block[1:]) if len(block) == 3 else (block[0], block[1] // 2)


def half(view, block, side, lead=0):
    if len(block) == 3:
        return view.at[(slice(None),) * lead + (side,)]
    return view.at[(slice(None),) * (lead + 1) + (columns_of(block[1], side),)]


def remote(source, target, send_sem, recv_sem, device):
    return pltpu.make_async_remote_copy(
        src_ref=source,
        dst_ref=target,
        send_sem=send_sem,
        recv_sem=recv_sem,
        device_id=device,
        device_id_type=pl.DeviceIdType.MESH,
    )


class Gather:
    def __init__(self, dims, own, whole, sems):
        self.dims, self.own, self.whole = dims, own, whole
        self.local_sem, self.send_sem, self.recv_sem = sems

    @staticmethod
    def sems(count, dims):
        copies = dims[0] + 2 * dims[1] * dims[2]
        return [pltpu.SemaphoreType.DMA((count,))] + [pltpu.SemaphoreType.DMA((count, copies))] * 2

    def line(self, which, plane, side):
        return half(self.whole[which].at[:, plane], self.own[which].shape, side, 1)

    def local(self, place, which):
        block = self.own[which].shape
        return pltpu.make_async_copy(
            half(self.own[which], block, place.core),
            half(self.whole[which].at[place.deep, place.plane(0, 0)], block, place.core),
            self.local_sem.at[which],
        )

    def copy(self, which, source, target, index, device):
        return remote(
            source, target, self.send_sem.at[which, index], self.recv_sem.at[which, index], device
        )

    def rise(self, place, which, hop):
        block = self.own[which].shape
        return self.copy(
            which,
            half(self.own[which], block, place.core),
            half(self.whole[which].at[place.deep, place.plane(0, 0)], block, place.core),
            hop,
            place.at(hop, 0, 0),
        )

    def leg_index(self, e, f):
        return self.dims[0] + e * self.dims[1] + f

    def hand_index(self, e, f):
        return self.leg_index(e, f) + self.dims[1] * self.dims[2]

    def onward(self, place, which, e, f):
        line = self.line(which, place.plane_behind(e, f), place.core)
        if f == 0:
            for hop in range(1, place.spans[2]):
                self.copy(which, line, line, self.leg_index(e, hop), place.at(0, 0, hop)).start()
        if f == 0 and e == 0:
            for hop in range(1, place.spans[1]):
                self.copy(which, line, line, self.leg_index(hop, 0), place.at(0, hop, 0)).start()
        self.copy(which, line, line, self.hand_index(e, f), place.other).start()

    def start(self, which):
        place = Place(self.dims)
        for hop in range(1, place.spans[0]):
            self.rise(place, which, hop).start()
        self.local(place, which).start()

    def leg(self, which, number):
        place = Place(self.dims)
        if number == 1:
            self.local(place, which).wait()
            for hop in range(1, place.spans[0]):
                self.rise(place, which, hop).wait_recv()
            self.onward(place, which, 0, 0)
            return
        for e in range(place.spans[1]):
            for f in range(place.spans[2]):
                if (number == 2 and f == 0 and e > 0) or (number == 3 and f > 0):
                    line = self.line(which, place.plane_behind(e, f), place.core)
                    self.copy(which, line, line, self.leg_index(e, f), place.other).wait_recv()
                    self.onward(place, which, e, f)

    def arrive(self, which):
        place, mirror = Place(self.dims), Place(self.dims, swapped=True)
        for e in range(place.spans[1]):
            for f in range(place.spans[2]):
                line = self.line(which, mirror.plane_behind(e, f), 1 - place.core)
                self.copy(which, line, line, self.hand_index(e, f), place.other).wait_recv()

    def drain(self, which):
        place = Place(self.dims)
        for hop in range(1, place.spans[0]):
            self.rise(place, which, hop).wait_send()
        for e in range(place.spans[1]):
            for f in range(place.spans[2]):
                line = self.line(which, place.plane_behind(e, f), place.core)
                if e > 0 or f > 0:
                    self.copy(which, line, line, self.leg_index(e, f), place.other).wait_send()
                self.copy(which, line, line, self.hand_index(e, f), place.other).wait_send()


class Reduce:
    def __init__(self, dims, grads, rooms, sems, results, resident):
        self.dims, self.grads, self.resident = dims, grads, resident
        count = len(grads)
        self.mine, self.swapped, self.third, self.second, self.first = (
            rooms[index * count : (index + 1) * count] for index in range(5)
        )
        self.load_sem, self.swap_send, self.swap_recv, self.send_sem, self.recv_sem = sems[:5]
        self.last_send, self.last_recv = sems[5:]
        self.results = results

    @staticmethod
    def rooms(dims, grads):
        depth, tall, wide = dims
        leads = (
            (tall, wide, depth),
            (depth, tall * wide),
            (tall - 1, wide, depth),
            (wide - 1, depth),
            (depth - 1,),
        )
        return [
            pltpu.VMEM(lead + half_shape(grad.shape[2:]), grad.dtype) for lead in leads for grad in grads
        ]

    @staticmethod
    def sems(count, dims):
        groups = dims[1] * dims[2]
        return (
            [pltpu.SemaphoreType.DMA((count, groups))] * 3
            + [pltpu.SemaphoreType.DMA((count, dims[0] + dims[1] + dims[2]))] * 2
            + [pltpu.SemaphoreType.DMA((count,))] * 2
        )

    def groups(self, place):
        return [
            (e, f)
            for f in range(place.spans[2] - 1, -1, -1)
            for e in range(place.spans[1] - 1, -1, -1)
        ]

    def number(self, e, f):
        return e * self.dims[1] + f

    def block(self, which):
        return self.grads[which].shape[2:]

    def load(self, place, which, e, f):
        return pltpu.make_async_copy(
            half(self.grads[which].at[:, place.plane(e, f)], self.block(which), place.core, 1),
            self.mine[which].at[f, e],
            self.load_sem.at[which, self.number(e, f)],
        )

    def swap(self, place, which, e, f, plane):
        return remote(
            half(self.grads[which].at[:, plane], self.block(which), 1 - place.core, 1),
            self.swapped[which].at[:, plane],
            self.swap_send.at[which, self.number(e, f)],
            self.swap_recv.at[which, self.number(e, f)],
            place.other,
        )

    def hop(self, which, source, target, index, device):
        return remote(
            source, target, self.send_sem.at[which, index], self.recv_sem.at[which, index], device
        )

    def third_hop(self, place, which, f):
        return self.hop(which, self.mine[which].at[f], self.third[which].at[f - 1], f, place.at(0, 0, f))

    def second_hop(self, place, which, e):
        return self.hop(
            which,
            self.mine[which].at[0, e],
            self.second[which].at[e - 1],
            self.dims[1] + e,
            place.at(0, e, 0),
        )

    def first_hop(self, place, which, d):
        return self.hop(
            which,
            self.mine[which].at[0, 0, place.level(d)],
            self.first[which].at[d - 1],
            self.dims[1] + self.dims[2] + d,
            place.at(d, 0, 0),
        )

    def start(self, which):
        place, mirror = Place(self.dims), Place(self.dims, swapped=True)
        for e, f in self.groups(place):
            self.swap(place, which, e, f, mirror.plane(e, f)).start()
            if not self.resident:
                self.load(place, which, e, f).start()

    def parts(self, place, which, e, f, z):
        plane = place.plane(e, f)
        if self.resident:
            found = [half(self.grads[which].at[z, plane], self.block(which), place.core)]
        else:
            found = [self.mine[which].at[f, e, z]]
        found.append(self.swapped[which].at[z, plane])
        if f == 0:
            found += [self.third[which].at[hop - 1, e, z] for hop in range(1, place.spans[2])]
        if f == 0 and e == 0:
            found += [self.second[which].at[hop - 1, z] for hop in range(1, place.spans[1])]
        return found

    def ready(self, place, which, e, f):
        if not self.resident:
            self.load(place, which, e, f).wait()
        self.swap(place, which, e, f, place.plane(e, f)).wait_recv()

    def added(self, parts, store, carry):
        rows = parts[0].shape[0]
        group = min(rows, 16)

        def some(index, carry):
            at_rows = pl.ds(pl.multiple_of(index * group, group), group)
            total = parts[0][at_rows, :].astype(jnp.float32)
            for part in parts[1:]:
                total = total + part[at_rows, :].astype(jnp.float32)
            return store(at_rows, total, carry)

        return lax.fori_loop(0, rows // group, some, carry)

    def sum_into(self, place, which, e, f, z):
        target = self.mine[which].at[f, e, z]

        def keep(at_rows, total, carry):
            target[at_rows, :] = total.astype(target.dtype)
            return carry

        self.added(self.parts(place, which, e, f, z), keep, 0)

    def leg(self, which, number):
        place = Place(self.dims)
        depth, span_e, span_f = place.spans
        if number == 1:
            for f in range(span_f - 1, 0, -1):
                for e in range(span_e - 1, -1, -1):
                    self.ready(place, which, e, f)
                    for z in range(depth):
                        self.sum_into(place, which, e, f, z)
                self.third_hop(place, which, f).start()
        elif number == 2:
            for f in range(1, span_f):
                self.third_hop(place, which, f).wait_recv()
            for e in range(span_e - 1, 0, -1):
                self.ready(place, which, e, 0)
                for z in range(depth):
                    self.sum_into(place, which, e, 0, z)
                self.second_hop(place, which, e).start()
        else:
            self.ready(place, which, 0, 0)
            if span_e == 1:
                for f in range(1, span_f):
                    self.third_hop(place, which, f).wait_recv()
            for e in range(1, span_e):
                self.second_hop(place, which, e).wait_recv()
            for d in range(1, depth):
                self.sum_into(place, which, 0, 0, place.level(d))
                self.first_hop(place, which, d).start()

    def result(self, which, side):
        return half(self.results[which], self.block(which), side)

    def last(self, place, which, side):
        share = self.result(which, side)
        return remote(share, share, self.last_send.at[which], self.last_recv.at[which], place.other)

    def finish(self, which, marks=None):
        place = Place(self.dims)
        parts = self.parts(place, which, 0, 0, place.deep)
        for d in range(1, place.spans[0]):
            self.first_hop(place, which, d).wait_recv()
            parts.append(self.first[which].at[d - 1])
        share = self.result(which, place.core)

        def store(at_rows, total, carry):
            share[at_rows, :] = total
            kept, plain = carry
            squared = total * total
            if marks is not None:
                marked = squared * marks[place.core, at_rows, :]
                plain = plain + folded_squares(marked)
                squared = squared - marked
            return (kept + folded_squares(squared), plain)

        squares = self.added(parts, store, (jnp.zeros((8, lanes), jnp.float32),) * 2)
        self.last(place, which, place.core).start()
        return squares

    def settle(self, which):
        place, mirror = Place(self.dims), Place(self.dims, swapped=True)
        last = self.last(place, which, 1 - place.core)
        last.wait_recv()
        last.wait_send()
        for e, f in self.groups(place):
            self.swap(place, which, e, f, mirror.plane(e, f)).wait_send()
        for f in range(1, place.spans[2]):
            self.third_hop(place, which, f).wait_send()
        for e in range(1, place.spans[1]):
            self.second_hop(place, which, e).wait_send()
        for d in range(1, place.spans[0]):
            self.first_hop(place, which, d).wait_send()


def folded_squares(values):
    total = None
    if values.shape[1] < lanes:
        first = lax.broadcasted_iota(jnp.int32, (values.shape[0], lanes), 1) == 0
        values = jnp.where(first, jnp.sum(values, axis=1, keepdims=True), 0.0)
    for row in range(0, values.shape[0], 8):
        for column in range(0, values.shape[1], lanes):
            piece = values[row : row + 8, column : column + lanes]
            total = piece if total is None else total + piece
    return total


def send_to_all(place, source, landing, send_sem, recv_sem):
    number = landing.shape[0]
    for hop in range(1, number):
        target = lax.rem(place.me + hop, number)
        remote(
            source(target), landing.at[place.me], send_sem.at[hop], recv_sem.at[hop], {"narrow": target}
        ).start()


def sum_of_all(place, own, landing, send_sem, recv_sem):
    number = landing.shape[0]
    landing[place.me] = own
    for hop in range(1, number):
        came = landing.at[lax.rem(place.me + number - hop, number)]
        copy = remote(came, came, send_sem.at[hop], recv_sem.at[hop], place.other)
        copy.wait_recv()
        copy.wait_send()
    total = landing[0]
    for spot in range(1, number):
        total = total + landing[spot]
    return total


def sum_of_cores(place, own, landing, send_sem, recv_sem):
    landing[place.core] = own
    copy = remote(landing.at[place.core], landing.at[place.core], send_sem, recv_sem, place.other)
    copy.start()
    copy.wait()
    return landing[0] + landing[1]


def grid_of(mesh):
    number = mesh.shape["narrow"]
    places = [getattr(device, "coords", None) for device in mesh.devices[0]]
    if all(place is not None for place in places):
        sizes = [len({place[axis] for place in places}) for axis in (2, 1, 0)]
        if sizes[0] * sizes[1] * sizes[2] == number:
            return tuple(sizes)
    side = round((number / 2) ** (1 / 3))
    return (2 * side, side, side) if 2 * side**3 == number else (number, 1, 1)


def plan_of(select_rows, state_size, tap_count, step_rows):
    plan, first = {}, 0
    for name, tall in (
        ("select", select_rows),
        ("decay", state_size),
        ("taps", tap_count),
        ("shift", 1),
        ("bias", 1),
        ("skip", 1),
        ("gain", 1),
    ):
        plan[name] = (first, tall)
        first += tall
    plan["step"] = (lanes, step_rows)
    plan["rows"] = -(-(lanes + step_rows) // 32) * 32
    return plan


def per_device(
    dims,
    tokens,
    cotangent,
    loss_mask,
    seq_lengths,
    norm_gain,
    in_proj,
    conv_weight,
    conv_bias,
    select_proj,
    step_proj,
    step_bias,
    decay_log,
    skip_scale,
    out_proj,
):
    half = jnp.bfloat16
    piece = skip_scale.shape[0]
    gain_piece = norm_gain.shape[0]
    rank, size = step_proj.shape[0], decay_log.shape[0]
    plan = plan_of(select_proj.shape[0], size, conv_weight.shape[0], rank)
    smalls = {
        "select": select_proj,
        "decay": decay_log,
        "taps": conv_weight,
        "shift": conv_bias[None],
        "bias": step_bias[None],
        "skip": skip_scale[None],
        "gain": norm_gain[None],
        "step": step_proj,
    }
    depth, planes = dims[0], dims[1] * dims[2]
    number = depth * planes
    in_rows = in_proj.shape[0]
    rows, model = tokens.shape
    inner = piece * number
    width = 4 * lanes
    blocks = inner // width
    chunks = rows // chunk
    mask_row = loss_mask[None]

    whole = pl.BlockSpec(memory_space=pltpu.VMEM)
    tall = pl.BlockSpec((rows, width), lambda b: (0, b))
    deep = pl.BlockSpec((chunks, chunk, width), lambda b: (0, 0, b))
    lead = pl.BlockSpec((rows, size, width), lambda b: (0, 0, b))
    first_w = pl.BlockSpec((model, width), lambda b: (0, b))
    second_w = pl.BlockSpec((model, width), lambda b: (0, b + blocks))
    out_w = pl.BlockSpec((width, model), lambda b: (b, 0))

    def thin(height):
        return pl.BlockSpec((height, width), lambda b: (0, b))

    def fixed(*dims_of):
        return pl.BlockSpec(dims_of, lambda b: (0,) * len(dims_of))

    scalars = pl.BlockSpec(memory_space=pltpu.SMEM)
    offset_buf = pltpu.VMEM((rows + 8, lanes), jnp.int32)
    packed = thin(plan["rows"])

    pair = (chunks, 2 * chunk, lanes)
    pair = (chunks, 2 * chunk, lanes)
    anywhere = pl.BlockSpec(memory_space=pl.ANY)
    small_half = (2, plan["rows"] // 2, piece)
    in_half = (2, in_rows, width)
    (
        branch,
        gate_pre,
        signal,
        slope,
        projected,
        flipped,
        grad_low,
        write_pair,
        read_pair,
        small,
        gain_value,
        in_blocks,
    ) = compute_call(
        functools.partial(front_kernel, plan, dims, tuple(smalls)),
        "front",
        blocks,
        [scalars, whole, whole, whole] + [whole] * (len(smalls) + 1),
        [tall, tall, tall, tall] + [whole] * 7 + [anywhere],
        [
            shape((rows, inner)),
            shape((rows, inner)),
            shape((rows, inner), half),
            shape((rows, inner)),
            shape((rows, lanes)),
            shape((model, rows), half),
            shape((rows, model), half),
            shape(pair, half),
            shape(pair, half),
            shape((plan["rows"], inner), half),
            shape((1, model)),
            shape((blocks, depth, planes) + in_half, half),
        ],
        [
            pltpu.VMEM((rows, model), half),
            offset_buf,
            pltpu.VMEM((plan["rows"], piece), jnp.float32),
            pltpu.VMEM(small_half, half),
            pltpu.VMEM((blocks,) + in_half, half),
            pltpu.VMEM((depth, planes) + small_half, half),
            pltpu.VMEM((blocks, depth, planes) + in_half, half),
            pltpu.SemaphoreType.DMA((blocks,)),
        ]
        + Gather.sems(blocks + 1, dims),
        4 * rows * model * inner,
        (seq_lengths, tokens, cotangent, mask_row, *smalls.values(), in_proj),
        collective_id=0,
    )
    groups = 2
    part, pieces = rows // groups, chunks // groups
    row_block = pltpu.VMEM((pieces, chunk, width), jnp.float32)
    spread_block = pltpu.VMEM((rows, size, lanes), jnp.float32)
    fold_block = pltpu.VMEM((width // lanes, chunk * chunk, lanes), jnp.float32)

    def by_group(order, *dims_of):
        middle = (0,) * (len(dims_of) - 2)
        return pl.BlockSpec(dims_of, lambda b, g: (order(g),) + middle + (b,))

    def by_token(order, *dims_of):
        return pl.BlockSpec(dims_of, lambda b, g: (order(g),) + (0,) * (len(dims_of) - 1))

    def by_channel(height):
        return pl.BlockSpec((height, width), lambda b, g: (0, b))

    def onward(g):
        return g

    def backward(g):
        return groups - 1 - g

    states, step, core, begins, out_blocks = compute_call(
        functools.partial(forward_kernel, plan, dims),
        "forward",
        (blocks, groups),
        [
            scalars,
            by_token(onward, part, lanes),
            by_channel(plan["rows"]),
            by_group(onward, part, width),
            whole,
            whole,
            whole,
        ],
        [
            by_group(onward, part, size, width),
            by_group(onward, pieces, chunk, width),
            by_group(onward, pieces, chunk, width),
            by_group(onward, 1, size, width),
            anywhere,
        ],
        [
            shape((rows, size, inner)),
            shape((chunks, chunk, inner)),
            shape((chunks, chunk, inner)),
            shape((groups, size, inner)),
            shape((depth, planes) + out_proj.shape, half),
        ],
        [
            offset_buf,
            pltpu.VMEM((part, width), jnp.float32),
            row_block,
            row_block,
            spread_block,
            spread_block,
            fold_block,
            pltpu.VMEM((size, width), jnp.float32),
            pltpu.VMEM(out_proj.shape, half),
        ]
        + Gather.sems(1, dims),
        15 * rows * inner * size,
        (seq_lengths, projected, small, signal, write_pair, read_pair, out_proj),
        collective_id=2,
    )
    core_grad, gate_grad, grad_skip, grad_outw, grad_in_gate, output = compute_call(
        functools.partial(middle_kernel, plan),
        "middle",
        blocks,
        [deep, packed, tall, tall, whole, out_w, whole, whole],
        [deep, tall, thin(1), out_w, first_w, fixed(rows, model)],
        [
            shape((chunks, chunk, inner)),
            shape((rows, inner), half),
            shape((1, inner)),
            shape((inner, model), half),
            shape((model, inner), half),
            shape((rows, model), half),
        ],
        [
            pltpu.VMEM((rows, width), jnp.float32),
            pltpu.VMEM((rows, width), half),
            pltpu.VMEM((rows, model), jnp.float32),
        ],
        8 * rows * model * inner,
        (core, small, signal, gate_pre, grad_low, out_blocks.reshape(inner, model), flipped, tokens),
    )
    early_grads = [
        grad_outw.reshape((depth, planes) + out_proj.shape),
        grad_in_gate.reshape(depth, planes, in_rows, inner),
    ]
    early_sums = [shape(grad.shape[2:]) for grad in early_grads]
    (
        signal_grad,
        grad_stepw,
        grad_bias,
        grad_decaylog,
        flat,
        out_sum,
        in_gate_sum,
        early_squares,
    ) = compute_call(
        functools.partial(backward_kernel, plan, dims),
        "backward",
        (blocks, groups),
        [
            scalars,
            by_token(backward, part, lanes),
            by_channel(plan["rows"]),
            by_group(backward, part, width),
            whole,
            whole,
            by_group(backward, pieces, chunk, width),
            by_group(backward, pieces, chunk, width),
            by_group(backward, part, size, width),
            by_group(backward, 1, size, width),
            anywhere,
            anywhere,
        ],
        [
            by_group(backward, part, width),
            by_channel(rank),
            by_channel(1),
            by_channel(size),
            whole,
        ]
        + [whole] * 3,
        [
            shape((rows, inner)),
            shape((rank, inner)),
            shape((1, inner)),
            shape((size, inner)),
            shape((rows, lanes), half),
            *early_sums,
            shape((8, lanes)),
        ],
        [
            offset_buf,
            row_block,
            row_block,
            spread_block,
            spread_block,
            fold_block,
            fold_block,
            row_block,
            row_block,
            pltpu.VMEM((part, width), half),
            pltpu.VMEM((size, width), jnp.float32),
            pltpu.VMEM((chunks, chunk, lanes), jnp.float32),
            spread_block,
            spread_block,
        ]
        + [pltpu.VMEM(early.shape, early.dtype) for early in early_sums]
        + Reduce.rooms(dims, early_grads)
        + Reduce.sems(2, dims),
        40 * rows * inner * size,
        (
            seq_lengths,
            projected,
            small,
            signal,
            write_pair,
            read_pair,
            step,
            core_grad,
            states,
            begins,
            *early_grads,
        ),
        collective_id=3,
    )

    plain_rows = np.zeros((plan["rows"], piece), np.float32)
    for name in ("bias", "decay", "skip"):
        first, count = plan[name]
        plain_rows[first : first + count] = 1.0
    late_grads = [shape((depth, planes) + small_half, jnp.float32 if piece >= lanes else half)]
    late_grads += [shape((depth, planes, in_rows, width), half)] * blocks
    taps_n = conv_weight.shape[0]
    late = {"taps": (0, taps_n), "shift": (taps_n, 1), "gain": (taps_n + 1, 1)}
    late_block = (8, piece)

    def weights(side):
        return pl.BlockSpec((None, depth * planes, None, in_rows, width), lambda b: (b, 0, side, 0, 0))

    in_whole = in_blocks.reshape(blocks, number, *in_half)
    tokens_grad, in_branch_sum, small_sum, late_sum, norms = compute_call(
        functools.partial(back_kernel, plan, dims),
        "back",
        blocks,
        [scalars, whole, whole, whole, packed, whole, tall, whole, tall, tall, tall, whole]
        + [weights(0), weights(1)]
        + [whole] * 6,
        [whole] * 5,
        [
            shape((rows, model), half),
            shape((in_rows, inner)),
            shape(small_half),
            shape(late_block),
            shape((2, 8, lanes)),
        ],
        [
            offset_buf,
            pltpu.VMEM((rows + 8, width), jnp.float32),
            pltpu.VMEM((rows, width), half),
            pltpu.VMEM((rows, model), jnp.float32),
            pltpu.VMEM((blocks,) + late_grads[1].shape, half),
            pltpu.VMEM(late_grads[0].shape, late_grads[0].dtype),
            pltpu.VMEM((number,) + late_block, jnp.float32),
            pltpu.VMEM((number,) + late_block, jnp.float32),
            pltpu.VMEM((2,) + late_block, jnp.float32),
            pltpu.VMEM((2, 8, lanes), jnp.float32),
            pltpu.VMEM((number, 2, 8, lanes), jnp.float32),
            pltpu.VMEM((2, 2, 8, lanes), jnp.float32),
            pltpu.VMEM((blocks, in_rows, width), jnp.float32),
            pltpu.VMEM(small_half, jnp.float32),
            pltpu.SemaphoreType.DMA((2, number)),
            pltpu.SemaphoreType.DMA((2, number)),
        ]
        + Reduce.rooms(dims, late_grads)
        + Reduce.sems(blocks + 1, dims),
        8 * rows * model * inner,
        (
            seq_lengths,
            tokens,
            grad_low,
            gain_value,
            small,
            flat,
            branch,
            signal,
            slope,
            signal_grad,
            gate_grad,
            flipped,
            in_whole,
            in_whole,
            grad_stepw,
            grad_bias,
            grad_decaylog,
            grad_skip,
            jnp.asarray(plain_rows.reshape(small_half)),
            early_squares,
        ),
        collective_id=1,
    )

    names = ("gain", "taps", "shift", "select", "step", "bias", "decay", "skip")
    own = (norm_gain, conv_weight, conv_bias, select_proj, step_proj, step_bias, decay_log, skip_scale)
    in_grad, out_grad, grad_tokens, gain_grad, *small_grads, decay_sq, plain_sq = pl.pallas_call(
        functools.partial(finish_kernel, plan, names, late),
        in_specs=[whole] * 7,
        out_specs=[whole] * (3 + len(names)) + [scalars] * 2,
        out_shape=[shape(in_proj.shape), shape(out_proj.shape), shape(tokens.shape, half)]
        + [shape(array.shape) for array in own]
        + [shape((1, 1))] * 2,
        name="finish",
    )(
        tokens_grad,
        in_branch_sum,
        in_gate_sum,
        out_sum,
        small_sum.reshape(plan["rows"], piece),
        late_sum,
        norms,
    )
    return (
        output,
        grad_tokens,
        gain_grad,
        in_grad,
        *small_grads,
        out_grad,
        decay_sq[0, 0],
        plain_sq[0, 0],
    )


def solution(mesh):
    placed = (
        P(("wide", "narrow"), None),
        P(("wide", "narrow"), None),
        P(("wide", "narrow")),
        P(("wide", "narrow"), None),
        P("narrow"),
        P("narrow", None),
        P(None, "narrow"),
        P("narrow"),
        P(None, "narrow"),
        P(None, "narrow"),
        P("narrow"),
        P(None, "narrow"),
        P("narrow"),
        P("narrow", None),
    )
    return jax.shard_map(
        functools.partial(per_device, grid_of(mesh)),
        mesh=mesh,
        in_specs=placed,
        out_specs=(
            P(("wide", "narrow"), None),
            P(("wide", "narrow"), None),
            P("narrow"),
            P("narrow", None),
            P(None, "narrow"),
            P("narrow"),
            P(None, "narrow"),
            P(None, "narrow"),
            P("narrow"),
            P(None, "narrow"),
            P("narrow"),
            P("narrow", None),
            P(),
            P(),
        ),
        check_vma=False,
    )
```

```python
import functools
import math

import jax
import jax.numpy as jnp
import numpy as np
from jax import lax
from jax.experimental import pallas as pl
from jax.experimental.pallas import tpu as pltpu
from jax.sharding import PartitionSpec as P

epsilon = 1e-05
chunk = 8
lanes = 128
log2e = math.log2(math.e)
ln2 = math.log(2.0)
far = 1e30


def contract(left, right, left_dim, right_dim):
    return lax.dot_general(
        left, right, (((left_dim,), (right_dim,)), ((), ())), preferred_element_type=jnp.float32
    )


def row_loop(rows, group, body, initial):
    def some(index, carry):
        return body(index, pl.ds(pl.multiple_of(index * group, group), group), carry)

    return lax.fori_loop(0, rows // group, some, initial)


def cut(tile):
    return pl.ds(tile * lanes, lanes)


def sigmoid(values):
    return 0.5 * jnp.tanh(0.5 * values) + 0.5


def softplus(values):
    small = jnp.exp(-jnp.abs(values))
    series = small * (1.0 - small * (0.5 - small * (1.0 / 3.0 - 0.25 * small)))
    return jnp.maximum(values, 0.0) + jnp.where(small < 0.03, series, jnp.log(1.0 + small))


def slope_of(step):
    series = step * (1.0 - step * (0.5 - step * (1.0 / 6.0 - step * (1.0 / 24.0))))
    return jnp.where(step < 0.03, series, 1.0 - jnp.exp(-step))


def fill_offsets(lengths_ref, offset_buf, rows):
    place = lax.broadcasted_iota(jnp.int32, offset_buf.shape, 0)
    start = jnp.zeros(offset_buf.shape, jnp.int32)
    ahead = jnp.int32(0)
    for index in range(lengths_ref.shape[1] - 1):
        ahead = ahead + lengths_ref[0, index]
        start = jnp.where(place >= ahead, ahead, start)
    offset_buf[...] = jnp.where(place < rows, place - start, 0)


def small_rows(small_ref, first, count):
    base = first // 16 * 16
    tall = -(-(first + count - base) // 16) * 16
    return small_ref[base : base + tall, :].astype(jnp.float32)[first - base : first - base + count]


def eight(values):
    total = values[:8]
    for row in range(8, values.shape[0], 8):
        total = total + values[row : row + 8]
    return total


def conv_rows(index, at, group, tile, branch_ref, offset_buf, taps, shift):
    count = taps.shape[0]
    here = slice(tile * lanes, (tile + 1) * lanes)
    current = branch_ref[at, cut(tile)]
    before = branch_ref[pl.ds(pl.multiple_of(jnp.maximum(index * group - 8, 0), 8), 8), cut(tile)]
    both = jnp.concatenate([before, current], axis=0)
    offsets = offset_buf[at, :]
    summed = shift[:, here] + taps[count - 1 : count, here] * current
    for tap in range(count - 1):
        lag = count - 1 - tap
        read = jnp.where(offsets >= lag, pltpu.roll(both, lag, 0)[8:], 0.0)
        summed = summed + taps[tap : tap + 1, here] * read
    return summed


def rows_of(blocks):
    return as_matrix(blocks[...][None])


def as_matrix(blocks):
    columns = blocks.shape[3]
    if blocks.shape[2] % 16:
        return blocks.astype(jnp.float32).reshape(-1, columns).astype(blocks.dtype)
    return blocks.reshape(-1, columns)


def front_kernel(
    plan,
    dims,
    names,
    lengths_ref,
    tokens_ref,
    cotangent_ref,
    mask_ref,
    *refs,
):
    smalls, in_ref, refs = refs[: len(names)], refs[len(names)], refs[len(names) + 1 :]
    branch_ref, signal_ref, slope_ref, projected_ref, flipped_ref, normed_ref, low_ref = refs[:7]
    write_pair, read_pair, small_out, gain_ref, whole_ref = refs[7:12]
    offset_buf, pack_buf, own_small, own_in, land_small, land_in, store_sem = refs[12:19]
    rows = tokens_ref.shape[0]
    width = branch_ref.shape[1]
    block = pl.program_id(0)
    last = whole_ref.shape[0]
    gather = Gather(
        dims,
        [own_small] + [own_in.at[index] for index in range(last)],
        [land_small] + [land_in.at[index] for index in range(last)],
        refs[19:],
    )

    def stored(index):
        return pltpu.make_async_copy(land_in.at[index], whole_ref.at[index], store_sem.at[index])

    @pl.when(block == 0)
    def _():
        pack_buf[...] = jnp.zeros_like(pack_buf)
        for name, ref in zip(names, smalls):
            first, tall = plan[name]
            pack_buf[first : first + tall, : ref.shape[1]] = ref[...]
        tall = pack_buf.shape[0] // 2
        for side in range(2):
            own_small[side] = pack_buf[side * tall : (side + 1) * tall, :].astype(own_small.dtype)
        for index in range(last):
            own_in[index] = in_ref[:, index * width : (index + 1) * width].astype(own_in.dtype)
        Place(dims).greet()
        for index in range(last + 1):
            gather.start(index)
        fill_offsets(lengths_ref, offset_buf, rows)
        down = lax.broadcasted_iota(jnp.int32, (rows, rows), 0)
        along = lax.broadcasted_iota(jnp.int32, (rows, rows), 1)
        diagonal = jnp.where(down == along, mask_ref[...].astype(jnp.float32), 0.0).astype(low_ref.dtype)
        low_ref[...] = jnp.dot(
            diagonal, cotangent_ref[...], preferred_element_type=jnp.float32
        ).astype(low_ref.dtype)
        projected_ref[...] = jnp.zeros_like(projected_ref)
        for which, number in ((0, 1), (1, 1), (0, 2), (1, 2), (2, 1), (0, 3)):
            gather.leg(which, number)
        gather.arrive(0)
        share = land_small.shape[4]
        gains = gain_ref.shape[1] // (land_small.shape[0] * land_small.shape[1])
        gain_row = plan["gain"][0]
        for z in range(land_small.shape[0]):
            for plane in range(land_small.shape[1]):
                owner = z * land_small.shape[1] + plane
                for side in range(2):
                    small_out[side * tall : (side + 1) * tall, owner * share : (owner + 1) * share] = land_small[
                        z, plane, side
                    ]
                side, row = gain_row // tall, gain_row % tall
                base = row // 16 * 16
                some = land_small[z, plane, side, base : base + 16, :].astype(jnp.float32)
                gain_ref[:, owner * gains : (owner + 1) * gains] = some[row - base : row - base + 1, :gains]

        def norm(index, at, carry):
            residual = tokens_ref[at, :].astype(jnp.float32)
            scale = lax.rsqrt(jnp.mean(residual * residual, axis=1, keepdims=True) + epsilon)
            normed_ref[at, :] = (residual * scale * gain_ref[...]).astype(normed_ref.dtype)
            return carry

        row_loop(rows, 16, norm, 0)
        flipped_ref[...] = normed_ref[...].T
        for which, number in ((2, 2), (1, 3), (3, 1)):
            gather.leg(which, number)

    def move_on(plan_of_moves):
        for moment, legs in plan_of_moves:

            @pl.when(block == moment)
            def _(legs=legs):
                for which, number in legs:
                    gather.leg(which, number)

    for index in range(last):

        @pl.when(block == index)
        def _(index=index):
            gather.arrive(index + 1)
            stored(index).start()

    branch_w = as_matrix(land_in[block])
    branch_ref[...] = jnp.dot(normed_ref[...], branch_w, preferred_element_type=jnp.float32)
    move_on(((0, ((3, 2), (4, 1), (2, 3))), (1, ((4, 2), (3, 3))), (2, ((4, 3),))))
    small_ref = small_out.at[:, pl.ds(pl.multiple_of(block * width, width), width)]
    taps = small_rows(small_ref, *plan["taps"])
    shift = small_rows(small_ref, *plan["shift"])

    def some(index, at, carry):
        for tile in range(width // lanes):
            summed = conv_rows(index, at, 32, tile, branch_ref, offset_buf, taps, shift)
            sigma = sigmoid(summed)
            active = summed * sigma
            signal_ref[at, cut(tile)] = active.astype(signal_ref.dtype)
            slope_ref[at, cut(tile)] = sigma + active * (1.0 - sigma)
        return carry

    row_loop(rows, 32, some, 0)
    projected_ref[...] += contract(signal_ref[...], small_ref[:lanes, :], 1, 1)

    @pl.when(block == pl.num_programs(0) - 1)
    def _():
        high, low = high_low(projected_ref[...])
        own = own_tokens(rows)
        rank = plan["step"][1]
        size = plan["decay"][1]
        entry = lax.broadcasted_iota(jnp.int32, (lanes, lanes), 0)
        lane = lax.rem(lax.broadcasted_iota(jnp.int32, (lanes, lanes), 1), size)
        for first, pair in ((rank, write_pair), (rank + size, read_pair)):
            spread = (entry == lane + first).astype(jnp.bfloat16)
            parts = [
                (jnp.dot(part.astype(jnp.bfloat16), spread, preferred_element_type=jnp.float32) * own).reshape(
                    rows // chunk, chunk, lanes
                )
                for part in (high, low)
            ]
            pair[...] = jnp.concatenate(parts, axis=1).astype(pair.dtype)
        for index in range(last + 1):
            gather.drain(index)
        for index in range(last):
            stored(index).wait()


def high_low(values):
    high = values.astype(jnp.bfloat16).astype(jnp.float32)
    return high, values - high


def own_tokens(rows):
    token = lax.rem(lax.broadcasted_iota(jnp.int32, (rows, lanes), 0), chunk)
    return (token == lax.div(lax.broadcasted_iota(jnp.int32, (rows, lanes), 1), lanes // chunk)).astype(
        jnp.float32
    )


def spread_all(pairs, target):
    some = 8

    def spread(index, carry):
        rows = jnp.concatenate([pairs[index * some + number] for number in range(some)], axis=1)
        wide = contract(rows, jnp.ones((rows.shape[0], lanes), rows.dtype), 0, 0)
        target[pl.ds(index * some * chunk, some * chunk)] = wide.reshape(some * chunk, -1, lanes)
        return carry

    lax.fori_loop(0, pairs.shape[0] // some, spread, 0)


def folded(buffer, tile):
    total = buffer[tile, pl.ds(0, chunk, stride=chunk), :]
    for row in range(1, chunk):
        total = total + buffer[tile, pl.ds(row, chunk, stride=chunk), :]
    return total


def forward_kernel(
    plan,
    dims,
    lengths_ref,
    projected_ref,
    small_ref,
    signal_ref,
    write_pair,
    read_pair,
    gate_own,
    out_own,
    states_ref,
    step_ref,
    core_ref,
    begin_ref,
    gate_whole,
    out_whole,
    offset_buf,
    pre_buf,
    decay_step,
    flows,
    write_wide,
    read_wide,
    fold_buf,
    held_buf,
    gate_low,
    out_low,
    *sems,
):
    rows, width = pre_buf.shape
    size = plan["decay"][1]
    half_size = size // 2
    tiles = width // lanes
    chunks = rows // chunk
    rank = plan["step"][1]
    group = pl.program_id(1)
    groups = pl.num_programs(1)
    moment = pl.program_id(0) * groups + group
    moments = pl.num_programs(0) * groups
    pieces = gate_low.shape[0]
    gather = Gather(
        dims,
        [buffer.at[index] for index in range(pieces) for buffer in (gate_low, out_low)],
        [buffer.at[index] for index in range(pieces) for buffer in (gate_whole, out_whole)],
        sems,
    )
    count = 2 * pieces

    @pl.when(moment == 0)
    def _():
        for index in range(pieces):
            for own, low in ((gate_own, gate_low), (out_own, out_low)):
                each = low.shape[2]
                low[index] = own[:, index * each : (index + 1) * each].astype(low.dtype)
        Place(dims).greet()
        for which in range(count):
            gather.start(which)
        fill_offsets(lengths_ref, offset_buf, offset_buf.shape[0] - 8)
        spread_all(write_pair, write_wide)
        spread_all(read_pair, read_wide)

    @pl.when(group == 0)
    def _():
        held_buf[...] = jnp.zeros_like(held_buf)

    begin_ref[0] = held_buf[...]
    pre_buf[...] = jnp.dot(
        projected_ref[:, :rank].astype(small_ref.dtype),
        small_ref[pl.ds(plan["step"][0], rank), :],
        preferred_element_type=jnp.float32,
    )
    bias = small_rows(small_ref, *plan["bias"])

    def before(index, at, carry):
        spot = pl.ds(pl.multiple_of(index * 4, 4), 4)
        inside = offset_buf[pl.ds(pl.multiple_of(group * rows + index * 32, 32), 32), :] > 0
        for tile in range(tiles):
            step = softplus(pre_buf[at, cut(tile)] + bias[:, tile * lanes : (tile + 1) * lanes])
            step_ref[spot, :, cut(tile)] = step.reshape(4, chunk, lanes)
            decay_step[spot, :, cut(tile)] = jnp.where(inside, step, far).reshape(4, chunk, lanes)
            flow = step * signal_ref[at, cut(tile)].astype(jnp.float32)
            flows[spot, :, cut(tile)] = flow.reshape(4, chunk, lanes)
        return carry

    row_loop(rows, 4 * chunk, before, 0)
    rates = -jnp.exp(small_rows(small_ref, *plan["decay"])) * log2e
    rates = [rates[:, tile * lanes : (tile + 1) * lanes] for tile in range(tiles)]

    def forward(index, held):
        held = list(held)
        for place in range(chunk):
            now = index * chunk + place
            write_now = write_wide[group * rows + now]
            read_now = read_wide[group * rows + now]
            for tile in range(tiles):
                decay = jnp.exp2(rates[tile] * decay_step[index, pl.ds(place, 1), cut(tile)])
                fresh = decay * held[tile] + write_now * flows[index, pl.ds(place, 1), cut(tile)]
                held[tile] = fresh
                states_ref[now, :, cut(tile)] = fresh
                product = read_now * fresh
                fold_buf[tile, pl.ds(place * chunk, chunk), :] = product[:half_size] + product[half_size:]
        for tile in range(tiles):
            core_ref[index, :, cut(tile)] = folded(fold_buf, tile)
        return tuple(held)

    held = tuple(held_buf[:, cut(tile)] for tile in range(tiles))
    schedule = {}
    for which in range(count):
        for number in (1, 2, 3):
            schedule.setdefault(min(1 + 2 * (which + number), 2 * 8), []).append((which, number))

    def move_on(legs):
        for which, number in legs:
            gather.leg(which, number)

    for half_loop in range(2):
        for point, legs in sorted(schedule.items()):
            if point < 16 and point % 2 == half_loop:
                pl.when(moment == point // 2)(functools.partial(move_on, legs))
        held = lax.fori_loop(half_loop * chunks // 2, (half_loop + 1) * chunks // 2, forward, held)
    for tile in range(tiles):
        held_buf[:, cut(tile)] = held[tile]

    @pl.when(moment == moments - 1)
    def _():
        move_on(schedule.get(16, ()))
        for which in range(count):
            gather.arrive(which)
        for which in range(count):
            gather.drain(which)


def middle_kernel(
    plan,
    core_ref,
    small_ref,
    signal_ref,
    gate_w,
    low_ref,
    out_w,
    flipped_ref,
    normed_ref,
    tokens_ref,
    core_grad_ref,
    gate_grad_ref,
    skip_grad_ref,
    out_grad_ref,
    in_grad_ref,
    output_ref,
    pre_buf,
    gate_buf,
    gated_buf,
    out_buf,
    total,
):
    rows, width = pre_buf.shape
    tiles = width // lanes
    block = pl.program_id(0)
    each = out_w.shape[3]
    for index in range(out_w.shape[0]):
        out_buf[:, index * each : (index + 1) * each] = as_matrix(out_w[index][None])
    gate_buf[...] = jnp.dot(normed_ref[...], rows_of(gate_w), preferred_element_type=jnp.float32)
    pre_buf[...] = contract(low_ref[...], out_buf[...], 1, 1)
    skip = small_rows(small_ref, *plan["skip"])

    def after(index, at, carry):
        spot = pl.ds(pl.multiple_of(index * 4, 4), 4)
        sums = []
        for tile in range(tiles):
            signal = signal_ref[at, cut(tile)].astype(jnp.float32)
            core = core_ref[spot, :, cut(tile)].reshape(4 * chunk, lanes)
            core = core + skip[:, tile * lanes : (tile + 1) * lanes] * signal
            gate = gate_buf[at, cut(tile)]
            sigma = sigmoid(gate)
            active = gate * sigma
            gated_buf[at, cut(tile)] = (core * active).astype(gated_buf.dtype)
            grad_gated = pre_buf[at, cut(tile)]
            grad_core = grad_gated * active
            core_grad_ref[spot, :, cut(tile)] = grad_core.reshape(4, chunk, lanes)
            slope = sigma + active * (1.0 - sigma)
            gate_grad_ref[at, cut(tile)] = (grad_gated * core * slope).astype(gate_grad_ref.dtype)
            sums.append(carry[tile] + eight(grad_core * signal))
        return tuple(sums)

    zero_rows = jnp.zeros((8, lanes), jnp.float32)
    skips = row_loop(rows, 4 * chunk, after, (zero_rows,) * tiles)
    for tile in range(tiles):
        skip_grad_ref[:, cut(tile)] = jnp.sum(skips[tile], axis=0, keepdims=True)
    out_grad_ref[...] = contract(gated_buf[...], low_ref[...], 0, 0).astype(out_grad_ref.dtype)
    in_grad_ref[...] = jnp.dot(
        flipped_ref[...], gate_grad_ref[...], preferred_element_type=jnp.float32
    ).astype(in_grad_ref.dtype)
    piece = jnp.dot(gated_buf[...], out_buf[...], preferred_element_type=jnp.float32)

    @pl.when(block == 0)
    def _():
        total[...] = piece

    @pl.when(block > 0)
    def _():
        total[...] += piece

    @pl.when(block == pl.num_programs(0) - 1)
    def _():
        output_ref[...] = (tokens_ref[...].astype(jnp.float32) + total[...]).astype(output_ref.dtype)


def backward_kernel(
    plan,
    dims,
    lengths_ref,
    projected_ref,
    small_ref,
    signal_ref,
    write_pair,
    read_pair,
    step_ref,
    core_grad_ref,
    states_ref,
    begin_ref,
    out_grad_ref,
    in_grad_ref,
    signal_grad_ref,
    step_w_grad_ref,
    bias_grad_ref,
    decay_grad_ref,
    flat_ref,
    out_sum_ref,
    in_sum_ref,
    square_ref,
    offset_buf,
    decay_step,
    flows,
    write_wide,
    read_wide,
    first_buf,
    second_buf,
    through_buf,
    scaled_buf,
    low_buf,
    incoming_buf,
    rank_buf,
    write_buf,
    read_buf,
    *parts,
):
    rows, width = low_buf.shape
    rank = plan["step"][1]
    size = plan["decay"][1]
    half_size = size // 2
    tiles = width // lanes
    chunks = rows // chunk
    block = pl.program_id(0)
    turn = pl.program_id(1)
    groups = pl.num_programs(1)
    group = groups - 1 - turn
    moment = block * groups + turn
    moments = pl.num_programs(0) * groups
    gate_result, out_result, parts = parts[0], parts[1], parts[2:]
    pieces = gate_result.shape[0]
    count = 2 * pieces

    def columns(ref, result, index):
        return ref.at[:, :, :, pl.ds(index * result.shape[2], result.shape[2])]

    both = ((in_grad_ref, gate_result), (out_grad_ref, out_result))
    reduce = Reduce(
        dims,
        [columns(ref, result, index) for index in range(pieces) for ref, result in both],
        parts[: 5 * count],
        parts[5 * count :],
        [result.at[index] for index in range(pieces) for _, result in both],
        False,
    )

    @pl.when(moment == 0)
    def _():
        Place(dims).greet()
        for which in range(count):
            reduce.start(which)
        fill_offsets(lengths_ref, offset_buf, offset_buf.shape[0] - 8)
        spread_all(write_pair, write_wide)
        spread_all(read_pair, read_wide)
        write_buf[...] = jnp.zeros_like(write_buf)
        read_buf[...] = jnp.zeros_like(read_buf)
        rank_buf[...] = jnp.zeros_like(rank_buf)

    @pl.when(turn == 0)
    def _():
        incoming_buf[...] = jnp.zeros_like(incoming_buf)
        decay_grad_ref[...] = jnp.zeros_like(decay_grad_ref)
        bias_grad_ref[...] = jnp.zeros_like(bias_grad_ref)
        step_w_grad_ref[...] = jnp.zeros_like(step_w_grad_ref)

    def before(index, at, carry):
        spot = pl.ds(pl.multiple_of(index * 4, 4), 4)
        offsets = offset_buf[pl.ds(pl.multiple_of(group * rows + index * 32, 32), 32), :]
        inside = (offsets > 0).reshape(4, chunk, lanes)
        for tile in range(tiles):
            step = step_ref[spot, :, cut(tile)]
            decay_step[spot, :, cut(tile)] = jnp.where(inside, step, far)
            signal = signal_ref[at, cut(tile)].astype(jnp.float32).reshape(4, chunk, lanes)
            flows[spot, :, cut(tile)] = step * signal
        return carry

    row_loop(rows, 4 * chunk, before, 0)
    rates = -jnp.exp(small_rows(small_ref, *plan["decay"])) * log2e
    rates = [rates[:, tile * lanes : (tile + 1) * lanes] for tile in range(tiles)]

    def backward(position, carried):
        index = chunks - 1 - position
        incoming, decay_sums = list(carried[0]), list(carried[1])
        for place in range(chunk - 1, -1, -1):
            now = index * chunk + place
            token = group * rows + now
            write_now = write_wide[token]
            read_now = read_wide[token]
            read_sum = None
            write_sum = None
            for tile in range(tiles):
                step_now = decay_step[index, pl.ds(place, 1), cut(tile)]
                grad_now = core_grad_ref[index, pl.ds(place, 1), cut(tile)]
                if place > 0:
                    earlier = states_ref[now - 1, :, cut(tile)]
                else:
                    earlier = jnp.where(
                        index > 0, states_ref[jnp.maximum(now - 1, 0), :, cut(tile)], begin_ref[0, :, cut(tile)]
                    )
                grad_state = incoming[tile] + read_now * grad_now
                through_read = states_ref[now, :, cut(tile)] * grad_now
                through_write = grad_state * flows[index, pl.ds(place, 1), cut(tile)]
                read_sum = through_read if read_sum is None else read_sum + through_read
                write_sum = through_write if write_sum is None else write_sum + through_write
                passed = grad_state * write_now
                first_buf[tile, pl.ds(place * chunk, chunk), :] = passed[:half_size] + passed[half_size:]
                leaving = jnp.exp2(rates[tile] * step_now) * grad_state
                incoming[tile] = leaving
                weighted = leaving * earlier
                scaled = weighted * rates[tile]
                second_buf[tile, pl.ds(place * chunk, chunk), :] = scaled[:half_size] + scaled[half_size:]
                decay_sums[tile] = decay_sums[tile] + weighted * step_now
            read_buf[token] += read_sum
            write_buf[token] += write_sum
        for tile in range(tiles):
            through_buf[index, :, cut(tile)] = folded(first_buf, tile)
            scaled_buf[index, :, cut(tile)] = folded(second_buf, tile)
        return (tuple(incoming), tuple(decay_sums))

    incoming = tuple(incoming_buf[:, cut(tile)] for tile in range(tiles))
    nothing = (jnp.zeros((size, lanes), jnp.float32),) * tiles
    schedule = {}
    for which in range(count):
        for number in (1, 2, 3):
            schedule.setdefault(which + which // 3 + 2 * number - 1, []).append((which, number))

    def move_on(legs):
        for which, number in legs:
            reduce.leg(which, number)

    carried = (incoming, nothing)
    for half_loop in range(2):
        for point, legs in sorted(schedule.items()):
            if point % 2 == half_loop:
                pl.when(moment == point // 2)(functools.partial(move_on, legs))
        carried = lax.fori_loop(half_loop * chunks // 2, (half_loop + 1) * chunks // 2, backward, carried)
    incoming, decay_sums = carried
    for tile in range(tiles):
        incoming_buf[:, cut(tile)] = incoming[tile]
        decay_grad_ref[:, cut(tile)] += decay_sums[tile] * rates[tile] * ln2
    skip = small_rows(small_ref, *plan["skip"])

    def after(index, at, carry):
        spot = pl.ds(pl.multiple_of(index * 4, 4), 4)
        sums = []
        for tile in range(tiles):
            signal = signal_ref[at, cut(tile)].astype(jnp.float32)
            step = step_ref[spot, :, cut(tile)].reshape(4 * chunk, lanes)
            through = through_buf[spot, :, cut(tile)].reshape(4 * chunk, lanes)
            scaled = scaled_buf[spot, :, cut(tile)].reshape(4 * chunk, lanes)
            core_grad = core_grad_ref[spot, :, cut(tile)].reshape(4 * chunk, lanes)
            grad_pre = (through * signal + ln2 * scaled) * slope_of(step)
            low_buf[at, cut(tile)] = grad_pre.astype(low_buf.dtype)
            signal_grad_ref[at, cut(tile)] = (
                through * step + skip[:, tile * lanes : (tile + 1) * lanes] * core_grad
            )
            sums.append(carry[tile] + eight(grad_pre))
        return tuple(sums)

    zero_rows = jnp.zeros((8, lanes), jnp.float32)
    sums = row_loop(rows, 4 * chunk, after, (zero_rows,) * tiles)
    for tile in range(tiles):
        bias_grad_ref[:, cut(tile)] += jnp.sum(sums[tile], axis=0, keepdims=True)
    step_w_grad_ref[...] += contract(
        projected_ref[:, :rank].astype(low_buf.dtype), low_buf[...], 0, 0
    )
    step_w = small_ref[pl.ds(plan["step"][0], rank), :]
    step_w = jnp.concatenate([step_w, jnp.zeros((lanes - rank, width), step_w.dtype)], axis=0)
    rank_buf[pl.ds(group * chunks, chunks)] += contract(low_buf[...], step_w, 1, 1).reshape(
        chunks, chunk, lanes
    )

    @pl.when(moment == moments - 1)
    def _():
        squares = jnp.zeros((8, lanes), jnp.float32)
        for which in range(count):
            squares = squares + reduce.finish(which)[0]
        square_ref[...] = squares
        some = 8
        entry = lax.rem(lax.broadcasted_iota(jnp.int32, (some * chunk * size, lanes), 0), size)
        target = lax.broadcasted_iota(jnp.int32, (some * chunk * size, lanes), 1)
        ones = jnp.ones((lanes, lanes), jnp.bfloat16)

        def lay(index, carry):
            lot = pl.ds(index * some * chunk, some * chunk)
            for number, buffer in enumerate((write_buf, read_buf)):
                high, low = high_low(buffer[lot].reshape(some * chunk * size, lanes))
                summed = jnp.dot(high.astype(jnp.bfloat16), ones, preferred_element_type=jnp.float32)
                summed += jnp.dot(low.astype(jnp.bfloat16), ones, preferred_element_type=jnp.float32)
                summed = jnp.where(target == entry + rank + number * size, summed, 0.0)
                summed = jnp.sum(summed.reshape(some * chunk, size, lanes), axis=1)
                rank_buf[pl.ds(index * some, some)] += summed.reshape(some, chunk, lanes)
            return carry

        lax.fori_loop(0, rank_buf.shape[0] // some, lay, 0)
        flat_ref[...] = rank_buf[...].reshape(flat_ref.shape).astype(flat_ref.dtype)
        for which in range(count):
            reduce.settle(which)
        for index in range(pieces):
            for target, result in ((out_sum_ref, out_result), (in_sum_ref, gate_result)):
                each = result.shape[2]
                target[:, index * each : (index + 1) * each] = result[index]


def back_kernel(
    plan,
    dims,
    lengths_ref,
    tokens_ref,
    low_ref,
    gain_ref,
    small_ref,
    flat_ref,
    branch_ref,
    signal_ref,
    slope_ref,
    signal_grad_ref,
    gate_grad_ref,
    flipped_ref,
    branch_w,
    gate_w,
    step_w_grad_ref,
    bias_grad_ref,
    decay_grad_ref,
    skip_grad_ref,
    plain_ref,
    earlier_ref,
    tokens_grad_ref,
    in_sum_ref,
    small_sum_ref,
    late_sum_ref,
    norm_ref,
    offset_buf,
    conv_buf,
    mixed_buf,
    total,
    in_stage,
    small_stage,
    late_stage,
    late_land,
    late_cores,
    norm_own,
    norm_land,
    norm_cores,
    in_result,
    small_result,
    direct_send,
    direct_recv,
    *parts,
):
    rows = tokens_ref.shape[0]
    width = branch_ref.shape[1]
    tiles = width // lanes
    block = pl.program_id(0)
    last = in_stage.shape[0]
    count = last + 1
    reduce = Reduce(
        dims,
        [small_stage] + [in_stage.at[index] for index in range(last)],
        parts[: 5 * count],
        parts[5 * count :],
        [small_result] + [in_result.at[index] for index in range(last)],
        True,
    )
    share = small_stage.shape[4]
    half_rows = small_stage.shape[3]
    planes = small_stage.shape[1]
    owners = small_stage.shape[0] * planes

    @pl.when(block == 0)
    def _():
        Place(dims).greet(everyone=True)
        select_grad = contract(flat_ref[...], signal_ref[...], 0, 0)
        step_first, step_tall = plan["step"]
        filler = jnp.zeros((2 * half_rows - step_first - step_tall, select_grad.shape[1]), jnp.float32)
        pieces = {
            "decay": decay_grad_ref[...],
            "bias": bias_grad_ref[...],
            "skip": skip_grad_ref[...],
            "step": step_w_grad_ref[...],
        }
        first = plan["select"][1]
        rows_now = [select_grad[:first]]
        for name in ("decay", "taps", "shift", "bias", "skip", "gain"):
            tall = plan[name][1]
            rows_now.append(
                pieces[name] if name in pieces else jnp.zeros((tall, select_grad.shape[1]), jnp.float32)
            )
            first += tall
        rows_now.append(jnp.zeros((step_first - first, select_grad.shape[1]), jnp.float32))
        rows_now.append(pieces["step"])
        if filler.shape[0]:
            rows_now.append(filler)
        everything = jnp.concatenate(rows_now, axis=0)
        for owner in range(owners):
            for side in range(2):
                small_stage[owner // planes, owner % planes, side] = everything[
                    side * half_rows : (side + 1) * half_rows, owner * share : (owner + 1) * share
                ].astype(small_stage.dtype)
        reduce.start(0)
        fill_offsets(lengths_ref, offset_buf, rows)

    taps = small_rows(small_ref, *plan["taps"])
    taps_count = taps.shape[0]
    conv_buf[pl.ds(0, rows), :] = signal_grad_ref[...] + jnp.dot(
        flat_ref[...], small_ref[:lanes, :], preferred_element_type=jnp.float32
    )
    conv_buf[pl.ds(rows, 8), :] = jnp.zeros((8, width), jnp.float32)

    def through_conv(index, at, carry):
        sums = []
        for tile in range(tiles):
            grad_conv = conv_buf[at, cut(tile)] * slope_ref[at, cut(tile)]
            conv_buf[at, cut(tile)] = grad_conv
            sums.append(carry[tile] + eight(grad_conv))
        return tuple(sums)

    zero_rows = jnp.zeros((8, lanes), jnp.float32)
    shift_sums = row_loop(rows, 32, through_conv, (zero_rows,) * tiles)

    def move_on(plan_of_moves):
        for moment, legs in plan_of_moves:

            @pl.when(block == moment)
            def _(legs=legs):
                for which, number in legs:
                    reduce.leg(which, number)

    move_on(((0, ((0, 1),)), (1, ((1, 1),)), (2, ((2, 1),)), (3, ((3, 1),))))

    def to_branch(index, at, carry):
        longer = pl.ds(pl.multiple_of(index * 32, 32), 40)
        offsets = offset_buf[longer, :]
        result = []
        for tile in range(tiles):
            here = slice(tile * lanes, (tile + 1) * lanes)
            grads = conv_buf[longer, cut(tile)]
            branch = branch_ref[at, cut(tile)]
            summed = taps[taps_count - 1 : taps_count, here] * grads[:32]
            sums = [None] * taps_count
            sums[taps_count - 1] = carry[tile][taps_count - 1] + eight(branch * grads[:32])
            for tap in range(taps_count - 1):
                lag = taps_count - 1 - tap
                moved = pltpu.roll(jnp.where(offsets >= lag, grads, 0.0), 40 - lag, 0)[:32]
                summed = summed + taps[tap : tap + 1, here] * moved
                sums[tap] = carry[tile][tap] + eight(branch * moved)
            mixed_buf[at, cut(tile)] = summed.astype(mixed_buf.dtype)
            result.append(tuple(sums))
        return tuple(result)

    sums = row_loop(rows, 32, to_branch, ((zero_rows,) * taps_count,) * tiles)
    late = [
        jnp.concatenate(
            [jnp.sum(sums[tile][tap], axis=0, keepdims=True) for tap in range(taps_count)]
            + [jnp.sum(shift_sums[tile], axis=0, keepdims=True)]
            + [jnp.zeros((8 - taps_count - 1, lanes), jnp.float32)],
            axis=0,
        )
        for tile in range(tiles)
    ]
    late = jnp.concatenate(late, axis=1)
    for piece in range(width // share):
        late_stage[block * (width // share) + piece] = late[:, piece * share : (piece + 1) * share]
    in_grad = jnp.dot(flipped_ref[...], mixed_buf[...], preferred_element_type=jnp.float32)
    in_stage[block] = in_grad.reshape(in_stage.shape[1:]).astype(in_stage.dtype)
    for index in range(last):

        @pl.when(block == index)
        def _(index=index):
            reduce.start(index + 1)

    grad_normed_piece = contract(mixed_buf[...], rows_of(branch_w), 1, 1)
    grad_normed_piece += contract(gate_grad_ref[...], rows_of(gate_w), 1, 1)

    @pl.when(block == 0)
    def _():
        total[...] = grad_normed_piece

    @pl.when(block > 0)
    def _():
        total[...] += grad_normed_piece

    move_on(((0, ((0, 2),)), (1, ((0, 3), (1, 2))), (2, ((2, 2), (1, 3))), (3, ((3, 2), (2, 3)))))

    @pl.when(block == pl.num_programs(0) - 1)
    def _():
        def finish(index, at, carry):
            residual = tokens_ref[at, :].astype(jnp.float32)
            scale = lax.rsqrt(jnp.mean(residual * residual, axis=1, keepdims=True) + epsilon)
            grad_normed = total[at, :]
            weighted = grad_normed * gain_ref[...]
            inner = jnp.mean(weighted * residual, axis=1, keepdims=True)
            grad_y = low_ref[at, :].astype(jnp.float32)
            result = grad_y + (scale * weighted - residual * (scale * scale * scale) * inner)
            tokens_grad_ref[at, :] = result.astype(tokens_grad_ref.dtype)
            return carry + eight(grad_normed * residual * scale)

        gains = row_loop(rows, 16, finish, jnp.zeros((8, total.shape[1]), jnp.float32))
        gains = jnp.sum(gains, axis=0, keepdims=True)
        place = Place(dims)
        each = gains.shape[1] // owners
        for owner in range(owners):
            late_stage[owner, taps_count + 1 : taps_count + 2, :each] = gains[
                :, owner * each : (owner + 1) * each
            ]
        late_sems = direct_send.at[0], direct_recv.at[0]
        norm_sems = direct_send.at[1], direct_recv.at[1]
        send_to_all(place, lambda target: late_stage.at[target], late_land, *late_sems)
        for which, number in ((4, 1), (3, 3), (4, 2)):
            reduce.leg(which, number)
        late_sum = sum_of_all(place, late_stage[place.me], late_land, *late_sems)
        late_sum = sum_of_cores(place, late_sum, late_cores, direct_send.at[0, 0], direct_recv.at[0, 0])
        late_sum_ref[...] = late_sum
        reduce.leg(4, 3)
        kept = earlier_ref[...] + folded_squares(late_sum * late_sum) * (1 - place.core).astype(jnp.float32)
        more, plain = reduce.finish(0, plain_ref)
        kept = kept + more
        for index in range(1, count):
            kept = kept + reduce.finish(index)[0]
        norm_own[...] = jnp.stack([kept, plain])
        send_to_all(place, lambda target: norm_own, norm_land, *norm_sems)
        norms = sum_of_all(place, norm_own[...], norm_land, *norm_sems)
        norm_ref[...] = sum_of_cores(place, norms, norm_cores, direct_send.at[1, 0], direct_recv.at[1, 0])
        for index in range(count):
            reduce.settle(index)
        for index in range(last):
            in_sum_ref[:, index * width : (index + 1) * width] = in_result[index]
        small_sum_ref[...] = small_result[...]


def finish_kernel(
    plan, names, late, tokens_ref, branch_ref, gate_ref, out_ref, small_ref, late_ref, norm_ref, *outs
):
    middle = branch_ref.shape[1]
    outs[0][:, :middle] = branch_ref[...]
    outs[0][:, middle:] = gate_ref[...]
    outs[1][...] = out_ref[...]
    outs[2][...] = tokens_ref[...]
    for name, target in zip(names, outs[3 : 3 + len(names)]):
        source, (first, count) = (late_ref, late[name]) if name in late else (small_ref, plan[name])
        if len(target.shape) == 1:
            target[...] = source[first, : target.shape[0]]
        else:
            target[...] = source[first : first + count, :]
    for index in range(2):
        outs[3 + len(names) + index][0, 0] = jnp.sum(norm_ref[index])


def shape(dims, kind=jnp.float32):
    return jax.ShapeDtypeStruct(dims, kind)


def compute_call(
    kernel, name, blocks, in_specs, out_specs, out_shape, scratch, flops, operands, collective_id=None
):
    return pl.pallas_call(
        kernel,
        grid=blocks if isinstance(blocks, tuple) else (blocks,),
        in_specs=in_specs,
        out_specs=out_specs,
        out_shape=out_shape,
        scratch_shapes=scratch,
        compiler_params=pltpu.CompilerParams(
            dimension_semantics=("arbitrary",) * (len(blocks) if isinstance(blocks, tuple) else 1),
            vmem_limit_bytes=62 * 1024 * 1024,
            collective_id=collective_id,
            has_side_effects=collective_id is not None,
        ),
        cost_estimate=pl.CostEstimate(flops=flops, bytes_accessed=40 << 20, transcendentals=0),
        name=name,
    )(*operands)


class Place:
    def __init__(self, dims, swapped=False):
        depth, tall, wide = dims
        self.dims = dims
        self.core = lax.axis_index("wide")
        self.me = lax.axis_index("narrow")
        self.across = lax.rem(self.me, wide)
        self.up = lax.rem(lax.div(self.me, wide), tall)
        self.deep = lax.div(self.me, wide * tall)
        side = 1 - self.core if swapped else self.core
        turn = side if tall == wide else 0
        self.second = (1 + turn * (wide - 1), self.across + turn * (self.up - self.across), wide)
        self.third = (wide - turn * (wide - 1), self.up + turn * (self.across - self.up), tall)
        self.spans = (depth, wide, tall)
        self.other = {"wide": 1 - self.core}

    def level(self, d):
        return lax.rem(self.deep + d, self.spans[0])

    def plane(self, e, f):
        return (
            lax.rem(self.second[1] + e, self.second[2]) * self.second[0]
            + lax.rem(self.third[1] + f, self.third[2]) * self.third[0]
        )

    def plane_behind(self, e, f):
        return self.plane((self.spans[1] - e) % self.spans[1], (self.spans[2] - f) % self.spans[2])

    def at(self, d, e, f):
        return {"narrow": self.level(d) * (self.dims[1] * self.dims[2]) + self.plane(e, f)}

    def greet(self, everyone=False):
        barrier = pltpu.get_barrier_semaphore()
        peers = [self.other]
        if everyone:
            number = self.spans[0] * self.spans[1] * self.spans[2]
            peers += [{"narrow": lax.rem(self.me + hop, number)} for hop in range(1, number)]
        else:
            for axis, size in enumerate(self.spans):
                for hop in range(1, size):
                    move = [0, 0, 0]
                    move[axis] = hop
                    peers.append(self.at(*move))
        for peer in peers:
            pl.semaphore_signal(barrier, inc=1, device_id=peer, device_id_type=pl.DeviceIdType.MESH)
        pl.semaphore_wait(barrier, len(peers))


def columns_of(width, side):
    return pl.ds(pl.multiple_of(side * (width // 2), lanes), width // 2)


def half_shape(block):
    return tuple(block[1:]) if len(block) == 3 else (block[0], block[1] // 2)


def half(view, block, side, lead=0):
    if len(block) == 3:
        return view.at[(slice(None),) * lead + (side,)]
    return view.at[(slice(None),) * (lead + 1) + (columns_of(block[1], side),)]


def remote(source, target, send_sem, recv_sem, device):
    return pltpu.make_async_remote_copy(
        src_ref=source,
        dst_ref=target,
        send_sem=send_sem,
        recv_sem=recv_sem,
        device_id=device,
        device_id_type=pl.DeviceIdType.MESH,
    )


class Gather:
    def __init__(self, dims, own, whole, sems):
        self.dims, self.own, self.whole = dims, own, whole
        self.local_sem, self.send_sem, self.recv_sem = sems

    @staticmethod
    def sems(count, dims):
        copies = dims[0] + 2 * dims[1] * dims[2]
        return [pltpu.SemaphoreType.DMA((count,))] + [pltpu.SemaphoreType.DMA((count, copies))] * 2

    def line(self, which, plane, side):
        return half(self.whole[which].at[:, plane], self.own[which].shape, side, 1)

    def local(self, place, which):
        block = self.own[which].shape
        return pltpu.make_async_copy(
            half(self.own[which], block, place.core),
            half(self.whole[which].at[place.deep, place.plane(0, 0)], block, place.core),
            self.local_sem.at[which],
        )

    def copy(self, which, source, target, index, device):
        return remote(
            source, target, self.send_sem.at[which, index], self.recv_sem.at[which, index], device
        )

    def rise(self, place, which, hop):
        block = self.own[which].shape
        return self.copy(
            which,
            half(self.own[which], block, place.core),
            half(self.whole[which].at[place.deep, place.plane(0, 0)], block, place.core),
            hop,
            place.at(hop, 0, 0),
        )

    def leg_index(self, e, f):
        return self.dims[0] + e * self.dims[1] + f

    def hand_index(self, e, f):
        return self.leg_index(e, f) + self.dims[1] * self.dims[2]

    def onward(self, place, which, e, f):
        line = self.line(which, place.plane_behind(e, f), place.core)
        if f == 0:
            for hop in range(1, place.spans[2]):
                self.copy(which, line, line, self.leg_index(e, hop), place.at(0, 0, hop)).start()
        if f == 0 and e == 0:
            for hop in range(1, place.spans[1]):
                self.copy(which, line, line, self.leg_index(hop, 0), place.at(0, hop, 0)).start()
        self.copy(which, line, line, self.hand_index(e, f), place.other).start()

    def start(self, which):
        place = Place(self.dims)
        for hop in range(1, place.spans[0]):
            self.rise(place, which, hop).start()
        self.local(place, which).start()

    def leg(self, which, number):
        place = Place(self.dims)
        if number == 1:
            self.local(place, which).wait()
            for hop in range(1, place.spans[0]):
                self.rise(place, which, hop).wait_recv()
            self.onward(place, which, 0, 0)
            return
        for e in range(place.spans[1]):
            for f in range(place.spans[2]):
                if (number == 2 and f == 0 and e > 0) or (number == 3 and f > 0):
                    line = self.line(which, place.plane_behind(e, f), place.core)
                    self.copy(which, line, line, self.leg_index(e, f), place.other).wait_recv()
                    self.onward(place, which, e, f)

    def arrive(self, which):
        place, mirror = Place(self.dims), Place(self.dims, swapped=True)
        for e in range(place.spans[1]):
            for f in range(place.spans[2]):
                line = self.line(which, mirror.plane_behind(e, f), 1 - place.core)
                self.copy(which, line, line, self.hand_index(e, f), place.other).wait_recv()

    def drain(self, which):
        place = Place(self.dims)
        for hop in range(1, place.spans[0]):
            self.rise(place, which, hop).wait_send()
        for e in range(place.spans[1]):
            for f in range(place.spans[2]):
                line = self.line(which, place.plane_behind(e, f), place.core)
                if e > 0 or f > 0:
                    self.copy(which, line, line, self.leg_index(e, f), place.other).wait_send()
                self.copy(which, line, line, self.hand_index(e, f), place.other).wait_send()


class Reduce:
    def __init__(self, dims, grads, rooms, sems, results, resident):
        self.dims, self.grads, self.resident = dims, grads, resident
        count = len(grads)
        self.mine, self.swapped, self.third, self.second, self.first = (
            rooms[index * count : (index + 1) * count] for index in range(5)
        )
        self.load_sem, self.swap_send, self.swap_recv, self.send_sem, self.recv_sem = sems[:5]
        self.last_send, self.last_recv = sems[5:]
        self.results = results

    @staticmethod
    def rooms(dims, grads):
        depth, tall, wide = dims
        leads = (
            (tall, wide, depth),
            (depth, tall * wide),
            (tall - 1, wide, depth),
            (wide - 1, depth),
            (depth - 1,),
        )
        return [
            pltpu.VMEM(lead + half_shape(grad.shape[2:]), grad.dtype) for lead in leads for grad in grads
        ]

    @staticmethod
    def sems(count, dims):
        groups = dims[1] * dims[2]
        return (
            [pltpu.SemaphoreType.DMA((count, groups))] * 3
            + [pltpu.SemaphoreType.DMA((count, dims[0] + dims[1] + dims[2]))] * 2
            + [pltpu.SemaphoreType.DMA((count,))] * 2
        )

    def groups(self, place):
        return [
            (e, f)
            for f in range(place.spans[2] - 1, -1, -1)
            for e in range(place.spans[1] - 1, -1, -1)
        ]

    def number(self, e, f):
        return e * self.dims[1] + f

    def block(self, which):
        return self.grads[which].shape[2:]

    def load(self, place, which, e, f):
        return pltpu.make_async_copy(
            half(self.grads[which].at[:, place.plane(e, f)], self.block(which), place.core, 1),
            self.mine[which].at[f, e],
            self.load_sem.at[which, self.number(e, f)],
        )

    def swap(self, place, which, e, f, plane):
        return remote(
            half(self.grads[which].at[:, plane], self.block(which), 1 - place.core, 1),
            self.swapped[which].at[:, plane],
            self.swap_send.at[which, self.number(e, f)],
            self.swap_recv.at[which, self.number(e, f)],
            place.other,
        )

    def hop(self, which, source, target, index, device):
        return remote(
            source, target, self.send_sem.at[which, index], self.recv_sem.at[which, index], device
        )

    def third_hop(self, place, which, f):
        return self.hop(which, self.mine[which].at[f], self.third[which].at[f - 1], f, place.at(0, 0, f))

    def second_hop(self, place, which, e):
        return self.hop(
            which,
            self.mine[which].at[0, e],
            self.second[which].at[e - 1],
            self.dims[1] + e,
            place.at(0, e, 0),
        )

    def first_hop(self, place, which, d):
        return self.hop(
            which,
            self.mine[which].at[0, 0, place.level(d)],
            self.first[which].at[d - 1],
            self.dims[1] + self.dims[2] + d,
            place.at(d, 0, 0),
        )

    def start(self, which):
        place, mirror = Place(self.dims), Place(self.dims, swapped=True)
        for e, f in self.groups(place):
            self.swap(place, which, e, f, mirror.plane(e, f)).start()
            if not self.resident:
                self.load(place, which, e, f).start()

    def parts(self, place, which, e, f, z):
        plane = place.plane(e, f)
        if self.resident:
            found = [half(self.grads[which].at[z, plane], self.block(which), place.core)]
        else:
            found = [self.mine[which].at[f, e, z]]
        found.append(self.swapped[which].at[z, plane])
        if f == 0:
            found += [self.third[which].at[hop - 1, e, z] for hop in range(1, place.spans[2])]
        if f == 0 and e == 0:
            found += [self.second[which].at[hop - 1, z] for hop in range(1, place.spans[1])]
        return found

    def ready(self, place, which, e, f):
        if not self.resident:
            self.load(place, which, e, f).wait()
        self.swap(place, which, e, f, place.plane(e, f)).wait_recv()

    def added(self, parts, store, carry):
        rows = parts[0].shape[0]
        group = min(rows, 16)

        def some(index, carry):
            at_rows = pl.ds(pl.multiple_of(index * group, group), group)
            total = parts[0][at_rows, :].astype(jnp.float32)
            for part in parts[1:]:
                total = total + part[at_rows, :].astype(jnp.float32)
            return store(at_rows, total, carry)

        return lax.fori_loop(0, rows // group, some, carry)

    def sum_into(self, place, which, e, f, z):
        target = self.mine[which].at[f, e, z]

        def keep(at_rows, total, carry):
            target[at_rows, :] = total.astype(target.dtype)
            return carry

        self.added(self.parts(place, which, e, f, z), keep, 0)

    def leg(self, which, number):
        place = Place(self.dims)
        depth, span_e, span_f = place.spans
        if number == 1:
            for f in range(span_f - 1, 0, -1):
                for e in range(span_e - 1, -1, -1):
                    self.ready(place, which, e, f)
                    for z in range(depth):
                        self.sum_into(place, which, e, f, z)
                self.third_hop(place, which, f).start()
        elif number == 2:
            for f in range(1, span_f):
                self.third_hop(place, which, f).wait_recv()
            for e in range(span_e - 1, 0, -1):
                self.ready(place, which, e, 0)
                for z in range(depth):
                    self.sum_into(place, which, e, 0, z)
                self.second_hop(place, which, e).start()
        else:
            self.ready(place, which, 0, 0)
            if span_e == 1:
                for f in range(1, span_f):
                    self.third_hop(place, which, f).wait_recv()
            for e in range(1, span_e):
                self.second_hop(place, which, e).wait_recv()
            for d in range(1, depth):
                self.sum_into(place, which, 0, 0, place.level(d))
                self.first_hop(place, which, d).start()

    def result(self, which, side):
        return half(self.results[which], self.block(which), side)

    def last(self, place, which, side):
        share = self.result(which, side)
        return remote(share, share, self.last_send.at[which], self.last_recv.at[which], place.other)

    def finish(self, which, marks=None):
        place = Place(self.dims)
        parts = self.parts(place, which, 0, 0, place.deep)
        for d in range(1, place.spans[0]):
            self.first_hop(place, which, d).wait_recv()
            parts.append(self.first[which].at[d - 1])
        share = self.result(which, place.core)

        def store(at_rows, total, carry):
            share[at_rows, :] = total
            kept, plain = carry
            squared = total * total
            if marks is not None:
                marked = squared * marks[place.core, at_rows, :]
                plain = plain + folded_squares(marked)
                squared = squared - marked
            return (kept + folded_squares(squared), plain)

        squares = self.added(parts, store, (jnp.zeros((8, lanes), jnp.float32),) * 2)
        self.last(place, which, place.core).start()
        return squares

    def settle(self, which):
        place, mirror = Place(self.dims), Place(self.dims, swapped=True)
        last = self.last(place, which, 1 - place.core)
        last.wait_recv()
        last.wait_send()
        for e, f in self.groups(place):
            self.swap(place, which, e, f, mirror.plane(e, f)).wait_send()
        for f in range(1, place.spans[2]):
            self.third_hop(place, which, f).wait_send()
        for e in range(1, place.spans[1]):
            self.second_hop(place, which, e).wait_send()
        for d in range(1, place.spans[0]):
            self.first_hop(place, which, d).wait_send()


def folded_squares(values):
    total = None
    if values.shape[1] < lanes:
        first = lax.broadcasted_iota(jnp.int32, (values.shape[0], lanes), 1) == 0
        values = jnp.where(first, jnp.sum(values, axis=1, keepdims=True), 0.0)
    for row in range(0, values.shape[0], 8):
        for column in range(0, values.shape[1], lanes):
            piece = values[row : row + 8, column : column + lanes]
            total = piece if total is None else total + piece
    return total


def send_to_all(place, source, landing, send_sem, recv_sem):
    number = landing.shape[0]
    for hop in range(1, number):
        target = lax.rem(place.me + hop, number)
        remote(
            source(target), landing.at[place.me], send_sem.at[hop], recv_sem.at[hop], {"narrow": target}
        ).start()


def sum_of_all(place, own, landing, send_sem, recv_sem):
    number = landing.shape[0]
    landing[place.me] = own
    for hop in range(1, number):
        came = landing.at[lax.rem(place.me + number - hop, number)]
        copy = remote(came, came, send_sem.at[hop], recv_sem.at[hop], place.other)
        copy.wait_recv()
        copy.wait_send()
    total = landing[0]
    for spot in range(1, number):
        total = total + landing[spot]
    return total


def sum_of_cores(place, own, landing, send_sem, recv_sem):
    landing[place.core] = own
    copy = remote(landing.at[place.core], landing.at[place.core], send_sem, recv_sem, place.other)
    copy.start()
    copy.wait()
    return landing[0] + landing[1]


def grid_of(mesh):
    number = mesh.shape["narrow"]
    places = [getattr(device, "coords", None) for device in mesh.devices[0]]
    if all(place is not None for place in places):
        sizes = [len({place[axis] for place in places}) for axis in (2, 1, 0)]
        if sizes[0] * sizes[1] * sizes[2] == number:
            return tuple(sizes)
    side = round((number / 2) ** (1 / 3))
    return (2 * side, side, side) if 2 * side**3 == number else (number, 1, 1)


def plan_of(select_rows, state_size, tap_count, step_rows):
    plan, first = {}, 0
    for name, tall in (
        ("select", select_rows),
        ("decay", state_size),
        ("taps", tap_count),
        ("shift", 1),
        ("bias", 1),
        ("skip", 1),
        ("gain", 1),
    ):
        plan[name] = (first, tall)
        first += tall
    plan["step"] = (lanes, step_rows)
    plan["rows"] = -(-(lanes + step_rows) // 32) * 32
    return plan


def per_device(
    dims,
    tokens,
    cotangent,
    loss_mask,
    seq_lengths,
    norm_gain,
    in_proj,
    conv_weight,
    conv_bias,
    select_proj,
    step_proj,
    step_bias,
    decay_log,
    skip_scale,
    out_proj,
):
    half = jnp.bfloat16
    piece = skip_scale.shape[0]
    gain_piece = norm_gain.shape[0]
    rank, size = step_proj.shape[0], decay_log.shape[0]
    plan = plan_of(select_proj.shape[0], size, conv_weight.shape[0], rank)
    smalls = {
        "select": select_proj,
        "decay": decay_log,
        "taps": conv_weight,
        "shift": conv_bias[None],
        "bias": step_bias[None],
        "skip": skip_scale[None],
        "gain": norm_gain[None],
        "step": step_proj,
    }
    depth, planes = dims[0], dims[1] * dims[2]
    number = depth * planes
    in_rows = in_proj.shape[0]
    rows, model = tokens.shape
    inner = piece * number
    width = 4 * lanes
    blocks = inner // width
    chunks = rows // chunk
    mask_row = loss_mask[None]

    whole = pl.BlockSpec(memory_space=pltpu.VMEM)
    tall = pl.BlockSpec((rows, width), lambda b: (0, b))
    deep = pl.BlockSpec((chunks, chunk, width), lambda b: (0, 0, b))
    lead = pl.BlockSpec((rows, size, width), lambda b: (0, 0, b))
    first_w = pl.BlockSpec((model, width), lambda b: (0, b))
    second_w = pl.BlockSpec((model, width), lambda b: (0, b + blocks))
    out_w = pl.BlockSpec((width, model), lambda b: (b, 0))

    def thin(height):
        return pl.BlockSpec((height, width), lambda b: (0, b))

    def fixed(*dims_of):
        return pl.BlockSpec(dims_of, lambda b: (0,) * len(dims_of))

    scalars = pl.BlockSpec(memory_space=pltpu.SMEM)
    offset_buf = pltpu.VMEM((rows + 8, lanes), jnp.int32)
    packed = thin(plan["rows"])

    pair = (chunks, 2 * chunk, lanes)
    pair = (chunks, 2 * chunk, lanes)
    anywhere = pl.BlockSpec(memory_space=pl.ANY)
    small_half = (2, plan["rows"] // 2, piece)
    in_half = (in_rows, width)
    out_half = (out_proj.shape[0], model // blocks)
    (
        branch,
        signal,
        slope,
        projected,
        flipped,
        normed,
        grad_low,
        write_pair,
        read_pair,
        small,
        gain_value,
        in_blocks,
    ) = compute_call(
        functools.partial(front_kernel, plan, dims, tuple(smalls)),
        "front",
        blocks,
        [scalars, whole, whole, whole] + [whole] * len(smalls) + [fixed(in_rows, inner)],
        [tall, tall, tall] + [whole] * 8 + [anywhere],
        [
            shape((rows, inner)),
            shape((rows, inner), half),
            shape((rows, inner)),
            shape((rows, lanes)),
            shape((model, rows), half),
            shape((rows, model), half),
            shape((rows, model), half),
            shape(pair, half),
            shape(pair, half),
            shape((plan["rows"], inner), half),
            shape((1, model)),
            shape((blocks, depth, planes) + in_half, half),
        ],
        [
            offset_buf,
            pltpu.VMEM((plan["rows"], piece), jnp.float32),
            pltpu.VMEM(small_half, half),
            pltpu.VMEM((blocks,) + in_half, half),
            pltpu.VMEM((depth, planes) + small_half, half),
            pltpu.VMEM((blocks, depth, planes) + in_half, half),
            pltpu.SemaphoreType.DMA((blocks,)),
        ]
        + Gather.sems(blocks + 1, dims),
        4 * rows * model * inner,
        (seq_lengths, tokens, cotangent, mask_row, *smalls.values(), in_proj),
        collective_id=0,
    )
    groups = 2
    part, pieces = rows // groups, chunks // groups
    row_block = pltpu.VMEM((pieces, chunk, width), jnp.float32)
    spread_block = pltpu.VMEM((rows, size, lanes), jnp.float32)
    fold_block = pltpu.VMEM((width // lanes, chunk * chunk, lanes), jnp.float32)

    def by_group(order, *dims_of):
        middle = (0,) * (len(dims_of) - 2)
        return pl.BlockSpec(dims_of, lambda b, g: (order(g),) + middle + (b,))

    def by_token(order, *dims_of):
        return pl.BlockSpec(dims_of, lambda b, g: (order(g),) + (0,) * (len(dims_of) - 1))

    def by_channel(height):
        return pl.BlockSpec((height, width), lambda b, g: (0, b))

    def onward(g):
        return g

    def backward(g):
        return groups - 1 - g

    states, step, core, begins, gate_blocks, out_blocks = compute_call(
        functools.partial(forward_kernel, plan, dims),
        "forward",
        (blocks, groups),
        [
            scalars,
            by_token(onward, part, lanes),
            by_channel(plan["rows"]),
            by_group(onward, part, width),
            whole,
            whole,
            pl.BlockSpec((in_rows, inner), lambda b, g: (0, 1)),
            whole,
        ],
        [
            by_group(onward, part, size, width),
            by_group(onward, pieces, chunk, width),
            by_group(onward, pieces, chunk, width),
            by_group(onward, 1, size, width),
            anywhere,
            anywhere,
        ],
        [
            shape((rows, size, inner)),
            shape((chunks, chunk, inner)),
            shape((chunks, chunk, inner)),
            shape((groups, size, inner)),
            shape((blocks, depth, planes) + in_half, half),
            shape((blocks, depth, planes) + out_half, half),
        ],
        [
            offset_buf,
            pltpu.VMEM((part, width), jnp.float32),
            row_block,
            row_block,
            spread_block,
            spread_block,
            fold_block,
            pltpu.VMEM((size, width), jnp.float32),
            pltpu.VMEM((blocks,) + in_half, half),
            pltpu.VMEM((blocks,) + out_half, half),
        ]
        + Gather.sems(2 * blocks, dims),
        15 * rows * inner * size,
        (seq_lengths, projected, small, signal, write_pair, read_pair, in_proj, out_proj),
        collective_id=2,
    )
    weights = pl.BlockSpec((None, number, in_rows, width), lambda b: (b, 0, 0, 0))
    per_block = width // out_half[0]
    out_pieces = pl.BlockSpec((blocks, per_block) + out_half, lambda b: (0, b, 0, 0))
    branch_whole = in_blocks.reshape(blocks, number, *in_half)
    gate_whole = gate_blocks.reshape(blocks, number, *in_half)
    out_whole = out_blocks.reshape(blocks, number, *out_half)
    core_grad, gate_grad, grad_skip, grad_outw, grad_in_gate, output = compute_call(
        functools.partial(middle_kernel, plan),
        "middle",
        blocks,
        [deep, packed, tall, weights, whole, out_pieces, whole, whole, whole],
        [deep, tall, thin(1), out_w, first_w, fixed(rows, model)],
        [
            shape((chunks, chunk, inner)),
            shape((rows, inner), half),
            shape((1, inner)),
            shape((inner, model), half),
            shape((model, inner), half),
            shape((rows, model), half),
        ],
        [
            pltpu.VMEM((rows, width), jnp.float32),
            pltpu.VMEM((rows, width), jnp.float32),
            pltpu.VMEM((rows, width), half),
            pltpu.VMEM((width, model), half),
            pltpu.VMEM((rows, model), jnp.float32),
        ],
        8 * rows * model * inner,
        (core, small, signal, gate_whole, grad_low, out_whole, flipped, normed, tokens),
    )
    early_grads = [
        grad_outw.reshape((depth, planes) + out_proj.shape),
        grad_in_gate.reshape(depth, planes, in_rows, inner),
    ]
    early_sums = [shape(grad.shape[2:]) for grad in early_grads]
    early_pieces = [shape((depth, planes) + block, half) for block in (in_half, out_half)] * blocks
    (
        signal_grad,
        grad_stepw,
        grad_bias,
        grad_decaylog,
        flat,
        out_sum,
        in_gate_sum,
        early_squares,
    ) = compute_call(
        functools.partial(backward_kernel, plan, dims),
        "backward",
        (blocks, groups),
        [
            scalars,
            by_token(backward, part, lanes),
            by_channel(plan["rows"]),
            by_group(backward, part, width),
            whole,
            whole,
            by_group(backward, pieces, chunk, width),
            by_group(backward, pieces, chunk, width),
            by_group(backward, part, size, width),
            by_group(backward, 1, size, width),
            anywhere,
            anywhere,
        ],
        [
            by_group(backward, part, width),
            by_channel(rank),
            by_channel(1),
            by_channel(size),
            whole,
        ]
        + [whole] * 3,
        [
            shape((rows, inner)),
            shape((rank, inner)),
            shape((1, inner)),
            shape((size, inner)),
            shape((rows, lanes), half),
            *early_sums,
            shape((8, lanes)),
        ],
        [
            offset_buf,
            row_block,
            row_block,
            spread_block,
            spread_block,
            fold_block,
            fold_block,
            row_block,
            row_block,
            pltpu.VMEM((part, width), half),
            pltpu.VMEM((size, width), jnp.float32),
            pltpu.VMEM((chunks, chunk, lanes), jnp.float32),
            spread_block,
            spread_block,
        ]
        + [pltpu.VMEM((blocks,) + block, jnp.float32) for block in (in_half, out_half)]
        + Reduce.rooms(dims, early_pieces)
        + Reduce.sems(2 * blocks, dims),
        40 * rows * inner * size,
        (
            seq_lengths,
            projected,
            small,
            signal,
            write_pair,
            read_pair,
            step,
            core_grad,
            states,
            begins,
            *early_grads,
        ),
        collective_id=3,
    )

    plain_rows = np.zeros((plan["rows"], piece), np.float32)
    for name in ("bias", "decay", "skip"):
        first, count = plan[name]
        plain_rows[first : first + count] = 1.0
    late_grads = [shape((depth, planes) + small_half, half)]
    late_grads += [shape((depth, planes, in_rows, width), half)] * blocks
    taps_n = conv_weight.shape[0]
    late = {"taps": (0, taps_n), "shift": (taps_n, 1), "gain": (taps_n + 1, 1)}
    late_block = (8, piece)

    tokens_grad, in_branch_sum, small_sum, late_sum, norms = compute_call(
        functools.partial(back_kernel, plan, dims),
        "back",
        blocks,
        [scalars, whole, whole, whole, packed, whole, tall, whole, tall, tall, tall, whole]
        + [weights, weights]
        + [whole] * 6,
        [whole] * 5,
        [
            shape((rows, model), half),
            shape((in_rows, inner)),
            shape(small_half),
            shape(late_block),
            shape((2, 8, lanes)),
        ],
        [
            offset_buf,
            pltpu.VMEM((rows + 8, width), jnp.float32),
            pltpu.VMEM((rows, width), half),
            pltpu.VMEM((rows, model), jnp.float32),
            pltpu.VMEM((blocks,) + late_grads[1].shape, half),
            pltpu.VMEM(late_grads[0].shape, late_grads[0].dtype),
            pltpu.VMEM((number,) + late_block, jnp.float32),
            pltpu.VMEM((number,) + late_block, jnp.float32),
            pltpu.VMEM((2,) + late_block, jnp.float32),
            pltpu.VMEM((2, 8, lanes), jnp.float32),
            pltpu.VMEM((number, 2, 8, lanes), jnp.float32),
            pltpu.VMEM((2, 2, 8, lanes), jnp.float32),
            pltpu.VMEM((blocks, in_rows, width), jnp.float32),
            pltpu.VMEM(small_half, jnp.float32),
            pltpu.SemaphoreType.DMA((2, number)),
            pltpu.SemaphoreType.DMA((2, number)),
        ]
        + Reduce.rooms(dims, late_grads)
        + Reduce.sems(blocks + 1, dims),
        8 * rows * model * inner,
        (
            seq_lengths,
            tokens,
            grad_low,
            gain_value,
            small,
            flat,
            branch,
            signal,
            slope,
            signal_grad,
            gate_grad,
            flipped,
            branch_whole,
            gate_whole,
            grad_stepw,
            grad_bias,
            grad_decaylog,
            grad_skip,
            jnp.asarray(plain_rows.reshape(small_half)),
            early_squares,
        ),
        collective_id=1,
    )

    names = ("gain", "taps", "shift", "select", "step", "bias", "decay", "skip")
    own = (norm_gain, conv_weight, conv_bias, select_proj, step_proj, step_bias, decay_log, skip_scale)
    in_grad, out_grad, grad_tokens, gain_grad, *small_grads, decay_sq, plain_sq = pl.pallas_call(
        functools.partial(finish_kernel, plan, names, late),
        in_specs=[whole] * 7,
        out_specs=[whole] * (3 + len(names)) + [scalars] * 2,
        out_shape=[shape(in_proj.shape), shape(out_proj.shape), shape(tokens.shape, half)]
        + [shape(array.shape) for array in own]
        + [shape((1, 1))] * 2,
        name="finish",
    )(
        tokens_grad,
        in_branch_sum,
        in_gate_sum,
        out_sum,
        small_sum.reshape(plan["rows"], piece),
        late_sum,
        norms,
    )
    return (
        output,
        grad_tokens,
        gain_grad,
        in_grad,
        *small_grads,
        out_grad,
        decay_sq[0, 0],
        plain_sq[0, 0],
    )


def solution(mesh):
    placed = (
        P(("wide", "narrow"), None),
        P(("wide", "narrow"), None),
        P(("wide", "narrow")),
        P(("wide", "narrow"), None),
        P("narrow"),
        P("narrow", None),
        P(None, "narrow"),
        P("narrow"),
        P(None, "narrow"),
        P(None, "narrow"),
        P("narrow"),
        P(None, "narrow"),
        P("narrow"),
        P("narrow", None),
    )
    return jax.shard_map(
        functools.partial(per_device, grid_of(mesh)),
        mesh=mesh,
        in_specs=placed,
        out_specs=(
            P(("wide", "narrow"), None),
            P(("wide", "narrow"), None),
            P("narrow"),
            P("narrow", None),
            P(None, "narrow"),
            P("narrow"),
            P(None, "narrow"),
            P(None, "narrow"),
            P("narrow"),
            P(None, "narrow"),
            P("narrow"),
            P("narrow", None),
            P(),
            P(),
        ),
        check_vma=False,
    )
```

```python
import functools
import math

import jax
import jax.numpy as jnp
import numpy as np
from jax import lax
from jax.experimental import pallas as pl
from jax.experimental.pallas import tpu as pltpu
from jax.sharding import PartitionSpec as P

epsilon = 1e-05
chunk = 8
lanes = 128
log2e = math.log2(math.e)
ln2 = math.log(2.0)
far = 1e30


def contract(left, right, left_dim, right_dim):
    return lax.dot_general(
        left, right, (((left_dim,), (right_dim,)), ((), ())), preferred_element_type=jnp.float32
    )


def row_loop(rows, group, body, initial):
    def some(index, carry):
        return body(index, pl.ds(pl.multiple_of(index * group, group), group), carry)

    return lax.fori_loop(0, rows // group, some, initial)


def cut(tile):
    return pl.ds(tile * lanes, lanes)


def sigmoid(values):
    return 0.5 * jnp.tanh(0.5 * values) + 0.5


def softplus(values):
    small = jnp.exp(-jnp.abs(values))
    series = small * (1.0 - small * (0.5 - small * (1.0 / 3.0 - 0.25 * small)))
    return jnp.maximum(values, 0.0) + jnp.where(small < 0.03, series, jnp.log(1.0 + small))


def slope_of(step):
    series = step * (1.0 - step * (0.5 - step * (1.0 / 6.0 - step * (1.0 / 24.0))))
    return jnp.where(step < 0.03, series, 1.0 - jnp.exp(-step))


def fill_offsets(lengths_ref, offset_buf, rows):
    place = lax.broadcasted_iota(jnp.int32, offset_buf.shape, 0)
    start = jnp.zeros(offset_buf.shape, jnp.int32)
    ahead = jnp.int32(0)
    for index in range(lengths_ref.shape[1] - 1):
        ahead = ahead + lengths_ref[0, index]
        start = jnp.where(place >= ahead, ahead, start)
    offset_buf[...] = jnp.where(place < rows, place - start, 0)


def small_rows(small_ref, first, count):
    base = first // 16 * 16
    tall = -(-(first + count - base) // 16) * 16
    return small_ref[base : base + tall, :].astype(jnp.float32)[first - base : first - base + count]


def eight(values):
    total = values[:8]
    for row in range(8, values.shape[0], 8):
        total = total + values[row : row + 8]
    return total


def conv_rows(index, at, group, tile, branch_ref, offset_buf, taps, shift):
    count = taps.shape[0]
    here = slice(tile * lanes, (tile + 1) * lanes)
    current = branch_ref[at, cut(tile)]
    before = branch_ref[pl.ds(pl.multiple_of(jnp.maximum(index * group - 8, 0), 8), 8), cut(tile)]
    both = jnp.concatenate([before, current], axis=0)
    offsets = offset_buf[at, :]
    summed = shift[:, here] + taps[count - 1 : count, here] * current
    for tap in range(count - 1):
        lag = count - 1 - tap
        read = jnp.where(offsets >= lag, pltpu.roll(both, lag, 0)[8:], 0.0)
        summed = summed + taps[tap : tap + 1, here] * read
    return summed


def rows_of(blocks):
    return as_matrix(blocks[...][None])


def as_matrix(blocks):
    columns = blocks.shape[3]
    if blocks.shape[2] % 16:
        return blocks.astype(jnp.float32).reshape(-1, columns).astype(blocks.dtype)
    return blocks.reshape(-1, columns)


def front_kernel(
    plan,
    dims,
    names,
    lengths_ref,
    tokens_ref,
    cotangent_ref,
    mask_ref,
    *refs,
):
    smalls, in_ref, refs = refs[: len(names)], refs[len(names)], refs[len(names) + 1 :]
    branch_ref, signal_ref, slope_ref, projected_ref, flipped_ref, normed_ref, low_ref = refs[:7]
    write_pair, read_pair, small_out, gain_ref, whole_ref = refs[7:12]
    offset_buf, pack_buf, own_small, own_in, land_small, land_in, store_sem = refs[12:19]
    rows = tokens_ref.shape[0]
    width = branch_ref.shape[1]
    block = pl.program_id(0)
    last = whole_ref.shape[0]
    gather = Gather(
        dims,
        [own_small] + [own_in.at[index] for index in range(last)],
        [land_small] + [land_in.at[index] for index in range(last)],
        refs[19:],
    )

    def stored(index):
        return pltpu.make_async_copy(land_in.at[index], whole_ref.at[index], store_sem.at[index])

    @pl.when(block == 0)
    def _():
        pack_buf[...] = jnp.zeros_like(pack_buf)
        for name, ref in zip(names, smalls):
            first, tall = plan[name]
            pack_buf[first : first + tall, : ref.shape[1]] = ref[...]
        tall = pack_buf.shape[0] // 2
        for side in range(2):
            own_small[side] = pack_buf[side * tall : (side + 1) * tall, :].astype(own_small.dtype)
        for index in range(last):
            own_in[index] = in_ref[:, index * width : (index + 1) * width].astype(own_in.dtype)
        Place(dims).greet()
        for index in range(last + 1):
            gather.start(index)
        fill_offsets(lengths_ref, offset_buf, rows)
        down = lax.broadcasted_iota(jnp.int32, (rows, rows), 0)
        along = lax.broadcasted_iota(jnp.int32, (rows, rows), 1)
        diagonal = jnp.where(down == along, mask_ref[...].astype(jnp.float32), 0.0).astype(low_ref.dtype)
        low_ref[...] = jnp.dot(
            diagonal, cotangent_ref[...], preferred_element_type=jnp.float32
        ).astype(low_ref.dtype)
        projected_ref[...] = jnp.zeros_like(projected_ref)
        for which, number in ((0, 1), (1, 1), (0, 2), (1, 2), (2, 1), (0, 3)):
            gather.leg(which, number)
        gather.arrive(0)
        share = land_small.shape[4]
        gains = gain_ref.shape[1] // (land_small.shape[0] * land_small.shape[1])
        gain_row = plan["gain"][0]
        for z in range(land_small.shape[0]):
            for plane in range(land_small.shape[1]):
                owner = z * land_small.shape[1] + plane
                for side in range(2):
                    small_out[side * tall : (side + 1) * tall, owner * share : (owner + 1) * share] = land_small[
                        z, plane, side
                    ]
                side, row = gain_row // tall, gain_row % tall
                base = row // 16 * 16
                some = land_small[z, plane, side, base : base + 16, :].astype(jnp.float32)
                gain_ref[:, owner * gains : (owner + 1) * gains] = some[row - base : row - base + 1, :gains]

        def norm(index, at, carry):
            residual = tokens_ref[at, :].astype(jnp.float32)
            scale = lax.rsqrt(jnp.mean(residual * residual, axis=1, keepdims=True) + epsilon)
            normed_ref[at, :] = (residual * scale * gain_ref[...]).astype(normed_ref.dtype)
            return carry

        row_loop(rows, 16, norm, 0)
        flipped_ref[...] = normed_ref[...].T
        for which, number in ((2, 2), (1, 3), (3, 1)):
            gather.leg(which, number)

    def move_on(plan_of_moves):
        for moment, legs in plan_of_moves:

            @pl.when(block == moment)
            def _(legs=legs):
                for which, number in legs:
                    gather.leg(which, number)

    for index in range(last):

        @pl.when(block == index)
        def _(index=index):
            gather.arrive(index + 1)
            stored(index).start()

    branch_w = as_matrix(land_in[block])
    branch_ref[...] = jnp.dot(normed_ref[...], branch_w, preferred_element_type=jnp.float32)
    move_on(((0, ((3, 2), (4, 1), (2, 3))), (1, ((4, 2), (3, 3))), (2, ((4, 3),))))
    small_ref = small_out.at[:, pl.ds(pl.multiple_of(block * width, width), width)]
    taps = small_rows(small_ref, *plan["taps"])
    shift = small_rows(small_ref, *plan["shift"])

    def some(index, at, carry):
        for tile in range(width // lanes):
            summed = conv_rows(index, at, 32, tile, branch_ref, offset_buf, taps, shift)
            sigma = sigmoid(summed)
            active = summed * sigma
            signal_ref[at, cut(tile)] = active.astype(signal_ref.dtype)
            slope_ref[at, cut(tile)] = sigma + active * (1.0 - sigma)
        return carry

    row_loop(rows, 32, some, 0)
    projected_ref[...] += contract(signal_ref[...], small_ref[:lanes, :], 1, 1)

    @pl.when(block == pl.num_programs(0) - 1)
    def _():
        high, low = high_low(projected_ref[...])
        own = own_tokens(rows)
        rank = plan["step"][1]
        size = plan["decay"][1]
        entry = lax.broadcasted_iota(jnp.int32, (lanes, lanes), 0)
        lane = lax.rem(lax.broadcasted_iota(jnp.int32, (lanes, lanes), 1), size)
        for first, pair in ((rank, write_pair), (rank + size, read_pair)):
            spread = (entry == lane + first).astype(jnp.bfloat16)
            parts = [
                (jnp.dot(part.astype(jnp.bfloat16), spread, preferred_element_type=jnp.float32) * own).reshape(
                    rows // chunk, chunk, lanes
                )
                for part in (high, low)
            ]
            pair[...] = jnp.concatenate(parts, axis=1).astype(pair.dtype)
        for index in range(last + 1):
            gather.drain(index)
        for index in range(last):
            stored(index).wait()


def high_low(values):
    high = values.astype(jnp.bfloat16).astype(jnp.float32)
    return high, values - high


def own_tokens(rows):
    token = lax.rem(lax.broadcasted_iota(jnp.int32, (rows, lanes), 0), chunk)
    return (token == lax.div(lax.broadcasted_iota(jnp.int32, (rows, lanes), 1), lanes // chunk)).astype(
        jnp.float32
    )


def spread_all(pairs, target):
    some = 8

    def spread(index, carry):
        rows = jnp.concatenate([pairs[index * some + number] for number in range(some)], axis=1)
        wide = contract(rows, jnp.ones((rows.shape[0], lanes), rows.dtype), 0, 0)
        target[pl.ds(index * some * chunk, some * chunk)] = wide.reshape(some * chunk, -1, lanes)
        return carry

    lax.fori_loop(0, pairs.shape[0] // some, spread, 0)


def folded(buffer, tile):
    total = buffer[tile, pl.ds(0, chunk, stride=chunk), :]
    for row in range(1, chunk):
        total = total + buffer[tile, pl.ds(row, chunk, stride=chunk), :]
    return total


def forward_kernel(
    plan,
    dims,
    lengths_ref,
    projected_ref,
    small_ref,
    signal_ref,
    write_pair,
    read_pair,
    gate_own,
    out_own,
    states_ref,
    step_ref,
    core_ref,
    begin_ref,
    gate_whole,
    out_whole,
    offset_buf,
    pre_buf,
    decay_step,
    flows,
    write_wide,
    read_wide,
    fold_buf,
    held_buf,
    gate_low,
    out_low,
    *sems,
):
    rows, width = pre_buf.shape
    size = plan["decay"][1]
    half_size = size // 2
    tiles = width // lanes
    chunks = rows // chunk
    rank = plan["step"][1]
    group = pl.program_id(1)
    groups = pl.num_programs(1)
    moment = pl.program_id(0) * groups + group
    moments = pl.num_programs(0) * groups
    pieces = gate_low.shape[0]
    gather = Gather(
        dims,
        [buffer.at[index] for index in range(pieces) for buffer in (gate_low, out_low)],
        [buffer.at[index] for index in range(pieces) for buffer in (gate_whole, out_whole)],
        sems,
    )
    count = 2 * pieces

    @pl.when(moment == 0)
    def _():
        for index in range(pieces):
            for own, low in ((gate_own, gate_low), (out_own, out_low)):
                each = low.shape[2]
                low[index] = own[:, index * each : (index + 1) * each].astype(low.dtype)
        Place(dims).greet()
        for which in range(count):
            gather.start(which)
        fill_offsets(lengths_ref, offset_buf, offset_buf.shape[0] - 8)
        spread_all(write_pair, write_wide)
        spread_all(read_pair, read_wide)

    @pl.when(group == 0)
    def _():
        held_buf[...] = jnp.zeros_like(held_buf)

    begin_ref[0] = held_buf[...]
    pre_buf[...] = jnp.dot(
        projected_ref[:, :rank].astype(small_ref.dtype),
        small_ref[pl.ds(plan["step"][0], rank), :],
        preferred_element_type=jnp.float32,
    )
    bias = small_rows(small_ref, *plan["bias"])

    def before(index, at, carry):
        spot = pl.ds(pl.multiple_of(index * 4, 4), 4)
        inside = offset_buf[pl.ds(pl.multiple_of(group * rows + index * 32, 32), 32), :] > 0
        for tile in range(tiles):
            step = softplus(pre_buf[at, cut(tile)] + bias[:, tile * lanes : (tile + 1) * lanes])
            step_ref[spot, :, cut(tile)] = step.reshape(4, chunk, lanes)
            decay_step[spot, :, cut(tile)] = jnp.where(inside, step, far).reshape(4, chunk, lanes)
            flow = step * signal_ref[at, cut(tile)].astype(jnp.float32)
            flows[spot, :, cut(tile)] = flow.reshape(4, chunk, lanes)
        return carry

    row_loop(rows, 4 * chunk, before, 0)
    rates = -jnp.exp(small_rows(small_ref, *plan["decay"])) * log2e
    rates = [rates[:, tile * lanes : (tile + 1) * lanes] for tile in range(tiles)]

    def forward(index, held):
        held = list(held)
        for place in range(chunk):
            now = index * chunk + place
            write_now = write_wide[group * rows + now]
            read_now = read_wide[group * rows + now]
            for tile in range(tiles):
                decay = jnp.exp2(rates[tile] * decay_step[index, pl.ds(place, 1), cut(tile)])
                fresh = decay * held[tile] + write_now * flows[index, pl.ds(place, 1), cut(tile)]
                held[tile] = fresh
                states_ref[now, :, cut(tile)] = fresh
                product = read_now * fresh
                fold_buf[tile, pl.ds(place * chunk, chunk), :] = product[:half_size] + product[half_size:]
        for tile in range(tiles):
            core_ref[index, :, cut(tile)] = folded(fold_buf, tile)
        return tuple(held)

    held = tuple(held_buf[:, cut(tile)] for tile in range(tiles))
    schedule = {}
    for which in range(count):
        for number in (1, 2, 3):
            schedule.setdefault(min(1 + 2 * (which + number), 2 * 8), []).append((which, number))

    def move_on(legs):
        for which, number in legs:
            gather.leg(which, number)

    for half_loop in range(2):
        for point, legs in sorted(schedule.items()):
            if point < 16 and point % 2 == half_loop:
                pl.when(moment == point // 2)(functools.partial(move_on, legs))
        held = lax.fori_loop(half_loop * chunks // 2, (half_loop + 1) * chunks // 2, forward, held)
    for tile in range(tiles):
        held_buf[:, cut(tile)] = held[tile]

    @pl.when(moment == moments - 1)
    def _():
        move_on(sorted(schedule.get(16, ()), key=sum))
        for which in range(count):
            gather.arrive(which)
        for which in range(count):
            gather.drain(which)


def middle_kernel(
    plan,
    core_ref,
    small_ref,
    signal_ref,
    gate_w,
    low_ref,
    out_w,
    flipped_ref,
    normed_ref,
    tokens_ref,
    core_grad_ref,
    gate_grad_ref,
    skip_grad_ref,
    out_grad_ref,
    in_grad_ref,
    output_ref,
    pre_buf,
    gate_buf,
    gated_buf,
    out_buf,
    total,
):
    rows, width = pre_buf.shape
    tiles = width // lanes
    block = pl.program_id(0)
    each = out_w.shape[3]
    for index in range(out_w.shape[0]):
        out_buf[:, index * each : (index + 1) * each] = as_matrix(out_w[index][None])
    gate_buf[...] = jnp.dot(normed_ref[...], rows_of(gate_w), preferred_element_type=jnp.float32)
    pre_buf[...] = contract(low_ref[...], out_buf[...], 1, 1)
    skip = small_rows(small_ref, *plan["skip"])

    def after(index, at, carry):
        spot = pl.ds(pl.multiple_of(index * 4, 4), 4)
        sums = []
        for tile in range(tiles):
            signal = signal_ref[at, cut(tile)].astype(jnp.float32)
            core = core_ref[spot, :, cut(tile)].reshape(4 * chunk, lanes)
            core = core + skip[:, tile * lanes : (tile + 1) * lanes] * signal
            gate = gate_buf[at, cut(tile)]
            sigma = sigmoid(gate)
            active = gate * sigma
            gated_buf[at, cut(tile)] = (core * active).astype(gated_buf.dtype)
            grad_gated = pre_buf[at, cut(tile)]
            grad_core = grad_gated * active
            core_grad_ref[spot, :, cut(tile)] = grad_core.reshape(4, chunk, lanes)
            slope = sigma + active * (1.0 - sigma)
            gate_grad_ref[at, cut(tile)] = (grad_gated * core * slope).astype(gate_grad_ref.dtype)
            sums.append(carry[tile] + eight(grad_core * signal))
        return tuple(sums)

    zero_rows = jnp.zeros((8, lanes), jnp.float32)
    skips = row_loop(rows, 4 * chunk, after, (zero_rows,) * tiles)
    for tile in range(tiles):
        skip_grad_ref[:, cut(tile)] = jnp.sum(skips[tile], axis=0, keepdims=True)
    out_grad = contract(gated_buf[...], low_ref[...], 0, 0).astype(out_grad_ref.dtype)
    for index in range(out_w.shape[0]):
        out_grad_ref[index] = out_grad[:, index * each : (index + 1) * each]
    in_grad_ref[...] = jnp.dot(
        flipped_ref[...], gate_grad_ref[...], preferred_element_type=jnp.float32
    ).astype(in_grad_ref.dtype)
    piece = jnp.dot(gated_buf[...], out_buf[...], preferred_element_type=jnp.float32)

    @pl.when(block == 0)
    def _():
        total[...] = piece

    @pl.when(block > 0)
    def _():
        total[...] += piece

    @pl.when(block == pl.num_programs(0) - 1)
    def _():
        output_ref[...] = (tokens_ref[...].astype(jnp.float32) + total[...]).astype(output_ref.dtype)


def backward_kernel(
    plan,
    dims,
    lengths_ref,
    projected_ref,
    small_ref,
    signal_ref,
    write_pair,
    read_pair,
    step_ref,
    core_grad_ref,
    states_ref,
    begin_ref,
    out_grad_ref,
    in_grad_ref,
    signal_grad_ref,
    step_w_grad_ref,
    bias_grad_ref,
    decay_grad_ref,
    flat_ref,
    out_sum_ref,
    in_sum_ref,
    square_ref,
    offset_buf,
    decay_step,
    flows,
    write_wide,
    read_wide,
    first_buf,
    second_buf,
    through_buf,
    scaled_buf,
    low_buf,
    incoming_buf,
    rank_buf,
    write_buf,
    read_buf,
    *parts,
):
    rows, width = low_buf.shape
    rank = plan["step"][1]
    size = plan["decay"][1]
    half_size = size // 2
    tiles = width // lanes
    chunks = rows // chunk
    block = pl.program_id(0)
    turn = pl.program_id(1)
    groups = pl.num_programs(1)
    group = groups - 1 - turn
    moment = block * groups + turn
    moments = pl.num_programs(0) * groups
    gate_result, out_result, parts = parts[0], parts[1], parts[2:]
    pieces = gate_result.shape[0]
    count = 2 * pieces

    both = ((in_grad_ref, gate_result), (out_grad_ref, out_result))
    reduce = Reduce(
        dims,
        [ref.at[index] for index in range(pieces) for ref, _ in both],
        parts[: 5 * count],
        parts[5 * count :],
        [result.at[index] for index in range(pieces) for _, result in both],
        False,
    )

    @pl.when(moment == 0)
    def _():
        Place(dims).greet()
        for which in range(count):
            reduce.start(which)
        fill_offsets(lengths_ref, offset_buf, offset_buf.shape[0] - 8)
        spread_all(write_pair, write_wide)
        spread_all(read_pair, read_wide)
        write_buf[...] = jnp.zeros_like(write_buf)
        read_buf[...] = jnp.zeros_like(read_buf)
        rank_buf[...] = jnp.zeros_like(rank_buf)

    @pl.when(turn == 0)
    def _():
        incoming_buf[...] = jnp.zeros_like(incoming_buf)
        decay_grad_ref[...] = jnp.zeros_like(decay_grad_ref)
        bias_grad_ref[...] = jnp.zeros_like(bias_grad_ref)
        step_w_grad_ref[...] = jnp.zeros_like(step_w_grad_ref)

    def before(index, at, carry):
        spot = pl.ds(pl.multiple_of(index * 4, 4), 4)
        offsets = offset_buf[pl.ds(pl.multiple_of(group * rows + index * 32, 32), 32), :]
        inside = (offsets > 0).reshape(4, chunk, lanes)
        for tile in range(tiles):
            step = step_ref[spot, :, cut(tile)]
            decay_step[spot, :, cut(tile)] = jnp.where(inside, step, far)
            signal = signal_ref[at, cut(tile)].astype(jnp.float32).reshape(4, chunk, lanes)
            flows[spot, :, cut(tile)] = step * signal
        return carry

    row_loop(rows, 4 * chunk, before, 0)
    rates = -jnp.exp(small_rows(small_ref, *plan["decay"])) * log2e
    rates = [rates[:, tile * lanes : (tile + 1) * lanes] for tile in range(tiles)]

    def backward(position, carried):
        index = chunks - 1 - position
        incoming, decay_sums = list(carried[0]), list(carried[1])
        for place in range(chunk - 1, -1, -1):
            now = index * chunk + place
            token = group * rows + now
            write_now = write_wide[token]
            read_now = read_wide[token]
            read_sum = None
            write_sum = None
            for tile in range(tiles):
                step_now = decay_step[index, pl.ds(place, 1), cut(tile)]
                grad_now = core_grad_ref[index, pl.ds(place, 1), cut(tile)]
                if place > 0:
                    earlier = states_ref[now - 1, :, cut(tile)]
                else:
                    earlier = jnp.where(
                        index > 0, states_ref[jnp.maximum(now - 1, 0), :, cut(tile)], begin_ref[0, :, cut(tile)]
                    )
                grad_state = incoming[tile] + read_now * grad_now
                through_read = states_ref[now, :, cut(tile)] * grad_now
                through_write = grad_state * flows[index, pl.ds(place, 1), cut(tile)]
                read_sum = through_read if read_sum is None else read_sum + through_read
                write_sum = through_write if write_sum is None else write_sum + through_write
                passed = grad_state * write_now
                first_buf[tile, pl.ds(place * chunk, chunk), :] = passed[:half_size] + passed[half_size:]
                leaving = jnp.exp2(rates[tile] * step_now) * grad_state
                incoming[tile] = leaving
                weighted = leaving * earlier
                scaled = weighted * rates[tile]
                second_buf[tile, pl.ds(place * chunk, chunk), :] = scaled[:half_size] + scaled[half_size:]
                decay_sums[tile] = decay_sums[tile] + weighted * step_now
            read_buf[token] += read_sum
            write_buf[token] += write_sum
        for tile in range(tiles):
            through_buf[index, :, cut(tile)] = folded(first_buf, tile)
            scaled_buf[index, :, cut(tile)] = folded(second_buf, tile)
        return (tuple(incoming), tuple(decay_sums))

    incoming = tuple(incoming_buf[:, cut(tile)] for tile in range(tiles))
    nothing = (jnp.zeros((size, lanes), jnp.float32),) * tiles
    schedule = {}
    for which in range(count):
        for number in (1, 2, 3):
            schedule.setdefault(which + which // 3 + 2 * number - 1, []).append((which, number))

    def move_on(legs):
        for which, number in legs:
            reduce.leg(which, number)

    carried = (incoming, nothing)
    for half_loop in range(2):
        for point, legs in sorted(schedule.items()):
            if point % 2 == half_loop:
                pl.when(moment == point // 2)(functools.partial(move_on, legs))
        carried = lax.fori_loop(half_loop * chunks // 2, (half_loop + 1) * chunks // 2, backward, carried)
    incoming, decay_sums = carried
    for tile in range(tiles):
        incoming_buf[:, cut(tile)] = incoming[tile]
        decay_grad_ref[:, cut(tile)] += decay_sums[tile] * rates[tile] * ln2
    skip = small_rows(small_ref, *plan["skip"])

    def after(index, at, carry):
        spot = pl.ds(pl.multiple_of(index * 4, 4), 4)
        sums = []
        for tile in range(tiles):
            signal = signal_ref[at, cut(tile)].astype(jnp.float32)
            step = step_ref[spot, :, cut(tile)].reshape(4 * chunk, lanes)
            through = through_buf[spot, :, cut(tile)].reshape(4 * chunk, lanes)
            scaled = scaled_buf[spot, :, cut(tile)].reshape(4 * chunk, lanes)
            core_grad = core_grad_ref[spot, :, cut(tile)].reshape(4 * chunk, lanes)
            grad_pre = (through * signal + ln2 * scaled) * slope_of(step)
            low_buf[at, cut(tile)] = grad_pre.astype(low_buf.dtype)
            signal_grad_ref[at, cut(tile)] = (
                through * step + skip[:, tile * lanes : (tile + 1) * lanes] * core_grad
            )
            sums.append(carry[tile] + eight(grad_pre))
        return tuple(sums)

    zero_rows = jnp.zeros((8, lanes), jnp.float32)
    sums = row_loop(rows, 4 * chunk, after, (zero_rows,) * tiles)
    for tile in range(tiles):
        bias_grad_ref[:, cut(tile)] += jnp.sum(sums[tile], axis=0, keepdims=True)
    step_w_grad_ref[...] += contract(
        projected_ref[:, :rank].astype(low_buf.dtype), low_buf[...], 0, 0
    )
    step_w = small_ref[pl.ds(plan["step"][0], rank), :]
    step_w = jnp.concatenate([step_w, jnp.zeros((lanes - rank, width), step_w.dtype)], axis=0)
    rank_buf[pl.ds(group * chunks, chunks)] += contract(low_buf[...], step_w, 1, 1).reshape(
        chunks, chunk, lanes
    )

    @pl.when(moment == moments - 1)
    def _():
        squares = jnp.zeros((8, lanes), jnp.float32)
        for which in range(count):
            squares = squares + reduce.finish(which)[0]
        square_ref[...] = squares
        some = 8
        entry = lax.rem(lax.broadcasted_iota(jnp.int32, (some * chunk * size, lanes), 0), size)
        target = lax.broadcasted_iota(jnp.int32, (some * chunk * size, lanes), 1)
        ones = jnp.ones((lanes, lanes), jnp.bfloat16)

        def lay(index, carry):
            lot = pl.ds(index * some * chunk, some * chunk)
            for number, buffer in enumerate((write_buf, read_buf)):
                high, low = high_low(buffer[lot].reshape(some * chunk * size, lanes))
                summed = jnp.dot(high.astype(jnp.bfloat16), ones, preferred_element_type=jnp.float32)
                summed += jnp.dot(low.astype(jnp.bfloat16), ones, preferred_element_type=jnp.float32)
                summed = jnp.where(target == entry + rank + number * size, summed, 0.0)
                summed = jnp.sum(summed.reshape(some * chunk, size, lanes), axis=1)
                rank_buf[pl.ds(index * some, some)] += summed.reshape(some, chunk, lanes)
            return carry

        lax.fori_loop(0, rank_buf.shape[0] // some, lay, 0)
        flat_ref[...] = rank_buf[...].reshape(flat_ref.shape).astype(flat_ref.dtype)
        for which in range(count):
            reduce.settle(which)
        for index in range(pieces):
            for target, result in ((out_sum_ref, out_result), (in_sum_ref, gate_result)):
                each = result.shape[2]
                target[:, index * each : (index + 1) * each] = result[index]


def back_kernel(
    plan,
    dims,
    lengths_ref,
    tokens_ref,
    low_ref,
    gain_ref,
    small_ref,
    flat_ref,
    branch_ref,
    signal_ref,
    slope_ref,
    signal_grad_ref,
    gate_grad_ref,
    flipped_ref,
    branch_w,
    gate_w,
    step_w_grad_ref,
    bias_grad_ref,
    decay_grad_ref,
    skip_grad_ref,
    plain_ref,
    earlier_ref,
    tokens_grad_ref,
    in_sum_ref,
    small_sum_ref,
    late_sum_ref,
    norm_ref,
    offset_buf,
    conv_buf,
    mixed_buf,
    total,
    in_stage,
    small_stage,
    late_stage,
    late_land,
    late_cores,
    norm_own,
    norm_land,
    norm_cores,
    in_result,
    small_result,
    direct_send,
    direct_recv,
    *parts,
):
    rows = tokens_ref.shape[0]
    width = branch_ref.shape[1]
    tiles = width // lanes
    block = pl.program_id(0)
    last = in_stage.shape[0]
    count = last + 1
    reduce = Reduce(
        dims,
        [small_stage] + [in_stage.at[index] for index in range(last)],
        parts[: 5 * count],
        parts[5 * count :],
        [small_result] + [in_result.at[index] for index in range(last)],
        True,
    )
    share = small_stage.shape[4]
    half_rows = small_stage.shape[3]
    planes = small_stage.shape[1]
    owners = small_stage.shape[0] * planes

    @pl.when(block == 0)
    def _():
        Place(dims).greet(everyone=True)
        select_grad = contract(flat_ref[...], signal_ref[...], 0, 0)
        step_first, step_tall = plan["step"]
        filler = jnp.zeros((2 * half_rows - step_first - step_tall, select_grad.shape[1]), jnp.float32)
        pieces = {
            "decay": decay_grad_ref[...],
            "bias": bias_grad_ref[...],
            "skip": skip_grad_ref[...],
            "step": step_w_grad_ref[...],
        }
        first = plan["select"][1]
        rows_now = [select_grad[:first]]
        for name in ("decay", "taps", "shift", "bias", "skip", "gain"):
            tall = plan[name][1]
            rows_now.append(
                pieces[name] if name in pieces else jnp.zeros((tall, select_grad.shape[1]), jnp.float32)
            )
            first += tall
        rows_now.append(jnp.zeros((step_first - first, select_grad.shape[1]), jnp.float32))
        rows_now.append(pieces["step"])
        if filler.shape[0]:
            rows_now.append(filler)
        everything = jnp.concatenate(rows_now, axis=0)
        for owner in range(owners):
            for side in range(2):
                small_stage[owner // planes, owner % planes, side] = everything[
                    side * half_rows : (side + 1) * half_rows, owner * share : (owner + 1) * share
                ].astype(small_stage.dtype)
        reduce.start(0)
        fill_offsets(lengths_ref, offset_buf, rows)

    taps = small_rows(small_ref, *plan["taps"])
    taps_count = taps.shape[0]
    conv_buf[pl.ds(0, rows), :] = signal_grad_ref[...] + jnp.dot(
        flat_ref[...], small_ref[:lanes, :], preferred_element_type=jnp.float32
    )
    conv_buf[pl.ds(rows, 8), :] = jnp.zeros((8, width), jnp.float32)

    def through_conv(index, at, carry):
        sums = []
        for tile in range(tiles):
            grad_conv = conv_buf[at, cut(tile)] * slope_ref[at, cut(tile)]
            conv_buf[at, cut(tile)] = grad_conv
            sums.append(carry[tile] + eight(grad_conv))
        return tuple(sums)

    zero_rows = jnp.zeros((8, lanes), jnp.float32)
    shift_sums = row_loop(rows, 32, through_conv, (zero_rows,) * tiles)

    def move_on(plan_of_moves):
        for moment, legs in plan_of_moves:

            @pl.when(block == moment)
            def _(legs=legs):
                for which, number in legs:
                    reduce.leg(which, number)

    move_on(((0, ((0, 1),)), (1, ((1, 1),)), (2, ((2, 1),)), (3, ((3, 1),))))

    def to_branch(index, at, carry):
        longer = pl.ds(pl.multiple_of(index * 32, 32), 40)
        offsets = offset_buf[longer, :]
        result = []
        for tile in range(tiles):
            here = slice(tile * lanes, (tile + 1) * lanes)
            grads = conv_buf[longer, cut(tile)]
            branch = branch_ref[at, cut(tile)]
            summed = taps[taps_count - 1 : taps_count, here] * grads[:32]
            sums = [None] * taps_count
            sums[taps_count - 1] = carry[tile][taps_count - 1] + eight(branch * grads[:32])
            for tap in range(taps_count - 1):
                lag = taps_count - 1 - tap
                moved = pltpu.roll(jnp.where(offsets >= lag, grads, 0.0), 40 - lag, 0)[:32]
                summed = summed + taps[tap : tap + 1, here] * moved
                sums[tap] = carry[tile][tap] + eight(branch * moved)
            mixed_buf[at, cut(tile)] = summed.astype(mixed_buf.dtype)
            result.append(tuple(sums))
        return tuple(result)

    sums = row_loop(rows, 32, to_branch, ((zero_rows,) * taps_count,) * tiles)
    late = [
        jnp.concatenate(
            [jnp.sum(sums[tile][tap], axis=0, keepdims=True) for tap in range(taps_count)]
            + [jnp.sum(shift_sums[tile], axis=0, keepdims=True)]
            + [jnp.zeros((8 - taps_count - 1, lanes), jnp.float32)],
            axis=0,
        )
        for tile in range(tiles)
    ]
    late = jnp.concatenate(late, axis=1)
    for piece in range(width // share):
        late_stage[block * (width // share) + piece] = late[:, piece * share : (piece + 1) * share]
    in_grad = jnp.dot(flipped_ref[...], mixed_buf[...], preferred_element_type=jnp.float32)
    in_stage[block] = in_grad.reshape(in_stage.shape[1:]).astype(in_stage.dtype)
    for index in range(last):

        @pl.when(block == index)
        def _(index=index):
            reduce.start(index + 1)

    grad_normed_piece = contract(mixed_buf[...], rows_of(branch_w), 1, 1)
    grad_normed_piece += contract(gate_grad_ref[...], rows_of(gate_w), 1, 1)

    @pl.when(block == 0)
    def _():
        total[...] = grad_normed_piece

    @pl.when(block > 0)
    def _():
        total[...] += grad_normed_piece

    move_on(((0, ((0, 2),)), (1, ((0, 3), (1, 2))), (2, ((2, 2), (1, 3))), (3, ((3, 2), (2, 3)))))

    @pl.when(block == pl.num_programs(0) - 1)
    def _():
        def finish(index, at, carry):
            residual = tokens_ref[at, :].astype(jnp.float32)
            scale = lax.rsqrt(jnp.mean(residual * residual, axis=1, keepdims=True) + epsilon)
            grad_normed = total[at, :]
            weighted = grad_normed * gain_ref[...]
            inner = jnp.mean(weighted * residual, axis=1, keepdims=True)
            grad_y = low_ref[at, :].astype(jnp.float32)
            result = grad_y + (scale * weighted - residual * (scale * scale * scale) * inner)
            tokens_grad_ref[at, :] = result.astype(tokens_grad_ref.dtype)
            return carry + eight(grad_normed * residual * scale)

        gains = row_loop(rows, 16, finish, jnp.zeros((8, total.shape[1]), jnp.float32))
        gains = jnp.sum(gains, axis=0, keepdims=True)
        place = Place(dims)
        each = gains.shape[1] // owners
        for owner in range(owners):
            late_stage[owner, taps_count + 1 : taps_count + 2, :each] = gains[
                :, owner * each : (owner + 1) * each
            ]
        late_sems = direct_send.at[0], direct_recv.at[0]
        norm_sems = direct_send.at[1], direct_recv.at[1]
        send_to_all(place, lambda target: late_stage.at[target], late_land, *late_sems)
        for which, number in ((4, 1), (3, 3), (4, 2)):
            reduce.leg(which, number)
        late_sum = sum_of_all(place, late_stage[place.me], late_land, *late_sems)
        late_sum = sum_of_cores(place, late_sum, late_cores, direct_send.at[0, 0], direct_recv.at[0, 0])
        late_sum_ref[...] = late_sum
        reduce.leg(4, 3)
        kept = earlier_ref[...] + folded_squares(late_sum * late_sum) * (1 - place.core).astype(jnp.float32)
        more, plain = reduce.finish(0, plain_ref)
        kept = kept + more
        for index in range(1, count):
            kept = kept + reduce.finish(index)[0]
        norm_own[...] = jnp.stack([kept, plain])
        send_to_all(place, lambda target: norm_own, norm_land, *norm_sems)
        norms = sum_of_all(place, norm_own[...], norm_land, *norm_sems)
        norm_ref[...] = sum_of_cores(place, norms, norm_cores, direct_send.at[1, 0], direct_recv.at[1, 0])
        for index in range(count):
            reduce.settle(index)
        for index in range(last):
            in_sum_ref[:, index * width : (index + 1) * width] = in_result[index]
        small_sum_ref[...] = small_result[...]


def finish_kernel(
    plan, names, late, tokens_ref, branch_ref, gate_ref, out_ref, small_ref, late_ref, norm_ref, *outs
):
    middle = branch_ref.shape[1]
    outs[0][:, :middle] = branch_ref[...]
    outs[0][:, middle:] = gate_ref[...]
    outs[1][...] = out_ref[...]
    outs[2][...] = tokens_ref[...]
    for name, target in zip(names, outs[3 : 3 + len(names)]):
        source, (first, count) = (late_ref, late[name]) if name in late else (small_ref, plan[name])
        if len(target.shape) == 1:
            target[...] = source[first, : target.shape[0]]
        else:
            target[...] = source[first : first + count, :]
    for index in range(2):
        outs[3 + len(names) + index][0, 0] = jnp.sum(norm_ref[index])


def shape(dims, kind=jnp.float32):
    return jax.ShapeDtypeStruct(dims, kind)


def compute_call(
    kernel, name, blocks, in_specs, out_specs, out_shape, scratch, flops, operands, collective_id=None
):
    return pl.pallas_call(
        kernel,
        grid=blocks if isinstance(blocks, tuple) else (blocks,),
        in_specs=in_specs,
        out_specs=out_specs,
        out_shape=out_shape,
        scratch_shapes=scratch,
        compiler_params=pltpu.CompilerParams(
            dimension_semantics=("arbitrary",) * (len(blocks) if isinstance(blocks, tuple) else 1),
            vmem_limit_bytes=62 * 1024 * 1024,
            collective_id=collective_id,
            has_side_effects=collective_id is not None,
        ),
        cost_estimate=pl.CostEstimate(flops=flops, bytes_accessed=40 << 20, transcendentals=0),
        name=name,
    )(*operands)


class Place:
    def __init__(self, dims, swapped=False):
        depth, tall, wide = dims
        self.dims = dims
        self.core = lax.axis_index("wide")
        self.me = lax.axis_index("narrow")
        self.across = lax.rem(self.me, wide)
        self.up = lax.rem(lax.div(self.me, wide), tall)
        self.deep = lax.div(self.me, wide * tall)
        side = 1 - self.core if swapped else self.core
        turn = side if tall == wide else 0
        self.second = (1 + turn * (wide - 1), self.across + turn * (self.up - self.across), wide)
        self.third = (wide - turn * (wide - 1), self.up + turn * (self.across - self.up), tall)
        self.spans = (depth, wide, tall)
        self.other = {"wide": 1 - self.core}

    def level(self, d):
        return lax.rem(self.deep + d, self.spans[0])

    def plane(self, e, f):
        return (
            lax.rem(self.second[1] + e, self.second[2]) * self.second[0]
            + lax.rem(self.third[1] + f, self.third[2]) * self.third[0]
        )

    def plane_behind(self, e, f):
        return self.plane((self.spans[1] - e) % self.spans[1], (self.spans[2] - f) % self.spans[2])

    def at(self, d, e, f):
        return {"narrow": self.level(d) * (self.dims[1] * self.dims[2]) + self.plane(e, f)}

    def greet(self, everyone=False):
        barrier = pltpu.get_barrier_semaphore()
        peers = [self.other]
        if everyone:
            number = self.spans[0] * self.spans[1] * self.spans[2]
            peers += [{"narrow": lax.rem(self.me + hop, number)} for hop in range(1, number)]
        else:
            for axis, size in enumerate(self.spans):
                for hop in range(1, size):
                    move = [0, 0, 0]
                    move[axis] = hop
                    peers.append(self.at(*move))
        for peer in peers:
            pl.semaphore_signal(barrier, inc=1, device_id=peer, device_id_type=pl.DeviceIdType.MESH)
        pl.semaphore_wait(barrier, len(peers))


def by_rows(block):
    return block[0] % 32 == 0


def half_shape(block):
    if len(block) == 3:
        return tuple(block[1:])
    return (block[0] // 2, block[1]) if by_rows(block) else (block[0], block[1] // 2)


def half(view, block, side, lead=0):
    ahead = (slice(None),) * lead
    if len(block) == 3:
        return view.at[ahead + (side,)]
    if by_rows(block):
        return view.at[ahead + (pl.ds(pl.multiple_of(side * (block[0] // 2), 16), block[0] // 2),)]
    columns = pl.ds(pl.multiple_of(side * (block[1] // 2), lanes), block[1] // 2)
    return view.at[ahead + (slice(None), columns)]


def remote(source, target, send_sem, recv_sem, device):
    return pltpu.make_async_remote_copy(
        src_ref=source,
        dst_ref=target,
        send_sem=send_sem,
        recv_sem=recv_sem,
        device_id=device,
        device_id_type=pl.DeviceIdType.MESH,
    )


class Gather:
    def __init__(self, dims, own, whole, sems):
        self.dims, self.own, self.whole = dims, own, whole
        self.local_sem, self.send_sem, self.recv_sem = sems

    @staticmethod
    def sems(count, dims):
        copies = dims[0] + 2 * dims[1] * dims[2]
        return [pltpu.SemaphoreType.DMA((count,))] + [pltpu.SemaphoreType.DMA((count, copies))] * 2

    def line(self, which, plane, side):
        return half(self.whole[which].at[:, plane], self.own[which].shape, side, 1)

    def local(self, place, which):
        block = self.own[which].shape
        return pltpu.make_async_copy(
            half(self.own[which], block, place.core),
            half(self.whole[which].at[place.deep, place.plane(0, 0)], block, place.core),
            self.local_sem.at[which],
        )

    def copy(self, which, source, target, index, device):
        return remote(
            source, target, self.send_sem.at[which, index], self.recv_sem.at[which, index], device
        )

    def rise(self, place, which, hop):
        block = self.own[which].shape
        return self.copy(
            which,
            half(self.own[which], block, place.core),
            half(self.whole[which].at[place.deep, place.plane(0, 0)], block, place.core),
            hop,
            place.at(hop, 0, 0),
        )

    def leg_index(self, e, f):
        return self.dims[0] + e * self.dims[1] + f

    def hand_index(self, e, f):
        return self.leg_index(e, f) + self.dims[1] * self.dims[2]

    def onward(self, place, which, e, f):
        line = self.line(which, place.plane_behind(e, f), place.core)
        if f == 0:
            for hop in range(1, place.spans[2]):
                self.copy(which, line, line, self.leg_index(e, hop), place.at(0, 0, hop)).start()
        if f == 0 and e == 0:
            for hop in range(1, place.spans[1]):
                self.copy(which, line, line, self.leg_index(hop, 0), place.at(0, hop, 0)).start()
        self.copy(which, line, line, self.hand_index(e, f), place.other).start()

    def start(self, which):
        place = Place(self.dims)
        for hop in range(1, place.spans[0]):
            self.rise(place, which, hop).start()
        self.local(place, which).start()

    def leg(self, which, number):
        place = Place(self.dims)
        if number == 1:
            self.local(place, which).wait()
            for hop in range(1, place.spans[0]):
                self.rise(place, which, hop).wait_recv()
            self.onward(place, which, 0, 0)
            return
        for e in range(place.spans[1]):
            for f in range(place.spans[2]):
                if (number == 2 and f == 0 and e > 0) or (number == 3 and f > 0):
                    line = self.line(which, place.plane_behind(e, f), place.core)
                    self.copy(which, line, line, self.leg_index(e, f), place.other).wait_recv()
                    self.onward(place, which, e, f)

    def arrive(self, which):
        place, mirror = Place(self.dims), Place(self.dims, swapped=True)
        for e in range(place.spans[1]):
            for f in range(place.spans[2]):
                line = self.line(which, mirror.plane_behind(e, f), 1 - place.core)
                self.copy(which, line, line, self.hand_index(e, f), place.other).wait_recv()

    def drain(self, which):
        place = Place(self.dims)
        for hop in range(1, place.spans[0]):
            self.rise(place, which, hop).wait_send()
        for e in range(place.spans[1]):
            for f in range(place.spans[2]):
                line = self.line(which, place.plane_behind(e, f), place.core)
                if e > 0 or f > 0:
                    self.copy(which, line, line, self.leg_index(e, f), place.other).wait_send()
                self.copy(which, line, line, self.hand_index(e, f), place.other).wait_send()


class Reduce:
    def __init__(self, dims, grads, rooms, sems, results, resident):
        self.dims, self.grads, self.resident = dims, grads, resident
        count = len(grads)
        self.mine, self.swapped, self.third, self.second, self.first = (
            rooms[index * count : (index + 1) * count] for index in range(5)
        )
        self.load_sem, self.swap_send, self.swap_recv, self.send_sem, self.recv_sem = sems[:5]
        self.last_send, self.last_recv = sems[5:]
        self.results = results

    @staticmethod
    def rooms(dims, grads):
        depth, tall, wide = dims
        leads = (
            (tall, wide, depth),
            (depth, tall * wide),
            (tall - 1, wide, depth),
            (wide - 1, depth),
            (depth - 1,),
        )
        return [
            pltpu.VMEM(lead + half_shape(grad.shape[2:]), grad.dtype) for lead in leads for grad in grads
        ]

    @staticmethod
    def sems(count, dims):
        groups = dims[1] * dims[2]
        return (
            [pltpu.SemaphoreType.DMA((count, groups))] * 3
            + [pltpu.SemaphoreType.DMA((count, dims[0] + dims[1] + dims[2]))] * 2
            + [pltpu.SemaphoreType.DMA((count,))] * 2
        )

    def groups(self, place):
        return [
            (e, f)
            for f in range(place.spans[2] - 1, -1, -1)
            for e in range(place.spans[1] - 1, -1, -1)
        ]

    def number(self, e, f):
        return e * self.dims[1] + f

    def block(self, which):
        return self.grads[which].shape[2:]

    def load(self, place, which, e, f):
        return pltpu.make_async_copy(
            half(self.grads[which].at[:, place.plane(e, f)], self.block(which), place.core, 1),
            self.mine[which].at[f, e],
            self.load_sem.at[which, self.number(e, f)],
        )

    def swap(self, place, which, e, f, plane):
        return remote(
            half(self.grads[which].at[:, plane], self.block(which), 1 - place.core, 1),
            self.swapped[which].at[:, plane],
            self.swap_send.at[which, self.number(e, f)],
            self.swap_recv.at[which, self.number(e, f)],
            place.other,
        )

    def hop(self, which, source, target, index, device):
        return remote(
            source, target, self.send_sem.at[which, index], self.recv_sem.at[which, index], device
        )

    def third_hop(self, place, which, f):
        return self.hop(which, self.mine[which].at[f], self.third[which].at[f - 1], f, place.at(0, 0, f))

    def second_hop(self, place, which, e):
        return self.hop(
            which,
            self.mine[which].at[0, e],
            self.second[which].at[e - 1],
            self.dims[1] + e,
            place.at(0, e, 0),
        )

    def first_hop(self, place, which, d):
        return self.hop(
            which,
            self.mine[which].at[0, 0, place.level(d)],
            self.first[which].at[d - 1],
            self.dims[1] + self.dims[2] + d,
            place.at(d, 0, 0),
        )

    def start(self, which):
        place, mirror = Place(self.dims), Place(self.dims, swapped=True)
        for e, f in self.groups(place):
            self.swap(place, which, e, f, mirror.plane(e, f)).start()
            if not self.resident:
                self.load(place, which, e, f).start()

    def parts(self, place, which, e, f, z):
        plane = place.plane(e, f)
        if self.resident:
            found = [half(self.grads[which].at[z, plane], self.block(which), place.core)]
        else:
            found = [self.mine[which].at[f, e, z]]
        found.append(self.swapped[which].at[z, plane])
        if f == 0:
            found += [self.third[which].at[hop - 1, e, z] for hop in range(1, place.spans[2])]
        if f == 0 and e == 0:
            found += [self.second[which].at[hop - 1, z] for hop in range(1, place.spans[1])]
        return found

    def ready(self, place, which, e, f):
        if not self.resident:
            self.load(place, which, e, f).wait()
        self.swap(place, which, e, f, place.plane(e, f)).wait_recv()

    def added(self, parts, store, carry):
        rows = parts[0].shape[0]
        group = min(rows, 16)

        def some(index, carry):
            at_rows = pl.ds(pl.multiple_of(index * group, group), group)
            total = parts[0][at_rows, :].astype(jnp.float32)
            for part in parts[1:]:
                total = total + part[at_rows, :].astype(jnp.float32)
            return store(at_rows, total, carry)

        return lax.fori_loop(0, rows // group, some, carry)

    def sum_into(self, place, which, e, f, z):
        target = self.mine[which].at[f, e, z]

        def keep(at_rows, total, carry):
            target[at_rows, :] = total.astype(target.dtype)
            return carry

        self.added(self.parts(place, which, e, f, z), keep, 0)

    def leg(self, which, number):
        place = Place(self.dims)
        depth, span_e, span_f = place.spans
        if number == 1:
            for f in range(span_f - 1, 0, -1):
                for e in range(span_e - 1, -1, -1):
                    self.ready(place, which, e, f)
                    for z in range(depth):
                        self.sum_into(place, which, e, f, z)
                self.third_hop(place, which, f).start()
        elif number == 2:
            for f in range(1, span_f):
                self.third_hop(place, which, f).wait_recv()
            for e in range(span_e - 1, 0, -1):
                self.ready(place, which, e, 0)
                for z in range(depth):
                    self.sum_into(place, which, e, 0, z)
                self.second_hop(place, which, e).start()
        else:
            self.ready(place, which, 0, 0)
            if span_e == 1:
                for f in range(1, span_f):
                    self.third_hop(place, which, f).wait_recv()
            for e in range(1, span_e):
                self.second_hop(place, which, e).wait_recv()
            for d in range(1, depth):
                self.sum_into(place, which, 0, 0, place.level(d))
                self.first_hop(place, which, d).start()

    def result(self, which, side):
        return half(self.results[which], self.block(which), side)

    def last(self, place, which, side):
        share = self.result(which, side)
        return remote(share, share, self.last_send.at[which], self.last_recv.at[which], place.other)

    def finish(self, which, marks=None):
        place = Place(self.dims)
        parts = self.parts(place, which, 0, 0, place.deep)
        for d in range(1, place.spans[0]):
            self.first_hop(place, which, d).wait_recv()
            parts.append(self.first[which].at[d - 1])
        share = self.result(which, place.core)

        def store(at_rows, total, carry):
            share[at_rows, :] = total
            kept, plain = carry
            squared = total * total
            if marks is not None:
                marked = squared * marks[place.core, at_rows, :]
                plain = plain + folded_squares(marked)
                squared = squared - marked
            return (kept + folded_squares(squared), plain)

        squares = self.added(parts, store, (jnp.zeros((8, lanes), jnp.float32),) * 2)
        self.last(place, which, place.core).start()
        return squares

    def settle(self, which):
        place, mirror = Place(self.dims), Place(self.dims, swapped=True)
        last = self.last(place, which, 1 - place.core)
        last.wait_recv()
        last.wait_send()
        for e, f in self.groups(place):
            self.swap(place, which, e, f, mirror.plane(e, f)).wait_send()
        for f in range(1, place.spans[2]):
            self.third_hop(place, which, f).wait_send()
        for e in range(1, place.spans[1]):
            self.second_hop(place, which, e).wait_send()
        for d in range(1, place.spans[0]):
            self.first_hop(place, which, d).wait_send()


def folded_squares(values):
    total = None
    if values.shape[1] < lanes:
        first = lax.broadcasted_iota(jnp.int32, (values.shape[0], lanes), 1) == 0
        values = jnp.where(first, jnp.sum(values, axis=1, keepdims=True), 0.0)
    for row in range(0, values.shape[0], 8):
        for column in range(0, values.shape[1], lanes):
            piece = values[row : row + 8, column : column + lanes]
            total = piece if total is None else total + piece
    return total


def send_to_all(place, source, landing, send_sem, recv_sem):
    number = landing.shape[0]
    for hop in range(1, number):
        target = lax.rem(place.me + hop, number)
        remote(
            source(target), landing.at[place.me], send_sem.at[hop], recv_sem.at[hop], {"narrow": target}
        ).start()


def sum_of_all(place, own, landing, send_sem, recv_sem):
    number = landing.shape[0]
    landing[place.me] = own
    for hop in range(1, number):
        came = landing.at[lax.rem(place.me + number - hop, number)]
        copy = remote(came, came, send_sem.at[hop], recv_sem.at[hop], place.other)
        copy.wait_recv()
        copy.wait_send()
    total = landing[0]
    for spot in range(1, number):
        total = total + landing[spot]
    return total


def sum_of_cores(place, own, landing, send_sem, recv_sem):
    landing[place.core] = own
    copy = remote(landing.at[place.core], landing.at[place.core], send_sem, recv_sem, place.other)
    copy.start()
    copy.wait()
    return landing[0] + landing[1]


def grid_of(mesh):
    number = mesh.shape["narrow"]
    places = [getattr(device, "coords", None) for device in mesh.devices[0]]
    if all(place is not None for place in places):
        sizes = [len({place[axis] for place in places}) for axis in (2, 1, 0)]
        if sizes[0] * sizes[1] * sizes[2] == number:
            return tuple(sizes)
    side = round((number / 2) ** (1 / 3))
    return (2 * side, side, side) if 2 * side**3 == number else (number, 1, 1)


def plan_of(select_rows, state_size, tap_count, step_rows):
    plan, first = {}, 0
    for name, tall in (
        ("select", select_rows),
        ("decay", state_size),
        ("taps", tap_count),
        ("shift", 1),
        ("bias", 1),
        ("skip", 1),
        ("gain", 1),
    ):
        plan[name] = (first, tall)
        first += tall
    plan["step"] = (lanes, step_rows)
    plan["rows"] = -(-(lanes + step_rows) // 32) * 32
    return plan


def per_device(
    dims,
    tokens,
    cotangent,
    loss_mask,
    seq_lengths,
    norm_gain,
    in_proj,
    conv_weight,
    conv_bias,
    select_proj,
    step_proj,
    step_bias,
    decay_log,
    skip_scale,
    out_proj,
):
    half = jnp.bfloat16
    piece = skip_scale.shape[0]
    gain_piece = norm_gain.shape[0]
    rank, size = step_proj.shape[0], decay_log.shape[0]
    plan = plan_of(select_proj.shape[0], size, conv_weight.shape[0], rank)
    smalls = {
        "select": select_proj,
        "decay": decay_log,
        "taps": conv_weight,
        "shift": conv_bias[None],
        "bias": step_bias[None],
        "skip": skip_scale[None],
        "gain": norm_gain[None],
        "step": step_proj,
    }
    depth, planes = dims[0], dims[1] * dims[2]
    number = depth * planes
    in_rows = in_proj.shape[0]
    rows, model = tokens.shape
    inner = piece * number
    width = 4 * lanes
    blocks = inner // width
    chunks = rows // chunk
    mask_row = loss_mask[None]

    whole = pl.BlockSpec(memory_space=pltpu.VMEM)
    tall = pl.BlockSpec((rows, width), lambda b: (0, b))
    deep = pl.BlockSpec((chunks, chunk, width), lambda b: (0, 0, b))
    lead = pl.BlockSpec((rows, size, width), lambda b: (0, 0, b))
    first_w = pl.BlockSpec((model, width), lambda b: (0, b))
    second_w = pl.BlockSpec((model, width), lambda b: (0, b + blocks))
    out_w = pl.BlockSpec((width, model), lambda b: (b, 0))

    def thin(height):
        return pl.BlockSpec((height, width), lambda b: (0, b))

    def fixed(*dims_of):
        return pl.BlockSpec(dims_of, lambda b: (0,) * len(dims_of))

    scalars = pl.BlockSpec(memory_space=pltpu.SMEM)
    offset_buf = pltpu.VMEM((rows + 8, lanes), jnp.int32)
    packed = thin(plan["rows"])

    pair = (chunks, 2 * chunk, lanes)
    pair = (chunks, 2 * chunk, lanes)
    anywhere = pl.BlockSpec(memory_space=pl.ANY)
    small_half = (2, plan["rows"] // 2, piece)
    in_half = (in_rows, width)
    out_half = (out_proj.shape[0], model // blocks)
    (
        branch,
        signal,
        slope,
        projected,
        flipped,
        normed,
        grad_low,
        write_pair,
        read_pair,
        small,
        gain_value,
        in_blocks,
    ) = compute_call(
        functools.partial(front_kernel, plan, dims, tuple(smalls)),
        "front",
        blocks,
        [scalars, whole, whole, whole] + [whole] * len(smalls) + [fixed(in_rows, inner)],
        [tall, tall, tall] + [whole] * 8 + [anywhere],
        [
            shape((rows, inner)),
            shape((rows, inner), half),
            shape((rows, inner)),
            shape((rows, lanes)),
            shape((model, rows), half),
            shape((rows, model), half),
            shape((rows, model), half),
            shape(pair, half),
            shape(pair, half),
            shape((plan["rows"], inner), half),
            shape((1, model)),
            shape((blocks, depth, planes) + in_half, half),
        ],
        [
            offset_buf,
            pltpu.VMEM((plan["rows"], piece), jnp.float32),
            pltpu.VMEM(small_half, half),
            pltpu.VMEM((blocks,) + in_half, half),
            pltpu.VMEM((depth, planes) + small_half, half),
            pltpu.VMEM((blocks, depth, planes) + in_half, half),
            pltpu.SemaphoreType.DMA((blocks,)),
        ]
        + Gather.sems(blocks + 1, dims),
        4 * rows * model * inner,
        (seq_lengths, tokens, cotangent, mask_row, *smalls.values(), in_proj),
        collective_id=0,
    )
    groups = 2
    part, pieces = rows // groups, chunks // groups
    row_block = pltpu.VMEM((pieces, chunk, width), jnp.float32)
    spread_block = pltpu.VMEM((rows, size, lanes), jnp.float32)
    fold_block = pltpu.VMEM((width // lanes, chunk * chunk, lanes), jnp.float32)

    def by_group(order, *dims_of):
        middle = (0,) * (len(dims_of) - 2)
        return pl.BlockSpec(dims_of, lambda b, g: (order(g),) + middle + (b,))

    def by_token(order, *dims_of):
        return pl.BlockSpec(dims_of, lambda b, g: (order(g),) + (0,) * (len(dims_of) - 1))

    def by_channel(height):
        return pl.BlockSpec((height, width), lambda b, g: (0, b))

    def onward(g):
        return g

    def backward(g):
        return groups - 1 - g

    states, step, core, begins, gate_blocks, out_blocks = compute_call(
        functools.partial(forward_kernel, plan, dims),
        "forward",
        (blocks, groups),
        [
            scalars,
            by_token(onward, part, lanes),
            by_channel(plan["rows"]),
            by_group(onward, part, width),
            whole,
            whole,
            pl.BlockSpec((in_rows, inner), lambda b, g: (0, 1)),
            whole,
        ],
        [
            by_group(onward, part, size, width),
            by_group(onward, pieces, chunk, width),
            by_group(onward, pieces, chunk, width),
            by_group(onward, 1, size, width),
            anywhere,
            anywhere,
        ],
        [
            shape((rows, size, inner)),
            shape((chunks, chunk, inner)),
            shape((chunks, chunk, inner)),
            shape((groups, size, inner)),
            shape((blocks, depth, planes) + in_half, half),
            shape((blocks, depth, planes) + out_half, half),
        ],
        [
            offset_buf,
            pltpu.VMEM((part, width), jnp.float32),
            row_block,
            row_block,
            spread_block,
            spread_block,
            fold_block,
            pltpu.VMEM((size, width), jnp.float32),
            pltpu.VMEM((blocks,) + in_half, half),
            pltpu.VMEM((blocks,) + out_half, half),
        ]
        + Gather.sems(2 * blocks, dims),
        15 * rows * inner * size,
        (seq_lengths, projected, small, signal, write_pair, read_pair, in_proj, out_proj),
        collective_id=2,
    )
    weights = pl.BlockSpec((None, number, in_rows, width), lambda b: (b, 0, 0, 0))
    per_block = width // out_half[0]
    out_pieces = pl.BlockSpec((blocks, per_block) + out_half, lambda b: (0, b, 0, 0))
    branch_whole = in_blocks.reshape(blocks, number, *in_half)
    gate_whole = gate_blocks.reshape(blocks, number, *in_half)
    out_whole = out_blocks.reshape(blocks, number, *out_half)
    core_grad, gate_grad, grad_skip, grad_outw, grad_in_gate, output = compute_call(
        functools.partial(middle_kernel, plan),
        "middle",
        blocks,
        [deep, packed, tall, weights, whole, out_pieces, whole, whole, whole],
        [
            deep,
            tall,
            thin(1),
            pl.BlockSpec((blocks, width, out_half[1]), lambda b: (0, b, 0)),
            pl.BlockSpec((None, model, width), lambda b: (b, 0, 0)),
            fixed(rows, model),
        ],
        [
            shape((chunks, chunk, inner)),
            shape((rows, inner), half),
            shape((1, inner)),
            shape((blocks, inner, out_half[1]), half),
            shape((blocks, model, width), half),
            shape((rows, model), half),
        ],
        [
            pltpu.VMEM((rows, width), jnp.float32),
            pltpu.VMEM((rows, width), jnp.float32),
            pltpu.VMEM((rows, width), half),
            pltpu.VMEM((width, model), half),
            pltpu.VMEM((rows, model), jnp.float32),
        ],
        8 * rows * model * inner,
        (core, small, signal, gate_whole, grad_low, out_whole, flipped, normed, tokens),
    )
    early_grads = [
        grad_outw.reshape((blocks, depth, planes) + out_half),
        grad_in_gate.reshape((blocks, depth, planes) + in_half),
    ]
    early_sums = [shape(out_proj.shape), shape((in_rows, inner))]
    early_pieces = [shape((depth, planes) + block, half) for block in (in_half, out_half)] * blocks
    (
        signal_grad,
        grad_stepw,
        grad_bias,
        grad_decaylog,
        flat,
        out_sum,
        in_gate_sum,
        early_squares,
    ) = compute_call(
        functools.partial(backward_kernel, plan, dims),
        "backward",
        (blocks, groups),
        [
            scalars,
            by_token(backward, part, lanes),
            by_channel(plan["rows"]),
            by_group(backward, part, width),
            whole,
            whole,
            by_group(backward, pieces, chunk, width),
            by_group(backward, pieces, chunk, width),
            by_group(backward, part, size, width),
            by_group(backward, 1, size, width),
            anywhere,
            anywhere,
        ],
        [
            by_group(backward, part, width),
            by_channel(rank),
            by_channel(1),
            by_channel(size),
            whole,
        ]
        + [whole] * 3,
        [
            shape((rows, inner)),
            shape((rank, inner)),
            shape((1, inner)),
            shape((size, inner)),
            shape((rows, lanes), half),
            *early_sums,
            shape((8, lanes)),
        ],
        [
            offset_buf,
            row_block,
            row_block,
            spread_block,
            spread_block,
            fold_block,
            fold_block,
            row_block,
            row_block,
            pltpu.VMEM((part, width), half),
            pltpu.VMEM((size, width), jnp.float32),
            pltpu.VMEM((chunks, chunk, lanes), jnp.float32),
            spread_block,
            spread_block,
        ]
        + [pltpu.VMEM((blocks,) + block, jnp.float32) for block in (in_half, out_half)]
        + Reduce.rooms(dims, early_pieces)
        + Reduce.sems(2 * blocks, dims),
        40 * rows * inner * size,
        (
            seq_lengths,
            projected,
            small,
            signal,
            write_pair,
            read_pair,
            step,
            core_grad,
            states,
            begins,
            *early_grads,
        ),
        collective_id=3,
    )

    plain_rows = np.zeros((plan["rows"], piece), np.float32)
    for name in ("bias", "decay", "skip"):
        first, count = plan[name]
        plain_rows[first : first + count] = 1.0
    late_grads = [shape((depth, planes) + small_half, half)]
    late_grads += [shape((depth, planes, in_rows, width), half)] * blocks
    taps_n = conv_weight.shape[0]
    late = {"taps": (0, taps_n), "shift": (taps_n, 1), "gain": (taps_n + 1, 1)}
    late_block = (8, piece)

    tokens_grad, in_branch_sum, small_sum, late_sum, norms = compute_call(
        functools.partial(back_kernel, plan, dims),
        "back",
        blocks,
        [scalars, whole, whole, whole, packed, whole, tall, whole, tall, tall, tall, whole]
        + [weights, weights]
        + [whole] * 6,
        [whole] * 5,
        [
            shape((rows, model), half),
            shape((in_rows, inner)),
            shape(small_half),
            shape(late_block),
            shape((2, 8, lanes)),
        ],
        [
            offset_buf,
            pltpu.VMEM((rows + 8, width), jnp.float32),
            pltpu.VMEM((rows, width), half),
            pltpu.VMEM((rows, model), jnp.float32),
            pltpu.VMEM((blocks,) + late_grads[1].shape, half),
            pltpu.VMEM(late_grads[0].shape, late_grads[0].dtype),
            pltpu.VMEM((number,) + late_block, jnp.float32),
            pltpu.VMEM((number,) + late_block, jnp.float32),
            pltpu.VMEM((2,) + late_block, jnp.float32),
            pltpu.VMEM((2, 8, lanes), jnp.float32),
            pltpu.VMEM((number, 2, 8, lanes), jnp.float32),
            pltpu.VMEM((2, 2, 8, lanes), jnp.float32),
            pltpu.VMEM((blocks, in_rows, width), jnp.float32),
            pltpu.VMEM(small_half, jnp.float32),
            pltpu.SemaphoreType.DMA((2, number)),
            pltpu.SemaphoreType.DMA((2, number)),
        ]
        + Reduce.rooms(dims, late_grads)
        + Reduce.sems(blocks + 1, dims),
        8 * rows * model * inner,
        (
            seq_lengths,
            tokens,
            grad_low,
            gain_value,
            small,
            flat,
            branch,
            signal,
            slope,
            signal_grad,
            gate_grad,
            flipped,
            branch_whole,
            gate_whole,
            grad_stepw,
            grad_bias,
            grad_decaylog,
            grad_skip,
            jnp.asarray(plain_rows.reshape(small_half)),
            early_squares,
        ),
        collective_id=1,
    )

    names = ("gain", "taps", "shift", "select", "step", "bias", "decay", "skip")
    own = (norm_gain, conv_weight, conv_bias, select_proj, step_proj, step_bias, decay_log, skip_scale)
    in_grad, out_grad, grad_tokens, gain_grad, *small_grads, decay_sq, plain_sq = pl.pallas_call(
        functools.partial(finish_kernel, plan, names, late),
        in_specs=[whole] * 7,
        out_specs=[whole] * (3 + len(names)) + [scalars] * 2,
        out_shape=[shape(in_proj.shape), shape(out_proj.shape), shape(tokens.shape, half)]
        + [shape(array.shape) for array in own]
        + [shape((1, 1))] * 2,
        name="finish",
    )(
        tokens_grad,
        in_branch_sum,
        in_gate_sum,
        out_sum,
        small_sum.reshape(plan["rows"], piece),
        late_sum,
        norms,
    )
    return (
        output,
        grad_tokens,
        gain_grad,
        in_grad,
        *small_grads,
        out_grad,
        decay_sq[0, 0],
        plain_sq[0, 0],
    )


def solution(mesh):
    placed = (
        P(("wide", "narrow"), None),
        P(("wide", "narrow"), None),
        P(("wide", "narrow")),
        P(("wide", "narrow"), None),
        P("narrow"),
        P("narrow", None),
        P(None, "narrow"),
        P("narrow"),
        P(None, "narrow"),
        P(None, "narrow"),
        P("narrow"),
        P(None, "narrow"),
        P("narrow"),
        P("narrow", None),
    )
    return jax.shard_map(
        functools.partial(per_device, grid_of(mesh)),
        mesh=mesh,
        in_specs=placed,
        out_specs=(
            P(("wide", "narrow"), None),
            P(("wide", "narrow"), None),
            P("narrow"),
            P("narrow", None),
            P(None, "narrow"),
            P("narrow"),
            P(None, "narrow"),
            P(None, "narrow"),
            P("narrow"),
            P(None, "narrow"),
            P("narrow"),
            P("narrow", None),
            P(),
            P(),
        ),
        check_vma=False,
    )
```

```python
import functools
import math

import jax
import jax.numpy as jnp
import numpy as np
from jax import lax
from jax.experimental import pallas as pl
from jax.experimental.pallas import tpu as pltpu
from jax.sharding import PartitionSpec as P

epsilon = 1e-05
chunk = 8
lanes = 128
log2e = math.log2(math.e)
ln2 = math.log(2.0)
far = 1e30


def contract(left, right, left_dim, right_dim):
    return lax.dot_general(
        left, right, (((left_dim,), (right_dim,)), ((), ())), preferred_element_type=jnp.float32
    )


def row_loop(rows, group, body, initial):
    def some(index, carry):
        return body(index, pl.ds(pl.multiple_of(index * group, group), group), carry)

    return lax.fori_loop(0, rows // group, some, initial)


def cut(tile):
    return pl.ds(tile * lanes, lanes)


def sigmoid(values):
    return 0.5 * jnp.tanh(0.5 * values) + 0.5


def softplus(values):
    small = jnp.exp(-jnp.abs(values))
    series = small * (1.0 - small * (0.5 - small * (1.0 / 3.0 - 0.25 * small)))
    return jnp.maximum(values, 0.0) + jnp.where(small < 0.03, series, jnp.log(1.0 + small))


def slope_of(step):
    series = step * (1.0 - step * (0.5 - step * (1.0 / 6.0 - step * (1.0 / 24.0))))
    return jnp.where(step < 0.03, series, 1.0 - jnp.exp(-step))


def fill_offsets(lengths_ref, offset_buf, rows):
    place = lax.broadcasted_iota(jnp.int32, offset_buf.shape, 0)
    start = jnp.zeros(offset_buf.shape, jnp.int32)
    ahead = jnp.int32(0)
    for index in range(lengths_ref.shape[1] - 1):
        ahead = ahead + lengths_ref[0, index]
        start = jnp.where(place >= ahead, ahead, start)
    offset_buf[...] = jnp.where(place < rows, place - start, 0)


def small_rows(small_ref, first, count):
    base = first // 16 * 16
    tall = -(-(first + count - base) // 16) * 16
    return small_ref[base : base + tall, :].astype(jnp.float32)[first - base : first - base + count]


def eight(values):
    total = values[:8]
    for row in range(8, values.shape[0], 8):
        total = total + values[row : row + 8]
    return total


def conv_rows(index, at, group, tile, branch_ref, offset_buf, taps, shift):
    count = taps.shape[0]
    here = slice(tile * lanes, (tile + 1) * lanes)
    current = branch_ref[at, cut(tile)]
    before = branch_ref[pl.ds(pl.multiple_of(jnp.maximum(index * group - 8, 0), 8), 8), cut(tile)]
    both = jnp.concatenate([before, current], axis=0)
    offsets = offset_buf[at, :]
    summed = shift[:, here] + taps[count - 1 : count, here] * current
    for tap in range(count - 1):
        lag = count - 1 - tap
        read = jnp.where(offsets >= lag, pltpu.roll(both, lag, 0)[8:], 0.0)
        summed = summed + taps[tap : tap + 1, here] * read
    return summed


def rows_of(blocks):
    return as_matrix(blocks[...][None])


def as_matrix(blocks):
    columns = blocks.shape[3]
    if blocks.shape[2] % 16:
        return blocks.astype(jnp.float32).reshape(-1, columns).astype(blocks.dtype)
    return blocks.reshape(-1, columns)


def front_kernel(
    plan,
    dims,
    names,
    lengths_ref,
    tokens_ref,
    cotangent_ref,
    mask_ref,
    *refs,
):
    smalls, in_ref, refs = refs[: len(names)], refs[len(names)], refs[len(names) + 1 :]
    branch_ref, signal_ref, slope_ref, projected_ref, flipped_ref, normed_ref, low_ref = refs[:7]
    write_pair, read_pair, small_out, gain_ref, whole_ref = refs[7:12]
    offset_buf, pack_buf, own_small, own_in, land_small, land_in, store_sem = refs[12:19]
    rows = tokens_ref.shape[0]
    width = branch_ref.shape[1]
    block = pl.program_id(0)
    last = whole_ref.shape[0]
    each = own_in.shape[2]
    gather = Gather(
        dims,
        [own_small] + [own_in.at[index] for index in range(last)],
        [land_small] + [land_in.at[index] for index in range(last)],
        refs[19:],
    )

    def stored(index):
        return pltpu.make_async_copy(land_in.at[index], whole_ref.at[index], store_sem.at[index])

    @pl.when(block == 0)
    def _():
        pack_buf[...] = jnp.zeros_like(pack_buf)
        for name, ref in zip(names, smalls):
            first, tall = plan[name]
            pack_buf[first : first + tall, : ref.shape[1]] = ref[...]
        tall = pack_buf.shape[0] // 2
        for side in range(2):
            own_small[side] = pack_buf[side * tall : (side + 1) * tall, :].astype(own_small.dtype)
        for index in range(last):
            own_in[index] = in_ref[:, index * each : (index + 1) * each].astype(own_in.dtype)
        Place(dims).greet()
        for index in range(last + 1):
            gather.start(index)
        fill_offsets(lengths_ref, offset_buf, rows)
        down = lax.broadcasted_iota(jnp.int32, (rows, rows), 0)
        along = lax.broadcasted_iota(jnp.int32, (rows, rows), 1)
        diagonal = jnp.where(down == along, mask_ref[...].astype(jnp.float32), 0.0).astype(low_ref.dtype)
        low_ref[...] = jnp.dot(
            diagonal, cotangent_ref[...], preferred_element_type=jnp.float32
        ).astype(low_ref.dtype)
        projected_ref[...] = jnp.zeros_like(projected_ref)
        for which, number in ((0, 1), (1, 1), (0, 2), (1, 2), (0, 3), (2, 1)):
            gather.leg(which, number)
        gather.arrive(0)
        share = land_small.shape[4]
        gains = gain_ref.shape[1] // (land_small.shape[0] * land_small.shape[1])
        gain_row = plan["gain"][0]
        for z in range(land_small.shape[0]):
            for plane in range(land_small.shape[1]):
                owner = z * land_small.shape[1] + plane
                for side in range(2):
                    small_out[side * tall : (side + 1) * tall, owner * share : (owner + 1) * share] = land_small[
                        z, plane, side
                    ]
                side, row = gain_row // tall, gain_row % tall
                base = row // 16 * 16
                some = land_small[z, plane, side, base : base + 16, :].astype(jnp.float32)
                gain_ref[:, owner * gains : (owner + 1) * gains] = some[row - base : row - base + 1, :gains]

        def norm(index, at, carry):
            residual = tokens_ref[at, :].astype(jnp.float32)
            scale = lax.rsqrt(jnp.mean(residual * residual, axis=1, keepdims=True) + epsilon)
            normed_ref[at, :] = (residual * scale * gain_ref[...]).astype(normed_ref.dtype)
            return carry

        row_loop(rows, 16, norm, 0)
        flipped_ref[...] = normed_ref[...].T
        gather.leg(1, 3)
        gather.leg(2, 2)

    def move_on(plan_of_moves):
        for moment, legs in plan_of_moves:

            @pl.when(block == moment)
            def _(legs=legs):
                for which, number in legs:
                    gather.leg(which, number)

    for index in range(last):

        @pl.when(block == index * (each // width))
        def _(index=index):
            gather.arrive(index + 1)
            stored(index).start()

    first = pl.multiple_of(lax.rem(block * width, each), width)
    branch_w = as_matrix(land_in[lax.div(block * width, each), :, :, :, pl.ds(first, width)])
    branch_ref[...] = jnp.dot(normed_ref[...], branch_w, preferred_element_type=jnp.float32)
    move_on(((0, ((2, 3),)),))
    small_ref = small_out.at[:, pl.ds(pl.multiple_of(block * width, width), width)]
    taps = small_rows(small_ref, *plan["taps"])
    shift = small_rows(small_ref, *plan["shift"])

    def some(index, at, carry):
        for tile in range(width // lanes):
            summed = conv_rows(index, at, 32, tile, branch_ref, offset_buf, taps, shift)
            sigma = sigmoid(summed)
            active = summed * sigma
            signal_ref[at, cut(tile)] = active.astype(signal_ref.dtype)
            slope_ref[at, cut(tile)] = sigma + active * (1.0 - sigma)
        return carry

    row_loop(rows, 32, some, 0)
    projected_ref[...] += contract(signal_ref[...], small_ref[:lanes, :], 1, 1)

    @pl.when(block == pl.num_programs(0) - 1)
    def _():
        high, low = high_low(projected_ref[...])
        own = own_tokens(rows)
        rank = plan["step"][1]
        size = plan["decay"][1]
        entry = lax.broadcasted_iota(jnp.int32, (lanes, lanes), 0)
        lane = lax.rem(lax.broadcasted_iota(jnp.int32, (lanes, lanes), 1), size)
        for first, pair in ((rank, write_pair), (rank + size, read_pair)):
            spread = (entry == lane + first).astype(jnp.bfloat16)
            parts = [
                (jnp.dot(part.astype(jnp.bfloat16), spread, preferred_element_type=jnp.float32) * own).reshape(
                    rows // chunk, chunk, lanes
                )
                for part in (high, low)
            ]
            pair[...] = jnp.concatenate(parts, axis=1).astype(pair.dtype)
        for index in range(last + 1):
            gather.drain(index)
        for index in range(last):
            stored(index).wait()


def high_low(values):
    high = values.astype(jnp.bfloat16).astype(jnp.float32)
    return high, values - high


def own_tokens(rows):
    token = lax.rem(lax.broadcasted_iota(jnp.int32, (rows, lanes), 0), chunk)
    return (token == lax.div(lax.broadcasted_iota(jnp.int32, (rows, lanes), 1), lanes // chunk)).astype(
        jnp.float32
    )


def spread_all(pairs, target):
    some = 8

    def spread(index, carry):
        rows = jnp.concatenate([pairs[index * some + number] for number in range(some)], axis=1)
        wide = contract(rows, jnp.ones((rows.shape[0], lanes), rows.dtype), 0, 0)
        target[pl.ds(index * some * chunk, some * chunk)] = wide.reshape(some * chunk, -1, lanes)
        return carry

    lax.fori_loop(0, pairs.shape[0] // some, spread, 0)


def folded(buffer, tile):
    total = buffer[tile, pl.ds(0, chunk, stride=chunk), :]
    for row in range(1, chunk):
        total = total + buffer[tile, pl.ds(row, chunk, stride=chunk), :]
    return total


def forward_kernel(
    plan,
    dims,
    lengths_ref,
    projected_ref,
    small_ref,
    signal_ref,
    write_pair,
    read_pair,
    gate_own,
    out_own,
    states_ref,
    step_ref,
    core_ref,
    begin_ref,
    gate_whole,
    out_whole,
    offset_buf,
    pre_buf,
    decay_step,
    flows,
    write_wide,
    read_wide,
    fold_buf,
    held_buf,
    gate_low,
    out_low,
    *sems,
):
    rows, width = pre_buf.shape
    size = plan["decay"][1]
    half_size = size // 2
    tiles = width // lanes
    chunks = rows // chunk
    rank = plan["step"][1]
    group = pl.program_id(1)
    groups = pl.num_programs(1)
    moment = pl.program_id(0) * groups + group
    moments = pl.num_programs(0) * groups
    pieces = gate_low.shape[0]
    gather = Gather(
        dims,
        [buffer.at[index] for index in range(pieces) for buffer in (gate_low, out_low)],
        [buffer.at[index] for index in range(pieces) for buffer in (gate_whole, out_whole)],
        sems,
    )
    count = 2 * pieces

    @pl.when(moment == 0)
    def _():
        for index in range(pieces):
            for own, low in ((gate_own, gate_low), (out_own, out_low)):
                each = low.shape[2]
                low[index] = own[:, index * each : (index + 1) * each].astype(low.dtype)
        Place(dims).greet()
        for which in range(count):
            gather.start(which)
        fill_offsets(lengths_ref, offset_buf, offset_buf.shape[0] - 8)
        spread_all(write_pair, write_wide)
        spread_all(read_pair, read_wide)

    @pl.when(group == 0)
    def _():
        held_buf[...] = jnp.zeros_like(held_buf)

    begin_ref[0] = held_buf[...]
    pre_buf[...] = jnp.dot(
        projected_ref[:, :rank].astype(small_ref.dtype),
        small_ref[pl.ds(plan["step"][0], rank), :],
        preferred_element_type=jnp.float32,
    )
    bias = small_rows(small_ref, *plan["bias"])

    def before(index, at, carry):
        spot = pl.ds(pl.multiple_of(index * 4, 4), 4)
        inside = offset_buf[pl.ds(pl.multiple_of(group * rows + index * 32, 32), 32), :] > 0
        for tile in range(tiles):
            step = softplus(pre_buf[at, cut(tile)] + bias[:, tile * lanes : (tile + 1) * lanes])
            step_ref[spot, :, cut(tile)] = step.reshape(4, chunk, lanes)
            decay_step[spot, :, cut(tile)] = jnp.where(inside, step, far).reshape(4, chunk, lanes)
            flow = step * signal_ref[at, cut(tile)].astype(jnp.float32)
            flows[spot, :, cut(tile)] = flow.reshape(4, chunk, lanes)
        return carry

    row_loop(rows, 4 * chunk, before, 0)
    rates = -jnp.exp(small_rows(small_ref, *plan["decay"])) * log2e
    rates = [rates[:, tile * lanes : (tile + 1) * lanes] for tile in range(tiles)]

    def forward(index, held):
        held = list(held)
        for place in range(chunk):
            now = index * chunk + place
            write_now = write_wide[group * rows + now]
            read_now = read_wide[group * rows + now]
            for tile in range(tiles):
                decay = jnp.exp2(rates[tile] * decay_step[index, pl.ds(place, 1), cut(tile)])
                fresh = decay * held[tile] + write_now * flows[index, pl.ds(place, 1), cut(tile)]
                held[tile] = fresh
                states_ref[now, :, cut(tile)] = fresh
                product = read_now * fresh
                fold_buf[tile, pl.ds(place * chunk, chunk), :] = product[:half_size] + product[half_size:]
        for tile in range(tiles):
            core_ref[index, :, cut(tile)] = folded(fold_buf, tile)
        return tuple(held)

    held = tuple(held_buf[:, cut(tile)] for tile in range(tiles))
    schedule = {}
    for which in range(count):
        for number in (1, 2, 3):
            schedule.setdefault(min(3 * (which + number), 2 * 8), []).append((which, number))

    def move_on(legs):
        for which, number in legs:
            gather.leg(which, number)

    for half_loop in range(2):
        for point, legs in sorted(schedule.items()):
            if point < 16 and point % 2 == half_loop:
                pl.when(moment == point // 2)(functools.partial(move_on, legs))
        held = lax.fori_loop(half_loop * chunks // 2, (half_loop + 1) * chunks // 2, forward, held)
    for tile in range(tiles):
        held_buf[:, cut(tile)] = held[tile]

    @pl.when(moment == moments - 1)
    def _():
        move_on(sorted(schedule.get(16, ()), key=sum))
        for which in range(count):
            gather.arrive(which)
        for which in range(count):
            gather.drain(which)


def middle_kernel(
    plan,
    core_ref,
    small_ref,
    signal_ref,
    gate_w,
    low_ref,
    out_w,
    flipped_ref,
    normed_ref,
    tokens_ref,
    core_grad_ref,
    gate_grad_ref,
    skip_grad_ref,
    out_grad_ref,
    in_grad_ref,
    output_ref,
    pre_buf,
    gate_buf,
    gated_buf,
    out_buf,
    total,
):
    rows, width = pre_buf.shape
    tiles = width // lanes
    block = pl.program_id(0)
    each = out_w.shape[3]
    for index in range(out_w.shape[0]):
        out_buf[:, index * each : (index + 1) * each] = as_matrix(out_w[index][None])
    gate_buf[...] = jnp.dot(normed_ref[...], rows_of(gate_w), preferred_element_type=jnp.float32)
    pre_buf[...] = contract(low_ref[...], out_buf[...], 1, 1)
    skip = small_rows(small_ref, *plan["skip"])

    def after(index, at, carry):
        spot = pl.ds(pl.multiple_of(index * 4, 4), 4)
        sums = []
        for tile in range(tiles):
            signal = signal_ref[at, cut(tile)].astype(jnp.float32)
            core = core_ref[spot, :, cut(tile)].reshape(4 * chunk, lanes)
            core = core + skip[:, tile * lanes : (tile + 1) * lanes] * signal
            gate = gate_buf[at, cut(tile)]
            sigma = sigmoid(gate)
            active = gate * sigma
            gated_buf[at, cut(tile)] = (core * active).astype(gated_buf.dtype)
            grad_gated = pre_buf[at, cut(tile)]
            grad_core = grad_gated * active
            core_grad_ref[spot, :, cut(tile)] = grad_core.reshape(4, chunk, lanes)
            slope = sigma + active * (1.0 - sigma)
            gate_grad_ref[at, cut(tile)] = (grad_gated * core * slope).astype(gate_grad_ref.dtype)
            sums.append(carry[tile] + eight(grad_core * signal))
        return tuple(sums)

    zero_rows = jnp.zeros((8, lanes), jnp.float32)
    skips = row_loop(rows, 4 * chunk, after, (zero_rows,) * tiles)
    for tile in range(tiles):
        skip_grad_ref[:, cut(tile)] = jnp.sum(skips[tile], axis=0, keepdims=True)
    out_grad = contract(gated_buf[...], low_ref[...], 0, 0).astype(out_grad_ref.dtype)
    for index in range(out_w.shape[0]):
        out_grad_ref[index] = out_grad[:, index * each : (index + 1) * each]
    in_grad_ref[...] = jnp.dot(
        flipped_ref[...], gate_grad_ref[...], preferred_element_type=jnp.float32
    ).astype(in_grad_ref.dtype)
    piece = jnp.dot(gated_buf[...], out_buf[...], preferred_element_type=jnp.float32)

    @pl.when(block == 0)
    def _():
        total[...] = piece

    @pl.when(block > 0)
    def _():
        total[...] += piece

    @pl.when(block == pl.num_programs(0) - 1)
    def _():
        output_ref[...] = (tokens_ref[...].astype(jnp.float32) + total[...]).astype(output_ref.dtype)


def backward_kernel(
    plan,
    dims,
    lengths_ref,
    projected_ref,
    small_ref,
    signal_ref,
    write_pair,
    read_pair,
    step_ref,
    core_grad_ref,
    states_ref,
    begin_ref,
    out_grad_ref,
    in_grad_ref,
    signal_grad_ref,
    step_w_grad_ref,
    bias_grad_ref,
    decay_grad_ref,
    flat_ref,
    out_sum_ref,
    in_sum_ref,
    square_ref,
    offset_buf,
    decay_step,
    flows,
    write_wide,
    read_wide,
    first_buf,
    second_buf,
    through_buf,
    scaled_buf,
    low_buf,
    incoming_buf,
    rank_buf,
    write_buf,
    read_buf,
    *parts,
):
    rows, width = low_buf.shape
    rank = plan["step"][1]
    size = plan["decay"][1]
    half_size = size // 2
    tiles = width // lanes
    chunks = rows // chunk
    block = pl.program_id(0)
    turn = pl.program_id(1)
    groups = pl.num_programs(1)
    group = groups - 1 - turn
    moment = block * groups + turn
    moments = pl.num_programs(0) * groups
    gate_result, out_result, parts = parts[0], parts[1], parts[2:]
    pieces = gate_result.shape[0]
    count = 2 * pieces

    both = ((in_grad_ref, gate_result), (out_grad_ref, out_result))
    reduce = Reduce(
        dims,
        [ref.at[index] for index in range(pieces) for ref, _ in both],
        parts[: 6 * count],
        parts[6 * count :],
        [result.at[index] for index in range(pieces) for _, result in both],
        False,
    )

    @pl.when(moment == 0)
    def _():
        Place(dims).greet()
        for which in range(count):
            reduce.start(which)
        fill_offsets(lengths_ref, offset_buf, offset_buf.shape[0] - 8)
        spread_all(write_pair, write_wide)
        spread_all(read_pair, read_wide)
        write_buf[...] = jnp.zeros_like(write_buf)
        read_buf[...] = jnp.zeros_like(read_buf)
        rank_buf[...] = jnp.zeros_like(rank_buf)

    @pl.when(turn == 0)
    def _():
        incoming_buf[...] = jnp.zeros_like(incoming_buf)
        decay_grad_ref[...] = jnp.zeros_like(decay_grad_ref)
        bias_grad_ref[...] = jnp.zeros_like(bias_grad_ref)
        step_w_grad_ref[...] = jnp.zeros_like(step_w_grad_ref)

    def before(index, at, carry):
        spot = pl.ds(pl.multiple_of(index * 4, 4), 4)
        offsets = offset_buf[pl.ds(pl.multiple_of(group * rows + index * 32, 32), 32), :]
        inside = (offsets > 0).reshape(4, chunk, lanes)
        for tile in range(tiles):
            step = step_ref[spot, :, cut(tile)]
            decay_step[spot, :, cut(tile)] = jnp.where(inside, step, far)
            signal = signal_ref[at, cut(tile)].astype(jnp.float32).reshape(4, chunk, lanes)
            flows[spot, :, cut(tile)] = step * signal
        return carry

    row_loop(rows, 4 * chunk, before, 0)
    rates = -jnp.exp(small_rows(small_ref, *plan["decay"])) * log2e
    rates = [rates[:, tile * lanes : (tile + 1) * lanes] for tile in range(tiles)]

    def backward(position, carried):
        index = chunks - 1 - position
        incoming, decay_sums = list(carried[0]), list(carried[1])
        for place in range(chunk - 1, -1, -1):
            now = index * chunk + place
            token = group * rows + now
            write_now = write_wide[token]
            read_now = read_wide[token]
            read_sum = None
            write_sum = None
            for tile in range(tiles):
                step_now = decay_step[index, pl.ds(place, 1), cut(tile)]
                grad_now = core_grad_ref[index, pl.ds(place, 1), cut(tile)]
                if place > 0:
                    earlier = states_ref[now - 1, :, cut(tile)]
                else:
                    earlier = jnp.where(
                        index > 0, states_ref[jnp.maximum(now - 1, 0), :, cut(tile)], begin_ref[0, :, cut(tile)]
                    )
                grad_state = incoming[tile] + read_now * grad_now
                through_read = states_ref[now, :, cut(tile)] * grad_now
                through_write = grad_state * flows[index, pl.ds(place, 1), cut(tile)]
                read_sum = through_read if read_sum is None else read_sum + through_read
                write_sum = through_write if write_sum is None else write_sum + through_write
                passed = grad_state * write_now
                first_buf[tile, pl.ds(place * chunk, chunk), :] = passed[:half_size] + passed[half_size:]
                leaving = jnp.exp2(rates[tile] * step_now) * grad_state
                incoming[tile] = leaving
                weighted = leaving * earlier
                scaled = weighted * rates[tile]
                second_buf[tile, pl.ds(place * chunk, chunk), :] = scaled[:half_size] + scaled[half_size:]
                decay_sums[tile] = decay_sums[tile] + weighted * step_now
            read_buf[token] += read_sum
            write_buf[token] += write_sum
        for tile in range(tiles):
            through_buf[index, :, cut(tile)] = folded(first_buf, tile)
            scaled_buf[index, :, cut(tile)] = folded(second_buf, tile)
        return (tuple(incoming), tuple(decay_sums))

    incoming = tuple(incoming_buf[:, cut(tile)] for tile in range(tiles))
    nothing = (jnp.zeros((size, lanes), jnp.float32),) * tiles
    schedule = {}
    for which in range(count):
        for number in (1, 2, 3):
            schedule.setdefault((2, 4, 7, 9)[which] + (0, 3, 5)[number - 1], []).append((which, number))

    def move_on(legs):
        for which, number in legs:
            reduce.leg(which, number)

    carried = (incoming, nothing)
    for half_loop in range(2):
        for point, legs in sorted(schedule.items()):
            if point % 2 == half_loop:
                pl.when(moment == point // 2)(functools.partial(move_on, legs))
        carried = lax.fori_loop(half_loop * chunks // 2, (half_loop + 1) * chunks // 2, backward, carried)
    incoming, decay_sums = carried
    for tile in range(tiles):
        incoming_buf[:, cut(tile)] = incoming[tile]
        decay_grad_ref[:, cut(tile)] += decay_sums[tile] * rates[tile] * ln2
    skip = small_rows(small_ref, *plan["skip"])

    def after(index, at, carry):
        spot = pl.ds(pl.multiple_of(index * 4, 4), 4)
        sums = []
        for tile in range(tiles):
            signal = signal_ref[at, cut(tile)].astype(jnp.float32)
            step = step_ref[spot, :, cut(tile)].reshape(4 * chunk, lanes)
            through = through_buf[spot, :, cut(tile)].reshape(4 * chunk, lanes)
            scaled = scaled_buf[spot, :, cut(tile)].reshape(4 * chunk, lanes)
            core_grad = core_grad_ref[spot, :, cut(tile)].reshape(4 * chunk, lanes)
            grad_pre = (through * signal + ln2 * scaled) * slope_of(step)
            low_buf[at, cut(tile)] = grad_pre.astype(low_buf.dtype)
            signal_grad_ref[at, cut(tile)] = (
                through * step + skip[:, tile * lanes : (tile + 1) * lanes] * core_grad
            )
            sums.append(carry[tile] + eight(grad_pre))
        return tuple(sums)

    zero_rows = jnp.zeros((8, lanes), jnp.float32)
    sums = row_loop(rows, 4 * chunk, after, (zero_rows,) * tiles)
    for tile in range(tiles):
        bias_grad_ref[:, cut(tile)] += jnp.sum(sums[tile], axis=0, keepdims=True)
    step_w_grad_ref[...] += contract(
        projected_ref[:, :rank].astype(low_buf.dtype), low_buf[...], 0, 0
    )
    step_w = small_ref[pl.ds(plan["step"][0], rank), :]
    step_w = jnp.concatenate([step_w, jnp.zeros((lanes - rank, width), step_w.dtype)], axis=0)
    rank_buf[pl.ds(group * chunks, chunks)] += contract(low_buf[...], step_w, 1, 1).reshape(
        chunks, chunk, lanes
    )

    @pl.when(moment == moments - 1)
    def _():
        squares = jnp.zeros((8, lanes), jnp.float32)
        for which in range(count):
            squares = squares + reduce.finish(which)[0]
        square_ref[...] = squares
        some = 8
        entry = lax.rem(lax.broadcasted_iota(jnp.int32, (some * chunk * size, lanes), 0), size)
        target = lax.broadcasted_iota(jnp.int32, (some * chunk * size, lanes), 1)
        ones = jnp.ones((lanes, lanes), jnp.bfloat16)

        def lay(index, carry):
            lot = pl.ds(index * some * chunk, some * chunk)
            for number, buffer in enumerate((write_buf, read_buf)):
                high, low = high_low(buffer[lot].reshape(some * chunk * size, lanes))
                summed = jnp.dot(high.astype(jnp.bfloat16), ones, preferred_element_type=jnp.float32)
                summed += jnp.dot(low.astype(jnp.bfloat16), ones, preferred_element_type=jnp.float32)
                summed = jnp.where(target == entry + rank + number * size, summed, 0.0)
                summed = jnp.sum(summed.reshape(some * chunk, size, lanes), axis=1)
                rank_buf[pl.ds(index * some, some)] += summed.reshape(some, chunk, lanes)
            return carry

        lax.fori_loop(0, rank_buf.shape[0] // some, lay, 0)
        flat_ref[...] = rank_buf[...].reshape(flat_ref.shape).astype(flat_ref.dtype)
        for which in range(count):
            reduce.settle(which)
        for index in range(pieces):
            for target, result in ((out_sum_ref, out_result), (in_sum_ref, gate_result)):
                each = result.shape[2]
                target[:, index * each : (index + 1) * each] = result[index]


def back_kernel(
    plan,
    dims,
    lengths_ref,
    tokens_ref,
    low_ref,
    gain_ref,
    small_ref,
    flat_ref,
    branch_ref,
    signal_ref,
    slope_ref,
    signal_grad_ref,
    gate_grad_ref,
    flipped_ref,
    branch_w,
    gate_w,
    step_w_grad_ref,
    bias_grad_ref,
    decay_grad_ref,
    skip_grad_ref,
    plain_ref,
    earlier_ref,
    tokens_grad_ref,
    in_sum_ref,
    small_sum_ref,
    late_sum_ref,
    norm_ref,
    offset_buf,
    conv_buf,
    mixed_buf,
    total,
    in_stage,
    small_stage,
    late_stage,
    late_land,
    late_cores,
    norm_own,
    norm_land,
    norm_cores,
    in_result,
    small_result,
    direct_send,
    direct_recv,
    *parts,
):
    rows = tokens_ref.shape[0]
    width = branch_ref.shape[1]
    tiles = width // lanes
    block = pl.program_id(0)
    last = in_stage.shape[0]
    count = last + 1
    reduce = Reduce(
        dims,
        [small_stage] + [in_stage.at[index] for index in range(last)],
        parts[: 5 * count],
        parts[5 * count :],
        [small_result] + [in_result.at[index] for index in range(last)],
        True,
    )
    share = small_stage.shape[4]
    half_rows = small_stage.shape[3]
    planes = small_stage.shape[1]
    owners = small_stage.shape[0] * planes

    @pl.when(block == 0)
    def _():
        Place(dims).greet(everyone=True)
        select_grad = contract(flat_ref[...], signal_ref[...], 0, 0)
        step_first, step_tall = plan["step"]
        filler = jnp.zeros((2 * half_rows - step_first - step_tall, select_grad.shape[1]), jnp.float32)
        pieces = {
            "decay": decay_grad_ref[...],
            "bias": bias_grad_ref[...],
            "skip": skip_grad_ref[...],
            "step": step_w_grad_ref[...],
        }
        first = plan["select"][1]
        rows_now = [select_grad[:first]]
        for name in ("decay", "taps", "shift", "bias", "skip", "gain"):
            tall = plan[name][1]
            rows_now.append(
                pieces[name] if name in pieces else jnp.zeros((tall, select_grad.shape[1]), jnp.float32)
            )
            first += tall
        rows_now.append(jnp.zeros((step_first - first, select_grad.shape[1]), jnp.float32))
        rows_now.append(pieces["step"])
        if filler.shape[0]:
            rows_now.append(filler)
        everything = jnp.concatenate(rows_now, axis=0)
        for owner in range(owners):
            for side in range(2):
                small_stage[owner // planes, owner % planes, side] = everything[
                    side * half_rows : (side + 1) * half_rows, owner * share : (owner + 1) * share
                ].astype(small_stage.dtype)
        reduce.start(0)
        fill_offsets(lengths_ref, offset_buf, rows)

    taps = small_rows(small_ref, *plan["taps"])
    taps_count = taps.shape[0]
    conv_buf[pl.ds(0, rows), :] = signal_grad_ref[...] + jnp.dot(
        flat_ref[...], small_ref[:lanes, :], preferred_element_type=jnp.float32
    )
    conv_buf[pl.ds(rows, 8), :] = jnp.zeros((8, width), jnp.float32)

    def through_conv(index, at, carry):
        sums = []
        for tile in range(tiles):
            grad_conv = conv_buf[at, cut(tile)] * slope_ref[at, cut(tile)]
            conv_buf[at, cut(tile)] = grad_conv
            sums.append(carry[tile] + eight(grad_conv))
        return tuple(sums)

    zero_rows = jnp.zeros((8, lanes), jnp.float32)
    shift_sums = row_loop(rows, 32, through_conv, (zero_rows,) * tiles)

    def move_on(plan_of_moves):
        for moment, legs in plan_of_moves:

            @pl.when(block == moment)
            def _(legs=legs):
                for which, number in legs:
                    reduce.leg(which, number)

    move_on(((0, ((0, 1),)), (1, ((1, 1),)), (2, ((2, 1),)), (3, ((3, 1),))))

    def to_branch(index, at, carry):
        longer = pl.ds(pl.multiple_of(index * 32, 32), 40)
        offsets = offset_buf[longer, :]
        result = []
        for tile in range(tiles):
            here = slice(tile * lanes, (tile + 1) * lanes)
            grads = conv_buf[longer, cut(tile)]
            branch = branch_ref[at, cut(tile)]
            summed = taps[taps_count - 1 : taps_count, here] * grads[:32]
            sums = [None] * taps_count
            sums[taps_count - 1] = carry[tile][taps_count - 1] + eight(branch * grads[:32])
            for tap in range(taps_count - 1):
                lag = taps_count - 1 - tap
                moved = pltpu.roll(jnp.where(offsets >= lag, grads, 0.0), 40 - lag, 0)[:32]
                summed = summed + taps[tap : tap + 1, here] * moved
                sums[tap] = carry[tile][tap] + eight(branch * moved)
            mixed_buf[at, cut(tile)] = summed.astype(mixed_buf.dtype)
            result.append(tuple(sums))
        return tuple(result)

    sums = row_loop(rows, 32, to_branch, ((zero_rows,) * taps_count,) * tiles)
    late = [
        jnp.concatenate(
            [jnp.sum(sums[tile][tap], axis=0, keepdims=True) for tap in range(taps_count)]
            + [jnp.sum(shift_sums[tile], axis=0, keepdims=True)]
            + [jnp.zeros((8 - taps_count - 1, lanes), jnp.float32)],
            axis=0,
        )
        for tile in range(tiles)
    ]
    late = jnp.concatenate(late, axis=1)
    for piece in range(width // share):
        late_stage[block * (width // share) + piece] = late[:, piece * share : (piece + 1) * share]
    in_grad = jnp.dot(flipped_ref[...], mixed_buf[...], preferred_element_type=jnp.float32)
    in_stage[block] = in_grad.reshape(in_stage.shape[1:]).astype(in_stage.dtype)
    for index in range(last):

        @pl.when(block == index)
        def _(index=index):
            reduce.start(index + 1)

    grad_normed_piece = contract(mixed_buf[...], rows_of(branch_w), 1, 1)
    grad_normed_piece += contract(gate_grad_ref[...], rows_of(gate_w), 1, 1)

    @pl.when(block == 0)
    def _():
        total[...] = grad_normed_piece

    @pl.when(block > 0)
    def _():
        total[...] += grad_normed_piece

    move_on(((0, ((0, 2),)), (1, ((0, 3), (1, 2))), (2, ((2, 2), (1, 3))), (3, ((3, 2), (2, 3)))))

    @pl.when(block == pl.num_programs(0) - 1)
    def _():
        def finish(index, at, carry):
            residual = tokens_ref[at, :].astype(jnp.float32)
            scale = lax.rsqrt(jnp.mean(residual * residual, axis=1, keepdims=True) + epsilon)
            grad_normed = total[at, :]
            weighted = grad_normed * gain_ref[...]
            inner = jnp.mean(weighted * residual, axis=1, keepdims=True)
            grad_y = low_ref[at, :].astype(jnp.float32)
            result = grad_y + (scale * weighted - residual * (scale * scale * scale) * inner)
            tokens_grad_ref[at, :] = result.astype(tokens_grad_ref.dtype)
            return carry + eight(grad_normed * residual * scale)

        gains = row_loop(rows, 16, finish, jnp.zeros((8, total.shape[1]), jnp.float32))
        gains = jnp.sum(gains, axis=0, keepdims=True)
        place = Place(dims)
        each = gains.shape[1] // owners
        for owner in range(owners):
            late_stage[owner, taps_count + 1 : taps_count + 2, :each] = gains[
                :, owner * each : (owner + 1) * each
            ]
        late_sems = direct_send.at[0], direct_recv.at[0]
        norm_sems = direct_send.at[1], direct_recv.at[1]
        send_to_all(place, lambda target: late_stage.at[target], late_land, *late_sems)
        for which, number in ((4, 1), (3, 3), (4, 2)):
            reduce.leg(which, number)
        late_sum = sum_of_all(place, late_stage[place.me], late_land, *late_sems)
        late_sum = sum_of_cores(place, late_sum, late_cores, direct_send.at[0, 0], direct_recv.at[0, 0])
        late_sum_ref[...] = late_sum
        reduce.leg(4, 3)
        kept = earlier_ref[...] + folded_squares(late_sum * late_sum) * (1 - place.core).astype(jnp.float32)
        more, plain = reduce.finish(0, plain_ref)
        kept = kept + more
        for index in range(1, count):
            kept = kept + reduce.finish(index)[0]
        norm_own[...] = jnp.stack([kept, plain])
        send_to_all(place, lambda target: norm_own, norm_land, *norm_sems)
        norms = sum_of_all(place, norm_own[...], norm_land, *norm_sems)
        norm_ref[...] = sum_of_cores(place, norms, norm_cores, direct_send.at[1, 0], direct_recv.at[1, 0])
        for index in range(count):
            reduce.settle(index)
        for index in range(last):
            in_sum_ref[:, index * width : (index + 1) * width] = in_result[index]
        small_sum_ref[...] = small_result[...]


def finish_kernel(
    plan, names, late, tokens_ref, branch_ref, gate_ref, out_ref, small_ref, late_ref, norm_ref, *outs
):
    middle = branch_ref.shape[1]
    outs[0][:, :middle] = branch_ref[...]
    outs[0][:, middle:] = gate_ref[...]
    outs[1][...] = out_ref[...]
    outs[2][...] = tokens_ref[...]
    for name, target in zip(names, outs[3 : 3 + len(names)]):
        source, (first, count) = (late_ref, late[name]) if name in late else (small_ref, plan[name])
        if len(target.shape) == 1:
            target[...] = source[first, : target.shape[0]]
        else:
            target[...] = source[first : first + count, :]
    for index in range(2):
        outs[3 + len(names) + index][0, 0] = jnp.sum(norm_ref[index])


def shape(dims, kind=jnp.float32):
    return jax.ShapeDtypeStruct(dims, kind)


def compute_call(
    kernel, name, blocks, in_specs, out_specs, out_shape, scratch, flops, operands, collective_id=None
):
    return pl.pallas_call(
        kernel,
        grid=blocks if isinstance(blocks, tuple) else (blocks,),
        in_specs=in_specs,
        out_specs=out_specs,
        out_shape=out_shape,
        scratch_shapes=scratch,
        compiler_params=pltpu.CompilerParams(
            dimension_semantics=("arbitrary",) * (len(blocks) if isinstance(blocks, tuple) else 1),
            vmem_limit_bytes=62 * 1024 * 1024,
            collective_id=collective_id,
            has_side_effects=collective_id is not None,
        ),
        cost_estimate=pl.CostEstimate(flops=flops, bytes_accessed=40 << 20, transcendentals=0),
        name=name,
    )(*operands)


class Place:
    def __init__(self, dims, swapped=False):
        depth, tall, wide = dims
        self.dims = dims
        self.core = lax.axis_index("wide")
        self.me = lax.axis_index("narrow")
        self.across = lax.rem(self.me, wide)
        self.up = lax.rem(lax.div(self.me, wide), tall)
        self.deep = lax.div(self.me, wide * tall)
        side = 1 - self.core if swapped else self.core
        turn = side if tall == wide else 0
        self.second = (1 + turn * (wide - 1), self.across + turn * (self.up - self.across), wide)
        self.third = (wide - turn * (wide - 1), self.up + turn * (self.across - self.up), tall)
        self.spans = (depth, wide, tall)
        self.other = {"wide": 1 - self.core}

    def level(self, d):
        return lax.rem(self.deep + d, self.spans[0])

    def plane(self, e, f):
        return (
            lax.rem(self.second[1] + e, self.second[2]) * self.second[0]
            + lax.rem(self.third[1] + f, self.third[2]) * self.third[0]
        )

    def plane_behind(self, e, f):
        return self.plane((self.spans[1] - e) % self.spans[1], (self.spans[2] - f) % self.spans[2])

    def at(self, d, e, f):
        return {"narrow": self.level(d) * (self.dims[1] * self.dims[2]) + self.plane(e, f)}

    def greet(self, everyone=False):
        barrier = pltpu.get_barrier_semaphore()
        peers = [self.other]
        if everyone:
            number = self.spans[0] * self.spans[1] * self.spans[2]
            peers += [{"narrow": lax.rem(self.me + hop, number)} for hop in range(1, number)]
        else:
            for axis, size in enumerate(self.spans):
                for hop in range(1, size):
                    move = [0, 0, 0]
                    move[axis] = hop
                    peers.append(self.at(*move))
        for peer in peers:
            pl.semaphore_signal(barrier, inc=1, device_id=peer, device_id_type=pl.DeviceIdType.MESH)
        pl.semaphore_wait(barrier, len(peers))


def by_rows(block):
    return block[0] % 32 == 0


def half_shape(block):
    if len(block) == 3:
        return tuple(block[1:])
    return (block[0] // 2, block[1]) if by_rows(block) else (block[0], block[1] // 2)


def half(view, block, side, lead=0):
    ahead = (slice(None),) * lead
    if len(block) == 3:
        return view.at[ahead + (side,)]
    if by_rows(block):
        return view.at[ahead + (pl.ds(pl.multiple_of(side * (block[0] // 2), 16), block[0] // 2),)]
    columns = pl.ds(pl.multiple_of(side * (block[1] // 2), lanes), block[1] // 2)
    return view.at[ahead + (slice(None), columns)]


def remote(source, target, send_sem, recv_sem, device):
    return pltpu.make_async_remote_copy(
        src_ref=source,
        dst_ref=target,
        send_sem=send_sem,
        recv_sem=recv_sem,
        device_id=device,
        device_id_type=pl.DeviceIdType.MESH,
    )


class Gather:
    def __init__(self, dims, own, whole, sems):
        self.dims, self.own, self.whole = dims, own, whole
        self.local_sem, self.send_sem, self.recv_sem = sems

    @staticmethod
    def sems(count, dims):
        copies = dims[0] + 2 * dims[1] * dims[2]
        return [pltpu.SemaphoreType.DMA((count,))] + [pltpu.SemaphoreType.DMA((count, copies))] * 2

    def line(self, which, plane, side):
        return half(self.whole[which].at[:, plane], self.own[which].shape, side, 1)

    def local(self, place, which):
        block = self.own[which].shape
        return pltpu.make_async_copy(
            half(self.own[which], block, place.core),
            half(self.whole[which].at[place.deep, place.plane(0, 0)], block, place.core),
            self.local_sem.at[which],
        )

    def copy(self, which, source, target, index, device):
        return remote(
            source, target, self.send_sem.at[which, index], self.recv_sem.at[which, index], device
        )

    def rise(self, place, which, hop):
        block = self.own[which].shape
        return self.copy(
            which,
            half(self.own[which], block, place.core),
            half(self.whole[which].at[place.deep, place.plane(0, 0)], block, place.core),
            hop,
            place.at(hop, 0, 0),
        )

    def leg_index(self, e, f):
        return self.dims[0] + e * self.dims[1] + f

    def hand_index(self, e, f):
        return self.leg_index(e, f) + self.dims[1] * self.dims[2]

    def onward(self, place, which, e, f):
        line = self.line(which, place.plane_behind(e, f), place.core)
        if f == 0:
            for hop in range(1, place.spans[2]):
                self.copy(which, line, line, self.leg_index(e, hop), place.at(0, 0, hop)).start()
        if f == 0 and e == 0:
            for hop in range(1, place.spans[1]):
                self.copy(which, line, line, self.leg_index(hop, 0), place.at(0, hop, 0)).start()
        self.copy(which, line, line, self.hand_index(e, f), place.other).start()

    def start(self, which):
        place = Place(self.dims)
        for hop in range(1, place.spans[0]):
            self.rise(place, which, hop).start()
        self.local(place, which).start()

    def leg(self, which, number):
        place = Place(self.dims)
        if number == 1:
            self.local(place, which).wait()
            for hop in range(1, place.spans[0]):
                self.rise(place, which, hop).wait_recv()
            self.onward(place, which, 0, 0)
            return
        for e in range(place.spans[1]):
            for f in range(place.spans[2]):
                if (number == 2 and f == 0 and e > 0) or (number == 3 and f > 0):
                    line = self.line(which, place.plane_behind(e, f), place.core)
                    self.copy(which, line, line, self.leg_index(e, f), place.other).wait_recv()
                    self.onward(place, which, e, f)

    def arrive(self, which):
        place, mirror = Place(self.dims), Place(self.dims, swapped=True)
        for e in range(place.spans[1]):
            for f in range(place.spans[2]):
                line = self.line(which, mirror.plane_behind(e, f), 1 - place.core)
                self.copy(which, line, line, self.hand_index(e, f), place.other).wait_recv()

    def drain(self, which):
        place = Place(self.dims)
        for hop in range(1, place.spans[0]):
            self.rise(place, which, hop).wait_send()
        for e in range(place.spans[1]):
            for f in range(place.spans[2]):
                line = self.line(which, place.plane_behind(e, f), place.core)
                if e > 0 or f > 0:
                    self.copy(which, line, line, self.leg_index(e, f), place.other).wait_send()
                self.copy(which, line, line, self.hand_index(e, f), place.other).wait_send()


class Reduce:
    def __init__(self, dims, grads, rooms, sems, results, resident):
        self.dims, self.grads, self.resident = dims, grads, resident
        count = len(grads)
        self.mine, self.swapped, self.third, self.second, self.first = (
            rooms[index * count : (index + 1) * count] for index in range(5)
        )
        self.loaded = None if resident else rooms[5 * count :]
        self.load_sem, self.swap_send, self.swap_recv, self.send_sem, self.recv_sem = sems[:5]
        self.last_send, self.last_recv = sems[5:]
        self.results = results

    @staticmethod
    def rooms(dims, grads, resident):
        depth, tall, wide = dims
        leads = (
            (tall, wide, depth),
            (depth, tall * wide),
            (tall - 1, wide, depth),
            (wide - 1, depth),
            (depth - 1,),
        )
        if not resident:
            leads += ((depth, tall * wide),)
        return [
            pltpu.VMEM(lead + half_shape(grad.shape[2:]), grad.dtype) for lead in leads for grad in grads
        ]

    @staticmethod
    def sems(count, dims):
        return (
            [pltpu.SemaphoreType.DMA((count,))] * 3
            + [pltpu.SemaphoreType.DMA((count, dims[0] + dims[1] + dims[2]))] * 2
            + [pltpu.SemaphoreType.DMA((count,))] * 2
        )

    def block(self, which):
        return self.grads[which].shape[2:]

    def load(self, place, which):
        return pltpu.make_async_copy(
            half(self.grads[which], self.block(which), place.core, 2),
            self.loaded[which],
            self.load_sem.at[which],
        )

    def swap(self, place, which):
        return remote(
            half(self.grads[which], self.block(which), 1 - place.core, 2),
            self.swapped[which],
            self.swap_send.at[which],
            self.swap_recv.at[which],
            place.other,
        )

    def hop(self, which, source, target, index, device):
        return remote(
            source, target, self.send_sem.at[which, index], self.recv_sem.at[which, index], device
        )

    def third_hop(self, place, which, f):
        return self.hop(which, self.mine[which].at[f], self.third[which].at[f - 1], f, place.at(0, 0, f))

    def second_hop(self, place, which, e):
        return self.hop(
            which,
            self.mine[which].at[0, e],
            self.second[which].at[e - 1],
            self.dims[1] + e,
            place.at(0, e, 0),
        )

    def first_hop(self, place, which, d):
        return self.hop(
            which,
            self.mine[which].at[0, 0, place.level(d)],
            self.first[which].at[d - 1],
            self.dims[1] + self.dims[2] + d,
            place.at(d, 0, 0),
        )

    def start(self, which):
        place = Place(self.dims)
        self.swap(place, which).start()
        if not self.resident:
            self.load(place, which).start()

    def parts(self, place, which, e, f, z):
        plane = place.plane(e, f)
        if self.resident:
            found = [half(self.grads[which].at[z, plane], self.block(which), place.core)]
        else:
            found = [self.loaded[which].at[z, plane]]
        found.append(self.swapped[which].at[z, plane])
        if f == 0:
            found += [self.third[which].at[hop - 1, e, z] for hop in range(1, place.spans[2])]
        if f == 0 and e == 0:
            found += [self.second[which].at[hop - 1, z] for hop in range(1, place.spans[1])]
        return found

    def ready(self, place, which):
        if not self.resident:
            self.load(place, which).wait()
        self.swap(place, which).wait_recv()

    def added(self, parts, store, carry):
        rows = parts[0].shape[0]
        group = min(rows, 16)

        def some(index, carry):
            at_rows = pl.ds(pl.multiple_of(index * group, group), group)
            total = parts[0][at_rows, :].astype(jnp.float32)
            for part in parts[1:]:
                total = total + part[at_rows, :].astype(jnp.float32)
            return store(at_rows, total, carry)

        return lax.fori_loop(0, rows // group, some, carry)

    def sum_into(self, place, which, e, f, z):
        target = self.mine[which].at[f, e, z]

        def keep(at_rows, total, carry):
            target[at_rows, :] = total.astype(target.dtype)
            return carry

        self.added(self.parts(place, which, e, f, z), keep, 0)

    def leg(self, which, number):
        place = Place(self.dims)
        depth, span_e, span_f = place.spans
        if number == 1:
            self.ready(place, which)
            for f in range(span_f - 1, 0, -1):
                for e in range(span_e - 1, -1, -1):
                    for z in range(depth):
                        self.sum_into(place, which, e, f, z)
                self.third_hop(place, which, f).start()
        elif number == 2:
            for f in range(1, span_f):
                self.third_hop(place, which, f).wait_recv()
            for e in range(span_e - 1, 0, -1):
                for z in range(depth):
                    self.sum_into(place, which, e, 0, z)
                self.second_hop(place, which, e).start()
        else:
            if span_e == 1:
                for f in range(1, span_f):
                    self.third_hop(place, which, f).wait_recv()
            for e in range(1, span_e):
                self.second_hop(place, which, e).wait_recv()
            for d in range(1, depth):
                self.sum_into(place, which, 0, 0, place.level(d))
                self.first_hop(place, which, d).start()

    def result(self, which, side):
        return half(self.results[which], self.block(which), side)

    def last(self, place, which, side):
        share = self.result(which, side)
        return remote(share, share, self.last_send.at[which], self.last_recv.at[which], place.other)

    def finish(self, which, marks=None):
        place = Place(self.dims)
        parts = self.parts(place, which, 0, 0, place.deep)
        for d in range(1, place.spans[0]):
            self.first_hop(place, which, d).wait_recv()
            parts.append(self.first[which].at[d - 1])
        share = self.result(which, place.core)

        def store(at_rows, total, carry):
            share[at_rows, :] = total
            kept, plain = carry
            squared = total * total
            if marks is not None:
                marked = squared * marks[place.core, at_rows, :]
                plain = plain + folded_squares(marked)
                squared = squared - marked
            return (kept + folded_squares(squared), plain)

        squares = self.added(parts, store, (jnp.zeros((8, lanes), jnp.float32),) * 2)
        self.last(place, which, place.core).start()
        return squares

    def settle(self, which):
        place = Place(self.dims)
        last = self.last(place, which, 1 - place.core)
        last.wait_recv()
        last.wait_send()
        self.swap(place, which).wait_send()
        for f in range(1, place.spans[2]):
            self.third_hop(place, which, f).wait_send()
        for e in range(1, place.spans[1]):
            self.second_hop(place, which, e).wait_send()
        for d in range(1, place.spans[0]):
            self.first_hop(place, which, d).wait_send()


def folded_squares(values):
    total = None
    if values.shape[1] < lanes:
        first = lax.broadcasted_iota(jnp.int32, (values.shape[0], lanes), 1) == 0
        values = jnp.where(first, jnp.sum(values, axis=1, keepdims=True), 0.0)
    for row in range(0, values.shape[0], 8):
        for column in range(0, values.shape[1], lanes):
            piece = values[row : row + 8, column : column + lanes]
            total = piece if total is None else total + piece
    return total


def send_to_all(place, source, landing, send_sem, recv_sem):
    number = landing.shape[0]
    for hop in range(1, number):
        target = lax.rem(place.me + hop, number)
        remote(
            source(target), landing.at[place.me], send_sem.at[hop], recv_sem.at[hop], {"narrow": target}
        ).start()


def sum_of_all(place, own, landing, send_sem, recv_sem):
    number = landing.shape[0]
    landing[place.me] = own
    for hop in range(1, number):
        came = landing.at[lax.rem(place.me + number - hop, number)]
        copy = remote(came, came, send_sem.at[hop], recv_sem.at[hop], place.other)
        copy.wait_recv()
        copy.wait_send()
    total = landing[0]
    for spot in range(1, number):
        total = total + landing[spot]
    return total


def sum_of_cores(place, own, landing, send_sem, recv_sem):
    landing[place.core] = own
    copy = remote(landing.at[place.core], landing.at[place.core], send_sem, recv_sem, place.other)
    copy.start()
    copy.wait()
    return landing[0] + landing[1]


def grid_of(mesh):
    number = mesh.shape["narrow"]
    places = [getattr(device, "coords", None) for device in mesh.devices[0]]
    if all(place is not None for place in places):
        sizes = [len({place[axis] for place in places}) for axis in (2, 1, 0)]
        if sizes[0] * sizes[1] * sizes[2] == number:
            return tuple(sizes)
    side = round((number / 2) ** (1 / 3))
    return (2 * side, side, side) if 2 * side**3 == number else (number, 1, 1)


def plan_of(select_rows, state_size, tap_count, step_rows):
    plan, first = {}, 0
    for name, tall in (
        ("select", select_rows),
        ("decay", state_size),
        ("taps", tap_count),
        ("shift", 1),
        ("bias", 1),
        ("skip", 1),
        ("gain", 1),
    ):
        plan[name] = (first, tall)
        first += tall
    plan["step"] = (lanes, step_rows)
    plan["rows"] = -(-(lanes + step_rows) // 32) * 32
    return plan


def per_device(
    dims,
    tokens,
    cotangent,
    loss_mask,
    seq_lengths,
    norm_gain,
    in_proj,
    conv_weight,
    conv_bias,
    select_proj,
    step_proj,
    step_bias,
    decay_log,
    skip_scale,
    out_proj,
):
    half = jnp.bfloat16
    piece = skip_scale.shape[0]
    gain_piece = norm_gain.shape[0]
    rank, size = step_proj.shape[0], decay_log.shape[0]
    plan = plan_of(select_proj.shape[0], size, conv_weight.shape[0], rank)
    smalls = {
        "select": select_proj,
        "decay": decay_log,
        "taps": conv_weight,
        "shift": conv_bias[None],
        "bias": step_bias[None],
        "skip": skip_scale[None],
        "gain": norm_gain[None],
        "step": step_proj,
    }
    depth, planes = dims[0], dims[1] * dims[2]
    number = depth * planes
    in_rows = in_proj.shape[0]
    rows, model = tokens.shape
    inner = piece * number
    width = 4 * lanes
    blocks = inner // width
    chunks = rows // chunk
    mask_row = loss_mask[None]

    whole = pl.BlockSpec(memory_space=pltpu.VMEM)
    tall = pl.BlockSpec((rows, width), lambda b: (0, b))
    deep = pl.BlockSpec((chunks, chunk, width), lambda b: (0, 0, b))
    lead = pl.BlockSpec((rows, size, width), lambda b: (0, 0, b))
    first_w = pl.BlockSpec((model, width), lambda b: (0, b))
    second_w = pl.BlockSpec((model, width), lambda b: (0, b + blocks))
    out_w = pl.BlockSpec((width, model), lambda b: (b, 0))

    def thin(height):
        return pl.BlockSpec((height, width), lambda b: (0, b))

    def fixed(*dims_of):
        return pl.BlockSpec(dims_of, lambda b: (0,) * len(dims_of))

    scalars = pl.BlockSpec(memory_space=pltpu.SMEM)
    offset_buf = pltpu.VMEM((rows + 8, lanes), jnp.int32)
    packed = thin(plan["rows"])

    pair = (chunks, 2 * chunk, lanes)
    pair = (chunks, 2 * chunk, lanes)
    anywhere = pl.BlockSpec(memory_space=pl.ANY)
    small_half = (2, plan["rows"] // 2, piece)
    in_half = (in_rows, width)
    shares = 2
    in_share = (in_rows, inner // shares)
    out_share = (out_proj.shape[0], model // shares)
    (
        branch,
        signal,
        slope,
        projected,
        flipped,
        normed,
        grad_low,
        write_pair,
        read_pair,
        small,
        gain_value,
        in_blocks,
    ) = compute_call(
        functools.partial(front_kernel, plan, dims, tuple(smalls)),
        "front",
        blocks,
        [scalars, whole, whole, whole] + [whole] * len(smalls) + [fixed(in_rows, inner)],
        [tall, tall, tall] + [whole] * 8 + [anywhere],
        [
            shape((rows, inner)),
            shape((rows, inner), half),
            shape((rows, inner)),
            shape((rows, lanes)),
            shape((model, rows), half),
            shape((rows, model), half),
            shape((rows, model), half),
            shape(pair, half),
            shape(pair, half),
            shape((plan["rows"], inner), half),
            shape((1, model)),
            shape((shares, depth, planes) + in_share, half),
        ],
        [
            offset_buf,
            pltpu.VMEM((plan["rows"], piece), jnp.float32),
            pltpu.VMEM(small_half, half),
            pltpu.VMEM((shares,) + in_share, half),
            pltpu.VMEM((depth, planes) + small_half, half),
            pltpu.VMEM((shares, depth, planes) + in_share, half),
            pltpu.SemaphoreType.DMA((shares,)),
        ]
        + Gather.sems(shares + 1, dims),
        4 * rows * model * inner,
        (seq_lengths, tokens, cotangent, mask_row, *smalls.values(), in_proj),
        collective_id=0,
    )
    groups = 2
    part, pieces = rows // groups, chunks // groups
    row_block = pltpu.VMEM((pieces, chunk, width), jnp.float32)
    spread_block = pltpu.VMEM((rows, size, lanes), jnp.float32)
    fold_block = pltpu.VMEM((width // lanes, chunk * chunk, lanes), jnp.float32)

    def by_group(order, *dims_of):
        middle = (0,) * (len(dims_of) - 2)
        return pl.BlockSpec(dims_of, lambda b, g: (order(g),) + middle + (b,))

    def by_token(order, *dims_of):
        return pl.BlockSpec(dims_of, lambda b, g: (order(g),) + (0,) * (len(dims_of) - 1))

    def by_channel(height):
        return pl.BlockSpec((height, width), lambda b, g: (0, b))

    def onward(g):
        return g

    def backward(g):
        return groups - 1 - g

    states, step, core, begins, gate_blocks, out_blocks = compute_call(
        functools.partial(forward_kernel, plan, dims),
        "forward",
        (blocks, groups),
        [
            scalars,
            by_token(onward, part, lanes),
            by_channel(plan["rows"]),
            by_group(onward, part, width),
            whole,
            whole,
            pl.BlockSpec((in_rows, inner), lambda b, g: (0, 1)),
            whole,
        ],
        [
            by_group(onward, part, size, width),
            by_group(onward, pieces, chunk, width),
            by_group(onward, pieces, chunk, width),
            by_group(onward, 1, size, width),
            anywhere,
            anywhere,
        ],
        [
            shape((rows, size, inner)),
            shape((chunks, chunk, inner)),
            shape((chunks, chunk, inner)),
            shape((groups, size, inner)),
            shape((shares, depth, planes) + in_share, half),
            shape((shares, depth, planes) + out_share, half),
        ],
        [
            offset_buf,
            pltpu.VMEM((part, width), jnp.float32),
            row_block,
            row_block,
            spread_block,
            spread_block,
            fold_block,
            pltpu.VMEM((size, width), jnp.float32),
            pltpu.VMEM((shares,) + in_share, half),
            pltpu.VMEM((shares,) + out_share, half),
        ]
        + Gather.sems(2 * shares, dims),
        15 * rows * inner * size,
        (seq_lengths, projected, small, signal, write_pair, read_pair, in_proj, out_proj),
        collective_id=2,
    )
    split = in_share[1] // width
    weights = pl.BlockSpec((None, number, in_rows, width), lambda b: (b // split, 0, 0, b % split))
    per_block = width // out_share[0]
    out_pieces = pl.BlockSpec((shares, per_block) + out_share, lambda b: (0, b, 0, 0))
    branch_whole = in_blocks.reshape(shares, number, *in_share)
    gate_whole = gate_blocks.reshape(shares, number, *in_share)
    out_whole = out_blocks.reshape(shares, number, *out_share)
    core_grad, gate_grad, grad_skip, grad_outw, grad_in_gate, output = compute_call(
        functools.partial(middle_kernel, plan),
        "middle",
        blocks,
        [deep, packed, tall, weights, whole, out_pieces, whole, whole, whole],
        [
            deep,
            tall,
            thin(1),
            pl.BlockSpec((shares, width, out_share[1]), lambda b: (0, b, 0)),
            pl.BlockSpec((None, model, width), lambda b: (b // split, 0, b % split)),
            fixed(rows, model),
        ],
        [
            shape((chunks, chunk, inner)),
            shape((rows, inner), half),
            shape((1, inner)),
            shape((shares, inner, out_share[1]), half),
            shape((shares, model, in_share[1]), half),
            shape((rows, model), half),
        ],
        [
            pltpu.VMEM((rows, width), jnp.float32),
            pltpu.VMEM((rows, width), jnp.float32),
            pltpu.VMEM((rows, width), half),
            pltpu.VMEM((width, model), half),
            pltpu.VMEM((rows, model), jnp.float32),
        ],
        8 * rows * model * inner,
        (core, small, signal, gate_whole, grad_low, out_whole, flipped, normed, tokens),
    )
    early_grads = [
        grad_outw.reshape((shares, depth, planes) + out_share),
        grad_in_gate.reshape((shares, depth, planes) + in_share),
    ]
    early_sums = [shape(out_proj.shape), shape((in_rows, inner))]
    early_pieces = [shape((depth, planes) + block, half) for block in (in_share, out_share)] * shares
    (
        signal_grad,
        grad_stepw,
        grad_bias,
        grad_decaylog,
        flat,
        out_sum,
        in_gate_sum,
        early_squares,
    ) = compute_call(
        functools.partial(backward_kernel, plan, dims),
        "backward",
        (blocks, groups),
        [
            scalars,
            by_token(backward, part, lanes),
            by_channel(plan["rows"]),
            by_group(backward, part, width),
            whole,
            whole,
            by_group(backward, pieces, chunk, width),
            by_group(backward, pieces, chunk, width),
            by_group(backward, part, size, width),
            by_group(backward, 1, size, width),
            anywhere,
            anywhere,
        ],
        [
            by_group(backward, part, width),
            by_channel(rank),
            by_channel(1),
            by_channel(size),
            whole,
        ]
        + [whole] * 3,
        [
            shape((rows, inner)),
            shape((rank, inner)),
            shape((1, inner)),
            shape((size, inner)),
            shape((rows, lanes), half),
            *early_sums,
            shape((8, lanes)),
        ],
        [
            offset_buf,
            row_block,
            row_block,
            spread_block,
            spread_block,
            fold_block,
            fold_block,
            row_block,
            row_block,
            pltpu.VMEM((part, width), half),
            pltpu.VMEM((size, width), jnp.float32),
            pltpu.VMEM((chunks, chunk, lanes), jnp.float32),
            spread_block,
            spread_block,
        ]
        + [pltpu.VMEM((shares,) + block, jnp.float32) for block in (in_share, out_share)]
        + Reduce.rooms(dims, early_pieces, False)
        + Reduce.sems(2 * shares, dims),
        40 * rows * inner * size,
        (
            seq_lengths,
            projected,
            small,
            signal,
            write_pair,
            read_pair,
            step,
            core_grad,
            states,
            begins,
            *early_grads,
        ),
        collective_id=3,
    )

    plain_rows = np.zeros((plan["rows"], piece), np.float32)
    for name in ("bias", "decay", "skip"):
        first, count = plan[name]
        plain_rows[first : first + count] = 1.0
    late_grads = [shape((depth, planes) + small_half, half)]
    late_grads += [shape((depth, planes, in_rows, width), half)] * blocks
    taps_n = conv_weight.shape[0]
    late = {"taps": (0, taps_n), "shift": (taps_n, 1), "gain": (taps_n + 1, 1)}
    late_block = (8, piece)

    tokens_grad, in_branch_sum, small_sum, late_sum, norms = compute_call(
        functools.partial(back_kernel, plan, dims),
        "back",
        blocks,
        [scalars, whole, whole, whole, packed, whole, tall, whole, tall, tall, tall, whole]
        + [weights, weights]
        + [whole] * 6,
        [whole] * 5,
        [
            shape((rows, model), half),
            shape((in_rows, inner)),
            shape(small_half),
            shape(late_block),
            shape((2, 8, lanes)),
        ],
        [
            offset_buf,
            pltpu.VMEM((rows + 8, width), jnp.float32),
            pltpu.VMEM((rows, width), half),
            pltpu.VMEM((rows, model), jnp.float32),
            pltpu.VMEM((blocks,) + late_grads[1].shape, half),
            pltpu.VMEM(late_grads[0].shape, late_grads[0].dtype),
            pltpu.VMEM((number,) + late_block, jnp.float32),
            pltpu.VMEM((number,) + late_block, jnp.float32),
            pltpu.VMEM((2,) + late_block, jnp.float32),
            pltpu.VMEM((2, 8, lanes), jnp.float32),
            pltpu.VMEM((number, 2, 8, lanes), jnp.float32),
            pltpu.VMEM((2, 2, 8, lanes), jnp.float32),
            pltpu.VMEM((blocks, in_rows, width), jnp.float32),
            pltpu.VMEM(small_half, jnp.float32),
            pltpu.SemaphoreType.DMA((2, number)),
            pltpu.SemaphoreType.DMA((2, number)),
        ]
        + Reduce.rooms(dims, late_grads, True)
        + Reduce.sems(blocks + 1, dims),
        8 * rows * model * inner,
        (
            seq_lengths,
            tokens,
            grad_low,
            gain_value,
            small,
            flat,
            branch,
            signal,
            slope,
            signal_grad,
            gate_grad,
            flipped,
            branch_whole,
            gate_whole,
            grad_stepw,
            grad_bias,
            grad_decaylog,
            grad_skip,
            jnp.asarray(plain_rows.reshape(small_half)),
            early_squares,
        ),
        collective_id=1,
    )

    names = ("gain", "taps", "shift", "select", "step", "bias", "decay", "skip")
    own = (norm_gain, conv_weight, conv_bias, select_proj, step_proj, step_bias, decay_log, skip_scale)
    in_grad, out_grad, grad_tokens, gain_grad, *small_grads, decay_sq, plain_sq = pl.pallas_call(
        functools.partial(finish_kernel, plan, names, late),
        in_specs=[whole] * 7,
        out_specs=[whole] * (3 + len(names)) + [scalars] * 2,
        out_shape=[shape(in_proj.shape), shape(out_proj.shape), shape(tokens.shape, half)]
        + [shape(array.shape) for array in own]
        + [shape((1, 1))] * 2,
        name="finish",
    )(
        tokens_grad,
        in_branch_sum,
        in_gate_sum,
        out_sum,
        small_sum.reshape(plan["rows"], piece),
        late_sum,
        norms,
    )
    return (
        output,
        grad_tokens,
        gain_grad,
        in_grad,
        *small_grads,
        out_grad,
        decay_sq[0, 0],
        plain_sq[0, 0],
    )


def solution(mesh):
    placed = (
        P(("wide", "narrow"), None),
        P(("wide", "narrow"), None),
        P(("wide", "narrow")),
        P(("wide", "narrow"), None),
        P("narrow"),
        P("narrow", None),
        P(None, "narrow"),
        P("narrow"),
        P(None, "narrow"),
        P(None, "narrow"),
        P("narrow"),
        P(None, "narrow"),
        P("narrow"),
        P("narrow", None),
    )
    return jax.shard_map(
        functools.partial(per_device, grid_of(mesh)),
        mesh=mesh,
        in_specs=placed,
        out_specs=(
            P(("wide", "narrow"), None),
            P(("wide", "narrow"), None),
            P("narrow"),
            P("narrow", None),
            P(None, "narrow"),
            P("narrow"),
            P(None, "narrow"),
            P(None, "narrow"),
            P("narrow"),
            P(None, "narrow"),
            P("narrow"),
            P("narrow", None),
            P(),
            P(),
        ),
        check_vma=False,
    )
```

```python
import functools
import math

import jax
import jax.numpy as jnp
import numpy as np
from jax import lax
from jax.experimental import pallas as pl
from jax.experimental.pallas import tpu as pltpu
from jax.sharding import PartitionSpec as P

epsilon = 1e-05
chunk = 8
lanes = 128
log2e = math.log2(math.e)
ln2 = math.log(2.0)
far = 1e30


def contract(left, right, left_dim, right_dim):
    return lax.dot_general(
        left, right, (((left_dim,), (right_dim,)), ((), ())), preferred_element_type=jnp.float32
    )


def row_loop(rows, group, body, initial):
    def some(index, carry):
        return body(index, pl.ds(pl.multiple_of(index * group, group), group), carry)

    return lax.fori_loop(0, rows // group, some, initial)


def cut(tile):
    return pl.ds(tile * lanes, lanes)


def sigmoid(values):
    return 0.5 * jnp.tanh(0.5 * values) + 0.5


def softplus(values):
    small = jnp.exp(-jnp.abs(values))
    series = small * (1.0 - small * (0.5 - small * (1.0 / 3.0 - 0.25 * small)))
    return jnp.maximum(values, 0.0) + jnp.where(small < 0.03, series, jnp.log(1.0 + small))


def slope_of(step):
    return 1.0 - jnp.exp(-step)


def fill_offsets(lengths_ref, offset_buf, rows):
    place = lax.broadcasted_iota(jnp.int32, offset_buf.shape, 0)
    start = jnp.zeros(offset_buf.shape, jnp.int32)
    ahead = jnp.int32(0)
    for index in range(lengths_ref.shape[1] - 1):
        ahead = ahead + lengths_ref[0, index]
        start = jnp.where(place >= ahead, ahead, start)
    offset_buf[...] = jnp.where(place < rows, place - start, 0)


def small_rows(small_ref, first, count):
    base = first // 16 * 16
    tall = -(-(first + count - base) // 16) * 16
    return small_ref[base : base + tall, :].astype(jnp.float32)[first - base : first - base + count]


def eight(values):
    total = values[:8]
    for row in range(8, values.shape[0], 8):
        total = total + values[row : row + 8]
    return total


def conv_rows(index, at, group, tile, branch_ref, offset_buf, taps, shift):
    count = taps.shape[0]
    here = slice(tile * lanes, (tile + 1) * lanes)
    current = branch_ref[at, cut(tile)]
    before = branch_ref[pl.ds(pl.multiple_of(jnp.maximum(index * group - 8, 0), 8), 8), cut(tile)]
    both = jnp.concatenate([before, current], axis=0)
    offsets = offset_buf[at, :]
    summed = shift[:, here] + taps[count - 1 : count, here] * current
    for tap in range(count - 1):
        lag = count - 1 - tap
        read = jnp.where(offsets >= lag, pltpu.roll(both, lag, 0)[8:], 0.0)
        summed = summed + taps[tap : tap + 1, here] * read
    return summed


def rows_of(blocks):
    return as_matrix(blocks[...][None])


def as_matrix(blocks):
    columns = blocks.shape[3]
    if blocks.shape[2] % 16:
        return blocks.astype(jnp.float32).reshape(-1, columns).astype(blocks.dtype)
    return blocks.reshape(-1, columns)


def front_kernel(
    plan,
    dims,
    names,
    lengths_ref,
    tokens_ref,
    cotangent_ref,
    mask_ref,
    *refs,
):
    smalls, in_ref, out_ref, refs = refs[: len(names)], refs[len(names)], refs[len(names) + 1], refs[len(names) + 2 :]
    branch_ref, signal_ref, slope_ref, projected_ref, flipped_ref, normed_ref, low_ref = refs[:7]
    write_pair, read_pair, small_out, gain_ref, whole_ref, out_whole = refs[7:13]
    offset_buf, pack_buf, own_small, own_in, own_out, land_small, land_in, store_sem = refs[13:21]
    own_gain, land_gain, gain_send, gain_recv = refs[21:25]
    rows = tokens_ref.shape[0]
    width = branch_ref.shape[1]
    block = pl.program_id(0)
    last = whole_ref.shape[0]
    outs = out_whole.shape[0]
    gather = Gather(
        dims,
        [own_small] + [own_in.at[index] for index in range(last)] + [own_out.at[index] for index in range(outs)],
        [land_small] + [land_in.at[index] for index in range(last)] + [out_whole.at[index] for index in range(outs)],
        refs[25:],
    )
    count = 1 + last + outs
    tall = pack_buf.shape[0] // 2

    def stored(index):
        return pltpu.make_async_copy(land_in.at[index], whole_ref.at[index], store_sem.at[index])

    def move_on(plan_of_moves):
        for moment, legs in plan_of_moves:

            @pl.when(block == moment)
            def _(legs=legs):
                for which, number in legs:
                    gather.leg(which, number)

    @pl.when(block == 0)
    def _():
        pack_buf[...] = jnp.zeros_like(pack_buf)
        for name, ref in zip(names, smalls):
            first, height = plan[name]
            pack_buf[first : first + height, : ref.shape[1]] = ref[...]
        own_gain[...] = jnp.zeros_like(own_gain)
        own_gain[0:1, : gain_ref.shape[1] // land_gain.shape[0]] = smalls[names.index("gain")][...]
        for side in range(2):
            own_small[side] = pack_buf[side * tall : (side + 1) * tall, :].astype(own_small.dtype)
        for index in range(last):
            own_in[index] = in_ref[:, index * width : (index + 1) * width].astype(own_in.dtype)
        place = Place(dims)
        place.greet(everyone=True)
        send_to_all(place, lambda target: own_gain, land_gain, gain_send, gain_recv)
        for index in (1, 0) + tuple(range(2, last + 1)):
            gather.start(index)
        each = own_out.shape[2]
        for index in range(outs):
            own_out[index] = out_ref[:, index * each : (index + 1) * each].astype(own_out.dtype)
            gather.start(last + 1 + index)
        fill_offsets(lengths_ref, offset_buf, rows)
        gather.leg(1, 1)
        gather.leg(0, 1)
        wait_for_all(place, own_gain[...], land_gain, gain_send, gain_recv)
        each = gain_ref.shape[1] // land_gain.shape[0]
        for owner in range(land_gain.shape[0]):
            gain_ref[:, owner * each : (owner + 1) * each] = (
                land_gain[owner, 0:1, :each].astype(jnp.bfloat16).astype(jnp.float32)
            )

        def norm(index, at, carry):
            residual = tokens_ref[at, :].astype(jnp.float32)
            scale = lax.rsqrt(jnp.mean(residual * residual, axis=1, keepdims=True) + epsilon)
            normed_ref[at, :] = (residual * scale * gain_ref[...]).astype(normed_ref.dtype)
            return carry

        row_loop(rows, 16, norm, 0)
        gather.leg(1, 2)
        gather.leg(0, 2)
        gather.leg(2, 1)
        flipped_ref[...] = normed_ref[...].T
        gather.leg(1, 3)
        gather.leg(0, 3)
        gather.leg(2, 2)
        down = lax.broadcasted_iota(jnp.int32, (rows, rows), 0)
        along = lax.broadcasted_iota(jnp.int32, (rows, rows), 1)
        diagonal = jnp.where(down == along, mask_ref[...].astype(jnp.float32), 0.0).astype(low_ref.dtype)
        low_ref[...] = jnp.dot(
            diagonal, cotangent_ref[...], preferred_element_type=jnp.float32
        ).astype(low_ref.dtype)
        projected_ref[...] = jnp.zeros_like(projected_ref)

    for index in range(last):

        @pl.when(block == index)
        def _(index=index):
            gather.arrive(index + 1)
            stored(index).start()

    branch_w = as_matrix(land_in[block])
    branch_ref[...] = jnp.dot(normed_ref[...], branch_w, preferred_element_type=jnp.float32)
    move_on(((0, ((3, 1), (2, 3))), (1, ((4, 2), (3, 3), (5, 1))), (2, ((4, 3), (5, 2), (6, 1))), (3, ((6, 2),))))

    @pl.when(block == 0)
    def _():
        gather.arrive(0)
        share = land_small.shape[4]
        for z in range(land_small.shape[0]):
            for plane in range(land_small.shape[1]):
                owner = z * land_small.shape[1] + plane
                for side in range(2):
                    small_out[side * tall : (side + 1) * tall, owner * share : (owner + 1) * share] = land_small[
                        z, plane, side
                    ]

    small_ref = small_out.at[:, pl.ds(pl.multiple_of(block * width, width), width)]
    taps = small_rows(small_ref, *plan["taps"])
    shift = small_rows(small_ref, *plan["shift"])

    def some(index, at, carry):
        for tile in range(width // lanes):
            summed = conv_rows(index, at, 32, tile, branch_ref, offset_buf, taps, shift)
            sigma = sigmoid(summed)
            active = summed * sigma
            signal_ref[at, cut(tile)] = active.astype(signal_ref.dtype)
            slope_ref[at, cut(tile)] = sigma + active * (1.0 - sigma)
        return carry

    row_loop(rows, 32, some, 0)
    move_on(((0, ((4, 1), (3, 2))), (2, ((5, 3),))))
    projected_ref[...] += contract(signal_ref[...], small_ref[:lanes, :], 1, 1)

    @pl.when(block == pl.num_programs(0) - 1)
    def _():
        gather.leg(count - 1, 3)
        high, low = high_low(projected_ref[...])
        own = own_tokens(rows)
        rank = plan["step"][1]
        size = plan["decay"][1]
        entry = lax.broadcasted_iota(jnp.int32, (lanes, lanes), 0)
        lane = lax.rem(lax.broadcasted_iota(jnp.int32, (lanes, lanes), 1), size)
        for first, pair in ((rank, write_pair), (rank + size, read_pair)):
            spread = (entry == lane + first).astype(jnp.bfloat16)
            parts = [
                (jnp.dot(part.astype(jnp.bfloat16), spread, preferred_element_type=jnp.float32) * own).reshape(
                    rows // chunk, chunk, lanes
                )
                for part in (high, low)
            ]
            pair[...] = jnp.concatenate(parts, axis=1).astype(pair.dtype)
        for index in range(outs):
            gather.arrive(last + 1 + index)
        for index in range(count):
            gather.drain(index)
        for index in range(last):
            stored(index).wait()


def high_low(values):
    high = values.astype(jnp.bfloat16).astype(jnp.float32)
    return high, values - high


def own_tokens(rows):
    token = lax.rem(lax.broadcasted_iota(jnp.int32, (rows, lanes), 0), chunk)
    return (token == lax.div(lax.broadcasted_iota(jnp.int32, (rows, lanes), 1), lanes // chunk)).astype(
        jnp.float32
    )


def spread_all(pairs, target):
    some = 8

    def spread(index, carry):
        rows = jnp.concatenate([pairs[index * some + number] for number in range(some)], axis=1)
        wide = contract(rows, jnp.ones((rows.shape[0], lanes), rows.dtype), 0, 0)
        target[pl.ds(index * some * chunk, some * chunk)] = wide.reshape(some * chunk, -1, lanes)
        return carry

    lax.fori_loop(0, pairs.shape[0] // some, spread, 0)


def folded(buffer, tile):
    total = buffer[tile, pl.ds(0, chunk, stride=chunk), :]
    for row in range(1, chunk):
        total = total + buffer[tile, pl.ds(row, chunk, stride=chunk), :]
    return total


def forward_kernel(
    plan,
    dims,
    lengths_ref,
    projected_ref,
    small_ref,
    signal_ref,
    write_pair,
    read_pair,
    gate_own,
    states_ref,
    step_ref,
    core_ref,
    begin_ref,
    gate_whole,
    offset_buf,
    pre_buf,
    decay_step,
    flows,
    write_wide,
    read_wide,
    fold_buf,
    held_buf,
    gate_low,
    *sems,
):
    rows, width = pre_buf.shape
    size = plan["decay"][1]
    half_size = size // 2
    tiles = width // lanes
    chunks = rows // chunk
    rank = plan["step"][1]
    group = pl.program_id(1)
    groups = pl.num_programs(1)
    moment = pl.program_id(0) * groups + group
    moments = pl.num_programs(0) * groups
    count = gate_low.shape[0]
    gather = Gather(
        dims,
        [gate_low.at[index] for index in range(count)],
        [gate_whole.at[index] for index in range(count)],
        sems,
    )

    @pl.when(moment == 0)
    def _():
        each = gate_low.shape[2]
        for index in range(count):
            gate_low[index] = gate_own[:, index * each : (index + 1) * each].astype(gate_low.dtype)
        Place(dims).greet()
        for which in range(count):
            gather.start(which)
        fill_offsets(lengths_ref, offset_buf, offset_buf.shape[0] - 8)
        spread_all(write_pair, write_wide)
        spread_all(read_pair, read_wide)

    @pl.when(group == 0)
    def _():
        held_buf[...] = jnp.zeros_like(held_buf)

    begin_ref[0] = held_buf[...]
    pre_buf[...] = jnp.dot(
        projected_ref[:, :rank].astype(small_ref.dtype),
        small_ref[pl.ds(plan["step"][0], rank), :],
        preferred_element_type=jnp.float32,
    )
    bias = small_rows(small_ref, *plan["bias"])

    def before(index, at, carry):
        spot = pl.ds(pl.multiple_of(index * 4, 4), 4)
        inside = offset_buf[pl.ds(pl.multiple_of(group * rows + index * 32, 32), 32), :] > 0
        for tile in range(tiles):
            step = softplus(pre_buf[at, cut(tile)] + bias[:, tile * lanes : (tile + 1) * lanes])
            step_ref[spot, :, cut(tile)] = step.reshape(4, chunk, lanes)
            decay_step[spot, :, cut(tile)] = jnp.where(inside, step, far).reshape(4, chunk, lanes)
            flow = step * signal_ref[at, cut(tile)].astype(jnp.float32)
            flows[spot, :, cut(tile)] = flow.reshape(4, chunk, lanes)
        return carry

    row_loop(rows, 4 * chunk, before, 0)
    rates = -jnp.exp(small_rows(small_ref, *plan["decay"])) * log2e
    rates = [rates[:, tile * lanes : (tile + 1) * lanes] for tile in range(tiles)]

    def forward(index, held):
        held = list(held)
        for place in range(chunk):
            now = index * chunk + place
            write_now = write_wide[group * rows + now]
            read_now = read_wide[group * rows + now]
            for tile in range(tiles):
                decay = jnp.exp2(rates[tile] * decay_step[index, pl.ds(place, 1), cut(tile)])
                fresh = decay * held[tile] + write_now * flows[index, pl.ds(place, 1), cut(tile)]
                held[tile] = fresh
                states_ref[now, :, cut(tile)] = fresh
                product = read_now * fresh
                fold_buf[tile, pl.ds(place * chunk, chunk), :] = product[:half_size] + product[half_size:]
        for tile in range(tiles):
            core_ref[index, :, cut(tile)] = folded(fold_buf, tile)
        return tuple(held)

    held = tuple(held_buf[:, cut(tile)] for tile in range(tiles))
    schedule = {}
    for which in range(count):
        for number in (1, 2, 3):
            schedule.setdefault(min((4, 7)[which] + (0, 4, 7)[number - 1], 2 * 8), []).append((which, number))

    def move_on(legs):
        for which, number in legs:
            gather.leg(which, number)

    for half_loop in range(2):
        for point, legs in sorted(schedule.items()):
            if point < 16 and point % 2 == half_loop:
                pl.when(moment == point // 2)(functools.partial(move_on, legs))
        held = lax.fori_loop(half_loop * chunks // 2, (half_loop + 1) * chunks // 2, forward, held)
    for tile in range(tiles):
        held_buf[:, cut(tile)] = held[tile]

    @pl.when(moment == moments - 1)
    def _():
        move_on(sorted(schedule.get(16, ()), key=sum))
        for which in range(count):
            gather.arrive(which)
        for which in range(count):
            gather.drain(which)


def middle_kernel(
    plan,
    core_ref,
    small_ref,
    signal_ref,
    gate_w,
    low_ref,
    out_w,
    flipped_ref,
    normed_ref,
    tokens_ref,
    core_grad_ref,
    gate_grad_ref,
    skip_grad_ref,
    out_grad_ref,
    in_grad_ref,
    output_ref,
    pre_buf,
    gate_buf,
    gated_buf,
    out_buf,
    total,
):
    rows, width = pre_buf.shape
    tiles = width // lanes
    block = pl.program_id(0)
    each = out_w.shape[3]
    for index in range(out_w.shape[0]):
        out_buf[:, index * each : (index + 1) * each] = as_matrix(out_w[index][None])
    gate_buf[...] = jnp.dot(normed_ref[...], rows_of(gate_w), preferred_element_type=jnp.float32)
    pre_buf[...] = contract(low_ref[...], out_buf[...], 1, 1)
    skip = small_rows(small_ref, *plan["skip"])

    def after(index, at, carry):
        spot = pl.ds(pl.multiple_of(index * 4, 4), 4)
        sums = []
        for tile in range(tiles):
            signal = signal_ref[at, cut(tile)].astype(jnp.float32)
            core = core_ref[spot, :, cut(tile)].reshape(4 * chunk, lanes)
            core = core + skip[:, tile * lanes : (tile + 1) * lanes] * signal
            gate = gate_buf[at, cut(tile)]
            sigma = sigmoid(gate)
            active = gate * sigma
            gated_buf[at, cut(tile)] = (core * active).astype(gated_buf.dtype)
            grad_gated = pre_buf[at, cut(tile)]
            grad_core = grad_gated * active
            core_grad_ref[spot, :, cut(tile)] = grad_core.reshape(4, chunk, lanes)
            slope = sigma + active * (1.0 - sigma)
            gate_grad_ref[at, cut(tile)] = (grad_gated * core * slope).astype(gate_grad_ref.dtype)
            sums.append(carry[tile] + eight(grad_core * signal))
        return tuple(sums)

    zero_rows = jnp.zeros((8, lanes), jnp.float32)
    skips = row_loop(rows, 4 * chunk, after, (zero_rows,) * tiles)
    for tile in range(tiles):
        skip_grad_ref[:, cut(tile)] = jnp.sum(skips[tile], axis=0, keepdims=True)
    out_grad = contract(gated_buf[...], low_ref[...], 0, 0).astype(out_grad_ref.dtype)
    for index in range(out_w.shape[0]):
        out_grad_ref[index] = out_grad[:, index * each : (index + 1) * each]
    in_grad_ref[...] = jnp.dot(
        flipped_ref[...], gate_grad_ref[...], preferred_element_type=jnp.float32
    ).astype(in_grad_ref.dtype)
    piece = jnp.dot(gated_buf[...], out_buf[...], preferred_element_type=jnp.float32)

    @pl.when(block == 0)
    def _():
        total[...] = piece

    @pl.when(block > 0)
    def _():
        total[...] += piece

    @pl.when(block == pl.num_programs(0) - 1)
    def _():
        output_ref[...] = (tokens_ref[...].astype(jnp.float32) + total[...]).astype(output_ref.dtype)


def backward_kernel(
    plan,
    dims,
    lengths_ref,
    projected_ref,
    small_ref,
    signal_ref,
    write_pair,
    read_pair,
    step_ref,
    core_grad_ref,
    states_ref,
    begin_ref,
    out_grad_ref,
    in_grad_ref,
    signal_grad_ref,
    step_w_grad_ref,
    bias_grad_ref,
    decay_grad_ref,
    flat_ref,
    out_sum_ref,
    in_sum_ref,
    square_ref,
    offset_buf,
    decay_step,
    flows,
    write_wide,
    read_wide,
    first_buf,
    second_buf,
    through_buf,
    scaled_buf,
    low_buf,
    incoming_buf,
    rank_buf,
    write_buf,
    read_buf,
    *parts,
):
    rows, width = low_buf.shape
    rank = plan["step"][1]
    size = plan["decay"][1]
    half_size = size // 2
    tiles = width // lanes
    chunks = rows // chunk
    block = pl.program_id(0)
    turn = pl.program_id(1)
    groups = pl.num_programs(1)
    group = groups - 1 - turn
    moment = block * groups + turn
    moments = pl.num_programs(0) * groups
    gate_result, out_result, parts = parts[0], parts[1], parts[2:]
    pieces = gate_result.shape[0]
    count = 2 * pieces

    both = ((in_grad_ref, gate_result), (out_grad_ref, out_result))
    reduce = Reduce(
        dims,
        [ref.at[index] for index in range(pieces) for ref, _ in both],
        parts[: 6 * count],
        parts[6 * count :],
        [result.at[index] for index in range(pieces) for _, result in both],
        False,
    )

    @pl.when(moment == 0)
    def _():
        Place(dims).greet()
        for which in range(count):
            reduce.start(which)
        fill_offsets(lengths_ref, offset_buf, offset_buf.shape[0] - 8)
        spread_all(write_pair, write_wide)
        spread_all(read_pair, read_wide)
        write_buf[...] = jnp.zeros_like(write_buf)
        read_buf[...] = jnp.zeros_like(read_buf)
        rank_buf[...] = jnp.zeros_like(rank_buf)

    @pl.when(turn == 0)
    def _():
        incoming_buf[...] = jnp.zeros_like(incoming_buf)
        decay_grad_ref[...] = jnp.zeros_like(decay_grad_ref)
        bias_grad_ref[...] = jnp.zeros_like(bias_grad_ref)
        step_w_grad_ref[...] = jnp.zeros_like(step_w_grad_ref)

    def before(index, at, carry):
        spot = pl.ds(pl.multiple_of(index * 4, 4), 4)
        offsets = offset_buf[pl.ds(pl.multiple_of(group * rows + index * 32, 32), 32), :]
        inside = (offsets > 0).reshape(4, chunk, lanes)
        for tile in range(tiles):
            step = step_ref[spot, :, cut(tile)]
            decay_step[spot, :, cut(tile)] = jnp.where(inside, step, far)
            signal = signal_ref[at, cut(tile)].astype(jnp.float32).reshape(4, chunk, lanes)
            flows[spot, :, cut(tile)] = step * signal
        return carry

    row_loop(rows, 4 * chunk, before, 0)
    rates = -jnp.exp(small_rows(small_ref, *plan["decay"])) * log2e
    rates = [rates[:, tile * lanes : (tile + 1) * lanes] for tile in range(tiles)]

    def backward(position, carried):
        index = chunks - 1 - position
        incoming, decay_sums = list(carried[0]), list(carried[1])
        for place in range(chunk - 1, -1, -1):
            now = index * chunk + place
            token = group * rows + now
            write_now = write_wide[token]
            read_now = read_wide[token]
            read_sum = None
            write_sum = None
            for tile in range(tiles):
                step_now = decay_step[index, pl.ds(place, 1), cut(tile)]
                grad_now = core_grad_ref[index, pl.ds(place, 1), cut(tile)]
                if place > 0:
                    earlier = states_ref[now - 1, :, cut(tile)]
                else:
                    earlier = jnp.where(
                        index > 0, states_ref[jnp.maximum(now - 1, 0), :, cut(tile)], begin_ref[0, :, cut(tile)]
                    )
                grad_state = incoming[tile] + read_now * grad_now
                through_read = states_ref[now, :, cut(tile)] * grad_now
                through_write = grad_state * flows[index, pl.ds(place, 1), cut(tile)]
                read_sum = through_read if read_sum is None else read_sum + through_read
                write_sum = through_write if write_sum is None else write_sum + through_write
                passed = grad_state * write_now
                first_buf[tile, pl.ds(place * chunk, chunk), :] = passed[:half_size] + passed[half_size:]
                leaving = jnp.exp2(rates[tile] * step_now) * grad_state
                incoming[tile] = leaving
                weighted = leaving * earlier
                scaled = weighted * rates[tile]
                second_buf[tile, pl.ds(place * chunk, chunk), :] = scaled[:half_size] + scaled[half_size:]
                decay_sums[tile] = decay_sums[tile] + weighted * step_now
            read_buf[token] += read_sum
            write_buf[token] += write_sum
        for tile in range(tiles):
            through_buf[index, :, cut(tile)] = folded(first_buf, tile)
            scaled_buf[index, :, cut(tile)] = folded(second_buf, tile)
        return (tuple(incoming), tuple(decay_sums))

    incoming = tuple(incoming_buf[:, cut(tile)] for tile in range(tiles))
    nothing = (jnp.zeros((size, lanes), jnp.float32),) * tiles
    schedule = {}
    for which in range(count):
        for number in (1, 2, 3):
            schedule.setdefault((2, 4, 7, 9)[which] + (0, 3, 5)[number - 1], []).append((which, number))

    def move_on(legs):
        for which, number in legs:
            reduce.leg(which, number)

    carried = (incoming, nothing)
    for half_loop in range(2):
        for point, legs in sorted(schedule.items()):
            if point % 2 == half_loop:
                pl.when(moment == point // 2)(functools.partial(move_on, legs))
        carried = lax.fori_loop(half_loop * chunks // 2, (half_loop + 1) * chunks // 2, backward, carried)
    incoming, decay_sums = carried
    for tile in range(tiles):
        incoming_buf[:, cut(tile)] = incoming[tile]
        decay_grad_ref[:, cut(tile)] += decay_sums[tile] * rates[tile] * ln2
    skip = small_rows(small_ref, *plan["skip"])

    def after(index, at, carry):
        spot = pl.ds(pl.multiple_of(index * 4, 4), 4)
        sums = []
        for tile in range(tiles):
            signal = signal_ref[at, cut(tile)].astype(jnp.float32)
            step = step_ref[spot, :, cut(tile)].reshape(4 * chunk, lanes)
            through = through_buf[spot, :, cut(tile)].reshape(4 * chunk, lanes)
            scaled = scaled_buf[spot, :, cut(tile)].reshape(4 * chunk, lanes)
            core_grad = core_grad_ref[spot, :, cut(tile)].reshape(4 * chunk, lanes)
            grad_pre = (through * signal + ln2 * scaled) * slope_of(step)
            low_buf[at, cut(tile)] = grad_pre.astype(low_buf.dtype)
            signal_grad_ref[at, cut(tile)] = (
                through * step + skip[:, tile * lanes : (tile + 1) * lanes] * core_grad
            )
            sums.append(carry[tile] + eight(grad_pre))
        return tuple(sums)

    zero_rows = jnp.zeros((8, lanes), jnp.float32)
    sums = row_loop(rows, 4 * chunk, after, (zero_rows,) * tiles)
    for tile in range(tiles):
        bias_grad_ref[:, cut(tile)] += jnp.sum(sums[tile], axis=0, keepdims=True)
    step_w_grad_ref[...] += contract(
        projected_ref[:, :rank].astype(low_buf.dtype), low_buf[...], 0, 0
    )
    step_w = small_ref[pl.ds(plan["step"][0], rank), :]
    step_w = jnp.concatenate([step_w, jnp.zeros((lanes - rank, width), step_w.dtype)], axis=0)
    rank_buf[pl.ds(group * chunks, chunks)] += contract(low_buf[...], step_w, 1, 1).reshape(
        chunks, chunk, lanes
    )

    @pl.when(moment == moments - 1)
    def _():
        squares = jnp.zeros((8, lanes), jnp.float32)
        for which in range(count):
            squares = squares + reduce.finish(which)[0]
        square_ref[...] = squares
        some = 8
        entry = lax.rem(lax.broadcasted_iota(jnp.int32, (some * chunk * size, lanes), 0), size)
        target = lax.broadcasted_iota(jnp.int32, (some * chunk * size, lanes), 1)
        ones = jnp.ones((lanes, lanes), jnp.bfloat16)

        def lay(index, carry):
            lot = pl.ds(index * some * chunk, some * chunk)
            for number, buffer in enumerate((write_buf, read_buf)):
                high, low = high_low(buffer[lot].reshape(some * chunk * size, lanes))
                summed = jnp.dot(high.astype(jnp.bfloat16), ones, preferred_element_type=jnp.float32)
                summed += jnp.dot(low.astype(jnp.bfloat16), ones, preferred_element_type=jnp.float32)
                summed = jnp.where(target == entry + rank + number * size, summed, 0.0)
                summed = jnp.sum(summed.reshape(some * chunk, size, lanes), axis=1)
                rank_buf[pl.ds(index * some, some)] += summed.reshape(some, chunk, lanes)
            return carry

        lax.fori_loop(0, rank_buf.shape[0] // some, lay, 0)
        flat_ref[...] = rank_buf[...].reshape(flat_ref.shape).astype(flat_ref.dtype)
        for which in range(count):
            reduce.settle(which)
        for index in range(pieces):
            for target, result in ((out_sum_ref, out_result), (in_sum_ref, gate_result)):
                each = result.shape[2]
                target[:, index * each : (index + 1) * each] = result[index]


def back_kernel(
    plan,
    dims,
    lengths_ref,
    tokens_ref,
    low_ref,
    gain_ref,
    small_ref,
    flat_ref,
    branch_ref,
    signal_ref,
    slope_ref,
    signal_grad_ref,
    gate_grad_ref,
    flipped_ref,
    branch_w,
    gate_w,
    step_w_grad_ref,
    bias_grad_ref,
    decay_grad_ref,
    skip_grad_ref,
    plain_ref,
    earlier_ref,
    tokens_grad_ref,
    in_sum_ref,
    small_sum_ref,
    late_sum_ref,
    norm_ref,
    offset_buf,
    conv_buf,
    mixed_buf,
    total,
    in_stage,
    small_stage,
    late_stage,
    late_land,
    late_cores,
    norm_own,
    norm_land,
    norm_cores,
    in_result,
    small_result,
    direct_send,
    direct_recv,
    *parts,
):
    rows = tokens_ref.shape[0]
    width = branch_ref.shape[1]
    tiles = width // lanes
    block = pl.program_id(0)
    last = in_stage.shape[0]
    count = last + 1
    reduce = Reduce(
        dims,
        [small_stage] + [in_stage.at[index] for index in range(last)],
        parts[: 5 * count],
        parts[5 * count :],
        [small_result] + [in_result.at[index] for index in range(last)],
        True,
    )
    share = small_stage.shape[4]
    half_rows = small_stage.shape[3]
    planes = small_stage.shape[1]
    owners = small_stage.shape[0] * planes

    @pl.when(block == 0)
    def _():
        Place(dims).greet(everyone=True)
        select_grad = contract(flat_ref[...], signal_ref[...], 0, 0)
        step_first, step_tall = plan["step"]
        filler = jnp.zeros((2 * half_rows - step_first - step_tall, select_grad.shape[1]), jnp.float32)
        pieces = {
            "decay": decay_grad_ref[...],
            "bias": bias_grad_ref[...],
            "skip": skip_grad_ref[...],
            "step": step_w_grad_ref[...],
        }
        first = plan["select"][1]
        rows_now = [select_grad[:first]]
        for name in ("decay", "taps", "shift", "bias", "skip", "gain"):
            tall = plan[name][1]
            rows_now.append(
                pieces[name] if name in pieces else jnp.zeros((tall, select_grad.shape[1]), jnp.float32)
            )
            first += tall
        rows_now.append(jnp.zeros((step_first - first, select_grad.shape[1]), jnp.float32))
        rows_now.append(pieces["step"])
        if filler.shape[0]:
            rows_now.append(filler)
        everything = jnp.concatenate(rows_now, axis=0)
        for owner in range(owners):
            for side in range(2):
                small_stage[owner // planes, owner % planes, side] = everything[
                    side * half_rows : (side + 1) * half_rows, owner * share : (owner + 1) * share
                ].astype(small_stage.dtype)
        reduce.start(0)
        fill_offsets(lengths_ref, offset_buf, rows)

    def move_on(plan_of_moves):
        for moment, legs in plan_of_moves:

            @pl.when(block == moment)
            def _(legs=legs):
                for which, number in legs:
                    reduce.leg(which, number)

    taps = small_rows(small_ref, *plan["taps"])
    taps_count = taps.shape[0]
    zero_rows = jnp.zeros((8, lanes), jnp.float32)

    @pl.when(block < last)
    def _():
        conv_buf[pl.ds(0, rows), :] = signal_grad_ref[...] + jnp.dot(
            flat_ref[...], small_ref[:lanes, :], preferred_element_type=jnp.float32
        )
        conv_buf[pl.ds(rows, 8), :] = jnp.zeros((8, width), jnp.float32)

        def through_conv(index, at, carry):
            sums = []
            for tile in range(tiles):
                grad_conv = conv_buf[at, cut(tile)] * slope_ref[at, cut(tile)]
                conv_buf[at, cut(tile)] = grad_conv
                sums.append(carry[tile] + eight(grad_conv))
            return tuple(sums)

        shift_sums = row_loop(rows, 32, through_conv, (zero_rows,) * tiles)
        move_on(((0, ((0, 1),)), (1, ((1, 1), (0, 3))), (2, ((2, 1), (1, 3))), (3, ((3, 1), (2, 3)))))

        def to_branch(index, at, carry):
            longer = pl.ds(pl.multiple_of(index * 32, 32), 40)
            offsets = offset_buf[longer, :]
            result = []
            for tile in range(tiles):
                here = slice(tile * lanes, (tile + 1) * lanes)
                grads = conv_buf[longer, cut(tile)]
                branch = branch_ref[at, cut(tile)]
                summed = taps[taps_count - 1 : taps_count, here] * grads[:32]
                sums = [None] * taps_count
                sums[taps_count - 1] = carry[tile][taps_count - 1] + eight(branch * grads[:32])
                for tap in range(taps_count - 1):
                    lag = taps_count - 1 - tap
                    moved = pltpu.roll(jnp.where(offsets >= lag, grads, 0.0), 40 - lag, 0)[:32]
                    summed = summed + taps[tap : tap + 1, here] * moved
                    sums[tap] = carry[tile][tap] + eight(branch * moved)
                mixed_buf[block, at, cut(tile)] = summed.astype(mixed_buf.dtype)
                result.append(tuple(sums))
            return tuple(result)

        sums = row_loop(rows, 32, to_branch, ((zero_rows,) * taps_count,) * tiles)
        in_grad = jnp.dot(flipped_ref[...], mixed_buf[block], preferred_element_type=jnp.float32)
        in_stage[block] = in_grad.reshape(in_stage.shape[1:]).astype(in_stage.dtype)
        for index in range(last):

            @pl.when(block == index)
            def _(index=index):
                reduce.start(index + 1)

        late = [
            jnp.concatenate(
                [jnp.sum(sums[tile][tap], axis=0, keepdims=True) for tap in range(taps_count)]
                + [jnp.sum(shift_sums[tile], axis=0, keepdims=True)]
                + [jnp.zeros((8 - taps_count - 1, lanes), jnp.float32)],
                axis=0,
            )
            for tile in range(tiles)
        ]
        late = jnp.concatenate(late, axis=1)
        for piece in range(width // share):
            late_stage[block * (width // share) + piece] = late[:, piece * share : (piece + 1) * share]
        move_on(((0, ((0, 2),)), (1, ((1, 2),)), (2, ((2, 2),)), (3, ((3, 2),))))

    @pl.when(block >= last)
    def _():
        grad_normed_piece = contract(mixed_buf[block - last], rows_of(branch_w), 1, 1)
        grad_normed_piece += contract(gate_grad_ref[...], rows_of(gate_w), 1, 1)

        @pl.when(block == last)
        def _():
            total[...] = grad_normed_piece

        @pl.when(block > last)
        def _():
            total[...] += grad_normed_piece

        move_on(((4, ((4, 1), (3, 3))), (6, ((4, 2),))))

    @pl.when(block == pl.num_programs(0) - 1)
    def _():
        def finish(index, at, carry):
            residual = tokens_ref[at, :].astype(jnp.float32)
            scale = lax.rsqrt(jnp.mean(residual * residual, axis=1, keepdims=True) + epsilon)
            grad_normed = total[at, :]
            weighted = grad_normed * gain_ref[...]
            inner = jnp.mean(weighted * residual, axis=1, keepdims=True)
            grad_y = low_ref[at, :].astype(jnp.float32)
            result = grad_y + (scale * weighted - residual * (scale * scale * scale) * inner)
            tokens_grad_ref[at, :] = result.astype(tokens_grad_ref.dtype)
            return carry + eight(grad_normed * residual * scale)

        gains = row_loop(rows, 16, finish, jnp.zeros((8, total.shape[1]), jnp.float32))
        gains = jnp.sum(gains, axis=0, keepdims=True)
        place = Place(dims)
        each = gains.shape[1] // owners
        for owner in range(owners):
            late_stage[owner, taps_count + 1 : taps_count + 2, :each] = gains[
                :, owner * each : (owner + 1) * each
            ]
        late_sems = direct_send.at[0], direct_recv.at[0]
        norm_sems = direct_send.at[1], direct_recv.at[1]
        send_to_all(place, lambda target: late_stage.at[target], late_land, *late_sems)
        reduce.leg(4, 3)
        late_sum = sum_of_all(place, late_stage[place.me], late_land, *late_sems)
        late_sum = sum_of_cores(place, late_sum, late_cores, direct_send.at[0, 0], direct_recv.at[0, 0])
        late_sum_ref[...] = late_sum
        kept = earlier_ref[...] + folded_squares(late_sum * late_sum) * (1 - place.core).astype(jnp.float32)
        more, plain = reduce.finish(0, plain_ref)
        kept = kept + more
        for index in range(1, count):
            kept = kept + reduce.finish(index)[0]
        norm_own[...] = jnp.stack([kept, plain])
        send_to_all(place, lambda target: norm_own, norm_land, *norm_sems)
        norms = sum_of_all(place, norm_own[...], norm_land, *norm_sems)
        norm_ref[...] = sum_of_cores(place, norms, norm_cores, direct_send.at[1, 0], direct_recv.at[1, 0])
        for index in range(count):
            reduce.settle(index)
        for index in range(last):
            in_sum_ref[:, index * width : (index + 1) * width] = in_result[index]
        small_sum_ref[...] = small_result[...]


def finish_kernel(
    plan, names, late, tokens_ref, branch_ref, gate_ref, out_ref, small_ref, late_ref, norm_ref, *outs
):
    middle = branch_ref.shape[1]
    outs[0][:, :middle] = branch_ref[...]
    outs[0][:, middle:] = gate_ref[...]
    outs[1][...] = out_ref[...]
    outs[2][...] = tokens_ref[...]
    for name, target in zip(names, outs[3 : 3 + len(names)]):
        source, (first, count) = (late_ref, late[name]) if name in late else (small_ref, plan[name])
        if len(target.shape) == 1:
            target[...] = source[first, : target.shape[0]]
        else:
            target[...] = source[first : first + count, :]
    for index in range(2):
        outs[3 + len(names) + index][0, 0] = jnp.sum(norm_ref[index])


def shape(dims, kind=jnp.float32):
    return jax.ShapeDtypeStruct(dims, kind)


def compute_call(
    kernel, name, blocks, in_specs, out_specs, out_shape, scratch, flops, operands, collective_id=None
):
    return pl.pallas_call(
        kernel,
        grid=blocks if isinstance(blocks, tuple) else (blocks,),
        in_specs=in_specs,
        out_specs=out_specs,
        out_shape=out_shape,
        scratch_shapes=scratch,
        compiler_params=pltpu.CompilerParams(
            dimension_semantics=("arbitrary",) * (len(blocks) if isinstance(blocks, tuple) else 1),
            vmem_limit_bytes=62 * 1024 * 1024,
            collective_id=collective_id,
            has_side_effects=collective_id is not None,
        ),
        cost_estimate=pl.CostEstimate(flops=flops, bytes_accessed=40 << 20, transcendentals=0),
        name=name,
    )(*operands)


class Place:
    def __init__(self, dims, swapped=False):
        depth, tall, wide = dims
        self.dims = dims
        self.core = lax.axis_index("wide")
        self.me = lax.axis_index("narrow")
        self.across = lax.rem(self.me, wide)
        self.up = lax.rem(lax.div(self.me, wide), tall)
        self.deep = lax.div(self.me, wide * tall)
        side = 1 - self.core if swapped else self.core
        turn = side if tall == wide else 0
        self.second = (1 + turn * (wide - 1), self.across + turn * (self.up - self.across), wide)
        self.third = (wide - turn * (wide - 1), self.up + turn * (self.across - self.up), tall)
        self.spans = (depth, wide, tall)
        self.other = {"wide": 1 - self.core}

    def level(self, d):
        return lax.rem(self.deep + d, self.spans[0])

    def plane(self, e, f):
        return (
            lax.rem(self.second[1] + e, self.second[2]) * self.second[0]
            + lax.rem(self.third[1] + f, self.third[2]) * self.third[0]
        )

    def plane_behind(self, e, f):
        return self.plane((self.spans[1] - e) % self.spans[1], (self.spans[2] - f) % self.spans[2])

    def at(self, d, e, f):
        return {"narrow": self.level(d) * (self.dims[1] * self.dims[2]) + self.plane(e, f)}

    def greet(self, everyone=False):
        barrier = pltpu.get_barrier_semaphore()
        peers = [self.other]
        if everyone:
            number = self.spans[0] * self.spans[1] * self.spans[2]
            peers += [{"narrow": lax.rem(self.me + hop, number)} for hop in range(1, number)]
        else:
            for axis, size in enumerate(self.spans):
                for hop in range(1, size):
                    move = [0, 0, 0]
                    move[axis] = hop
                    peers.append(self.at(*move))
        for peer in peers:
            pl.semaphore_signal(barrier, inc=1, device_id=peer, device_id_type=pl.DeviceIdType.MESH)
        pl.semaphore_wait(barrier, len(peers))


def by_rows(block):
    return block[0] % 32 == 0


def half_shape(block):
    if len(block) == 3:
        return tuple(block[1:])
    return (block[0] // 2, block[1]) if by_rows(block) else (block[0], block[1] // 2)


def half(view, block, side, lead=0):
    ahead = (slice(None),) * lead
    if len(block) == 3:
        return view.at[ahead + (side,)]
    if by_rows(block):
        return view.at[ahead + (pl.ds(pl.multiple_of(side * (block[0] // 2), 16), block[0] // 2),)]
    columns = pl.ds(pl.multiple_of(side * (block[1] // 2), lanes), block[1] // 2)
    return view.at[ahead + (slice(None), columns)]


def remote(source, target, send_sem, recv_sem, device):
    return pltpu.make_async_remote_copy(
        src_ref=source,
        dst_ref=target,
        send_sem=send_sem,
        recv_sem=recv_sem,
        device_id=device,
        device_id_type=pl.DeviceIdType.MESH,
    )


class Gather:
    def __init__(self, dims, own, whole, sems):
        self.dims, self.own, self.whole = dims, own, whole
        self.local_sem, self.send_sem, self.recv_sem = sems

    @staticmethod
    def sems(count, dims):
        copies = dims[0] + 2 * dims[1] * dims[2]
        return [pltpu.SemaphoreType.DMA((count,))] + [pltpu.SemaphoreType.DMA((count, copies))] * 2

    def line(self, which, plane, side):
        return half(self.whole[which].at[:, plane], self.own[which].shape, side, 1)

    def local(self, place, which):
        block = self.own[which].shape
        return pltpu.make_async_copy(
            half(self.own[which], block, place.core),
            half(self.whole[which].at[place.deep, place.plane(0, 0)], block, place.core),
            self.local_sem.at[which],
        )

    def copy(self, which, source, target, index, device):
        return remote(
            source, target, self.send_sem.at[which, index], self.recv_sem.at[which, index], device
        )

    def rise(self, place, which, hop):
        block = self.own[which].shape
        return self.copy(
            which,
            half(self.own[which], block, place.core),
            half(self.whole[which].at[place.deep, place.plane(0, 0)], block, place.core),
            hop,
            place.at(hop, 0, 0),
        )

    def leg_index(self, e, f):
        return self.dims[0] + e * self.dims[1] + f

    def hand_index(self, e, f):
        return self.leg_index(e, f) + self.dims[1] * self.dims[2]

    def onward(self, place, which, e, f):
        line = self.line(which, place.plane_behind(e, f), place.core)
        if f == 0:
            for hop in range(1, place.spans[2]):
                self.copy(which, line, line, self.leg_index(e, hop), place.at(0, 0, hop)).start()
        if f == 0 and e == 0:
            for hop in range(1, place.spans[1]):
                self.copy(which, line, line, self.leg_index(hop, 0), place.at(0, hop, 0)).start()
        self.copy(which, line, line, self.hand_index(e, f), place.other).start()

    def start(self, which):
        place = Place(self.dims)
        for hop in range(1, place.spans[0]):
            self.rise(place, which, hop).start()
        self.local(place, which).start()

    def leg(self, which, number):
        place = Place(self.dims)
        if number == 1:
            self.local(place, which).wait()
            for hop in range(1, place.spans[0]):
                self.rise(place, which, hop).wait_recv()
            self.onward(place, which, 0, 0)
            return
        for e in range(place.spans[1]):
            for f in range(place.spans[2]):
                if (number == 2 and f == 0 and e > 0) or (number == 3 and f > 0):
                    line = self.line(which, place.plane_behind(e, f), place.core)
                    self.copy(which, line, line, self.leg_index(e, f), place.other).wait_recv()
                    self.onward(place, which, e, f)

    def arrive(self, which):
        place, mirror = Place(self.dims), Place(self.dims, swapped=True)
        for e in range(place.spans[1]):
            for f in range(place.spans[2]):
                line = self.line(which, mirror.plane_behind(e, f), 1 - place.core)
                self.copy(which, line, line, self.hand_index(e, f), place.other).wait_recv()

    def drain(self, which):
        place = Place(self.dims)
        for hop in range(1, place.spans[0]):
            self.rise(place, which, hop).wait_send()
        for e in range(place.spans[1]):
            for f in range(place.spans[2]):
                line = self.line(which, place.plane_behind(e, f), place.core)
                if e > 0 or f > 0:
                    self.copy(which, line, line, self.leg_index(e, f), place.other).wait_send()
                self.copy(which, line, line, self.hand_index(e, f), place.other).wait_send()


class Reduce:
    def __init__(self, dims, grads, rooms, sems, results, resident):
        self.dims, self.grads, self.resident = dims, grads, resident
        count = len(grads)
        self.mine, self.swapped, self.third, self.second, self.first = (
            rooms[index * count : (index + 1) * count] for index in range(5)
        )
        self.loaded = None if resident else rooms[5 * count :]
        self.load_sem, self.swap_send, self.swap_recv, self.send_sem, self.recv_sem = sems[:5]
        self.last_send, self.last_recv = sems[5:]
        self.results = results

    @staticmethod
    def rooms(dims, grads, resident):
        depth, tall, wide = dims
        leads = (
            (tall, wide, depth),
            (depth, tall * wide),
            (tall - 1, wide, depth),
            (wide - 1, depth),
            (depth - 1,),
        )
        if not resident:
            leads += ((depth, tall * wide),)
        return [
            pltpu.VMEM(lead + half_shape(grad.shape[2:]), grad.dtype) for lead in leads for grad in grads
        ]

    @staticmethod
    def sems(count, dims):
        return (
            [pltpu.SemaphoreType.DMA((count,))] * 3
            + [pltpu.SemaphoreType.DMA((count, dims[0] + dims[1] + dims[2]))] * 2
            + [pltpu.SemaphoreType.DMA((count,))] * 2
        )

    def block(self, which):
        return self.grads[which].shape[2:]

    def load(self, place, which):
        return pltpu.make_async_copy(
            half(self.grads[which], self.block(which), place.core, 2),
            self.loaded[which],
            self.load_sem.at[which],
        )

    def swap(self, place, which):
        return remote(
            half(self.grads[which], self.block(which), 1 - place.core, 2),
            self.swapped[which],
            self.swap_send.at[which],
            self.swap_recv.at[which],
            place.other,
        )

    def hop(self, which, source, target, index, device):
        return remote(
            source, target, self.send_sem.at[which, index], self.recv_sem.at[which, index], device
        )

    def third_hop(self, place, which, f):
        return self.hop(which, self.mine[which].at[f], self.third[which].at[f - 1], f, place.at(0, 0, f))

    def second_hop(self, place, which, e):
        return self.hop(
            which,
            self.mine[which].at[0, e],
            self.second[which].at[e - 1],
            self.dims[1] + e,
            place.at(0, e, 0),
        )

    def first_hop(self, place, which, d):
        return self.hop(
            which,
            self.mine[which].at[0, 0, place.level(d)],
            self.first[which].at[d - 1],
            self.dims[1] + self.dims[2] + d,
            place.at(d, 0, 0),
        )

    def start(self, which):
        place = Place(self.dims)
        self.swap(place, which).start()
        if not self.resident:
            self.load(place, which).start()

    def parts(self, place, which, e, f, z):
        plane = place.plane(e, f)
        if self.resident:
            found = [half(self.grads[which].at[z, plane], self.block(which), place.core)]
        else:
            found = [self.loaded[which].at[z, plane]]
        found.append(self.swapped[which].at[z, plane])
        if f == 0:
            found += [self.third[which].at[hop - 1, e, z] for hop in range(1, place.spans[2])]
        if f == 0 and e == 0:
            found += [self.second[which].at[hop - 1, z] for hop in range(1, place.spans[1])]
        return found

    def ready(self, place, which):
        if not self.resident:
            self.load(place, which).wait()
        self.swap(place, which).wait_recv()

    def added(self, parts, store, carry):
        rows = parts[0].shape[0]
        group = min(rows, 16)

        def some(index, carry):
            at_rows = pl.ds(pl.multiple_of(index * group, group), group)
            total = parts[0][at_rows, :].astype(jnp.float32)
            for part in parts[1:]:
                total = total + part[at_rows, :].astype(jnp.float32)
            return store(at_rows, total, carry)

        return lax.fori_loop(0, rows // group, some, carry)

    def sum_into(self, place, which, e, f, z):
        target = self.mine[which].at[f, e, z]

        def keep(at_rows, total, carry):
            target[at_rows, :] = total.astype(target.dtype)
            return carry

        self.added(self.parts(place, which, e, f, z), keep, 0)

    def leg(self, which, number):
        place = Place(self.dims)
        depth, span_e, span_f = place.spans
        if number == 1:
            self.ready(place, which)
            for f in range(span_f - 1, 0, -1):
                for e in range(span_e - 1, -1, -1):
                    for z in range(depth):
                        self.sum_into(place, which, e, f, z)
                self.third_hop(place, which, f).start()
        elif number == 2:
            for f in range(1, span_f):
                self.third_hop(place, which, f).wait_recv()
            for e in range(span_e - 1, 0, -1):
                for z in range(depth):
                    self.sum_into(place, which, e, 0, z)
                self.second_hop(place, which, e).start()
        else:
            if span_e == 1:
                for f in range(1, span_f):
                    self.third_hop(place, which, f).wait_recv()
            for e in range(1, span_e):
                self.second_hop(place, which, e).wait_recv()
            for d in range(1, depth):
                self.sum_into(place, which, 0, 0, place.level(d))
                self.first_hop(place, which, d).start()

    def result(self, which, side):
        return half(self.results[which], self.block(which), side)

    def last(self, place, which, side):
        share = self.result(which, side)
        return remote(share, share, self.last_send.at[which], self.last_recv.at[which], place.other)

    def finish(self, which, marks=None):
        place = Place(self.dims)
        parts = self.parts(place, which, 0, 0, place.deep)
        for d in range(1, place.spans[0]):
            self.first_hop(place, which, d).wait_recv()
            parts.append(self.first[which].at[d - 1])
        share = self.result(which, place.core)

        def store(at_rows, total, carry):
            share[at_rows, :] = total
            kept, plain = carry
            squared = total * total
            if marks is not None:
                marked = squared * marks[place.core, at_rows, :]
                plain = plain + folded_squares(marked)
                squared = squared - marked
            return (kept + folded_squares(squared), plain)

        squares = self.added(parts, store, (jnp.zeros((8, lanes), jnp.float32),) * 2)
        self.last(place, which, place.core).start()
        return squares

    def settle(self, which):
        place = Place(self.dims)
        last = self.last(place, which, 1 - place.core)
        last.wait_recv()
        last.wait_send()
        self.swap(place, which).wait_send()
        for f in range(1, place.spans[2]):
            self.third_hop(place, which, f).wait_send()
        for e in range(1, place.spans[1]):
            self.second_hop(place, which, e).wait_send()
        for d in range(1, place.spans[0]):
            self.first_hop(place, which, d).wait_send()


def folded_squares(values):
    total = None
    if values.shape[1] < lanes:
        first = lax.broadcasted_iota(jnp.int32, (values.shape[0], lanes), 1) == 0
        values = jnp.where(first, jnp.sum(values, axis=1, keepdims=True), 0.0)
    for row in range(0, values.shape[0], 8):
        for column in range(0, values.shape[1], lanes):
            piece = values[row : row + 8, column : column + lanes]
            total = piece if total is None else total + piece
    return total


def send_to_all(place, source, landing, send_sem, recv_sem):
    number = landing.shape[0]
    for hop in range(1, number):
        target = lax.rem(place.me + hop, number)
        remote(
            source(target), landing.at[place.me], send_sem.at[hop], recv_sem.at[hop], {"narrow": target}
        ).start()


def wait_for_all(place, own, landing, send_sem, recv_sem):
    number = landing.shape[0]
    landing[place.me] = own
    for hop in range(1, number):
        came = landing.at[lax.rem(place.me + number - hop, number)]
        copy = remote(came, came, send_sem.at[hop], recv_sem.at[hop], place.other)
        copy.wait_recv()
        copy.wait_send()


def sum_of_all(place, own, landing, send_sem, recv_sem):
    number = landing.shape[0]
    wait_for_all(place, own, landing, send_sem, recv_sem)
    total = landing[0]
    for spot in range(1, number):
        total = total + landing[spot]
    return total


def sum_of_cores(place, own, landing, send_sem, recv_sem):
    landing[place.core] = own
    copy = remote(landing.at[place.core], landing.at[place.core], send_sem, recv_sem, place.other)
    copy.start()
    copy.wait()
    return landing[0] + landing[1]


def grid_of(mesh):
    number = mesh.shape["narrow"]
    places = [getattr(device, "coords", None) for device in mesh.devices[0]]
    if all(place is not None for place in places):
        sizes = [len({place[axis] for place in places}) for axis in (2, 1, 0)]
        if sizes[0] * sizes[1] * sizes[2] == number:
            return tuple(sizes)
    side = round((number / 2) ** (1 / 3))
    return (2 * side, side, side) if 2 * side**3 == number else (number, 1, 1)


def plan_of(select_rows, state_size, tap_count, step_rows):
    plan, first = {}, 0
    for name, tall in (
        ("select", select_rows),
        ("decay", state_size),
        ("taps", tap_count),
        ("shift", 1),
        ("bias", 1),
        ("skip", 1),
        ("gain", 1),
    ):
        plan[name] = (first, tall)
        first += tall
    plan["step"] = (lanes, step_rows)
    plan["rows"] = -(-(lanes + step_rows) // 32) * 32
    return plan


def per_device(
    dims,
    tokens,
    cotangent,
    loss_mask,
    seq_lengths,
    norm_gain,
    in_proj,
    conv_weight,
    conv_bias,
    select_proj,
    step_proj,
    step_bias,
    decay_log,
    skip_scale,
    out_proj,
):
    half = jnp.bfloat16
    piece = skip_scale.shape[0]
    gain_piece = norm_gain.shape[0]
    rank, size = step_proj.shape[0], decay_log.shape[0]
    plan = plan_of(select_proj.shape[0], size, conv_weight.shape[0], rank)
    smalls = {
        "select": select_proj,
        "decay": decay_log,
        "taps": conv_weight,
        "shift": conv_bias[None],
        "bias": step_bias[None],
        "skip": skip_scale[None],
        "gain": norm_gain[None],
        "step": step_proj,
    }
    depth, planes = dims[0], dims[1] * dims[2]
    number = depth * planes
    in_rows = in_proj.shape[0]
    rows, model = tokens.shape
    inner = piece * number
    width = 4 * lanes
    blocks = inner // width
    chunks = rows // chunk
    mask_row = loss_mask[None]

    whole = pl.BlockSpec(memory_space=pltpu.VMEM)
    tall = pl.BlockSpec((rows, width), lambda b: (0, b))
    deep = pl.BlockSpec((chunks, chunk, width), lambda b: (0, 0, b))
    lead = pl.BlockSpec((rows, size, width), lambda b: (0, 0, b))
    first_w = pl.BlockSpec((model, width), lambda b: (0, b))
    second_w = pl.BlockSpec((model, width), lambda b: (0, b + blocks))
    out_w = pl.BlockSpec((width, model), lambda b: (b, 0))

    def thin(height):
        return pl.BlockSpec((height, width), lambda b: (0, b))

    def fixed(*dims_of):
        return pl.BlockSpec(dims_of, lambda b: (0,) * len(dims_of))

    scalars = pl.BlockSpec(memory_space=pltpu.SMEM)
    offset_buf = pltpu.VMEM((rows + 8, lanes), jnp.int32)
    packed = thin(plan["rows"])

    pair = (chunks, 2 * chunk, lanes)
    pair = (chunks, 2 * chunk, lanes)
    anywhere = pl.BlockSpec(memory_space=pl.ANY)
    small_half = (2, plan["rows"] // 2, piece)
    in_piece = (in_rows, width)
    shares = 2
    in_share = (in_rows, inner // shares)
    out_share = (out_proj.shape[0], model // shares)
    (
        branch,
        signal,
        slope,
        projected,
        flipped,
        normed,
        grad_low,
        write_pair,
        read_pair,
        small,
        gain_value,
        in_blocks,
        out_blocks,
    ) = compute_call(
        functools.partial(front_kernel, plan, dims, tuple(smalls)),
        "front",
        blocks,
        [scalars, whole, whole, whole] + [whole] * len(smalls) + [fixed(in_rows, inner), whole],
        [tall, tall, tall] + [whole] * 8 + [anywhere] * 2,
        [
            shape((rows, inner)),
            shape((rows, inner), half),
            shape((rows, inner)),
            shape((rows, lanes)),
            shape((model, rows), half),
            shape((rows, model), half),
            shape((rows, model), half),
            shape(pair, half),
            shape(pair, half),
            shape((plan["rows"], inner), half),
            shape((1, model)),
            shape((blocks, depth, planes) + in_piece, half),
            shape((shares, depth, planes) + out_share, half),
        ],
        [
            offset_buf,
            pltpu.VMEM((plan["rows"], piece), jnp.float32),
            pltpu.VMEM(small_half, half),
            pltpu.VMEM((blocks,) + in_piece, half),
            pltpu.VMEM((shares,) + out_share, half),
            pltpu.VMEM((depth, planes) + small_half, half),
            pltpu.VMEM((blocks, depth, planes) + in_piece, half),
            pltpu.SemaphoreType.DMA((blocks,)),
            pltpu.VMEM((8, piece), jnp.float32),
            pltpu.VMEM((number, 8, piece), jnp.float32),
            pltpu.SemaphoreType.DMA((number,)),
            pltpu.SemaphoreType.DMA((number,)),
        ]
        + Gather.sems(1 + blocks + shares, dims),
        4 * rows * model * inner,
        (seq_lengths, tokens, cotangent, mask_row, *smalls.values(), in_proj, out_proj),
        collective_id=0,
    )
    groups = 2
    part, pieces = rows // groups, chunks // groups
    row_block = pltpu.VMEM((pieces, chunk, width), jnp.float32)
    spread_block = pltpu.VMEM((rows, size, lanes), jnp.float32)
    fold_block = pltpu.VMEM((width // lanes, chunk * chunk, lanes), jnp.float32)

    def by_group(order, *dims_of):
        middle = (0,) * (len(dims_of) - 2)
        return pl.BlockSpec(dims_of, lambda b, g: (order(g),) + middle + (b,))

    def by_token(order, *dims_of):
        return pl.BlockSpec(dims_of, lambda b, g: (order(g),) + (0,) * (len(dims_of) - 1))

    def by_channel(height):
        return pl.BlockSpec((height, width), lambda b, g: (0, b))

    def onward(g):
        return g

    def backward(g):
        return groups - 1 - g

    states, step, core, begins, gate_blocks = compute_call(
        functools.partial(forward_kernel, plan, dims),
        "forward",
        (blocks, groups),
        [
            scalars,
            by_token(onward, part, lanes),
            by_channel(plan["rows"]),
            by_group(onward, part, width),
            whole,
            whole,
            pl.BlockSpec((in_rows, inner), lambda b, g: (0, 1)),
        ],
        [
            by_group(onward, part, size, width),
            by_group(onward, pieces, chunk, width),
            by_group(onward, pieces, chunk, width),
            by_group(onward, 1, size, width),
            anywhere,
        ],
        [
            shape((rows, size, inner)),
            shape((chunks, chunk, inner)),
            shape((chunks, chunk, inner)),
            shape((groups, size, inner)),
            shape((shares, depth, planes) + in_share, half),
        ],
        [
            offset_buf,
            pltpu.VMEM((part, width), jnp.float32),
            row_block,
            row_block,
            spread_block,
            spread_block,
            fold_block,
            pltpu.VMEM((size, width), jnp.float32),
            pltpu.VMEM((shares,) + in_share, half),
        ]
        + Gather.sems(shares, dims),
        15 * rows * inner * size,
        (seq_lengths, projected, small, signal, write_pair, read_pair, in_proj),
        collective_id=2,
    )
    split = in_share[1] // width
    weights = pl.BlockSpec((None, number, in_rows, width), lambda b: (b // split, 0, 0, b % split))
    per_block = width // out_share[0]
    out_pieces = pl.BlockSpec((shares, per_block) + out_share, lambda b: (0, b, 0, 0))
    branch_whole = in_blocks.reshape(blocks, number, *in_piece)
    gate_whole = gate_blocks.reshape(shares, number, *in_share)
    out_whole = out_blocks.reshape(shares, number, *out_share)
    core_grad, gate_grad, grad_skip, grad_outw, grad_in_gate, output = compute_call(
        functools.partial(middle_kernel, plan),
        "middle",
        blocks,
        [deep, packed, tall, weights, whole, out_pieces, whole, whole, whole],
        [
            deep,
            tall,
            thin(1),
            pl.BlockSpec((shares, width, out_share[1]), lambda b: (0, b, 0)),
            pl.BlockSpec((None, model, width), lambda b: (b // split, 0, b % split)),
            fixed(rows, model),
        ],
        [
            shape((chunks, chunk, inner)),
            shape((rows, inner), half),
            shape((1, inner)),
            shape((shares, inner, out_share[1]), half),
            shape((shares, model, in_share[1]), half),
            shape((rows, model), half),
        ],
        [
            pltpu.VMEM((rows, width), jnp.float32),
            pltpu.VMEM((rows, width), jnp.float32),
            pltpu.VMEM((rows, width), half),
            pltpu.VMEM((width, model), half),
            pltpu.VMEM((rows, model), jnp.float32),
        ],
        8 * rows * model * inner,
        (core, small, signal, gate_whole, grad_low, out_whole, flipped, normed, tokens),
    )
    early_grads = [
        grad_outw.reshape((shares, depth, planes) + out_share),
        grad_in_gate.reshape((shares, depth, planes) + in_share),
    ]
    early_sums = [shape(out_proj.shape), shape((in_rows, inner))]
    early_pieces = [shape((depth, planes) + block, half) for block in (in_share, out_share)] * shares
    (
        signal_grad,
        grad_stepw,
        grad_bias,
        grad_decaylog,
        flat,
        out_sum,
        in_gate_sum,
        early_squares,
    ) = compute_call(
        functools.partial(backward_kernel, plan, dims),
        "backward",
        (blocks, groups),
        [
            scalars,
            by_token(backward, part, lanes),
            by_channel(plan["rows"]),
            by_group(backward, part, width),
            whole,
            whole,
            by_group(backward, pieces, chunk, width),
            by_group(backward, pieces, chunk, width),
            by_group(backward, part, size, width),
            by_group(backward, 1, size, width),
            anywhere,
            anywhere,
        ],
        [
            by_group(backward, part, width),
            by_channel(rank),
            by_channel(1),
            by_channel(size),
            whole,
        ]
        + [whole] * 3,
        [
            shape((rows, inner)),
            shape((rank, inner)),
            shape((1, inner)),
            shape((size, inner)),
            shape((rows, lanes), half),
            *early_sums,
            shape((8, lanes)),
        ],
        [
            offset_buf,
            row_block,
            row_block,
            spread_block,
            spread_block,
            fold_block,
            fold_block,
            row_block,
            row_block,
            pltpu.VMEM((part, width), half),
            pltpu.VMEM((size, width), jnp.float32),
            pltpu.VMEM((chunks, chunk, lanes), jnp.float32),
            spread_block,
            spread_block,
        ]
        + [pltpu.VMEM((shares,) + block, jnp.float32) for block in (in_share, out_share)]
        + Reduce.rooms(dims, early_pieces, False)
        + Reduce.sems(2 * shares, dims),
        40 * rows * inner * size,
        (
            seq_lengths,
            projected,
            small,
            signal,
            write_pair,
            read_pair,
            step,
            core_grad,
            states,
            begins,
            *early_grads,
        ),
        collective_id=3,
    )

    plain_rows = np.zeros((plan["rows"], piece), np.float32)
    for name in ("bias", "decay", "skip"):
        first, count = plan[name]
        plain_rows[first : first + count] = 1.0
    late_grads = [shape((depth, planes) + small_half, half)]
    late_grads += [shape((depth, planes, in_rows, width), half)] * blocks
    taps_n = conv_weight.shape[0]
    late = {"taps": (0, taps_n), "shift": (taps_n, 1), "gain": (taps_n + 1, 1)}
    late_block = (8, piece)

    early_tall = pl.BlockSpec((rows, width), lambda b: (0, jnp.minimum(b, blocks - 1)))
    late_tall = pl.BlockSpec((rows, width), lambda b: (0, jnp.maximum(b - blocks, 0)))
    tokens_grad, in_branch_sum, small_sum, late_sum, norms = compute_call(
        functools.partial(back_kernel, plan, dims),
        "back",
        2 * blocks,
        [scalars, whole, whole, whole]
        + [pl.BlockSpec((plan["rows"], width), lambda b: (0, jnp.minimum(b, blocks - 1))), whole]
        + [early_tall, whole, early_tall, early_tall, late_tall, whole]
        + [
            pl.BlockSpec((None, number, in_rows, width), lambda b: (jnp.maximum(b - blocks, 0), 0, 0, 0)),
            pl.BlockSpec(
                (None, number, in_rows, width),
                lambda b: (jnp.maximum(b - blocks, 0) // split, 0, 0, jnp.maximum(b - blocks, 0) % split),
            ),
        ]
        + [whole] * 6,
        [whole] * 5,
        [
            shape((rows, model), half),
            shape((in_rows, inner)),
            shape(small_half),
            shape(late_block),
            shape((2, 8, lanes)),
        ],
        [
            offset_buf,
            pltpu.VMEM((rows + 8, width), jnp.float32),
            pltpu.VMEM((blocks, rows, width), half),
            pltpu.VMEM((rows, model), jnp.float32),
            pltpu.VMEM((blocks,) + late_grads[1].shape, half),
            pltpu.VMEM(late_grads[0].shape, late_grads[0].dtype),
            pltpu.VMEM((number,) + late_block, jnp.float32),
            pltpu.VMEM((number,) + late_block, jnp.float32),
            pltpu.VMEM((2,) + late_block, jnp.float32),
            pltpu.VMEM((2, 8, lanes), jnp.float32),
            pltpu.VMEM((number, 2, 8, lanes), jnp.float32),
            pltpu.VMEM((2, 2, 8, lanes), jnp.float32),
            pltpu.VMEM((blocks, in_rows, width), jnp.float32),
            pltpu.VMEM(small_half, jnp.float32),
            pltpu.SemaphoreType.DMA((2, number)),
            pltpu.SemaphoreType.DMA((2, number)),
        ]
        + Reduce.rooms(dims, late_grads, True)
        + Reduce.sems(blocks + 1, dims),
        8 * rows * model * inner,
        (
            seq_lengths,
            tokens,
            grad_low,
            gain_value,
            small,
            flat,
            branch,
            signal,
            slope,
            signal_grad,
            gate_grad,
            flipped,
            branch_whole,
            gate_whole,
            grad_stepw,
            grad_bias,
            grad_decaylog,
            grad_skip,
            jnp.asarray(plain_rows.reshape(small_half)),
            early_squares,
        ),
        collective_id=1,
    )

    names = ("gain", "taps", "shift", "select", "step", "bias", "decay", "skip")
    own = (norm_gain, conv_weight, conv_bias, select_proj, step_proj, step_bias, decay_log, skip_scale)
    in_grad, out_grad, grad_tokens, gain_grad, *small_grads, decay_sq, plain_sq = pl.pallas_call(
        functools.partial(finish_kernel, plan, names, late),
        in_specs=[whole] * 7,
        out_specs=[whole] * (3 + len(names)) + [scalars] * 2,
        out_shape=[shape(in_proj.shape), shape(out_proj.shape), shape(tokens.shape, half)]
        + [shape(array.shape) for array in own]
        + [shape((1, 1))] * 2,
        name="finish",
    )(
        tokens_grad,
        in_branch_sum,
        in_gate_sum,
        out_sum,
        small_sum.reshape(plan["rows"], piece),
        late_sum,
        norms,
    )
    return (
        output,
        grad_tokens,
        gain_grad,
        in_grad,
        *small_grads,
        out_grad,
        decay_sq[0, 0],
        plain_sq[0, 0],
    )


def solution(mesh):
    placed = (
        P(("wide", "narrow"), None),
        P(("wide", "narrow"), None),
        P(("wide", "narrow")),
        P(("wide", "narrow"), None),
        P("narrow"),
        P("narrow", None),
        P(None, "narrow"),
        P("narrow"),
        P(None, "narrow"),
        P(None, "narrow"),
        P("narrow"),
        P(None, "narrow"),
        P("narrow"),
        P("narrow", None),
    )
    return jax.shard_map(
        functools.partial(per_device, grid_of(mesh)),
        mesh=mesh,
        in_specs=placed,
        out_specs=(
            P(("wide", "narrow"), None),
            P(("wide", "narrow"), None),
            P("narrow"),
            P("narrow", None),
            P(None, "narrow"),
            P("narrow"),
            P(None, "narrow"),
            P(None, "narrow"),
            P("narrow"),
            P(None, "narrow"),
            P("narrow"),
            P("narrow", None),
            P(),
            P(),
        ),
        check_vma=False,
    )
```

```python
import functools
import math

import jax
import jax.numpy as jnp
import numpy as np
from jax import lax
from jax.experimental import pallas as pl
from jax.experimental.pallas import tpu as pltpu
from jax.sharding import PartitionSpec as P

epsilon = 1e-05
chunk = 8
lanes = 128
log2e = math.log2(math.e)
ln2 = math.log(2.0)
far = 1e30
tiny = 1e-30


def contract(left, right, left_dim, right_dim):
    return lax.dot_general(
        left, right, (((left_dim,), (right_dim,)), ((), ())), preferred_element_type=jnp.float32
    )


def row_loop(rows, group, body, initial):
    def some(index, carry):
        return body(index, pl.ds(pl.multiple_of(index * group, group), group), carry)

    return lax.fori_loop(0, rows // group, some, initial)


def cut(tile):
    return pl.ds(tile * lanes, lanes)


def sigmoid(values):
    return 0.5 * jnp.tanh(0.5 * values) + 0.5


def softplus(values):
    small = jnp.exp(-jnp.abs(values))
    series = small * (1.0 - small * (0.5 - small * (1.0 / 3.0 - 0.25 * small)))
    return jnp.maximum(values, 0.0) + jnp.where(small < 0.03, series, jnp.log(1.0 + small))


def slope_of(step):
    return 1.0 - jnp.exp(-step)


def fill_offsets(lengths_ref, offset_buf, rows):
    place = lax.broadcasted_iota(jnp.int32, offset_buf.shape, 0)
    start = jnp.zeros(offset_buf.shape, jnp.int32)
    ahead = jnp.int32(0)
    for index in range(lengths_ref.shape[1] - 1):
        ahead = ahead + lengths_ref[0, index]
        start = jnp.where(place >= ahead, ahead, start)
    offset_buf[...] = jnp.where(place < rows, place - start, 0)


def small_rows(small_ref, first, count):
    base = first // 16 * 16
    tall = -(-(first + count - base) // 16) * 16
    return small_ref[base : base + tall, :].astype(jnp.float32)[first - base : first - base + count]


def eight(values):
    total = values[:8]
    for row in range(8, values.shape[0], 8):
        total = total + values[row : row + 8]
    return total


def conv_rows(index, at, group, tile, branch_ref, offset_buf, taps, shift):
    count = taps.shape[0]
    here = slice(tile * lanes, (tile + 1) * lanes)
    current = branch_ref[at, cut(tile)]
    before = branch_ref[pl.ds(pl.multiple_of(jnp.maximum(index * group - 8, 0), 8), 8), cut(tile)]
    both = jnp.concatenate([before, current], axis=0)
    offsets = offset_buf[at, :]
    summed = shift[:, here] + taps[count - 1 : count, here] * current
    for tap in range(count - 1):
        lag = count - 1 - tap
        read = jnp.where(offsets >= lag, pltpu.roll(both, lag, 0)[8:], 0.0)
        summed = summed + taps[tap : tap + 1, here] * read
    return summed


def rows_of(blocks):
    return as_matrix(blocks[...][None])


def as_matrix(blocks):
    columns = blocks.shape[3]
    if blocks.shape[2] % 16:
        return blocks.astype(jnp.float32).reshape(-1, columns).astype(blocks.dtype)
    return blocks.reshape(-1, columns)


def front_kernel(
    plan,
    dims,
    names,
    lengths_ref,
    tokens_ref,
    cotangent_ref,
    mask_ref,
    *refs,
):
    smalls, in_ref, out_ref, refs = refs[: len(names)], refs[len(names)], refs[len(names) + 1], refs[len(names) + 2 :]
    branch_ref, signal_ref, slope_ref, projected_ref, flipped_ref, normed_ref, low_ref = refs[:7]
    write_pair, read_pair, small_out, gain_ref, whole_ref, gate_lines, out_lines = refs[7:14]
    offset_buf, pack_buf, own_small, own_in, own_gate, own_out, land_small, land_in, store_sem = refs[14:23]
    own_gain, land_gain, gain_send, gain_recv = refs[23:27]
    rows = tokens_ref.shape[0]
    width = branch_ref.shape[1]
    block = pl.program_id(0)
    last = whole_ref.shape[0]
    shares = own_out.shape[0]
    gather = Gather(
        dims,
        [own_small] + [own_in.at[index] for index in range(last)],
        [land_small] + [land_in.at[index] for index in range(last)],
        refs[27:30],
    )
    rise = Rise(
        dims,
        [own.at[index] for index in range(shares) for own in (own_gate, own_out)],
        [lines.at[index] for index in range(shares) for lines in (gate_lines, out_lines)],
        refs[30:],
    )
    tall = pack_buf.shape[0] // 2

    def stored(index):
        return pltpu.make_async_copy(land_in.at[index], whole_ref.at[index], store_sem.at[index])

    def move_on(plan_of_moves):
        for moment, legs in plan_of_moves:

            @pl.when(block == moment)
            def _(legs=legs):
                for which, number in legs:
                    gather.leg(which, number)

    @pl.when(block == 0)
    def _():
        pack_buf[...] = jnp.zeros_like(pack_buf)
        for name, ref in zip(names, smalls):
            first, height = plan[name]
            pack_buf[first : first + height, : ref.shape[1]] = ref[...]
        own_gain[...] = jnp.zeros_like(own_gain)
        own_gain[0:1, : gain_ref.shape[1] // land_gain.shape[0]] = smalls[names.index("gain")][...]
        for side in range(2):
            own_small[side] = pack_buf[side * tall : (side + 1) * tall, :].astype(own_small.dtype)
        for index in range(last):
            own_in[index] = in_ref[:, index * width : (index + 1) * width].astype(own_in.dtype)
        place = Place(dims)
        place.greet(everyone=True)
        send_to_all(place, lambda target: own_gain, land_gain, gain_send, gain_recv)
        for index in (1, 0) + tuple(range(2, last + 1)):
            gather.start(index)
        first = last * width
        for index in range(shares):
            each = own_gate.shape[2]
            own_gate[index] = in_ref[:, first + index * each : first + (index + 1) * each].astype(own_gate.dtype)
            each = own_out.shape[2]
            own_out[index] = out_ref[:, index * each : (index + 1) * each].astype(own_out.dtype)
        for index in range(2 * shares):
            rise.start(index)
        fill_offsets(lengths_ref, offset_buf, rows)
        gather.leg(1, 1)
        gather.leg(0, 1)
        wait_for_all(place, own_gain[...], land_gain, gain_send, gain_recv)
        each = gain_ref.shape[1] // land_gain.shape[0]
        for owner in range(land_gain.shape[0]):
            gain_ref[:, owner * each : (owner + 1) * each] = (
                land_gain[owner, 0:1, :each].astype(jnp.bfloat16).astype(jnp.float32)
            )

        def norm(index, at, carry):
            residual = tokens_ref[at, :].astype(jnp.float32)
            scale = lax.rsqrt(jnp.mean(residual * residual, axis=1, keepdims=True) + epsilon)
            normed_ref[at, :] = (residual * scale * gain_ref[...]).astype(normed_ref.dtype)
            return carry

        row_loop(rows, 16, norm, 0)
        gather.leg(1, 2)
        gather.leg(0, 2)
        gather.leg(2, 1)
        flipped_ref[...] = normed_ref[...].T
        gather.leg(1, 3)
        gather.leg(0, 3)
        gather.leg(2, 2)
        down = lax.broadcasted_iota(jnp.int32, (rows, rows), 0)
        along = lax.broadcasted_iota(jnp.int32, (rows, rows), 1)
        diagonal = jnp.where(down == along, mask_ref[...].astype(jnp.float32), 0.0).astype(low_ref.dtype)
        low_ref[...] = jnp.dot(
            diagonal, cotangent_ref[...], preferred_element_type=jnp.float32
        ).astype(low_ref.dtype)
        projected_ref[...] = jnp.zeros_like(projected_ref)

    for index in range(last):

        @pl.when(block == index)
        def _(index=index):
            gather.arrive(index + 1)
            stored(index).start()

    branch_w = as_matrix(land_in[block])
    branch_ref[...] = jnp.dot(normed_ref[...], branch_w, preferred_element_type=jnp.float32)
    move_on(((0, ((3, 1), (2, 3))), (1, ((4, 2), (3, 3))), (2, ((4, 3),))))

    @pl.when(block == 0)
    def _():
        gather.arrive(0)
        share = land_small.shape[4]
        for z in range(land_small.shape[0]):
            for plane in range(land_small.shape[1]):
                owner = z * land_small.shape[1] + plane
                for side in range(2):
                    small_out[side * tall : (side + 1) * tall, owner * share : (owner + 1) * share] = land_small[
                        z, plane, side
                    ]

    small_ref = small_out.at[:, pl.ds(pl.multiple_of(block * width, width), width)]
    taps = small_rows(small_ref, *plan["taps"])
    shift = small_rows(small_ref, *plan["shift"])

    def some(index, at, carry):
        for tile in range(width // lanes):
            summed = conv_rows(index, at, 32, tile, branch_ref, offset_buf, taps, shift)
            sigma = sigmoid(summed)
            active = summed * sigma
            signal_ref[at, cut(tile)] = active.astype(signal_ref.dtype)
            slope_ref[at, cut(tile)] = sigma + active * (1.0 - sigma)
        return carry

    row_loop(rows, 32, some, 0)
    move_on(((0, ((4, 1), (3, 2))),))
    projected_ref[...] += contract(signal_ref[...], small_ref[:lanes, :], 1, 1)

    @pl.when(block == pl.num_programs(0) - 1)
    def _():
        high, low = high_low(projected_ref[...])
        own = own_tokens(rows)
        rank = plan["step"][1]
        size = plan["decay"][1]
        entry = lax.broadcasted_iota(jnp.int32, (lanes, lanes), 0)
        lane = lax.rem(lax.broadcasted_iota(jnp.int32, (lanes, lanes), 1), size)
        for first, pair in ((rank, write_pair), (rank + size, read_pair)):
            spread = (entry == lane + first).astype(jnp.bfloat16)
            parts = [
                (jnp.dot(part.astype(jnp.bfloat16), spread, preferred_element_type=jnp.float32) * own).reshape(
                    rows // chunk, chunk, lanes
                )
                for part in (high, low)
            ]
            pair[...] = jnp.concatenate(parts, axis=1).astype(pair.dtype)
        for index in range(last + 1):
            gather.drain(index)
        for index in range(2 * shares):
            rise.finish(index)
        for index in range(last):
            stored(index).wait()


def high_low(values):
    high = values.astype(jnp.bfloat16).astype(jnp.float32)
    return high, values - high


def own_tokens(rows):
    token = lax.rem(lax.broadcasted_iota(jnp.int32, (rows, lanes), 0), chunk)
    return (token == lax.div(lax.broadcasted_iota(jnp.int32, (rows, lanes), 1), lanes // chunk)).astype(
        jnp.float32
    )


def spread_all(pairs, target):
    some = 8

    def spread(index, carry):
        rows = jnp.concatenate([pairs[index * some + number] for number in range(some)], axis=1)
        wide = contract(rows, jnp.ones((rows.shape[0], lanes), rows.dtype), 0, 0)
        target[pl.ds(index * some * chunk, some * chunk)] = wide.reshape(some * chunk, -1, lanes)
        return carry

    lax.fori_loop(0, pairs.shape[0] // some, spread, 0)


def folded(buffer, tile):
    total = buffer[tile, pl.ds(0, chunk, stride=chunk), :]
    for row in range(1, chunk):
        total = total + buffer[tile, pl.ds(row, chunk, stride=chunk), :]
    return total


def forward_kernel(
    plan,
    dims,
    lengths_ref,
    projected_ref,
    small_ref,
    signal_ref,
    write_pair,
    read_pair,
    gate_lines,
    out_lines,
    states_ref,
    step_ref,
    core_ref,
    begin_ref,
    gate_whole,
    out_whole,
    offset_buf,
    pre_buf,
    decay_step,
    flows,
    write_wide,
    read_wide,
    fold_buf,
    held_buf,
    *sems,
):
    rows, width = pre_buf.shape
    size = plan["decay"][1]
    half_size = size // 2
    tiles = width // lanes
    chunks = rows // chunk
    rank = plan["step"][1]
    group = pl.program_id(1)
    groups = pl.num_programs(1)
    moment = pl.program_id(0) * groups + group
    moments = pl.num_programs(0) * groups
    shares = gate_whole.shape[0]
    count = 2 * shares
    gather = Gather(
        dims,
        [lines.at[index] for index in range(shares) for lines in (gate_lines, out_lines)],
        [whole.at[index] for index in range(shares) for whole in (gate_whole, out_whole)],
        sems,
        [whole.shape[3:] for _ in range(shares) for whole in (gate_whole, out_whole)],
    )

    @pl.when(moment == 0)
    def _():
        Place(dims).greet()
        for which in range(count):
            gather.start(which)
        fill_offsets(lengths_ref, offset_buf, offset_buf.shape[0] - 8)
        spread_all(write_pair, write_wide)
        spread_all(read_pair, read_wide)

    @pl.when(group == 0)
    def _():
        held_buf[...] = jnp.zeros_like(held_buf)

    begin_ref[0] = held_buf[...]
    pre_buf[...] = jnp.dot(
        projected_ref[:, :rank].astype(small_ref.dtype),
        small_ref[pl.ds(plan["step"][0], rank), :],
        preferred_element_type=jnp.float32,
    )
    bias = small_rows(small_ref, *plan["bias"])

    def before(index, at, carry):
        spot = pl.ds(pl.multiple_of(index * 4, 4), 4)
        inside = offset_buf[pl.ds(pl.multiple_of(group * rows + index * 32, 32), 32), :] > 0
        for tile in range(tiles):
            step = softplus(pre_buf[at, cut(tile)] + bias[:, tile * lanes : (tile + 1) * lanes])
            step_ref[spot, :, cut(tile)] = step.reshape(4, chunk, lanes)
            decay_step[spot, :, cut(tile)] = jnp.where(inside, step, far).reshape(4, chunk, lanes)
            flow = step * signal_ref[at, cut(tile)].astype(jnp.float32)
            flows[spot, :, cut(tile)] = flow.reshape(4, chunk, lanes)
        return carry

    row_loop(rows, 4 * chunk, before, 0)
    rates = -jnp.exp(small_rows(small_ref, *plan["decay"])) * log2e
    rates = [rates[:, tile * lanes : (tile + 1) * lanes] for tile in range(tiles)]

    def forward(index, held):
        held = list(held)
        for place in range(chunk):
            now = index * chunk + place
            write_now = write_wide[group * rows + now]
            read_now = read_wide[group * rows + now]
            for tile in range(tiles):
                decay = jnp.exp2(rates[tile] * decay_step[index, pl.ds(place, 1), cut(tile)])
                fresh = decay * held[tile] + write_now * flows[index, pl.ds(place, 1), cut(tile)]
                held[tile] = fresh
                states_ref[now, :, cut(tile)] = fresh
                product = read_now * fresh
                fold_buf[tile, pl.ds(place * chunk, chunk), :] = product[:half_size] + product[half_size:]
        for tile in range(tiles):
            core_ref[index, :, cut(tile)] = folded(fold_buf, tile)
        return tuple(held)

    held = tuple(held_buf[:, cut(tile)] for tile in range(tiles))
    schedule = {}
    for which in range(count):
        for number in (2, 3):
            schedule.setdefault((3, 6, 9, 12)[which] + 3 * (number - 2), []).append((which, number))

    def move_on(legs):
        for which, number in legs:
            gather.leg(which, number)

    for half_loop in range(2):
        for point, legs in sorted(schedule.items()):
            if point < 16 and point % 2 == half_loop:
                pl.when(moment == point // 2)(functools.partial(move_on, legs))
        held = lax.fori_loop(half_loop * chunks // 2, (half_loop + 1) * chunks // 2, forward, held)
    for tile in range(tiles):
        held_buf[:, cut(tile)] = held[tile]

    @pl.when(moment == moments - 1)
    def _():
        for which in range(count):
            gather.arrive(which)
        for which in range(count):
            gather.drain(which)


def middle_kernel(
    plan,
    core_ref,
    small_ref,
    signal_ref,
    gate_w,
    low_ref,
    out_w,
    flipped_ref,
    normed_ref,
    tokens_ref,
    core_grad_ref,
    gate_grad_ref,
    skip_grad_ref,
    out_grad_ref,
    in_grad_ref,
    output_ref,
    pre_buf,
    gate_buf,
    gated_buf,
    out_buf,
    total,
):
    rows, width = pre_buf.shape
    tiles = width // lanes
    block = pl.program_id(0)
    each = out_w.shape[3]
    for index in range(out_w.shape[0]):
        out_buf[:, index * each : (index + 1) * each] = as_matrix(out_w[index][None])
    gate_buf[...] = jnp.dot(normed_ref[...], rows_of(gate_w), preferred_element_type=jnp.float32)
    pre_buf[...] = contract(low_ref[...], out_buf[...], 1, 1)
    skip = small_rows(small_ref, *plan["skip"])

    def after(index, at, carry):
        spot = pl.ds(pl.multiple_of(index * 4, 4), 4)
        sums = []
        for tile in range(tiles):
            signal = signal_ref[at, cut(tile)].astype(jnp.float32)
            core = core_ref[spot, :, cut(tile)].reshape(4 * chunk, lanes)
            core = core + skip[:, tile * lanes : (tile + 1) * lanes] * signal
            gate = gate_buf[at, cut(tile)]
            sigma = sigmoid(gate)
            active = gate * sigma
            gated_buf[at, cut(tile)] = (core * active).astype(gated_buf.dtype)
            grad_gated = pre_buf[at, cut(tile)]
            grad_core = grad_gated * active
            core_grad_ref[spot, :, cut(tile)] = grad_core.reshape(4, chunk, lanes)
            slope = sigma + active * (1.0 - sigma)
            gate_grad_ref[at, cut(tile)] = (grad_gated * core * slope).astype(gate_grad_ref.dtype)
            sums.append(carry[tile] + eight(grad_core * signal))
        return tuple(sums)

    zero_rows = jnp.zeros((8, lanes), jnp.float32)
    skips = row_loop(rows, 4 * chunk, after, (zero_rows,) * tiles)
    for tile in range(tiles):
        skip_grad_ref[:, cut(tile)] = jnp.sum(skips[tile], axis=0, keepdims=True)
    out_grad = contract(gated_buf[...], low_ref[...], 0, 0).astype(out_grad_ref.dtype)
    for index in range(out_w.shape[0]):
        out_grad_ref[index] = out_grad[:, index * each : (index + 1) * each]
    in_grad_ref[...] = jnp.dot(
        flipped_ref[...], gate_grad_ref[...], preferred_element_type=jnp.float32
    ).astype(in_grad_ref.dtype)
    piece = jnp.dot(gated_buf[...], out_buf[...], preferred_element_type=jnp.float32)

    @pl.when(block == 0)
    def _():
        total[...] = piece

    @pl.when(block > 0)
    def _():
        total[...] += piece

    @pl.when(block == pl.num_programs(0) - 1)
    def _():
        output_ref[...] = (tokens_ref[...].astype(jnp.float32) + total[...]).astype(output_ref.dtype)


def backward_kernel(
    plan,
    dims,
    lengths_ref,
    projected_ref,
    small_ref,
    signal_ref,
    write_pair,
    read_pair,
    step_ref,
    core_grad_ref,
    states_ref,
    begin_ref,
    out_grad_ref,
    in_grad_ref,
    signal_grad_ref,
    step_w_grad_ref,
    bias_grad_ref,
    decay_grad_ref,
    flat_ref,
    out_sum_ref,
    in_sum_ref,
    square_ref,
    offset_buf,
    decay_step,
    flows,
    write_wide,
    read_wide,
    first_buf,
    second_buf,
    through_buf,
    scaled_buf,
    low_buf,
    incoming_buf,
    rank_buf,
    write_buf,
    read_buf,
    *parts,
):
    rows, width = low_buf.shape
    rank = plan["step"][1]
    size = plan["decay"][1]
    half_size = size // 2
    tiles = width // lanes
    chunks = rows // chunk
    block = pl.program_id(0)
    turn = pl.program_id(1)
    groups = pl.num_programs(1)
    group = groups - 1 - turn
    moment = block * groups + turn
    moments = pl.num_programs(0) * groups
    gate_result, out_result, parts = parts[0], parts[1], parts[2:]
    pieces = gate_result.shape[0]
    count = 2 * pieces

    both = ((in_grad_ref, gate_result), (out_grad_ref, out_result))
    reduce = Reduce(
        dims,
        [ref.at[index] for index in range(pieces) for ref, _ in both],
        parts[: 6 * count],
        parts[6 * count :],
        [result.at[index] for index in range(pieces) for _, result in both],
        False,
    )

    @pl.when(moment == 0)
    def _():
        Place(dims).greet()
        for which in range(count):
            reduce.start(which)
        fill_offsets(lengths_ref, offset_buf, offset_buf.shape[0] - 8)
        spread_all(write_pair, write_wide)
        spread_all(read_pair, read_wide)
        write_buf[...] = jnp.zeros_like(write_buf)
        read_buf[...] = jnp.zeros_like(read_buf)
        rank_buf[...] = jnp.zeros_like(rank_buf)

    @pl.when(turn == 0)
    def _():
        incoming_buf[...] = jnp.zeros_like(incoming_buf)
        decay_grad_ref[...] = jnp.zeros_like(decay_grad_ref)
        bias_grad_ref[...] = jnp.zeros_like(bias_grad_ref)
        step_w_grad_ref[...] = jnp.zeros_like(step_w_grad_ref)

    def before(index, at, carry):
        spot = pl.ds(pl.multiple_of(index * 4, 4), 4)
        offsets = offset_buf[pl.ds(pl.multiple_of(group * rows + index * 32, 32), 32), :]
        inside = (offsets > 0).reshape(4, chunk, lanes)
        for tile in range(tiles):
            step = step_ref[spot, :, cut(tile)]
            decay_step[spot, :, cut(tile)] = jnp.where(inside, step, far)
            signal = signal_ref[at, cut(tile)].astype(jnp.float32).reshape(4, chunk, lanes)
            flows[spot, :, cut(tile)] = step * signal
        return carry

    row_loop(rows, 4 * chunk, before, 0)
    rates = -jnp.exp(small_rows(small_ref, *plan["decay"])) * log2e
    rates = [rates[:, tile * lanes : (tile + 1) * lanes] for tile in range(tiles)]

    def backward(position, carried):
        index = chunks - 1 - position
        incoming, decay_sums, current = (list(tiles_of) for tiles_of in carried)
        for place in range(chunk - 1, -1, -1):
            now = index * chunk + place
            token = group * rows + now
            write_now = write_wide[token]
            read_now = read_wide[token]
            read_sum = None
            write_sum = None
            for tile in range(tiles):
                grad_now = core_grad_ref[index, pl.ds(place, 1), cut(tile)]
                if place > 0:
                    earlier = states_ref[now - 1, :, cut(tile)]
                else:
                    earlier = jnp.where(
                        index > 0, states_ref[jnp.maximum(now - 1, 0), :, cut(tile)], begin_ref[0, :, cut(tile)]
                    )
                grad_state = incoming[tile] + read_now * grad_now
                through_read = current[tile] * grad_now
                current[tile] = earlier
                through_write = grad_state * flows[index, pl.ds(place, 1), cut(tile)]
                read_sum = through_read if read_sum is None else read_sum + through_read
                write_sum = through_write if write_sum is None else write_sum + through_write
                passed = grad_state * write_now
                first_buf[tile, pl.ds(place * chunk, chunk), :] = passed[:half_size] + passed[half_size:]
                exponent = rates[tile] * decay_step[index, pl.ds(place, 1), cut(tile)]
                leaving = jnp.exp2(exponent) * grad_state
                incoming[tile] = leaving
                weighted = (leaving * earlier) * exponent
                second_buf[tile, pl.ds(place * chunk, chunk), :] = weighted[:half_size] + weighted[half_size:]
                decay_sums[tile] = decay_sums[tile] + weighted
            read_buf[token] += read_sum
            write_buf[token] += write_sum
        for tile in range(tiles):
            through_buf[index, :, cut(tile)] = folded(first_buf, tile)
            scaled_buf[index, :, cut(tile)] = folded(second_buf, tile)
        return (tuple(incoming), tuple(decay_sums), tuple(current))

    incoming = tuple(incoming_buf[:, cut(tile)] for tile in range(tiles))
    nothing = (jnp.zeros((size, lanes), jnp.float32),) * tiles
    current = tuple(states_ref[rows - 1, :, cut(tile)] for tile in range(tiles))
    schedule = {}
    for which in range(count):
        for number in (1, 2, 3):
            schedule.setdefault((2, 4, 7, 9)[which] + (0, 3, 5)[number - 1], []).append((which, number))

    def move_on(legs):
        for which, number in legs:
            reduce.leg(which, number)

    carried = (incoming, nothing, current)
    for half_loop in range(2):
        for point, legs in sorted(schedule.items()):
            if point % 2 == half_loop:
                pl.when(moment == point // 2)(functools.partial(move_on, legs))
        carried = lax.fori_loop(half_loop * chunks // 2, (half_loop + 1) * chunks // 2, backward, carried)
    incoming, decay_sums, _ = carried
    for tile in range(tiles):
        incoming_buf[:, cut(tile)] = incoming[tile]
        decay_grad_ref[:, cut(tile)] += decay_sums[tile] * ln2
    skip = small_rows(small_ref, *plan["skip"])

    def after(index, at, carry):
        spot = pl.ds(pl.multiple_of(index * 4, 4), 4)
        sums = []
        for tile in range(tiles):
            signal = signal_ref[at, cut(tile)].astype(jnp.float32)
            step = step_ref[spot, :, cut(tile)].reshape(4 * chunk, lanes)
            through = through_buf[spot, :, cut(tile)].reshape(4 * chunk, lanes)
            scaled = scaled_buf[spot, :, cut(tile)].reshape(4 * chunk, lanes)
            core_grad = core_grad_ref[spot, :, cut(tile)].reshape(4 * chunk, lanes)
            grad_pre = (through * signal + ln2 * scaled / jnp.maximum(step, tiny)) * slope_of(step)
            low_buf[at, cut(tile)] = grad_pre.astype(low_buf.dtype)
            signal_grad_ref[at, cut(tile)] = (
                through * step + skip[:, tile * lanes : (tile + 1) * lanes] * core_grad
            )
            sums.append(carry[tile] + eight(grad_pre))
        return tuple(sums)

    zero_rows = jnp.zeros((8, lanes), jnp.float32)
    sums = row_loop(rows, 4 * chunk, after, (zero_rows,) * tiles)
    for tile in range(tiles):
        bias_grad_ref[:, cut(tile)] += jnp.sum(sums[tile], axis=0, keepdims=True)
    step_w_grad_ref[...] += contract(
        projected_ref[:, :rank].astype(low_buf.dtype), low_buf[...], 0, 0
    )
    step_w = small_ref[pl.ds(plan["step"][0], rank), :]
    step_w = jnp.concatenate([step_w, jnp.zeros((lanes - rank, width), step_w.dtype)], axis=0)
    rank_buf[pl.ds(group * chunks, chunks)] += contract(low_buf[...], step_w, 1, 1).reshape(
        chunks, chunk, lanes
    )

    @pl.when(moment == moments - 1)
    def _():
        squares = jnp.zeros((8, lanes), jnp.float32)
        for which in range(count):
            squares = squares + reduce.finish(which)[0]
        square_ref[...] = squares
        some = 8
        entry = lax.rem(lax.broadcasted_iota(jnp.int32, (some * chunk * size, lanes), 0), size)
        target = lax.broadcasted_iota(jnp.int32, (some * chunk * size, lanes), 1)
        ones = jnp.ones((lanes, lanes), jnp.bfloat16)

        def lay(index, carry):
            lot = pl.ds(index * some * chunk, some * chunk)
            for number, buffer in enumerate((write_buf, read_buf)):
                high, low = high_low(buffer[lot].reshape(some * chunk * size, lanes))
                summed = jnp.dot(high.astype(jnp.bfloat16), ones, preferred_element_type=jnp.float32)
                summed += jnp.dot(low.astype(jnp.bfloat16), ones, preferred_element_type=jnp.float32)
                summed = jnp.where(target == entry + rank + number * size, summed, 0.0)
                summed = jnp.sum(summed.reshape(some * chunk, size, lanes), axis=1)
                rank_buf[pl.ds(index * some, some)] += summed.reshape(some, chunk, lanes)
            return carry

        lax.fori_loop(0, rank_buf.shape[0] // some, lay, 0)
        flat_ref[...] = rank_buf[...].reshape(flat_ref.shape).astype(flat_ref.dtype)
        for which in range(count):
            reduce.settle(which)
        for index in range(pieces):
            for target, result in ((out_sum_ref, out_result), (in_sum_ref, gate_result)):
                each = result.shape[2]
                target[:, index * each : (index + 1) * each] = result[index]


def back_kernel(
    plan,
    dims,
    lengths_ref,
    tokens_ref,
    low_ref,
    gain_ref,
    small_ref,
    flat_ref,
    branch_ref,
    signal_ref,
    slope_ref,
    signal_grad_ref,
    gate_grad_ref,
    flipped_ref,
    branch_w,
    gate_w,
    step_w_grad_ref,
    bias_grad_ref,
    decay_grad_ref,
    skip_grad_ref,
    plain_ref,
    earlier_ref,
    tokens_grad_ref,
    in_sum_ref,
    small_sum_ref,
    late_sum_ref,
    norm_ref,
    offset_buf,
    conv_buf,
    mixed_buf,
    total,
    in_stage,
    small_stage,
    late_stage,
    late_land,
    late_cores,
    norm_own,
    norm_land,
    norm_cores,
    in_result,
    small_result,
    direct_send,
    direct_recv,
    *parts,
):
    rows = tokens_ref.shape[0]
    width = branch_ref.shape[1]
    tiles = width // lanes
    block = pl.program_id(0)
    last = in_stage.shape[0]
    count = last + 1
    reduce = Reduce(
        dims,
        [small_stage] + [in_stage.at[index] for index in range(last)],
        parts[: 5 * count],
        parts[5 * count :],
        [small_result] + [in_result.at[index] for index in range(last)],
        True,
    )
    share = small_stage.shape[4]
    half_rows = small_stage.shape[3]
    planes = small_stage.shape[1]
    owners = small_stage.shape[0] * planes

    @pl.when(block == 0)
    def _():
        Place(dims).greet(everyone=True)
        select_grad = contract(flat_ref[...], signal_ref[...], 0, 0)
        step_first, step_tall = plan["step"]
        filler = jnp.zeros((2 * half_rows - step_first - step_tall, select_grad.shape[1]), jnp.float32)
        pieces = {
            "decay": decay_grad_ref[...],
            "bias": bias_grad_ref[...],
            "skip": skip_grad_ref[...],
            "step": step_w_grad_ref[...],
        }
        first = plan["select"][1]
        rows_now = [select_grad[:first]]
        for name in ("decay", "taps", "shift", "bias", "skip", "gain"):
            tall = plan[name][1]
            rows_now.append(
                pieces[name] if name in pieces else jnp.zeros((tall, select_grad.shape[1]), jnp.float32)
            )
            first += tall
        rows_now.append(jnp.zeros((step_first - first, select_grad.shape[1]), jnp.float32))
        rows_now.append(pieces["step"])
        if filler.shape[0]:
            rows_now.append(filler)
        everything = jnp.concatenate(rows_now, axis=0)
        for owner in range(owners):
            for side in range(2):
                small_stage[owner // planes, owner % planes, side] = everything[
                    side * half_rows : (side + 1) * half_rows, owner * share : (owner + 1) * share
                ].astype(small_stage.dtype)
        reduce.start(0)
        fill_offsets(lengths_ref, offset_buf, rows)

    def move_on(plan_of_moves):
        for moment, legs in plan_of_moves:

            @pl.when(block == moment)
            def _(legs=legs):
                for which, number in legs:
                    reduce.leg(which, number)

    taps = small_rows(small_ref, *plan["taps"])
    taps_count = taps.shape[0]
    zero_rows = jnp.zeros((8, lanes), jnp.float32)

    @pl.when(block < last)
    def _():
        conv_buf[pl.ds(0, rows), :] = signal_grad_ref[...] + jnp.dot(
            flat_ref[...], small_ref[:lanes, :], preferred_element_type=jnp.float32
        )
        conv_buf[pl.ds(rows, 8), :] = jnp.zeros((8, width), jnp.float32)

        def through_conv(index, at, carry):
            sums = []
            for tile in range(tiles):
                grad_conv = conv_buf[at, cut(tile)] * slope_ref[at, cut(tile)]
                conv_buf[at, cut(tile)] = grad_conv
                sums.append(carry[tile] + eight(grad_conv))
            return tuple(sums)

        shift_sums = row_loop(rows, 32, through_conv, (zero_rows,) * tiles)
        move_on(((0, ((0, 1),)), (1, ((1, 1), (0, 3))), (2, ((2, 1), (1, 3))), (3, ((3, 1), (2, 3)))))

        def to_branch(index, at, carry):
            longer = pl.ds(pl.multiple_of(index * 32, 32), 40)
            offsets = offset_buf[longer, :]
            result = []
            for tile in range(tiles):
                here = slice(tile * lanes, (tile + 1) * lanes)
                grads = conv_buf[longer, cut(tile)]
                branch = branch_ref[at, cut(tile)]
                summed = taps[taps_count - 1 : taps_count, here] * grads[:32]
                sums = [None] * taps_count
                sums[taps_count - 1] = carry[tile][taps_count - 1] + eight(branch * grads[:32])
                for tap in range(taps_count - 1):
                    lag = taps_count - 1 - tap
                    moved = pltpu.roll(jnp.where(offsets >= lag, grads, 0.0), 40 - lag, 0)[:32]
                    summed = summed + taps[tap : tap + 1, here] * moved
                    sums[tap] = carry[tile][tap] + eight(branch * moved)
                mixed_buf[block, at, cut(tile)] = summed.astype(mixed_buf.dtype)
                result.append(tuple(sums))
            return tuple(result)

        sums = row_loop(rows, 32, to_branch, ((zero_rows,) * taps_count,) * tiles)
        in_grad = jnp.dot(flipped_ref[...], mixed_buf[block], preferred_element_type=jnp.float32)
        in_stage[block] = in_grad.reshape(in_stage.shape[1:]).astype(in_stage.dtype)
        for index in range(last):

            @pl.when(block == index)
            def _(index=index):
                reduce.start(index + 1)

        late = [
            jnp.concatenate(
                [jnp.sum(sums[tile][tap], axis=0, keepdims=True) for tap in range(taps_count)]
                + [jnp.sum(shift_sums[tile], axis=0, keepdims=True)]
                + [jnp.zeros((8 - taps_count - 1, lanes), jnp.float32)],
                axis=0,
            )
            for tile in range(tiles)
        ]
        late = jnp.concatenate(late, axis=1)
        for piece in range(width // share):
            late_stage[block * (width // share) + piece] = late[:, piece * share : (piece + 1) * share]
        move_on(((0, ((0, 2),)), (1, ((1, 2),)), (2, ((2, 2),)), (3, ((3, 2),))))

    @pl.when(block >= last)
    def _():
        grad_normed_piece = contract(mixed_buf[block - last], rows_of(branch_w), 1, 1)
        grad_normed_piece += contract(gate_grad_ref[...], rows_of(gate_w), 1, 1)

        @pl.when(block == last)
        def _():
            total[...] = grad_normed_piece

        @pl.when(block > last)
        def _():
            total[...] += grad_normed_piece

        move_on(((4, ((4, 1), (3, 3))), (6, ((4, 2),)), (7, ((4, 3),))))

    @pl.when(block == pl.num_programs(0) - 1)
    def _():
        def finish(index, at, carry):
            residual = tokens_ref[at, :].astype(jnp.float32)
            scale = lax.rsqrt(jnp.mean(residual * residual, axis=1, keepdims=True) + epsilon)
            grad_normed = total[at, :]
            weighted = grad_normed * gain_ref[...]
            inner = jnp.mean(weighted * residual, axis=1, keepdims=True)
            grad_y = low_ref[at, :].astype(jnp.float32)
            result = grad_y + (scale * weighted - residual * (scale * scale * scale) * inner)
            tokens_grad_ref[at, :] = result.astype(tokens_grad_ref.dtype)
            return carry + eight(grad_normed * residual * scale)

        gains = row_loop(rows, 16, finish, jnp.zeros((8, total.shape[1]), jnp.float32))
        gains = jnp.sum(gains, axis=0, keepdims=True)
        place = Place(dims)
        each = gains.shape[1] // owners
        for owner in range(owners):
            late_stage[owner, taps_count + 1 : taps_count + 2, :each] = gains[
                :, owner * each : (owner + 1) * each
            ]
        late_sems = direct_send.at[0], direct_recv.at[0]
        norm_sems = direct_send.at[1], direct_recv.at[1]
        send_to_all(place, lambda target: late_stage.at[target], late_land, *late_sems)
        late_sum = sum_of_all(place, late_stage[place.me], late_land, *late_sems)
        late_sum = sum_of_cores(place, late_sum, late_cores, direct_send.at[0, 0], direct_recv.at[0, 0])
        late_sum_ref[...] = late_sum
        kept = earlier_ref[...] + folded_squares(late_sum * late_sum) * (1 - place.core).astype(jnp.float32)
        more, plain = reduce.finish(0, plain_ref)
        kept = kept + more
        for index in range(1, count):
            kept = kept + reduce.finish(index)[0]
        norm_own[...] = jnp.stack([kept, plain])
        send_to_all(place, lambda target: norm_own, norm_land, *norm_sems)
        norms = sum_of_all(place, norm_own[...], norm_land, *norm_sems)
        norm_ref[...] = sum_of_cores(place, norms, norm_cores, direct_send.at[1, 0], direct_recv.at[1, 0])
        for index in range(count):
            reduce.settle(index)
        for index in range(last):
            in_sum_ref[:, index * width : (index + 1) * width] = in_result[index]
        small_sum_ref[...] = small_result[...]


def finish_kernel(
    plan, names, late, tokens_ref, branch_ref, gate_ref, out_ref, small_ref, late_ref, norm_ref, *outs
):
    middle = branch_ref.shape[1]
    outs[0][:, :middle] = branch_ref[...]
    outs[0][:, middle:] = gate_ref[...]
    outs[1][...] = out_ref[...]
    outs[2][...] = tokens_ref[...]
    for name, target in zip(names, outs[3 : 3 + len(names)]):
        source, (first, count) = (late_ref, late[name]) if name in late else (small_ref, plan[name])
        if len(target.shape) == 1:
            target[...] = source[first, : target.shape[0]]
        else:
            target[...] = source[first : first + count, :]
    for index in range(2):
        outs[3 + len(names) + index][0, 0] = jnp.sum(norm_ref[index])


def shape(dims, kind=jnp.float32):
    return jax.ShapeDtypeStruct(dims, kind)


def compute_call(
    kernel, name, blocks, in_specs, out_specs, out_shape, scratch, flops, operands, collective_id=None
):
    return pl.pallas_call(
        kernel,
        grid=blocks if isinstance(blocks, tuple) else (blocks,),
        in_specs=in_specs,
        out_specs=out_specs,
        out_shape=out_shape,
        scratch_shapes=scratch,
        compiler_params=pltpu.CompilerParams(
            dimension_semantics=("arbitrary",) * (len(blocks) if isinstance(blocks, tuple) else 1),
            vmem_limit_bytes=62 * 1024 * 1024,
            collective_id=collective_id,
            has_side_effects=collective_id is not None,
        ),
        cost_estimate=pl.CostEstimate(flops=flops, bytes_accessed=40 << 20, transcendentals=0),
        name=name,
    )(*operands)


class Place:
    def __init__(self, dims, swapped=False):
        depth, tall, wide = dims
        self.dims = dims
        self.core = lax.axis_index("wide")
        self.me = lax.axis_index("narrow")
        self.across = lax.rem(self.me, wide)
        self.up = lax.rem(lax.div(self.me, wide), tall)
        self.deep = lax.div(self.me, wide * tall)
        side = 1 - self.core if swapped else self.core
        turn = side if tall == wide else 0
        self.second = (1 + turn * (wide - 1), self.across + turn * (self.up - self.across), wide)
        self.third = (wide - turn * (wide - 1), self.up + turn * (self.across - self.up), tall)
        self.spans = (depth, wide, tall)
        self.other = {"wide": 1 - self.core}

    def level(self, d):
        return lax.rem(self.deep + d, self.spans[0])

    def plane(self, e, f):
        return (
            lax.rem(self.second[1] + e, self.second[2]) * self.second[0]
            + lax.rem(self.third[1] + f, self.third[2]) * self.third[0]
        )

    def plane_behind(self, e, f):
        return self.plane((self.spans[1] - e) % self.spans[1], (self.spans[2] - f) % self.spans[2])

    def at(self, d, e, f):
        return {"narrow": self.level(d) * (self.dims[1] * self.dims[2]) + self.plane(e, f)}

    def greet(self, everyone=False):
        barrier = pltpu.get_barrier_semaphore()
        peers = [self.other]
        if everyone:
            number = self.spans[0] * self.spans[1] * self.spans[2]
            peers += [{"narrow": lax.rem(self.me + hop, number)} for hop in range(1, number)]
        else:
            for axis, size in enumerate(self.spans):
                for hop in range(1, size):
                    move = [0, 0, 0]
                    move[axis] = hop
                    peers.append(self.at(*move))
        for peer in peers:
            pl.semaphore_signal(barrier, inc=1, device_id=peer, device_id_type=pl.DeviceIdType.MESH)
        pl.semaphore_wait(barrier, len(peers))


def by_rows(block):
    return block[0] % 32 == 0


def half_shape(block):
    if len(block) == 3:
        return tuple(block[1:])
    return (block[0] // 2, block[1]) if by_rows(block) else (block[0], block[1] // 2)


def half(view, block, side, lead=0):
    ahead = (slice(None),) * lead
    if len(block) == 3:
        return view.at[ahead + (side,)]
    if by_rows(block):
        return view.at[ahead + (pl.ds(pl.multiple_of(side * (block[0] // 2), 16), block[0] // 2),)]
    columns = pl.ds(pl.multiple_of(side * (block[1] // 2), lanes), block[1] // 2)
    return view.at[ahead + (slice(None), columns)]


def remote(source, target, send_sem, recv_sem, device):
    return pltpu.make_async_remote_copy(
        src_ref=source,
        dst_ref=target,
        send_sem=send_sem,
        recv_sem=recv_sem,
        device_id=device,
        device_id_type=pl.DeviceIdType.MESH,
    )


class Gather:
    def __init__(self, dims, own, whole, sems, blocks=None):
        self.dims, self.own, self.whole = dims, own, whole
        self.local_sem, self.send_sem, self.recv_sem = sems
        self.lined = blocks is not None
        self.blocks = blocks or [block.shape for block in own]

    @staticmethod
    def sems(count, dims):
        copies = dims[0] + 2 * dims[1] * dims[2]
        return [pltpu.SemaphoreType.DMA((count,))] + [pltpu.SemaphoreType.DMA((count, copies))] * 2

    def line(self, which, plane, side):
        return half(self.whole[which].at[:, plane], self.blocks[which], side, 1)

    def local(self, place, which):
        block = self.blocks[which]
        if self.lined:
            return pltpu.make_async_copy(
                self.own[which], self.line(which, place.plane(0, 0), place.core), self.local_sem.at[which]
            )
        return pltpu.make_async_copy(
            half(self.own[which], block, place.core),
            half(self.whole[which].at[place.deep, place.plane(0, 0)], block, place.core),
            self.local_sem.at[which],
        )

    def copy(self, which, source, target, index, device):
        return remote(
            source, target, self.send_sem.at[which, index], self.recv_sem.at[which, index], device
        )

    def rise(self, place, which, hop):
        block = self.blocks[which]
        return self.copy(
            which,
            half(self.own[which], block, place.core),
            half(self.whole[which].at[place.deep, place.plane(0, 0)], block, place.core),
            hop,
            place.at(hop, 0, 0),
        )

    def leg_index(self, e, f):
        return self.dims[0] + e * self.dims[1] + f

    def hand_index(self, e, f):
        return self.leg_index(e, f) + self.dims[1] * self.dims[2]

    def onward(self, place, which, e, f):
        line = self.line(which, place.plane_behind(e, f), place.core)
        source = self.own[which] if self.lined and e == 0 and f == 0 else line
        if f == 0:
            for hop in range(1, place.spans[2]):
                self.copy(which, source, line, self.leg_index(e, hop), place.at(0, 0, hop)).start()
        if f == 0 and e == 0:
            for hop in range(1, place.spans[1]):
                self.copy(which, source, line, self.leg_index(hop, 0), place.at(0, hop, 0)).start()
        self.copy(which, source, line, self.hand_index(e, f), place.other).start()

    def start(self, which):
        place = Place(self.dims)
        if self.lined:
            self.onward(place, which, 0, 0)
            self.local(place, which).start()
            return
        for hop in range(1, place.spans[0]):
            self.rise(place, which, hop).start()
        self.local(place, which).start()

    def leg(self, which, number):
        place = Place(self.dims)
        if number == 1:
            self.local(place, which).wait()
            for hop in range(1, place.spans[0]):
                self.rise(place, which, hop).wait_recv()
            self.onward(place, which, 0, 0)
            return
        for e in range(place.spans[1]):
            for f in range(place.spans[2]):
                if (number == 2 and f == 0 and e > 0) or (number == 3 and f > 0):
                    line = self.line(which, place.plane_behind(e, f), place.core)
                    self.copy(which, line, line, self.leg_index(e, f), place.other).wait_recv()
                    self.onward(place, which, e, f)

    def arrive(self, which):
        place, mirror = Place(self.dims), Place(self.dims, swapped=True)
        for e in range(place.spans[1]):
            for f in range(place.spans[2]):
                line = self.line(which, mirror.plane_behind(e, f), 1 - place.core)
                self.copy(which, line, line, self.hand_index(e, f), place.other).wait_recv()

    def drain(self, which):
        place = Place(self.dims)
        if self.lined:
            self.local(place, which).wait()
        else:
            for hop in range(1, place.spans[0]):
                self.rise(place, which, hop).wait_send()
        for e in range(place.spans[1]):
            for f in range(place.spans[2]):
                line = self.line(which, place.plane_behind(e, f), place.core)
                if e > 0 or f > 0:
                    self.copy(which, line, line, self.leg_index(e, f), place.other).wait_send()
                self.copy(which, line, line, self.hand_index(e, f), place.other).wait_send()


class Rise:
    def __init__(self, dims, own, lines, sems):
        self.dims, self.own, self.lines = dims, own, lines
        self.local_sem, self.send_sem, self.recv_sem = sems

    @staticmethod
    def sems(count, dims):
        return [pltpu.SemaphoreType.DMA((count,))] + [pltpu.SemaphoreType.DMA((count, dims[0]))] * 2

    def copies(self, place, which):
        source = half(self.own[which], self.own[which].shape, place.core)
        target = self.lines[which].at[place.deep]
        local = pltpu.make_async_copy(source, target, self.local_sem.at[which])
        return local, [
            remote(
                source, target, self.send_sem.at[which, hop], self.recv_sem.at[which, hop], place.at(hop, 0, 0)
            )
            for hop in range(1, place.spans[0])
        ]

    def start(self, which):
        local, sends = self.copies(Place(self.dims), which)
        for copy in [*sends, local]:
            copy.start()

    def finish(self, which):
        local, sends = self.copies(Place(self.dims), which)
        local.wait()
        for copy in sends:
            copy.wait_recv()
            copy.wait_send()


class Reduce:
    def __init__(self, dims, grads, rooms, sems, results, resident):
        self.dims, self.grads, self.resident = dims, grads, resident
        count = len(grads)
        self.mine, self.swapped, self.third, self.second, self.first = (
            rooms[index * count : (index + 1) * count] for index in range(5)
        )
        self.loaded = None if resident else rooms[5 * count :]
        self.load_sem, self.swap_send, self.swap_recv, self.send_sem, self.recv_sem = sems[:5]
        self.last_send, self.last_recv = sems[5:]
        self.results = results

    @staticmethod
    def rooms(dims, grads, resident):
        depth, tall, wide = dims
        leads = (
            (tall, wide, depth),
            (depth, tall * wide),
            (tall - 1, wide, depth),
            (wide - 1, depth),
            (depth - 1,),
        )
        if not resident:
            leads += ((depth, tall * wide),)
        return [
            pltpu.VMEM(lead + half_shape(grad.shape[2:]), grad.dtype) for lead in leads for grad in grads
        ]

    @staticmethod
    def sems(count, dims):
        return (
            [pltpu.SemaphoreType.DMA((count,))] * 3
            + [pltpu.SemaphoreType.DMA((count, dims[0] + dims[1] + dims[2]))] * 2
            + [pltpu.SemaphoreType.DMA((count,))] * 2
        )

    def block(self, which):
        return self.grads[which].shape[2:]

    def load(self, place, which):
        return pltpu.make_async_copy(
            half(self.grads[which], self.block(which), place.core, 2),
            self.loaded[which],
            self.load_sem.at[which],
        )

    def swap(self, place, which):
        return remote(
            half(self.grads[which], self.block(which), 1 - place.core, 2),
            self.swapped[which],
            self.swap_send.at[which],
            self.swap_recv.at[which],
            place.other,
        )

    def hop(self, which, source, target, index, device):
        return remote(
            source, target, self.send_sem.at[which, index], self.recv_sem.at[which, index], device
        )

    def third_hop(self, place, which, f):
        return self.hop(which, self.mine[which].at[f], self.third[which].at[f - 1], f, place.at(0, 0, f))

    def second_hop(self, place, which, e):
        return self.hop(
            which,
            self.mine[which].at[0, e],
            self.second[which].at[e - 1],
            self.dims[1] + e,
            place.at(0, e, 0),
        )

    def first_hop(self, place, which, d):
        return self.hop(
            which,
            self.mine[which].at[0, 0, place.level(d)],
            self.first[which].at[d - 1],
            self.dims[1] + self.dims[2] + d,
            place.at(d, 0, 0),
        )

    def start(self, which):
        place = Place(self.dims)
        self.swap(place, which).start()
        if not self.resident:
            self.load(place, which).start()

    def parts(self, place, which, e, f, z):
        plane = place.plane(e, f)
        if self.resident:
            found = [half(self.grads[which].at[z, plane], self.block(which), place.core)]
        else:
            found = [self.loaded[which].at[z, plane]]
        found.append(self.swapped[which].at[z, plane])
        if f == 0:
            found += [self.third[which].at[hop - 1, e, z] for hop in range(1, place.spans[2])]
        if f == 0 and e == 0:
            found += [self.second[which].at[hop - 1, z] for hop in range(1, place.spans[1])]
        return found

    def ready(self, place, which):
        if not self.resident:
            self.load(place, which).wait()
        self.swap(place, which).wait_recv()

    def added(self, parts, store, carry):
        rows = parts[0].shape[0]
        group = min(rows, 16)

        def some(index, carry):
            at_rows = pl.ds(pl.multiple_of(index * group, group), group)
            total = parts[0][at_rows, :].astype(jnp.float32)
            for part in parts[1:]:
                total = total + part[at_rows, :].astype(jnp.float32)
            return store(at_rows, total, carry)

        return lax.fori_loop(0, rows // group, some, carry)

    def sum_into(self, place, which, e, f, z):
        target = self.mine[which].at[f, e, z]

        def keep(at_rows, total, carry):
            target[at_rows, :] = total.astype(target.dtype)
            return carry

        self.added(self.parts(place, which, e, f, z), keep, 0)

    def leg(self, which, number):
        place = Place(self.dims)
        depth, span_e, span_f = place.spans
        if number == 1:
            self.ready(place, which)
            for f in range(span_f - 1, 0, -1):
                for e in range(span_e - 1, -1, -1):
                    for z in range(depth):
                        self.sum_into(place, which, e, f, z)
                self.third_hop(place, which, f).start()
        elif number == 2:
            for f in range(1, span_f):
                self.third_hop(place, which, f).wait_recv()
            for e in range(span_e - 1, 0, -1):
                for z in range(depth):
                    self.sum_into(place, which, e, 0, z)
                self.second_hop(place, which, e).start()
        else:
            if span_e == 1:
                for f in range(1, span_f):
                    self.third_hop(place, which, f).wait_recv()
            for e in range(1, span_e):
                self.second_hop(place, which, e).wait_recv()
            for d in range(1, depth):
                self.sum_into(place, which, 0, 0, place.level(d))
                self.first_hop(place, which, d).start()

    def result(self, which, side):
        return half(self.results[which], self.block(which), side)

    def last(self, place, which, side):
        share = self.result(which, side)
        return remote(share, share, self.last_send.at[which], self.last_recv.at[which], place.other)

    def finish(self, which, marks=None):
        place = Place(self.dims)
        parts = self.parts(place, which, 0, 0, place.deep)
        for d in range(1, place.spans[0]):
            self.first_hop(place, which, d).wait_recv()
            parts.append(self.first[which].at[d - 1])
        share = self.result(which, place.core)

        def store(at_rows, total, carry):
            share[at_rows, :] = total
            kept, plain = carry
            squared = total * total
            if marks is not None:
                marked = squared * marks[place.core, at_rows, :]
                plain = plain + folded_squares(marked)
                squared = squared - marked
            return (kept + folded_squares(squared), plain)

        squares = self.added(parts, store, (jnp.zeros((8, lanes), jnp.float32),) * 2)
        self.last(place, which, place.core).start()
        return squares

    def settle(self, which):
        place = Place(self.dims)
        last = self.last(place, which, 1 - place.core)
        last.wait_recv()
        last.wait_send()
        self.swap(place, which).wait_send()
        for f in range(1, place.spans[2]):
            self.third_hop(place, which, f).wait_send()
        for e in range(1, place.spans[1]):
            self.second_hop(place, which, e).wait_send()
        for d in range(1, place.spans[0]):
            self.first_hop(place, which, d).wait_send()


def folded_squares(values):
    total = None
    if values.shape[1] < lanes:
        first = lax.broadcasted_iota(jnp.int32, (values.shape[0], lanes), 1) == 0
        values = jnp.where(first, jnp.sum(values, axis=1, keepdims=True), 0.0)
    for row in range(0, values.shape[0], 8):
        for column in range(0, values.shape[1], lanes):
            piece = values[row : row + 8, column : column + lanes]
            total = piece if total is None else total + piece
    return total


def send_to_all(place, source, landing, send_sem, recv_sem):
    number = landing.shape[0]
    for hop in range(1, number):
        target = lax.rem(place.me + hop, number)
        remote(
            source(target), landing.at[place.me], send_sem.at[hop], recv_sem.at[hop], {"narrow": target}
        ).start()


def wait_for_all(place, own, landing, send_sem, recv_sem):
    number = landing.shape[0]
    landing[place.me] = own
    for hop in range(1, number):
        came = landing.at[lax.rem(place.me + number - hop, number)]
        copy = remote(came, came, send_sem.at[hop], recv_sem.at[hop], place.other)
        copy.wait_recv()
        copy.wait_send()


def sum_of_all(place, own, landing, send_sem, recv_sem):
    number = landing.shape[0]
    wait_for_all(place, own, landing, send_sem, recv_sem)
    total = landing[0]
    for spot in range(1, number):
        total = total + landing[spot]
    return total


def sum_of_cores(place, own, landing, send_sem, recv_sem):
    landing[place.core] = own
    copy = remote(landing.at[place.core], landing.at[place.core], send_sem, recv_sem, place.other)
    copy.start()
    copy.wait()
    return landing[0] + landing[1]


def grid_of(mesh):
    number = mesh.shape["narrow"]
    places = [getattr(device, "coords", None) for device in mesh.devices[0]]
    if all(place is not None for place in places):
        sizes = [len({place[axis] for place in places}) for axis in (2, 1, 0)]
        if sizes[0] * sizes[1] * sizes[2] == number:
            return tuple(sizes)
    side = round((number / 2) ** (1 / 3))
    return (2 * side, side, side) if 2 * side**3 == number else (number, 1, 1)


def plan_of(select_rows, state_size, tap_count, step_rows):
    plan, first = {}, 0
    for name, tall in (
        ("select", select_rows),
        ("decay", state_size),
        ("taps", tap_count),
        ("shift", 1),
        ("bias", 1),
        ("skip", 1),
        ("gain", 1),
    ):
        plan[name] = (first, tall)
        first += tall
    plan["step"] = (lanes, step_rows)
    plan["rows"] = -(-(lanes + step_rows) // 32) * 32
    return plan


def per_device(
    dims,
    tokens,
    cotangent,
    loss_mask,
    seq_lengths,
    norm_gain,
    in_proj,
    conv_weight,
    conv_bias,
    select_proj,
    step_proj,
    step_bias,
    decay_log,
    skip_scale,
    out_proj,
):
    half = jnp.bfloat16
    piece = skip_scale.shape[0]
    gain_piece = norm_gain.shape[0]
    rank, size = step_proj.shape[0], decay_log.shape[0]
    plan = plan_of(select_proj.shape[0], size, conv_weight.shape[0], rank)
    smalls = {
        "select": select_proj,
        "decay": decay_log,
        "taps": conv_weight,
        "shift": conv_bias[None],
        "bias": step_bias[None],
        "skip": skip_scale[None],
        "gain": norm_gain[None],
        "step": step_proj,
    }
    depth, planes = dims[0], dims[1] * dims[2]
    number = depth * planes
    in_rows = in_proj.shape[0]
    rows, model = tokens.shape
    inner = piece * number
    width = 4 * lanes
    blocks = inner // width
    chunks = rows // chunk
    mask_row = loss_mask[None]

    whole = pl.BlockSpec(memory_space=pltpu.VMEM)
    tall = pl.BlockSpec((rows, width), lambda b: (0, b))
    deep = pl.BlockSpec((chunks, chunk, width), lambda b: (0, 0, b))
    lead = pl.BlockSpec((rows, size, width), lambda b: (0, 0, b))
    first_w = pl.BlockSpec((model, width), lambda b: (0, b))
    second_w = pl.BlockSpec((model, width), lambda b: (0, b + blocks))
    out_w = pl.BlockSpec((width, model), lambda b: (b, 0))

    def thin(height):
        return pl.BlockSpec((height, width), lambda b: (0, b))

    def fixed(*dims_of):
        return pl.BlockSpec(dims_of, lambda b: (0,) * len(dims_of))

    scalars = pl.BlockSpec(memory_space=pltpu.SMEM)
    offset_buf = pltpu.VMEM((rows + 8, lanes), jnp.int32)
    packed = thin(plan["rows"])

    pair = (chunks, 2 * chunk, lanes)
    pair = (chunks, 2 * chunk, lanes)
    anywhere = pl.BlockSpec(memory_space=pl.ANY)
    small_half = (2, plan["rows"] // 2, piece)
    in_piece = (in_rows, width)
    shares = 2
    in_share = (in_rows, inner // shares)
    out_share = (out_proj.shape[0], model // shares)
    lines = [shape((shares, depth) + half_shape(block), half) for block in (in_share, out_share)]
    (
        branch,
        signal,
        slope,
        projected,
        flipped,
        normed,
        grad_low,
        write_pair,
        read_pair,
        small,
        gain_value,
        in_blocks,
        gate_lines,
        out_lines,
    ) = compute_call(
        functools.partial(front_kernel, plan, dims, tuple(smalls)),
        "front",
        blocks,
        [scalars, whole, whole, whole] + [whole] * len(smalls) + [whole] * 2,
        [tall, tall, tall] + [whole] * 8 + [anywhere] * 3,
        [
            shape((rows, inner)),
            shape((rows, inner), half),
            shape((rows, inner)),
            shape((rows, lanes)),
            shape((model, rows), half),
            shape((rows, model), half),
            shape((rows, model), half),
            shape(pair, half),
            shape(pair, half),
            shape((plan["rows"], inner), half),
            shape((1, model)),
            shape((blocks, depth, planes) + in_piece, half),
            *lines,
        ],
        [
            offset_buf,
            pltpu.VMEM((plan["rows"], piece), jnp.float32),
            pltpu.VMEM(small_half, half),
            pltpu.VMEM((blocks,) + in_piece, half),
            pltpu.VMEM((shares,) + in_share, half),
            pltpu.VMEM((shares,) + out_share, half),
            pltpu.VMEM((depth, planes) + small_half, half),
            pltpu.VMEM((blocks, depth, planes) + in_piece, half),
            pltpu.SemaphoreType.DMA((blocks,)),
            pltpu.VMEM((8, piece), jnp.float32),
            pltpu.VMEM((number, 8, piece), jnp.float32),
            pltpu.SemaphoreType.DMA((number,)),
            pltpu.SemaphoreType.DMA((number,)),
        ]
        + Gather.sems(1 + blocks, dims)
        + Rise.sems(2 * shares, dims),
        4 * rows * model * inner,
        (seq_lengths, tokens, cotangent, mask_row, *smalls.values(), in_proj, out_proj),
        collective_id=0,
    )
    groups = 2
    part, pieces = rows // groups, chunks // groups
    row_block = pltpu.VMEM((pieces, chunk, width), jnp.float32)
    spread_block = pltpu.VMEM((rows, size, lanes), jnp.float32)
    fold_block = pltpu.VMEM((width // lanes, chunk * chunk, lanes), jnp.float32)

    def by_group(order, *dims_of):
        middle = (0,) * (len(dims_of) - 2)
        return pl.BlockSpec(dims_of, lambda b, g: (order(g),) + middle + (b,))

    def by_token(order, *dims_of):
        return pl.BlockSpec(dims_of, lambda b, g: (order(g),) + (0,) * (len(dims_of) - 1))

    def by_channel(height):
        return pl.BlockSpec((height, width), lambda b, g: (0, b))

    def onward(g):
        return g

    def backward(g):
        return groups - 1 - g

    states, step, core, begins, gate_blocks, out_blocks = compute_call(
        functools.partial(forward_kernel, plan, dims),
        "forward",
        (blocks, groups),
        [
            scalars,
            by_token(onward, part, lanes),
            by_channel(plan["rows"]),
            by_group(onward, part, width),
            whole,
            whole,
            anywhere,
            anywhere,
        ],
        [
            by_group(onward, part, size, width),
            by_group(onward, pieces, chunk, width),
            by_group(onward, pieces, chunk, width),
            by_group(onward, 1, size, width),
            anywhere,
            anywhere,
        ],
        [
            shape((rows, size, inner)),
            shape((chunks, chunk, inner)),
            shape((chunks, chunk, inner)),
            shape((groups, size, inner)),
            shape((shares, depth, planes) + in_share, half),
            shape((shares, depth, planes) + out_share, half),
        ],
        [
            offset_buf,
            pltpu.VMEM((part, width), jnp.float32),
            row_block,
            row_block,
            spread_block,
            spread_block,
            fold_block,
            pltpu.VMEM((size, width), jnp.float32),
        ]
        + Gather.sems(2 * shares, dims),
        15 * rows * inner * size,
        (seq_lengths, projected, small, signal, write_pair, read_pair, gate_lines, out_lines),
        collective_id=2,
    )
    split = in_share[1] // width
    weights = pl.BlockSpec((None, number, in_rows, width), lambda b: (b // split, 0, 0, b % split))
    per_block = width // out_share[0]
    out_pieces = pl.BlockSpec((shares, per_block) + out_share, lambda b: (0, b, 0, 0))
    branch_whole = in_blocks.reshape(blocks, number, *in_piece)
    gate_whole = gate_blocks.reshape(shares, number, *in_share)
    out_whole = out_blocks.reshape(shares, number, *out_share)
    core_grad, gate_grad, grad_skip, grad_outw, grad_in_gate, output = compute_call(
        functools.partial(middle_kernel, plan),
        "middle",
        blocks,
        [deep, packed, tall, weights, whole, out_pieces, whole, whole, whole],
        [
            deep,
            tall,
            thin(1),
            pl.BlockSpec((shares, width, out_share[1]), lambda b: (0, b, 0)),
            pl.BlockSpec((None, model, width), lambda b: (b // split, 0, b % split)),
            fixed(rows, model),
        ],
        [
            shape((chunks, chunk, inner)),
            shape((rows, inner), half),
            shape((1, inner)),
            shape((shares, inner, out_share[1]), half),
            shape((shares, model, in_share[1]), half),
            shape((rows, model), half),
        ],
        [
            pltpu.VMEM((rows, width), jnp.float32),
            pltpu.VMEM((rows, width), jnp.float32),
            pltpu.VMEM((rows, width), half),
            pltpu.VMEM((width, model), half),
            pltpu.VMEM((rows, model), jnp.float32),
        ],
        8 * rows * model * inner,
        (core, small, signal, gate_whole, grad_low, out_whole, flipped, normed, tokens),
    )
    early_grads = [
        grad_outw.reshape((shares, depth, planes) + out_share),
        grad_in_gate.reshape((shares, depth, planes) + in_share),
    ]
    early_sums = [shape(out_proj.shape), shape((in_rows, inner))]
    early_pieces = [shape((depth, planes) + block, half) for block in (in_share, out_share)] * shares
    (
        signal_grad,
        grad_stepw,
        grad_bias,
        grad_decaylog,
        flat,
        out_sum,
        in_gate_sum,
        early_squares,
    ) = compute_call(
        functools.partial(backward_kernel, plan, dims),
        "backward",
        (blocks, groups),
        [
            scalars,
            by_token(backward, part, lanes),
            by_channel(plan["rows"]),
            by_group(backward, part, width),
            whole,
            whole,
            by_group(backward, pieces, chunk, width),
            by_group(backward, pieces, chunk, width),
            by_group(backward, part, size, width),
            by_group(backward, 1, size, width),
            anywhere,
            anywhere,
        ],
        [
            by_group(backward, part, width),
            by_channel(rank),
            by_channel(1),
            by_channel(size),
            whole,
        ]
        + [whole] * 3,
        [
            shape((rows, inner)),
            shape((rank, inner)),
            shape((1, inner)),
            shape((size, inner)),
            shape((rows, lanes), half),
            *early_sums,
            shape((8, lanes)),
        ],
        [
            offset_buf,
            row_block,
            row_block,
            spread_block,
            spread_block,
            fold_block,
            fold_block,
            row_block,
            row_block,
            pltpu.VMEM((part, width), half),
            pltpu.VMEM((size, width), jnp.float32),
            pltpu.VMEM((chunks, chunk, lanes), jnp.float32),
            spread_block,
            spread_block,
        ]
        + [pltpu.VMEM((shares,) + block, jnp.float32) for block in (in_share, out_share)]
        + Reduce.rooms(dims, early_pieces, False)
        + Reduce.sems(2 * shares, dims),
        40 * rows * inner * size,
        (
            seq_lengths,
            projected,
            small,
            signal,
            write_pair,
            read_pair,
            step,
            core_grad,
            states,
            begins,
            *early_grads,
        ),
        collective_id=3,
    )

    plain_rows = np.zeros((plan["rows"], piece), np.float32)
    for name in ("bias", "decay", "skip"):
        first, count = plan[name]
        plain_rows[first : first + count] = 1.0
    late_grads = [shape((depth, planes) + small_half, half)]
    late_grads += [shape((depth, planes, in_rows, width), half)] * blocks
    taps_n = conv_weight.shape[0]
    late = {"taps": (0, taps_n), "shift": (taps_n, 1), "gain": (taps_n + 1, 1)}
    late_block = (8, piece)

    early_tall = pl.BlockSpec((rows, width), lambda b: (0, jnp.minimum(b, blocks - 1)))
    late_tall = pl.BlockSpec((rows, width), lambda b: (0, jnp.maximum(b - blocks, 0)))
    tokens_grad, in_branch_sum, small_sum, late_sum, norms = compute_call(
        functools.partial(back_kernel, plan, dims),
        "back",
        2 * blocks,
        [scalars, whole, whole, whole]
        + [pl.BlockSpec((plan["rows"], width), lambda b: (0, jnp.minimum(b, blocks - 1))), whole]
        + [early_tall, whole, early_tall, early_tall, late_tall, whole]
        + [
            pl.BlockSpec((None, number, in_rows, width), lambda b: (jnp.maximum(b - blocks, 0), 0, 0, 0)),
            pl.BlockSpec(
                (None, number, in_rows, width),
                lambda b: (jnp.maximum(b - blocks, 0) // split, 0, 0, jnp.maximum(b - blocks, 0) % split),
            ),
        ]
        + [whole] * 6,
        [whole] * 5,
        [
            shape((rows, model), half),
            shape((in_rows, inner)),
            shape(small_half),
            shape(late_block),
            shape((2, 8, lanes)),
        ],
        [
            offset_buf,
            pltpu.VMEM((rows + 8, width), jnp.float32),
            pltpu.VMEM((blocks, rows, width), half),
            pltpu.VMEM((rows, model), jnp.float32),
            pltpu.VMEM((blocks,) + late_grads[1].shape, half),
            pltpu.VMEM(late_grads[0].shape, late_grads[0].dtype),
            pltpu.VMEM((number,) + late_block, jnp.float32),
            pltpu.VMEM((number,) + late_block, jnp.float32),
            pltpu.VMEM((2,) + late_block, jnp.float32),
            pltpu.VMEM((2, 8, lanes), jnp.float32),
            pltpu.VMEM((number, 2, 8, lanes), jnp.float32),
            pltpu.VMEM((2, 2, 8, lanes), jnp.float32),
            pltpu.VMEM((blocks, in_rows, width), jnp.float32),
            pltpu.VMEM(small_half, jnp.float32),
            pltpu.SemaphoreType.DMA((2, number)),
            pltpu.SemaphoreType.DMA((2, number)),
        ]
        + Reduce.rooms(dims, late_grads, True)
        + Reduce.sems(blocks + 1, dims),
        8 * rows * model * inner,
        (
            seq_lengths,
            tokens,
            grad_low,
            gain_value,
            small,
            flat,
            branch,
            signal,
            slope,
            signal_grad,
            gate_grad,
            flipped,
            branch_whole,
            gate_whole,
            grad_stepw,
            grad_bias,
            grad_decaylog,
            grad_skip,
            jnp.asarray(plain_rows.reshape(small_half)),
            early_squares,
        ),
        collective_id=1,
    )

    names = ("gain", "taps", "shift", "select", "step", "bias", "decay", "skip")
    own = (norm_gain, conv_weight, conv_bias, select_proj, step_proj, step_bias, decay_log, skip_scale)
    in_grad, out_grad, grad_tokens, gain_grad, *small_grads, decay_sq, plain_sq = pl.pallas_call(
        functools.partial(finish_kernel, plan, names, late),
        in_specs=[whole] * 7,
        out_specs=[whole] * (3 + len(names)) + [scalars] * 2,
        out_shape=[shape(in_proj.shape), shape(out_proj.shape), shape(tokens.shape, half)]
        + [shape(array.shape) for array in own]
        + [shape((1, 1))] * 2,
        name="finish",
    )(
        tokens_grad,
        in_branch_sum,
        in_gate_sum,
        out_sum,
        small_sum.reshape(plan["rows"], piece),
        late_sum,
        norms,
    )
    return (
        output,
        grad_tokens,
        gain_grad,
        in_grad,
        *small_grads,
        out_grad,
        decay_sq[0, 0],
        plain_sq[0, 0],
    )


def solution(mesh):
    placed = (
        P(("wide", "narrow"), None),
        P(("wide", "narrow"), None),
        P(("wide", "narrow")),
        P(("wide", "narrow"), None),
        P("narrow"),
        P("narrow", None),
        P(None, "narrow"),
        P("narrow"),
        P(None, "narrow"),
        P(None, "narrow"),
        P("narrow"),
        P(None, "narrow"),
        P("narrow"),
        P("narrow", None),
    )
    return jax.shard_map(
        functools.partial(per_device, grid_of(mesh)),
        mesh=mesh,
        in_specs=placed,
        out_specs=(
            P(("wide", "narrow"), None),
            P(("wide", "narrow"), None),
            P("narrow"),
            P("narrow", None),
            P(None, "narrow"),
            P("narrow"),
            P(None, "narrow"),
            P(None, "narrow"),
            P("narrow"),
            P(None, "narrow"),
            P("narrow"),
            P("narrow", None),
            P(),
            P(),
        ),
        check_vma=False,
    )
```

```python
import functools
import math

import jax
import jax.numpy as jnp
import numpy as np
from jax import lax
from jax.experimental import pallas as pl
from jax.experimental.pallas import tpu as pltpu
from jax.sharding import PartitionSpec as P

epsilon = 1e-05
chunk = 8
lanes = 128
log2e = math.log2(math.e)
ln2 = math.log(2.0)
far = 1e30
tiny = 1e-30


def contract(left, right, left_dim, right_dim):
    return lax.dot_general(
        left, right, (((left_dim,), (right_dim,)), ((), ())), preferred_element_type=jnp.float32
    )


def row_loop(rows, group, body, initial):
    def some(index, carry):
        return body(index, pl.ds(pl.multiple_of(index * group, group), group), carry)

    return lax.fori_loop(0, rows // group, some, initial)


def cut(tile):
    return pl.ds(tile * lanes, lanes)


def sigmoid(values):
    return 0.5 * jnp.tanh(0.5 * values) + 0.5


def softplus(values):
    small = jnp.exp(-jnp.abs(values))
    series = small * (1.0 - small * (0.5 - small * (1.0 / 3.0 - 0.25 * small)))
    return jnp.maximum(values, 0.0) + jnp.where(small < 0.03, series, jnp.log(1.0 + small))


def slope_of(step):
    return 1.0 - jnp.exp(-step)


def fill_offsets(lengths_ref, offset_buf, rows):
    place = lax.broadcasted_iota(jnp.int32, offset_buf.shape, 0)
    start = jnp.zeros(offset_buf.shape, jnp.int32)
    ahead = jnp.int32(0)
    for index in range(lengths_ref.shape[1] - 1):
        ahead = ahead + lengths_ref[0, index]
        start = jnp.where(place >= ahead, ahead, start)
    offset_buf[...] = jnp.where(place < rows, place - start, 0)


def small_rows(small_ref, first, count):
    base = first // 16 * 16
    tall = -(-(first + count - base) // 16) * 16
    return small_ref[base : base + tall, :].astype(jnp.float32)[first - base : first - base + count]


def eight(values):
    total = values[:8]
    for row in range(8, values.shape[0], 8):
        total = total + values[row : row + 8]
    return total


def conv_rows(index, at, group, tile, branch_ref, offset_buf, taps, shift):
    count = taps.shape[0]
    here = slice(tile * lanes, (tile + 1) * lanes)
    current = branch_ref[at, cut(tile)]
    before = branch_ref[pl.ds(pl.multiple_of(jnp.maximum(index * group - 8, 0), 8), 8), cut(tile)]
    both = jnp.concatenate([before, current], axis=0)
    offsets = offset_buf[at, :]
    summed = shift[:, here] + taps[count - 1 : count, here] * current
    for tap in range(count - 1):
        lag = count - 1 - tap
        read = jnp.where(offsets >= lag, pltpu.roll(both, lag, 0)[8:], 0.0)
        summed = summed + taps[tap : tap + 1, here] * read
    return summed


def rows_of(blocks):
    return as_matrix(blocks[...][None])


def as_matrix(blocks):
    columns = blocks.shape[3]
    if blocks.shape[2] % 16:
        return blocks.astype(jnp.float32).reshape(-1, columns).astype(blocks.dtype)
    return blocks.reshape(-1, columns)


def front_kernel(
    plan,
    dims,
    names,
    lengths_ref,
    tokens_ref,
    cotangent_ref,
    mask_ref,
    *refs,
):
    smalls, in_ref, out_ref, refs = refs[: len(names)], refs[len(names)], refs[len(names) + 1], refs[len(names) + 2 :]
    branch_ref, signal_ref, slope_ref, projected_ref, flipped_ref, normed_ref, low_ref = refs[:7]
    write_pair, read_pair, small_out, gain_ref, whole_ref, gate_lines, out_lines = refs[7:14]
    offset_buf, pack_buf, own_small, own_in, own_gate, own_out, land_small, land_in, store_sem = refs[14:23]
    own_gain, land_gain, gain_send, gain_recv = refs[23:27]
    rows = tokens_ref.shape[0]
    width = branch_ref.shape[1]
    block = pl.program_id(0)
    last = whole_ref.shape[0]
    shares = own_out.shape[0]
    gather = Gather(
        dims,
        [own_small] + [own_in.at[index] for index in range(last)],
        [land_small] + [land_in.at[index] for index in range(last)],
        refs[27:30],
    )
    rise = Rise(
        dims,
        [own.at[index] for index in range(shares) for own in (own_gate, own_out)],
        [lines.at[index] for index in range(shares) for lines in (gate_lines, out_lines)],
        refs[30:],
    )
    tall = pack_buf.shape[0] // 2

    def stored(index):
        return pltpu.make_async_copy(land_in.at[index], whole_ref.at[index], store_sem.at[index])

    def move_on(plan_of_moves):
        for moment, legs in plan_of_moves:

            @pl.when(block == moment)
            def _(legs=legs):
                for which, number in legs:
                    gather.leg(which, number)

    @pl.when(block == 0)
    def _():
        pack_buf[...] = jnp.zeros_like(pack_buf)
        for name, ref in zip(names, smalls):
            first, height = plan[name]
            pack_buf[first : first + height, : ref.shape[1]] = ref[...]
        own_gain[...] = jnp.zeros_like(own_gain)
        own_gain[0:1, : gain_ref.shape[1] // land_gain.shape[0]] = smalls[names.index("gain")][...]
        for side in range(2):
            own_small[side] = pack_buf[side * tall : (side + 1) * tall, :].astype(own_small.dtype)
        for index in range(last):
            own_in[index] = in_ref[:, index * width : (index + 1) * width].astype(own_in.dtype)
        place = Place(dims)
        place.greet(everyone=True)
        send_to_all(place, lambda target: own_gain, land_gain, gain_send, gain_recv)
        for index in (1, 0) + tuple(range(2, last + 1)):
            gather.start(index)
        first = last * width
        for index in range(shares):
            each = own_gate.shape[2]
            own_gate[index] = in_ref[:, first + index * each : first + (index + 1) * each].astype(own_gate.dtype)
            each = own_out.shape[2]
            own_out[index] = out_ref[:, index * each : (index + 1) * each].astype(own_out.dtype)
        for index in range(2 * shares):
            rise.start(index)
        fill_offsets(lengths_ref, offset_buf, rows)
        gather.leg(1, 1)
        gather.leg(0, 1)
        wait_for_all(place, own_gain[...], land_gain, gain_send, gain_recv)
        each = gain_ref.shape[1] // land_gain.shape[0]
        for owner in range(land_gain.shape[0]):
            gain_ref[:, owner * each : (owner + 1) * each] = (
                land_gain[owner, 0:1, :each].astype(jnp.bfloat16).astype(jnp.float32)
            )

        def norm(index, at, carry):
            residual = tokens_ref[at, :].astype(jnp.float32)
            scale = lax.rsqrt(jnp.mean(residual * residual, axis=1, keepdims=True) + epsilon)
            normed_ref[at, :] = (residual * scale * gain_ref[...]).astype(normed_ref.dtype)
            return carry

        row_loop(rows, 16, norm, 0)
        gather.leg(1, 2)
        gather.leg(0, 2)
        gather.leg(2, 1)
        flipped_ref[...] = normed_ref[...].T
        gather.leg(1, 3)
        gather.leg(0, 3)
        gather.leg(2, 2)
        down = lax.broadcasted_iota(jnp.int32, (rows, rows), 0)
        along = lax.broadcasted_iota(jnp.int32, (rows, rows), 1)
        diagonal = jnp.where(down == along, mask_ref[...].astype(jnp.float32), 0.0).astype(low_ref.dtype)
        low_ref[...] = jnp.dot(
            diagonal, cotangent_ref[...], preferred_element_type=jnp.float32
        ).astype(low_ref.dtype)
        projected_ref[...] = jnp.zeros_like(projected_ref)

    for index in range(last):

        @pl.when(block == index)
        def _(index=index):
            gather.arrive(index + 1)
            stored(index).start()

    branch_w = as_matrix(land_in[block])
    branch_ref[...] = jnp.dot(normed_ref[...], branch_w, preferred_element_type=jnp.float32)
    move_on(((0, ((3, 1), (2, 3))), (1, ((4, 2), (3, 3))), (2, ((4, 3),))))

    @pl.when(block == 0)
    def _():
        gather.arrive(0)
        share = land_small.shape[4]
        for z in range(land_small.shape[0]):
            for plane in range(land_small.shape[1]):
                owner = z * land_small.shape[1] + plane
                for side in range(2):
                    small_out[side * tall : (side + 1) * tall, owner * share : (owner + 1) * share] = land_small[
                        z, plane, side
                    ]

    small_ref = small_out.at[:, pl.ds(pl.multiple_of(block * width, width), width)]
    taps = small_rows(small_ref, *plan["taps"])
    shift = small_rows(small_ref, *plan["shift"])

    def some(index, at, carry):
        for tile in range(width // lanes):
            summed = conv_rows(index, at, 32, tile, branch_ref, offset_buf, taps, shift)
            sigma = sigmoid(summed)
            active = summed * sigma
            signal_ref[at, cut(tile)] = active.astype(signal_ref.dtype)
            slope_ref[at, cut(tile)] = sigma + active * (1.0 - sigma)
        return carry

    row_loop(rows, 32, some, 0)
    move_on(((0, ((4, 1), (3, 2))),))
    projected_ref[...] += contract(signal_ref[...], small_ref[:lanes, :], 1, 1)

    @pl.when(block == pl.num_programs(0) - 1)
    def _():
        high, low = high_low(projected_ref[...])
        own = own_tokens(rows)
        rank = plan["step"][1]
        size = plan["decay"][1]
        entry = lax.broadcasted_iota(jnp.int32, (lanes, lanes), 0)
        lane = lax.rem(lax.broadcasted_iota(jnp.int32, (lanes, lanes), 1), size)
        for first, pair in ((rank, write_pair), (rank + size, read_pair)):
            spread = (entry == lane + first).astype(jnp.bfloat16)
            parts = [
                (jnp.dot(part.astype(jnp.bfloat16), spread, preferred_element_type=jnp.float32) * own).reshape(
                    rows // chunk, chunk, lanes
                )
                for part in (high, low)
            ]
            pair[...] = jnp.concatenate(parts, axis=1).astype(pair.dtype)
        for index in range(last + 1):
            gather.drain(index)
        for index in range(2 * shares):
            rise.finish(index)
        for index in range(last):
            stored(index).wait()


def high_low(values):
    high = values.astype(jnp.bfloat16).astype(jnp.float32)
    return high, values - high


def own_tokens(rows):
    token = lax.rem(lax.broadcasted_iota(jnp.int32, (rows, lanes), 0), chunk)
    return (token == lax.div(lax.broadcasted_iota(jnp.int32, (rows, lanes), 1), lanes // chunk)).astype(
        jnp.float32
    )


def spread_all(pairs, target):
    some = 8

    def spread(index, carry):
        rows = jnp.concatenate([pairs[index * some + number] for number in range(some)], axis=1)
        wide = contract(rows, jnp.ones((rows.shape[0], lanes), rows.dtype), 0, 0)
        target[pl.ds(index * some * chunk, some * chunk)] = wide.reshape(some * chunk, -1, lanes)
        return carry

    lax.fori_loop(0, pairs.shape[0] // some, spread, 0)


def joined(first, second, hop):
    low = lax.bitwise_and(lax.broadcasted_iota(jnp.int32, first.shape, 0), hop) == 0
    return jnp.where(low, first, second) + pltpu.roll(jnp.where(low, second, first), hop, 0)


def folded(buffer, tile):
    parts = [buffer[tile, pl.ds(row * chunk, chunk), :] for row in range(chunk)]
    hop = 1
    while len(parts) > 1:
        parts = [joined(parts[index], parts[index + 1], hop) for index in range(0, len(parts), 2)]
        hop *= 2
    return parts[0]


def forward_kernel(
    plan,
    dims,
    lengths_ref,
    projected_ref,
    small_ref,
    signal_ref,
    write_pair,
    read_pair,
    gate_lines,
    out_lines,
    states_ref,
    step_ref,
    core_ref,
    begin_ref,
    gate_whole,
    out_whole,
    offset_buf,
    pre_buf,
    decay_step,
    flows,
    write_wide,
    read_wide,
    fold_buf,
    held_buf,
    *sems,
):
    rows, width = pre_buf.shape
    size = plan["decay"][1]
    half_size = size // 2
    tiles = width // lanes
    chunks = rows // chunk
    rank = plan["step"][1]
    group = pl.program_id(1)
    groups = pl.num_programs(1)
    moment = pl.program_id(0) * groups + group
    moments = pl.num_programs(0) * groups
    shares = gate_whole.shape[0]
    count = 2 * shares
    gather = Gather(
        dims,
        [lines.at[index] for index in range(shares) for lines in (gate_lines, out_lines)],
        [whole.at[index] for index in range(shares) for whole in (gate_whole, out_whole)],
        sems,
        [whole.shape[3:] for _ in range(shares) for whole in (gate_whole, out_whole)],
    )

    @pl.when(moment == 0)
    def _():
        Place(dims).greet()
        for which in range(count):
            gather.start(which)
        fill_offsets(lengths_ref, offset_buf, offset_buf.shape[0] - 8)
        spread_all(write_pair, write_wide)
        spread_all(read_pair, read_wide)

    @pl.when(group == 0)
    def _():
        held_buf[...] = jnp.zeros_like(held_buf)

    begin_ref[0] = held_buf[...]
    pre_buf[...] = jnp.dot(
        projected_ref[:, :rank].astype(small_ref.dtype),
        small_ref[pl.ds(plan["step"][0], rank), :],
        preferred_element_type=jnp.float32,
    )
    bias = small_rows(small_ref, *plan["bias"])

    def before(index, at, carry):
        spot = pl.ds(pl.multiple_of(index * 4, 4), 4)
        inside = offset_buf[pl.ds(pl.multiple_of(group * rows + index * 32, 32), 32), :] > 0
        for tile in range(tiles):
            step = softplus(pre_buf[at, cut(tile)] + bias[:, tile * lanes : (tile + 1) * lanes])
            step_ref[spot, :, cut(tile)] = step.reshape(4, chunk, lanes)
            decay_step[spot, :, cut(tile)] = jnp.where(inside, step, far).reshape(4, chunk, lanes)
            flow = step * signal_ref[at, cut(tile)].astype(jnp.float32)
            flows[spot, :, cut(tile)] = flow.reshape(4, chunk, lanes)
        return carry

    row_loop(rows, 4 * chunk, before, 0)
    rates = -jnp.exp(small_rows(small_ref, *plan["decay"])) * log2e
    rates = [rates[:, tile * lanes : (tile + 1) * lanes] for tile in range(tiles)]

    def forward(index, held):
        held = list(held)
        for place in range(chunk):
            now = index * chunk + place
            write_now = write_wide[group * rows + now]
            read_now = read_wide[group * rows + now]
            for tile in range(tiles):
                decay = jnp.exp2(rates[tile] * decay_step[index, pl.ds(place, 1), cut(tile)])
                fresh = decay * held[tile] + write_now * flows[index, pl.ds(place, 1), cut(tile)]
                held[tile] = fresh
                states_ref[now, :, cut(tile)] = fresh
                product = read_now * fresh
                fold_buf[tile, pl.ds(place * chunk, chunk), :] = product[:half_size] + product[half_size:]
        for tile in range(tiles):
            core_ref[index, :, cut(tile)] = folded(fold_buf, tile)
        return tuple(held)

    held = tuple(held_buf[:, cut(tile)] for tile in range(tiles))
    schedule = {}
    for which in range(count):
        for number in (2, 3):
            schedule.setdefault((3, 6, 9, 12)[which] + 3 * (number - 2), []).append((which, number))

    def move_on(legs):
        for which, number in legs:
            gather.leg(which, number)

    for half_loop in range(2):
        for point, legs in sorted(schedule.items()):
            if point < 16 and point % 2 == half_loop:
                pl.when(moment == point // 2)(functools.partial(move_on, legs))
        held = lax.fori_loop(half_loop * chunks // 2, (half_loop + 1) * chunks // 2, forward, held)
    for tile in range(tiles):
        held_buf[:, cut(tile)] = held[tile]

    @pl.when(moment == moments - 1)
    def _():
        for which in range(count):
            gather.arrive(which)
        for which in range(count):
            gather.drain(which)


def middle_kernel(
    plan,
    core_ref,
    small_ref,
    signal_ref,
    gate_w,
    low_ref,
    out_w,
    flipped_ref,
    normed_ref,
    tokens_ref,
    core_grad_ref,
    gate_grad_ref,
    skip_grad_ref,
    out_grad_ref,
    in_grad_ref,
    output_ref,
    pre_buf,
    gate_buf,
    gated_buf,
    out_buf,
    total,
):
    rows, width = pre_buf.shape
    tiles = width // lanes
    block = pl.program_id(0)
    each = out_w.shape[3]
    for index in range(out_w.shape[0]):
        out_buf[:, index * each : (index + 1) * each] = as_matrix(out_w[index][None])
    gate_buf[...] = jnp.dot(normed_ref[...], rows_of(gate_w), preferred_element_type=jnp.float32)
    pre_buf[...] = contract(low_ref[...], out_buf[...], 1, 1)
    skip = small_rows(small_ref, *plan["skip"])

    def after(index, at, carry):
        spot = pl.ds(pl.multiple_of(index * 4, 4), 4)
        sums = []
        for tile in range(tiles):
            signal = signal_ref[at, cut(tile)].astype(jnp.float32)
            core = core_ref[spot, :, cut(tile)].reshape(4 * chunk, lanes)
            core = core + skip[:, tile * lanes : (tile + 1) * lanes] * signal
            gate = gate_buf[at, cut(tile)]
            sigma = sigmoid(gate)
            active = gate * sigma
            gated_buf[at, cut(tile)] = (core * active).astype(gated_buf.dtype)
            grad_gated = pre_buf[at, cut(tile)]
            grad_core = grad_gated * active
            core_grad_ref[spot, :, cut(tile)] = grad_core.reshape(4, chunk, lanes)
            slope = sigma + active * (1.0 - sigma)
            gate_grad_ref[at, cut(tile)] = (grad_gated * core * slope).astype(gate_grad_ref.dtype)
            sums.append(carry[tile] + eight(grad_core * signal))
        return tuple(sums)

    zero_rows = jnp.zeros((8, lanes), jnp.float32)
    skips = row_loop(rows, 4 * chunk, after, (zero_rows,) * tiles)
    for tile in range(tiles):
        skip_grad_ref[:, cut(tile)] = jnp.sum(skips[tile], axis=0, keepdims=True)
    out_grad = contract(gated_buf[...], low_ref[...], 0, 0).astype(out_grad_ref.dtype)
    for index in range(out_w.shape[0]):
        out_grad_ref[index] = out_grad[:, index * each : (index + 1) * each]
    in_grad_ref[...] = jnp.dot(
        flipped_ref[...], gate_grad_ref[...], preferred_element_type=jnp.float32
    ).astype(in_grad_ref.dtype)
    piece = jnp.dot(gated_buf[...], out_buf[...], preferred_element_type=jnp.float32)

    @pl.when(block == 0)
    def _():
        total[...] = piece

    @pl.when(block > 0)
    def _():
        total[...] += piece

    @pl.when(block == pl.num_programs(0) - 1)
    def _():
        output_ref[...] = (tokens_ref[...].astype(jnp.float32) + total[...]).astype(output_ref.dtype)


def backward_kernel(
    plan,
    dims,
    lengths_ref,
    projected_ref,
    small_ref,
    signal_ref,
    write_pair,
    read_pair,
    step_ref,
    core_grad_ref,
    states_ref,
    begin_ref,
    out_grad_ref,
    in_grad_ref,
    signal_grad_ref,
    step_w_grad_ref,
    bias_grad_ref,
    decay_grad_ref,
    flat_ref,
    out_sum_ref,
    in_sum_ref,
    square_ref,
    offset_buf,
    decay_step,
    flows,
    write_wide,
    read_wide,
    first_buf,
    second_buf,
    through_buf,
    scaled_buf,
    low_buf,
    incoming_buf,
    rank_buf,
    write_buf,
    read_buf,
    *parts,
):
    rows, width = low_buf.shape
    rank = plan["step"][1]
    size = plan["decay"][1]
    half_size = size // 2
    tiles = width // lanes
    chunks = rows // chunk
    block = pl.program_id(0)
    turn = pl.program_id(1)
    groups = pl.num_programs(1)
    group = groups - 1 - turn
    moment = block * groups + turn
    moments = pl.num_programs(0) * groups
    gate_result, out_result, parts = parts[0], parts[1], parts[2:]
    pieces = gate_result.shape[0]
    count = 2 * pieces

    both = ((in_grad_ref, gate_result), (out_grad_ref, out_result))
    reduce = Reduce(
        dims,
        [ref.at[index] for index in range(pieces) for ref, _ in both],
        parts[: 6 * count],
        parts[6 * count :],
        [result.at[index] for index in range(pieces) for _, result in both],
        False,
    )

    @pl.when(moment == 0)
    def _():
        Place(dims).greet()
        for which in range(count):
            reduce.start(which)
        fill_offsets(lengths_ref, offset_buf, offset_buf.shape[0] - 8)
        spread_all(write_pair, write_wide)
        spread_all(read_pair, read_wide)
        write_buf[...] = jnp.zeros_like(write_buf)
        read_buf[...] = jnp.zeros_like(read_buf)
        rank_buf[...] = jnp.zeros_like(rank_buf)

    @pl.when(turn == 0)
    def _():
        incoming_buf[...] = jnp.zeros_like(incoming_buf)
        decay_grad_ref[...] = jnp.zeros_like(decay_grad_ref)
        bias_grad_ref[...] = jnp.zeros_like(bias_grad_ref)
        step_w_grad_ref[...] = jnp.zeros_like(step_w_grad_ref)

    def before(index, at, carry):
        spot = pl.ds(pl.multiple_of(index * 4, 4), 4)
        offsets = offset_buf[pl.ds(pl.multiple_of(group * rows + index * 32, 32), 32), :]
        inside = (offsets > 0).reshape(4, chunk, lanes)
        for tile in range(tiles):
            step = step_ref[spot, :, cut(tile)]
            decay_step[spot, :, cut(tile)] = jnp.where(inside, step, far)
            signal = signal_ref[at, cut(tile)].astype(jnp.float32).reshape(4, chunk, lanes)
            flows[spot, :, cut(tile)] = step * signal
        return carry

    row_loop(rows, 4 * chunk, before, 0)
    rates = -jnp.exp(small_rows(small_ref, *plan["decay"])) * log2e
    rates = [rates[:, tile * lanes : (tile + 1) * lanes] for tile in range(tiles)]

    def backward(position, carried):
        index = chunks - 1 - position
        incoming, decay_sums, current = (list(tiles_of) for tiles_of in carried)
        for place in range(chunk - 1, -1, -1):
            now = index * chunk + place
            token = group * rows + now
            write_now = write_wide[token]
            read_now = read_wide[token]
            read_sum = None
            write_sum = None
            for tile in range(tiles):
                grad_now = core_grad_ref[index, pl.ds(place, 1), cut(tile)]
                if place > 0:
                    earlier = states_ref[now - 1, :, cut(tile)]
                else:
                    earlier = jnp.where(
                        index > 0, states_ref[jnp.maximum(now - 1, 0), :, cut(tile)], begin_ref[0, :, cut(tile)]
                    )
                grad_state = incoming[tile] + read_now * grad_now
                through_read = current[tile] * grad_now
                current[tile] = earlier
                through_write = grad_state * flows[index, pl.ds(place, 1), cut(tile)]
                read_sum = through_read if read_sum is None else read_sum + through_read
                write_sum = through_write if write_sum is None else write_sum + through_write
                passed = grad_state * write_now
                first_buf[tile, pl.ds(place * chunk, chunk), :] = passed[:half_size] + passed[half_size:]
                exponent = rates[tile] * decay_step[index, pl.ds(place, 1), cut(tile)]
                leaving = jnp.exp2(exponent) * grad_state
                incoming[tile] = leaving
                weighted = (leaving * earlier) * exponent
                second_buf[tile, pl.ds(place * chunk, chunk), :] = weighted[:half_size] + weighted[half_size:]
                decay_sums[tile] = decay_sums[tile] + weighted
            read_buf[token] += read_sum
            write_buf[token] += write_sum
        for tile in range(tiles):
            through_buf[index, :, cut(tile)] = folded(first_buf, tile)
            scaled_buf[index, :, cut(tile)] = folded(second_buf, tile)
        return (tuple(incoming), tuple(decay_sums), tuple(current))

    incoming = tuple(incoming_buf[:, cut(tile)] for tile in range(tiles))
    nothing = (jnp.zeros((size, lanes), jnp.float32),) * tiles
    current = tuple(states_ref[rows - 1, :, cut(tile)] for tile in range(tiles))
    schedule = {}
    for which in range(count):
        for number in (1, 2, 3):
            schedule.setdefault((2, 4, 7, 9)[which] + (0, 3, 5)[number - 1], []).append((which, number))

    def move_on(legs):
        for which, number in legs:
            reduce.leg(which, number)

    carried = (incoming, nothing, current)
    for half_loop in range(2):
        for point, legs in sorted(schedule.items()):
            if point % 2 == half_loop:
                pl.when(moment == point // 2)(functools.partial(move_on, legs))
        carried = lax.fori_loop(half_loop * chunks // 2, (half_loop + 1) * chunks // 2, backward, carried)
    incoming, decay_sums, _ = carried
    for tile in range(tiles):
        incoming_buf[:, cut(tile)] = incoming[tile]
        decay_grad_ref[:, cut(tile)] += decay_sums[tile] * ln2
    skip = small_rows(small_ref, *plan["skip"])

    def after(index, at, carry):
        spot = pl.ds(pl.multiple_of(index * 4, 4), 4)
        sums = []
        for tile in range(tiles):
            signal = signal_ref[at, cut(tile)].astype(jnp.float32)
            step = step_ref[spot, :, cut(tile)].reshape(4 * chunk, lanes)
            through = through_buf[spot, :, cut(tile)].reshape(4 * chunk, lanes)
            scaled = scaled_buf[spot, :, cut(tile)].reshape(4 * chunk, lanes)
            core_grad = core_grad_ref[spot, :, cut(tile)].reshape(4 * chunk, lanes)
            grad_pre = (through * signal + ln2 * scaled / jnp.maximum(step, tiny)) * slope_of(step)
            low_buf[at, cut(tile)] = grad_pre.astype(low_buf.dtype)
            signal_grad_ref[at, cut(tile)] = (
                through * step + skip[:, tile * lanes : (tile + 1) * lanes] * core_grad
            )
            sums.append(carry[tile] + eight(grad_pre))
        return tuple(sums)

    zero_rows = jnp.zeros((8, lanes), jnp.float32)
    sums = row_loop(rows, 4 * chunk, after, (zero_rows,) * tiles)
    for tile in range(tiles):
        bias_grad_ref[:, cut(tile)] += jnp.sum(sums[tile], axis=0, keepdims=True)
    step_w_grad_ref[...] += contract(
        projected_ref[:, :rank].astype(low_buf.dtype), low_buf[...], 0, 0
    )
    step_w = small_ref[pl.ds(plan["step"][0], rank), :]
    step_w = jnp.concatenate([step_w, jnp.zeros((lanes - rank, width), step_w.dtype)], axis=0)
    rank_buf[pl.ds(group * chunks, chunks)] += contract(low_buf[...], step_w, 1, 1).reshape(
        chunks, chunk, lanes
    )

    @pl.when(moment == moments - 1)
    def _():
        squares = jnp.zeros((8, lanes), jnp.float32)
        for which in range(count):
            squares = squares + reduce.finish(which)[0]
        square_ref[...] = squares
        some = 8
        entry = lax.rem(lax.broadcasted_iota(jnp.int32, (some * chunk * size, lanes), 0), size)
        target = lax.broadcasted_iota(jnp.int32, (some * chunk * size, lanes), 1)
        ones = jnp.ones((lanes, lanes), jnp.bfloat16)

        def lay(index, carry):
            lot = pl.ds(index * some * chunk, some * chunk)
            for number, buffer in enumerate((write_buf, read_buf)):
                high, low = high_low(buffer[lot].reshape(some * chunk * size, lanes))
                summed = jnp.dot(high.astype(jnp.bfloat16), ones, preferred_element_type=jnp.float32)
                summed += jnp.dot(low.astype(jnp.bfloat16), ones, preferred_element_type=jnp.float32)
                summed = jnp.where(target == entry + rank + number * size, summed, 0.0)
                summed = jnp.sum(summed.reshape(some * chunk, size, lanes), axis=1)
                rank_buf[pl.ds(index * some, some)] += summed.reshape(some, chunk, lanes)
            return carry

        lax.fori_loop(0, rank_buf.shape[0] // some, lay, 0)
        flat_ref[...] = rank_buf[...].reshape(flat_ref.shape).astype(flat_ref.dtype)
        for which in range(count):
            reduce.settle(which)
        for index in range(pieces):
            for target, result in ((out_sum_ref, out_result), (in_sum_ref, gate_result)):
                each = result.shape[2]
                target[:, index * each : (index + 1) * each] = result[index]


def back_kernel(
    plan,
    dims,
    lengths_ref,
    tokens_ref,
    low_ref,
    gain_ref,
    small_ref,
    flat_ref,
    branch_ref,
    signal_ref,
    slope_ref,
    signal_grad_ref,
    gate_grad_ref,
    flipped_ref,
    branch_w,
    gate_w,
    step_w_grad_ref,
    bias_grad_ref,
    decay_grad_ref,
    skip_grad_ref,
    plain_ref,
    earlier_ref,
    tokens_grad_ref,
    in_sum_ref,
    small_sum_ref,
    late_sum_ref,
    norm_ref,
    offset_buf,
    conv_buf,
    mixed_buf,
    total,
    in_stage,
    small_stage,
    late_stage,
    late_land,
    late_cores,
    norm_own,
    norm_land,
    norm_cores,
    in_result,
    small_result,
    direct_send,
    direct_recv,
    *parts,
):
    rows = tokens_ref.shape[0]
    width = branch_ref.shape[1]
    tiles = width // lanes
    block = pl.program_id(0)
    last = in_stage.shape[0]
    count = last + 1
    reduce = Reduce(
        dims,
        [small_stage] + [in_stage.at[index] for index in range(last)],
        parts[: 5 * count],
        parts[5 * count :],
        [small_result] + [in_result.at[index] for index in range(last)],
        True,
    )
    share = small_stage.shape[4]
    half_rows = small_stage.shape[3]
    planes = small_stage.shape[1]
    owners = small_stage.shape[0] * planes

    @pl.when(block == 0)
    def _():
        Place(dims).greet(everyone=True)
        select_grad = contract(flat_ref[...], signal_ref[...], 0, 0)
        step_first, step_tall = plan["step"]
        filler = jnp.zeros((2 * half_rows - step_first - step_tall, select_grad.shape[1]), jnp.float32)
        pieces = {
            "decay": decay_grad_ref[...],
            "bias": bias_grad_ref[...],
            "skip": skip_grad_ref[...],
            "step": step_w_grad_ref[...],
        }
        first = plan["select"][1]
        rows_now = [select_grad[:first]]
        for name in ("decay", "taps", "shift", "bias", "skip", "gain"):
            tall = plan[name][1]
            rows_now.append(
                pieces[name] if name in pieces else jnp.zeros((tall, select_grad.shape[1]), jnp.float32)
            )
            first += tall
        rows_now.append(jnp.zeros((step_first - first, select_grad.shape[1]), jnp.float32))
        rows_now.append(pieces["step"])
        if filler.shape[0]:
            rows_now.append(filler)
        everything = jnp.concatenate(rows_now, axis=0)
        for owner in range(owners):
            for side in range(2):
                small_stage[owner // planes, owner % planes, side] = everything[
                    side * half_rows : (side + 1) * half_rows, owner * share : (owner + 1) * share
                ].astype(small_stage.dtype)
        reduce.start(0)
        fill_offsets(lengths_ref, offset_buf, rows)

    def move_on(plan_of_moves):
        for moment, legs in plan_of_moves:

            @pl.when(block == moment)
            def _(legs=legs):
                for which, number in legs:
                    reduce.leg(which, number)

    taps = small_rows(small_ref, *plan["taps"])
    taps_count = taps.shape[0]
    zero_rows = jnp.zeros((8, lanes), jnp.float32)

    @pl.when(block < last)
    def _():
        conv_buf[pl.ds(0, rows), :] = signal_grad_ref[...] + jnp.dot(
            flat_ref[...], small_ref[:lanes, :], preferred_element_type=jnp.float32
        )
        conv_buf[pl.ds(rows, 8), :] = jnp.zeros((8, width), jnp.float32)

        def through_conv(index, at, carry):
            sums = []
            for tile in range(tiles):
                grad_conv = conv_buf[at, cut(tile)] * slope_ref[at, cut(tile)]
                conv_buf[at, cut(tile)] = grad_conv
                sums.append(carry[tile] + eight(grad_conv))
            return tuple(sums)

        shift_sums = row_loop(rows, 32, through_conv, (zero_rows,) * tiles)
        move_on(((0, ((0, 1),)), (1, ((1, 1), (0, 3))), (2, ((2, 1), (1, 3))), (3, ((3, 1), (2, 3)))))

        def to_branch(index, at, carry):
            longer = pl.ds(pl.multiple_of(index * 32, 32), 40)
            offsets = offset_buf[longer, :]
            result = []
            for tile in range(tiles):
                here = slice(tile * lanes, (tile + 1) * lanes)
                grads = conv_buf[longer, cut(tile)]
                branch = branch_ref[at, cut(tile)]
                summed = taps[taps_count - 1 : taps_count, here] * grads[:32]
                sums = [None] * taps_count
                sums[taps_count - 1] = carry[tile][taps_count - 1] + eight(branch * grads[:32])
                for tap in range(taps_count - 1):
                    lag = taps_count - 1 - tap
                    moved = pltpu.roll(jnp.where(offsets >= lag, grads, 0.0), 40 - lag, 0)[:32]
                    summed = summed + taps[tap : tap + 1, here] * moved
                    sums[tap] = carry[tile][tap] + eight(branch * moved)
                mixed_buf[block, at, cut(tile)] = summed.astype(mixed_buf.dtype)
                result.append(tuple(sums))
            return tuple(result)

        sums = row_loop(rows, 32, to_branch, ((zero_rows,) * taps_count,) * tiles)
        in_grad = jnp.dot(flipped_ref[...], mixed_buf[block], preferred_element_type=jnp.float32)
        in_stage[block] = in_grad.reshape(in_stage.shape[1:]).astype(in_stage.dtype)
        for index in range(last):

            @pl.when(block == index)
            def _(index=index):
                reduce.start(index + 1)

        late = [
            jnp.concatenate(
                [jnp.sum(sums[tile][tap], axis=0, keepdims=True) for tap in range(taps_count)]
                + [jnp.sum(shift_sums[tile], axis=0, keepdims=True)]
                + [jnp.zeros((8 - taps_count - 1, lanes), jnp.float32)],
                axis=0,
            )
            for tile in range(tiles)
        ]
        late = jnp.concatenate(late, axis=1)
        for piece in range(width // share):
            late_stage[block * (width // share) + piece] = late[:, piece * share : (piece + 1) * share]
        move_on(((0, ((0, 2),)), (1, ((1, 2),)), (2, ((2, 2),)), (3, ((3, 2),))))

    @pl.when(block >= last)
    def _():
        grad_normed_piece = contract(mixed_buf[block - last], rows_of(branch_w), 1, 1)
        grad_normed_piece += contract(gate_grad_ref[...], rows_of(gate_w), 1, 1)

        @pl.when(block == last)
        def _():
            total[...] = grad_normed_piece

        @pl.when(block > last)
        def _():
            total[...] += grad_normed_piece

        move_on(((4, ((4, 1), (3, 3))), (6, ((4, 2),)), (7, ((4, 3),))))

    @pl.when(block == pl.num_programs(0) - 1)
    def _():
        def finish(index, at, carry):
            residual = tokens_ref[at, :].astype(jnp.float32)
            scale = lax.rsqrt(jnp.mean(residual * residual, axis=1, keepdims=True) + epsilon)
            grad_normed = total[at, :]
            weighted = grad_normed * gain_ref[...]
            inner = jnp.mean(weighted * residual, axis=1, keepdims=True)
            grad_y = low_ref[at, :].astype(jnp.float32)
            result = grad_y + (scale * weighted - residual * (scale * scale * scale) * inner)
            tokens_grad_ref[at, :] = result.astype(tokens_grad_ref.dtype)
            return carry + eight(grad_normed * residual * scale)

        gains = row_loop(rows, 16, finish, jnp.zeros((8, total.shape[1]), jnp.float32))
        gains = jnp.sum(gains, axis=0, keepdims=True)
        place = Place(dims)
        each = gains.shape[1] // owners
        for owner in range(owners):
            late_stage[owner, taps_count + 1 : taps_count + 2, :each] = gains[
                :, owner * each : (owner + 1) * each
            ]
        late_sems = direct_send.at[0], direct_recv.at[0]
        norm_sems = direct_send.at[1], direct_recv.at[1]
        send_to_all(place, lambda target: late_stage.at[target], late_land, *late_sems)
        late_sum = sum_of_all(place, late_stage[place.me], late_land, *late_sems)
        late_sum = sum_of_cores(place, late_sum, late_cores, direct_send.at[0, 0], direct_recv.at[0, 0])
        late_sum_ref[...] = late_sum
        kept = earlier_ref[...] + folded_squares(late_sum * late_sum) * (1 - place.core).astype(jnp.float32)
        more, plain = reduce.finish(0, plain_ref)
        kept = kept + more
        for index in range(1, count):
            kept = kept + reduce.finish(index)[0]
        norm_own[...] = jnp.stack([kept, plain])
        send_to_all(place, lambda target: norm_own, norm_land, *norm_sems)
        norms = sum_of_all(place, norm_own[...], norm_land, *norm_sems)
        norm_ref[...] = sum_of_cores(place, norms, norm_cores, direct_send.at[1, 0], direct_recv.at[1, 0])
        for index in range(count):
            reduce.settle(index)
        for index in range(last):
            in_sum_ref[:, index * width : (index + 1) * width] = in_result[index]
        small_sum_ref[...] = small_result[...]


def finish_kernel(
    plan, names, late, tokens_ref, branch_ref, gate_ref, out_ref, small_ref, late_ref, norm_ref, *outs
):
    middle = branch_ref.shape[1]
    outs[0][:, :middle] = branch_ref[...]
    outs[0][:, middle:] = gate_ref[...]
    outs[1][...] = out_ref[...]
    outs[2][...] = tokens_ref[...]
    for name, target in zip(names, outs[3 : 3 + len(names)]):
        source, (first, count) = (late_ref, late[name]) if name in late else (small_ref, plan[name])
        if len(target.shape) == 1:
            target[...] = source[first, : target.shape[0]]
        else:
            target[...] = source[first : first + count, :]
    for index in range(2):
        outs[3 + len(names) + index][0, 0] = jnp.sum(norm_ref[index])


def shape(dims, kind=jnp.float32):
    return jax.ShapeDtypeStruct(dims, kind)


def compute_call(
    kernel, name, blocks, in_specs, out_specs, out_shape, scratch, flops, operands, collective_id=None
):
    return pl.pallas_call(
        kernel,
        grid=blocks if isinstance(blocks, tuple) else (blocks,),
        in_specs=in_specs,
        out_specs=out_specs,
        out_shape=out_shape,
        scratch_shapes=scratch,
        compiler_params=pltpu.CompilerParams(
            dimension_semantics=("arbitrary",) * (len(blocks) if isinstance(blocks, tuple) else 1),
            vmem_limit_bytes=62 * 1024 * 1024,
            collective_id=collective_id,
            has_side_effects=collective_id is not None,
        ),
        cost_estimate=pl.CostEstimate(flops=flops, bytes_accessed=40 << 20, transcendentals=0),
        name=name,
    )(*operands)


class Place:
    def __init__(self, dims, swapped=False):
        depth, tall, wide = dims
        self.dims = dims
        self.core = lax.axis_index("wide")
        self.me = lax.axis_index("narrow")
        self.across = lax.rem(self.me, wide)
        self.up = lax.rem(lax.div(self.me, wide), tall)
        self.deep = lax.div(self.me, wide * tall)
        side = 1 - self.core if swapped else self.core
        turn = side if tall == wide else 0
        self.second = (1 + turn * (wide - 1), self.across + turn * (self.up - self.across), wide)
        self.third = (wide - turn * (wide - 1), self.up + turn * (self.across - self.up), tall)
        self.spans = (depth, wide, tall)
        self.other = {"wide": 1 - self.core}

    def level(self, d):
        return lax.rem(self.deep + d, self.spans[0])

    def plane(self, e, f):
        return (
            lax.rem(self.second[1] + e, self.second[2]) * self.second[0]
            + lax.rem(self.third[1] + f, self.third[2]) * self.third[0]
        )

    def plane_behind(self, e, f):
        return self.plane((self.spans[1] - e) % self.spans[1], (self.spans[2] - f) % self.spans[2])

    def at(self, d, e, f):
        return {"narrow": self.level(d) * (self.dims[1] * self.dims[2]) + self.plane(e, f)}

    def greet(self, everyone=False):
        barrier = pltpu.get_barrier_semaphore()
        peers = [self.other]
        if everyone:
            number = self.spans[0] * self.spans[1] * self.spans[2]
            peers += [{"narrow": lax.rem(self.me + hop, number)} for hop in range(1, number)]
        else:
            for axis, size in enumerate(self.spans):
                for hop in range(1, size):
                    move = [0, 0, 0]
                    move[axis] = hop
                    peers.append(self.at(*move))
        for peer in peers:
            pl.semaphore_signal(barrier, inc=1, device_id=peer, device_id_type=pl.DeviceIdType.MESH)
        pl.semaphore_wait(barrier, len(peers))


def by_rows(block):
    return block[0] % 32 == 0


def half_shape(block):
    if len(block) == 3:
        return tuple(block[1:])
    return (block[0] // 2, block[1]) if by_rows(block) else (block[0], block[1] // 2)


def half(view, block, side, lead=0):
    ahead = (slice(None),) * lead
    if len(block) == 3:
        return view.at[ahead + (side,)]
    if by_rows(block):
        return view.at[ahead + (pl.ds(pl.multiple_of(side * (block[0] // 2), 16), block[0] // 2),)]
    columns = pl.ds(pl.multiple_of(side * (block[1] // 2), lanes), block[1] // 2)
    return view.at[ahead + (slice(None), columns)]


def remote(source, target, send_sem, recv_sem, device):
    return pltpu.make_async_remote_copy(
        src_ref=source,
        dst_ref=target,
        send_sem=send_sem,
        recv_sem=recv_sem,
        device_id=device,
        device_id_type=pl.DeviceIdType.MESH,
    )


class Gather:
    def __init__(self, dims, own, whole, sems, blocks=None):
        self.dims, self.own, self.whole = dims, own, whole
        self.local_sem, self.send_sem, self.recv_sem = sems
        self.lined = blocks is not None
        self.blocks = blocks or [block.shape for block in own]

    @staticmethod
    def sems(count, dims):
        copies = dims[0] + 2 * dims[1] * dims[2]
        return [pltpu.SemaphoreType.DMA((count,))] + [pltpu.SemaphoreType.DMA((count, copies))] * 2

    def line(self, which, plane, side):
        return half(self.whole[which].at[:, plane], self.blocks[which], side, 1)

    def local(self, place, which):
        block = self.blocks[which]
        if self.lined:
            return pltpu.make_async_copy(
                self.own[which], self.line(which, place.plane(0, 0), place.core), self.local_sem.at[which]
            )
        return pltpu.make_async_copy(
            half(self.own[which], block, place.core),
            half(self.whole[which].at[place.deep, place.plane(0, 0)], block, place.core),
            self.local_sem.at[which],
        )

    def copy(self, which, source, target, index, device):
        return remote(
            source, target, self.send_sem.at[which, index], self.recv_sem.at[which, index], device
        )

    def rise(self, place, which, hop):
        block = self.blocks[which]
        return self.copy(
            which,
            half(self.own[which], block, place.core),
            half(self.whole[which].at[place.deep, place.plane(0, 0)], block, place.core),
            hop,
            place.at(hop, 0, 0),
        )

    def leg_index(self, e, f):
        return self.dims[0] + e * self.dims[1] + f

    def hand_index(self, e, f):
        return self.leg_index(e, f) + self.dims[1] * self.dims[2]

    def onward(self, place, which, e, f):
        line = self.line(which, place.plane_behind(e, f), place.core)
        source = self.own[which] if self.lined and e == 0 and f == 0 else line
        if f == 0:
            for hop in range(1, place.spans[2]):
                self.copy(which, source, line, self.leg_index(e, hop), place.at(0, 0, hop)).start()
        if f == 0 and e == 0:
            for hop in range(1, place.spans[1]):
                self.copy(which, source, line, self.leg_index(hop, 0), place.at(0, hop, 0)).start()
        self.copy(which, source, line, self.hand_index(e, f), place.other).start()

    def start(self, which):
        place = Place(self.dims)
        if self.lined:
            self.onward(place, which, 0, 0)
            self.local(place, which).start()
            return
        for hop in range(1, place.spans[0]):
            self.rise(place, which, hop).start()
        self.local(place, which).start()

    def leg(self, which, number):
        place = Place(self.dims)
        if number == 1:
            self.local(place, which).wait()
            for hop in range(1, place.spans[0]):
                self.rise(place, which, hop).wait_recv()
            self.onward(place, which, 0, 0)
            return
        for e in range(place.spans[1]):
            for f in range(place.spans[2]):
                if (number == 2 and f == 0 and e > 0) or (number == 3 and f > 0):
                    line = self.line(which, place.plane_behind(e, f), place.core)
                    self.copy(which, line, line, self.leg_index(e, f), place.other).wait_recv()
                    self.onward(place, which, e, f)

    def arrive(self, which):
        place, mirror = Place(self.dims), Place(self.dims, swapped=True)
        for e in range(place.spans[1]):
            for f in range(place.spans[2]):
                line = self.line(which, mirror.plane_behind(e, f), 1 - place.core)
                self.copy(which, line, line, self.hand_index(e, f), place.other).wait_recv()

    def drain(self, which):
        place = Place(self.dims)
        if self.lined:
            self.local(place, which).wait()
        else:
            for hop in range(1, place.spans[0]):
                self.rise(place, which, hop).wait_send()
        for e in range(place.spans[1]):
            for f in range(place.spans[2]):
                line = self.line(which, place.plane_behind(e, f), place.core)
                if e > 0 or f > 0:
                    self.copy(which, line, line, self.leg_index(e, f), place.other).wait_send()
                self.copy(which, line, line, self.hand_index(e, f), place.other).wait_send()


class Rise:
    def __init__(self, dims, own, lines, sems):
        self.dims, self.own, self.lines = dims, own, lines
        self.local_sem, self.send_sem, self.recv_sem = sems

    @staticmethod
    def sems(count, dims):
        return [pltpu.SemaphoreType.DMA((count,))] + [pltpu.SemaphoreType.DMA((count, dims[0]))] * 2

    def copies(self, place, which):
        source = half(self.own[which], self.own[which].shape, place.core)
        target = self.lines[which].at[place.deep]
        local = pltpu.make_async_copy(source, target, self.local_sem.at[which])
        return local, [
            remote(
                source, target, self.send_sem.at[which, hop], self.recv_sem.at[which, hop], place.at(hop, 0, 0)
            )
            for hop in range(1, place.spans[0])
        ]

    def start(self, which):
        local, sends = self.copies(Place(self.dims), which)
        for copy in [*sends, local]:
            copy.start()

    def finish(self, which):
        local, sends = self.copies(Place(self.dims), which)
        local.wait()
        for copy in sends:
            copy.wait_recv()
            copy.wait_send()


class Reduce:
    def __init__(self, dims, grads, rooms, sems, results, resident):
        self.dims, self.grads, self.resident = dims, grads, resident
        count = len(grads)
        self.mine, self.swapped, self.third, self.second, self.first = (
            rooms[index * count : (index + 1) * count] for index in range(5)
        )
        self.loaded = None if resident else rooms[5 * count :]
        self.load_sem, self.swap_send, self.swap_recv, self.send_sem, self.recv_sem = sems[:5]
        self.last_send, self.last_recv = sems[5:]
        self.results = results

    @staticmethod
    def rooms(dims, grads, resident):
        depth, tall, wide = dims
        leads = (
            (tall, wide, depth),
            (depth, tall * wide),
            (tall - 1, wide, depth),
            (wide - 1, depth),
            (depth - 1,),
        )
        if not resident:
            leads += ((depth, tall * wide),)
        return [
            pltpu.VMEM(lead + half_shape(grad.shape[2:]), grad.dtype) for lead in leads for grad in grads
        ]

    @staticmethod
    def sems(count, dims):
        return (
            [pltpu.SemaphoreType.DMA((count,))] * 3
            + [pltpu.SemaphoreType.DMA((count, dims[0] + dims[1] + dims[2]))] * 2
            + [pltpu.SemaphoreType.DMA((count,))] * 2
        )

    def block(self, which):
        return self.grads[which].shape[2:]

    def load(self, place, which):
        return pltpu.make_async_copy(
            half(self.grads[which], self.block(which), place.core, 2),
            self.loaded[which],
            self.load_sem.at[which],
        )

    def swap(self, place, which):
        return remote(
            half(self.grads[which], self.block(which), 1 - place.core, 2),
            self.swapped[which],
            self.swap_send.at[which],
            self.swap_recv.at[which],
            place.other,
        )

    def hop(self, which, source, target, index, device):
        return remote(
            source, target, self.send_sem.at[which, index], self.recv_sem.at[which, index], device
        )

    def third_hop(self, place, which, f):
        return self.hop(which, self.mine[which].at[f], self.third[which].at[f - 1], f, place.at(0, 0, f))

    def second_hop(self, place, which, e):
        return self.hop(
            which,
            self.mine[which].at[0, e],
            self.second[which].at[e - 1],
            self.dims[1] + e,
            place.at(0, e, 0),
        )

    def first_hop(self, place, which, d):
        return self.hop(
            which,
            self.mine[which].at[0, 0, place.level(d)],
            self.first[which].at[d - 1],
            self.dims[1] + self.dims[2] + d,
            place.at(d, 0, 0),
        )

    def start(self, which):
        place = Place(self.dims)
        self.swap(place, which).start()
        if not self.resident:
            self.load(place, which).start()

    def parts(self, place, which, e, f, z):
        plane = place.plane(e, f)
        if self.resident:
            found = [half(self.grads[which].at[z, plane], self.block(which), place.core)]
        else:
            found = [self.loaded[which].at[z, plane]]
        found.append(self.swapped[which].at[z, plane])
        if f == 0:
            found += [self.third[which].at[hop - 1, e, z] for hop in range(1, place.spans[2])]
        if f == 0 and e == 0:
            found += [self.second[which].at[hop - 1, z] for hop in range(1, place.spans[1])]
        return found

    def ready(self, place, which):
        if not self.resident:
            self.load(place, which).wait()
        self.swap(place, which).wait_recv()

    def added(self, parts, store, carry):
        rows = parts[0].shape[0]
        group = min(rows, 16)

        def some(index, carry):
            at_rows = pl.ds(pl.multiple_of(index * group, group), group)
            total = parts[0][at_rows, :].astype(jnp.float32)
            for part in parts[1:]:
                total = total + part[at_rows, :].astype(jnp.float32)
            return store(at_rows, total, carry)

        return lax.fori_loop(0, rows // group, some, carry)

    def sum_into(self, place, which, e, f, z):
        target = self.mine[which].at[f, e, z]

        def keep(at_rows, total, carry):
            target[at_rows, :] = total.astype(target.dtype)
            return carry

        self.added(self.parts(place, which, e, f, z), keep, 0)

    def leg(self, which, number):
        place = Place(self.dims)
        depth, span_e, span_f = place.spans
        if number == 1:
            self.ready(place, which)
            for f in range(span_f - 1, 0, -1):
                for e in range(span_e - 1, -1, -1):
                    for z in range(depth):
                        self.sum_into(place, which, e, f, z)
                self.third_hop(place, which, f).start()
        elif number == 2:
            for f in range(1, span_f):
                self.third_hop(place, which, f).wait_recv()
            for e in range(span_e - 1, 0, -1):
                for z in range(depth):
                    self.sum_into(place, which, e, 0, z)
                self.second_hop(place, which, e).start()
        else:
            if span_e == 1:
                for f in range(1, span_f):
                    self.third_hop(place, which, f).wait_recv()
            for e in range(1, span_e):
                self.second_hop(place, which, e).wait_recv()
            for d in range(1, depth):
                self.sum_into(place, which, 0, 0, place.level(d))
                self.first_hop(place, which, d).start()

    def result(self, which, side):
        return half(self.results[which], self.block(which), side)

    def last(self, place, which, side):
        share = self.result(which, side)
        return remote(share, share, self.last_send.at[which], self.last_recv.at[which], place.other)

    def finish(self, which, marks=None):
        place = Place(self.dims)
        parts = self.parts(place, which, 0, 0, place.deep)
        for d in range(1, place.spans[0]):
            self.first_hop(place, which, d).wait_recv()
            parts.append(self.first[which].at[d - 1])
        share = self.result(which, place.core)

        def store(at_rows, total, carry):
            share[at_rows, :] = total
            kept, plain = carry
            squared = total * total
            if marks is not None:
                marked = squared * marks[place.core, at_rows, :]
                plain = plain + folded_squares(marked)
                squared = squared - marked
            return (kept + folded_squares(squared), plain)

        squares = self.added(parts, store, (jnp.zeros((8, lanes), jnp.float32),) * 2)
        self.last(place, which, place.core).start()
        return squares

    def settle(self, which):
        place = Place(self.dims)
        last = self.last(place, which, 1 - place.core)
        last.wait_recv()
        last.wait_send()
        self.swap(place, which).wait_send()
        for f in range(1, place.spans[2]):
            self.third_hop(place, which, f).wait_send()
        for e in range(1, place.spans[1]):
            self.second_hop(place, which, e).wait_send()
        for d in range(1, place.spans[0]):
            self.first_hop(place, which, d).wait_send()


def folded_squares(values):
    total = None
    if values.shape[1] < lanes:
        first = lax.broadcasted_iota(jnp.int32, (values.shape[0], lanes), 1) == 0
        values = jnp.where(first, jnp.sum(values, axis=1, keepdims=True), 0.0)
    for row in range(0, values.shape[0], 8):
        for column in range(0, values.shape[1], lanes):
            piece = values[row : row + 8, column : column + lanes]
            total = piece if total is None else total + piece
    return total


def send_to_all(place, source, landing, send_sem, recv_sem):
    number = landing.shape[0]
    for hop in range(1, number):
        target = lax.rem(place.me + hop, number)
        remote(
            source(target), landing.at[place.me], send_sem.at[hop], recv_sem.at[hop], {"narrow": target}
        ).start()


def wait_for_all(place, own, landing, send_sem, recv_sem):
    number = landing.shape[0]
    landing[place.me] = own
    for hop in range(1, number):
        came = landing.at[lax.rem(place.me + number - hop, number)]
        copy = remote(came, came, send_sem.at[hop], recv_sem.at[hop], place.other)
        copy.wait_recv()
        copy.wait_send()


def sum_of_all(place, own, landing, send_sem, recv_sem):
    number = landing.shape[0]
    wait_for_all(place, own, landing, send_sem, recv_sem)
    total = landing[0]
    for spot in range(1, number):
        total = total + landing[spot]
    return total


def sum_of_cores(place, own, landing, send_sem, recv_sem):
    landing[place.core] = own
    copy = remote(landing.at[place.core], landing.at[place.core], send_sem, recv_sem, place.other)
    copy.start()
    copy.wait()
    return landing[0] + landing[1]


def grid_of(mesh):
    number = mesh.shape["narrow"]
    places = [getattr(device, "coords", None) for device in mesh.devices[0]]
    if all(place is not None for place in places):
        sizes = [len({place[axis] for place in places}) for axis in (2, 1, 0)]
        if sizes[0] * sizes[1] * sizes[2] == number:
            return tuple(sizes)
    side = round((number / 2) ** (1 / 3))
    return (2 * side, side, side) if 2 * side**3 == number else (number, 1, 1)


def plan_of(select_rows, state_size, tap_count, step_rows):
    plan, first = {}, 0
    for name, tall in (
        ("select", select_rows),
        ("decay", state_size),
        ("taps", tap_count),
        ("shift", 1),
        ("bias", 1),
        ("skip", 1),
        ("gain", 1),
    ):
        plan[name] = (first, tall)
        first += tall
    plan["step"] = (lanes, step_rows)
    plan["rows"] = -(-(lanes + step_rows) // 32) * 32
    return plan


def per_device(
    dims,
    tokens,
    cotangent,
    loss_mask,
    seq_lengths,
    norm_gain,
    in_proj,
    conv_weight,
    conv_bias,
    select_proj,
    step_proj,
    step_bias,
    decay_log,
    skip_scale,
    out_proj,
):
    half = jnp.bfloat16
    piece = skip_scale.shape[0]
    gain_piece = norm_gain.shape[0]
    rank, size = step_proj.shape[0], decay_log.shape[0]
    plan = plan_of(select_proj.shape[0], size, conv_weight.shape[0], rank)
    smalls = {
        "select": select_proj,
        "decay": decay_log,
        "taps": conv_weight,
        "shift": conv_bias[None],
        "bias": step_bias[None],
        "skip": skip_scale[None],
        "gain": norm_gain[None],
        "step": step_proj,
    }
    depth, planes = dims[0], dims[1] * dims[2]
    number = depth * planes
    in_rows = in_proj.shape[0]
    rows, model = tokens.shape
    inner = piece * number
    width = 4 * lanes
    blocks = inner // width
    chunks = rows // chunk
    mask_row = loss_mask[None]

    whole = pl.BlockSpec(memory_space=pltpu.VMEM)
    tall = pl.BlockSpec((rows, width), lambda b: (0, b))
    deep = pl.BlockSpec((chunks, chunk, width), lambda b: (0, 0, b))
    lead = pl.BlockSpec((rows, size, width), lambda b: (0, 0, b))
    first_w = pl.BlockSpec((model, width), lambda b: (0, b))
    second_w = pl.BlockSpec((model, width), lambda b: (0, b + blocks))
    out_w = pl.BlockSpec((width, model), lambda b: (b, 0))

    def thin(height):
        return pl.BlockSpec((height, width), lambda b: (0, b))

    def fixed(*dims_of):
        return pl.BlockSpec(dims_of, lambda b: (0,) * len(dims_of))

    scalars = pl.BlockSpec(memory_space=pltpu.SMEM)
    offset_buf = pltpu.VMEM((rows + 8, lanes), jnp.int32)
    packed = thin(plan["rows"])

    pair = (chunks, 2 * chunk, lanes)
    pair = (chunks, 2 * chunk, lanes)
    anywhere = pl.BlockSpec(memory_space=pl.ANY)
    small_half = (2, plan["rows"] // 2, piece)
    in_piece = (in_rows, width)
    shares = 2
    in_share = (in_rows, inner // shares)
    out_share = (out_proj.shape[0], model // shares)
    lines = [shape((shares, depth) + half_shape(block), half) for block in (in_share, out_share)]
    (
        branch,
        signal,
        slope,
        projected,
        flipped,
        normed,
        grad_low,
        write_pair,
        read_pair,
        small,
        gain_value,
        in_blocks,
        gate_lines,
        out_lines,
    ) = compute_call(
        functools.partial(front_kernel, plan, dims, tuple(smalls)),
        "front",
        blocks,
        [scalars, whole, whole, whole] + [whole] * len(smalls) + [whole] * 2,
        [tall, tall, tall] + [whole] * 8 + [anywhere] * 3,
        [
            shape((rows, inner)),
            shape((rows, inner), half),
            shape((rows, inner)),
            shape((rows, lanes)),
            shape((model, rows), half),
            shape((rows, model), half),
            shape((rows, model), half),
            shape(pair, half),
            shape(pair, half),
            shape((plan["rows"], inner), half),
            shape((1, model)),
            shape((blocks, depth, planes) + in_piece, half),
            *lines,
        ],
        [
            offset_buf,
            pltpu.VMEM((plan["rows"], piece), jnp.float32),
            pltpu.VMEM(small_half, half),
            pltpu.VMEM((blocks,) + in_piece, half),
            pltpu.VMEM((shares,) + in_share, half),
            pltpu.VMEM((shares,) + out_share, half),
            pltpu.VMEM((depth, planes) + small_half, half),
            pltpu.VMEM((blocks, depth, planes) + in_piece, half),
            pltpu.SemaphoreType.DMA((blocks,)),
            pltpu.VMEM((8, piece), jnp.float32),
            pltpu.VMEM((number, 8, piece), jnp.float32),
            pltpu.SemaphoreType.DMA((number,)),
            pltpu.SemaphoreType.DMA((number,)),
        ]
        + Gather.sems(1 + blocks, dims)
        + Rise.sems(2 * shares, dims),
        4 * rows * model * inner,
        (seq_lengths, tokens, cotangent, mask_row, *smalls.values(), in_proj, out_proj),
        collective_id=0,
    )
    groups = 2
    part, pieces = rows // groups, chunks // groups
    row_block = pltpu.VMEM((pieces, chunk, width), jnp.float32)
    spread_block = pltpu.VMEM((rows, size, lanes), jnp.float32)
    fold_block = pltpu.VMEM((width // lanes, chunk * chunk, lanes), jnp.float32)

    def by_group(order, *dims_of):
        middle = (0,) * (len(dims_of) - 2)
        return pl.BlockSpec(dims_of, lambda b, g: (order(g),) + middle + (b,))

    def by_token(order, *dims_of):
        return pl.BlockSpec(dims_of, lambda b, g: (order(g),) + (0,) * (len(dims_of) - 1))

    def by_channel(height):
        return pl.BlockSpec((height, width), lambda b, g: (0, b))

    def onward(g):
        return g

    def backward(g):
        return groups - 1 - g

    states, step, core, begins, gate_blocks, out_blocks = compute_call(
        functools.partial(forward_kernel, plan, dims),
        "forward",
        (blocks, groups),
        [
            scalars,
            by_token(onward, part, lanes),
            by_channel(plan["rows"]),
            by_group(onward, part, width),
            whole,
            whole,
            anywhere,
            anywhere,
        ],
        [
            by_group(onward, part, size, width),
            by_group(onward, pieces, chunk, width),
            by_group(onward, pieces, chunk, width),
            by_group(onward, 1, size, width),
            anywhere,
            anywhere,
        ],
        [
            shape((rows, size, inner)),
            shape((chunks, chunk, inner)),
            shape((chunks, chunk, inner)),
            shape((groups, size, inner)),
            shape((shares, depth, planes) + in_share, half),
            shape((shares, depth, planes) + out_share, half),
        ],
        [
            offset_buf,
            pltpu.VMEM((part, width), jnp.float32),
            row_block,
            row_block,
            spread_block,
            spread_block,
            fold_block,
            pltpu.VMEM((size, width), jnp.float32),
        ]
        + Gather.sems(2 * shares, dims),
        15 * rows * inner * size,
        (seq_lengths, projected, small, signal, write_pair, read_pair, gate_lines, out_lines),
        collective_id=2,
    )
    split = in_share[1] // width
    weights = pl.BlockSpec((None, number, in_rows, width), lambda b: (b // split, 0, 0, b % split))
    per_block = width // out_share[0]
    out_pieces = pl.BlockSpec((shares, per_block) + out_share, lambda b: (0, b, 0, 0))
    branch_whole = in_blocks.reshape(blocks, number, *in_piece)
    gate_whole = gate_blocks.reshape(shares, number, *in_share)
    out_whole = out_blocks.reshape(shares, number, *out_share)
    core_grad, gate_grad, grad_skip, grad_outw, grad_in_gate, output = compute_call(
        functools.partial(middle_kernel, plan),
        "middle",
        blocks,
        [deep, packed, tall, weights, whole, out_pieces, whole, whole, whole],
        [
            deep,
            tall,
            thin(1),
            pl.BlockSpec((shares, width, out_share[1]), lambda b: (0, b, 0)),
            pl.BlockSpec((None, model, width), lambda b: (b // split, 0, b % split)),
            fixed(rows, model),
        ],
        [
            shape((chunks, chunk, inner)),
            shape((rows, inner), half),
            shape((1, inner)),
            shape((shares, inner, out_share[1]), half),
            shape((shares, model, in_share[1]), half),
            shape((rows, model), half),
        ],
        [
            pltpu.VMEM((rows, width), jnp.float32),
            pltpu.VMEM((rows, width), jnp.float32),
            pltpu.VMEM((rows, width), half),
            pltpu.VMEM((width, model), half),
            pltpu.VMEM((rows, model), jnp.float32),
        ],
        8 * rows * model * inner,
        (core, small, signal, gate_whole, grad_low, out_whole, flipped, normed, tokens),
    )
    early_grads = [
        grad_outw.reshape((shares, depth, planes) + out_share),
        grad_in_gate.reshape((shares, depth, planes) + in_share),
    ]
    early_sums = [shape(out_proj.shape), shape((in_rows, inner))]
    early_pieces = [shape((depth, planes) + block, half) for block in (in_share, out_share)] * shares
    (
        signal_grad,
        grad_stepw,
        grad_bias,
        grad_decaylog,
        flat,
        out_sum,
        in_gate_sum,
        early_squares,
    ) = compute_call(
        functools.partial(backward_kernel, plan, dims),
        "backward",
        (blocks, groups),
        [
            scalars,
            by_token(backward, part, lanes),
            by_channel(plan["rows"]),
            by_group(backward, part, width),
            whole,
            whole,
            by_group(backward, pieces, chunk, width),
            by_group(backward, pieces, chunk, width),
            by_group(backward, part, size, width),
            by_group(backward, 1, size, width),
            anywhere,
            anywhere,
        ],
        [
            by_group(backward, part, width),
            by_channel(rank),
            by_channel(1),
            by_channel(size),
            whole,
        ]
        + [whole] * 3,
        [
            shape((rows, inner)),
            shape((rank, inner)),
            shape((1, inner)),
            shape((size, inner)),
            shape((rows, lanes), half),
            *early_sums,
            shape((8, lanes)),
        ],
        [
            offset_buf,
            row_block,
            row_block,
            spread_block,
            spread_block,
            fold_block,
            fold_block,
            row_block,
            row_block,
            pltpu.VMEM((part, width), half),
            pltpu.VMEM((size, width), jnp.float32),
            pltpu.VMEM((chunks, chunk, lanes), jnp.float32),
            spread_block,
            spread_block,
        ]
        + [pltpu.VMEM((shares,) + block, jnp.float32) for block in (in_share, out_share)]
        + Reduce.rooms(dims, early_pieces, False)
        + Reduce.sems(2 * shares, dims),
        40 * rows * inner * size,
        (
            seq_lengths,
            projected,
            small,
            signal,
            write_pair,
            read_pair,
            step,
            core_grad,
            states,
            begins,
            *early_grads,
        ),
        collective_id=3,
    )

    plain_rows = np.zeros((plan["rows"], piece), np.float32)
    for name in ("bias", "decay", "skip"):
        first, count = plan[name]
        plain_rows[first : first + count] = 1.0
    late_grads = [shape((depth, planes) + small_half, half)]
    late_grads += [shape((depth, planes, in_rows, width), half)] * blocks
    taps_n = conv_weight.shape[0]
    late = {"taps": (0, taps_n), "shift": (taps_n, 1), "gain": (taps_n + 1, 1)}
    late_block = (8, piece)

    early_tall = pl.BlockSpec((rows, width), lambda b: (0, jnp.minimum(b, blocks - 1)))
    late_tall = pl.BlockSpec((rows, width), lambda b: (0, jnp.maximum(b - blocks, 0)))
    tokens_grad, in_branch_sum, small_sum, late_sum, norms = compute_call(
        functools.partial(back_kernel, plan, dims),
        "back",
        2 * blocks,
        [scalars, whole, whole, whole]
        + [pl.BlockSpec((plan["rows"], width), lambda b: (0, jnp.minimum(b, blocks - 1))), whole]
        + [early_tall, whole, early_tall, early_tall, late_tall, whole]
        + [
            pl.BlockSpec((None, number, in_rows, width), lambda b: (jnp.maximum(b - blocks, 0), 0, 0, 0)),
            pl.BlockSpec(
                (None, number, in_rows, width),
                lambda b: (jnp.maximum(b - blocks, 0) // split, 0, 0, jnp.maximum(b - blocks, 0) % split),
            ),
        ]
        + [whole] * 6,
        [whole] * 5,
        [
            shape((rows, model), half),
            shape((in_rows, inner)),
            shape(small_half),
            shape(late_block),
            shape((2, 8, lanes)),
        ],
        [
            offset_buf,
            pltpu.VMEM((rows + 8, width), jnp.float32),
            pltpu.VMEM((blocks, rows, width), half),
            pltpu.VMEM((rows, model), jnp.float32),
            pltpu.VMEM((blocks,) + late_grads[1].shape, half),
            pltpu.VMEM(late_grads[0].shape, late_grads[0].dtype),
            pltpu.VMEM((number,) + late_block, jnp.float32),
            pltpu.VMEM((number,) + late_block, jnp.float32),
            pltpu.VMEM((2,) + late_block, jnp.float32),
            pltpu.VMEM((2, 8, lanes), jnp.float32),
            pltpu.VMEM((number, 2, 8, lanes), jnp.float32),
            pltpu.VMEM((2, 2, 8, lanes), jnp.float32),
            pltpu.VMEM((blocks, in_rows, width), jnp.float32),
            pltpu.VMEM(small_half, jnp.float32),
            pltpu.SemaphoreType.DMA((2, number)),
            pltpu.SemaphoreType.DMA((2, number)),
        ]
        + Reduce.rooms(dims, late_grads, True)
        + Reduce.sems(blocks + 1, dims),
        8 * rows * model * inner,
        (
            seq_lengths,
            tokens,
            grad_low,
            gain_value,
            small,
            flat,
            branch,
            signal,
            slope,
            signal_grad,
            gate_grad,
            flipped,
            branch_whole,
            gate_whole,
            grad_stepw,
            grad_bias,
            grad_decaylog,
            grad_skip,
            jnp.asarray(plain_rows.reshape(small_half)),
            early_squares,
        ),
        collective_id=1,
    )

    names = ("gain", "taps", "shift", "select", "step", "bias", "decay", "skip")
    own = (norm_gain, conv_weight, conv_bias, select_proj, step_proj, step_bias, decay_log, skip_scale)
    in_grad, out_grad, grad_tokens, gain_grad, *small_grads, decay_sq, plain_sq = pl.pallas_call(
        functools.partial(finish_kernel, plan, names, late),
        in_specs=[whole] * 7,
        out_specs=[whole] * (3 + len(names)) + [scalars] * 2,
        out_shape=[shape(in_proj.shape), shape(out_proj.shape), shape(tokens.shape, half)]
        + [shape(array.shape) for array in own]
        + [shape((1, 1))] * 2,
        name="finish",
    )(
        tokens_grad,
        in_branch_sum,
        in_gate_sum,
        out_sum,
        small_sum.reshape(plan["rows"], piece),
        late_sum,
        norms,
    )
    return (
        output,
        grad_tokens,
        gain_grad,
        in_grad,
        *small_grads,
        out_grad,
        decay_sq[0, 0],
        plain_sq[0, 0],
    )


def solution(mesh):
    placed = (
        P(("wide", "narrow"), None),
        P(("wide", "narrow"), None),
        P(("wide", "narrow")),
        P(("wide", "narrow"), None),
        P("narrow"),
        P("narrow", None),
        P(None, "narrow"),
        P("narrow"),
        P(None, "narrow"),
        P(None, "narrow"),
        P("narrow"),
        P(None, "narrow"),
        P("narrow"),
        P("narrow", None),
    )
    return jax.shard_map(
        functools.partial(per_device, grid_of(mesh)),
        mesh=mesh,
        in_specs=placed,
        out_specs=(
            P(("wide", "narrow"), None),
            P(("wide", "narrow"), None),
            P("narrow"),
            P("narrow", None),
            P(None, "narrow"),
            P("narrow"),
            P(None, "narrow"),
            P(None, "narrow"),
            P("narrow"),
            P(None, "narrow"),
            P("narrow"),
            P("narrow", None),
            P(),
            P(),
        ),
        check_vma=False,
    )
```

```python
import functools
import math

import jax
import jax.numpy as jnp
import numpy as np
from jax import lax
from jax.experimental import pallas as pl
from jax.experimental.pallas import tpu as pltpu
from jax.sharding import PartitionSpec as P

epsilon = 1e-05
chunk = 8
lanes = 128
log2e = math.log2(math.e)
ln2 = math.log(2.0)
far = 1e30
tiny = 1e-30


def contract(left, right, left_dim, right_dim):
    return lax.dot_general(
        left, right, (((left_dim,), (right_dim,)), ((), ())), preferred_element_type=jnp.float32
    )


def row_loop(rows, group, body, initial):
    def some(index, carry):
        return body(index, pl.ds(pl.multiple_of(index * group, group), group), carry)

    return lax.fori_loop(0, rows // group, some, initial)


def cut(tile):
    return pl.ds(tile * lanes, lanes)


def sigmoid(values):
    return 0.5 * jnp.tanh(0.5 * values) + 0.5


def softplus(values):
    small = jnp.exp(-jnp.abs(values))
    series = small * (1.0 - small * (0.5 - small * (1.0 / 3.0 - 0.25 * small)))
    return jnp.maximum(values, 0.0) + jnp.where(small < 0.03, series, jnp.log(1.0 + small))


def slope_of(step):
    return 1.0 - jnp.exp(-step)


def fill_offsets(lengths_ref, offset_buf, rows):
    place = lax.broadcasted_iota(jnp.int32, offset_buf.shape, 0)
    start = jnp.zeros(offset_buf.shape, jnp.int32)
    ahead = jnp.int32(0)
    for index in range(lengths_ref.shape[1] - 1):
        ahead = ahead + lengths_ref[0, index]
        start = jnp.where(place >= ahead, ahead, start)
    offset_buf[...] = jnp.where(place < rows, place - start, 0)


def small_rows(small_ref, first, count):
    base = first // 16 * 16
    tall = -(-(first + count - base) // 16) * 16
    return small_ref[base : base + tall, :].astype(jnp.float32)[first - base : first - base + count]


def eight(values):
    total = values[:8]
    for row in range(8, values.shape[0], 8):
        total = total + values[row : row + 8]
    return total


def conv_rows(index, at, group, tile, branch_ref, offset_buf, taps, shift):
    count = taps.shape[0]
    here = slice(tile * lanes, (tile + 1) * lanes)
    current = branch_ref[at, cut(tile)]
    before = branch_ref[pl.ds(pl.multiple_of(jnp.maximum(index * group - 8, 0), 8), 8), cut(tile)]
    both = jnp.concatenate([before, current], axis=0)
    offsets = offset_buf[at, :]
    summed = shift[:, here] + taps[count - 1 : count, here] * current
    for tap in range(count - 1):
        lag = count - 1 - tap
        read = jnp.where(offsets >= lag, pltpu.roll(both, lag, 0)[8:], 0.0)
        summed = summed + taps[tap : tap + 1, here] * read
    return summed


def rows_of(blocks):
    return as_matrix(blocks[...][None])


def as_matrix(blocks):
    columns = blocks.shape[3]
    if blocks.shape[2] % 16:
        return blocks.astype(jnp.float32).reshape(-1, columns).astype(blocks.dtype)
    return blocks.reshape(-1, columns)


def front_kernel(
    plan,
    dims,
    names,
    lengths_ref,
    tokens_ref,
    cotangent_ref,
    mask_ref,
    *refs,
):
    smalls, in_ref, out_ref, refs = refs[: len(names)], refs[len(names)], refs[len(names) + 1], refs[len(names) + 2 :]
    branch_ref, signal_ref, slope_ref, projected_ref, flipped_ref, normed_ref, low_ref = refs[:7]
    write_pair, read_pair, small_out, gain_ref, whole_ref, gate_lines, out_lines = refs[7:14]
    offset_buf, pack_buf, own_small, own_in, own_gate, own_out, land_small, land_in, store_sem = refs[14:23]
    own_gain, land_gain, gain_send, gain_recv = refs[23:27]
    rows = tokens_ref.shape[0]
    width = branch_ref.shape[1]
    block = pl.program_id(0)
    last = whole_ref.shape[0]
    shares = own_out.shape[0]
    gather = Gather(
        dims,
        [own_small] + [own_in.at[index] for index in range(last)],
        [land_small] + [land_in.at[index] for index in range(last)],
        refs[27:30],
    )
    rise = Rise(
        dims,
        [own.at[index] for index in range(shares) for own in (own_gate, own_out)],
        [lines.at[index] for index in range(shares) for lines in (gate_lines, out_lines)],
        refs[30:],
    )
    tall = pack_buf.shape[0] // 2

    def stored(index):
        return pltpu.make_async_copy(land_in.at[index], whole_ref.at[index], store_sem.at[index])

    def move_on(plan_of_moves):
        for moment, legs in plan_of_moves:

            @pl.when(block == moment)
            def _(legs=legs):
                for which, number in legs:
                    gather.leg(which, number)

    @pl.when(block == 0)
    def _():
        pack_buf[...] = jnp.zeros_like(pack_buf)
        for name, ref in zip(names, smalls):
            first, height = plan[name]
            pack_buf[first : first + height, : ref.shape[1]] = ref[...]
        own_gain[...] = jnp.zeros_like(own_gain)
        own_gain[0:1, : gain_ref.shape[1] // land_gain.shape[0]] = smalls[names.index("gain")][...]
        for side in range(2):
            own_small[side] = pack_buf[side * tall : (side + 1) * tall, :].astype(own_small.dtype)
        for index in range(last):
            own_in[index] = in_ref[:, index * width : (index + 1) * width].astype(own_in.dtype)
        place = Place(dims)
        place.greet(everyone=True)
        send_to_all(place, lambda target: own_gain, land_gain, gain_send, gain_recv)
        for index in (1, 0) + tuple(range(2, last + 1)):
            gather.start(index)
        first = last * width
        for index in range(shares):
            each = own_gate.shape[2]
            own_gate[index] = in_ref[:, first + index * each : first + (index + 1) * each].astype(own_gate.dtype)
            each = own_out.shape[2]
            own_out[index] = out_ref[:, index * each : (index + 1) * each].astype(own_out.dtype)
        for index in range(2 * shares):
            rise.start(index)
        fill_offsets(lengths_ref, offset_buf, rows)
        gather.leg(1, 1)
        gather.leg(0, 1)
        wait_for_all(place, own_gain[...], land_gain, gain_send, gain_recv)
        each = gain_ref.shape[1] // land_gain.shape[0]
        for owner in range(land_gain.shape[0]):
            gain_ref[:, owner * each : (owner + 1) * each] = (
                land_gain[owner, 0:1, :each].astype(jnp.bfloat16).astype(jnp.float32)
            )

        def norm(index, at, carry):
            residual = tokens_ref[at, :].astype(jnp.float32)
            scale = lax.rsqrt(jnp.mean(residual * residual, axis=1, keepdims=True) + epsilon)
            normed_ref[at, :] = (residual * scale * gain_ref[...]).astype(normed_ref.dtype)
            return carry

        row_loop(rows, 16, norm, 0)
        gather.leg(1, 2)
        gather.leg(0, 2)
        gather.leg(2, 1)
        flipped_ref[...] = normed_ref[...].T
        gather.leg(1, 3)
        gather.leg(0, 3)
        gather.leg(2, 2)
        down = lax.broadcasted_iota(jnp.int32, (rows, rows), 0)
        along = lax.broadcasted_iota(jnp.int32, (rows, rows), 1)
        diagonal = jnp.where(down == along, mask_ref[...].astype(jnp.float32), 0.0).astype(low_ref.dtype)
        low_ref[...] = jnp.dot(
            diagonal, cotangent_ref[...], preferred_element_type=jnp.float32
        ).astype(low_ref.dtype)
        projected_ref[...] = jnp.zeros_like(projected_ref)

    for index in range(last):

        @pl.when(block == index)
        def _(index=index):
            gather.arrive(index + 1)
            stored(index).start()

    branch_w = as_matrix(land_in[block])
    branch_ref[...] = jnp.dot(normed_ref[...], branch_w, preferred_element_type=jnp.float32)
    move_on(((0, ((3, 1), (2, 3))), (1, ((4, 2), (3, 3))), (2, ((4, 3),))))

    @pl.when(block == 0)
    def _():
        gather.arrive(0)
        share = land_small.shape[4]
        for z in range(land_small.shape[0]):
            for plane in range(land_small.shape[1]):
                owner = z * land_small.shape[1] + plane
                for side in range(2):
                    small_out[side * tall : (side + 1) * tall, owner * share : (owner + 1) * share] = land_small[
                        z, plane, side
                    ]

    small_ref = small_out.at[:, pl.ds(pl.multiple_of(block * width, width), width)]
    taps = small_rows(small_ref, *plan["taps"])
    shift = small_rows(small_ref, *plan["shift"])

    def some(index, at, carry):
        for tile in range(width // lanes):
            summed = conv_rows(index, at, 32, tile, branch_ref, offset_buf, taps, shift)
            sigma = sigmoid(summed)
            active = summed * sigma
            signal_ref[at, cut(tile)] = active.astype(signal_ref.dtype)
            slope_ref[at, cut(tile)] = sigma + active * (1.0 - sigma)
        return carry

    row_loop(rows, 32, some, 0)
    move_on(((0, ((4, 1), (3, 2))),))
    projected_ref[...] += contract(signal_ref[...], small_ref[:lanes, :], 1, 1)

    @pl.when(block == pl.num_programs(0) - 1)
    def _():
        high, low = high_low(projected_ref[...])
        own = own_tokens(rows)
        rank = plan["step"][1]
        size = plan["decay"][1]
        entry = lax.broadcasted_iota(jnp.int32, (lanes, lanes), 0)
        lane = lax.rem(lax.broadcasted_iota(jnp.int32, (lanes, lanes), 1), size)
        for first, pair in ((rank, write_pair), (rank + size, read_pair)):
            spread = (entry == lane + first).astype(jnp.bfloat16)
            parts = [
                (jnp.dot(part.astype(jnp.bfloat16), spread, preferred_element_type=jnp.float32) * own).reshape(
                    rows // chunk, chunk, lanes
                )
                for part in (high, low)
            ]
            pair[...] = jnp.concatenate(parts, axis=1).astype(pair.dtype)
        for index in range(last + 1):
            gather.drain(index)
        for index in range(2 * shares):
            rise.finish(index)
        for index in range(last):
            stored(index).wait()


def high_low(values):
    high = values.astype(jnp.bfloat16).astype(jnp.float32)
    return high, values - high


def own_tokens(rows):
    token = lax.rem(lax.broadcasted_iota(jnp.int32, (rows, lanes), 0), chunk)
    return (token == lax.div(lax.broadcasted_iota(jnp.int32, (rows, lanes), 1), lanes // chunk)).astype(
        jnp.float32
    )


def spread_all(pairs, target):
    some = 8

    def spread(index, carry):
        rows = jnp.concatenate([pairs[index * some + number] for number in range(some)], axis=1)
        wide = contract(rows, jnp.ones((rows.shape[0], lanes), rows.dtype), 0, 0)
        target[pl.ds(index * some * chunk, some * chunk)] = wide.reshape(some * chunk, -1, lanes)
        return carry

    lax.fori_loop(0, pairs.shape[0] // some, spread, 0)


def joined(first, second, hop):
    low = lax.bitwise_and(lax.broadcasted_iota(jnp.int32, first.shape, 0), hop) == 0
    return jnp.where(low, first, second) + pltpu.roll(jnp.where(low, second, first), hop, 0)


def folded(buffer, tile):
    parts = [buffer[tile, pl.ds(row * chunk, chunk), :] for row in range(chunk)]
    hop = 1
    while len(parts) > 1:
        parts = [joined(parts[index], parts[index + 1], hop) for index in range(0, len(parts), 2)]
        hop *= 2
    return parts[0]


def forward_kernel(
    plan,
    dims,
    lengths_ref,
    projected_ref,
    small_ref,
    signal_ref,
    write_pair,
    read_pair,
    gate_lines,
    out_lines,
    states_ref,
    step_ref,
    core_ref,
    begin_ref,
    gate_whole,
    out_whole,
    offset_buf,
    pre_buf,
    decay_step,
    flows,
    write_wide,
    read_wide,
    fold_buf,
    held_buf,
    *sems,
):
    rows, width = pre_buf.shape
    size = plan["decay"][1]
    half_size = size // 2
    tiles = width // lanes
    chunks = rows // chunk
    rank = plan["step"][1]
    group = pl.program_id(1)
    groups = pl.num_programs(1)
    moment = pl.program_id(0) * groups + group
    moments = pl.num_programs(0) * groups
    shares = gate_whole.shape[0]
    count = 2 * shares
    gather = Gather(
        dims,
        [lines.at[index] for index in range(shares) for lines in (gate_lines, out_lines)],
        [whole.at[index] for index in range(shares) for whole in (gate_whole, out_whole)],
        sems,
        [whole.shape[3:] for _ in range(shares) for whole in (gate_whole, out_whole)],
    )

    @pl.when(moment == 0)
    def _():
        Place(dims).greet()
        for which in range(count):
            gather.start(which)
        fill_offsets(lengths_ref, offset_buf, offset_buf.shape[0] - 8)
        spread_all(write_pair, write_wide)
        spread_all(read_pair, read_wide)

    @pl.when(group == 0)
    def _():
        held_buf[...] = jnp.zeros_like(held_buf)

    begin_ref[0] = held_buf[...]
    pre_buf[...] = jnp.dot(
        projected_ref[:, :rank].astype(small_ref.dtype),
        small_ref[pl.ds(plan["step"][0], rank), :],
        preferred_element_type=jnp.float32,
    )
    bias = small_rows(small_ref, *plan["bias"])

    def before(index, at, carry):
        spot = pl.ds(pl.multiple_of(index * 4, 4), 4)
        inside = offset_buf[pl.ds(pl.multiple_of(group * rows + index * 32, 32), 32), :] > 0
        for tile in range(tiles):
            step = softplus(pre_buf[at, cut(tile)] + bias[:, tile * lanes : (tile + 1) * lanes])
            step_ref[spot, :, cut(tile)] = step.reshape(4, chunk, lanes)
            decay_step[spot, :, cut(tile)] = jnp.where(inside, step, far).reshape(4, chunk, lanes)
            flow = step * signal_ref[at, cut(tile)].astype(jnp.float32)
            flows[spot, :, cut(tile)] = flow.reshape(4, chunk, lanes)
        return carry

    row_loop(rows, 4 * chunk, before, 0)
    rates = -jnp.exp(small_rows(small_ref, *plan["decay"])) * log2e
    rates = [rates[:, tile * lanes : (tile + 1) * lanes] for tile in range(tiles)]

    def forward(index, held):
        held = list(held)
        for place in range(chunk):
            now = index * chunk + place
            write_now = write_wide[group * rows + now]
            read_now = read_wide[group * rows + now]
            for tile in range(tiles):
                decay = jnp.exp2(rates[tile] * decay_step[index, pl.ds(place, 1), cut(tile)])
                fresh = decay * held[tile] + write_now * flows[index, pl.ds(place, 1), cut(tile)]
                held[tile] = fresh
                states_ref[now, :, cut(tile)] = fresh
                product = read_now * fresh
                fold_buf[tile, pl.ds(place * chunk, chunk), :] = product[:half_size] + product[half_size:]
        for tile in range(tiles):
            core_ref[index, :, cut(tile)] = folded(fold_buf, tile)
        return tuple(held)

    held = tuple(held_buf[:, cut(tile)] for tile in range(tiles))
    schedule = {}
    for which in range(count):
        for number in (2, 3):
            schedule.setdefault((3, 6, 9, 12)[which] + 3 * (number - 2), []).append((which, number))

    def move_on(legs):
        for which, number in legs:
            gather.leg(which, number)

    for half_loop in range(2):
        for point, legs in sorted(schedule.items()):
            if point < 16 and point % 2 == half_loop:
                pl.when(moment == point // 2)(functools.partial(move_on, legs))
        held = lax.fori_loop(half_loop * chunks // 2, (half_loop + 1) * chunks // 2, forward, held)
    for tile in range(tiles):
        held_buf[:, cut(tile)] = held[tile]

    @pl.when(moment == moments - 1)
    def _():
        for which in range(count):
            gather.arrive(which)
        for which in range(count):
            gather.drain(which)


def middle_kernel(
    plan,
    core_ref,
    small_ref,
    signal_ref,
    gate_w,
    low_ref,
    out_w,
    flipped_ref,
    normed_ref,
    tokens_ref,
    core_grad_ref,
    gate_grad_ref,
    skip_grad_ref,
    out_grad_ref,
    in_grad_ref,
    output_ref,
    pre_buf,
    gate_buf,
    gated_buf,
    out_buf,
    total,
):
    rows, width = pre_buf.shape
    tiles = width // lanes
    block = pl.program_id(0)
    each = out_w.shape[3]
    for index in range(out_w.shape[0]):
        out_buf[:, index * each : (index + 1) * each] = as_matrix(out_w[index][None])
    gate_buf[...] = jnp.dot(normed_ref[...], rows_of(gate_w), preferred_element_type=jnp.float32)
    pre_buf[...] = contract(low_ref[...], out_buf[...], 1, 1)
    skip = small_rows(small_ref, *plan["skip"])

    def after(index, at, carry):
        spot = pl.ds(pl.multiple_of(index * 4, 4), 4)
        sums = []
        for tile in range(tiles):
            signal = signal_ref[at, cut(tile)].astype(jnp.float32)
            core = core_ref[spot, :, cut(tile)].reshape(4 * chunk, lanes)
            core = core + skip[:, tile * lanes : (tile + 1) * lanes] * signal
            gate = gate_buf[at, cut(tile)]
            sigma = sigmoid(gate)
            active = gate * sigma
            gated_buf[at, cut(tile)] = (core * active).astype(gated_buf.dtype)
            grad_gated = pre_buf[at, cut(tile)]
            grad_core = grad_gated * active
            core_grad_ref[spot, :, cut(tile)] = grad_core.reshape(4, chunk, lanes)
            slope = sigma + active * (1.0 - sigma)
            gate_grad_ref[at, cut(tile)] = (grad_gated * core * slope).astype(gate_grad_ref.dtype)
            sums.append(carry[tile] + eight(grad_core * signal))
        return tuple(sums)

    zero_rows = jnp.zeros((8, lanes), jnp.float32)
    skips = row_loop(rows, 4 * chunk, after, (zero_rows,) * tiles)
    for tile in range(tiles):
        skip_grad_ref[:, cut(tile)] = jnp.sum(skips[tile], axis=0, keepdims=True)
    out_grad = contract(gated_buf[...], low_ref[...], 0, 0).astype(out_grad_ref.dtype)
    for index in range(out_w.shape[0]):
        out_grad_ref[index] = out_grad[:, index * each : (index + 1) * each]
    in_grad_ref[...] = jnp.dot(
        flipped_ref[...], gate_grad_ref[...], preferred_element_type=jnp.float32
    ).astype(in_grad_ref.dtype)
    piece = jnp.dot(gated_buf[...], out_buf[...], preferred_element_type=jnp.float32)

    @pl.when(block == 0)
    def _():
        total[...] = piece

    @pl.when(block > 0)
    def _():
        total[...] += piece

    @pl.when(block == pl.num_programs(0) - 1)
    def _():
        output_ref[...] = (tokens_ref[...].astype(jnp.float32) + total[...]).astype(output_ref.dtype)


def backward_kernel(
    plan,
    lengths_ref,
    projected_ref,
    small_ref,
    signal_ref,
    write_pair,
    read_pair,
    step_ref,
    core_grad_ref,
    states_ref,
    begin_ref,
    signal_grad_ref,
    step_w_grad_ref,
    bias_grad_ref,
    decay_grad_ref,
    flat_ref,
    offset_buf,
    decay_step,
    flows,
    write_wide,
    read_wide,
    first_buf,
    second_buf,
    through_buf,
    scaled_buf,
    low_buf,
    incoming_buf,
    rank_buf,
    write_buf,
    read_buf,
):
    rows, width = low_buf.shape
    rank = plan["step"][1]
    size = plan["decay"][1]
    half_size = size // 2
    tiles = width // lanes
    chunks = rows // chunk
    block = pl.program_id(0)
    turn = pl.program_id(1)
    groups = pl.num_programs(1)
    group = groups - 1 - turn
    moment = block * groups + turn
    moments = pl.num_programs(0) * groups
    @pl.when(moment == 0)
    def _():
        fill_offsets(lengths_ref, offset_buf, offset_buf.shape[0] - 8)
        spread_all(write_pair, write_wide)
        spread_all(read_pair, read_wide)
        write_buf[...] = jnp.zeros_like(write_buf)
        read_buf[...] = jnp.zeros_like(read_buf)
        rank_buf[...] = jnp.zeros_like(rank_buf)

    @pl.when(turn == 0)
    def _():
        incoming_buf[...] = jnp.zeros_like(incoming_buf)
        decay_grad_ref[...] = jnp.zeros_like(decay_grad_ref)
        bias_grad_ref[...] = jnp.zeros_like(bias_grad_ref)
        step_w_grad_ref[...] = jnp.zeros_like(step_w_grad_ref)

    def before(index, at, carry):
        spot = pl.ds(pl.multiple_of(index * 4, 4), 4)
        offsets = offset_buf[pl.ds(pl.multiple_of(group * rows + index * 32, 32), 32), :]
        inside = (offsets > 0).reshape(4, chunk, lanes)
        for tile in range(tiles):
            step = step_ref[spot, :, cut(tile)]
            decay_step[spot, :, cut(tile)] = jnp.where(inside, step, far)
            signal = signal_ref[at, cut(tile)].astype(jnp.float32).reshape(4, chunk, lanes)
            flows[spot, :, cut(tile)] = step * signal
        return carry

    row_loop(rows, 4 * chunk, before, 0)
    rates = -jnp.exp(small_rows(small_ref, *plan["decay"])) * log2e
    rates = [rates[:, tile * lanes : (tile + 1) * lanes] for tile in range(tiles)]

    def backward(position, carried):
        index = chunks - 1 - position
        incoming, decay_sums, current = (list(tiles_of) for tiles_of in carried)
        for place in range(chunk - 1, -1, -1):
            now = index * chunk + place
            token = group * rows + now
            write_now = write_wide[token]
            read_now = read_wide[token]
            read_sum = None
            write_sum = None
            for tile in range(tiles):
                grad_now = core_grad_ref[index, pl.ds(place, 1), cut(tile)]
                if place > 0:
                    earlier = states_ref[now - 1, :, cut(tile)]
                else:
                    earlier = jnp.where(
                        index > 0, states_ref[jnp.maximum(now - 1, 0), :, cut(tile)], begin_ref[0, :, cut(tile)]
                    )
                grad_state = incoming[tile] + read_now * grad_now
                through_read = current[tile] * grad_now
                current[tile] = earlier
                through_write = grad_state * flows[index, pl.ds(place, 1), cut(tile)]
                read_sum = through_read if read_sum is None else read_sum + through_read
                write_sum = through_write if write_sum is None else write_sum + through_write
                passed = grad_state * write_now
                first_buf[tile, pl.ds(place * chunk, chunk), :] = passed[:half_size] + passed[half_size:]
                exponent = rates[tile] * decay_step[index, pl.ds(place, 1), cut(tile)]
                leaving = jnp.exp2(exponent) * grad_state
                incoming[tile] = leaving
                weighted = (leaving * earlier) * exponent
                second_buf[tile, pl.ds(place * chunk, chunk), :] = weighted[:half_size] + weighted[half_size:]
                decay_sums[tile] = decay_sums[tile] + weighted
            read_buf[token] += read_sum
            write_buf[token] += write_sum
        for tile in range(tiles):
            through_buf[index, :, cut(tile)] = folded(first_buf, tile)
            scaled_buf[index, :, cut(tile)] = folded(second_buf, tile)
        return (tuple(incoming), tuple(decay_sums), tuple(current))

    incoming = tuple(incoming_buf[:, cut(tile)] for tile in range(tiles))
    nothing = (jnp.zeros((size, lanes), jnp.float32),) * tiles
    current = tuple(states_ref[rows - 1, :, cut(tile)] for tile in range(tiles))
    carried = lax.fori_loop(0, chunks, backward, (incoming, nothing, current))
    incoming, decay_sums, _ = carried
    for tile in range(tiles):
        incoming_buf[:, cut(tile)] = incoming[tile]
        decay_grad_ref[:, cut(tile)] += decay_sums[tile] * ln2
    skip = small_rows(small_ref, *plan["skip"])

    def after(index, at, carry):
        spot = pl.ds(pl.multiple_of(index * 4, 4), 4)
        sums = []
        for tile in range(tiles):
            signal = signal_ref[at, cut(tile)].astype(jnp.float32)
            step = step_ref[spot, :, cut(tile)].reshape(4 * chunk, lanes)
            through = through_buf[spot, :, cut(tile)].reshape(4 * chunk, lanes)
            scaled = scaled_buf[spot, :, cut(tile)].reshape(4 * chunk, lanes)
            core_grad = core_grad_ref[spot, :, cut(tile)].reshape(4 * chunk, lanes)
            grad_pre = (through * signal + ln2 * scaled / jnp.maximum(step, tiny)) * slope_of(step)
            low_buf[at, cut(tile)] = grad_pre.astype(low_buf.dtype)
            signal_grad_ref[at, cut(tile)] = (
                through * step + skip[:, tile * lanes : (tile + 1) * lanes] * core_grad
            )
            sums.append(carry[tile] + eight(grad_pre))
        return tuple(sums)

    zero_rows = jnp.zeros((8, lanes), jnp.float32)
    sums = row_loop(rows, 4 * chunk, after, (zero_rows,) * tiles)
    for tile in range(tiles):
        bias_grad_ref[:, cut(tile)] += jnp.sum(sums[tile], axis=0, keepdims=True)
    step_w_grad_ref[...] += contract(
        projected_ref[:, :rank].astype(low_buf.dtype), low_buf[...], 0, 0
    )
    step_w = small_ref[pl.ds(plan["step"][0], rank), :]
    step_w = jnp.concatenate([step_w, jnp.zeros((lanes - rank, width), step_w.dtype)], axis=0)
    rank_buf[pl.ds(group * chunks, chunks)] += contract(low_buf[...], step_w, 1, 1).reshape(
        chunks, chunk, lanes
    )

    @pl.when(moment == moments - 1)
    def _():
        some = 8
        entry = lax.rem(lax.broadcasted_iota(jnp.int32, (some * chunk * size, lanes), 0), size)
        target = lax.broadcasted_iota(jnp.int32, (some * chunk * size, lanes), 1)
        ones = jnp.ones((lanes, lanes), jnp.bfloat16)

        def lay(index, carry):
            lot = pl.ds(index * some * chunk, some * chunk)
            for number, buffer in enumerate((write_buf, read_buf)):
                high, low = high_low(buffer[lot].reshape(some * chunk * size, lanes))
                summed = jnp.dot(high.astype(jnp.bfloat16), ones, preferred_element_type=jnp.float32)
                summed += jnp.dot(low.astype(jnp.bfloat16), ones, preferred_element_type=jnp.float32)
                summed = jnp.where(target == entry + rank + number * size, summed, 0.0)
                summed = jnp.sum(summed.reshape(some * chunk, size, lanes), axis=1)
                rank_buf[pl.ds(index * some, some)] += summed.reshape(some, chunk, lanes)
            return carry

        lax.fori_loop(0, rank_buf.shape[0] // some, lay, 0)
        flat_ref[...] = rank_buf[...].reshape(flat_ref.shape).astype(flat_ref.dtype)


def back_kernel(
    plan,
    dims,
    lengths_ref,
    tokens_ref,
    low_ref,
    gain_ref,
    small_ref,
    flat_ref,
    branch_ref,
    signal_ref,
    slope_ref,
    signal_grad_ref,
    gate_grad_ref,
    flipped_ref,
    branch_w,
    gate_w,
    step_w_grad_ref,
    bias_grad_ref,
    decay_grad_ref,
    skip_grad_ref,
    plain_ref,
    out_grad_ref,
    gate_grads_ref,
    tokens_grad_ref,
    in_sum_ref,
    out_sum_ref,
    gate_sum_ref,
    small_sum_ref,
    late_sum_ref,
    norm_ref,
    offset_buf,
    conv_buf,
    mixed_buf,
    total,
    in_stage,
    small_stage,
    late_stage,
    late_land,
    late_cores,
    norm_own,
    norm_land,
    norm_cores,
    in_result,
    small_result,
    direct_send,
    direct_recv,
    gate_result,
    out_result,
    *parts,
):
    rows = tokens_ref.shape[0]
    width = branch_ref.shape[1]
    tiles = width // lanes
    block = pl.program_id(0)
    last = in_stage.shape[0]
    count = last + 1
    reduce = Reduce(
        dims,
        [small_stage] + [in_stage.at[index] for index in range(last)],
        parts[: 5 * count],
        parts[5 * count : 5 * count + 7],
        [small_result] + [in_result.at[index] for index in range(last)],
        True,
    )
    parts = parts[5 * count + 7 :]
    early_count = 2 * gate_result.shape[0]
    both = ((gate_grads_ref, gate_result), (out_grad_ref, out_result))
    early = Reduce(
        dims,
        [ref.at[index] for index in range(early_count // 2) for ref, _ in both],
        parts[: 6 * early_count],
        parts[6 * early_count :],
        [result.at[index] for index in range(early_count // 2) for _, result in both],
        False,
    )
    share = small_stage.shape[4]
    half_rows = small_stage.shape[3]
    planes = small_stage.shape[1]
    owners = small_stage.shape[0] * planes

    @pl.when(block == 0)
    def _():
        Place(dims).greet(everyone=True)
        for which in range(early_count):
            early.start(which)
        select_grad = contract(flat_ref[...], signal_ref[...], 0, 0)
        step_first, step_tall = plan["step"]
        filler = jnp.zeros((2 * half_rows - step_first - step_tall, select_grad.shape[1]), jnp.float32)
        pieces = {
            "decay": decay_grad_ref[...],
            "bias": bias_grad_ref[...],
            "skip": skip_grad_ref[...],
            "step": step_w_grad_ref[...],
        }
        first = plan["select"][1]
        rows_now = [select_grad[:first]]
        for name in ("decay", "taps", "shift", "bias", "skip", "gain"):
            tall = plan[name][1]
            rows_now.append(
                pieces[name] if name in pieces else jnp.zeros((tall, select_grad.shape[1]), jnp.float32)
            )
            first += tall
        rows_now.append(jnp.zeros((step_first - first, select_grad.shape[1]), jnp.float32))
        rows_now.append(pieces["step"])
        if filler.shape[0]:
            rows_now.append(filler)
        everything = jnp.concatenate(rows_now, axis=0)
        for owner in range(owners):
            for side in range(2):
                small_stage[owner // planes, owner % planes, side] = everything[
                    side * half_rows : (side + 1) * half_rows, owner * share : (owner + 1) * share
                ].astype(small_stage.dtype)
        reduce.start(0)
        fill_offsets(lengths_ref, offset_buf, rows)

    def move_on(plan_of_moves):
        for moment, legs in plan_of_moves:

            @pl.when(block == moment)
            def _(legs=legs):
                for which, number in legs:
                    if which < 0:
                        early.leg(-1 - which, number)
                    else:
                        reduce.leg(which, number)

    taps = small_rows(small_ref, *plan["taps"])
    taps_count = taps.shape[0]
    zero_rows = jnp.zeros((8, lanes), jnp.float32)

    @pl.when(block < last)
    def _():
        conv_buf[pl.ds(0, rows), :] = signal_grad_ref[...] + jnp.dot(
            flat_ref[...], small_ref[:lanes, :], preferred_element_type=jnp.float32
        )
        conv_buf[pl.ds(rows, 8), :] = jnp.zeros((8, width), jnp.float32)

        def through_conv(index, at, carry):
            sums = []
            for tile in range(tiles):
                grad_conv = conv_buf[at, cut(tile)] * slope_ref[at, cut(tile)]
                conv_buf[at, cut(tile)] = grad_conv
                sums.append(carry[tile] + eight(grad_conv))
            return tuple(sums)

        shift_sums = row_loop(rows, 32, through_conv, (zero_rows,) * tiles)
        move_on(
            (
                (0, ((-1, 1), (0, 1))),
                (1, ((1, 1), (-1, 2), (0, 3))),
                (2, ((2, 1), (-2, 2), (1, 3))),
                (3, ((3, 1), (-3, 2), (2, 3), (-2, 3))),
            )
        )

        def to_branch(index, at, carry):
            longer = pl.ds(pl.multiple_of(index * 32, 32), 40)
            offsets = offset_buf[longer, :]
            result = []
            for tile in range(tiles):
                here = slice(tile * lanes, (tile + 1) * lanes)
                grads = conv_buf[longer, cut(tile)]
                branch = branch_ref[at, cut(tile)]
                summed = taps[taps_count - 1 : taps_count, here] * grads[:32]
                sums = [None] * taps_count
                sums[taps_count - 1] = carry[tile][taps_count - 1] + eight(branch * grads[:32])
                for tap in range(taps_count - 1):
                    lag = taps_count - 1 - tap
                    moved = pltpu.roll(jnp.where(offsets >= lag, grads, 0.0), 40 - lag, 0)[:32]
                    summed = summed + taps[tap : tap + 1, here] * moved
                    sums[tap] = carry[tile][tap] + eight(branch * moved)
                mixed_buf[block, at, cut(tile)] = summed.astype(mixed_buf.dtype)
                result.append(tuple(sums))
            return tuple(result)

        sums = row_loop(rows, 32, to_branch, ((zero_rows,) * taps_count,) * tiles)
        in_grad = jnp.dot(flipped_ref[...], mixed_buf[block], preferred_element_type=jnp.float32)
        in_stage[block] = in_grad.reshape(in_stage.shape[1:]).astype(in_stage.dtype)
        for index in range(last):

            @pl.when(block == index)
            def _(index=index):
                reduce.start(index + 1)

        late = [
            jnp.concatenate(
                [jnp.sum(sums[tile][tap], axis=0, keepdims=True) for tap in range(taps_count)]
                + [jnp.sum(shift_sums[tile], axis=0, keepdims=True)]
                + [jnp.zeros((8 - taps_count - 1, lanes), jnp.float32)],
                axis=0,
            )
            for tile in range(tiles)
        ]
        late = jnp.concatenate(late, axis=1)
        for piece in range(width // share):
            late_stage[block * (width // share) + piece] = late[:, piece * share : (piece + 1) * share]
        move_on(
            (
                (0, ((0, 2), (-2, 1))),
                (1, ((1, 2), (-3, 1))),
                (2, ((2, 2), (-1, 3), (-4, 1))),
                (3, ((3, 2), (-4, 2))),
            )
        )

    @pl.when(block >= last)
    def _():
        grad_normed_piece = contract(mixed_buf[block - last], rows_of(branch_w), 1, 1)
        grad_normed_piece += contract(gate_grad_ref[...], rows_of(gate_w), 1, 1)

        @pl.when(block == last)
        def _():
            total[...] = grad_normed_piece

        @pl.when(block > last)
        def _():
            total[...] += grad_normed_piece

        move_on(((4, ((4, 1), (3, 3))), (5, ((-3, 3),)), (6, ((4, 2), (-4, 3))), (7, ((4, 3),))))

    @pl.when(block == pl.num_programs(0) - 1)
    def _():
        def finish(index, at, carry):
            residual = tokens_ref[at, :].astype(jnp.float32)
            scale = lax.rsqrt(jnp.mean(residual * residual, axis=1, keepdims=True) + epsilon)
            grad_normed = total[at, :]
            weighted = grad_normed * gain_ref[...]
            inner = jnp.mean(weighted * residual, axis=1, keepdims=True)
            grad_y = low_ref[at, :].astype(jnp.float32)
            result = grad_y + (scale * weighted - residual * (scale * scale * scale) * inner)
            tokens_grad_ref[at, :] = result.astype(tokens_grad_ref.dtype)
            return carry + eight(grad_normed * residual * scale)

        gains = row_loop(rows, 16, finish, jnp.zeros((8, total.shape[1]), jnp.float32))
        gains = jnp.sum(gains, axis=0, keepdims=True)
        place = Place(dims)
        each = gains.shape[1] // owners
        for owner in range(owners):
            late_stage[owner, taps_count + 1 : taps_count + 2, :each] = gains[
                :, owner * each : (owner + 1) * each
            ]
        late_sems = direct_send.at[0], direct_recv.at[0]
        norm_sems = direct_send.at[1], direct_recv.at[1]
        send_to_all(place, lambda target: late_stage.at[target], late_land, *late_sems)
        late_sum = sum_of_all(place, late_stage[place.me], late_land, *late_sems)
        late_sum = sum_of_cores(place, late_sum, late_cores, direct_send.at[0, 0], direct_recv.at[0, 0])
        late_sum_ref[...] = late_sum
        kept = folded_squares(late_sum * late_sum) * (1 - place.core).astype(jnp.float32)
        for index in range(early_count):
            kept = kept + early.finish(index)[0]
        more, plain = reduce.finish(0, plain_ref)
        kept = kept + more
        for index in range(1, count):
            kept = kept + reduce.finish(index)[0]
        norm_own[...] = jnp.stack([kept, plain])
        send_to_all(place, lambda target: norm_own, norm_land, *norm_sems)
        norms = sum_of_all(place, norm_own[...], norm_land, *norm_sems)
        norm_ref[...] = sum_of_cores(place, norms, norm_cores, direct_send.at[1, 0], direct_recv.at[1, 0])
        for index in range(count):
            reduce.settle(index)
        for index in range(early_count):
            early.settle(index)
        for index in range(early_count // 2):
            for target, result in ((out_sum_ref, out_result), (gate_sum_ref, gate_result)):
                each = result.shape[2]
                target[:, index * each : (index + 1) * each] = result[index]
        for index in range(last):
            in_sum_ref[:, index * width : (index + 1) * width] = in_result[index]
        small_sum_ref[...] = small_result[...]


def finish_kernel(
    plan, names, late, tokens_ref, branch_ref, gate_ref, out_ref, small_ref, late_ref, norm_ref, *outs
):
    middle = branch_ref.shape[1]
    outs[0][:, :middle] = branch_ref[...]
    outs[0][:, middle:] = gate_ref[...]
    outs[1][...] = out_ref[...]
    outs[2][...] = tokens_ref[...]
    for name, target in zip(names, outs[3 : 3 + len(names)]):
        source, (first, count) = (late_ref, late[name]) if name in late else (small_ref, plan[name])
        if len(target.shape) == 1:
            target[...] = source[first, : target.shape[0]]
        else:
            target[...] = source[first : first + count, :]
    for index in range(2):
        outs[3 + len(names) + index][0, 0] = jnp.sum(norm_ref[index])


def shape(dims, kind=jnp.float32):
    return jax.ShapeDtypeStruct(dims, kind)


def compute_call(
    kernel, name, blocks, in_specs, out_specs, out_shape, scratch, flops, operands, collective_id=None, room=62.0
):
    return pl.pallas_call(
        kernel,
        grid=blocks if isinstance(blocks, tuple) else (blocks,),
        in_specs=in_specs,
        out_specs=out_specs,
        out_shape=out_shape,
        scratch_shapes=scratch,
        compiler_params=pltpu.CompilerParams(
            dimension_semantics=("arbitrary",) * (len(blocks) if isinstance(blocks, tuple) else 1),
            vmem_limit_bytes=int(room * 1024 * 1024),
            collective_id=collective_id,
            has_side_effects=collective_id is not None,
        ),
        cost_estimate=pl.CostEstimate(flops=flops, bytes_accessed=40 << 20, transcendentals=0),
        name=name,
    )(*operands)


class Place:
    def __init__(self, dims, swapped=False):
        depth, tall, wide = dims
        self.dims = dims
        self.core = lax.axis_index("wide")
        self.me = lax.axis_index("narrow")
        self.across = lax.rem(self.me, wide)
        self.up = lax.rem(lax.div(self.me, wide), tall)
        self.deep = lax.div(self.me, wide * tall)
        side = 1 - self.core if swapped else self.core
        turn = side if tall == wide else 0
        self.second = (1 + turn * (wide - 1), self.across + turn * (self.up - self.across), wide)
        self.third = (wide - turn * (wide - 1), self.up + turn * (self.across - self.up), tall)
        self.spans = (depth, wide, tall)
        self.other = {"wide": 1 - self.core}

    def level(self, d):
        return lax.rem(self.deep + d, self.spans[0])

    def plane(self, e, f):
        return (
            lax.rem(self.second[1] + e, self.second[2]) * self.second[0]
            + lax.rem(self.third[1] + f, self.third[2]) * self.third[0]
        )

    def plane_behind(self, e, f):
        return self.plane((self.spans[1] - e) % self.spans[1], (self.spans[2] - f) % self.spans[2])

    def at(self, d, e, f):
        return {"narrow": self.level(d) * (self.dims[1] * self.dims[2]) + self.plane(e, f)}

    def greet(self, everyone=False):
        barrier = pltpu.get_barrier_semaphore()
        peers = [self.other]
        if everyone:
            number = self.spans[0] * self.spans[1] * self.spans[2]
            peers += [{"narrow": lax.rem(self.me + hop, number)} for hop in range(1, number)]
        else:
            for axis, size in enumerate(self.spans):
                for hop in range(1, size):
                    move = [0, 0, 0]
                    move[axis] = hop
                    peers.append(self.at(*move))
        for peer in peers:
            pl.semaphore_signal(barrier, inc=1, device_id=peer, device_id_type=pl.DeviceIdType.MESH)
        pl.semaphore_wait(barrier, len(peers))


def by_rows(block):
    return block[0] % 32 == 0


def half_shape(block):
    if len(block) == 3:
        return tuple(block[1:])
    return (block[0] // 2, block[1]) if by_rows(block) else (block[0], block[1] // 2)


def half(view, block, side, lead=0):
    ahead = (slice(None),) * lead
    if len(block) == 3:
        return view.at[ahead + (side,)]
    if by_rows(block):
        return view.at[ahead + (pl.ds(pl.multiple_of(side * (block[0] // 2), 16), block[0] // 2),)]
    columns = pl.ds(pl.multiple_of(side * (block[1] // 2), lanes), block[1] // 2)
    return view.at[ahead + (slice(None), columns)]


def remote(source, target, send_sem, recv_sem, device):
    return pltpu.make_async_remote_copy(
        src_ref=source,
        dst_ref=target,
        send_sem=send_sem,
        recv_sem=recv_sem,
        device_id=device,
        device_id_type=pl.DeviceIdType.MESH,
    )


class Gather:
    def __init__(self, dims, own, whole, sems, blocks=None):
        self.dims, self.own, self.whole = dims, own, whole
        self.local_sem, self.send_sem, self.recv_sem = sems
        self.lined = blocks is not None
        self.blocks = blocks or [block.shape for block in own]

    @staticmethod
    def sems(count, dims):
        copies = dims[0] + 2 * dims[1] * dims[2]
        return [pltpu.SemaphoreType.DMA((count,))] + [pltpu.SemaphoreType.DMA((count, copies))] * 2

    def line(self, which, plane, side):
        return half(self.whole[which].at[:, plane], self.blocks[which], side, 1)

    def local(self, place, which):
        block = self.blocks[which]
        if self.lined:
            return pltpu.make_async_copy(
                self.own[which], self.line(which, place.plane(0, 0), place.core), self.local_sem.at[which]
            )
        return pltpu.make_async_copy(
            half(self.own[which], block, place.core),
            half(self.whole[which].at[place.deep, place.plane(0, 0)], block, place.core),
            self.local_sem.at[which],
        )

    def copy(self, which, source, target, index, device):
        return remote(
            source, target, self.send_sem.at[which, index], self.recv_sem.at[which, index], device
        )

    def rise(self, place, which, hop):
        block = self.blocks[which]
        return self.copy(
            which,
            half(self.own[which], block, place.core),
            half(self.whole[which].at[place.deep, place.plane(0, 0)], block, place.core),
            hop,
            place.at(hop, 0, 0),
        )

    def leg_index(self, e, f):
        return self.dims[0] + e * self.dims[1] + f

    def hand_index(self, e, f):
        return self.leg_index(e, f) + self.dims[1] * self.dims[2]

    def onward(self, place, which, e, f):
        line = self.line(which, place.plane_behind(e, f), place.core)
        source = self.own[which] if self.lined and e == 0 and f == 0 else line
        if f == 0:
            for hop in range(1, place.spans[2]):
                self.copy(which, source, line, self.leg_index(e, hop), place.at(0, 0, hop)).start()
        if f == 0 and e == 0:
            for hop in range(1, place.spans[1]):
                self.copy(which, source, line, self.leg_index(hop, 0), place.at(0, hop, 0)).start()
        self.copy(which, source, line, self.hand_index(e, f), place.other).start()

    def start(self, which):
        place = Place(self.dims)
        if self.lined:
            self.onward(place, which, 0, 0)
            self.local(place, which).start()
            return
        for hop in range(1, place.spans[0]):
            self.rise(place, which, hop).start()
        self.local(place, which).start()

    def leg(self, which, number):
        place = Place(self.dims)
        if number == 1:
            self.local(place, which).wait()
            for hop in range(1, place.spans[0]):
                self.rise(place, which, hop).wait_recv()
            self.onward(place, which, 0, 0)
            return
        for e in range(place.spans[1]):
            for f in range(place.spans[2]):
                if (number == 2 and f == 0 and e > 0) or (number == 3 and f > 0):
                    line = self.line(which, place.plane_behind(e, f), place.core)
                    self.copy(which, line, line, self.leg_index(e, f), place.other).wait_recv()
                    self.onward(place, which, e, f)

    def arrive(self, which):
        place, mirror = Place(self.dims), Place(self.dims, swapped=True)
        for e in range(place.spans[1]):
            for f in range(place.spans[2]):
                line = self.line(which, mirror.plane_behind(e, f), 1 - place.core)
                self.copy(which, line, line, self.hand_index(e, f), place.other).wait_recv()

    def drain(self, which):
        place = Place(self.dims)
        if self.lined:
            self.local(place, which).wait()
        else:
            for hop in range(1, place.spans[0]):
                self.rise(place, which, hop).wait_send()
        for e in range(place.spans[1]):
            for f in range(place.spans[2]):
                line = self.line(which, place.plane_behind(e, f), place.core)
                if e > 0 or f > 0:
                    self.copy(which, line, line, self.leg_index(e, f), place.other).wait_send()
                self.copy(which, line, line, self.hand_index(e, f), place.other).wait_send()


class Rise:
    def __init__(self, dims, own, lines, sems):
        self.dims, self.own, self.lines = dims, own, lines
        self.local_sem, self.send_sem, self.recv_sem = sems

    @staticmethod
    def sems(count, dims):
        return [pltpu.SemaphoreType.DMA((count,))] + [pltpu.SemaphoreType.DMA((count, dims[0]))] * 2

    def copies(self, place, which):
        source = half(self.own[which], self.own[which].shape, place.core)
        target = self.lines[which].at[place.deep]
        local = pltpu.make_async_copy(source, target, self.local_sem.at[which])
        return local, [
            remote(
                source, target, self.send_sem.at[which, hop], self.recv_sem.at[which, hop], place.at(hop, 0, 0)
            )
            for hop in range(1, place.spans[0])
        ]

    def start(self, which):
        local, sends = self.copies(Place(self.dims), which)
        for copy in [*sends, local]:
            copy.start()

    def finish(self, which):
        local, sends = self.copies(Place(self.dims), which)
        local.wait()
        for copy in sends:
            copy.wait_recv()
            copy.wait_send()


class Reduce:
    def __init__(self, dims, grads, rooms, sems, results, resident):
        self.dims, self.grads, self.resident = dims, grads, resident
        count = len(grads)
        self.mine, self.swapped, self.third, self.second, self.first = (
            rooms[index * count : (index + 1) * count] for index in range(5)
        )
        self.loaded = None if resident else rooms[5 * count :]
        self.load_sem, self.swap_send, self.swap_recv, self.send_sem, self.recv_sem = sems[:5]
        self.last_send, self.last_recv = sems[5:]
        self.results = results

    @staticmethod
    def rooms(dims, grads, resident):
        depth, tall, wide = dims
        leads = (
            (tall, wide, depth),
            (depth, tall * wide),
            (tall - 1, wide, depth),
            (wide - 1, depth),
            (depth - 1,),
        )
        if not resident:
            leads += ((depth, tall * wide),)
        return [
            pltpu.VMEM(lead + half_shape(grad.shape[2:]), grad.dtype) for lead in leads for grad in grads
        ]

    @staticmethod
    def sems(count, dims):
        return (
            [pltpu.SemaphoreType.DMA((count,))] * 3
            + [pltpu.SemaphoreType.DMA((count, dims[0] + dims[1] + dims[2]))] * 2
            + [pltpu.SemaphoreType.DMA((count,))] * 2
        )

    def block(self, which):
        return self.grads[which].shape[2:]

    def load(self, place, which):
        return pltpu.make_async_copy(
            half(self.grads[which], self.block(which), place.core, 2),
            self.loaded[which],
            self.load_sem.at[which],
        )

    def swap(self, place, which):
        return remote(
            half(self.grads[which], self.block(which), 1 - place.core, 2),
            self.swapped[which],
            self.swap_send.at[which],
            self.swap_recv.at[which],
            place.other,
        )

    def hop(self, which, source, target, index, device):
        return remote(
            source, target, self.send_sem.at[which, index], self.recv_sem.at[which, index], device
        )

    def third_hop(self, place, which, f):
        return self.hop(which, self.mine[which].at[f], self.third[which].at[f - 1], f, place.at(0, 0, f))

    def second_hop(self, place, which, e):
        return self.hop(
            which,
            self.mine[which].at[0, e],
            self.second[which].at[e - 1],
            self.dims[1] + e,
            place.at(0, e, 0),
        )

    def first_hop(self, place, which, d):
        return self.hop(
            which,
            self.mine[which].at[0, 0, place.level(d)],
            self.first[which].at[d - 1],
            self.dims[1] + self.dims[2] + d,
            place.at(d, 0, 0),
        )

    def start(self, which):
        place = Place(self.dims)
        self.swap(place, which).start()
        if not self.resident:
            self.load(place, which).start()

    def parts(self, place, which, e, f, z):
        plane = place.plane(e, f)
        if self.resident:
            found = [half(self.grads[which].at[z, plane], self.block(which), place.core)]
        else:
            found = [self.loaded[which].at[z, plane]]
        found.append(self.swapped[which].at[z, plane])
        if f == 0:
            found += [self.third[which].at[hop - 1, e, z] for hop in range(1, place.spans[2])]
        if f == 0 and e == 0:
            found += [self.second[which].at[hop - 1, z] for hop in range(1, place.spans[1])]
        return found

    def ready(self, place, which):
        if not self.resident:
            self.load(place, which).wait()
        self.swap(place, which).wait_recv()

    def added(self, parts, store, carry):
        rows = parts[0].shape[0]
        group = min(rows, 16)

        def some(index, carry):
            at_rows = pl.ds(pl.multiple_of(index * group, group), group)
            total = parts[0][at_rows, :].astype(jnp.float32)
            for part in parts[1:]:
                total = total + part[at_rows, :].astype(jnp.float32)
            return store(at_rows, total, carry)

        return lax.fori_loop(0, rows // group, some, carry)

    def sum_into(self, place, which, e, f, z):
        target = self.mine[which].at[f, e, z]

        def keep(at_rows, total, carry):
            target[at_rows, :] = total.astype(target.dtype)
            return carry

        self.added(self.parts(place, which, e, f, z), keep, 0)

    def leg(self, which, number):
        place = Place(self.dims)
        depth, span_e, span_f = place.spans
        if number == 1:
            self.ready(place, which)
            for f in range(span_f - 1, 0, -1):
                for e in range(span_e - 1, -1, -1):
                    for z in range(depth):
                        self.sum_into(place, which, e, f, z)
                self.third_hop(place, which, f).start()
        elif number == 2:
            for f in range(1, span_f):
                self.third_hop(place, which, f).wait_recv()
            for e in range(span_e - 1, 0, -1):
                for z in range(depth):
                    self.sum_into(place, which, e, 0, z)
                self.second_hop(place, which, e).start()
        else:
            if span_e == 1:
                for f in range(1, span_f):
                    self.third_hop(place, which, f).wait_recv()
            for e in range(1, span_e):
                self.second_hop(place, which, e).wait_recv()
            for d in range(1, depth):
                self.sum_into(place, which, 0, 0, place.level(d))
                self.first_hop(place, which, d).start()

    def result(self, which, side):
        return half(self.results[which], self.block(which), side)

    def last(self, place, which, side):
        share = self.result(which, side)
        return remote(share, share, self.last_send.at[which], self.last_recv.at[which], place.other)

    def finish(self, which, marks=None):
        place = Place(self.dims)
        parts = self.parts(place, which, 0, 0, place.deep)
        for d in range(1, place.spans[0]):
            self.first_hop(place, which, d).wait_recv()
            parts.append(self.first[which].at[d - 1])
        share = self.result(which, place.core)

        def store(at_rows, total, carry):
            share[at_rows, :] = total
            kept, plain = carry
            squared = total * total
            if marks is not None:
                marked = squared * marks[place.core, at_rows, :]
                plain = plain + folded_squares(marked)
                squared = squared - marked
            return (kept + folded_squares(squared), plain)

        squares = self.added(parts, store, (jnp.zeros((8, lanes), jnp.float32),) * 2)
        self.last(place, which, place.core).start()
        return squares

    def settle(self, which):
        place = Place(self.dims)
        last = self.last(place, which, 1 - place.core)
        last.wait_recv()
        last.wait_send()
        self.swap(place, which).wait_send()
        for f in range(1, place.spans[2]):
            self.third_hop(place, which, f).wait_send()
        for e in range(1, place.spans[1]):
            self.second_hop(place, which, e).wait_send()
        for d in range(1, place.spans[0]):
            self.first_hop(place, which, d).wait_send()


def folded_squares(values):
    total = None
    if values.shape[1] < lanes:
        first = lax.broadcasted_iota(jnp.int32, (values.shape[0], lanes), 1) == 0
        values = jnp.where(first, jnp.sum(values, axis=1, keepdims=True), 0.0)
    for row in range(0, values.shape[0], 8):
        for column in range(0, values.shape[1], lanes):
            piece = values[row : row + 8, column : column + lanes]
            total = piece if total is None else total + piece
    return total


def send_to_all(place, source, landing, send_sem, recv_sem):
    number = landing.shape[0]
    for hop in range(1, number):
        target = lax.rem(place.me + hop, number)
        remote(
            source(target), landing.at[place.me], send_sem.at[hop], recv_sem.at[hop], {"narrow": target}
        ).start()


def wait_for_all(place, own, landing, send_sem, recv_sem):
    number = landing.shape[0]
    landing[place.me] = own
    for hop in range(1, number):
        came = landing.at[lax.rem(place.me + number - hop, number)]
        copy = remote(came, came, send_sem.at[hop], recv_sem.at[hop], place.other)
        copy.wait_recv()
        copy.wait_send()


def sum_of_all(place, own, landing, send_sem, recv_sem):
    number = landing.shape[0]
    wait_for_all(place, own, landing, send_sem, recv_sem)
    total = landing[0]
    for spot in range(1, number):
        total = total + landing[spot]
    return total


def sum_of_cores(place, own, landing, send_sem, recv_sem):
    landing[place.core] = own
    copy = remote(landing.at[place.core], landing.at[place.core], send_sem, recv_sem, place.other)
    copy.start()
    copy.wait()
    return landing[0] + landing[1]


def grid_of(mesh):
    number = mesh.shape["narrow"]
    places = [getattr(device, "coords", None) for device in mesh.devices[0]]
    if all(place is not None for place in places):
        sizes = [len({place[axis] for place in places}) for axis in (2, 1, 0)]
        if sizes[0] * sizes[1] * sizes[2] == number:
            return tuple(sizes)
    side = round((number / 2) ** (1 / 3))
    return (2 * side, side, side) if 2 * side**3 == number else (number, 1, 1)


def plan_of(select_rows, state_size, tap_count, step_rows):
    plan, first = {}, 0
    for name, tall in (
        ("select", select_rows),
        ("decay", state_size),
        ("taps", tap_count),
        ("shift", 1),
        ("bias", 1),
        ("skip", 1),
        ("gain", 1),
    ):
        plan[name] = (first, tall)
        first += tall
    plan["step"] = (lanes, step_rows)
    plan["rows"] = -(-(lanes + step_rows) // 32) * 32
    return plan


def per_device(
    dims,
    tokens,
    cotangent,
    loss_mask,
    seq_lengths,
    norm_gain,
    in_proj,
    conv_weight,
    conv_bias,
    select_proj,
    step_proj,
    step_bias,
    decay_log,
    skip_scale,
    out_proj,
):
    half = jnp.bfloat16
    piece = skip_scale.shape[0]
    gain_piece = norm_gain.shape[0]
    rank, size = step_proj.shape[0], decay_log.shape[0]
    plan = plan_of(select_proj.shape[0], size, conv_weight.shape[0], rank)
    smalls = {
        "select": select_proj,
        "decay": decay_log,
        "taps": conv_weight,
        "shift": conv_bias[None],
        "bias": step_bias[None],
        "skip": skip_scale[None],
        "gain": norm_gain[None],
        "step": step_proj,
    }
    depth, planes = dims[0], dims[1] * dims[2]
    number = depth * planes
    in_rows = in_proj.shape[0]
    rows, model = tokens.shape
    inner = piece * number
    width = 4 * lanes
    blocks = inner // width
    chunks = rows // chunk
    mask_row = loss_mask[None]

    whole = pl.BlockSpec(memory_space=pltpu.VMEM)
    tall = pl.BlockSpec((rows, width), lambda b: (0, b))
    deep = pl.BlockSpec((chunks, chunk, width), lambda b: (0, 0, b))
    lead = pl.BlockSpec((rows, size, width), lambda b: (0, 0, b))
    first_w = pl.BlockSpec((model, width), lambda b: (0, b))
    second_w = pl.BlockSpec((model, width), lambda b: (0, b + blocks))
    out_w = pl.BlockSpec((width, model), lambda b: (b, 0))

    def thin(height):
        return pl.BlockSpec((height, width), lambda b: (0, b))

    def fixed(*dims_of):
        return pl.BlockSpec(dims_of, lambda b: (0,) * len(dims_of))

    scalars = pl.BlockSpec(memory_space=pltpu.SMEM)
    offset_buf = pltpu.VMEM((rows + 8, lanes), jnp.int32)
    packed = thin(plan["rows"])

    pair = (chunks, 2 * chunk, lanes)
    pair = (chunks, 2 * chunk, lanes)
    anywhere = pl.BlockSpec(memory_space=pl.ANY)
    small_half = (2, plan["rows"] // 2, piece)
    in_piece = (in_rows, width)
    shares = 2
    in_share = (in_rows, inner // shares)
    out_share = (out_proj.shape[0], model // shares)
    lines = [shape((shares, depth) + half_shape(block), half) for block in (in_share, out_share)]
    (
        branch,
        signal,
        slope,
        projected,
        flipped,
        normed,
        grad_low,
        write_pair,
        read_pair,
        small,
        gain_value,
        in_blocks,
        gate_lines,
        out_lines,
    ) = compute_call(
        functools.partial(front_kernel, plan, dims, tuple(smalls)),
        "front",
        blocks,
        [scalars, whole, whole, whole] + [whole] * len(smalls) + [whole] * 2,
        [tall, tall, tall] + [whole] * 8 + [anywhere] * 3,
        [
            shape((rows, inner)),
            shape((rows, inner), half),
            shape((rows, inner)),
            shape((rows, lanes)),
            shape((model, rows), half),
            shape((rows, model), half),
            shape((rows, model), half),
            shape(pair, half),
            shape(pair, half),
            shape((plan["rows"], inner), half),
            shape((1, model)),
            shape((blocks, depth, planes) + in_piece, half),
            *lines,
        ],
        [
            offset_buf,
            pltpu.VMEM((plan["rows"], piece), jnp.float32),
            pltpu.VMEM(small_half, half),
            pltpu.VMEM((blocks,) + in_piece, half),
            pltpu.VMEM((shares,) + in_share, half),
            pltpu.VMEM((shares,) + out_share, half),
            pltpu.VMEM((depth, planes) + small_half, half),
            pltpu.VMEM((blocks, depth, planes) + in_piece, half),
            pltpu.SemaphoreType.DMA((blocks,)),
            pltpu.VMEM((8, piece), jnp.float32),
            pltpu.VMEM((number, 8, piece), jnp.float32),
            pltpu.SemaphoreType.DMA((number,)),
            pltpu.SemaphoreType.DMA((number,)),
        ]
        + Gather.sems(1 + blocks, dims)
        + Rise.sems(2 * shares, dims),
        4 * rows * model * inner,
        (seq_lengths, tokens, cotangent, mask_row, *smalls.values(), in_proj, out_proj),
        collective_id=0,
    )
    groups = 2
    part, pieces = rows // groups, chunks // groups
    row_block = pltpu.VMEM((pieces, chunk, width), jnp.float32)
    spread_block = pltpu.VMEM((rows, size, lanes), jnp.float32)
    fold_block = pltpu.VMEM((width // lanes, chunk * chunk, lanes), jnp.float32)

    def by_group(order, *dims_of):
        middle = (0,) * (len(dims_of) - 2)
        return pl.BlockSpec(dims_of, lambda b, g: (order(g),) + middle + (b,))

    def by_token(order, *dims_of):
        return pl.BlockSpec(dims_of, lambda b, g: (order(g),) + (0,) * (len(dims_of) - 1))

    def by_channel(height):
        return pl.BlockSpec((height, width), lambda b, g: (0, b))

    def onward(g):
        return g

    def backward(g):
        return groups - 1 - g

    states, step, core, begins, gate_blocks, out_blocks = compute_call(
        functools.partial(forward_kernel, plan, dims),
        "forward",
        (blocks, groups),
        [
            scalars,
            by_token(onward, part, lanes),
            by_channel(plan["rows"]),
            by_group(onward, part, width),
            whole,
            whole,
            anywhere,
            anywhere,
        ],
        [
            by_group(onward, part, size, width),
            by_group(onward, pieces, chunk, width),
            by_group(onward, pieces, chunk, width),
            by_group(onward, 1, size, width),
            anywhere,
            anywhere,
        ],
        [
            shape((rows, size, inner)),
            shape((chunks, chunk, inner)),
            shape((chunks, chunk, inner)),
            shape((groups, size, inner)),
            shape((shares, depth, planes) + in_share, half),
            shape((shares, depth, planes) + out_share, half),
        ],
        [
            offset_buf,
            pltpu.VMEM((part, width), jnp.float32),
            row_block,
            row_block,
            spread_block,
            spread_block,
            fold_block,
            pltpu.VMEM((size, width), jnp.float32),
        ]
        + Gather.sems(2 * shares, dims),
        15 * rows * inner * size,
        (seq_lengths, projected, small, signal, write_pair, read_pair, gate_lines, out_lines),
        collective_id=2,
    )
    split = in_share[1] // width
    weights = pl.BlockSpec((None, number, in_rows, width), lambda b: (b // split, 0, 0, b % split))
    per_block = width // out_share[0]
    out_pieces = pl.BlockSpec((shares, per_block) + out_share, lambda b: (0, b, 0, 0))
    branch_whole = in_blocks.reshape(blocks, number, *in_piece)
    gate_whole = gate_blocks.reshape(shares, number, *in_share)
    out_whole = out_blocks.reshape(shares, number, *out_share)
    core_grad, gate_grad, grad_skip, grad_outw, grad_in_gate, output = compute_call(
        functools.partial(middle_kernel, plan),
        "middle",
        blocks,
        [deep, packed, tall, weights, whole, out_pieces, whole, whole, whole],
        [
            deep,
            tall,
            thin(1),
            pl.BlockSpec((shares, width, out_share[1]), lambda b: (0, b, 0)),
            pl.BlockSpec((None, model, width), lambda b: (b // split, 0, b % split)),
            fixed(rows, model),
        ],
        [
            shape((chunks, chunk, inner)),
            shape((rows, inner), half),
            shape((1, inner)),
            shape((shares, inner, out_share[1]), half),
            shape((shares, model, in_share[1]), half),
            shape((rows, model), half),
        ],
        [
            pltpu.VMEM((rows, width), jnp.float32),
            pltpu.VMEM((rows, width), jnp.float32),
            pltpu.VMEM((rows, width), half),
            pltpu.VMEM((width, model), half),
            pltpu.VMEM((rows, model), jnp.float32),
        ],
        8 * rows * model * inner,
        (core, small, signal, gate_whole, grad_low, out_whole, flipped, normed, tokens),
    )
    early_grads = [
        grad_outw.reshape((shares, depth, planes) + out_share),
        grad_in_gate.reshape((shares, depth, planes) + in_share),
    ]
    early_sums = [shape(out_proj.shape), shape((in_rows, inner))]
    early_pieces = [shape((depth, planes) + block, half) for block in (in_share, out_share)] * shares
    (
        signal_grad,
        grad_stepw,
        grad_bias,
        grad_decaylog,
        flat,
    ) = compute_call(
        functools.partial(backward_kernel, plan),
        "backward",
        (blocks, groups),
        [
            scalars,
            by_token(backward, part, lanes),
            by_channel(plan["rows"]),
            by_group(backward, part, width),
            whole,
            whole,
            by_group(backward, pieces, chunk, width),
            by_group(backward, pieces, chunk, width),
            by_group(backward, part, size, width),
            by_group(backward, 1, size, width),
        ],
        [
            by_group(backward, part, width),
            by_channel(rank),
            by_channel(1),
            by_channel(size),
            whole,
        ],
        [
            shape((rows, inner)),
            shape((rank, inner)),
            shape((1, inner)),
            shape((size, inner)),
            shape((rows, lanes), half),
        ],
        [
            offset_buf,
            row_block,
            row_block,
            spread_block,
            spread_block,
            fold_block,
            fold_block,
            row_block,
            row_block,
            pltpu.VMEM((part, width), half),
            pltpu.VMEM((size, width), jnp.float32),
            pltpu.VMEM((chunks, chunk, lanes), jnp.float32),
            spread_block,
            spread_block,
        ],
        40 * rows * inner * size,
        (
            seq_lengths,
            projected,
            small,
            signal,
            write_pair,
            read_pair,
            step,
            core_grad,
            states,
            begins,
        ),
    )

    plain_rows = np.zeros((plan["rows"], piece), np.float32)
    for name in ("bias", "decay", "skip"):
        first, count = plan[name]
        plain_rows[first : first + count] = 1.0
    late_grads = [shape((depth, planes) + small_half, half)]
    late_grads += [shape((depth, planes, in_rows, width), half)] * blocks
    taps_n = conv_weight.shape[0]
    late = {"taps": (0, taps_n), "shift": (taps_n, 1), "gain": (taps_n + 1, 1)}
    late_block = (8, piece)

    mode = {} if piece >= lanes else {"pipeline_mode": pl.Buffered(1)}
    early_tall = pl.BlockSpec((rows, width), lambda b: (0, jnp.minimum(b, blocks - 1)), **mode)
    late_tall = pl.BlockSpec((rows, width), lambda b: (0, jnp.maximum(b - blocks, 0)), **mode)
    tokens_grad, in_branch_sum, out_sum, in_gate_sum, small_sum, late_sum, norms = compute_call(
        functools.partial(back_kernel, plan, dims),
        "back",
        2 * blocks,
        [scalars, whole, whole, whole]
        + [pl.BlockSpec((plan["rows"], width), lambda b: (0, jnp.minimum(b, blocks - 1))), whole]
        + [early_tall, whole, early_tall, early_tall, late_tall, whole]
        + [
            pl.BlockSpec(
                (None, number, in_rows, width), lambda b: (jnp.maximum(b - blocks, 0), 0, 0, 0), **mode
            ),
            pl.BlockSpec(
                (None, number, in_rows, width),
                lambda b: (jnp.maximum(b - blocks, 0) // split, 0, 0, jnp.maximum(b - blocks, 0) % split),
                **mode,
            ),
        ]
        + [whole] * 5
        + [anywhere] * 2,
        [whole] * 7,
        [
            shape((rows, model), half),
            shape((in_rows, inner)),
            *early_sums,
            shape(small_half),
            shape(late_block),
            shape((2, 8, lanes)),
        ],
        [
            offset_buf,
            pltpu.VMEM((rows + 8, width), jnp.float32),
            pltpu.VMEM((blocks, rows, width), half),
            pltpu.VMEM((rows, model), jnp.float32),
            pltpu.VMEM((blocks,) + late_grads[1].shape, half),
            pltpu.VMEM(late_grads[0].shape, late_grads[0].dtype),
            pltpu.VMEM((number,) + late_block, jnp.float32),
            pltpu.VMEM((number,) + late_block, jnp.float32),
            pltpu.VMEM((2,) + late_block, jnp.float32),
            pltpu.VMEM((2, 8, lanes), jnp.float32),
            pltpu.VMEM((number, 2, 8, lanes), jnp.float32),
            pltpu.VMEM((2, 2, 8, lanes), jnp.float32),
            pltpu.VMEM((blocks, in_rows, width), jnp.float32),
            pltpu.VMEM(small_half, jnp.float32),
            pltpu.SemaphoreType.DMA((2, number)),
            pltpu.SemaphoreType.DMA((2, number)),
        ]
        + [pltpu.VMEM((shares,) + block, jnp.float32) for block in (in_share, out_share)]
        + Reduce.rooms(dims, late_grads, True)
        + Reduce.sems(blocks + 1, dims)
        + Reduce.rooms(dims, early_pieces, False)
        + Reduce.sems(2 * shares, dims),
        8 * rows * model * inner,
        (
            seq_lengths,
            tokens,
            grad_low,
            gain_value,
            small,
            flat,
            branch,
            signal,
            slope,
            signal_grad,
            gate_grad,
            flipped,
            branch_whole,
            gate_whole,
            grad_stepw,
            grad_bias,
            grad_decaylog,
            grad_skip,
            jnp.asarray(plain_rows.reshape(small_half)),
            *early_grads,
        ),
        collective_id=1,
        room=62.0 if piece >= lanes else 63.75,
    )

    names = ("gain", "taps", "shift", "select", "step", "bias", "decay", "skip")
    own = (norm_gain, conv_weight, conv_bias, select_proj, step_proj, step_bias, decay_log, skip_scale)
    in_grad, out_grad, grad_tokens, gain_grad, *small_grads, decay_sq, plain_sq = pl.pallas_call(
        functools.partial(finish_kernel, plan, names, late),
        in_specs=[whole] * 7,
        out_specs=[whole] * (3 + len(names)) + [scalars] * 2,
        out_shape=[shape(in_proj.shape), shape(out_proj.shape), shape(tokens.shape, half)]
        + [shape(array.shape) for array in own]
        + [shape((1, 1))] * 2,
        name="finish",
    )(
        tokens_grad,
        in_branch_sum,
        in_gate_sum,
        out_sum,
        small_sum.reshape(plan["rows"], piece),
        late_sum,
        norms,
    )
    return (
        output,
        grad_tokens,
        gain_grad,
        in_grad,
        *small_grads,
        out_grad,
        decay_sq[0, 0],
        plain_sq[0, 0],
    )


def solution(mesh):
    placed = (
        P(("wide", "narrow"), None),
        P(("wide", "narrow"), None),
        P(("wide", "narrow")),
        P(("wide", "narrow"), None),
        P("narrow"),
        P("narrow", None),
        P(None, "narrow"),
        P("narrow"),
        P(None, "narrow"),
        P(None, "narrow"),
        P("narrow"),
        P(None, "narrow"),
        P("narrow"),
        P("narrow", None),
    )
    return jax.shard_map(
        functools.partial(per_device, grid_of(mesh)),
        mesh=mesh,
        in_specs=placed,
        out_specs=(
            P(("wide", "narrow"), None),
            P(("wide", "narrow"), None),
            P("narrow"),
            P("narrow", None),
            P(None, "narrow"),
            P("narrow"),
            P(None, "narrow"),
            P(None, "narrow"),
            P("narrow"),
            P(None, "narrow"),
            P("narrow"),
            P("narrow", None),
            P(),
            P(),
        ),
        check_vma=False,
    )
```

```python
import functools
import math

import jax
import jax.numpy as jnp
import numpy as np
from jax import lax
from jax.experimental import pallas as pl
from jax.experimental.pallas import tpu as pltpu
from jax.sharding import PartitionSpec as P

epsilon = 1e-05
chunk = 8
lanes = 128
log2e = math.log2(math.e)
ln2 = math.log(2.0)
far = 1e30
tiny = 1e-30


def contract(left, right, left_dim, right_dim):
    return lax.dot_general(
        left, right, (((left_dim,), (right_dim,)), ((), ())), preferred_element_type=jnp.float32
    )


def row_loop(rows, group, body, initial):
    def some(index, carry):
        return body(index, pl.ds(pl.multiple_of(index * group, group), group), carry)

    return lax.fori_loop(0, rows // group, some, initial)


def cut(tile):
    return pl.ds(tile * lanes, lanes)


def sigmoid(values):
    return 0.5 * jnp.tanh(0.5 * values) + 0.5


def softplus(values):
    small = jnp.exp(-jnp.abs(values))
    series = small * (1.0 - small * (0.5 - small * (1.0 / 3.0 - 0.25 * small)))
    return jnp.maximum(values, 0.0) + jnp.where(small < 0.03, series, jnp.log(1.0 + small))


def slope_of(step):
    return 1.0 - jnp.exp(-step)


def fill_offsets(lengths_ref, offset_buf, rows):
    place = lax.broadcasted_iota(jnp.int32, offset_buf.shape, 0)
    start = jnp.zeros(offset_buf.shape, jnp.int32)
    ahead = jnp.int32(0)
    for index in range(lengths_ref.shape[1] - 1):
        ahead = ahead + lengths_ref[0, index]
        start = jnp.where(place >= ahead, ahead, start)
    offset_buf[...] = jnp.where(place < rows, place - start, 0)


def small_rows(small_ref, first, count):
    base = first // 16 * 16
    tall = -(-(first + count - base) // 16) * 16
    return small_ref[base : base + tall, :].astype(jnp.float32)[first - base : first - base + count]


def eight(values):
    total = values[:8]
    for row in range(8, values.shape[0], 8):
        total = total + values[row : row + 8]
    return total


def conv_rows(index, at, group, tile, branch_ref, offset_buf, taps, shift):
    count = taps.shape[0]
    here = slice(tile * lanes, (tile + 1) * lanes)
    current = branch_ref[at, cut(tile)]
    before = branch_ref[pl.ds(pl.multiple_of(jnp.maximum(index * group - 8, 0), 8), 8), cut(tile)]
    both = jnp.concatenate([before, current], axis=0)
    offsets = offset_buf[at, :]
    summed = shift[:, here] + taps[count - 1 : count, here] * current
    for tap in range(count - 1):
        lag = count - 1 - tap
        read = jnp.where(offsets >= lag, pltpu.roll(both, lag, 0)[8:], 0.0)
        summed = summed + taps[tap : tap + 1, here] * read
    return summed


def rows_of(blocks):
    return as_matrix(blocks[...][None])


def as_matrix(blocks):
    columns = blocks.shape[3]
    if blocks.shape[2] % 16:
        return blocks.astype(jnp.float32).reshape(-1, columns).astype(blocks.dtype)
    return blocks.reshape(-1, columns)


def front_kernel(
    plan,
    dims,
    names,
    lengths_ref,
    tokens_ref,
    cotangent_ref,
    mask_ref,
    *refs,
):
    smalls, in_ref, out_ref, refs = refs[: len(names)], refs[len(names)], refs[len(names) + 1], refs[len(names) + 2 :]
    branch_ref, signal_ref, slope_ref, projected_ref, flipped_ref, normed_ref, low_ref = refs[:7]
    write_pair, read_pair, small_out, gain_ref, whole_ref, gate_lines, out_lines = refs[7:14]
    offset_buf, pack_buf, own_small, own_in, own_gate, own_out, land_small, land_in, store_sem = refs[14:23]
    own_gain, land_gain, gain_send, gain_recv = refs[23:27]
    rows = tokens_ref.shape[0]
    width = branch_ref.shape[1]
    block = pl.program_id(0)
    last = whole_ref.shape[0]
    shares = own_out.shape[0]
    gather = Gather(
        dims,
        [own_small] + [own_in.at[index] for index in range(last)],
        [land_small] + [land_in.at[index] for index in range(last)],
        refs[27:30],
    )
    rise = Rise(
        dims,
        [own.at[index] for index in range(shares) for own in (own_gate, own_out)],
        [lines.at[index] for index in range(shares) for lines in (gate_lines, out_lines)],
        refs[30:],
    )
    tall = pack_buf.shape[0] // 2

    def stored(index):
        return pltpu.make_async_copy(land_in.at[index], whole_ref.at[index], store_sem.at[index])

    def move_on(plan_of_moves):
        for moment, legs in plan_of_moves:

            @pl.when(block == moment)
            def _(legs=legs):
                for which, number in legs:
                    gather.leg(which, number)

    @pl.when(block == 0)
    def _():
        pack_buf[...] = jnp.zeros_like(pack_buf)
        for name, ref in zip(names, smalls):
            first, height = plan[name]
            pack_buf[first : first + height, : ref.shape[1]] = ref[...]
        own_gain[...] = jnp.zeros_like(own_gain)
        own_gain[0:1, : gain_ref.shape[1] // land_gain.shape[0]] = smalls[names.index("gain")][...]
        for side in range(2):
            own_small[side] = pack_buf[side * tall : (side + 1) * tall, :].astype(own_small.dtype)
        for index in range(last):
            own_in[index] = in_ref[:, index * width : (index + 1) * width].astype(own_in.dtype)
        place = Place(dims)
        place.greet(everyone=True)
        send_to_all(place, lambda target: own_gain, land_gain, gain_send, gain_recv)
        for index in (1, 0) + tuple(range(2, last + 1)):
            gather.start(index)
        first = last * width
        for index in range(shares):
            each = own_gate.shape[2]
            own_gate[index] = in_ref[:, first + index * each : first + (index + 1) * each].astype(own_gate.dtype)
            each = own_out.shape[2]
            own_out[index] = out_ref[:, index * each : (index + 1) * each].astype(own_out.dtype)
        for index in range(2 * shares):
            rise.start(index)
        fill_offsets(lengths_ref, offset_buf, rows)
        gather.leg(1, 1)
        gather.leg(0, 1)
        wait_for_all(place, own_gain[...], land_gain, gain_send, gain_recv)
        each = gain_ref.shape[1] // land_gain.shape[0]
        for owner in range(land_gain.shape[0]):
            gain_ref[:, owner * each : (owner + 1) * each] = (
                land_gain[owner, 0:1, :each].astype(jnp.bfloat16).astype(jnp.float32)
            )

        def norm(index, at, carry):
            residual = tokens_ref[at, :].astype(jnp.float32)
            scale = lax.rsqrt(jnp.mean(residual * residual, axis=1, keepdims=True) + epsilon)
            normed_ref[at, :] = (residual * scale * gain_ref[...]).astype(normed_ref.dtype)
            return carry

        row_loop(rows, 16, norm, 0)
        gather.leg(1, 2)
        gather.leg(0, 2)
        gather.leg(2, 1)
        flipped_ref[...] = normed_ref[...].T
        gather.leg(1, 3)
        gather.leg(0, 3)
        gather.leg(2, 2)
        down = lax.broadcasted_iota(jnp.int32, (rows, rows), 0)
        along = lax.broadcasted_iota(jnp.int32, (rows, rows), 1)
        diagonal = jnp.where(down == along, mask_ref[...].astype(jnp.float32), 0.0).astype(low_ref.dtype)
        low_ref[...] = jnp.dot(
            diagonal, cotangent_ref[...], preferred_element_type=jnp.float32
        ).astype(low_ref.dtype)
        projected_ref[...] = jnp.zeros_like(projected_ref)

    for index in range(last):

        @pl.when(block == index)
        def _(index=index):
            gather.arrive(index + 1)
            stored(index).start()

    branch_w = as_matrix(land_in[block])
    branch_ref[...] = jnp.dot(normed_ref[...], branch_w, preferred_element_type=jnp.float32)
    move_on(((0, ((3, 1), (2, 3))), (1, ((4, 2), (3, 3))), (2, ((4, 3),))))

    @pl.when(block == 0)
    def _():
        gather.arrive(0)
        share = land_small.shape[4]
        for z in range(land_small.shape[0]):
            for plane in range(land_small.shape[1]):
                owner = z * land_small.shape[1] + plane
                for side in range(2):
                    small_out[side * tall : (side + 1) * tall, owner * share : (owner + 1) * share] = land_small[
                        z, plane, side
                    ]

    small_ref = small_out.at[:, pl.ds(pl.multiple_of(block * width, width), width)]
    taps = small_rows(small_ref, *plan["taps"])
    shift = small_rows(small_ref, *plan["shift"])

    def some(index, at, carry):
        for tile in range(width // lanes):
            summed = conv_rows(index, at, 32, tile, branch_ref, offset_buf, taps, shift)
            sigma = sigmoid(summed)
            active = summed * sigma
            signal_ref[at, cut(tile)] = active.astype(signal_ref.dtype)
            slope_ref[at, cut(tile)] = sigma + active * (1.0 - sigma)
        return carry

    row_loop(rows, 32, some, 0)
    move_on(((0, ((4, 1), (3, 2))),))
    projected_ref[...] += contract(signal_ref[...], small_ref[:lanes, :], 1, 1)

    @pl.when(block == pl.num_programs(0) - 1)
    def _():
        high, low = high_low(projected_ref[...])
        own = own_tokens(rows)
        rank = plan["step"][1]
        size = plan["decay"][1]
        entry = lax.broadcasted_iota(jnp.int32, (lanes, lanes), 0)
        lane = lax.rem(lax.broadcasted_iota(jnp.int32, (lanes, lanes), 1), size)
        for first, pair in ((rank, write_pair), (rank + size, read_pair)):
            spread = (entry == lane + first).astype(jnp.bfloat16)
            parts = [
                (jnp.dot(part.astype(jnp.bfloat16), spread, preferred_element_type=jnp.float32) * own).reshape(
                    rows // chunk, chunk, lanes
                )
                for part in (high, low)
            ]
            pair[...] = jnp.concatenate(parts, axis=1).astype(pair.dtype)
        for index in range(last + 1):
            gather.drain(index)
        for index in range(2 * shares):
            rise.finish(index)
        for index in range(last):
            stored(index).wait()


def high_low(values):
    high = values.astype(jnp.bfloat16).astype(jnp.float32)
    return high, values - high


def own_tokens(rows):
    token = lax.rem(lax.broadcasted_iota(jnp.int32, (rows, lanes), 0), chunk)
    return (token == lax.div(lax.broadcasted_iota(jnp.int32, (rows, lanes), 1), lanes // chunk)).astype(
        jnp.float32
    )


def spread_all(pairs, target):
    some = 8

    def spread(index, carry):
        rows = jnp.concatenate([pairs[index * some + number] for number in range(some)], axis=1)
        wide = contract(rows, jnp.ones((rows.shape[0], lanes), rows.dtype), 0, 0)
        target[pl.ds(index * some * chunk, some * chunk)] = wide.reshape(some * chunk, -1, lanes)
        return carry

    lax.fori_loop(0, pairs.shape[0] // some, spread, 0)


def joined(first, second, hop):
    low = lax.bitwise_and(lax.broadcasted_iota(jnp.int32, first.shape, 0), hop) == 0
    return jnp.where(low, first, second) + pltpu.roll(jnp.where(low, second, first), hop, 0)


def folded(buffer, tile):
    parts = [buffer[tile, pl.ds(row * chunk, chunk), :] for row in range(chunk)]
    hop = 1
    while len(parts) > 1:
        parts = [joined(parts[index], parts[index + 1], hop) for index in range(0, len(parts), 2)]
        hop *= 2
    return parts[0]


def forward_kernel(
    plan,
    dims,
    lengths_ref,
    projected_ref,
    small_ref,
    signal_ref,
    write_pair,
    read_pair,
    gate_lines,
    out_lines,
    states_ref,
    step_ref,
    core_ref,
    begin_ref,
    gate_whole,
    out_whole,
    offset_buf,
    pre_buf,
    decay_step,
    flows,
    write_wide,
    read_wide,
    fold_a,
    fold_b,
    held_buf,
    *sems,
):
    rows, width = pre_buf.shape
    size = plan["decay"][1]
    half_size = size // 2
    tiles = width // lanes
    chunks = rows // chunk
    rank = plan["step"][1]
    group = pl.program_id(1)
    groups = pl.num_programs(1)
    moment = pl.program_id(0) * groups + group
    moments = pl.num_programs(0) * groups
    shares = gate_whole.shape[0]
    count = 2 * shares
    gather = Gather(
        dims,
        [lines.at[index] for index in range(shares) for lines in (gate_lines, out_lines)],
        [whole.at[index] for index in range(shares) for whole in (gate_whole, out_whole)],
        sems,
        [whole.shape[3:] for _ in range(shares) for whole in (gate_whole, out_whole)],
    )

    @pl.when(moment == 0)
    def _():
        Place(dims).greet()
        for which in range(count):
            gather.start(which)
        fill_offsets(lengths_ref, offset_buf, offset_buf.shape[0] - 8)
        spread_all(write_pair, write_wide)
        spread_all(read_pair, read_wide)

    @pl.when(group == 0)
    def _():
        held_buf[...] = jnp.zeros_like(held_buf)

    begin_ref[0] = held_buf[...]
    pre_buf[...] = jnp.dot(
        projected_ref[:, :rank].astype(small_ref.dtype),
        small_ref[pl.ds(plan["step"][0], rank), :],
        preferred_element_type=jnp.float32,
    )
    bias = small_rows(small_ref, *plan["bias"])

    def before(index, at, carry):
        spot = pl.ds(pl.multiple_of(index * 4, 4), 4)
        inside = offset_buf[pl.ds(pl.multiple_of(group * rows + index * 32, 32), 32), :] > 0
        for tile in range(tiles):
            step = softplus(pre_buf[at, cut(tile)] + bias[:, tile * lanes : (tile + 1) * lanes])
            step_ref[spot, :, cut(tile)] = step.reshape(4, chunk, lanes)
            decay_step[spot, :, cut(tile)] = jnp.where(inside, step, far).reshape(4, chunk, lanes)
            flow = step * signal_ref[at, cut(tile)].astype(jnp.float32)
            flows[spot, :, cut(tile)] = flow.reshape(4, chunk, lanes)
        return carry

    row_loop(rows, 4 * chunk, before, 0)
    rates = -jnp.exp(small_rows(small_ref, *plan["decay"])) * log2e
    rates = [rates[:, tile * lanes : (tile + 1) * lanes] for tile in range(tiles)]

    def advance(index, held, fold_buf):
        held = list(held)
        for place in range(chunk):
            now = index * chunk + place
            write_now = write_wide[group * rows + now]
            read_now = read_wide[group * rows + now]
            for tile in range(tiles):
                decay = jnp.exp2(rates[tile] * decay_step[index, pl.ds(place, 1), cut(tile)])
                fresh = decay * held[tile] + write_now * flows[index, pl.ds(place, 1), cut(tile)]
                held[tile] = fresh
                states_ref[now, :, cut(tile)] = fresh
                product = read_now * fresh
                fold_buf[tile, pl.ds(place * chunk, chunk), :] = product[:half_size] + product[half_size:]
        return tuple(held)

    def forward(pair, held):
        index = 2 * pair
        held = advance(index, held, fold_a)
        for tile in range(tiles):
            core_ref[index, :, cut(tile)] = folded(fold_a, tile)
        held = advance(index + 1, held, fold_b)
        for tile in range(tiles):
            core_ref[index + 1, :, cut(tile)] = folded(fold_b, tile)
        return held

    held = tuple(held_buf[:, cut(tile)] for tile in range(tiles))
    schedule = {}
    for which in range(count):
        for number in (2, 3):
            point = ((3, 5, 7, 10), (6, 8, 11, 14))[number - 2][which]
            schedule.setdefault(point, []).append((which, number))

    def move_on(legs):
        for which, number in legs:
            gather.leg(which, number)

    for half_loop in range(2):
        for point, legs in sorted(schedule.items()):
            if point < 16 and point % 2 == half_loop:
                pl.when(moment == point // 2)(functools.partial(move_on, legs))
        held = lax.fori_loop(half_loop * chunks // 4, (half_loop + 1) * chunks // 4, forward, held)
    for tile in range(tiles):
        held_buf[:, cut(tile)] = held[tile]

    @pl.when(moment == moments - 1)
    def _():
        for which in range(count):
            gather.arrive(which)
        for which in range(count):
            gather.drain(which)


def middle_kernel(
    plan,
    core_ref,
    small_ref,
    signal_ref,
    gate_w,
    low_ref,
    out_w,
    flipped_ref,
    normed_ref,
    tokens_ref,
    core_grad_ref,
    gate_grad_ref,
    skip_grad_ref,
    out_grad_ref,
    in_grad_ref,
    output_ref,
    pre_buf,
    gate_buf,
    gated_buf,
    out_buf,
    total,
):
    rows, width = pre_buf.shape
    tiles = width // lanes
    block = pl.program_id(0)
    each = out_w.shape[3]
    for index in range(out_w.shape[0]):
        out_buf[:, index * each : (index + 1) * each] = as_matrix(out_w[index][None])
    gate_buf[...] = jnp.dot(normed_ref[...], rows_of(gate_w), preferred_element_type=jnp.float32)
    pre_buf[...] = contract(low_ref[...], out_buf[...], 1, 1)
    skip = small_rows(small_ref, *plan["skip"])

    def after(index, at, carry):
        spot = pl.ds(pl.multiple_of(index * 4, 4), 4)
        sums = []
        for tile in range(tiles):
            signal = signal_ref[at, cut(tile)].astype(jnp.float32)
            core = core_ref[spot, :, cut(tile)].reshape(4 * chunk, lanes)
            core = core + skip[:, tile * lanes : (tile + 1) * lanes] * signal
            gate = gate_buf[at, cut(tile)]
            sigma = sigmoid(gate)
            active = gate * sigma
            gated_buf[at, cut(tile)] = (core * active).astype(gated_buf.dtype)
            grad_gated = pre_buf[at, cut(tile)]
            grad_core = grad_gated * active
            core_grad_ref[spot, :, cut(tile)] = grad_core.reshape(4, chunk, lanes)
            slope = sigma + active * (1.0 - sigma)
            gate_grad_ref[at, cut(tile)] = (grad_gated * core * slope).astype(gate_grad_ref.dtype)
            sums.append(carry[tile] + eight(grad_core * signal))
        return tuple(sums)

    zero_rows = jnp.zeros((8, lanes), jnp.float32)
    skips = row_loop(rows, 4 * chunk, after, (zero_rows,) * tiles)
    for tile in range(tiles):
        skip_grad_ref[:, cut(tile)] = jnp.sum(skips[tile], axis=0, keepdims=True)
    out_grad = contract(gated_buf[...], low_ref[...], 0, 0).astype(out_grad_ref.dtype)
    for index in range(out_w.shape[0]):
        out_grad_ref[index] = out_grad[:, index * each : (index + 1) * each]
    in_grad_ref[...] = jnp.dot(
        flipped_ref[...], gate_grad_ref[...], preferred_element_type=jnp.float32
    ).astype(in_grad_ref.dtype)
    piece = jnp.dot(gated_buf[...], out_buf[...], preferred_element_type=jnp.float32)

    @pl.when(block == 0)
    def _():
        total[...] = piece

    @pl.when(block > 0)
    def _():
        total[...] += piece

    @pl.when(block == pl.num_programs(0) - 1)
    def _():
        output_ref[...] = (tokens_ref[...].astype(jnp.float32) + total[...]).astype(output_ref.dtype)


def backward_kernel(
    plan,
    dims,
    lengths_ref,
    projected_ref,
    small_ref,
    signal_ref,
    write_pair,
    read_pair,
    step_ref,
    core_grad_ref,
    states_ref,
    begin_ref,
    out_grad_ref,
    in_grad_ref,
    signal_grad_ref,
    step_w_grad_ref,
    bias_grad_ref,
    decay_grad_ref,
    flat_ref,
    out_sum_ref,
    in_sum_ref,
    square_ref,
    offset_buf,
    decay_step,
    flows,
    write_wide,
    read_wide,
    first_a,
    first_b,
    second_a,
    second_b,
    through_buf,
    scaled_buf,
    low_buf,
    incoming_buf,
    rank_buf,
    write_buf,
    read_buf,
    *parts,
):
    rows, width = low_buf.shape
    rank = plan["step"][1]
    size = plan["decay"][1]
    half_size = size // 2
    tiles = width // lanes
    chunks = rows // chunk
    block = pl.program_id(0)
    turn = pl.program_id(1)
    groups = pl.num_programs(1)
    group = groups - 1 - turn
    moment = block * groups + turn
    moments = pl.num_programs(0) * groups
    gate_result, out_result, parts = parts[0], parts[1], parts[2:]
    pieces = gate_result.shape[0]
    count = 2 * pieces

    both = ((in_grad_ref, gate_result), (out_grad_ref, out_result))
    reduce = Reduce(
        dims,
        [ref.at[index] for index in range(pieces) for ref, _ in both],
        parts[: 6 * count],
        parts[6 * count :],
        [result.at[index] for index in range(pieces) for _, result in both],
        False,
    )

    @pl.when(moment == 0)
    def _():
        Place(dims).greet()
        for which in range(count):
            reduce.start(which)
        fill_offsets(lengths_ref, offset_buf, offset_buf.shape[0] - 8)
        spread_all(write_pair, write_wide)
        spread_all(read_pair, read_wide)
        write_buf[...] = jnp.zeros_like(write_buf)
        read_buf[...] = jnp.zeros_like(read_buf)
        rank_buf[...] = jnp.zeros_like(rank_buf)

    @pl.when(turn == 0)
    def _():
        incoming_buf[...] = jnp.zeros_like(incoming_buf)
        decay_grad_ref[...] = jnp.zeros_like(decay_grad_ref)
        bias_grad_ref[...] = jnp.zeros_like(bias_grad_ref)
        step_w_grad_ref[...] = jnp.zeros_like(step_w_grad_ref)

    def before(index, at, carry):
        spot = pl.ds(pl.multiple_of(index * 4, 4), 4)
        offsets = offset_buf[pl.ds(pl.multiple_of(group * rows + index * 32, 32), 32), :]
        inside = (offsets > 0).reshape(4, chunk, lanes)
        for tile in range(tiles):
            step = step_ref[spot, :, cut(tile)]
            decay_step[spot, :, cut(tile)] = jnp.where(inside, step, far)
            signal = signal_ref[at, cut(tile)].astype(jnp.float32).reshape(4, chunk, lanes)
            flows[spot, :, cut(tile)] = step * signal
        return carry

    row_loop(rows, 4 * chunk, before, 0)
    rates = -jnp.exp(small_rows(small_ref, *plan["decay"])) * log2e
    rates = [rates[:, tile * lanes : (tile + 1) * lanes] for tile in range(tiles)]

    def retreat(index, carried, first_buf, second_buf):
        incoming, decay_sums, current = (list(tiles_of) for tiles_of in carried)
        for place in range(chunk - 1, -1, -1):
            now = index * chunk + place
            token = group * rows + now
            write_now = write_wide[token]
            read_now = read_wide[token]
            read_sum = None
            write_sum = None
            for tile in range(tiles):
                grad_now = core_grad_ref[index, pl.ds(place, 1), cut(tile)]
                if place > 0:
                    earlier = states_ref[now - 1, :, cut(tile)]
                else:
                    earlier = jnp.where(
                        index > 0, states_ref[jnp.maximum(now - 1, 0), :, cut(tile)], begin_ref[0, :, cut(tile)]
                    )
                grad_state = incoming[tile] + read_now * grad_now
                through_read = current[tile] * grad_now
                current[tile] = earlier
                through_write = grad_state * flows[index, pl.ds(place, 1), cut(tile)]
                read_sum = through_read if read_sum is None else read_sum + through_read
                write_sum = through_write if write_sum is None else write_sum + through_write
                passed = grad_state * write_now
                first_buf[tile, pl.ds(place * chunk, chunk), :] = passed[:half_size] + passed[half_size:]
                exponent = rates[tile] * decay_step[index, pl.ds(place, 1), cut(tile)]
                leaving = jnp.exp2(exponent) * grad_state
                incoming[tile] = leaving
                weighted = (leaving * earlier) * exponent
                second_buf[tile, pl.ds(place * chunk, chunk), :] = weighted[:half_size] + weighted[half_size:]
                decay_sums[tile] = decay_sums[tile] + weighted
            read_buf[token] += read_sum
            write_buf[token] += write_sum
        return (tuple(incoming), tuple(decay_sums), tuple(current))

    def backward(pair, carried):
        index = chunks - 1 - 2 * pair
        for here, first_buf, second_buf in ((index, first_a, second_a), (index - 1, first_b, second_b)):
            carried = retreat(here, carried, first_buf, second_buf)
            for tile in range(tiles):
                through_buf[here, :, cut(tile)] = folded(first_buf, tile)
                scaled_buf[here, :, cut(tile)] = folded(second_buf, tile)
        return carried

    incoming = tuple(incoming_buf[:, cut(tile)] for tile in range(tiles))
    nothing = (jnp.zeros((size, lanes), jnp.float32),) * tiles
    current = tuple(states_ref[rows - 1, :, cut(tile)] for tile in range(tiles))
    schedule = {}
    for which in range(count):
        for number in (1, 2, 3):
            schedule.setdefault((2, 4, 7, 9)[which] + (0, 3, 5)[number - 1], []).append((which, number))

    def move_on(legs):
        for which, number in legs:
            reduce.leg(which, number)

    carried = (incoming, nothing, current)
    for half_loop in range(2):
        for point, legs in sorted(schedule.items()):
            if point % 2 == half_loop:
                pl.when(moment == point // 2)(functools.partial(move_on, legs))
        carried = lax.fori_loop(half_loop * chunks // 4, (half_loop + 1) * chunks // 4, backward, carried)
    incoming, decay_sums, _ = carried
    for tile in range(tiles):
        incoming_buf[:, cut(tile)] = incoming[tile]
        decay_grad_ref[:, cut(tile)] += decay_sums[tile] * ln2
    skip = small_rows(small_ref, *plan["skip"])

    def after(index, at, carry):
        spot = pl.ds(pl.multiple_of(index * 4, 4), 4)
        sums = []
        for tile in range(tiles):
            signal = signal_ref[at, cut(tile)].astype(jnp.float32)
            step = step_ref[spot, :, cut(tile)].reshape(4 * chunk, lanes)
            through = through_buf[spot, :, cut(tile)].reshape(4 * chunk, lanes)
            scaled = scaled_buf[spot, :, cut(tile)].reshape(4 * chunk, lanes)
            core_grad = core_grad_ref[spot, :, cut(tile)].reshape(4 * chunk, lanes)
            grad_pre = (through * signal + ln2 * scaled / jnp.maximum(step, tiny)) * slope_of(step)
            low_buf[at, cut(tile)] = grad_pre.astype(low_buf.dtype)
            signal_grad_ref[at, cut(tile)] = (
                through * step + skip[:, tile * lanes : (tile + 1) * lanes] * core_grad
            )
            sums.append(carry[tile] + eight(grad_pre))
        return tuple(sums)

    zero_rows = jnp.zeros((8, lanes), jnp.float32)
    sums = row_loop(rows, 4 * chunk, after, (zero_rows,) * tiles)
    for tile in range(tiles):
        bias_grad_ref[:, cut(tile)] += jnp.sum(sums[tile], axis=0, keepdims=True)
    step_w_grad_ref[...] += contract(
        projected_ref[:, :rank].astype(low_buf.dtype), low_buf[...], 0, 0
    )
    step_w = small_ref[pl.ds(plan["step"][0], rank), :]
    step_w = jnp.concatenate([step_w, jnp.zeros((lanes - rank, width), step_w.dtype)], axis=0)
    rank_buf[pl.ds(group * chunks, chunks)] += contract(low_buf[...], step_w, 1, 1).reshape(
        chunks, chunk, lanes
    )

    @pl.when(moment == moments - 1)
    def _():
        squares = jnp.zeros((8, lanes), jnp.float32)
        for which in range(count):
            squares = squares + reduce.finish(which)[0]
        square_ref[...] = squares
        some = 8
        entry = lax.rem(lax.broadcasted_iota(jnp.int32, (some * chunk * size, lanes), 0), size)
        target = lax.broadcasted_iota(jnp.int32, (some * chunk * size, lanes), 1)
        ones = jnp.ones((lanes, lanes), jnp.bfloat16)

        def lay(index, carry):
            lot = pl.ds(index * some * chunk, some * chunk)
            for number, buffer in enumerate((write_buf, read_buf)):
                high, low = high_low(buffer[lot].reshape(some * chunk * size, lanes))
                summed = jnp.dot(high.astype(jnp.bfloat16), ones, preferred_element_type=jnp.float32)
                summed += jnp.dot(low.astype(jnp.bfloat16), ones, preferred_element_type=jnp.float32)
                summed = jnp.where(target == entry + rank + number * size, summed, 0.0)
                summed = jnp.sum(summed.reshape(some * chunk, size, lanes), axis=1)
                rank_buf[pl.ds(index * some, some)] += summed.reshape(some, chunk, lanes)
            return carry

        lax.fori_loop(0, rank_buf.shape[0] // some, lay, 0)
        flat_ref[...] = rank_buf[...].reshape(flat_ref.shape).astype(flat_ref.dtype)
        for which in range(count):
            reduce.settle(which)
        for index in range(pieces):
            for target, result in ((out_sum_ref, out_result), (in_sum_ref, gate_result)):
                each = result.shape[2]
                target[:, index * each : (index + 1) * each] = result[index]


def back_kernel(
    plan,
    dims,
    lengths_ref,
    tokens_ref,
    low_ref,
    gain_ref,
    small_ref,
    flat_ref,
    branch_ref,
    signal_ref,
    slope_ref,
    signal_grad_ref,
    gate_grad_ref,
    flipped_ref,
    branch_w,
    gate_w,
    step_w_grad_ref,
    bias_grad_ref,
    decay_grad_ref,
    skip_grad_ref,
    plain_ref,
    earlier_ref,
    tokens_grad_ref,
    in_sum_ref,
    small_sum_ref,
    late_sum_ref,
    norm_ref,
    offset_buf,
    conv_buf,
    mixed_buf,
    total,
    in_stage,
    small_stage,
    late_stage,
    late_land,
    norm_own,
    norm_land,
    in_result,
    small_result,
    direct_send,
    direct_recv,
    *parts,
):
    rows = tokens_ref.shape[0]
    width = branch_ref.shape[1]
    tiles = width // lanes
    block = pl.program_id(0)
    last = in_stage.shape[0]
    count = last + 1
    reduce = Reduce(
        dims,
        [small_stage] + [in_stage.at[index] for index in range(last)],
        parts[: 5 * count],
        parts[5 * count :],
        [small_result] + [in_result.at[index] for index in range(last)],
        True,
    )
    share = small_stage.shape[4]
    half_rows = small_stage.shape[3]
    planes = small_stage.shape[1]
    owners = small_stage.shape[0] * planes

    @pl.when(block == 0)
    def _():
        Place(dims).greet(everyone=True)
        select_grad = contract(flat_ref[...], signal_ref[...], 0, 0)
        step_first, step_tall = plan["step"]
        filler = jnp.zeros((2 * half_rows - step_first - step_tall, select_grad.shape[1]), jnp.float32)
        pieces = {
            "decay": decay_grad_ref[...],
            "bias": bias_grad_ref[...],
            "skip": skip_grad_ref[...],
            "step": step_w_grad_ref[...],
        }
        first = plan["select"][1]
        rows_now = [select_grad[:first]]
        for name in ("decay", "taps", "shift", "bias", "skip", "gain"):
            tall = plan[name][1]
            rows_now.append(
                pieces[name] if name in pieces else jnp.zeros((tall, select_grad.shape[1]), jnp.float32)
            )
            first += tall
        rows_now.append(jnp.zeros((step_first - first, select_grad.shape[1]), jnp.float32))
        rows_now.append(pieces["step"])
        if filler.shape[0]:
            rows_now.append(filler)
        everything = jnp.concatenate(rows_now, axis=0)
        for owner in range(owners):
            for side in range(2):
                small_stage[owner // planes, owner % planes, side] = everything[
                    side * half_rows : (side + 1) * half_rows, owner * share : (owner + 1) * share
                ].astype(small_stage.dtype)
        reduce.start(0)
        fill_offsets(lengths_ref, offset_buf, rows)

    def move_on(plan_of_moves):
        for moment, legs in plan_of_moves:

            @pl.when(block == moment)
            def _(legs=legs):
                for which, number in legs:
                    reduce.leg(which, number)

    taps = small_rows(small_ref, *plan["taps"])
    taps_count = taps.shape[0]
    zero_rows = jnp.zeros((8, lanes), jnp.float32)

    @pl.when(block < last)
    def _():
        conv_buf[pl.ds(0, rows), :] = signal_grad_ref[...] + jnp.dot(
            flat_ref[...], small_ref[:lanes, :], preferred_element_type=jnp.float32
        )
        conv_buf[pl.ds(rows, 8), :] = jnp.zeros((8, width), jnp.float32)

        def through_conv(index, at, carry):
            sums = []
            for tile in range(tiles):
                grad_conv = conv_buf[at, cut(tile)] * slope_ref[at, cut(tile)]
                conv_buf[at, cut(tile)] = grad_conv
                sums.append(carry[tile] + eight(grad_conv))
            return tuple(sums)

        shift_sums = row_loop(rows, 32, through_conv, (zero_rows,) * tiles)
        move_on(((0, ((0, 1),)), (1, ((1, 1), (0, 3))), (2, ((2, 1), (1, 3))), (3, ((3, 1), (2, 3)))))

        def to_branch(index, at, carry):
            longer = pl.ds(pl.multiple_of(index * 32, 32), 40)
            offsets = offset_buf[longer, :]
            result = []
            for tile in range(tiles):
                here = slice(tile * lanes, (tile + 1) * lanes)
                grads = conv_buf[longer, cut(tile)]
                branch = branch_ref[at, cut(tile)]
                summed = taps[taps_count - 1 : taps_count, here] * grads[:32]
                sums = [None] * taps_count
                sums[taps_count - 1] = carry[tile][taps_count - 1] + eight(branch * grads[:32])
                for tap in range(taps_count - 1):
                    lag = taps_count - 1 - tap
                    moved = pltpu.roll(jnp.where(offsets >= lag, grads, 0.0), 40 - lag, 0)[:32]
                    summed = summed + taps[tap : tap + 1, here] * moved
                    sums[tap] = carry[tile][tap] + eight(branch * moved)
                mixed_buf[block, at, cut(tile)] = summed.astype(mixed_buf.dtype)
                result.append(tuple(sums))
            return tuple(result)

        sums = row_loop(rows, 32, to_branch, ((zero_rows,) * taps_count,) * tiles)
        in_grad = jnp.dot(flipped_ref[...], mixed_buf[block], preferred_element_type=jnp.float32)
        in_stage[block] = in_grad.reshape(in_stage.shape[1:]).astype(in_stage.dtype)
        for index in range(last):

            @pl.when(block == index)
            def _(index=index):
                reduce.start(index + 1)

        late = [
            jnp.concatenate(
                [jnp.sum(sums[tile][tap], axis=0, keepdims=True) for tap in range(taps_count)]
                + [jnp.sum(shift_sums[tile], axis=0, keepdims=True)]
                + [jnp.zeros((8 - taps_count - 1, lanes), jnp.float32)],
                axis=0,
            )
            for tile in range(tiles)
        ]
        late = jnp.concatenate(late, axis=1)
        for piece in range(width // share):
            late_stage[block * (width // share) + piece] = late[:, piece * share : (piece + 1) * share]
        move_on(((0, ((0, 2),)), (1, ((1, 2),)), (2, ((2, 2),)), (3, ((3, 2),))))

    @pl.when(block >= last)
    def _():
        grad_normed_piece = contract(mixed_buf[block - last], rows_of(branch_w), 1, 1)
        grad_normed_piece += contract(gate_grad_ref[...], rows_of(gate_w), 1, 1)

        @pl.when(block == last)
        def _():
            total[...] = grad_normed_piece

        @pl.when(block > last)
        def _():
            total[...] += grad_normed_piece

        move_on(((4, ((4, 1), (3, 3))), (6, ((4, 2),)), (7, ((4, 3),))))

    @pl.when(block == pl.num_programs(0) - 1)
    def _():
        def finish(index, at, carry):
            residual = tokens_ref[at, :].astype(jnp.float32)
            scale = lax.rsqrt(jnp.mean(residual * residual, axis=1, keepdims=True) + epsilon)
            grad_normed = total[at, :]
            weighted = grad_normed * gain_ref[...]
            inner = jnp.mean(weighted * residual, axis=1, keepdims=True)
            grad_y = low_ref[at, :].astype(jnp.float32)
            result = grad_y + (scale * weighted - residual * (scale * scale * scale) * inner)
            tokens_grad_ref[at, :] = result.astype(tokens_grad_ref.dtype)
            return carry + eight(grad_normed * residual * scale)

        gains = row_loop(rows, 16, finish, jnp.zeros((8, total.shape[1]), jnp.float32))
        gains = jnp.sum(gains, axis=0, keepdims=True)
        place = Place(dims)
        each = gains.shape[1] // owners
        for owner in range(owners):
            late_stage[owner, taps_count + 1 : taps_count + 2, :each] = gains[
                :, owner * each : (owner + 1) * each
            ]
        late_sems = direct_send.at[0], direct_recv.at[0]
        norm_sems = direct_send.at[1], direct_recv.at[1]
        send_to_everyone(place, lambda chip: late_stage.at[chip], late_land, *late_sems)
        more, plain = reduce.finish(0, plain_ref)
        kept = earlier_ref[...] + more
        for index in range(1, count - 1):
            kept = kept + reduce.finish(index)[0]
        late_sum = sum_of_everyone(place, late_stage[place.me], late_land, *late_sems)
        late_sum_ref[...] = late_sum
        kept = kept + folded_squares(late_sum * late_sum) * (1 - place.core).astype(jnp.float32)
        kept = kept + reduce.finish(count - 1)[0]
        norm_own[...] = jnp.stack([kept, plain])
        send_to_everyone(place, lambda chip: norm_own, norm_land, *norm_sems)
        norm_ref[...] = sum_of_everyone(place, norm_own[...], norm_land, *norm_sems)
        for index in range(count):
            reduce.settle(index)
        for index in range(last):
            in_sum_ref[:, index * width : (index + 1) * width] = in_result[index]
        small_sum_ref[...] = small_result[...]


def finish_kernel(
    plan, names, late, tokens_ref, branch_ref, gate_ref, out_ref, small_ref, late_ref, norm_ref, *outs
):
    middle = branch_ref.shape[1]
    outs[0][:, :middle] = branch_ref[...]
    outs[0][:, middle:] = gate_ref[...]
    outs[1][...] = out_ref[...]
    outs[2][...] = tokens_ref[...]
    for name, target in zip(names, outs[3 : 3 + len(names)]):
        source, (first, count) = (late_ref, late[name]) if name in late else (small_ref, plan[name])
        if len(target.shape) == 1:
            target[...] = source[first, : target.shape[0]]
        else:
            target[...] = source[first : first + count, :]
    for index in range(2):
        outs[3 + len(names) + index][0, 0] = jnp.sum(norm_ref[index])


def shape(dims, kind=jnp.float32):
    return jax.ShapeDtypeStruct(dims, kind)


def compute_call(
    kernel, name, blocks, in_specs, out_specs, out_shape, scratch, flops, operands, collective_id=None
):
    return pl.pallas_call(
        kernel,
        grid=blocks if isinstance(blocks, tuple) else (blocks,),
        in_specs=in_specs,
        out_specs=out_specs,
        out_shape=out_shape,
        scratch_shapes=scratch,
        compiler_params=pltpu.CompilerParams(
            dimension_semantics=("arbitrary",) * (len(blocks) if isinstance(blocks, tuple) else 1),
            vmem_limit_bytes=62 * 1024 * 1024,
            collective_id=collective_id,
            has_side_effects=collective_id is not None,
        ),
        cost_estimate=pl.CostEstimate(flops=flops, bytes_accessed=40 << 20, transcendentals=0),
        name=name,
    )(*operands)


class Place:
    def __init__(self, dims, swapped=False):
        depth, tall, wide = dims
        self.dims = dims
        self.core = lax.axis_index("wide")
        self.me = lax.axis_index("narrow")
        self.across = lax.rem(self.me, wide)
        self.up = lax.rem(lax.div(self.me, wide), tall)
        self.deep = lax.div(self.me, wide * tall)
        side = 1 - self.core if swapped else self.core
        turn = side if tall == wide else 0
        self.second = (1 + turn * (wide - 1), self.across + turn * (self.up - self.across), wide)
        self.third = (wide - turn * (wide - 1), self.up + turn * (self.across - self.up), tall)
        self.spans = (depth, wide, tall)
        self.other = {"wide": 1 - self.core}

    def level(self, d):
        return lax.rem(self.deep + d, self.spans[0])

    def plane(self, e, f):
        return (
            lax.rem(self.second[1] + e, self.second[2]) * self.second[0]
            + lax.rem(self.third[1] + f, self.third[2]) * self.third[0]
        )

    def plane_behind(self, e, f):
        return self.plane((self.spans[1] - e) % self.spans[1], (self.spans[2] - f) % self.spans[2])

    def at(self, d, e, f):
        return {"narrow": self.level(d) * (self.dims[1] * self.dims[2]) + self.plane(e, f)}

    def greet(self, everyone=False):
        barrier = pltpu.get_barrier_semaphore()
        peers = [self.other]
        if everyone:
            number = self.spans[0] * self.spans[1] * self.spans[2]
            for hop in range(1, number):
                chip = lax.rem(self.me + hop, number)
                peers += [{"narrow": chip}, {"wide": 1 - self.core, "narrow": chip}]
        else:
            for axis, size in enumerate(self.spans):
                for hop in range(1, size):
                    move = [0, 0, 0]
                    move[axis] = hop
                    peers.append(self.at(*move))
        for peer in peers:
            pl.semaphore_signal(barrier, inc=1, device_id=peer, device_id_type=pl.DeviceIdType.MESH)
        pl.semaphore_wait(barrier, len(peers))


def by_rows(block):
    return block[0] % 32 == 0


def half_shape(block):
    if len(block) == 3:
        return tuple(block[1:])
    return (block[0] // 2, block[1]) if by_rows(block) else (block[0], block[1] // 2)


def half(view, block, side, lead=0):
    ahead = (slice(None),) * lead
    if len(block) == 3:
        return view.at[ahead + (side,)]
    if by_rows(block):
        return view.at[ahead + (pl.ds(pl.multiple_of(side * (block[0] // 2), 16), block[0] // 2),)]
    columns = pl.ds(pl.multiple_of(side * (block[1] // 2), lanes), block[1] // 2)
    return view.at[ahead + (slice(None), columns)]


def remote(source, target, send_sem, recv_sem, device):
    return pltpu.make_async_remote_copy(
        src_ref=source,
        dst_ref=target,
        send_sem=send_sem,
        recv_sem=recv_sem,
        device_id=device,
        device_id_type=pl.DeviceIdType.MESH,
    )


class Gather:
    def __init__(self, dims, own, whole, sems, blocks=None):
        self.dims, self.own, self.whole = dims, own, whole
        self.local_sem, self.send_sem, self.recv_sem = sems
        self.lined = blocks is not None
        self.blocks = blocks or [block.shape for block in own]

    @staticmethod
    def sems(count, dims):
        copies = dims[0] + 2 * dims[1] * dims[2]
        return [pltpu.SemaphoreType.DMA((count,))] + [pltpu.SemaphoreType.DMA((count, copies))] * 2

    def line(self, which, plane, side):
        return half(self.whole[which].at[:, plane], self.blocks[which], side, 1)

    def local(self, place, which):
        block = self.blocks[which]
        if self.lined:
            return pltpu.make_async_copy(
                self.own[which], self.line(which, place.plane(0, 0), place.core), self.local_sem.at[which]
            )
        return pltpu.make_async_copy(
            half(self.own[which], block, place.core),
            half(self.whole[which].at[place.deep, place.plane(0, 0)], block, place.core),
            self.local_sem.at[which],
        )

    def copy(self, which, source, target, index, device):
        return remote(
            source, target, self.send_sem.at[which, index], self.recv_sem.at[which, index], device
        )

    def rise(self, place, which, hop):
        block = self.blocks[which]
        return self.copy(
            which,
            half(self.own[which], block, place.core),
            half(self.whole[which].at[place.deep, place.plane(0, 0)], block, place.core),
            hop,
            place.at(hop, 0, 0),
        )

    def leg_index(self, e, f):
        return self.dims[0] + e * self.dims[1] + f

    def hand_index(self, e, f):
        return self.leg_index(e, f) + self.dims[1] * self.dims[2]

    def onward(self, place, which, e, f):
        line = self.line(which, place.plane_behind(e, f), place.core)
        source = self.own[which] if self.lined and e == 0 and f == 0 else line
        if f == 0:
            for hop in range(1, place.spans[2]):
                self.copy(which, source, line, self.leg_index(e, hop), place.at(0, 0, hop)).start()
        if f == 0 and e == 0:
            for hop in range(1, place.spans[1]):
                self.copy(which, source, line, self.leg_index(hop, 0), place.at(0, hop, 0)).start()
        self.copy(which, source, line, self.hand_index(e, f), place.other).start()

    def start(self, which):
        place = Place(self.dims)
        if self.lined:
            self.onward(place, which, 0, 0)
            self.local(place, which).start()
            return
        for hop in range(1, place.spans[0]):
            self.rise(place, which, hop).start()
        self.local(place, which).start()

    def leg(self, which, number):
        place = Place(self.dims)
        if number == 1:
            self.local(place, which).wait()
            for hop in range(1, place.spans[0]):
                self.rise(place, which, hop).wait_recv()
            self.onward(place, which, 0, 0)
            return
        for e in range(place.spans[1]):
            for f in range(place.spans[2]):
                if (number == 2 and f == 0 and e > 0) or (number == 3 and f > 0):
                    line = self.line(which, place.plane_behind(e, f), place.core)
                    self.copy(which, line, line, self.leg_index(e, f), place.other).wait_recv()
                    self.onward(place, which, e, f)

    def arrive(self, which):
        place, mirror = Place(self.dims), Place(self.dims, swapped=True)
        for e in range(place.spans[1]):
            for f in range(place.spans[2]):
                line = self.line(which, mirror.plane_behind(e, f), 1 - place.core)
                self.copy(which, line, line, self.hand_index(e, f), place.other).wait_recv()

    def drain(self, which):
        place = Place(self.dims)
        if self.lined:
            self.local(place, which).wait()
        else:
            for hop in range(1, place.spans[0]):
                self.rise(place, which, hop).wait_send()
        for e in range(place.spans[1]):
            for f in range(place.spans[2]):
                line = self.line(which, place.plane_behind(e, f), place.core)
                if e > 0 or f > 0:
                    self.copy(which, line, line, self.leg_index(e, f), place.other).wait_send()
                self.copy(which, line, line, self.hand_index(e, f), place.other).wait_send()


class Rise:
    def __init__(self, dims, own, lines, sems):
        self.dims, self.own, self.lines = dims, own, lines
        self.local_sem, self.send_sem, self.recv_sem = sems

    @staticmethod
    def sems(count, dims):
        return [pltpu.SemaphoreType.DMA((count,))] + [pltpu.SemaphoreType.DMA((count, dims[0]))] * 2

    def copies(self, place, which):
        source = half(self.own[which], self.own[which].shape, place.core)
        target = self.lines[which].at[place.deep]
        local = pltpu.make_async_copy(source, target, self.local_sem.at[which])
        return local, [
            remote(
                source, target, self.send_sem.at[which, hop], self.recv_sem.at[which, hop], place.at(hop, 0, 0)
            )
            for hop in range(1, place.spans[0])
        ]

    def start(self, which):
        local, sends = self.copies(Place(self.dims), which)
        for copy in [*sends, local]:
            copy.start()

    def finish(self, which):
        local, sends = self.copies(Place(self.dims), which)
        local.wait()
        for copy in sends:
            copy.wait_recv()
            copy.wait_send()


class Reduce:
    def __init__(self, dims, grads, rooms, sems, results, resident):
        self.dims, self.grads, self.resident = dims, grads, resident
        count = len(grads)
        self.mine, self.swapped, self.third, self.second, self.first = (
            rooms[index * count : (index + 1) * count] for index in range(5)
        )
        self.loaded = None if resident else rooms[5 * count :]
        self.load_sem, self.swap_send, self.swap_recv, self.send_sem, self.recv_sem = sems[:5]
        self.last_send, self.last_recv = sems[5:]
        self.results = results

    @staticmethod
    def rooms(dims, grads, resident):
        depth, tall, wide = dims
        leads = (
            (tall, wide, depth),
            (depth, tall * wide),
            (tall - 1, wide, depth),
            (wide - 1, depth),
            (depth - 1,),
        )
        if not resident:
            leads += ((depth, tall * wide),)
        return [
            pltpu.VMEM(lead + half_shape(grad.shape[2:]), grad.dtype) for lead in leads for grad in grads
        ]

    @staticmethod
    def sems(count, dims):
        return (
            [pltpu.SemaphoreType.DMA((count,))] * 3
            + [pltpu.SemaphoreType.DMA((count, dims[0] + dims[1] + dims[2]))] * 2
            + [pltpu.SemaphoreType.DMA((count,))] * 2
        )

    def block(self, which):
        return self.grads[which].shape[2:]

    def load(self, place, which):
        return pltpu.make_async_copy(
            half(self.grads[which], self.block(which), place.core, 2),
            self.loaded[which],
            self.load_sem.at[which],
        )

    def swap(self, place, which):
        return remote(
            half(self.grads[which], self.block(which), 1 - place.core, 2),
            self.swapped[which],
            self.swap_send.at[which],
            self.swap_recv.at[which],
            place.other,
        )

    def hop(self, which, source, target, index, device):
        return remote(
            source, target, self.send_sem.at[which, index], self.recv_sem.at[which, index], device
        )

    def third_hop(self, place, which, f):
        return self.hop(which, self.mine[which].at[f], self.third[which].at[f - 1], f, place.at(0, 0, f))

    def second_hop(self, place, which, e):
        return self.hop(
            which,
            self.mine[which].at[0, e],
            self.second[which].at[e - 1],
            self.dims[1] + e,
            place.at(0, e, 0),
        )

    def first_hop(self, place, which, d):
        return self.hop(
            which,
            self.mine[which].at[0, 0, place.level(d)],
            self.first[which].at[d - 1],
            self.dims[1] + self.dims[2] + d,
            place.at(d, 0, 0),
        )

    def start(self, which):
        place = Place(self.dims)
        self.swap(place, which).start()
        if not self.resident:
            self.load(place, which).start()

    def parts(self, place, which, e, f, z):
        plane = place.plane(e, f)
        if self.resident:
            found = [half(self.grads[which].at[z, plane], self.block(which), place.core)]
        else:
            found = [self.loaded[which].at[z, plane]]
        found.append(self.swapped[which].at[z, plane])
        if f == 0:
            found += [self.third[which].at[hop - 1, e, z] for hop in range(1, place.spans[2])]
        if f == 0 and e == 0:
            found += [self.second[which].at[hop - 1, z] for hop in range(1, place.spans[1])]
        return found

    def ready(self, place, which):
        if not self.resident:
            self.load(place, which).wait()
        self.swap(place, which).wait_recv()

    def added(self, parts, store, carry):
        rows = parts[0].shape[0]
        group = min(rows, 16)

        def some(index, carry):
            at_rows = pl.ds(pl.multiple_of(index * group, group), group)
            total = parts[0][at_rows, :].astype(jnp.float32)
            for part in parts[1:]:
                total = total + part[at_rows, :].astype(jnp.float32)
            return store(at_rows, total, carry)

        return lax.fori_loop(0, rows // group, some, carry)

    def sum_into(self, place, which, e, f, z):
        target = self.mine[which].at[f, e, z]

        def keep(at_rows, total, carry):
            target[at_rows, :] = total.astype(target.dtype)
            return carry

        self.added(self.parts(place, which, e, f, z), keep, 0)

    def leg(self, which, number):
        place = Place(self.dims)
        depth, span_e, span_f = place.spans
        if number == 1:
            self.ready(place, which)
            for f in range(span_f - 1, 0, -1):
                for e in range(span_e - 1, -1, -1):
                    for z in range(depth):
                        self.sum_into(place, which, e, f, z)
                self.third_hop(place, which, f).start()
        elif number == 2:
            for f in range(1, span_f):
                self.third_hop(place, which, f).wait_recv()
            for e in range(span_e - 1, 0, -1):
                for z in range(depth):
                    self.sum_into(place, which, e, 0, z)
                self.second_hop(place, which, e).start()
        else:
            if span_e == 1:
                for f in range(1, span_f):
                    self.third_hop(place, which, f).wait_recv()
            for e in range(1, span_e):
                self.second_hop(place, which, e).wait_recv()
            for d in range(1, depth):
                self.sum_into(place, which, 0, 0, place.level(d))
                self.first_hop(place, which, d).start()

    def result(self, which, side):
        return half(self.results[which], self.block(which), side)

    def last(self, place, which, side):
        share = self.result(which, side)
        return remote(share, share, self.last_send.at[which], self.last_recv.at[which], place.other)

    def finish(self, which, marks=None):
        place = Place(self.dims)
        parts = self.parts(place, which, 0, 0, place.deep)
        for d in range(1, place.spans[0]):
            self.first_hop(place, which, d).wait_recv()
            parts.append(self.first[which].at[d - 1])
        share = self.result(which, place.core)

        def store(at_rows, total, carry):
            share[at_rows, :] = total
            kept, plain = carry
            squared = total * total
            if marks is not None:
                marked = squared * marks[place.core, at_rows, :]
                plain = plain + folded_squares(marked)
                squared = squared - marked
            return (kept + folded_squares(squared), plain)

        squares = self.added(parts, store, (jnp.zeros((8, lanes), jnp.float32),) * 2)
        self.last(place, which, place.core).start()
        return squares

    def settle(self, which):
        place = Place(self.dims)
        last = self.last(place, which, 1 - place.core)
        last.wait_recv()
        last.wait_send()
        self.swap(place, which).wait_send()
        for f in range(1, place.spans[2]):
            self.third_hop(place, which, f).wait_send()
        for e in range(1, place.spans[1]):
            self.second_hop(place, which, e).wait_send()
        for d in range(1, place.spans[0]):
            self.first_hop(place, which, d).wait_send()


def folded_squares(values):
    total = None
    if values.shape[1] < lanes:
        first = lax.broadcasted_iota(jnp.int32, (values.shape[0], lanes), 1) == 0
        values = jnp.where(first, jnp.sum(values, axis=1, keepdims=True), 0.0)
    for row in range(0, values.shape[0], 8):
        for column in range(0, values.shape[1], lanes):
            piece = values[row : row + 8, column : column + lanes]
            total = piece if total is None else total + piece
    return total


def send_to_all(place, source, landing, send_sem, recv_sem):
    number = landing.shape[0]
    for hop in range(1, number):
        target = lax.rem(place.me + hop, number)
        remote(
            source(target), landing.at[place.me], send_sem.at[hop], recv_sem.at[hop], {"narrow": target}
        ).start()


def wait_for_all(place, own, landing, send_sem, recv_sem):
    number = landing.shape[0]
    landing[place.me] = own
    for hop in range(1, number):
        came = landing.at[lax.rem(place.me + number - hop, number)]
        copy = remote(came, came, send_sem.at[hop], recv_sem.at[hop], place.other)
        copy.wait_recv()
        copy.wait_send()


def send_to_everyone(place, source, landing, send_sem, recv_sem):
    number = landing.shape[1]
    target = landing.at[place.core, place.me]

    def send(hop, carry):
        chip = lax.rem(place.me + hop, number)
        for turn in range(2):
            device = {"wide": lax.rem(place.core + turn, 2), "narrow": chip}
            remote(source(chip), target, send_sem.at[turn, hop], recv_sem.at[turn, hop], device).start()
        return carry

    lax.fori_loop(1, number, send, 0)
    remote(source(place.me), target, send_sem.at[1, 0], recv_sem.at[1, 0], place.other).start()


def sum_of_everyone(place, own, landing, send_sem, recv_sem):
    number = landing.shape[1]
    landing[place.core, place.me] = own

    def wait(turn, hop):
        came = landing.at[lax.rem(place.core + turn, 2), lax.rem(place.me + number - hop, number)]
        copy = remote(came, came, send_sem.at[turn, hop], recv_sem.at[turn, hop], place.other)
        copy.wait_recv()
        copy.wait_send()

    def wait_both(hop, carry):
        wait(0, hop)
        wait(1, hop)
        return carry

    lax.fori_loop(1, number, wait_both, 0)
    wait(1, 0)

    def add(spot, total):
        return total + landing[0, spot] + landing[1, spot]

    return lax.fori_loop(1, number, add, landing[0, 0] + landing[1, 0])


def grid_of(mesh):
    number = mesh.shape["narrow"]
    places = [getattr(device, "coords", None) for device in mesh.devices[0]]
    if all(place is not None for place in places):
        sizes = [len({place[axis] for place in places}) for axis in (2, 1, 0)]
        if sizes[0] * sizes[1] * sizes[2] == number:
            return tuple(sizes)
    side = round((number / 2) ** (1 / 3))
    return (2 * side, side, side) if 2 * side**3 == number else (number, 1, 1)


def plan_of(select_rows, state_size, tap_count, step_rows):
    plan, first = {}, 0
    for name, tall in (
        ("select", select_rows),
        ("decay", state_size),
        ("taps", tap_count),
        ("shift", 1),
        ("bias", 1),
        ("skip", 1),
        ("gain", 1),
    ):
        plan[name] = (first, tall)
        first += tall
    plan["step"] = (lanes, step_rows)
    plan["rows"] = -(-(lanes + step_rows) // 32) * 32
    return plan


def per_device(
    dims,
    tokens,
    cotangent,
    loss_mask,
    seq_lengths,
    norm_gain,
    in_proj,
    conv_weight,
    conv_bias,
    select_proj,
    step_proj,
    step_bias,
    decay_log,
    skip_scale,
    out_proj,
):
    half = jnp.bfloat16
    piece = skip_scale.shape[0]
    gain_piece = norm_gain.shape[0]
    rank, size = step_proj.shape[0], decay_log.shape[0]
    plan = plan_of(select_proj.shape[0], size, conv_weight.shape[0], rank)
    smalls = {
        "select": select_proj,
        "decay": decay_log,
        "taps": conv_weight,
        "shift": conv_bias[None],
        "bias": step_bias[None],
        "skip": skip_scale[None],
        "gain": norm_gain[None],
        "step": step_proj,
    }
    depth, planes = dims[0], dims[1] * dims[2]
    number = depth * planes
    in_rows = in_proj.shape[0]
    rows, model = tokens.shape
    inner = piece * number
    width = 4 * lanes
    blocks = inner // width
    chunks = rows // chunk
    mask_row = loss_mask[None]

    whole = pl.BlockSpec(memory_space=pltpu.VMEM)
    tall = pl.BlockSpec((rows, width), lambda b: (0, b))
    deep = pl.BlockSpec((chunks, chunk, width), lambda b: (0, 0, b))
    lead = pl.BlockSpec((rows, size, width), lambda b: (0, 0, b))
    first_w = pl.BlockSpec((model, width), lambda b: (0, b))
    second_w = pl.BlockSpec((model, width), lambda b: (0, b + blocks))
    out_w = pl.BlockSpec((width, model), lambda b: (b, 0))

    def thin(height):
        return pl.BlockSpec((height, width), lambda b: (0, b))

    def fixed(*dims_of):
        return pl.BlockSpec(dims_of, lambda b: (0,) * len(dims_of))

    scalars = pl.BlockSpec(memory_space=pltpu.SMEM)
    offset_buf = pltpu.VMEM((rows + 8, lanes), jnp.int32)
    packed = thin(plan["rows"])

    pair = (chunks, 2 * chunk, lanes)
    pair = (chunks, 2 * chunk, lanes)
    anywhere = pl.BlockSpec(memory_space=pl.ANY)
    small_half = (2, plan["rows"] // 2, piece)
    in_piece = (in_rows, width)
    shares = 2
    in_share = (in_rows, inner // shares)
    out_share = (out_proj.shape[0], model // shares)
    lines = [shape((shares, depth) + half_shape(block), half) for block in (in_share, out_share)]
    (
        branch,
        signal,
        slope,
        projected,
        flipped,
        normed,
        grad_low,
        write_pair,
        read_pair,
        small,
        gain_value,
        in_blocks,
        gate_lines,
        out_lines,
    ) = compute_call(
        functools.partial(front_kernel, plan, dims, tuple(smalls)),
        "front",
        blocks,
        [scalars, whole, whole, whole] + [whole] * len(smalls) + [whole] * 2,
        [tall, tall, tall] + [whole] * 8 + [anywhere] * 3,
        [
            shape((rows, inner)),
            shape((rows, inner), half),
            shape((rows, inner)),
            shape((rows, lanes)),
            shape((model, rows), half),
            shape((rows, model), half),
            shape((rows, model), half),
            shape(pair, half),
            shape(pair, half),
            shape((plan["rows"], inner), half),
            shape((1, model)),
            shape((blocks, depth, planes) + in_piece, half),
            *lines,
        ],
        [
            offset_buf,
            pltpu.VMEM((plan["rows"], piece), jnp.float32),
            pltpu.VMEM(small_half, half),
            pltpu.VMEM((blocks,) + in_piece, half),
            pltpu.VMEM((shares,) + in_share, half),
            pltpu.VMEM((shares,) + out_share, half),
            pltpu.VMEM((depth, planes) + small_half, half),
            pltpu.VMEM((blocks, depth, planes) + in_piece, half),
            pltpu.SemaphoreType.DMA((blocks,)),
            pltpu.VMEM((8, piece), jnp.float32),
            pltpu.VMEM((number, 8, piece), jnp.float32),
            pltpu.SemaphoreType.DMA((number,)),
            pltpu.SemaphoreType.DMA((number,)),
        ]
        + Gather.sems(1 + blocks, dims)
        + Rise.sems(2 * shares, dims),
        4 * rows * model * inner,
        (seq_lengths, tokens, cotangent, mask_row, *smalls.values(), in_proj, out_proj),
        collective_id=0,
    )
    groups = 2
    part, pieces = rows // groups, chunks // groups
    row_block = pltpu.VMEM((pieces, chunk, width), jnp.float32)
    spread_block = pltpu.VMEM((rows, size, lanes), jnp.float32)
    fold_block = pltpu.VMEM((width // lanes, chunk * chunk, lanes), jnp.float32)

    def by_group(order, *dims_of):
        middle = (0,) * (len(dims_of) - 2)
        return pl.BlockSpec(dims_of, lambda b, g: (order(g),) + middle + (b,))

    def by_token(order, *dims_of):
        return pl.BlockSpec(dims_of, lambda b, g: (order(g),) + (0,) * (len(dims_of) - 1))

    def by_channel(height):
        return pl.BlockSpec((height, width), lambda b, g: (0, b))

    def onward(g):
        return g

    def backward(g):
        return groups - 1 - g

    states, step, core, begins, gate_blocks, out_blocks = compute_call(
        functools.partial(forward_kernel, plan, dims),
        "forward",
        (blocks, groups),
        [
            scalars,
            by_token(onward, part, lanes),
            by_channel(plan["rows"]),
            by_group(onward, part, width),
            whole,
            whole,
            anywhere,
            anywhere,
        ],
        [
            by_group(onward, part, size, width),
            by_group(onward, pieces, chunk, width),
            by_group(onward, pieces, chunk, width),
            by_group(onward, 1, size, width),
            anywhere,
            anywhere,
        ],
        [
            shape((rows, size, inner)),
            shape((chunks, chunk, inner)),
            shape((chunks, chunk, inner)),
            shape((groups, size, inner)),
            shape((shares, depth, planes) + in_share, half),
            shape((shares, depth, planes) + out_share, half),
        ],
        [
            offset_buf,
            pltpu.VMEM((part, width), jnp.float32),
            row_block,
            row_block,
            spread_block,
            spread_block,
            fold_block,
            fold_block,
            pltpu.VMEM((size, width), jnp.float32),
        ]
        + Gather.sems(2 * shares, dims),
        15 * rows * inner * size,
        (seq_lengths, projected, small, signal, write_pair, read_pair, gate_lines, out_lines),
        collective_id=2,
    )
    split = in_share[1] // width
    weights = pl.BlockSpec((None, number, in_rows, width), lambda b: (b // split, 0, 0, b % split))
    per_block = width // out_share[0]
    out_pieces = pl.BlockSpec((shares, per_block) + out_share, lambda b: (0, b, 0, 0))
    branch_whole = in_blocks.reshape(blocks, number, *in_piece)
    gate_whole = gate_blocks.reshape(shares, number, *in_share)
    out_whole = out_blocks.reshape(shares, number, *out_share)
    core_grad, gate_grad, grad_skip, grad_outw, grad_in_gate, output = compute_call(
        functools.partial(middle_kernel, plan),
        "middle",
        blocks,
        [deep, packed, tall, weights, whole, out_pieces, whole, whole, whole],
        [
            deep,
            tall,
            thin(1),
            pl.BlockSpec((shares, width, out_share[1]), lambda b: (0, b, 0)),
            pl.BlockSpec((None, model, width), lambda b: (b // split, 0, b % split)),
            fixed(rows, model),
        ],
        [
            shape((chunks, chunk, inner)),
            shape((rows, inner), half),
            shape((1, inner)),
            shape((shares, inner, out_share[1]), half),
            shape((shares, model, in_share[1]), half),
            shape((rows, model), half),
        ],
        [
            pltpu.VMEM((rows, width), jnp.float32),
            pltpu.VMEM((rows, width), jnp.float32),
            pltpu.VMEM((rows, width), half),
            pltpu.VMEM((width, model), half),
            pltpu.VMEM((rows, model), jnp.float32),
        ],
        8 * rows * model * inner,
        (core, small, signal, gate_whole, grad_low, out_whole, flipped, normed, tokens),
    )
    early_grads = [
        grad_outw.reshape((shares, depth, planes) + out_share),
        grad_in_gate.reshape((shares, depth, planes) + in_share),
    ]
    early_sums = [shape(out_proj.shape), shape((in_rows, inner))]
    early_pieces = [shape((depth, planes) + block, half) for block in (in_share, out_share)] * shares
    (
        signal_grad,
        grad_stepw,
        grad_bias,
        grad_decaylog,
        flat,
        out_sum,
        in_gate_sum,
        early_squares,
    ) = compute_call(
        functools.partial(backward_kernel, plan, dims),
        "backward",
        (blocks, groups),
        [
            scalars,
            by_token(backward, part, lanes),
            by_channel(plan["rows"]),
            by_group(backward, part, width),
            whole,
            whole,
            by_group(backward, pieces, chunk, width),
            by_group(backward, pieces, chunk, width),
            by_group(backward, part, size, width),
            by_group(backward, 1, size, width),
            anywhere,
            anywhere,
        ],
        [
            by_group(backward, part, width),
            by_channel(rank),
            by_channel(1),
            by_channel(size),
            whole,
        ]
        + [whole] * 3,
        [
            shape((rows, inner)),
            shape((rank, inner)),
            shape((1, inner)),
            shape((size, inner)),
            shape((rows, lanes), half),
            *early_sums,
            shape((8, lanes)),
        ],
        [
            offset_buf,
            row_block,
            row_block,
            spread_block,
            spread_block,
            fold_block,
            fold_block,
            fold_block,
            fold_block,
            row_block,
            row_block,
            pltpu.VMEM((part, width), half),
            pltpu.VMEM((size, width), jnp.float32),
            pltpu.VMEM((chunks, chunk, lanes), jnp.float32),
            spread_block,
            spread_block,
        ]
        + [pltpu.VMEM((shares,) + block, jnp.float32) for block in (in_share, out_share)]
        + Reduce.rooms(dims, early_pieces, False)
        + Reduce.sems(2 * shares, dims),
        40 * rows * inner * size,
        (
            seq_lengths,
            projected,
            small,
            signal,
            write_pair,
            read_pair,
            step,
            core_grad,
            states,
            begins,
            *early_grads,
        ),
        collective_id=3,
    )

    plain_rows = np.zeros((plan["rows"], piece), np.float32)
    for name in ("bias", "decay", "skip"):
        first, count = plan[name]
        plain_rows[first : first + count] = 1.0
    late_grads = [shape((depth, planes) + small_half, half)]
    late_grads += [shape((depth, planes, in_rows, width), half)] * blocks
    taps_n = conv_weight.shape[0]
    late = {"taps": (0, taps_n), "shift": (taps_n, 1), "gain": (taps_n + 1, 1)}
    late_block = (8, piece)

    early_tall = pl.BlockSpec((rows, width), lambda b: (0, jnp.minimum(b, blocks - 1)))
    late_tall = pl.BlockSpec((rows, width), lambda b: (0, jnp.maximum(b - blocks, 0)))
    tokens_grad, in_branch_sum, small_sum, late_sum, norms = compute_call(
        functools.partial(back_kernel, plan, dims),
        "back",
        2 * blocks,
        [scalars, whole, whole, whole]
        + [pl.BlockSpec((plan["rows"], width), lambda b: (0, jnp.minimum(b, blocks - 1))), whole]
        + [early_tall, whole, early_tall, early_tall, late_tall, whole]
        + [
            pl.BlockSpec((None, number, in_rows, width), lambda b: (jnp.maximum(b - blocks, 0), 0, 0, 0)),
            pl.BlockSpec(
                (None, number, in_rows, width),
                lambda b: (jnp.maximum(b - blocks, 0) // split, 0, 0, jnp.maximum(b - blocks, 0) % split),
            ),
        ]
        + [whole] * 6,
        [whole] * 5,
        [
            shape((rows, model), half),
            shape((in_rows, inner)),
            shape(small_half),
            shape(late_block),
            shape((2, 8, lanes)),
        ],
        [
            offset_buf,
            pltpu.VMEM((rows + 8, width), jnp.float32),
            pltpu.VMEM((blocks, rows, width), half),
            pltpu.VMEM((rows, model), jnp.float32),
            pltpu.VMEM((blocks,) + late_grads[1].shape, half),
            pltpu.VMEM(late_grads[0].shape, late_grads[0].dtype),
            pltpu.VMEM((number,) + late_block, jnp.float32),
            pltpu.VMEM((2, number) + late_block, jnp.float32),
            pltpu.VMEM((2, 8, lanes), jnp.float32),
            pltpu.VMEM((2, number, 2, 8, lanes), jnp.float32),
            pltpu.VMEM((blocks, in_rows, width), jnp.float32),
            pltpu.VMEM(small_half, jnp.float32),
            pltpu.SemaphoreType.DMA((2, 2, number)),
            pltpu.SemaphoreType.DMA((2, 2, number)),
        ]
        + Reduce.rooms(dims, late_grads, True)
        + Reduce.sems(blocks + 1, dims),
        8 * rows * model * inner,
        (
            seq_lengths,
            tokens,
            grad_low,
            gain_value,
            small,
            flat,
            branch,
            signal,
            slope,
            signal_grad,
            gate_grad,
            flipped,
            branch_whole,
            gate_whole,
            grad_stepw,
            grad_bias,
            grad_decaylog,
            grad_skip,
            jnp.asarray(plain_rows.reshape(small_half)),
            early_squares,
        ),
        collective_id=1,
    )

    names = ("gain", "taps", "shift", "select", "step", "bias", "decay", "skip")
    own = (norm_gain, conv_weight, conv_bias, select_proj, step_proj, step_bias, decay_log, skip_scale)
    in_grad, out_grad, grad_tokens, gain_grad, *small_grads, decay_sq, plain_sq = pl.pallas_call(
        functools.partial(finish_kernel, plan, names, late),
        in_specs=[whole] * 7,
        out_specs=[whole] * (3 + len(names)) + [scalars] * 2,
        out_shape=[shape(in_proj.shape), shape(out_proj.shape), shape(tokens.shape, half)]
        + [shape(array.shape) for array in own]
        + [shape((1, 1))] * 2,
        name="finish",
    )(
        tokens_grad,
        in_branch_sum,
        in_gate_sum,
        out_sum,
        small_sum.reshape(plan["rows"], piece),
        late_sum,
        norms,
    )
    return (
        output,
        grad_tokens,
        gain_grad,
        in_grad,
        *small_grads,
        out_grad,
        decay_sq[0, 0],
        plain_sq[0, 0],
    )


def solution(mesh):
    placed = (
        P(("wide", "narrow"), None),
        P(("wide", "narrow"), None),
        P(("wide", "narrow")),
        P(("wide", "narrow"), None),
        P("narrow"),
        P("narrow", None),
        P(None, "narrow"),
        P("narrow"),
        P(None, "narrow"),
        P(None, "narrow"),
        P("narrow"),
        P(None, "narrow"),
        P("narrow"),
        P("narrow", None),
    )
    return jax.shard_map(
        functools.partial(per_device, grid_of(mesh)),
        mesh=mesh,
        in_specs=placed,
        out_specs=(
            P(("wide", "narrow"), None),
            P(("wide", "narrow"), None),
            P("narrow"),
            P("narrow", None),
            P(None, "narrow"),
            P("narrow"),
            P(None, "narrow"),
            P(None, "narrow"),
            P("narrow"),
            P(None, "narrow"),
            P("narrow"),
            P("narrow", None),
            P(),
            P(),
        ),
        check_vma=False,
    )
```

```python
import functools
import math

import jax
import jax.numpy as jnp
import numpy as np
from jax import lax
from jax.experimental import pallas as pl
from jax.experimental.pallas import tpu as pltpu
from jax.sharding import PartitionSpec as P

epsilon = 1e-05
chunk = 8
lanes = 128
log2e = math.log2(math.e)
ln2 = math.log(2.0)
far = 1e30
tiny = 1e-30


def contract(left, right, left_dim, right_dim):
    return lax.dot_general(
        left, right, (((left_dim,), (right_dim,)), ((), ())), preferred_element_type=jnp.float32
    )


def row_loop(rows, group, body, initial):
    def some(index, carry):
        return body(index, pl.ds(pl.multiple_of(index * group, group), group), carry)

    return lax.fori_loop(0, rows // group, some, initial)


def cut(tile):
    return pl.ds(tile * lanes, lanes)


def sigmoid(values):
    return 0.5 * jnp.tanh(0.5 * values) + 0.5


def softplus(values):
    small = jnp.exp(-jnp.abs(values))
    series = small * (1.0 - small * (0.5 - small * (1.0 / 3.0 - 0.25 * small)))
    return jnp.maximum(values, 0.0) + jnp.where(small < 0.03, series, jnp.log(1.0 + small))


def slope_of(step):
    return 1.0 - jnp.exp(-step)


def fill_offsets(lengths_ref, offset_buf, rows):
    place = lax.broadcasted_iota(jnp.int32, offset_buf.shape, 0)
    start = jnp.zeros(offset_buf.shape, jnp.int32)
    ahead = jnp.int32(0)
    for index in range(lengths_ref.shape[1] - 1):
        ahead = ahead + lengths_ref[0, index]
        start = jnp.where(place >= ahead, ahead, start)
    offset_buf[...] = jnp.where(place < rows, place - start, 0)


def small_rows(small_ref, first, count):
    base = first // 16 * 16
    tall = -(-(first + count - base) // 16) * 16
    return small_ref[base : base + tall, :].astype(jnp.float32)[first - base : first - base + count]


def eight(values):
    total = values[:8]
    for row in range(8, values.shape[0], 8):
        total = total + values[row : row + 8]
    return total


def conv_rows(index, at, group, tile, branch_ref, offset_buf, taps, shift):
    count = taps.shape[0]
    here = slice(tile * lanes, (tile + 1) * lanes)
    current = branch_ref[at, cut(tile)]
    before = branch_ref[pl.ds(pl.multiple_of(jnp.maximum(index * group - 8, 0), 8), 8), cut(tile)]
    both = jnp.concatenate([before, current], axis=0)
    offsets = offset_buf[at, :]
    summed = shift[:, here] + taps[count - 1 : count, here] * current
    for tap in range(count - 1):
        lag = count - 1 - tap
        read = jnp.where(offsets >= lag, pltpu.roll(both, lag, 0)[8:], 0.0)
        summed = summed + taps[tap : tap + 1, here] * read
    return summed


def rows_of(blocks):
    return as_matrix(blocks[...][None])


def as_matrix(blocks):
    columns = blocks.shape[3]
    if blocks.shape[2] % 16:
        return blocks.astype(jnp.float32).reshape(-1, columns).astype(blocks.dtype)
    return blocks.reshape(-1, columns)


def front_kernel(
    plan,
    dims,
    names,
    lengths_ref,
    tokens_ref,
    cotangent_ref,
    mask_ref,
    *refs,
):
    smalls, in_ref, out_ref, refs = refs[: len(names)], refs[len(names)], refs[len(names) + 1], refs[len(names) + 2 :]
    branch_ref, signal_ref, slope_ref, projected_ref, flipped_ref, normed_ref, low_ref = refs[:7]
    write_pair, read_pair, small_out, gain_ref, whole_ref, gate_lines, out_lines = refs[7:14]
    offset_buf, pack_buf, own_small, own_in, own_gate, own_out, land_small, land_in, store_sem = refs[14:23]
    own_gain, land_gain, gain_send, gain_recv = refs[23:27]
    rows = tokens_ref.shape[0]
    width = branch_ref.shape[1]
    block = pl.program_id(0)
    last = whole_ref.shape[0]
    shares = own_out.shape[0]
    gather = Gather(
        dims,
        [own_small] + [own_in.at[index] for index in range(last)],
        [land_small] + [land_in.at[index] for index in range(last)],
        refs[27:30],
    )
    rise = Rise(
        dims,
        [own.at[index] for index in range(shares) for own in (own_gate, own_out)],
        [lines.at[index] for index in range(shares) for lines in (gate_lines, out_lines)],
        refs[30:],
    )
    tall = pack_buf.shape[0] // 2

    def stored(index):
        return pltpu.make_async_copy(land_in.at[index], whole_ref.at[index], store_sem.at[index])

    def move_on(plan_of_moves):
        for moment, legs in plan_of_moves:

            @pl.when(block == moment)
            def _(legs=legs):
                for which, number in legs:
                    gather.leg(which, number)

    @pl.when(block == 0)
    def _():
        pack_buf[...] = jnp.zeros_like(pack_buf)
        for name, ref in zip(names, smalls):
            first, height = plan[name]
            pack_buf[first : first + height, : ref.shape[1]] = ref[...]
        own_gain[...] = jnp.zeros_like(own_gain)
        own_gain[0:1, : gain_ref.shape[1] // land_gain.shape[0]] = smalls[names.index("gain")][...]
        for side in range(2):
            own_small[side] = pack_buf[side * tall : (side + 1) * tall, :].astype(own_small.dtype)
        for index in range(last):
            own_in[index] = in_ref[:, index * width : (index + 1) * width].astype(own_in.dtype)
        place = Place(dims)
        place.greet(everyone=True)
        send_to_all(place, lambda target: own_gain, land_gain, gain_send, gain_recv)
        for index in (1, 0) + tuple(range(2, last + 1)):
            gather.start(index)
        first = last * width
        for index in range(shares):
            each = own_gate.shape[2]
            own_gate[index] = in_ref[:, first + index * each : first + (index + 1) * each].astype(own_gate.dtype)
            each = own_out.shape[2]
            own_out[index] = out_ref[:, index * each : (index + 1) * each].astype(own_out.dtype)
        fill_offsets(lengths_ref, offset_buf, rows)
        gather.leg(1, 1)
        gather.leg(0, 1)
        wait_for_all(place, own_gain[...], land_gain, gain_send, gain_recv)
        each = gain_ref.shape[1] // land_gain.shape[0]
        for owner in range(land_gain.shape[0]):
            gain_ref[:, owner * each : (owner + 1) * each] = (
                land_gain[owner, 0:1, :each].astype(jnp.bfloat16).astype(jnp.float32)
            )

        def norm(index, at, carry):
            residual = tokens_ref[at, :].astype(jnp.float32)
            scale = lax.rsqrt(jnp.mean(residual * residual, axis=1, keepdims=True) + epsilon)
            normed_ref[at, :] = (residual * scale * gain_ref[...]).astype(normed_ref.dtype)
            return carry

        row_loop(rows, 16, norm, 0)
        gather.leg(1, 2)
        gather.leg(0, 2)
        gather.leg(2, 1)
        rise.start(0)
        flipped_ref[...] = normed_ref[...].T
        gather.leg(1, 3)
        gather.leg(0, 3)
        gather.leg(2, 2)
        down = lax.broadcasted_iota(jnp.int32, (rows, rows), 0)
        along = lax.broadcasted_iota(jnp.int32, (rows, rows), 1)
        diagonal = jnp.where(down == along, mask_ref[...].astype(jnp.float32), 0.0).astype(low_ref.dtype)
        low_ref[...] = jnp.dot(
            diagonal, cotangent_ref[...], preferred_element_type=jnp.float32
        ).astype(low_ref.dtype)
        projected_ref[...] = jnp.zeros_like(projected_ref)

    for index in range(last):

        @pl.when(block == index)
        def _(index=index):
            gather.arrive(index + 1)
            stored(index).start()

    branch_w = as_matrix(land_in[block])
    branch_ref[...] = jnp.dot(normed_ref[...], branch_w, preferred_element_type=jnp.float32)
    move_on(((0, ((3, 1), (2, 3))), (1, ((4, 2), (3, 3))), (2, ((4, 3),))))
    pl.when(block == 0)(functools.partial(rise.start, 1))

    @pl.when(block == 0)
    def _():
        gather.arrive(0)
        share = land_small.shape[4]
        for z in range(land_small.shape[0]):
            for plane in range(land_small.shape[1]):
                owner = z * land_small.shape[1] + plane
                for side in range(2):
                    small_out[side * tall : (side + 1) * tall, owner * share : (owner + 1) * share] = land_small[
                        z, plane, side
                    ]

    small_ref = small_out.at[:, pl.ds(pl.multiple_of(block * width, width), width)]
    taps = small_rows(small_ref, *plan["taps"])
    shift = small_rows(small_ref, *plan["shift"])

    def some(index, at, carry):
        for tile in range(width // lanes):
            summed = conv_rows(index, at, 32, tile, branch_ref, offset_buf, taps, shift)
            sigma = sigmoid(summed)
            active = summed * sigma
            signal_ref[at, cut(tile)] = active.astype(signal_ref.dtype)
            slope_ref[at, cut(tile)] = sigma + active * (1.0 - sigma)
        return carry

    row_loop(rows, 32, some, 0)
    move_on(((0, ((4, 1), (3, 2))),))

    @pl.when(block == 0)
    def _():
        for index in range(2, 2 * shares):
            rise.start(index)

    projected_ref[...] += contract(signal_ref[...], small_ref[:lanes, :], 1, 1)

    @pl.when(block == pl.num_programs(0) - 1)
    def _():
        high, low = high_low(projected_ref[...])
        own = own_tokens(rows)
        rank = plan["step"][1]
        size = plan["decay"][1]
        entry = lax.broadcasted_iota(jnp.int32, (lanes, lanes), 0)
        lane = lax.rem(lax.broadcasted_iota(jnp.int32, (lanes, lanes), 1), size)
        for first, pair in ((rank, write_pair), (rank + size, read_pair)):
            spread = (entry == lane + first).astype(jnp.bfloat16)
            parts = [
                (jnp.dot(part.astype(jnp.bfloat16), spread, preferred_element_type=jnp.float32) * own).reshape(
                    rows // chunk, chunk, lanes
                )
                for part in (high, low)
            ]
            pair[...] = jnp.concatenate(parts, axis=1).astype(pair.dtype)
        for index in range(last + 1):
            gather.drain(index)
        for index in range(2 * shares):
            rise.finish(index)
        for index in range(last):
            stored(index).wait()


def high_low(values):
    high = values.astype(jnp.bfloat16).astype(jnp.float32)
    return high, values - high


def own_tokens(rows):
    token = lax.rem(lax.broadcasted_iota(jnp.int32, (rows, lanes), 0), chunk)
    return (token == lax.div(lax.broadcasted_iota(jnp.int32, (rows, lanes), 1), lanes // chunk)).astype(
        jnp.float32
    )


def spread_all(pairs, target):
    some = 8

    def spread(index, carry):
        rows = jnp.concatenate([pairs[index * some + number] for number in range(some)], axis=1)
        wide = contract(rows, jnp.ones((rows.shape[0], lanes), rows.dtype), 0, 0)
        target[pl.ds(index * some * chunk, some * chunk)] = wide.reshape(some * chunk, -1, lanes)
        return carry

    lax.fori_loop(0, pairs.shape[0] // some, spread, 0)


def joined(first, second, hop):
    low = lax.bitwise_and(lax.broadcasted_iota(jnp.int32, first.shape, 0), hop) == 0
    return jnp.where(low, first, second) + pltpu.roll(jnp.where(low, second, first), hop, 0)


def folded(buffer, tile):
    parts = [buffer[tile, pl.ds(row * chunk, chunk), :] for row in range(chunk)]
    hop = 1
    while len(parts) > 1:
        parts = [joined(parts[index], parts[index + 1], hop) for index in range(0, len(parts), 2)]
        hop *= 2
    return parts[0]


def forward_kernel(
    plan,
    dims,
    lengths_ref,
    projected_ref,
    small_ref,
    signal_ref,
    write_pair,
    read_pair,
    gate_lines,
    out_lines,
    states_ref,
    step_ref,
    core_ref,
    begin_ref,
    gate_whole,
    out_whole,
    offset_buf,
    pre_buf,
    decay_step,
    flows,
    write_wide,
    read_wide,
    fold_a,
    fold_b,
    held_buf,
    *sems,
):
    rows, width = pre_buf.shape
    size = plan["decay"][1]
    half_size = size // 2
    tiles = width // lanes
    chunks = rows // chunk
    rank = plan["step"][1]
    group = pl.program_id(1)
    groups = pl.num_programs(1)
    moment = pl.program_id(0) * groups + group
    moments = pl.num_programs(0) * groups
    shares = gate_whole.shape[0]
    count = 2 * shares
    gather = Gather(
        dims,
        [lines.at[index] for index in range(shares) for lines in (gate_lines, out_lines)],
        [whole.at[index] for index in range(shares) for whole in (gate_whole, out_whole)],
        sems,
        [whole.shape[3:] for _ in range(shares) for whole in (gate_whole, out_whole)],
    )

    @pl.when(moment == 0)
    def _():
        Place(dims).greet()
        for which in range(count):
            gather.start(which)
        fill_offsets(lengths_ref, offset_buf, offset_buf.shape[0] - 8)
        spread_all(write_pair, write_wide)
        spread_all(read_pair, read_wide)

    @pl.when(group == 0)
    def _():
        held_buf[...] = jnp.zeros_like(held_buf)

    begin_ref[0] = held_buf[...]
    pre_buf[...] = jnp.dot(
        projected_ref[:, :rank].astype(small_ref.dtype),
        small_ref[pl.ds(plan["step"][0], rank), :],
        preferred_element_type=jnp.float32,
    )
    bias = small_rows(small_ref, *plan["bias"])

    def before(index, at, carry):
        spot = pl.ds(pl.multiple_of(index * 4, 4), 4)
        inside = offset_buf[pl.ds(pl.multiple_of(group * rows + index * 32, 32), 32), :] > 0
        for tile in range(tiles):
            step = softplus(pre_buf[at, cut(tile)] + bias[:, tile * lanes : (tile + 1) * lanes])
            step_ref[spot, :, cut(tile)] = step.reshape(4, chunk, lanes)
            decay_step[spot, :, cut(tile)] = jnp.where(inside, step, far).reshape(4, chunk, lanes)
            flow = step * signal_ref[at, cut(tile)].astype(jnp.float32)
            flows[spot, :, cut(tile)] = flow.reshape(4, chunk, lanes)
        return carry

    row_loop(rows, 4 * chunk, before, 0)
    rates = -jnp.exp(small_rows(small_ref, *plan["decay"])) * log2e
    rates = [rates[:, tile * lanes : (tile + 1) * lanes] for tile in range(tiles)]

    def advance(index, held, fold_buf):
        held = list(held)
        for place in range(chunk):
            now = index * chunk + place
            write_now = write_wide[group * rows + now]
            read_now = read_wide[group * rows + now]
            for tile in range(tiles):
                decay = jnp.exp2(rates[tile] * decay_step[index, pl.ds(place, 1), cut(tile)])
                fresh = decay * held[tile] + write_now * flows[index, pl.ds(place, 1), cut(tile)]
                held[tile] = fresh
                states_ref[now, :, cut(tile)] = fresh
                product = read_now * fresh
                fold_buf[tile, pl.ds(place * chunk, chunk), :] = product[:half_size] + product[half_size:]
        return tuple(held)

    def forward(pair, held):
        index = 2 * pair
        held = advance(index, held, fold_a)
        for tile in range(tiles):
            core_ref[index, :, cut(tile)] = folded(fold_a, tile)
        held = advance(index + 1, held, fold_b)
        for tile in range(tiles):
            core_ref[index + 1, :, cut(tile)] = folded(fold_b, tile)
        return held

    held = tuple(held_buf[:, cut(tile)] for tile in range(tiles))
    schedule = {}
    for which in range(count):
        for number in (2, 3):
            point = ((3, 5, 7, 10), (6, 8, 11, 14))[number - 2][which]
            schedule.setdefault(point, []).append((which, number))

    def move_on(legs):
        for which, number in legs:
            gather.leg(which, number)

    for half_loop in range(2):
        for point, legs in sorted(schedule.items()):
            if point < 16 and point % 2 == half_loop:
                pl.when(moment == point // 2)(functools.partial(move_on, legs))
        held = lax.fori_loop(half_loop * chunks // 4, (half_loop + 1) * chunks // 4, forward, held)
    for tile in range(tiles):
        held_buf[:, cut(tile)] = held[tile]

    @pl.when(moment == moments - 1)
    def _():
        for which in range(count):
            gather.arrive(which)
        for which in range(count):
            gather.drain(which)


def middle_kernel(
    plan,
    core_ref,
    small_ref,
    signal_ref,
    gate_w,
    low_ref,
    out_w,
    flipped_ref,
    normed_ref,
    tokens_ref,
    core_grad_ref,
    gate_grad_ref,
    skip_grad_ref,
    out_grad_ref,
    in_grad_ref,
    output_ref,
    pre_buf,
    gate_buf,
    gated_buf,
    out_buf,
    total,
):
    rows, width = pre_buf.shape
    tiles = width // lanes
    block = pl.program_id(0)
    each = out_w.shape[3]
    for index in range(out_w.shape[0]):
        out_buf[:, index * each : (index + 1) * each] = as_matrix(out_w[index][None])
    gate_buf[...] = jnp.dot(normed_ref[...], rows_of(gate_w), preferred_element_type=jnp.float32)
    pre_buf[...] = contract(low_ref[...], out_buf[...], 1, 1)
    skip = small_rows(small_ref, *plan["skip"])

    def after(index, at, carry):
        spot = pl.ds(pl.multiple_of(index * 4, 4), 4)
        sums = []
        for tile in range(tiles):
            signal = signal_ref[at, cut(tile)].astype(jnp.float32)
            core = core_ref[spot, :, cut(tile)].reshape(4 * chunk, lanes)
            core = core + skip[:, tile * lanes : (tile + 1) * lanes] * signal
            gate = gate_buf[at, cut(tile)]
            sigma = sigmoid(gate)
            active = gate * sigma
            gated_buf[at, cut(tile)] = (core * active).astype(gated_buf.dtype)
            grad_gated = pre_buf[at, cut(tile)]
            grad_core = grad_gated * active
            core_grad_ref[spot, :, cut(tile)] = grad_core.reshape(4, chunk, lanes)
            slope = sigma + active * (1.0 - sigma)
            gate_grad_ref[at, cut(tile)] = (grad_gated * core * slope).astype(gate_grad_ref.dtype)
            sums.append(carry[tile] + eight(grad_core * signal))
        return tuple(sums)

    zero_rows = jnp.zeros((8, lanes), jnp.float32)
    skips = row_loop(rows, 4 * chunk, after, (zero_rows,) * tiles)
    for tile in range(tiles):
        skip_grad_ref[:, cut(tile)] = jnp.sum(skips[tile], axis=0, keepdims=True)
    out_grad = contract(gated_buf[...], low_ref[...], 0, 0).astype(out_grad_ref.dtype)
    for index in range(out_w.shape[0]):
        out_grad_ref[index] = out_grad[:, index * each : (index + 1) * each]
    in_grad_ref[...] = jnp.dot(
        flipped_ref[...], gate_grad_ref[...], preferred_element_type=jnp.float32
    ).astype(in_grad_ref.dtype)
    piece = jnp.dot(gated_buf[...], out_buf[...], preferred_element_type=jnp.float32)

    @pl.when(block == 0)
    def _():
        total[...] = piece

    @pl.when(block > 0)
    def _():
        total[...] += piece

    @pl.when(block == pl.num_programs(0) - 1)
    def _():
        output_ref[...] = (tokens_ref[...].astype(jnp.float32) + total[...]).astype(output_ref.dtype)


def backward_kernel(
    plan,
    dims,
    lengths_ref,
    projected_ref,
    small_ref,
    signal_ref,
    write_pair,
    read_pair,
    step_ref,
    core_grad_ref,
    states_ref,
    begin_ref,
    out_grad_ref,
    in_grad_ref,
    signal_grad_ref,
    step_w_grad_ref,
    bias_grad_ref,
    decay_grad_ref,
    flat_ref,
    out_sum_ref,
    in_sum_ref,
    square_ref,
    offset_buf,
    decay_step,
    flows,
    write_wide,
    read_wide,
    first_a,
    first_b,
    second_a,
    second_b,
    through_buf,
    scaled_buf,
    low_buf,
    incoming_buf,
    rank_buf,
    write_buf,
    read_buf,
    *parts,
):
    rows, width = low_buf.shape
    rank = plan["step"][1]
    size = plan["decay"][1]
    half_size = size // 2
    tiles = width // lanes
    chunks = rows // chunk
    block = pl.program_id(0)
    turn = pl.program_id(1)
    groups = pl.num_programs(1)
    group = groups - 1 - turn
    moment = block * groups + turn
    moments = pl.num_programs(0) * groups
    gate_result, out_result, parts = parts[0], parts[1], parts[2:]
    pieces = gate_result.shape[0]
    count = 2 * pieces

    both = ((in_grad_ref, gate_result), (out_grad_ref, out_result))
    reduce = Reduce(
        dims,
        [ref.at[index] for index in range(pieces) for ref, _ in both],
        parts[: 6 * count],
        parts[6 * count :],
        [result.at[index] for index in range(pieces) for _, result in both],
        False,
    )

    @pl.when(moment == 0)
    def _():
        Place(dims).greet()
        for which in range(count):
            reduce.start(which)
        fill_offsets(lengths_ref, offset_buf, offset_buf.shape[0] - 8)
        spread_all(write_pair, write_wide)
        spread_all(read_pair, read_wide)
        write_buf[...] = jnp.zeros_like(write_buf)
        read_buf[...] = jnp.zeros_like(read_buf)
        rank_buf[...] = jnp.zeros_like(rank_buf)

    @pl.when(turn == 0)
    def _():
        incoming_buf[...] = jnp.zeros_like(incoming_buf)
        decay_grad_ref[...] = jnp.zeros_like(decay_grad_ref)
        bias_grad_ref[...] = jnp.zeros_like(bias_grad_ref)
        step_w_grad_ref[...] = jnp.zeros_like(step_w_grad_ref)

    def before(index, at, carry):
        spot = pl.ds(pl.multiple_of(index * 4, 4), 4)
        offsets = offset_buf[pl.ds(pl.multiple_of(group * rows + index * 32, 32), 32), :]
        inside = (offsets > 0).reshape(4, chunk, lanes)
        for tile in range(tiles):
            step = step_ref[spot, :, cut(tile)]
            decay_step[spot, :, cut(tile)] = jnp.where(inside, step, far)
            signal = signal_ref[at, cut(tile)].astype(jnp.float32).reshape(4, chunk, lanes)
            flows[spot, :, cut(tile)] = step * signal
        return carry

    row_loop(rows, 4 * chunk, before, 0)
    rates = -jnp.exp(small_rows(small_ref, *plan["decay"])) * log2e
    rates = [rates[:, tile * lanes : (tile + 1) * lanes] for tile in range(tiles)]

    def retreat(index, carried, first_buf, second_buf):
        incoming, decay_sums, current = (list(tiles_of) for tiles_of in carried)
        for place in range(chunk - 1, -1, -1):
            now = index * chunk + place
            token = group * rows + now
            write_now = write_wide[token]
            read_now = read_wide[token]
            read_sum = None
            write_sum = None
            for tile in range(tiles):
                grad_now = core_grad_ref[index, pl.ds(place, 1), cut(tile)]
                if place > 0:
                    earlier = states_ref[now - 1, :, cut(tile)]
                else:
                    earlier = jnp.where(
                        index > 0, states_ref[jnp.maximum(now - 1, 0), :, cut(tile)], begin_ref[0, :, cut(tile)]
                    )
                grad_state = incoming[tile] + read_now * grad_now
                through_read = current[tile] * grad_now
                current[tile] = earlier
                through_write = grad_state * flows[index, pl.ds(place, 1), cut(tile)]
                read_sum = through_read if read_sum is None else read_sum + through_read
                write_sum = through_write if write_sum is None else write_sum + through_write
                passed = grad_state * write_now
                first_buf[tile, pl.ds(place * chunk, chunk), :] = passed[:half_size] + passed[half_size:]
                exponent = rates[tile] * decay_step[index, pl.ds(place, 1), cut(tile)]
                leaving = jnp.exp2(exponent) * grad_state
                incoming[tile] = leaving
                weighted = (leaving * earlier) * exponent
                second_buf[tile, pl.ds(place * chunk, chunk), :] = weighted[:half_size] + weighted[half_size:]
                decay_sums[tile] = decay_sums[tile] + weighted
            read_buf[token] += read_sum
            write_buf[token] += write_sum
        return (tuple(incoming), tuple(decay_sums), tuple(current))

    def backward(pair, carried):
        index = chunks - 1 - 2 * pair
        for here, first_buf, second_buf in ((index, first_a, second_a), (index - 1, first_b, second_b)):
            carried = retreat(here, carried, first_buf, second_buf)
            for tile in range(tiles):
                through_buf[here, :, cut(tile)] = folded(first_buf, tile)
                scaled_buf[here, :, cut(tile)] = folded(second_buf, tile)
        return carried

    incoming = tuple(incoming_buf[:, cut(tile)] for tile in range(tiles))
    nothing = (jnp.zeros((size, lanes), jnp.float32),) * tiles
    current = tuple(states_ref[rows - 1, :, cut(tile)] for tile in range(tiles))
    schedule = {}
    for which in range(count):
        for number in (1, 2, 3):
            schedule.setdefault((2, 4, 7, 9)[which] + (0, 3, 5)[number - 1], []).append((which, number))

    def move_on(legs):
        for which, number in legs:
            reduce.leg(which, number)

    carried = (incoming, nothing, current)
    for half_loop in range(2):
        for point, legs in sorted(schedule.items()):
            if point % 2 == half_loop:
                pl.when(moment == point // 2)(functools.partial(move_on, legs))
        carried = lax.fori_loop(half_loop * chunks // 4, (half_loop + 1) * chunks // 4, backward, carried)
    incoming, decay_sums, _ = carried
    for tile in range(tiles):
        incoming_buf[:, cut(tile)] = incoming[tile]
        decay_grad_ref[:, cut(tile)] += decay_sums[tile] * ln2
    skip = small_rows(small_ref, *plan["skip"])

    def after(index, at, carry):
        spot = pl.ds(pl.multiple_of(index * 4, 4), 4)
        sums = []
        for tile in range(tiles):
            signal = signal_ref[at, cut(tile)].astype(jnp.float32)
            step = step_ref[spot, :, cut(tile)].reshape(4 * chunk, lanes)
            through = through_buf[spot, :, cut(tile)].reshape(4 * chunk, lanes)
            scaled = scaled_buf[spot, :, cut(tile)].reshape(4 * chunk, lanes)
            core_grad = core_grad_ref[spot, :, cut(tile)].reshape(4 * chunk, lanes)
            grad_pre = (through * signal + ln2 * scaled / jnp.maximum(step, tiny)) * slope_of(step)
            low_buf[at, cut(tile)] = grad_pre.astype(low_buf.dtype)
            signal_grad_ref[at, cut(tile)] = (
                through * step + skip[:, tile * lanes : (tile + 1) * lanes] * core_grad
            )
            sums.append(carry[tile] + eight(grad_pre))
        return tuple(sums)

    zero_rows = jnp.zeros((8, lanes), jnp.float32)
    sums = row_loop(rows, 4 * chunk, after, (zero_rows,) * tiles)
    for tile in range(tiles):
        bias_grad_ref[:, cut(tile)] += jnp.sum(sums[tile], axis=0, keepdims=True)
    step_w_grad_ref[...] += contract(
        projected_ref[:, :rank].astype(low_buf.dtype), low_buf[...], 0, 0
    )
    step_w = small_ref[pl.ds(plan["step"][0], rank), :]
    step_w = jnp.concatenate([step_w, jnp.zeros((lanes - rank, width), step_w.dtype)], axis=0)
    rank_buf[pl.ds(group * chunks, chunks)] += contract(low_buf[...], step_w, 1, 1).reshape(
        chunks, chunk, lanes
    )

    @pl.when(moment == moments - 1)
    def _():
        squares = jnp.zeros((8, lanes), jnp.float32)
        for which in range(count):
            squares = squares + reduce.finish(which)[0]
        square_ref[...] = squares
        some = 8
        entry = lax.rem(lax.broadcasted_iota(jnp.int32, (some * chunk * size, lanes), 0), size)
        target = lax.broadcasted_iota(jnp.int32, (some * chunk * size, lanes), 1)
        ones = jnp.ones((lanes, lanes), jnp.bfloat16)

        def lay(index, carry):
            lot = pl.ds(index * some * chunk, some * chunk)
            for number, buffer in enumerate((write_buf, read_buf)):
                high, low = high_low(buffer[lot].reshape(some * chunk * size, lanes))
                summed = jnp.dot(high.astype(jnp.bfloat16), ones, preferred_element_type=jnp.float32)
                summed += jnp.dot(low.astype(jnp.bfloat16), ones, preferred_element_type=jnp.float32)
                summed = jnp.where(target == entry + rank + number * size, summed, 0.0)
                summed = jnp.sum(summed.reshape(some * chunk, size, lanes), axis=1)
                rank_buf[pl.ds(index * some, some)] += summed.reshape(some, chunk, lanes)
            return carry

        lax.fori_loop(0, rank_buf.shape[0] // some, lay, 0)
        flat_ref[...] = rank_buf[...].reshape(flat_ref.shape).astype(flat_ref.dtype)
        for which in range(count):
            reduce.settle(which)
        for index in range(pieces):
            for target, result in ((out_sum_ref, out_result), (in_sum_ref, gate_result)):
                each = result.shape[2]
                target[:, index * each : (index + 1) * each] = result[index]


def back_kernel(
    plan,
    dims,
    lengths_ref,
    tokens_ref,
    low_ref,
    gain_ref,
    small_ref,
    flat_ref,
    branch_ref,
    signal_ref,
    slope_ref,
    signal_grad_ref,
    gate_grad_ref,
    flipped_ref,
    branch_w,
    gate_w,
    step_w_grad_ref,
    bias_grad_ref,
    decay_grad_ref,
    skip_grad_ref,
    plain_ref,
    earlier_ref,
    tokens_grad_ref,
    in_sum_ref,
    small_sum_ref,
    late_sum_ref,
    norm_ref,
    offset_buf,
    conv_buf,
    mixed_buf,
    total,
    in_stage,
    small_stage,
    late_stage,
    late_land,
    norm_own,
    norm_land,
    in_result,
    small_result,
    direct_send,
    direct_recv,
    *parts,
):
    rows = tokens_ref.shape[0]
    width = branch_ref.shape[1]
    tiles = width // lanes
    block = pl.program_id(0)
    last = in_stage.shape[0]
    count = last + 1
    reduce = Reduce(
        dims,
        [small_stage] + [in_stage.at[index] for index in range(last)],
        parts[: 5 * count],
        parts[5 * count :],
        [small_result] + [in_result.at[index] for index in range(last)],
        True,
    )
    share = small_stage.shape[4]
    half_rows = small_stage.shape[3]
    planes = small_stage.shape[1]
    owners = small_stage.shape[0] * planes

    @pl.when(block == 0)
    def _():
        Place(dims).greet(everyone=True)
        fill_offsets(lengths_ref, offset_buf, rows)

    def move_on(plan_of_moves):
        for moment, legs in plan_of_moves:

            @pl.when(block == moment)
            def _(legs=legs):
                for which, number in legs:
                    reduce.leg(which, number)

    taps = small_rows(small_ref, *plan["taps"])
    taps_count = taps.shape[0]
    zero_rows = jnp.zeros((8, lanes), jnp.float32)

    @pl.when(block < last)
    def _():
        conv_buf[pl.ds(0, rows), :] = signal_grad_ref[...] + jnp.dot(
            flat_ref[...], small_ref[:lanes, :], preferred_element_type=jnp.float32
        )
        conv_buf[pl.ds(rows, 8), :] = jnp.zeros((8, width), jnp.float32)

        def through_conv(index, at, carry):
            sums = []
            for tile in range(tiles):
                grad_conv = conv_buf[at, cut(tile)] * slope_ref[at, cut(tile)]
                conv_buf[at, cut(tile)] = grad_conv
                sums.append(carry[tile] + eight(grad_conv))
            return tuple(sums)

        shift_sums = row_loop(rows, 32, through_conv, (zero_rows,) * tiles)
        def to_branch(index, at, carry):
            longer = pl.ds(pl.multiple_of(index * 32, 32), 40)
            offsets = offset_buf[longer, :]
            result = []
            for tile in range(tiles):
                here = slice(tile * lanes, (tile + 1) * lanes)
                grads = conv_buf[longer, cut(tile)]
                branch = branch_ref[at, cut(tile)]
                summed = taps[taps_count - 1 : taps_count, here] * grads[:32]
                sums = [None] * taps_count
                sums[taps_count - 1] = carry[tile][taps_count - 1] + eight(branch * grads[:32])
                for tap in range(taps_count - 1):
                    lag = taps_count - 1 - tap
                    moved = pltpu.roll(jnp.where(offsets >= lag, grads, 0.0), 40 - lag, 0)[:32]
                    summed = summed + taps[tap : tap + 1, here] * moved
                    sums[tap] = carry[tile][tap] + eight(branch * moved)
                mixed_buf[block, at, cut(tile)] = summed.astype(mixed_buf.dtype)
                result.append(tuple(sums))
            return tuple(result)

        sums = row_loop(rows, 32, to_branch, ((zero_rows,) * taps_count,) * tiles)
        in_grad = jnp.dot(flipped_ref[...], mixed_buf[block], preferred_element_type=jnp.float32)
        in_stage[block] = in_grad.reshape(in_stage.shape[1:]).astype(in_stage.dtype)
        for index in range(last):

            @pl.when(block == index)
            def _(index=index):
                reduce.start(index + 1)

        late = [
            jnp.concatenate(
                [jnp.sum(sums[tile][tap], axis=0, keepdims=True) for tap in range(taps_count)]
                + [jnp.sum(shift_sums[tile], axis=0, keepdims=True)]
                + [jnp.zeros((8 - taps_count - 1, lanes), jnp.float32)],
                axis=0,
            )
            for tile in range(tiles)
        ]
        late = jnp.concatenate(late, axis=1)
        for piece in range(width // share):
            late_stage[block * (width // share) + piece] = late[:, piece * share : (piece + 1) * share]
        move_on(
            (
                (1, ((1, 1), (0, 1))),
                (2, ((2, 1), (1, 2), (0, 2))),
                (3, ((3, 1), (2, 2), (1, 3), (0, 3))),
            )
        )

        @pl.when(block == 0)
        def _():
            select_grad = contract(flat_ref[...], signal_ref[...], 0, 0)
            step_first, step_tall = plan["step"]
            filler = jnp.zeros((2 * half_rows - step_first - step_tall, select_grad.shape[1]), jnp.float32)
            pieces = {
                "decay": decay_grad_ref[...],
                "bias": bias_grad_ref[...],
                "skip": skip_grad_ref[...],
                "step": step_w_grad_ref[...],
            }
            first = plan["select"][1]
            rows_now = [select_grad[:first]]
            for name in ("decay", "taps", "shift", "bias", "skip", "gain"):
                tall = plan[name][1]
                rows_now.append(
                    pieces[name] if name in pieces else jnp.zeros((tall, select_grad.shape[1]), jnp.float32)
                )
                first += tall
            rows_now.append(jnp.zeros((step_first - first, select_grad.shape[1]), jnp.float32))
            rows_now.append(pieces["step"])
            if filler.shape[0]:
                rows_now.append(filler)
            everything = jnp.concatenate(rows_now, axis=0)
            for owner in range(owners):
                for side in range(2):
                    small_stage[owner // planes, owner % planes, side] = everything[
                        side * half_rows : (side + 1) * half_rows, owner * share : (owner + 1) * share
                    ].astype(small_stage.dtype)
            reduce.start(0)

    @pl.when(block >= last)
    def _():
        grad_normed_piece = contract(mixed_buf[block - last], rows_of(branch_w), 1, 1)
        grad_normed_piece += contract(gate_grad_ref[...], rows_of(gate_w), 1, 1)

        @pl.when(block == last)
        def _():
            total[...] = grad_normed_piece

        @pl.when(block > last)
        def _():
            total[...] += grad_normed_piece

        move_on(((4, ((3, 2),)), (5, ((4, 1), (2, 3))), (6, ((3, 3),)), (7, ((4, 2),))))

    @pl.when(block == pl.num_programs(0) - 1)
    def _():
        def finish(index, at, carry):
            residual = tokens_ref[at, :].astype(jnp.float32)
            scale = lax.rsqrt(jnp.mean(residual * residual, axis=1, keepdims=True) + epsilon)
            grad_normed = total[at, :]
            weighted = grad_normed * gain_ref[...]
            inner = jnp.mean(weighted * residual, axis=1, keepdims=True)
            grad_y = low_ref[at, :].astype(jnp.float32)
            result = grad_y + (scale * weighted - residual * (scale * scale * scale) * inner)
            tokens_grad_ref[at, :] = result.astype(tokens_grad_ref.dtype)
            return carry + eight(grad_normed * residual * scale)

        gains = row_loop(rows, 16, finish, jnp.zeros((8, total.shape[1]), jnp.float32))
        gains = jnp.sum(gains, axis=0, keepdims=True)
        place = Place(dims)
        each = gains.shape[1] // owners
        for owner in range(owners):
            late_stage[owner, taps_count + 1 : taps_count + 2, :each] = gains[
                :, owner * each : (owner + 1) * each
            ]
        late_sems = direct_send.at[0], direct_recv.at[0]
        norm_sems = direct_send.at[1], direct_recv.at[1]
        send_to_everyone(place, lambda chip: late_stage.at[chip], late_land, *late_sems)
        reduce.leg(4, 3)
        more, plain = reduce.finish(0, plain_ref)
        kept = earlier_ref[...] + more
        for index in range(1, count - 1):
            kept = kept + reduce.finish(index)[0]
        late_sum = sum_of_everyone(place, late_stage[place.me], late_land, *late_sems)
        late_sum_ref[...] = late_sum
        kept = kept + folded_squares(late_sum * late_sum) * (1 - place.core).astype(jnp.float32)
        kept = kept + reduce.finish(count - 1)[0]
        norm_own[...] = jnp.stack([kept, plain])
        send_to_everyone(place, lambda chip: norm_own, norm_land, *norm_sems)
        norm_ref[...] = sum_of_everyone(place, norm_own[...], norm_land, *norm_sems)
        for index in range(count):
            reduce.settle(index)
        for index in range(last):
            in_sum_ref[:, index * width : (index + 1) * width] = in_result[index]
        small_sum_ref[...] = small_result[...]


def finish_kernel(
    plan, names, late, tokens_ref, branch_ref, gate_ref, out_ref, small_ref, late_ref, norm_ref, *outs
):
    middle = branch_ref.shape[1]
    outs[0][:, :middle] = branch_ref[...]
    outs[0][:, middle:] = gate_ref[...]
    outs[1][...] = out_ref[...]
    outs[2][...] = tokens_ref[...]
    for name, target in zip(names, outs[3 : 3 + len(names)]):
        source, (first, count) = (late_ref, late[name]) if name in late else (small_ref, plan[name])
        if len(target.shape) == 1:
            target[...] = source[first, : target.shape[0]]
        else:
            target[...] = source[first : first + count, :]
    for index in range(2):
        outs[3 + len(names) + index][0, 0] = jnp.sum(norm_ref[index])


def shape(dims, kind=jnp.float32):
    return jax.ShapeDtypeStruct(dims, kind)


def compute_call(
    kernel, name, blocks, in_specs, out_specs, out_shape, scratch, flops, operands, collective_id=None
):
    return pl.pallas_call(
        kernel,
        grid=blocks if isinstance(blocks, tuple) else (blocks,),
        in_specs=in_specs,
        out_specs=out_specs,
        out_shape=out_shape,
        scratch_shapes=scratch,
        compiler_params=pltpu.CompilerParams(
            dimension_semantics=("arbitrary",) * (len(blocks) if isinstance(blocks, tuple) else 1),
            vmem_limit_bytes=62 * 1024 * 1024,
            collective_id=collective_id,
            has_side_effects=collective_id is not None,
        ),
        cost_estimate=pl.CostEstimate(flops=flops, bytes_accessed=40 << 20, transcendentals=0),
        name=name,
    )(*operands)


class Place:
    def __init__(self, dims, swapped=False):
        depth, tall, wide = dims
        self.dims = dims
        self.core = lax.axis_index("wide")
        self.me = lax.axis_index("narrow")
        self.across = lax.rem(self.me, wide)
        self.up = lax.rem(lax.div(self.me, wide), tall)
        self.deep = lax.div(self.me, wide * tall)
        side = 1 - self.core if swapped else self.core
        turn = side if tall == wide else 0
        self.second = (1 + turn * (wide - 1), self.across + turn * (self.up - self.across), wide)
        self.third = (wide - turn * (wide - 1), self.up + turn * (self.across - self.up), tall)
        self.spans = (depth, wide, tall)
        self.other = {"wide": 1 - self.core}

    def level(self, d):
        return lax.rem(self.deep + d, self.spans[0])

    def plane(self, e, f):
        return (
            lax.rem(self.second[1] + e, self.second[2]) * self.second[0]
            + lax.rem(self.third[1] + f, self.third[2]) * self.third[0]
        )

    def plane_behind(self, e, f):
        return self.plane((self.spans[1] - e) % self.spans[1], (self.spans[2] - f) % self.spans[2])

    def at(self, d, e, f):
        return {"narrow": self.level(d) * (self.dims[1] * self.dims[2]) + self.plane(e, f)}

    def greet(self, everyone=False):
        barrier = pltpu.get_barrier_semaphore()
        peers = [self.other]
        if everyone:
            number = self.spans[0] * self.spans[1] * self.spans[2]
            for hop in range(1, number):
                chip = lax.rem(self.me + hop, number)
                peers += [{"narrow": chip}, {"wide": 1 - self.core, "narrow": chip}]
        else:
            for axis, size in enumerate(self.spans):
                for hop in range(1, size):
                    move = [0, 0, 0]
                    move[axis] = hop
                    peers.append(self.at(*move))
        for peer in peers:
            pl.semaphore_signal(barrier, inc=1, device_id=peer, device_id_type=pl.DeviceIdType.MESH)
        pl.semaphore_wait(barrier, len(peers))


def by_rows(block):
    return block[0] % 32 == 0


def half_shape(block):
    if len(block) == 3:
        return tuple(block[1:])
    return (block[0] // 2, block[1]) if by_rows(block) else (block[0], block[1] // 2)


def half(view, block, side, lead=0):
    ahead = (slice(None),) * lead
    if len(block) == 3:
        return view.at[ahead + (side,)]
    if by_rows(block):
        return view.at[ahead + (pl.ds(pl.multiple_of(side * (block[0] // 2), 16), block[0] // 2),)]
    columns = pl.ds(pl.multiple_of(side * (block[1] // 2), lanes), block[1] // 2)
    return view.at[ahead + (slice(None), columns)]


def remote(source, target, send_sem, recv_sem, device):
    return pltpu.make_async_remote_copy(
        src_ref=source,
        dst_ref=target,
        send_sem=send_sem,
        recv_sem=recv_sem,
        device_id=device,
        device_id_type=pl.DeviceIdType.MESH,
    )


class Gather:
    def __init__(self, dims, own, whole, sems, blocks=None):
        self.dims, self.own, self.whole = dims, own, whole
        self.local_sem, self.send_sem, self.recv_sem = sems
        self.lined = blocks is not None
        self.blocks = blocks or [block.shape for block in own]

    @staticmethod
    def sems(count, dims):
        copies = dims[0] + 2 * dims[1] * dims[2]
        return [pltpu.SemaphoreType.DMA((count,))] + [pltpu.SemaphoreType.DMA((count, copies))] * 2

    def line(self, which, plane, side):
        return half(self.whole[which].at[:, plane], self.blocks[which], side, 1)

    def local(self, place, which):
        block = self.blocks[which]
        if self.lined:
            return pltpu.make_async_copy(
                self.own[which], self.line(which, place.plane(0, 0), place.core), self.local_sem.at[which]
            )
        return pltpu.make_async_copy(
            half(self.own[which], block, place.core),
            half(self.whole[which].at[place.deep, place.plane(0, 0)], block, place.core),
            self.local_sem.at[which],
        )

    def copy(self, which, source, target, index, device):
        return remote(
            source, target, self.send_sem.at[which, index], self.recv_sem.at[which, index], device
        )

    def rise(self, place, which, hop):
        block = self.blocks[which]
        return self.copy(
            which,
            half(self.own[which], block, place.core),
            half(self.whole[which].at[place.deep, place.plane(0, 0)], block, place.core),
            hop,
            place.at(hop, 0, 0),
        )

    def leg_index(self, e, f):
        return self.dims[0] + e * self.dims[1] + f

    def hand_index(self, e, f):
        return self.leg_index(e, f) + self.dims[1] * self.dims[2]

    def onward(self, place, which, e, f):
        line = self.line(which, place.plane_behind(e, f), place.core)
        source = self.own[which] if self.lined and e == 0 and f == 0 else line
        if f == 0:
            for hop in range(1, place.spans[2]):
                self.copy(which, source, line, self.leg_index(e, hop), place.at(0, 0, hop)).start()
        if f == 0 and e == 0:
            for hop in range(1, place.spans[1]):
                self.copy(which, source, line, self.leg_index(hop, 0), place.at(0, hop, 0)).start()
        self.copy(which, source, line, self.hand_index(e, f), place.other).start()

    def start(self, which):
        place = Place(self.dims)
        if self.lined:
            self.onward(place, which, 0, 0)
            self.local(place, which).start()
            return
        for hop in range(1, place.spans[0]):
            self.rise(place, which, hop).start()
        self.local(place, which).start()

    def leg(self, which, number):
        place = Place(self.dims)
        if number == 1:
            self.local(place, which).wait()
            for hop in range(1, place.spans[0]):
                self.rise(place, which, hop).wait_recv()
            self.onward(place, which, 0, 0)
            return
        for e in range(place.spans[1]):
            for f in range(place.spans[2]):
                if (number == 2 and f == 0 and e > 0) or (number == 3 and f > 0):
                    line = self.line(which, place.plane_behind(e, f), place.core)
                    self.copy(which, line, line, self.leg_index(e, f), place.other).wait_recv()
                    self.onward(place, which, e, f)

    def arrive(self, which):
        place, mirror = Place(self.dims), Place(self.dims, swapped=True)
        for e in range(place.spans[1]):
            for f in range(place.spans[2]):
                line = self.line(which, mirror.plane_behind(e, f), 1 - place.core)
                self.copy(which, line, line, self.hand_index(e, f), place.other).wait_recv()

    def drain(self, which):
        place = Place(self.dims)
        if self.lined:
            self.local(place, which).wait()
        else:
            for hop in range(1, place.spans[0]):
                self.rise(place, which, hop).wait_send()
        for e in range(place.spans[1]):
            for f in range(place.spans[2]):
                line = self.line(which, place.plane_behind(e, f), place.core)
                if e > 0 or f > 0:
                    self.copy(which, line, line, self.leg_index(e, f), place.other).wait_send()
                self.copy(which, line, line, self.hand_index(e, f), place.other).wait_send()


class Rise:
    def __init__(self, dims, own, lines, sems):
        self.dims, self.own, self.lines = dims, own, lines
        self.local_sem, self.send_sem, self.recv_sem = sems

    @staticmethod
    def sems(count, dims):
        return [pltpu.SemaphoreType.DMA((count,))] + [pltpu.SemaphoreType.DMA((count, dims[0]))] * 2

    def copies(self, place, which):
        source = half(self.own[which], self.own[which].shape, place.core)
        target = self.lines[which].at[place.deep]
        local = pltpu.make_async_copy(source, target, self.local_sem.at[which])
        return local, [
            remote(
                source, target, self.send_sem.at[which, hop], self.recv_sem.at[which, hop], place.at(hop, 0, 0)
            )
            for hop in range(1, place.spans[0])
        ]

    def start(self, which):
        local, sends = self.copies(Place(self.dims), which)
        for copy in [*sends, local]:
            copy.start()

    def finish(self, which):
        local, sends = self.copies(Place(self.dims), which)
        local.wait()
        for copy in sends:
            copy.wait_recv()
            copy.wait_send()


class Reduce:
    def __init__(self, dims, grads, rooms, sems, results, resident):
        self.dims, self.grads, self.resident = dims, grads, resident
        count = len(grads)
        self.mine, self.swapped, self.third, self.second, self.first = (
            rooms[index * count : (index + 1) * count] for index in range(5)
        )
        self.loaded = None if resident else rooms[5 * count :]
        self.load_sem, self.swap_send, self.swap_recv, self.send_sem, self.recv_sem = sems[:5]
        self.last_send, self.last_recv = sems[5:]
        self.results = results

    @staticmethod
    def rooms(dims, grads, resident):
        depth, tall, wide = dims
        leads = (
            (tall, wide, depth),
            (depth, tall * wide),
            (tall - 1, wide, depth),
            (wide - 1, depth),
            (depth - 1,),
        )
        if not resident:
            leads += ((depth, tall * wide),)
        return [
            pltpu.VMEM(lead + half_shape(grad.shape[2:]), grad.dtype) for lead in leads for grad in grads
        ]

    @staticmethod
    def sems(count, dims):
        return (
            [pltpu.SemaphoreType.DMA((count,))] * 3
            + [pltpu.SemaphoreType.DMA((count, dims[0] + dims[1] + dims[2]))] * 2
            + [pltpu.SemaphoreType.DMA((count,))] * 2
        )

    def block(self, which):
        return self.grads[which].shape[2:]

    def load(self, place, which):
        return pltpu.make_async_copy(
            half(self.grads[which], self.block(which), place.core, 2),
            self.loaded[which],
            self.load_sem.at[which],
        )

    def swap(self, place, which):
        return remote(
            half(self.grads[which], self.block(which), 1 - place.core, 2),
            self.swapped[which],
            self.swap_send.at[which],
            self.swap_recv.at[which],
            place.other,
        )

    def hop(self, which, source, target, index, device):
        return remote(
            source, target, self.send_sem.at[which, index], self.recv_sem.at[which, index], device
        )

    def third_hop(self, place, which, f):
        return self.hop(which, self.mine[which].at[f], self.third[which].at[f - 1], f, place.at(0, 0, f))

    def second_hop(self, place, which, e):
        return self.hop(
            which,
            self.mine[which].at[0, e],
            self.second[which].at[e - 1],
            self.dims[1] + e,
            place.at(0, e, 0),
        )

    def first_hop(self, place, which, d):
        return self.hop(
            which,
            self.mine[which].at[0, 0, place.level(d)],
            self.first[which].at[d - 1],
            self.dims[1] + self.dims[2] + d,
            place.at(d, 0, 0),
        )

    def start(self, which):
        place = Place(self.dims)
        self.swap(place, which).start()
        if not self.resident:
            self.load(place, which).start()

    def parts(self, place, which, e, f, z):
        plane = place.plane(e, f)
        if self.resident:
            found = [half(self.grads[which].at[z, plane], self.block(which), place.core)]
        else:
            found = [self.loaded[which].at[z, plane]]
        found.append(self.swapped[which].at[z, plane])
        if f == 0:
            found += [self.third[which].at[hop - 1, e, z] for hop in range(1, place.spans[2])]
        if f == 0 and e == 0:
            found += [self.second[which].at[hop - 1, z] for hop in range(1, place.spans[1])]
        return found

    def ready(self, place, which):
        if not self.resident:
            self.load(place, which).wait()
        self.swap(place, which).wait_recv()

    def added(self, parts, store, carry):
        rows = parts[0].shape[0]
        group = min(rows, 16)

        def some(index, carry):
            at_rows = pl.ds(pl.multiple_of(index * group, group), group)
            total = parts[0][at_rows, :].astype(jnp.float32)
            for part in parts[1:]:
                total = total + part[at_rows, :].astype(jnp.float32)
            return store(at_rows, total, carry)

        return lax.fori_loop(0, rows // group, some, carry)

    def sum_into(self, place, which, e, f, z):
        target = self.mine[which].at[f, e, z]

        def keep(at_rows, total, carry):
            target[at_rows, :] = total.astype(target.dtype)
            return carry

        self.added(self.parts(place, which, e, f, z), keep, 0)

    def leg(self, which, number):
        place = Place(self.dims)
        depth, span_e, span_f = place.spans
        if number == 1:
            self.ready(place, which)
            for f in range(span_f - 1, 0, -1):
                for e in range(span_e - 1, -1, -1):
                    for z in range(depth):
                        self.sum_into(place, which, e, f, z)
                self.third_hop(place, which, f).start()
        elif number == 2:
            for f in range(1, span_f):
                self.third_hop(place, which, f).wait_recv()
            for e in range(span_e - 1, 0, -1):
                for z in range(depth):
                    self.sum_into(place, which, e, 0, z)
                self.second_hop(place, which, e).start()
        else:
            if span_e == 1:
                for f in range(1, span_f):
                    self.third_hop(place, which, f).wait_recv()
            for e in range(1, span_e):
                self.second_hop(place, which, e).wait_recv()
            for d in range(1, depth):
                self.sum_into(place, which, 0, 0, place.level(d))
                self.first_hop(place, which, d).start()

    def result(self, which, side):
        return half(self.results[which], self.block(which), side)

    def last(self, place, which, side):
        share = self.result(which, side)
        return remote(share, share, self.last_send.at[which], self.last_recv.at[which], place.other)

    def finish(self, which, marks=None):
        place = Place(self.dims)
        parts = self.parts(place, which, 0, 0, place.deep)
        for d in range(1, place.spans[0]):
            self.first_hop(place, which, d).wait_recv()
            parts.append(self.first[which].at[d - 1])
        share = self.result(which, place.core)

        def store(at_rows, total, carry):
            share[at_rows, :] = total
            kept, plain = carry
            squared = total * total
            if marks is not None:
                marked = squared * marks[place.core, at_rows, :]
                plain = plain + folded_squares(marked)
                squared = squared - marked
            return (kept + folded_squares(squared), plain)

        squares = self.added(parts, store, (jnp.zeros((8, lanes), jnp.float32),) * 2)
        self.last(place, which, place.core).start()
        return squares

    def settle(self, which):
        place = Place(self.dims)
        last = self.last(place, which, 1 - place.core)
        last.wait_recv()
        last.wait_send()
        self.swap(place, which).wait_send()
        for f in range(1, place.spans[2]):
            self.third_hop(place, which, f).wait_send()
        for e in range(1, place.spans[1]):
            self.second_hop(place, which, e).wait_send()
        for d in range(1, place.spans[0]):
            self.first_hop(place, which, d).wait_send()


def folded_squares(values):
    total = None
    if values.shape[1] < lanes:
        first = lax.broadcasted_iota(jnp.int32, (values.shape[0], lanes), 1) == 0
        values = jnp.where(first, jnp.sum(values, axis=1, keepdims=True), 0.0)
    for row in range(0, values.shape[0], 8):
        for column in range(0, values.shape[1], lanes):
            piece = values[row : row + 8, column : column + lanes]
            total = piece if total is None else total + piece
    return total


def send_to_all(place, source, landing, send_sem, recv_sem):
    number = landing.shape[0]
    for hop in range(1, number):
        target = lax.rem(place.me + hop, number)
        remote(
            source(target), landing.at[place.me], send_sem.at[hop], recv_sem.at[hop], {"narrow": target}
        ).start()


def wait_for_all(place, own, landing, send_sem, recv_sem):
    number = landing.shape[0]
    landing[place.me] = own
    for hop in range(1, number):
        came = landing.at[lax.rem(place.me + number - hop, number)]
        copy = remote(came, came, send_sem.at[hop], recv_sem.at[hop], place.other)
        copy.wait_recv()
        copy.wait_send()


def send_to_everyone(place, source, landing, send_sem, recv_sem):
    number = landing.shape[1]
    target = landing.at[place.core, place.me]

    def send(hop, carry):
        chip = lax.rem(place.me + hop, number)
        for turn in range(2):
            device = {"wide": lax.rem(place.core + turn, 2), "narrow": chip}
            remote(source(chip), target, send_sem.at[turn, hop], recv_sem.at[turn, hop], device).start()
        return carry

    lax.fori_loop(1, number, send, 0)
    remote(source(place.me), target, send_sem.at[1, 0], recv_sem.at[1, 0], place.other).start()


def sum_of_everyone(place, own, landing, send_sem, recv_sem):
    number = landing.shape[1]
    landing[place.core, place.me] = own

    def wait(turn, hop):
        came = landing.at[lax.rem(place.core + turn, 2), lax.rem(place.me + number - hop, number)]
        copy = remote(came, came, send_sem.at[turn, hop], recv_sem.at[turn, hop], place.other)
        copy.wait_recv()
        copy.wait_send()

    def wait_both(hop, carry):
        wait(0, hop)
        wait(1, hop)
        return carry

    lax.fori_loop(1, number, wait_both, 0)
    wait(1, 0)

    def add(spot, total):
        return total + landing[0, spot] + landing[1, spot]

    return lax.fori_loop(1, number, add, landing[0, 0] + landing[1, 0])


def grid_of(mesh):
    number = mesh.shape["narrow"]
    places = [getattr(device, "coords", None) for device in mesh.devices[0]]
    if all(place is not None for place in places):
        sizes = [len({place[axis] for place in places}) for axis in (2, 1, 0)]
        if sizes[0] * sizes[1] * sizes[2] == number:
            return tuple(sizes)
    side = round((number / 2) ** (1 / 3))
    return (2 * side, side, side) if 2 * side**3 == number else (number, 1, 1)


def plan_of(select_rows, state_size, tap_count, step_rows):
    plan, first = {}, 0
    for name, tall in (
        ("select", select_rows),
        ("decay", state_size),
        ("taps", tap_count),
        ("shift", 1),
        ("bias", 1),
        ("skip", 1),
        ("gain", 1),
    ):
        plan[name] = (first, tall)
        first += tall
    plan["step"] = (lanes, step_rows)
    plan["rows"] = -(-(lanes + step_rows) // 32) * 32
    return plan


def per_device(
    dims,
    tokens,
    cotangent,
    loss_mask,
    seq_lengths,
    norm_gain,
    in_proj,
    conv_weight,
    conv_bias,
    select_proj,
    step_proj,
    step_bias,
    decay_log,
    skip_scale,
    out_proj,
):
    half = jnp.bfloat16
    piece = skip_scale.shape[0]
    gain_piece = norm_gain.shape[0]
    rank, size = step_proj.shape[0], decay_log.shape[0]
    plan = plan_of(select_proj.shape[0], size, conv_weight.shape[0], rank)
    smalls = {
        "select": select_proj,
        "decay": decay_log,
        "taps": conv_weight,
        "shift": conv_bias[None],
        "bias": step_bias[None],
        "skip": skip_scale[None],
        "gain": norm_gain[None],
        "step": step_proj,
    }
    depth, planes = dims[0], dims[1] * dims[2]
    number = depth * planes
    in_rows = in_proj.shape[0]
    rows, model = tokens.shape
    inner = piece * number
    width = 4 * lanes
    blocks = inner // width
    chunks = rows // chunk
    mask_row = loss_mask[None]

    whole = pl.BlockSpec(memory_space=pltpu.VMEM)
    tall = pl.BlockSpec((rows, width), lambda b: (0, b))
    deep = pl.BlockSpec((chunks, chunk, width), lambda b: (0, 0, b))
    lead = pl.BlockSpec((rows, size, width), lambda b: (0, 0, b))
    first_w = pl.BlockSpec((model, width), lambda b: (0, b))
    second_w = pl.BlockSpec((model, width), lambda b: (0, b + blocks))
    out_w = pl.BlockSpec((width, model), lambda b: (b, 0))

    def thin(height):
        return pl.BlockSpec((height, width), lambda b: (0, b))

    def fixed(*dims_of):
        return pl.BlockSpec(dims_of, lambda b: (0,) * len(dims_of))

    scalars = pl.BlockSpec(memory_space=pltpu.SMEM)
    offset_buf = pltpu.VMEM((rows + 8, lanes), jnp.int32)
    packed = thin(plan["rows"])

    pair = (chunks, 2 * chunk, lanes)
    pair = (chunks, 2 * chunk, lanes)
    anywhere = pl.BlockSpec(memory_space=pl.ANY)
    small_half = (2, plan["rows"] // 2, piece)
    in_piece = (in_rows, width)
    shares = 2
    in_share = (in_rows, inner // shares)
    out_share = (out_proj.shape[0], model // shares)
    lines = [shape((shares, depth) + half_shape(block), half) for block in (in_share, out_share)]
    (
        branch,
        signal,
        slope,
        projected,
        flipped,
        normed,
        grad_low,
        write_pair,
        read_pair,
        small,
        gain_value,
        in_blocks,
        gate_lines,
        out_lines,
    ) = compute_call(
        functools.partial(front_kernel, plan, dims, tuple(smalls)),
        "front",
        blocks,
        [scalars, whole, whole, whole] + [whole] * len(smalls) + [whole] * 2,
        [tall, tall, tall] + [whole] * 8 + [anywhere] * 3,
        [
            shape((rows, inner)),
            shape((rows, inner), half),
            shape((rows, inner)),
            shape((rows, lanes)),
            shape((model, rows), half),
            shape((rows, model), half),
            shape((rows, model), half),
            shape(pair, half),
            shape(pair, half),
            shape((plan["rows"], inner), half),
            shape((1, model)),
            shape((blocks, depth, planes) + in_piece, half),
            *lines,
        ],
        [
            offset_buf,
            pltpu.VMEM((plan["rows"], piece), jnp.float32),
            pltpu.VMEM(small_half, half),
            pltpu.VMEM((blocks,) + in_piece, half),
            pltpu.VMEM((shares,) + in_share, half),
            pltpu.VMEM((shares,) + out_share, half),
            pltpu.VMEM((depth, planes) + small_half, half),
            pltpu.VMEM((blocks, depth, planes) + in_piece, half),
            pltpu.SemaphoreType.DMA((blocks,)),
            pltpu.VMEM((8, piece), jnp.float32),
            pltpu.VMEM((number, 8, piece), jnp.float32),
            pltpu.SemaphoreType.DMA((number,)),
            pltpu.SemaphoreType.DMA((number,)),
        ]
        + Gather.sems(1 + blocks, dims)
        + Rise.sems(2 * shares, dims),
        4 * rows * model * inner,
        (seq_lengths, tokens, cotangent, mask_row, *smalls.values(), in_proj, out_proj),
        collective_id=0,
    )
    groups = 2
    part, pieces = rows // groups, chunks // groups
    row_block = pltpu.VMEM((pieces, chunk, width), jnp.float32)
    spread_block = pltpu.VMEM((rows, size, lanes), jnp.float32)
    fold_block = pltpu.VMEM((width // lanes, chunk * chunk, lanes), jnp.float32)

    def by_group(order, *dims_of):
        middle = (0,) * (len(dims_of) - 2)
        return pl.BlockSpec(dims_of, lambda b, g: (order(g),) + middle + (b,))

    def by_token(order, *dims_of):
        return pl.BlockSpec(dims_of, lambda b, g: (order(g),) + (0,) * (len(dims_of) - 1))

    def by_channel(height):
        return pl.BlockSpec((height, width), lambda b, g: (0, b))

    def onward(g):
        return g

    def backward(g):
        return groups - 1 - g

    states, step, core, begins, gate_blocks, out_blocks = compute_call(
        functools.partial(forward_kernel, plan, dims),
        "forward",
        (blocks, groups),
        [
            scalars,
            by_token(onward, part, lanes),
            by_channel(plan["rows"]),
            by_group(onward, part, width),
            whole,
            whole,
            anywhere,
            anywhere,
        ],
        [
            by_group(onward, part, size, width),
            by_group(onward, pieces, chunk, width),
            by_group(onward, pieces, chunk, width),
            by_group(onward, 1, size, width),
            anywhere,
            anywhere,
        ],
        [
            shape((rows, size, inner)),
            shape((chunks, chunk, inner)),
            shape((chunks, chunk, inner)),
            shape((groups, size, inner)),
            shape((shares, depth, planes) + in_share, half),
            shape((shares, depth, planes) + out_share, half),
        ],
        [
            offset_buf,
            pltpu.VMEM((part, width), jnp.float32),
            row_block,
            row_block,
            spread_block,
            spread_block,
            fold_block,
            fold_block,
            pltpu.VMEM((size, width), jnp.float32),
        ]
        + Gather.sems(2 * shares, dims),
        15 * rows * inner * size,
        (seq_lengths, projected, small, signal, write_pair, read_pair, gate_lines, out_lines),
        collective_id=2,
    )
    split = in_share[1] // width
    weights = pl.BlockSpec((None, number, in_rows, width), lambda b: (b // split, 0, 0, b % split))
    per_block = width // out_share[0]
    out_pieces = pl.BlockSpec((shares, per_block) + out_share, lambda b: (0, b, 0, 0))
    branch_whole = in_blocks.reshape(blocks, number, *in_piece)
    gate_whole = gate_blocks.reshape(shares, number, *in_share)
    out_whole = out_blocks.reshape(shares, number, *out_share)
    core_grad, gate_grad, grad_skip, grad_outw, grad_in_gate, output = compute_call(
        functools.partial(middle_kernel, plan),
        "middle",
        blocks,
        [deep, packed, tall, weights, whole, out_pieces, whole, whole, whole],
        [
            deep,
            tall,
            thin(1),
            pl.BlockSpec((shares, width, out_share[1]), lambda b: (0, b, 0)),
            pl.BlockSpec((None, model, width), lambda b: (b // split, 0, b % split)),
            fixed(rows, model),
        ],
        [
            shape((chunks, chunk, inner)),
            shape((rows, inner), half),
            shape((1, inner)),
            shape((shares, inner, out_share[1]), half),
            shape((shares, model, in_share[1]), half),
            shape((rows, model), half),
        ],
        [
            pltpu.VMEM((rows, width), jnp.float32),
            pltpu.VMEM((rows, width), jnp.float32),
            pltpu.VMEM((rows, width), half),
            pltpu.VMEM((width, model), half),
            pltpu.VMEM((rows, model), jnp.float32),
        ],
        8 * rows * model * inner,
        (core, small, signal, gate_whole, grad_low, out_whole, flipped, normed, tokens),
    )
    early_grads = [
        grad_outw.reshape((shares, depth, planes) + out_share),
        grad_in_gate.reshape((shares, depth, planes) + in_share),
    ]
    early_sums = [shape(out_proj.shape), shape((in_rows, inner))]
    early_pieces = [shape((depth, planes) + block, half) for block in (in_share, out_share)] * shares
    (
        signal_grad,
        grad_stepw,
        grad_bias,
        grad_decaylog,
        flat,
        out_sum,
        in_gate_sum,
        early_squares,
    ) = compute_call(
        functools.partial(backward_kernel, plan, dims),
        "backward",
        (blocks, groups),
        [
            scalars,
            by_token(backward, part, lanes),
            by_channel(plan["rows"]),
            by_group(backward, part, width),
            whole,
            whole,
            by_group(backward, pieces, chunk, width),
            by_group(backward, pieces, chunk, width),
            by_group(backward, part, size, width),
            by_group(backward, 1, size, width),
            anywhere,
            anywhere,
        ],
        [
            by_group(backward, part, width),
            by_channel(rank),
            by_channel(1),
            by_channel(size),
            whole,
        ]
        + [whole] * 3,
        [
            shape((rows, inner)),
            shape((rank, inner)),
            shape((1, inner)),
            shape((size, inner)),
            shape((rows, lanes), half),
            *early_sums,
            shape((8, lanes)),
        ],
        [
            offset_buf,
            row_block,
            row_block,
            spread_block,
            spread_block,
            fold_block,
            fold_block,
            fold_block,
            fold_block,
            row_block,
            row_block,
            pltpu.VMEM((part, width), half),
            pltpu.VMEM((size, width), jnp.float32),
            pltpu.VMEM((chunks, chunk, lanes), jnp.float32),
            spread_block,
            spread_block,
        ]
        + [pltpu.VMEM((shares,) + block, jnp.float32) for block in (in_share, out_share)]
        + Reduce.rooms(dims, early_pieces, False)
        + Reduce.sems(2 * shares, dims),
        40 * rows * inner * size,
        (
            seq_lengths,
            projected,
            small,
            signal,
            write_pair,
            read_pair,
            step,
            core_grad,
            states,
            begins,
            *early_grads,
        ),
        collective_id=3,
    )

    plain_rows = np.zeros((plan["rows"], piece), np.float32)
    for name in ("bias", "decay", "skip"):
        first, count = plan[name]
        plain_rows[first : first + count] = 1.0
    late_grads = [shape((depth, planes) + small_half, half)]
    late_grads += [shape((depth, planes, in_rows, width), half)] * blocks
    taps_n = conv_weight.shape[0]
    late = {"taps": (0, taps_n), "shift": (taps_n, 1), "gain": (taps_n + 1, 1)}
    late_block = (8, piece)

    early_tall = pl.BlockSpec((rows, width), lambda b: (0, jnp.minimum(b, blocks - 1)))
    late_tall = pl.BlockSpec((rows, width), lambda b: (0, jnp.maximum(b - blocks, 0)))
    tokens_grad, in_branch_sum, small_sum, late_sum, norms = compute_call(
        functools.partial(back_kernel, plan, dims),
        "back",
        2 * blocks,
        [scalars, whole, whole, whole]
        + [pl.BlockSpec((plan["rows"], width), lambda b: (0, jnp.minimum(b, blocks - 1))), whole]
        + [early_tall, whole, early_tall, early_tall, late_tall, whole]
        + [
            pl.BlockSpec((None, number, in_rows, width), lambda b: (jnp.maximum(b - blocks, 0), 0, 0, 0)),
            pl.BlockSpec(
                (None, number, in_rows, width),
                lambda b: (jnp.maximum(b - blocks, 0) // split, 0, 0, jnp.maximum(b - blocks, 0) % split),
            ),
        ]
        + [whole] * 6,
        [whole] * 5,
        [
            shape((rows, model), half),
            shape((in_rows, inner)),
            shape(small_half),
            shape(late_block),
            shape((2, 8, lanes)),
        ],
        [
            offset_buf,
            pltpu.VMEM((rows + 8, width), jnp.float32),
            pltpu.VMEM((blocks, rows, width), half),
            pltpu.VMEM((rows, model), jnp.float32),
            pltpu.VMEM((blocks,) + late_grads[1].shape, half),
            pltpu.VMEM(late_grads[0].shape, late_grads[0].dtype),
            pltpu.VMEM((number,) + late_block, jnp.float32),
            pltpu.VMEM((2, number) + late_block, jnp.float32),
            pltpu.VMEM((2, 8, lanes), jnp.float32),
            pltpu.VMEM((2, number, 2, 8, lanes), jnp.float32),
            pltpu.VMEM((blocks, in_rows, width), jnp.float32),
            pltpu.VMEM(small_half, jnp.float32),
            pltpu.SemaphoreType.DMA((2, 2, number)),
            pltpu.SemaphoreType.DMA((2, 2, number)),
        ]
        + Reduce.rooms(dims, late_grads, True)
        + Reduce.sems(blocks + 1, dims),
        8 * rows * model * inner,
        (
            seq_lengths,
            tokens,
            grad_low,
            gain_value,
            small,
            flat,
            branch,
            signal,
            slope,
            signal_grad,
            gate_grad,
            flipped,
            branch_whole,
            gate_whole,
            grad_stepw,
            grad_bias,
            grad_decaylog,
            grad_skip,
            jnp.asarray(plain_rows.reshape(small_half)),
            early_squares,
        ),
        collective_id=1,
    )

    names = ("gain", "taps", "shift", "select", "step", "bias", "decay", "skip")
    own = (norm_gain, conv_weight, conv_bias, select_proj, step_proj, step_bias, decay_log, skip_scale)
    in_grad, out_grad, grad_tokens, gain_grad, *small_grads, decay_sq, plain_sq = pl.pallas_call(
        functools.partial(finish_kernel, plan, names, late),
        in_specs=[whole] * 7,
        out_specs=[whole] * (3 + len(names)) + [scalars] * 2,
        out_shape=[shape(in_proj.shape), shape(out_proj.shape), shape(tokens.shape, half)]
        + [shape(array.shape) for array in own]
        + [shape((1, 1))] * 2,
        name="finish",
    )(
        tokens_grad,
        in_branch_sum,
        in_gate_sum,
        out_sum,
        small_sum.reshape(plan["rows"], piece),
        late_sum,
        norms,
    )
    return (
        output,
        grad_tokens,
        gain_grad,
        in_grad,
        *small_grads,
        out_grad,
        decay_sq[0, 0],
        plain_sq[0, 0],
    )


def solution(mesh):
    placed = (
        P(("wide", "narrow"), None),
        P(("wide", "narrow"), None),
        P(("wide", "narrow")),
        P(("wide", "narrow"), None),
        P("narrow"),
        P("narrow", None),
        P(None, "narrow"),
        P("narrow"),
        P(None, "narrow"),
        P(None, "narrow"),
        P("narrow"),
        P(None, "narrow"),
        P("narrow"),
        P("narrow", None),
    )
    return jax.shard_map(
        functools.partial(per_device, grid_of(mesh)),
        mesh=mesh,
        in_specs=placed,
        out_specs=(
            P(("wide", "narrow"), None),
            P(("wide", "narrow"), None),
            P("narrow"),
            P("narrow", None),
            P(None, "narrow"),
            P("narrow"),
            P(None, "narrow"),
            P(None, "narrow"),
            P("narrow"),
            P(None, "narrow"),
            P("narrow"),
            P("narrow", None),
            P(),
            P(),
        ),
        check_vma=False,
    )
```

```python
import functools
import math

import jax
import jax.numpy as jnp
import numpy as np
from jax import lax
from jax.experimental import pallas as pl
from jax.experimental.pallas import tpu as pltpu
from jax.sharding import PartitionSpec as P

epsilon = 1e-05
chunk = 8
lanes = 128
log2e = math.log2(math.e)
ln2 = math.log(2.0)
far = 1e30
tiny = 1e-30


def contract(left, right, left_dim, right_dim):
    return lax.dot_general(
        left, right, (((left_dim,), (right_dim,)), ((), ())), preferred_element_type=jnp.float32
    )


def row_loop(rows, group, body, initial):
    def some(index, carry):
        return body(index, pl.ds(pl.multiple_of(index * group, group), group), carry)

    return lax.fori_loop(0, rows // group, some, initial)


def cut(tile):
    return pl.ds(tile * lanes, lanes)


def sigmoid(values):
    return 0.5 * jnp.tanh(0.5 * values) + 0.5


def softplus(values):
    small = jnp.exp(-jnp.abs(values))
    series = small * (1.0 - small * (0.5 - small * (1.0 / 3.0 - 0.25 * small)))
    return jnp.maximum(values, 0.0) + jnp.where(small < 0.03, series, jnp.log(1.0 + small))


def slope_of(step):
    return 1.0 - jnp.exp(-step)


def fill_offsets(lengths_ref, offset_buf, rows):
    place = lax.broadcasted_iota(jnp.int32, offset_buf.shape, 0)
    start = jnp.zeros(offset_buf.shape, jnp.int32)
    ahead = jnp.int32(0)
    for index in range(lengths_ref.shape[1] - 1):
        ahead = ahead + lengths_ref[0, index]
        start = jnp.where(place >= ahead, ahead, start)
    offset_buf[...] = jnp.where(place < rows, place - start, 0)


def small_rows(small_ref, first, count):
    base = first // 16 * 16
    tall = -(-(first + count - base) // 16) * 16
    return small_ref[base : base + tall, :].astype(jnp.float32)[first - base : first - base + count]


def eight(values):
    total = values[:8]
    for row in range(8, values.shape[0], 8):
        total = total + values[row : row + 8]
    return total


def conv_rows(index, at, group, tile, branch_ref, offset_buf, taps, shift):
    count = taps.shape[0]
    here = slice(tile * lanes, (tile + 1) * lanes)
    current = branch_ref[at, cut(tile)]
    before = branch_ref[pl.ds(pl.multiple_of(jnp.maximum(index * group - 8, 0), 8), 8), cut(tile)]
    both = jnp.concatenate([before, current], axis=0)
    offsets = offset_buf[at, :]
    summed = shift[:, here] + taps[count - 1 : count, here] * current
    for tap in range(count - 1):
        lag = count - 1 - tap
        read = jnp.where(offsets >= lag, pltpu.roll(both, lag, 0)[8:], 0.0)
        summed = summed + taps[tap : tap + 1, here] * read
    return summed


def rows_of(blocks):
    return as_matrix(blocks[...][None])


def as_matrix(blocks):
    columns = blocks.shape[3]
    if blocks.shape[2] % 16:
        return blocks.astype(jnp.float32).reshape(-1, columns).astype(blocks.dtype)
    return blocks.reshape(-1, columns)


def front_kernel(
    plan,
    dims,
    names,
    lengths_ref,
    tokens_ref,
    cotangent_ref,
    mask_ref,
    *refs,
):
    smalls, in_ref, out_ref, refs = refs[: len(names)], refs[len(names)], refs[len(names) + 1], refs[len(names) + 2 :]
    branch_ref, signal_ref, slope_ref, projected_ref, flipped_ref, normed_ref, low_ref = refs[:7]
    write_pair, read_pair, small_out, gain_ref, whole_ref, gate_lines, out_lines = refs[7:14]
    offset_buf, pack_buf, own_small, own_in, own_gate, own_out, land_small, land_in, store_sem = refs[14:23]
    own_gain, land_gain, gain_send, gain_recv = refs[23:27]
    rows = tokens_ref.shape[0]
    width = branch_ref.shape[1]
    block = pl.program_id(0)
    last = whole_ref.shape[0]
    shares = own_out.shape[0]
    gather = Gather(
        dims,
        [own_small] + [own_in.at[index] for index in range(last)],
        [land_small] + [land_in.at[index] for index in range(last)],
        refs[27:30],
    )
    rise = Rise(
        dims,
        [own.at[index] for index in range(shares) for own in (own_gate, own_out)],
        [lines.at[index] for index in range(shares) for lines in (gate_lines, out_lines)],
        refs[30:],
    )
    tall = pack_buf.shape[0] // 2

    def stored(index):
        return pltpu.make_async_copy(land_in.at[index], whole_ref.at[index], store_sem.at[index])

    def move_on(plan_of_moves):
        for moment, legs in plan_of_moves:

            @pl.when(block == moment)
            def _(legs=legs):
                for which, number in legs:
                    gather.leg(which, number)

    @pl.when(block == 0)
    def _():
        pack_buf[...] = jnp.zeros_like(pack_buf)
        for name, ref in zip(names, smalls):
            first, height = plan[name]
            pack_buf[first : first + height, : ref.shape[1]] = ref[...]
        own_gain[...] = jnp.zeros_like(own_gain)
        own_gain[0:1, : gain_ref.shape[1] // land_gain.shape[0]] = smalls[names.index("gain")][...]
        for side in range(2):
            own_small[side] = pack_buf[side * tall : (side + 1) * tall, :].astype(own_small.dtype)
        for index in range(last):
            own_in[index] = in_ref[:, index * width : (index + 1) * width].astype(own_in.dtype)
        place = Place(dims)
        place.greet(everyone=True)
        send_to_all(place, lambda target: own_gain, land_gain, gain_send, gain_recv)
        for index in (1, 0) + tuple(range(2, last + 1)):
            gather.start(index)
        first = last * width
        for index in range(shares):
            each = own_gate.shape[2]
            own_gate[index] = in_ref[:, first + index * each : first + (index + 1) * each].astype(own_gate.dtype)
            each = own_out.shape[2]
            own_out[index] = out_ref[:, index * each : (index + 1) * each].astype(own_out.dtype)
        fill_offsets(lengths_ref, offset_buf, rows)
        gather.leg(1, 1)
        gather.leg(0, 1)
        wait_for_all(place, own_gain[...], land_gain, gain_send, gain_recv)
        each = gain_ref.shape[1] // land_gain.shape[0]
        for owner in range(land_gain.shape[0]):
            gain_ref[:, owner * each : (owner + 1) * each] = (
                land_gain[owner, 0:1, :each].astype(jnp.bfloat16).astype(jnp.float32)
            )

        def norm(index, at, carry):
            residual = tokens_ref[at, :].astype(jnp.float32)
            scale = lax.rsqrt(jnp.mean(residual * residual, axis=1, keepdims=True) + epsilon)
            normed_ref[at, :] = (residual * scale * gain_ref[...]).astype(normed_ref.dtype)
            return carry

        row_loop(rows, 16, norm, 0)
        gather.leg(1, 2)
        gather.leg(0, 2)
        gather.leg(2, 1)
        rise.start(0)
        gather.leg(1, 3)
        gather.leg(0, 3)
        gather.leg(2, 2)
        projected_ref[...] = jnp.zeros_like(projected_ref)

    for index in range(last):

        @pl.when(block == index)
        def _(index=index):
            gather.arrive(index + 1)
            stored(index).start()

    branch_w = as_matrix(land_in[block])
    branch_ref[...] = jnp.dot(normed_ref[...], branch_w, preferred_element_type=jnp.float32)
    move_on(((0, ((3, 1), (2, 3))), (1, ((4, 2), (3, 3))), (2, ((4, 3),))))
    pl.when(block == 0)(functools.partial(rise.start, 1))

    @pl.when(block == 0)
    def _():
        gather.arrive(0)
        share = land_small.shape[4]
        for z in range(land_small.shape[0]):
            for plane in range(land_small.shape[1]):
                owner = z * land_small.shape[1] + plane
                for side in range(2):
                    small_out[side * tall : (side + 1) * tall, owner * share : (owner + 1) * share] = land_small[
                        z, plane, side
                    ]

    small_ref = small_out.at[:, pl.ds(pl.multiple_of(block * width, width), width)]
    taps = small_rows(small_ref, *plan["taps"])
    shift = small_rows(small_ref, *plan["shift"])

    def some(index, at, carry):
        for tile in range(width // lanes):
            summed = conv_rows(index, at, 32, tile, branch_ref, offset_buf, taps, shift)
            sigma = sigmoid(summed)
            active = summed * sigma
            signal_ref[at, cut(tile)] = active.astype(signal_ref.dtype)
            slope_ref[at, cut(tile)] = sigma + active * (1.0 - sigma)
        return carry

    row_loop(rows, 32, some, 0)
    move_on(((0, ((4, 1), (3, 2))),))

    @pl.when(block == 0)
    def _():
        for index in range(2, 2 * shares):
            rise.start(index)

    projected_ref[...] += contract(signal_ref[...], small_ref[:lanes, :], 1, 1)

    @pl.when(block == pl.num_programs(0) - 1)
    def _():
        high, low = high_low(projected_ref[...])
        own = own_tokens(rows)
        rank = plan["step"][1]
        size = plan["decay"][1]
        entry = lax.broadcasted_iota(jnp.int32, (lanes, lanes), 0)
        lane = lax.rem(lax.broadcasted_iota(jnp.int32, (lanes, lanes), 1), size)
        for first, pair in ((rank, write_pair), (rank + size, read_pair)):
            spread = (entry == lane + first).astype(jnp.bfloat16)
            parts = [
                (jnp.dot(part.astype(jnp.bfloat16), spread, preferred_element_type=jnp.float32) * own).reshape(
                    rows // chunk, chunk, lanes
                )
                for part in (high, low)
            ]
            pair[...] = jnp.concatenate(parts, axis=1).astype(pair.dtype)
        flipped_ref[...] = normed_ref[...].T
        down = lax.broadcasted_iota(jnp.int32, (rows, rows), 0)
        along = lax.broadcasted_iota(jnp.int32, (rows, rows), 1)
        diagonal = jnp.where(down == along, mask_ref[...].astype(jnp.float32), 0.0).astype(low_ref.dtype)
        low_ref[...] = jnp.dot(
            diagonal, cotangent_ref[...], preferred_element_type=jnp.float32
        ).astype(low_ref.dtype)
        for index in range(last + 1):
            gather.drain(index)
        for index in range(2 * shares):
            rise.finish(index)
        for index in range(last):
            stored(index).wait()


def high_low(values):
    high = values.astype(jnp.bfloat16).astype(jnp.float32)
    return high, values - high


def own_tokens(rows):
    token = lax.rem(lax.broadcasted_iota(jnp.int32, (rows, lanes), 0), chunk)
    return (token == lax.div(lax.broadcasted_iota(jnp.int32, (rows, lanes), 1), lanes // chunk)).astype(
        jnp.float32
    )


def spread_all(pairs, target):
    some = 8

    def spread(index, carry):
        rows = jnp.concatenate([pairs[index * some + number] for number in range(some)], axis=1)
        wide = contract(rows, jnp.ones((rows.shape[0], lanes), rows.dtype), 0, 0)
        target[pl.ds(index * some * chunk, some * chunk)] = wide.reshape(some * chunk, -1, lanes)
        return carry

    lax.fori_loop(0, pairs.shape[0] // some, spread, 0)


def joined(first, second, hop):
    low = lax.bitwise_and(lax.broadcasted_iota(jnp.int32, first.shape, 0), hop) == 0
    return jnp.where(low, first, second) + pltpu.roll(jnp.where(low, second, first), hop, 0)


def folded(buffer, tile):
    parts = [buffer[tile, pl.ds(row * chunk, chunk), :] for row in range(chunk)]
    hop = 1
    while len(parts) > 1:
        parts = [joined(parts[index], parts[index + 1], hop) for index in range(0, len(parts), 2)]
        hop *= 2
    return parts[0]


def forward_kernel(
    plan,
    dims,
    lengths_ref,
    projected_ref,
    small_ref,
    signal_ref,
    write_pair,
    read_pair,
    gate_lines,
    out_lines,
    states_ref,
    step_ref,
    core_ref,
    begin_ref,
    gate_whole,
    out_whole,
    offset_buf,
    pre_buf,
    decay_step,
    flows,
    write_wide,
    read_wide,
    fold_a,
    fold_b,
    held_buf,
    *sems,
):
    rows, width = pre_buf.shape
    size = plan["decay"][1]
    half_size = size // 2
    tiles = width // lanes
    chunks = rows // chunk
    rank = plan["step"][1]
    group = pl.program_id(1)
    groups = pl.num_programs(1)
    moment = pl.program_id(0) * groups + group
    moments = pl.num_programs(0) * groups
    shares = gate_whole.shape[0]
    count = 2 * shares
    gather = Gather(
        dims,
        [lines.at[index] for index in range(shares) for lines in (gate_lines, out_lines)],
        [whole.at[index] for index in range(shares) for whole in (gate_whole, out_whole)],
        sems,
        [whole.shape[3:] for _ in range(shares) for whole in (gate_whole, out_whole)],
    )

    @pl.when(moment == 0)
    def _():
        Place(dims).greet()
        for which in range(count):
            gather.start(which)
        fill_offsets(lengths_ref, offset_buf, offset_buf.shape[0] - 8)
        spread_all(write_pair, write_wide)
        spread_all(read_pair, read_wide)

    @pl.when(group == 0)
    def _():
        held_buf[...] = jnp.zeros_like(held_buf)

    begin_ref[0] = held_buf[...]
    pre_buf[...] = jnp.dot(
        projected_ref[:, :rank].astype(small_ref.dtype),
        small_ref[pl.ds(plan["step"][0], rank), :],
        preferred_element_type=jnp.float32,
    )
    bias = small_rows(small_ref, *plan["bias"])

    def before(index, at, carry):
        spot = pl.ds(pl.multiple_of(index * 4, 4), 4)
        inside = offset_buf[pl.ds(pl.multiple_of(group * rows + index * 32, 32), 32), :] > 0
        for tile in range(tiles):
            step = softplus(pre_buf[at, cut(tile)] + bias[:, tile * lanes : (tile + 1) * lanes])
            step_ref[spot, :, cut(tile)] = step.reshape(4, chunk, lanes)
            decay_step[spot, :, cut(tile)] = jnp.where(inside, step, far).reshape(4, chunk, lanes)
            flow = step * signal_ref[at, cut(tile)].astype(jnp.float32)
            flows[spot, :, cut(tile)] = flow.reshape(4, chunk, lanes)
        return carry

    row_loop(rows, 4 * chunk, before, 0)
    rates = -jnp.exp(small_rows(small_ref, *plan["decay"])) * log2e
    rates = [rates[:, tile * lanes : (tile + 1) * lanes] for tile in range(tiles)]

    def advance(index, held, fold_buf):
        held = list(held)
        for place in range(chunk):
            now = index * chunk + place
            write_now = write_wide[group * rows + now]
            read_now = read_wide[group * rows + now]
            for tile in range(tiles):
                decay = jnp.exp2(rates[tile] * decay_step[index, pl.ds(place, 1), cut(tile)])
                fresh = decay * held[tile] + write_now * flows[index, pl.ds(place, 1), cut(tile)]
                held[tile] = fresh
                states_ref[now, :, cut(tile)] = fresh
                product = read_now * fresh
                fold_buf[tile, pl.ds(place * chunk, chunk), :] = product[:half_size] + product[half_size:]
        return tuple(held)

    def forward(pair, held):
        index = 2 * pair
        held = advance(index, held, fold_a)
        for tile in range(tiles):
            core_ref[index, :, cut(tile)] = folded(fold_a, tile)
        held = advance(index + 1, held, fold_b)
        for tile in range(tiles):
            core_ref[index + 1, :, cut(tile)] = folded(fold_b, tile)
        return held

    held = tuple(held_buf[:, cut(tile)] for tile in range(tiles))
    schedule = {}
    for which in range(count):
        for number in (2, 3):
            point = ((3, 5, 7, 10), (6, 8, 11, 14))[number - 2][which]
            schedule.setdefault(point, []).append((which, number))

    def move_on(legs):
        for which, number in legs:
            gather.leg(which, number)

    for half_loop in range(2):
        for point, legs in sorted(schedule.items()):
            if point < 16 and point % 2 == half_loop:
                pl.when(moment == point // 2)(functools.partial(move_on, legs))
        held = lax.fori_loop(half_loop * chunks // 4, (half_loop + 1) * chunks // 4, forward, held)
    for tile in range(tiles):
        held_buf[:, cut(tile)] = held[tile]

    @pl.when(moment == moments - 1)
    def _():
        for which in range(count):
            gather.arrive(which)
        for which in range(count):
            gather.drain(which)


def middle_kernel(
    plan,
    core_ref,
    small_ref,
    signal_ref,
    gate_w,
    low_ref,
    out_w,
    flipped_ref,
    normed_ref,
    tokens_ref,
    core_grad_ref,
    gate_grad_ref,
    skip_grad_ref,
    out_grad_ref,
    in_grad_ref,
    output_ref,
    pre_buf,
    gate_buf,
    gated_buf,
    out_buf,
    total,
):
    rows, width = pre_buf.shape
    tiles = width // lanes
    block = pl.program_id(0)
    each = out_w.shape[3]
    for index in range(out_w.shape[0]):
        out_buf[:, index * each : (index + 1) * each] = as_matrix(out_w[index][None])
    gate_buf[...] = jnp.dot(normed_ref[...], rows_of(gate_w), preferred_element_type=jnp.float32)
    pre_buf[...] = contract(low_ref[...], out_buf[...], 1, 1)
    skip = small_rows(small_ref, *plan["skip"])

    def after(index, at, carry):
        spot = pl.ds(pl.multiple_of(index * 4, 4), 4)
        sums = []
        for tile in range(tiles):
            signal = signal_ref[at, cut(tile)].astype(jnp.float32)
            core = core_ref[spot, :, cut(tile)].reshape(4 * chunk, lanes)
            core = core + skip[:, tile * lanes : (tile + 1) * lanes] * signal
            gate = gate_buf[at, cut(tile)]
            sigma = sigmoid(gate)
            active = gate * sigma
            gated_buf[at, cut(tile)] = (core * active).astype(gated_buf.dtype)
            grad_gated = pre_buf[at, cut(tile)]
            grad_core = grad_gated * active
            core_grad_ref[spot, :, cut(tile)] = grad_core.reshape(4, chunk, lanes)
            slope = sigma + active * (1.0 - sigma)
            gate_grad_ref[at, cut(tile)] = (grad_gated * core * slope).astype(gate_grad_ref.dtype)
            sums.append(carry[tile] + eight(grad_core * signal))
        return tuple(sums)

    zero_rows = jnp.zeros((8, lanes), jnp.float32)
    skips = row_loop(rows, 4 * chunk, after, (zero_rows,) * tiles)
    for tile in range(tiles):
        skip_grad_ref[:, cut(tile)] = jnp.sum(skips[tile], axis=0, keepdims=True)
    out_grad = contract(gated_buf[...], low_ref[...], 0, 0).astype(out_grad_ref.dtype)
    for index in range(out_w.shape[0]):
        out_grad_ref[index] = out_grad[:, index * each : (index + 1) * each]
    in_grad_ref[...] = jnp.dot(
        flipped_ref[...], gate_grad_ref[...], preferred_element_type=jnp.float32
    ).astype(in_grad_ref.dtype)
    piece = jnp.dot(gated_buf[...], out_buf[...], preferred_element_type=jnp.float32)

    @pl.when(block == 0)
    def _():
        total[...] = piece

    @pl.when(block > 0)
    def _():
        total[...] += piece

    @pl.when(block == pl.num_programs(0) - 1)
    def _():
        output_ref[...] = (tokens_ref[...].astype(jnp.float32) + total[...]).astype(output_ref.dtype)


def backward_kernel(
    plan,
    dims,
    lengths_ref,
    projected_ref,
    small_ref,
    signal_ref,
    write_pair,
    read_pair,
    step_ref,
    core_grad_ref,
    states_ref,
    begin_ref,
    out_grad_ref,
    in_grad_ref,
    signal_grad_ref,
    step_w_grad_ref,
    bias_grad_ref,
    decay_grad_ref,
    flat_ref,
    out_sum_ref,
    in_sum_ref,
    square_ref,
    offset_buf,
    decay_step,
    flows,
    write_wide,
    read_wide,
    first_a,
    first_b,
    second_a,
    second_b,
    through_buf,
    scaled_buf,
    low_buf,
    incoming_buf,
    rank_buf,
    write_buf,
    read_buf,
    *parts,
):
    rows, width = low_buf.shape
    rank = plan["step"][1]
    size = plan["decay"][1]
    half_size = size // 2
    tiles = width // lanes
    chunks = rows // chunk
    block = pl.program_id(0)
    turn = pl.program_id(1)
    groups = pl.num_programs(1)
    group = groups - 1 - turn
    moment = block * groups + turn
    moments = pl.num_programs(0) * groups
    gate_result, out_result, parts = parts[0], parts[1], parts[2:]
    pieces = gate_result.shape[0]
    count = 2 * pieces

    both = ((in_grad_ref, gate_result), (out_grad_ref, out_result))
    reduce = Reduce(
        dims,
        [ref.at[index] for index in range(pieces) for ref, _ in both],
        parts[: 6 * count],
        parts[6 * count :],
        [result.at[index] for index in range(pieces) for _, result in both],
        False,
    )

    @pl.when(moment == 0)
    def _():
        Place(dims).greet()
        for which in range(count):
            reduce.start(which)
        fill_offsets(lengths_ref, offset_buf, offset_buf.shape[0] - 8)
        spread_all(write_pair, write_wide)
        spread_all(read_pair, read_wide)
        write_buf[...] = jnp.zeros_like(write_buf)
        read_buf[...] = jnp.zeros_like(read_buf)
        rank_buf[...] = jnp.zeros_like(rank_buf)

    @pl.when(turn == 0)
    def _():
        incoming_buf[...] = jnp.zeros_like(incoming_buf)
        decay_grad_ref[...] = jnp.zeros_like(decay_grad_ref)
        bias_grad_ref[...] = jnp.zeros_like(bias_grad_ref)
        step_w_grad_ref[...] = jnp.zeros_like(step_w_grad_ref)

    def before(index, at, carry):
        spot = pl.ds(pl.multiple_of(index * 4, 4), 4)
        offsets = offset_buf[pl.ds(pl.multiple_of(group * rows + index * 32, 32), 32), :]
        inside = (offsets > 0).reshape(4, chunk, lanes)
        for tile in range(tiles):
            step = step_ref[spot, :, cut(tile)]
            decay_step[spot, :, cut(tile)] = jnp.where(inside, step, far)
            signal = signal_ref[at, cut(tile)].astype(jnp.float32).reshape(4, chunk, lanes)
            flows[spot, :, cut(tile)] = step * signal
        return carry

    row_loop(rows, 4 * chunk, before, 0)
    rates = -jnp.exp(small_rows(small_ref, *plan["decay"])) * log2e
    rates = [rates[:, tile * lanes : (tile + 1) * lanes] for tile in range(tiles)]

    def retreat(index, carried, first_buf, second_buf):
        incoming, decay_sums, current = (list(tiles_of) for tiles_of in carried)
        for place in range(chunk - 1, -1, -1):
            now = index * chunk + place
            token = group * rows + now
            write_now = write_wide[token]
            read_now = read_wide[token]
            read_sum = None
            write_sum = None
            for tile in range(tiles):
                grad_now = core_grad_ref[index, pl.ds(place, 1), cut(tile)]
                if place > 0:
                    earlier = states_ref[now - 1, :, cut(tile)]
                else:
                    earlier = jnp.where(
                        index > 0, states_ref[jnp.maximum(now - 1, 0), :, cut(tile)], begin_ref[0, :, cut(tile)]
                    )
                grad_state = incoming[tile] + read_now * grad_now
                through_read = current[tile] * grad_now
                current[tile] = earlier
                through_write = grad_state * flows[index, pl.ds(place, 1), cut(tile)]
                read_sum = through_read if read_sum is None else read_sum + through_read
                write_sum = through_write if write_sum is None else write_sum + through_write
                passed = grad_state * write_now
                first_buf[tile, pl.ds(place * chunk, chunk), :] = passed[:half_size] + passed[half_size:]
                exponent = rates[tile] * decay_step[index, pl.ds(place, 1), cut(tile)]
                leaving = jnp.exp2(exponent) * grad_state
                incoming[tile] = leaving
                weighted = (leaving * earlier) * exponent
                second_buf[tile, pl.ds(place * chunk, chunk), :] = weighted[:half_size] + weighted[half_size:]
                decay_sums[tile] = decay_sums[tile] + weighted
            read_buf[token] += read_sum
            write_buf[token] += write_sum
        return (tuple(incoming), tuple(decay_sums), tuple(current))

    def backward(pair, carried):
        index = chunks - 1 - 2 * pair
        for here, first_buf, second_buf in ((index, first_a, second_a), (index - 1, first_b, second_b)):
            carried = retreat(here, carried, first_buf, second_buf)
            for tile in range(tiles):
                through_buf[here, :, cut(tile)] = folded(first_buf, tile)
                scaled_buf[here, :, cut(tile)] = folded(second_buf, tile)
        return carried

    incoming = tuple(incoming_buf[:, cut(tile)] for tile in range(tiles))
    nothing = (jnp.zeros((size, lanes), jnp.float32),) * tiles
    current = tuple(states_ref[rows - 1, :, cut(tile)] for tile in range(tiles))
    schedule = {}
    for which in range(count):
        for number in (1, 2, 3):
            point = ((4, 6, 8, 11), (6, 9, 11, 13), (8, 11, 13, 15))[number - 1][which]
            schedule.setdefault(point, []).append((which, number))

    def move_on(legs):
        for which, number in legs:
            reduce.leg(which, number)

    carried = (incoming, nothing, current)
    for half_loop in range(2):
        for point, legs in sorted(schedule.items()):
            if point % 2 == half_loop:
                pl.when(moment == point // 2)(functools.partial(move_on, legs))
        carried = lax.fori_loop(half_loop * chunks // 4, (half_loop + 1) * chunks // 4, backward, carried)
    incoming, decay_sums, _ = carried
    for tile in range(tiles):
        incoming_buf[:, cut(tile)] = incoming[tile]
        decay_grad_ref[:, cut(tile)] += decay_sums[tile] * ln2
    skip = small_rows(small_ref, *plan["skip"])

    def after(index, at, carry):
        spot = pl.ds(pl.multiple_of(index * 4, 4), 4)
        sums = []
        for tile in range(tiles):
            signal = signal_ref[at, cut(tile)].astype(jnp.float32)
            step = step_ref[spot, :, cut(tile)].reshape(4 * chunk, lanes)
            through = through_buf[spot, :, cut(tile)].reshape(4 * chunk, lanes)
            scaled = scaled_buf[spot, :, cut(tile)].reshape(4 * chunk, lanes)
            core_grad = core_grad_ref[spot, :, cut(tile)].reshape(4 * chunk, lanes)
            grad_pre = (through * signal + ln2 * scaled / jnp.maximum(step, tiny)) * slope_of(step)
            low_buf[at, cut(tile)] = grad_pre.astype(low_buf.dtype)
            signal_grad_ref[at, cut(tile)] = (
                through * step + skip[:, tile * lanes : (tile + 1) * lanes] * core_grad
            )
            sums.append(carry[tile] + eight(grad_pre))
        return tuple(sums)

    zero_rows = jnp.zeros((8, lanes), jnp.float32)
    sums = row_loop(rows, 4 * chunk, after, (zero_rows,) * tiles)
    for tile in range(tiles):
        bias_grad_ref[:, cut(tile)] += jnp.sum(sums[tile], axis=0, keepdims=True)
    step_w_grad_ref[...] += contract(
        projected_ref[:, :rank].astype(low_buf.dtype), low_buf[...], 0, 0
    )
    step_w = small_ref[pl.ds(plan["step"][0], rank), :]
    step_w = jnp.concatenate([step_w, jnp.zeros((lanes - rank, width), step_w.dtype)], axis=0)
    rank_buf[pl.ds(group * chunks, chunks)] += contract(low_buf[...], step_w, 1, 1).reshape(
        chunks, chunk, lanes
    )

    @pl.when(moment == moments - 1)
    def _():
        squares = jnp.zeros((8, lanes), jnp.float32)
        for which in range(count):
            squares = squares + reduce.finish(which)[0]
        square_ref[...] = squares
        some = 8
        entry = lax.rem(lax.broadcasted_iota(jnp.int32, (some * chunk * size, lanes), 0), size)
        target = lax.broadcasted_iota(jnp.int32, (some * chunk * size, lanes), 1)
        ones = jnp.ones((lanes, lanes), jnp.bfloat16)

        def lay(index, carry):
            lot = pl.ds(index * some * chunk, some * chunk)
            for number, buffer in enumerate((write_buf, read_buf)):
                high, low = high_low(buffer[lot].reshape(some * chunk * size, lanes))
                summed = jnp.dot(high.astype(jnp.bfloat16), ones, preferred_element_type=jnp.float32)
                summed += jnp.dot(low.astype(jnp.bfloat16), ones, preferred_element_type=jnp.float32)
                summed = jnp.where(target == entry + rank + number * size, summed, 0.0)
                summed = jnp.sum(summed.reshape(some * chunk, size, lanes), axis=1)
                rank_buf[pl.ds(index * some, some)] += summed.reshape(some, chunk, lanes)
            return carry

        lax.fori_loop(0, rank_buf.shape[0] // some, lay, 0)
        flat_ref[...] = rank_buf[...].reshape(flat_ref.shape).astype(flat_ref.dtype)
        for which in range(count):
            reduce.settle(which)
        for index in range(pieces):
            for target, result in ((out_sum_ref, out_result), (in_sum_ref, gate_result)):
                each = result.shape[2]
                target[:, index * each : (index + 1) * each] = result[index]


def back_kernel(
    plan,
    dims,
    lengths_ref,
    tokens_ref,
    low_ref,
    gain_ref,
    small_ref,
    flat_ref,
    branch_ref,
    signal_ref,
    slope_ref,
    signal_grad_ref,
    gate_grad_ref,
    flipped_ref,
    branch_w,
    gate_w,
    step_w_grad_ref,
    bias_grad_ref,
    decay_grad_ref,
    skip_grad_ref,
    plain_ref,
    earlier_ref,
    tokens_grad_ref,
    in_sum_ref,
    small_sum_ref,
    late_sum_ref,
    norm_ref,
    offset_buf,
    conv_buf,
    mixed_buf,
    total,
    in_stage,
    small_stage,
    late_stage,
    late_land,
    norm_own,
    norm_land,
    in_result,
    small_result,
    direct_send,
    direct_recv,
    *parts,
):
    rows = tokens_ref.shape[0]
    width = branch_ref.shape[1]
    tiles = width // lanes
    block = pl.program_id(0)
    last = in_stage.shape[0]
    count = last + 1
    reduce = Reduce(
        dims,
        [small_stage] + [in_stage.at[index] for index in range(last)],
        parts[: 5 * count],
        parts[5 * count :],
        [small_result] + [in_result.at[index] for index in range(last)],
        True,
    )
    share = small_stage.shape[4]
    half_rows = small_stage.shape[3]
    planes = small_stage.shape[1]
    owners = small_stage.shape[0] * planes

    @pl.when(block == 0)
    def _():
        Place(dims).greet(everyone=True)
        fill_offsets(lengths_ref, offset_buf, rows)

    def move_on(plan_of_moves):
        for moment, legs in plan_of_moves:

            @pl.when(block == moment)
            def _(legs=legs):
                for which, number in legs:
                    reduce.leg(which, number)

    taps = small_rows(small_ref, *plan["taps"])
    taps_count = taps.shape[0]
    zero_rows = jnp.zeros((8, lanes), jnp.float32)

    @pl.when(block < last)
    def _():
        conv_buf[pl.ds(0, rows), :] = signal_grad_ref[...] + jnp.dot(
            flat_ref[...], small_ref[:lanes, :], preferred_element_type=jnp.float32
        )
        conv_buf[pl.ds(rows, 8), :] = jnp.zeros((8, width), jnp.float32)

        def through_conv(index, at, carry):
            sums = []
            for tile in range(tiles):
                grad_conv = conv_buf[at, cut(tile)] * slope_ref[at, cut(tile)]
                conv_buf[at, cut(tile)] = grad_conv
                sums.append(carry[tile] + eight(grad_conv))
            return tuple(sums)

        shift_sums = row_loop(rows, 32, through_conv, (zero_rows,) * tiles)
        def to_branch(index, at, carry):
            longer = pl.ds(pl.multiple_of(index * 32, 32), 40)
            offsets = offset_buf[longer, :]
            result = []
            for tile in range(tiles):
                here = slice(tile * lanes, (tile + 1) * lanes)
                grads = conv_buf[longer, cut(tile)]
                branch = branch_ref[at, cut(tile)]
                summed = taps[taps_count - 1 : taps_count, here] * grads[:32]
                sums = [None] * taps_count
                sums[taps_count - 1] = carry[tile][taps_count - 1] + eight(branch * grads[:32])
                for tap in range(taps_count - 1):
                    lag = taps_count - 1 - tap
                    moved = pltpu.roll(jnp.where(offsets >= lag, grads, 0.0), 40 - lag, 0)[:32]
                    summed = summed + taps[tap : tap + 1, here] * moved
                    sums[tap] = carry[tile][tap] + eight(branch * moved)
                mixed_buf[block, at, cut(tile)] = summed.astype(mixed_buf.dtype)
                result.append(tuple(sums))
            return tuple(result)

        sums = row_loop(rows, 32, to_branch, ((zero_rows,) * taps_count,) * tiles)
        in_grad = jnp.dot(flipped_ref[...], mixed_buf[block], preferred_element_type=jnp.float32)
        in_stage[block] = in_grad.reshape(in_stage.shape[1:]).astype(in_stage.dtype)
        for index in range(last):

            @pl.when(block == index)
            def _(index=index):
                reduce.start(index + 1)

        late = [
            jnp.concatenate(
                [jnp.sum(sums[tile][tap], axis=0, keepdims=True) for tap in range(taps_count)]
                + [jnp.sum(shift_sums[tile], axis=0, keepdims=True)]
                + [jnp.zeros((8 - taps_count - 1, lanes), jnp.float32)],
                axis=0,
            )
            for tile in range(tiles)
        ]
        late = jnp.concatenate(late, axis=1)
        for piece in range(width // share):
            late_stage[block * (width // share) + piece] = late[:, piece * share : (piece + 1) * share]
        move_on(
            (
                (1, ((1, 1), (0, 1))),
                (2, ((2, 1), (1, 2), (0, 2))),
                (3, ((3, 1), (2, 2), (1, 3), (0, 3))),
            )
        )

        @pl.when(block == 0)
        def _():
            select_grad = contract(flat_ref[...], signal_ref[...], 0, 0)
            step_first, step_tall = plan["step"]
            filler = jnp.zeros((2 * half_rows - step_first - step_tall, select_grad.shape[1]), jnp.float32)
            pieces = {
                "decay": decay_grad_ref[...],
                "bias": bias_grad_ref[...],
                "skip": skip_grad_ref[...],
                "step": step_w_grad_ref[...],
            }
            first = plan["select"][1]
            rows_now = [select_grad[:first]]
            for name in ("decay", "taps", "shift", "bias", "skip", "gain"):
                tall = plan[name][1]
                rows_now.append(
                    pieces[name] if name in pieces else jnp.zeros((tall, select_grad.shape[1]), jnp.float32)
                )
                first += tall
            rows_now.append(jnp.zeros((step_first - first, select_grad.shape[1]), jnp.float32))
            rows_now.append(pieces["step"])
            if filler.shape[0]:
                rows_now.append(filler)
            everything = jnp.concatenate(rows_now, axis=0)
            for owner in range(owners):
                for side in range(2):
                    small_stage[owner // planes, owner % planes, side] = everything[
                        side * half_rows : (side + 1) * half_rows, owner * share : (owner + 1) * share
                    ].astype(small_stage.dtype)
            reduce.start(0)

    @pl.when(block >= last)
    def _():
        grad_normed_piece = contract(mixed_buf[block - last], rows_of(branch_w), 1, 1)
        grad_normed_piece += contract(gate_grad_ref[...], rows_of(gate_w), 1, 1)

        @pl.when(block == last)
        def _():
            total[...] = grad_normed_piece

        @pl.when(block > last)
        def _():
            total[...] += grad_normed_piece

        move_on(((4, ((3, 2),)), (5, ((4, 1), (2, 3))), (6, ((3, 3),)), (7, ((4, 2),))))

    @pl.when(block == pl.num_programs(0) - 1)
    def _():
        def scaled_tokens(at):
            residual = tokens_ref[at, :].astype(jnp.float32)
            return residual, lax.rsqrt(jnp.mean(residual * residual, axis=1, keepdims=True) + epsilon)

        def gain_rows(index, at, carry):
            residual, scale = scaled_tokens(at)
            return carry + eight(total[at, :] * residual * scale)

        gains = row_loop(rows, 16, gain_rows, jnp.zeros((8, total.shape[1]), jnp.float32))
        gains = jnp.sum(gains, axis=0, keepdims=True)
        place = Place(dims)
        each = gains.shape[1] // owners
        for owner in range(owners):
            late_stage[owner, taps_count + 1 : taps_count + 2, :each] = gains[
                :, owner * each : (owner + 1) * each
            ]
        late_sems = direct_send.at[0], direct_recv.at[0]
        norm_sems = direct_send.at[1], direct_recv.at[1]
        send_to_everyone(place, lambda chip: late_stage.at[chip], late_land, *late_sems)
        reduce.leg(4, 3)

        def token_rows(index, at, carry):
            residual, scale = scaled_tokens(at)
            weighted = total[at, :] * gain_ref[...]
            inner = jnp.mean(weighted * residual, axis=1, keepdims=True)
            grad_y = low_ref[at, :].astype(jnp.float32)
            result = grad_y + (scale * weighted - residual * (scale * scale * scale) * inner)
            tokens_grad_ref[at, :] = result.astype(tokens_grad_ref.dtype)
            return carry

        row_loop(rows, 16, token_rows, 0)
        more, plain = reduce.finish(0, plain_ref)
        kept = earlier_ref[...] + more
        for index in range(1, count - 1):
            kept = kept + reduce.finish(index)[0]
        late_sum = sum_of_everyone(place, late_stage[place.me], late_land, *late_sems)
        late_sum_ref[...] = late_sum
        kept = kept + folded_squares(late_sum * late_sum) * (1 - place.core).astype(jnp.float32)
        kept = kept + reduce.finish(count - 1)[0]
        norm_own[...] = jnp.stack([kept, plain])
        send_to_everyone(place, lambda chip: norm_own, norm_land, *norm_sems)
        norm_ref[...] = sum_of_everyone(place, norm_own[...], norm_land, *norm_sems)
        for index in range(count):
            reduce.settle(index)
        for index in range(last):
            in_sum_ref[:, index * width : (index + 1) * width] = in_result[index]
        small_sum_ref[...] = small_result[...]


def finish_kernel(
    plan, names, late, tokens_ref, branch_ref, gate_ref, out_ref, small_ref, late_ref, norm_ref, *outs
):
    middle = branch_ref.shape[1]
    outs[0][:, :middle] = branch_ref[...]
    outs[0][:, middle:] = gate_ref[...]
    outs[1][...] = out_ref[...]
    outs[2][...] = tokens_ref[...]
    for name, target in zip(names, outs[3 : 3 + len(names)]):
        source, (first, count) = (late_ref, late[name]) if name in late else (small_ref, plan[name])
        if len(target.shape) == 1:
            target[...] = source[first, : target.shape[0]]
        else:
            target[...] = source[first : first + count, :]
    for index in range(2):
        outs[3 + len(names) + index][0, 0] = jnp.sum(norm_ref[index])


def shape(dims, kind=jnp.float32):
    return jax.ShapeDtypeStruct(dims, kind)


def compute_call(
    kernel, name, blocks, in_specs, out_specs, out_shape, scratch, flops, operands, collective_id=None
):
    return pl.pallas_call(
        kernel,
        grid=blocks if isinstance(blocks, tuple) else (blocks,),
        in_specs=in_specs,
        out_specs=out_specs,
        out_shape=out_shape,
        scratch_shapes=scratch,
        compiler_params=pltpu.CompilerParams(
            dimension_semantics=("arbitrary",) * (len(blocks) if isinstance(blocks, tuple) else 1),
            vmem_limit_bytes=62 * 1024 * 1024,
            collective_id=collective_id,
            has_side_effects=collective_id is not None,
        ),
        cost_estimate=pl.CostEstimate(flops=flops, bytes_accessed=40 << 20, transcendentals=0),
        name=name,
    )(*operands)


class Place:
    def __init__(self, dims, swapped=False):
        depth, tall, wide = dims
        self.dims = dims
        self.core = lax.axis_index("wide")
        self.me = lax.axis_index("narrow")
        self.across = lax.rem(self.me, wide)
        self.up = lax.rem(lax.div(self.me, wide), tall)
        self.deep = lax.div(self.me, wide * tall)
        side = 1 - self.core if swapped else self.core
        turn = side if tall == wide else 0
        self.second = (1 + turn * (wide - 1), self.across + turn * (self.up - self.across), wide)
        self.third = (wide - turn * (wide - 1), self.up + turn * (self.across - self.up), tall)
        self.spans = (depth, wide, tall)
        self.other = {"wide": 1 - self.core}

    def level(self, d):
        return lax.rem(self.deep + d, self.spans[0])

    def plane(self, e, f):
        return (
            lax.rem(self.second[1] + e, self.second[2]) * self.second[0]
            + lax.rem(self.third[1] + f, self.third[2]) * self.third[0]
        )

    def plane_behind(self, e, f):
        return self.plane((self.spans[1] - e) % self.spans[1], (self.spans[2] - f) % self.spans[2])

    def at(self, d, e, f):
        return {"narrow": self.level(d) * (self.dims[1] * self.dims[2]) + self.plane(e, f)}

    def greet(self, everyone=False):
        barrier = pltpu.get_barrier_semaphore()
        peers = [self.other]
        if everyone:
            number = self.spans[0] * self.spans[1] * self.spans[2]
            for hop in range(1, number):
                chip = lax.rem(self.me + hop, number)
                peers += [{"narrow": chip}, {"wide": 1 - self.core, "narrow": chip}]
        else:
            for axis, size in enumerate(self.spans):
                for hop in range(1, size):
                    move = [0, 0, 0]
                    move[axis] = hop
                    peers.append(self.at(*move))
        for peer in peers:
            pl.semaphore_signal(barrier, inc=1, device_id=peer, device_id_type=pl.DeviceIdType.MESH)
        pl.semaphore_wait(barrier, len(peers))


def by_rows(block):
    return block[0] % 32 == 0


def half_shape(block):
    if len(block) == 3:
        return tuple(block[1:])
    return (block[0] // 2, block[1]) if by_rows(block) else (block[0], block[1] // 2)


def half(view, block, side, lead=0):
    ahead = (slice(None),) * lead
    if len(block) == 3:
        return view.at[ahead + (side,)]
    if by_rows(block):
        return view.at[ahead + (pl.ds(pl.multiple_of(side * (block[0] // 2), 16), block[0] // 2),)]
    columns = pl.ds(pl.multiple_of(side * (block[1] // 2), lanes), block[1] // 2)
    return view.at[ahead + (slice(None), columns)]


def remote(source, target, send_sem, recv_sem, device):
    return pltpu.make_async_remote_copy(
        src_ref=source,
        dst_ref=target,
        send_sem=send_sem,
        recv_sem=recv_sem,
        device_id=device,
        device_id_type=pl.DeviceIdType.MESH,
    )


class Gather:
    def __init__(self, dims, own, whole, sems, blocks=None):
        self.dims, self.own, self.whole = dims, own, whole
        self.local_sem, self.send_sem, self.recv_sem = sems
        self.lined = blocks is not None
        self.blocks = blocks or [block.shape for block in own]

    @staticmethod
    def sems(count, dims):
        copies = dims[0] + 2 * dims[1] * dims[2]
        return [pltpu.SemaphoreType.DMA((count,))] + [pltpu.SemaphoreType.DMA((count, copies))] * 2

    def line(self, which, plane, side):
        return half(self.whole[which].at[:, plane], self.blocks[which], side, 1)

    def local(self, place, which):
        block = self.blocks[which]
        if self.lined:
            return pltpu.make_async_copy(
                self.own[which], self.line(which, place.plane(0, 0), place.core), self.local_sem.at[which]
            )
        return pltpu.make_async_copy(
            half(self.own[which], block, place.core),
            half(self.whole[which].at[place.deep, place.plane(0, 0)], block, place.core),
            self.local_sem.at[which],
        )

    def copy(self, which, source, target, index, device):
        return remote(
            source, target, self.send_sem.at[which, index], self.recv_sem.at[which, index], device
        )

    def rise(self, place, which, hop):
        block = self.blocks[which]
        return self.copy(
            which,
            half(self.own[which], block, place.core),
            half(self.whole[which].at[place.deep, place.plane(0, 0)], block, place.core),
            hop,
            place.at(hop, 0, 0),
        )

    def leg_index(self, e, f):
        return self.dims[0] + e * self.dims[1] + f

    def hand_index(self, e, f):
        return self.leg_index(e, f) + self.dims[1] * self.dims[2]

    def onward(self, place, which, e, f):
        line = self.line(which, place.plane_behind(e, f), place.core)
        source = self.own[which] if self.lined and e == 0 and f == 0 else line
        if f == 0:
            for hop in range(1, place.spans[2]):
                self.copy(which, source, line, self.leg_index(e, hop), place.at(0, 0, hop)).start()
        if f == 0 and e == 0:
            for hop in range(1, place.spans[1]):
                self.copy(which, source, line, self.leg_index(hop, 0), place.at(0, hop, 0)).start()
        self.copy(which, source, line, self.hand_index(e, f), place.other).start()

    def start(self, which):
        place = Place(self.dims)
        if self.lined:
            self.onward(place, which, 0, 0)
            self.local(place, which).start()
            return
        for hop in range(1, place.spans[0]):
            self.rise(place, which, hop).start()
        self.local(place, which).start()

    def leg(self, which, number):
        place = Place(self.dims)
        if number == 1:
            self.local(place, which).wait()
            for hop in range(1, place.spans[0]):
                self.rise(place, which, hop).wait_recv()
            self.onward(place, which, 0, 0)
            return
        for e in range(place.spans[1]):
            for f in range(place.spans[2]):
                if (number == 2 and f == 0 and e > 0) or (number == 3 and f > 0):
                    line = self.line(which, place.plane_behind(e, f), place.core)
                    self.copy(which, line, line, self.leg_index(e, f), place.other).wait_recv()
                    self.onward(place, which, e, f)

    def arrive(self, which):
        place, mirror = Place(self.dims), Place(self.dims, swapped=True)
        for e in range(place.spans[1]):
            for f in range(place.spans[2]):
                line = self.line(which, mirror.plane_behind(e, f), 1 - place.core)
                self.copy(which, line, line, self.hand_index(e, f), place.other).wait_recv()

    def drain(self, which):
        place = Place(self.dims)
        if self.lined:
            self.local(place, which).wait()
        else:
            for hop in range(1, place.spans[0]):
                self.rise(place, which, hop).wait_send()
        for e in range(place.spans[1]):
            for f in range(place.spans[2]):
                line = self.line(which, place.plane_behind(e, f), place.core)
                if e > 0 or f > 0:
                    self.copy(which, line, line, self.leg_index(e, f), place.other).wait_send()
                self.copy(which, line, line, self.hand_index(e, f), place.other).wait_send()


class Rise:
    def __init__(self, dims, own, lines, sems):
        self.dims, self.own, self.lines = dims, own, lines
        self.local_sem, self.send_sem, self.recv_sem = sems

    @staticmethod
    def sems(count, dims):
        return [pltpu.SemaphoreType.DMA((count,))] + [pltpu.SemaphoreType.DMA((count, dims[0]))] * 2

    def copies(self, place, which):
        source = half(self.own[which], self.own[which].shape, place.core)
        target = self.lines[which].at[place.deep]
        local = pltpu.make_async_copy(source, target, self.local_sem.at[which])
        return local, [
            remote(
                source, target, self.send_sem.at[which, hop], self.recv_sem.at[which, hop], place.at(hop, 0, 0)
            )
            for hop in range(1, place.spans[0])
        ]

    def start(self, which):
        local, sends = self.copies(Place(self.dims), which)
        for copy in [*sends, local]:
            copy.start()

    def finish(self, which):
        local, sends = self.copies(Place(self.dims), which)
        local.wait()
        for copy in sends:
            copy.wait_recv()
            copy.wait_send()


class Reduce:
    def __init__(self, dims, grads, rooms, sems, results, resident):
        self.dims, self.grads, self.resident = dims, grads, resident
        count = len(grads)
        self.mine, self.swapped, self.third, self.second, self.first = (
            rooms[index * count : (index + 1) * count] for index in range(5)
        )
        self.loaded = None if resident else rooms[5 * count :]
        self.load_sem, self.swap_send, self.swap_recv, self.send_sem, self.recv_sem = sems[:5]
        self.last_send, self.last_recv = sems[5:]
        self.results = results

    @staticmethod
    def rooms(dims, grads, resident):
        depth, tall, wide = dims
        leads = (
            (tall, wide, depth),
            (depth, tall * wide),
            (tall - 1, wide, depth),
            (wide - 1, depth),
            (depth - 1,),
        )
        if not resident:
            leads += ((depth, tall * wide),)
        return [
            pltpu.VMEM(lead + half_shape(grad.shape[2:]), grad.dtype) for lead in leads for grad in grads
        ]

    @staticmethod
    def sems(count, dims):
        return (
            [pltpu.SemaphoreType.DMA((count,))] * 3
            + [pltpu.SemaphoreType.DMA((count, dims[0] + dims[1] + dims[2]))] * 2
            + [pltpu.SemaphoreType.DMA((count,))] * 2
        )

    def block(self, which):
        return self.grads[which].shape[2:]

    def load(self, place, which):
        return pltpu.make_async_copy(
            half(self.grads[which], self.block(which), place.core, 2),
            self.loaded[which],
            self.load_sem.at[which],
        )

    def swap(self, place, which):
        return remote(
            half(self.grads[which], self.block(which), 1 - place.core, 2),
            self.swapped[which],
            self.swap_send.at[which],
            self.swap_recv.at[which],
            place.other,
        )

    def hop(self, which, source, target, index, device):
        return remote(
            source, target, self.send_sem.at[which, index], self.recv_sem.at[which, index], device
        )

    def third_hop(self, place, which, f):
        return self.hop(which, self.mine[which].at[f], self.third[which].at[f - 1], f, place.at(0, 0, f))

    def second_hop(self, place, which, e):
        return self.hop(
            which,
            self.mine[which].at[0, e],
            self.second[which].at[e - 1],
            self.dims[1] + e,
            place.at(0, e, 0),
        )

    def first_hop(self, place, which, d):
        return self.hop(
            which,
            self.mine[which].at[0, 0, place.level(d)],
            self.first[which].at[d - 1],
            self.dims[1] + self.dims[2] + d,
            place.at(d, 0, 0),
        )

    def start(self, which):
        place = Place(self.dims)
        self.swap(place, which).start()
        if not self.resident:
            self.load(place, which).start()

    def parts(self, place, which, e, f, z):
        plane = place.plane(e, f)
        if self.resident:
            found = [half(self.grads[which].at[z, plane], self.block(which), place.core)]
        else:
            found = [self.loaded[which].at[z, plane]]
        found.append(self.swapped[which].at[z, plane])
        if f == 0:
            found += [self.third[which].at[hop - 1, e, z] for hop in range(1, place.spans[2])]
        if f == 0 and e == 0:
            found += [self.second[which].at[hop - 1, z] for hop in range(1, place.spans[1])]
        return found

    def ready(self, place, which):
        if not self.resident:
            self.load(place, which).wait()
        self.swap(place, which).wait_recv()

    def added(self, parts, store, carry):
        rows = parts[0].shape[0]
        group = min(rows, 16)

        def some(index, carry):
            at_rows = pl.ds(pl.multiple_of(index * group, group), group)
            total = parts[0][at_rows, :].astype(jnp.float32)
            for part in parts[1:]:
                total = total + part[at_rows, :].astype(jnp.float32)
            return store(at_rows, total, carry)

        return lax.fori_loop(0, rows // group, some, carry)

    def sum_into(self, place, which, e, f, z):
        target = self.mine[which].at[f, e, z]

        def keep(at_rows, total, carry):
            target[at_rows, :] = total.astype(target.dtype)
            return carry

        self.added(self.parts(place, which, e, f, z), keep, 0)

    def leg(self, which, number):
        place = Place(self.dims)
        depth, span_e, span_f = place.spans
        if number == 1:
            self.ready(place, which)
            for f in range(span_f - 1, 0, -1):
                for e in range(span_e - 1, -1, -1):
                    for z in range(depth):
                        self.sum_into(place, which, e, f, z)
                self.third_hop(place, which, f).start()
        elif number == 2:
            for f in range(1, span_f):
                self.third_hop(place, which, f).wait_recv()
            for e in range(span_e - 1, 0, -1):
                for z in range(depth):
                    self.sum_into(place, which, e, 0, z)
                self.second_hop(place, which, e).start()
        else:
            if span_e == 1:
                for f in range(1, span_f):
                    self.third_hop(place, which, f).wait_recv()
            for e in range(1, span_e):
                self.second_hop(place, which, e).wait_recv()
            for d in range(1, depth):
                self.sum_into(place, which, 0, 0, place.level(d))
                self.first_hop(place, which, d).start()

    def result(self, which, side):
        return half(self.results[which], self.block(which), side)

    def last(self, place, which, side):
        share = self.result(which, side)
        return remote(share, share, self.last_send.at[which], self.last_recv.at[which], place.other)

    def finish(self, which, marks=None):
        place = Place(self.dims)
        parts = self.parts(place, which, 0, 0, place.deep)
        for d in range(1, place.spans[0]):
            self.first_hop(place, which, d).wait_recv()
            parts.append(self.first[which].at[d - 1])
        share = self.result(which, place.core)

        def store(at_rows, total, carry):
            share[at_rows, :] = total
            kept, plain = carry
            squared = total * total
            if marks is not None:
                marked = squared * marks[place.core, at_rows, :]
                plain = plain + folded_squares(marked)
                squared = squared - marked
            return (kept + folded_squares(squared), plain)

        squares = self.added(parts, store, (jnp.zeros((8, lanes), jnp.float32),) * 2)
        self.last(place, which, place.core).start()
        return squares

    def settle(self, which):
        place = Place(self.dims)
        last = self.last(place, which, 1 - place.core)
        last.wait_recv()
        last.wait_send()
        self.swap(place, which).wait_send()
        for f in range(1, place.spans[2]):
            self.third_hop(place, which, f).wait_send()
        for e in range(1, place.spans[1]):
            self.second_hop(place, which, e).wait_send()
        for d in range(1, place.spans[0]):
            self.first_hop(place, which, d).wait_send()


def folded_squares(values):
    total = None
    if values.shape[1] < lanes:
        first = lax.broadcasted_iota(jnp.int32, (values.shape[0], lanes), 1) == 0
        values = jnp.where(first, jnp.sum(values, axis=1, keepdims=True), 0.0)
    for row in range(0, values.shape[0], 8):
        for column in range(0, values.shape[1], lanes):
            piece = values[row : row + 8, column : column + lanes]
            total = piece if total is None else total + piece
    return total


def send_to_all(place, source, landing, send_sem, recv_sem):
    number = landing.shape[0]
    for hop in range(1, number):
        target = lax.rem(place.me + hop, number)
        remote(
            source(target), landing.at[place.me], send_sem.at[hop], recv_sem.at[hop], {"narrow": target}
        ).start()


def wait_for_all(place, own, landing, send_sem, recv_sem):
    number = landing.shape[0]
    landing[place.me] = own
    for hop in range(1, number):
        came = landing.at[lax.rem(place.me + number - hop, number)]
        copy = remote(came, came, send_sem.at[hop], recv_sem.at[hop], place.other)
        copy.wait_recv()
        copy.wait_send()


def send_to_everyone(place, source, landing, send_sem, recv_sem):
    number = landing.shape[1]
    target = landing.at[place.core, place.me]

    def send(hop, carry):
        chip = lax.rem(place.me + hop, number)
        for turn in range(2):
            device = {"wide": lax.rem(place.core + turn, 2), "narrow": chip}
            remote(source(chip), target, send_sem.at[turn, hop], recv_sem.at[turn, hop], device).start()
        return carry

    lax.fori_loop(1, number, send, 0)
    remote(source(place.me), target, send_sem.at[1, 0], recv_sem.at[1, 0], place.other).start()


def sum_of_everyone(place, own, landing, send_sem, recv_sem):
    number = landing.shape[1]
    landing[place.core, place.me] = own

    def wait(turn, hop):
        came = landing.at[lax.rem(place.core + turn, 2), lax.rem(place.me + number - hop, number)]
        copy = remote(came, came, send_sem.at[turn, hop], recv_sem.at[turn, hop], place.other)
        copy.wait_recv()
        copy.wait_send()

    def wait_both(hop, carry):
        wait(0, hop)
        wait(1, hop)
        return carry

    lax.fori_loop(1, number, wait_both, 0)
    wait(1, 0)

    def add(spot, total):
        return total + landing[0, spot] + landing[1, spot]

    return lax.fori_loop(1, number, add, landing[0, 0] + landing[1, 0])


def grid_of(mesh):
    number = mesh.shape["narrow"]
    places = [getattr(device, "coords", None) for device in mesh.devices[0]]
    if all(place is not None for place in places):
        sizes = [len({place[axis] for place in places}) for axis in (2, 1, 0)]
        if sizes[0] * sizes[1] * sizes[2] == number:
            return tuple(sizes)
    side = round((number / 2) ** (1 / 3))
    return (2 * side, side, side) if 2 * side**3 == number else (number, 1, 1)


def plan_of(select_rows, state_size, tap_count, step_rows):
    plan, first = {}, 0
    for name, tall in (
        ("select", select_rows),
        ("decay", state_size),
        ("taps", tap_count),
        ("shift", 1),
        ("bias", 1),
        ("skip", 1),
        ("gain", 1),
    ):
        plan[name] = (first, tall)
        first += tall
    plan["step"] = (lanes, step_rows)
    plan["rows"] = -(-(lanes + step_rows) // 32) * 32
    return plan


def per_device(
    dims,
    tokens,
    cotangent,
    loss_mask,
    seq_lengths,
    norm_gain,
    in_proj,
    conv_weight,
    conv_bias,
    select_proj,
    step_proj,
    step_bias,
    decay_log,
    skip_scale,
    out_proj,
):
    half = jnp.bfloat16
    piece = skip_scale.shape[0]
    gain_piece = norm_gain.shape[0]
    rank, size = step_proj.shape[0], decay_log.shape[0]
    plan = plan_of(select_proj.shape[0], size, conv_weight.shape[0], rank)
    smalls = {
        "select": select_proj,
        "decay": decay_log,
        "taps": conv_weight,
        "shift": conv_bias[None],
        "bias": step_bias[None],
        "skip": skip_scale[None],
        "gain": norm_gain[None],
        "step": step_proj,
    }
    depth, planes = dims[0], dims[1] * dims[2]
    number = depth * planes
    in_rows = in_proj.shape[0]
    rows, model = tokens.shape
    inner = piece * number
    width = 4 * lanes
    blocks = inner // width
    chunks = rows // chunk
    mask_row = loss_mask[None]

    whole = pl.BlockSpec(memory_space=pltpu.VMEM)
    tall = pl.BlockSpec((rows, width), lambda b: (0, b))
    deep = pl.BlockSpec((chunks, chunk, width), lambda b: (0, 0, b))
    lead = pl.BlockSpec((rows, size, width), lambda b: (0, 0, b))
    first_w = pl.BlockSpec((model, width), lambda b: (0, b))
    second_w = pl.BlockSpec((model, width), lambda b: (0, b + blocks))
    out_w = pl.BlockSpec((width, model), lambda b: (b, 0))

    def thin(height):
        return pl.BlockSpec((height, width), lambda b: (0, b))

    def fixed(*dims_of):
        return pl.BlockSpec(dims_of, lambda b: (0,) * len(dims_of))

    scalars = pl.BlockSpec(memory_space=pltpu.SMEM)
    offset_buf = pltpu.VMEM((rows + 8, lanes), jnp.int32)
    packed = thin(plan["rows"])

    pair = (chunks, 2 * chunk, lanes)
    pair = (chunks, 2 * chunk, lanes)
    anywhere = pl.BlockSpec(memory_space=pl.ANY)
    small_half = (2, plan["rows"] // 2, piece)
    in_piece = (in_rows, width)
    shares = 2
    in_share = (in_rows, inner // shares)
    out_share = (out_proj.shape[0], model // shares)
    lines = [shape((shares, depth) + half_shape(block), half) for block in (in_share, out_share)]
    (
        branch,
        signal,
        slope,
        projected,
        flipped,
        normed,
        grad_low,
        write_pair,
        read_pair,
        small,
        gain_value,
        in_blocks,
        gate_lines,
        out_lines,
    ) = compute_call(
        functools.partial(front_kernel, plan, dims, tuple(smalls)),
        "front",
        blocks,
        [scalars, whole, whole, whole] + [whole] * len(smalls) + [whole] * 2,
        [tall, tall, tall] + [whole] * 8 + [anywhere] * 3,
        [
            shape((rows, inner)),
            shape((rows, inner), half),
            shape((rows, inner)),
            shape((rows, lanes)),
            shape((model, rows), half),
            shape((rows, model), half),
            shape((rows, model), half),
            shape(pair, half),
            shape(pair, half),
            shape((plan["rows"], inner), half),
            shape((1, model)),
            shape((blocks, depth, planes) + in_piece, half),
            *lines,
        ],
        [
            offset_buf,
            pltpu.VMEM((plan["rows"], piece), jnp.float32),
            pltpu.VMEM(small_half, half),
            pltpu.VMEM((blocks,) + in_piece, half),
            pltpu.VMEM((shares,) + in_share, half),
            pltpu.VMEM((shares,) + out_share, half),
            pltpu.VMEM((depth, planes) + small_half, half),
            pltpu.VMEM((blocks, depth, planes) + in_piece, half),
            pltpu.SemaphoreType.DMA((blocks,)),
            pltpu.VMEM((8, piece), jnp.float32),
            pltpu.VMEM((number, 8, piece), jnp.float32),
            pltpu.SemaphoreType.DMA((number,)),
            pltpu.SemaphoreType.DMA((number,)),
        ]
        + Gather.sems(1 + blocks, dims)
        + Rise.sems(2 * shares, dims),
        4 * rows * model * inner,
        (seq_lengths, tokens, cotangent, mask_row, *smalls.values(), in_proj, out_proj),
        collective_id=0,
    )
    groups = 2
    part, pieces = rows // groups, chunks // groups
    row_block = pltpu.VMEM((pieces, chunk, width), jnp.float32)
    spread_block = pltpu.VMEM((rows, size, lanes), jnp.float32)
    fold_block = pltpu.VMEM((width // lanes, chunk * chunk, lanes), jnp.float32)

    def by_group(order, *dims_of):
        middle = (0,) * (len(dims_of) - 2)
        return pl.BlockSpec(dims_of, lambda b, g: (order(g),) + middle + (b,))

    def by_token(order, *dims_of):
        return pl.BlockSpec(dims_of, lambda b, g: (order(g),) + (0,) * (len(dims_of) - 1))

    def by_channel(height):
        return pl.BlockSpec((height, width), lambda b, g: (0, b))

    def onward(g):
        return g

    def backward(g):
        return groups - 1 - g

    states, step, core, begins, gate_blocks, out_blocks = compute_call(
        functools.partial(forward_kernel, plan, dims),
        "forward",
        (blocks, groups),
        [
            scalars,
            by_token(onward, part, lanes),
            by_channel(plan["rows"]),
            by_group(onward, part, width),
            whole,
            whole,
            anywhere,
            anywhere,
        ],
        [
            by_group(onward, part, size, width),
            by_group(onward, pieces, chunk, width),
            by_group(onward, pieces, chunk, width),
            by_group(onward, 1, size, width),
            anywhere,
            anywhere,
        ],
        [
            shape((rows, size, inner)),
            shape((chunks, chunk, inner)),
            shape((chunks, chunk, inner)),
            shape((groups, size, inner)),
            shape((shares, depth, planes) + in_share, half),
            shape((shares, depth, planes) + out_share, half),
        ],
        [
            offset_buf,
            pltpu.VMEM((part, width), jnp.float32),
            row_block,
            row_block,
            spread_block,
            spread_block,
            fold_block,
            fold_block,
            pltpu.VMEM((size, width), jnp.float32),
        ]
        + Gather.sems(2 * shares, dims),
        15 * rows * inner * size,
        (seq_lengths, projected, small, signal, write_pair, read_pair, gate_lines, out_lines),
        collective_id=2,
    )
    split = in_share[1] // width
    weights = pl.BlockSpec((None, number, in_rows, width), lambda b: (b // split, 0, 0, b % split))
    per_block = width // out_share[0]
    out_pieces = pl.BlockSpec((shares, per_block) + out_share, lambda b: (0, b, 0, 0))
    branch_whole = in_blocks.reshape(blocks, number, *in_piece)
    gate_whole = gate_blocks.reshape(shares, number, *in_share)
    out_whole = out_blocks.reshape(shares, number, *out_share)
    core_grad, gate_grad, grad_skip, grad_outw, grad_in_gate, output = compute_call(
        functools.partial(middle_kernel, plan),
        "middle",
        blocks,
        [deep, packed, tall, weights, whole, out_pieces, whole, whole, whole],
        [
            deep,
            tall,
            thin(1),
            pl.BlockSpec((shares, width, out_share[1]), lambda b: (0, b, 0)),
            pl.BlockSpec((None, model, width), lambda b: (b // split, 0, b % split)),
            fixed(rows, model),
        ],
        [
            shape((chunks, chunk, inner)),
            shape((rows, inner), half),
            shape((1, inner)),
            shape((shares, inner, out_share[1]), half),
            shape((shares, model, in_share[1]), half),
            shape((rows, model), half),
        ],
        [
            pltpu.VMEM((rows, width), jnp.float32),
            pltpu.VMEM((rows, width), jnp.float32),
            pltpu.VMEM((rows, width), half),
            pltpu.VMEM((width, model), half),
            pltpu.VMEM((rows, model), jnp.float32),
        ],
        8 * rows * model * inner,
        (core, small, signal, gate_whole, grad_low, out_whole, flipped, normed, tokens),
    )
    early_grads = [
        grad_outw.reshape((shares, depth, planes) + out_share),
        grad_in_gate.reshape((shares, depth, planes) + in_share),
    ]
    early_sums = [shape(out_proj.shape), shape((in_rows, inner))]
    early_pieces = [shape((depth, planes) + block, half) for block in (in_share, out_share)] * shares
    (
        signal_grad,
        grad_stepw,
        grad_bias,
        grad_decaylog,
        flat,
        out_sum,
        in_gate_sum,
        early_squares,
    ) = compute_call(
        functools.partial(backward_kernel, plan, dims),
        "backward",
        (blocks, groups),
        [
            scalars,
            by_token(backward, part, lanes),
            by_channel(plan["rows"]),
            by_group(backward, part, width),
            whole,
            whole,
            by_group(backward, pieces, chunk, width),
            by_group(backward, pieces, chunk, width),
            by_group(backward, part, size, width),
            by_group(backward, 1, size, width),
            anywhere,
            anywhere,
        ],
        [
            by_group(backward, part, width),
            by_channel(rank),
            by_channel(1),
            by_channel(size),
            whole,
        ]
        + [whole] * 3,
        [
            shape((rows, inner)),
            shape((rank, inner)),
            shape((1, inner)),
            shape((size, inner)),
            shape((rows, lanes), half),
            *early_sums,
            shape((8, lanes)),
        ],
        [
            offset_buf,
            row_block,
            row_block,
            spread_block,
            spread_block,
            fold_block,
            fold_block,
            fold_block,
            fold_block,
            row_block,
            row_block,
            pltpu.VMEM((part, width), half),
            pltpu.VMEM((size, width), jnp.float32),
            pltpu.VMEM((chunks, chunk, lanes), jnp.float32),
            spread_block,
            spread_block,
        ]
        + [pltpu.VMEM((shares,) + block, jnp.float32) for block in (in_share, out_share)]
        + Reduce.rooms(dims, early_pieces, False)
        + Reduce.sems(2 * shares, dims),
        40 * rows * inner * size,
        (
            seq_lengths,
            projected,
            small,
            signal,
            write_pair,
            read_pair,
            step,
            core_grad,
            states,
            begins,
            *early_grads,
        ),
        collective_id=3,
    )

    plain_rows = np.zeros((plan["rows"], piece), np.float32)
    for name in ("bias", "decay", "skip"):
        first, count = plan[name]
        plain_rows[first : first + count] = 1.0
    late_grads = [shape((depth, planes) + small_half, half)]
    late_grads += [shape((depth, planes, in_rows, width), half)] * blocks
    taps_n = conv_weight.shape[0]
    late = {"taps": (0, taps_n), "shift": (taps_n, 1), "gain": (taps_n + 1, 1)}
    late_block = (8, piece)

    early_tall = pl.BlockSpec((rows, width), lambda b: (0, jnp.minimum(b, blocks - 1)))
    late_tall = pl.BlockSpec((rows, width), lambda b: (0, jnp.maximum(b - blocks, 0)))
    tokens_grad, in_branch_sum, small_sum, late_sum, norms = compute_call(
        functools.partial(back_kernel, plan, dims),
        "back",
        2 * blocks,
        [scalars, whole, whole, whole]
        + [pl.BlockSpec((plan["rows"], width), lambda b: (0, jnp.minimum(b, blocks - 1))), whole]
        + [early_tall, whole, early_tall, early_tall, late_tall, whole]
        + [
            pl.BlockSpec((None, number, in_rows, width), lambda b: (jnp.maximum(b - blocks, 0), 0, 0, 0)),
            pl.BlockSpec(
                (None, number, in_rows, width),
                lambda b: (jnp.maximum(b - blocks, 0) // split, 0, 0, jnp.maximum(b - blocks, 0) % split),
            ),
        ]
        + [whole] * 6,
        [whole] * 5,
        [
            shape((rows, model), half),
            shape((in_rows, inner)),
            shape(small_half),
            shape(late_block),
            shape((2, 8, lanes)),
        ],
        [
            offset_buf,
            pltpu.VMEM((rows + 8, width), jnp.float32),
            pltpu.VMEM((blocks, rows, width), half),
            pltpu.VMEM((rows, model), jnp.float32),
            pltpu.VMEM((blocks,) + late_grads[1].shape, half),
            pltpu.VMEM(late_grads[0].shape, late_grads[0].dtype),
            pltpu.VMEM((number,) + late_block, jnp.float32),
            pltpu.VMEM((2, number) + late_block, jnp.float32),
            pltpu.VMEM((2, 8, lanes), jnp.float32),
            pltpu.VMEM((2, number, 2, 8, lanes), jnp.float32),
            pltpu.VMEM((blocks, in_rows, width), jnp.float32),
            pltpu.VMEM(small_half, jnp.float32),
            pltpu.SemaphoreType.DMA((2, 2, number)),
            pltpu.SemaphoreType.DMA((2, 2, number)),
        ]
        + Reduce.rooms(dims, late_grads, True)
        + Reduce.sems(blocks + 1, dims),
        8 * rows * model * inner,
        (
            seq_lengths,
            tokens,
            grad_low,
            gain_value,
            small,
            flat,
            branch,
            signal,
            slope,
            signal_grad,
            gate_grad,
            flipped,
            branch_whole,
            gate_whole,
            grad_stepw,
            grad_bias,
            grad_decaylog,
            grad_skip,
            jnp.asarray(plain_rows.reshape(small_half)),
            early_squares,
        ),
        collective_id=1,
    )

    names = ("gain", "taps", "shift", "select", "step", "bias", "decay", "skip")
    own = (norm_gain, conv_weight, conv_bias, select_proj, step_proj, step_bias, decay_log, skip_scale)
    in_grad, out_grad, grad_tokens, gain_grad, *small_grads, decay_sq, plain_sq = pl.pallas_call(
        functools.partial(finish_kernel, plan, names, late),
        in_specs=[whole] * 7,
        out_specs=[whole] * (3 + len(names)) + [scalars] * 2,
        out_shape=[shape(in_proj.shape), shape(out_proj.shape), shape(tokens.shape, half)]
        + [shape(array.shape) for array in own]
        + [shape((1, 1))] * 2,
        name="finish",
    )(
        tokens_grad,
        in_branch_sum,
        in_gate_sum,
        out_sum,
        small_sum.reshape(plan["rows"], piece),
        late_sum,
        norms,
    )
    return (
        output,
        grad_tokens,
        gain_grad,
        in_grad,
        *small_grads,
        out_grad,
        decay_sq[0, 0],
        plain_sq[0, 0],
    )


def solution(mesh):
    placed = (
        P(("wide", "narrow"), None),
        P(("wide", "narrow"), None),
        P(("wide", "narrow")),
        P(("wide", "narrow"), None),
        P("narrow"),
        P("narrow", None),
        P(None, "narrow"),
        P("narrow"),
        P(None, "narrow"),
        P(None, "narrow"),
        P("narrow"),
        P(None, "narrow"),
        P("narrow"),
        P("narrow", None),
    )
    return jax.shard_map(
        functools.partial(per_device, grid_of(mesh)),
        mesh=mesh,
        in_specs=placed,
        out_specs=(
            P(("wide", "narrow"), None),
            P(("wide", "narrow"), None),
            P("narrow"),
            P("narrow", None),
            P(None, "narrow"),
            P("narrow"),
            P(None, "narrow"),
            P(None, "narrow"),
            P("narrow"),
            P(None, "narrow"),
            P("narrow"),
            P("narrow", None),
            P(),
            P(),
        ),
        check_vma=False,
    )
```

```python
import functools
import math

import jax
import jax.numpy as jnp
import numpy as np
from jax import lax
from jax.experimental import pallas as pl
from jax.experimental.pallas import tpu as pltpu
from jax.sharding import PartitionSpec as P

epsilon = 1e-05
chunk = 8
lanes = 128
log2e = math.log2(math.e)
ln2 = math.log(2.0)
far = 1e30
tiny = 1e-30


def contract(left, right, left_dim, right_dim):
    return lax.dot_general(
        left, right, (((left_dim,), (right_dim,)), ((), ())), preferred_element_type=jnp.float32
    )


def row_loop(rows, group, body, initial):
    def some(index, carry):
        return body(index, pl.ds(pl.multiple_of(index * group, group), group), carry)

    return lax.fori_loop(0, rows // group, some, initial)


def cut(tile):
    return pl.ds(tile * lanes, lanes)


def sigmoid(values):
    return 0.5 * jnp.tanh(0.5 * values) + 0.5


def softplus(values):
    small = jnp.exp(-jnp.abs(values))
    series = small * (1.0 - small * (0.5 - small * (1.0 / 3.0 - 0.25 * small)))
    return jnp.maximum(values, 0.0) + jnp.where(small < 0.03, series, jnp.log(1.0 + small))


def slope_of(step):
    return 1.0 - jnp.exp(-step)


def fill_offsets(lengths_ref, offset_buf, rows):
    place = lax.broadcasted_iota(jnp.int32, offset_buf.shape, 0)
    start = jnp.zeros(offset_buf.shape, jnp.int32)
    ahead = jnp.int32(0)
    for index in range(lengths_ref.shape[1] - 1):
        ahead = ahead + lengths_ref[0, index]
        start = jnp.where(place >= ahead, ahead, start)
    offset_buf[...] = jnp.where(place < rows, place - start, 0)


def small_rows(small_ref, first, count):
    base = first // 16 * 16
    tall = -(-(first + count - base) // 16) * 16
    return small_ref[base : base + tall, :].astype(jnp.float32)[first - base : first - base + count]


def eight(values):
    total = values[:8]
    for row in range(8, values.shape[0], 8):
        total = total + values[row : row + 8]
    return total


def conv_rows(index, at, group, tile, branch_ref, offset_buf, taps, shift):
    count = taps.shape[0]
    here = slice(tile * lanes, (tile + 1) * lanes)
    current = branch_ref[at, cut(tile)]
    before = branch_ref[pl.ds(pl.multiple_of(jnp.maximum(index * group - 8, 0), 8), 8), cut(tile)]
    both = jnp.concatenate([before, current], axis=0)
    offsets = offset_buf[at, :]
    summed = shift[:, here] + taps[count - 1 : count, here] * current
    for tap in range(count - 1):
        lag = count - 1 - tap
        read = jnp.where(offsets >= lag, pltpu.roll(both, lag, 0)[8:], 0.0)
        summed = summed + taps[tap : tap + 1, here] * read
    return summed


def rows_of(blocks):
    return as_matrix(blocks[...][None])


def as_matrix(blocks):
    columns = blocks.shape[3]
    if blocks.shape[2] % 16:
        return blocks.astype(jnp.float32).reshape(-1, columns).astype(blocks.dtype)
    return blocks.reshape(-1, columns)


def front_kernel(
    plan,
    dims,
    names,
    lengths_ref,
    tokens_ref,
    cotangent_ref,
    mask_ref,
    *refs,
):
    smalls, in_ref, out_ref, refs = refs[: len(names)], refs[len(names)], refs[len(names) + 1], refs[len(names) + 2 :]
    branch_ref, signal_ref, slope_ref, projected_ref, flipped_ref, normed_ref, low_ref = refs[:7]
    write_pair, read_pair, small_out, gain_ref, whole_ref, gate_lines, out_lines = refs[7:14]
    offset_buf, pack_buf, own_small, own_in, own_gate, own_out, land_small, land_in, store_sem = refs[14:23]
    own_gain, land_gain, gain_send, gain_recv = refs[23:27]
    rows = tokens_ref.shape[0]
    width = branch_ref.shape[1]
    block = pl.program_id(0)
    last = whole_ref.shape[0]
    shares = own_out.shape[0]
    gather = Gather(
        dims,
        [own_small] + [own_in.at[index] for index in range(last)],
        [land_small] + [land_in.at[index] for index in range(last)],
        refs[27:30],
    )
    rise = Rise(
        dims,
        [own.at[index] for index in range(shares) for own in (own_gate, own_out)],
        [lines.at[index] for index in range(shares) for lines in (gate_lines, out_lines)],
        refs[30:],
    )
    tall = pack_buf.shape[0] // 2

    def stored(index):
        return pltpu.make_async_copy(land_in.at[index], whole_ref.at[index], store_sem.at[index])

    def move_on(plan_of_moves):
        for moment, legs in plan_of_moves:

            @pl.when(block == moment)
            def _(legs=legs):
                for which, number in legs:
                    gather.leg(which, number)

    @pl.when(block == 0)
    def _():
        pack_buf[...] = jnp.zeros_like(pack_buf)
        for name, ref in zip(names, smalls):
            first, height = plan[name]
            pack_buf[first : first + height, : ref.shape[1]] = ref[...]
        own_gain[...] = jnp.zeros_like(own_gain)
        own_gain[0:1, : gain_ref.shape[1] // land_gain.shape[0]] = smalls[names.index("gain")][...]
        for side in range(2):
            own_small[side] = pack_buf[side * tall : (side + 1) * tall, :].astype(own_small.dtype)
        for index in range(last):
            own_in[index] = in_ref[:, index * width : (index + 1) * width].astype(own_in.dtype)
        place = Place(dims)
        place.greet(everyone=True)
        send_to_all(place, lambda target: own_gain, land_gain, gain_send, gain_recv)
        for index in (1, 0) + tuple(range(2, last + 1)):
            gather.start(index)
        first = last * width
        for index in range(shares):
            each = own_gate.shape[2]
            own_gate[index] = in_ref[:, first + index * each : first + (index + 1) * each].astype(own_gate.dtype)
            each = own_out.shape[2]
            own_out[index] = out_ref[:, index * each : (index + 1) * each].astype(own_out.dtype)
        fill_offsets(lengths_ref, offset_buf, rows)
        gather.leg(1, 1)
        gather.leg(0, 1)
        wait_for_all(place, own_gain[...], land_gain, gain_send, gain_recv)
        each = gain_ref.shape[1] // land_gain.shape[0]
        for owner in range(land_gain.shape[0]):
            gain_ref[:, owner * each : (owner + 1) * each] = (
                land_gain[owner, 0:1, :each].astype(jnp.bfloat16).astype(jnp.float32)
            )

        def norm(index, at, carry):
            residual = tokens_ref[at, :].astype(jnp.float32)
            scale = lax.rsqrt(jnp.mean(residual * residual, axis=1, keepdims=True) + epsilon)
            normed_ref[at, :] = (residual * scale * gain_ref[...]).astype(normed_ref.dtype)
            return carry

        row_loop(rows, 16, norm, 0)
        gather.leg(1, 2)
        gather.leg(0, 2)
        gather.leg(2, 1)
        rise.start(0)
        gather.leg(1, 3)
        gather.leg(0, 3)
        gather.leg(2, 2)
        projected_ref[...] = jnp.zeros_like(projected_ref)

    for index in range(last):

        @pl.when(block == index)
        def _(index=index):
            gather.arrive(index + 1)
            stored(index).start()

    branch_w = as_matrix(land_in[block])
    branch_ref[...] = jnp.dot(normed_ref[...], branch_w, preferred_element_type=jnp.float32)
    move_on(((0, ((3, 1), (2, 3))), (1, ((4, 2), (3, 3))), (2, ((4, 3),))))
    pl.when(block == 0)(functools.partial(rise.start, 1))

    @pl.when(block == 0)
    def _():
        gather.arrive(0)
        share = land_small.shape[4]
        for z in range(land_small.shape[0]):
            for plane in range(land_small.shape[1]):
                owner = z * land_small.shape[1] + plane
                for side in range(2):
                    small_out[side * tall : (side + 1) * tall, owner * share : (owner + 1) * share] = land_small[
                        z, plane, side
                    ]

    small_ref = small_out.at[:, pl.ds(pl.multiple_of(block * width, width), width)]
    taps = small_rows(small_ref, *plan["taps"])
    shift = small_rows(small_ref, *plan["shift"])

    def some(index, at, carry):
        for tile in range(width // lanes):
            summed = conv_rows(index, at, 32, tile, branch_ref, offset_buf, taps, shift)
            sigma = sigmoid(summed)
            active = summed * sigma
            signal_ref[at, cut(tile)] = active.astype(signal_ref.dtype)
            slope_ref[at, cut(tile)] = sigma + active * (1.0 - sigma)
        return carry

    row_loop(rows, 32, some, 0)
    move_on(((0, ((4, 1), (3, 2))),))

    @pl.when(block == 0)
    def _():
        for index in range(2, 2 * shares):
            rise.start(index)

    projected_ref[...] += contract(signal_ref[...], small_ref[:lanes, :], 1, 1)

    @pl.when(block == pl.num_programs(0) - 1)
    def _():
        high, low = high_low(projected_ref[...])
        own = own_tokens(rows)
        rank = plan["step"][1]
        size = plan["decay"][1]
        entry = lax.broadcasted_iota(jnp.int32, (lanes, lanes), 0)
        lane = lax.rem(lax.broadcasted_iota(jnp.int32, (lanes, lanes), 1), size)
        for first, pair in ((rank, write_pair), (rank + size, read_pair)):
            spread = (entry == lane + first).astype(jnp.bfloat16)
            parts = [
                (jnp.dot(part.astype(jnp.bfloat16), spread, preferred_element_type=jnp.float32) * own).reshape(
                    rows // chunk, chunk, lanes
                )
                for part in (high, low)
            ]
            pair[...] = jnp.concatenate(parts, axis=1).astype(pair.dtype)
        flipped_ref[...] = normed_ref[...].T
        down = lax.broadcasted_iota(jnp.int32, (rows, rows), 0)
        along = lax.broadcasted_iota(jnp.int32, (rows, rows), 1)
        diagonal = jnp.where(down == along, mask_ref[...].astype(jnp.float32), 0.0).astype(low_ref.dtype)
        low_ref[...] = jnp.dot(
            diagonal, cotangent_ref[...], preferred_element_type=jnp.float32
        ).astype(low_ref.dtype)
        for index in range(last + 1):
            gather.drain(index)
        for index in range(2 * shares):
            rise.finish(index)
        for index in range(last):
            stored(index).wait()


def high_low(values):
    high = values.astype(jnp.bfloat16).astype(jnp.float32)
    return high, values - high


def own_tokens(rows):
    token = lax.rem(lax.broadcasted_iota(jnp.int32, (rows, lanes), 0), chunk)
    return (token == lax.div(lax.broadcasted_iota(jnp.int32, (rows, lanes), 1), lanes // chunk)).astype(
        jnp.float32
    )


def spread_all(pairs, target):
    some = 8

    def spread(index, carry):
        rows = jnp.concatenate([pairs[index * some + number] for number in range(some)], axis=1)
        wide = contract(rows, jnp.ones((rows.shape[0], lanes), rows.dtype), 0, 0)
        target[pl.ds(index * some * chunk, some * chunk)] = wide.reshape(some * chunk, -1, lanes)
        return carry

    lax.fori_loop(0, pairs.shape[0] // some, spread, 0)


def joined(first, second, hop):
    low = lax.bitwise_and(lax.broadcasted_iota(jnp.int32, first.shape, 0), hop) == 0
    return jnp.where(low, first, second) + pltpu.roll(jnp.where(low, second, first), hop, 0)


def folded(buffer, tile):
    parts = [buffer[tile, pl.ds(row * chunk, chunk), :] for row in range(chunk)]
    hop = 1
    while len(parts) > 1:
        parts = [joined(parts[index], parts[index + 1], hop) for index in range(0, len(parts), 2)]
        hop *= 2
    return parts[0]


def forward_kernel(
    plan,
    dims,
    lengths_ref,
    projected_ref,
    small_ref,
    signal_ref,
    write_pair,
    read_pair,
    gate_lines,
    out_lines,
    states_ref,
    step_ref,
    core_ref,
    begin_ref,
    gate_whole,
    out_whole,
    offset_buf,
    pre_buf,
    decay_step,
    flows,
    write_wide,
    read_wide,
    fold_a,
    fold_b,
    held_buf,
    *sems,
):
    rows, width = pre_buf.shape
    size = plan["decay"][1]
    half_size = size // 2
    tiles = width // lanes
    chunks = rows // chunk
    rank = plan["step"][1]
    group = pl.program_id(1)
    groups = pl.num_programs(1)
    moment = pl.program_id(0) * groups + group
    moments = pl.num_programs(0) * groups
    shares = gate_whole.shape[0]
    count = 2 * shares
    gather = Gather(
        dims,
        [lines.at[index] for index in range(shares) for lines in (gate_lines, out_lines)],
        [whole.at[index] for index in range(shares) for whole in (gate_whole, out_whole)],
        sems,
        [whole.shape[3:] for _ in range(shares) for whole in (gate_whole, out_whole)],
    )

    @pl.when(moment == 0)
    def _():
        Place(dims).greet()
        for which in range(count):
            gather.start(which)
        fill_offsets(lengths_ref, offset_buf, offset_buf.shape[0] - 8)
        spread_all(write_pair, write_wide)
        spread_all(read_pair, read_wide)

    @pl.when(group == 0)
    def _():
        held_buf[...] = jnp.zeros_like(held_buf)

    begin_ref[0] = held_buf[...]
    pre_buf[...] = jnp.dot(
        projected_ref[:, :rank].astype(small_ref.dtype),
        small_ref[pl.ds(plan["step"][0], rank), :],
        preferred_element_type=jnp.float32,
    )
    bias = small_rows(small_ref, *plan["bias"])

    def before(index, at, carry):
        spot = pl.ds(pl.multiple_of(index * 4, 4), 4)
        inside = offset_buf[pl.ds(pl.multiple_of(group * rows + index * 32, 32), 32), :] > 0
        for tile in range(tiles):
            step = softplus(pre_buf[at, cut(tile)] + bias[:, tile * lanes : (tile + 1) * lanes])
            step_ref[spot, :, cut(tile)] = step.reshape(4, chunk, lanes)
            decay_step[spot, :, cut(tile)] = jnp.where(inside, step, far).reshape(4, chunk, lanes)
            flow = step * signal_ref[at, cut(tile)].astype(jnp.float32)
            flows[spot, :, cut(tile)] = flow.reshape(4, chunk, lanes)
        return carry

    row_loop(rows, 4 * chunk, before, 0)
    rates = -jnp.exp(small_rows(small_ref, *plan["decay"])) * log2e
    rates = [rates[:, tile * lanes : (tile + 1) * lanes] for tile in range(tiles)]

    def advance(index, held, fold_buf):
        held = list(held)
        for place in range(chunk):
            now = index * chunk + place
            write_now = write_wide[group * rows + now]
            read_now = read_wide[group * rows + now]
            for tile in range(tiles):
                decay = jnp.exp2(rates[tile] * decay_step[index, pl.ds(place, 1), cut(tile)])
                fresh = decay * held[tile] + write_now * flows[index, pl.ds(place, 1), cut(tile)]
                held[tile] = fresh
                states_ref[now, :, cut(tile)] = fresh
                product = read_now * fresh
                fold_buf[tile, pl.ds(place * chunk, chunk), :] = product[:half_size] + product[half_size:]
        return tuple(held)

    def forward(pair, held):
        index = 2 * pair
        held = advance(index, held, fold_a)
        for tile in range(tiles):
            core_ref[index, :, cut(tile)] = folded(fold_a, tile)
        held = advance(index + 1, held, fold_b)
        for tile in range(tiles):
            core_ref[index + 1, :, cut(tile)] = folded(fold_b, tile)
        return held

    held = tuple(held_buf[:, cut(tile)] for tile in range(tiles))
    schedule = {}
    for which in range(count):
        for number in (2, 3):
            point = ((3, 5, 7, 9), (10, 12, 13, 15))[number - 2][which]
            schedule.setdefault(point, []).append((which, number))

    def move_on(legs):
        for which, number in legs:
            gather.leg(which, number)

    for half_loop in range(2):
        for point, legs in sorted(schedule.items()):
            if point < 16 and point % 2 == half_loop:
                pl.when(moment == point // 2)(functools.partial(move_on, legs))
        held = lax.fori_loop(half_loop * chunks // 4, (half_loop + 1) * chunks // 4, forward, held)
    for tile in range(tiles):
        held_buf[:, cut(tile)] = held[tile]

    @pl.when(moment == moments - 1)
    def _():
        for which in range(count):
            gather.arrive(which)
        for which in range(count):
            gather.drain(which)


def middle_kernel(
    plan,
    core_ref,
    small_ref,
    signal_ref,
    gate_w,
    low_ref,
    out_w,
    flipped_ref,
    normed_ref,
    tokens_ref,
    core_grad_ref,
    gate_grad_ref,
    skip_grad_ref,
    out_grad_ref,
    in_grad_ref,
    output_ref,
    pre_buf,
    gate_buf,
    gated_buf,
    out_buf,
    total,
):
    rows, width = pre_buf.shape
    tiles = width // lanes
    block = pl.program_id(0)
    each = out_w.shape[3]
    for index in range(out_w.shape[0]):
        out_buf[:, index * each : (index + 1) * each] = as_matrix(out_w[index][None])
    gate_buf[...] = jnp.dot(normed_ref[...], rows_of(gate_w), preferred_element_type=jnp.float32)
    pre_buf[...] = contract(low_ref[...], out_buf[...], 1, 1)
    skip = small_rows(small_ref, *plan["skip"])

    def after(index, at, carry):
        spot = pl.ds(pl.multiple_of(index * 4, 4), 4)
        sums = []
        for tile in range(tiles):
            signal = signal_ref[at, cut(tile)].astype(jnp.float32)
            core = core_ref[spot, :, cut(tile)].reshape(4 * chunk, lanes)
            core = core + skip[:, tile * lanes : (tile + 1) * lanes] * signal
            gate = gate_buf[at, cut(tile)]
            sigma = sigmoid(gate)
            active = gate * sigma
            gated_buf[at, cut(tile)] = (core * active).astype(gated_buf.dtype)
            grad_gated = pre_buf[at, cut(tile)]
            grad_core = grad_gated * active
            core_grad_ref[spot, :, cut(tile)] = grad_core.reshape(4, chunk, lanes)
            slope = sigma + active * (1.0 - sigma)
            gate_grad_ref[at, cut(tile)] = (grad_gated * core * slope).astype(gate_grad_ref.dtype)
            sums.append(carry[tile] + eight(grad_core * signal))
        return tuple(sums)

    zero_rows = jnp.zeros((8, lanes), jnp.float32)
    skips = row_loop(rows, 4 * chunk, after, (zero_rows,) * tiles)
    for tile in range(tiles):
        skip_grad_ref[:, cut(tile)] = jnp.sum(skips[tile], axis=0, keepdims=True)
    out_grad = contract(gated_buf[...], low_ref[...], 0, 0).astype(out_grad_ref.dtype)
    for index in range(out_w.shape[0]):
        out_grad_ref[index] = out_grad[:, index * each : (index + 1) * each]
    in_grad_ref[...] = jnp.dot(
        flipped_ref[...], gate_grad_ref[...], preferred_element_type=jnp.float32
    ).astype(in_grad_ref.dtype)
    piece = jnp.dot(gated_buf[...], out_buf[...], preferred_element_type=jnp.float32)

    @pl.when(block == 0)
    def _():
        total[...] = piece

    @pl.when(block > 0)
    def _():
        total[...] += piece

    @pl.when(block == pl.num_programs(0) - 1)
    def _():
        output_ref[...] = (tokens_ref[...].astype(jnp.float32) + total[...]).astype(output_ref.dtype)


def backward_kernel(
    plan,
    dims,
    lengths_ref,
    projected_ref,
    small_ref,
    signal_ref,
    write_pair,
    read_pair,
    step_ref,
    core_grad_ref,
    states_ref,
    begin_ref,
    out_grad_ref,
    in_grad_ref,
    signal_grad_ref,
    step_w_grad_ref,
    bias_grad_ref,
    decay_grad_ref,
    flat_ref,
    out_sum_ref,
    in_sum_ref,
    square_ref,
    offset_buf,
    decay_step,
    flows,
    write_wide,
    read_wide,
    first_a,
    first_b,
    second_a,
    second_b,
    through_buf,
    scaled_buf,
    low_buf,
    incoming_buf,
    rank_buf,
    write_buf,
    read_buf,
    *parts,
):
    rows, width = low_buf.shape
    rank = plan["step"][1]
    size = plan["decay"][1]
    half_size = size // 2
    tiles = width // lanes
    chunks = rows // chunk
    block = pl.program_id(0)
    turn = pl.program_id(1)
    groups = pl.num_programs(1)
    group = groups - 1 - turn
    moment = block * groups + turn
    moments = pl.num_programs(0) * groups
    gate_result, out_result, parts = parts[0], parts[1], parts[2:]
    pieces = gate_result.shape[0]
    count = 2 * pieces

    both = ((in_grad_ref, gate_result), (out_grad_ref, out_result))
    reduce = Reduce(
        dims,
        [ref.at[index] for index in range(pieces) for ref, _ in both],
        parts[: 6 * count],
        parts[6 * count :],
        [result.at[index] for index in range(pieces) for _, result in both],
        False,
    )

    @pl.when(moment == 0)
    def _():
        Place(dims).greet()
        for which in range(count):
            reduce.start(which)
        fill_offsets(lengths_ref, offset_buf, offset_buf.shape[0] - 8)
        spread_all(write_pair, write_wide)
        spread_all(read_pair, read_wide)
        write_buf[...] = jnp.zeros_like(write_buf)
        read_buf[...] = jnp.zeros_like(read_buf)
        rank_buf[...] = jnp.zeros_like(rank_buf)

    @pl.when(turn == 0)
    def _():
        incoming_buf[...] = jnp.zeros_like(incoming_buf)
        decay_grad_ref[...] = jnp.zeros_like(decay_grad_ref)
        bias_grad_ref[...] = jnp.zeros_like(bias_grad_ref)
        step_w_grad_ref[...] = jnp.zeros_like(step_w_grad_ref)

    def before(index, at, carry):
        spot = pl.ds(pl.multiple_of(index * 4, 4), 4)
        offsets = offset_buf[pl.ds(pl.multiple_of(group * rows + index * 32, 32), 32), :]
        inside = (offsets > 0).reshape(4, chunk, lanes)
        for tile in range(tiles):
            step = step_ref[spot, :, cut(tile)]
            decay_step[spot, :, cut(tile)] = jnp.where(inside, step, far)
            signal = signal_ref[at, cut(tile)].astype(jnp.float32).reshape(4, chunk, lanes)
            flows[spot, :, cut(tile)] = step * signal
        return carry

    row_loop(rows, 4 * chunk, before, 0)
    rates = -jnp.exp(small_rows(small_ref, *plan["decay"])) * log2e
    rates = [rates[:, tile * lanes : (tile + 1) * lanes] for tile in range(tiles)]

    def retreat(index, carried, first_buf, second_buf):
        incoming, decay_sums, current = (list(tiles_of) for tiles_of in carried)
        for place in range(chunk - 1, -1, -1):
            now = index * chunk + place
            token = group * rows + now
            write_now = write_wide[token]
            read_now = read_wide[token]
            read_sum = None
            write_sum = None
            for tile in range(tiles):
                grad_now = core_grad_ref[index, pl.ds(place, 1), cut(tile)]
                if place > 0:
                    earlier = states_ref[now - 1, :, cut(tile)]
                else:
                    earlier = jnp.where(
                        index > 0, states_ref[jnp.maximum(now - 1, 0), :, cut(tile)], begin_ref[0, :, cut(tile)]
                    )
                grad_state = incoming[tile] + read_now * grad_now
                through_read = current[tile] * grad_now
                current[tile] = earlier
                through_write = grad_state * flows[index, pl.ds(place, 1), cut(tile)]
                read_sum = through_read if read_sum is None else read_sum + through_read
                write_sum = through_write if write_sum is None else write_sum + through_write
                passed = grad_state * write_now
                first_buf[tile, pl.ds(place * chunk, chunk), :] = passed[:half_size] + passed[half_size:]
                exponent = rates[tile] * decay_step[index, pl.ds(place, 1), cut(tile)]
                leaving = jnp.exp2(exponent) * grad_state
                incoming[tile] = leaving
                weighted = (leaving * earlier) * exponent
                second_buf[tile, pl.ds(place * chunk, chunk), :] = weighted[:half_size] + weighted[half_size:]
                decay_sums[tile] = decay_sums[tile] + weighted
            read_buf[token] += read_sum
            write_buf[token] += write_sum
        return (tuple(incoming), tuple(decay_sums), tuple(current))

    def backward(pair, carried):
        index = chunks - 1 - 2 * pair
        for here, first_buf, second_buf in ((index, first_a, second_a), (index - 1, first_b, second_b)):
            carried = retreat(here, carried, first_buf, second_buf)
            for tile in range(tiles):
                through_buf[here, :, cut(tile)] = folded(first_buf, tile)
                scaled_buf[here, :, cut(tile)] = folded(second_buf, tile)
        return carried

    incoming = tuple(incoming_buf[:, cut(tile)] for tile in range(tiles))
    nothing = (jnp.zeros((size, lanes), jnp.float32),) * tiles
    current = tuple(states_ref[rows - 1, :, cut(tile)] for tile in range(tiles))
    schedule = {}
    for which in range(count):
        for number in (1, 2, 3):
            point = ((2, 4, 6, 8), (4, 6, 8, 10), (6, 8, 10, 12))[number - 1][which]
            schedule.setdefault(point, []).append((which, number))

    def move_on(legs):
        for which, number in legs:
            reduce.leg(which, number)

    carried = (incoming, nothing, current)
    for half_loop in range(2):
        for point, legs in sorted(schedule.items()):
            if point % 2 == half_loop:
                pl.when(moment == point // 2)(functools.partial(move_on, legs))
        carried = lax.fori_loop(half_loop * chunks // 4, (half_loop + 1) * chunks // 4, backward, carried)
    incoming, decay_sums, _ = carried
    for tile in range(tiles):
        incoming_buf[:, cut(tile)] = incoming[tile]
        decay_grad_ref[:, cut(tile)] += decay_sums[tile] * ln2
    skip = small_rows(small_ref, *plan["skip"])

    def after(index, at, carry):
        spot = pl.ds(pl.multiple_of(index * 4, 4), 4)
        sums = []
        for tile in range(tiles):
            signal = signal_ref[at, cut(tile)].astype(jnp.float32)
            step = step_ref[spot, :, cut(tile)].reshape(4 * chunk, lanes)
            through = through_buf[spot, :, cut(tile)].reshape(4 * chunk, lanes)
            scaled = scaled_buf[spot, :, cut(tile)].reshape(4 * chunk, lanes)
            core_grad = core_grad_ref[spot, :, cut(tile)].reshape(4 * chunk, lanes)
            grad_pre = (through * signal + ln2 * scaled / jnp.maximum(step, tiny)) * slope_of(step)
            low_buf[at, cut(tile)] = grad_pre.astype(low_buf.dtype)
            signal_grad_ref[at, cut(tile)] = (
                through * step + skip[:, tile * lanes : (tile + 1) * lanes] * core_grad
            )
            sums.append(carry[tile] + eight(grad_pre))
        return tuple(sums)

    zero_rows = jnp.zeros((8, lanes), jnp.float32)
    sums = row_loop(rows, 4 * chunk, after, (zero_rows,) * tiles)
    for tile in range(tiles):
        bias_grad_ref[:, cut(tile)] += jnp.sum(sums[tile], axis=0, keepdims=True)
    step_w_grad_ref[...] += contract(
        projected_ref[:, :rank].astype(low_buf.dtype), low_buf[...], 0, 0
    )
    step_w = small_ref[pl.ds(plan["step"][0], rank), :]
    step_w = jnp.concatenate([step_w, jnp.zeros((lanes - rank, width), step_w.dtype)], axis=0)
    rank_buf[pl.ds(group * chunks, chunks)] += contract(low_buf[...], step_w, 1, 1).reshape(
        chunks, chunk, lanes
    )

    @pl.when(moment == moments - 1)
    def _():
        squares = jnp.zeros((8, lanes), jnp.float32)
        for which in range(count):
            squares = squares + reduce.finish(which)[0]
        square_ref[...] = squares
        some = 8
        entry = lax.rem(lax.broadcasted_iota(jnp.int32, (some * chunk * size, lanes), 0), size)
        target = lax.broadcasted_iota(jnp.int32, (some * chunk * size, lanes), 1)
        ones = jnp.ones((lanes, lanes), jnp.bfloat16)

        def lay(index, carry):
            lot = pl.ds(index * some * chunk, some * chunk)
            for number, buffer in enumerate((write_buf, read_buf)):
                high, low = high_low(buffer[lot].reshape(some * chunk * size, lanes))
                summed = jnp.dot(high.astype(jnp.bfloat16), ones, preferred_element_type=jnp.float32)
                summed += jnp.dot(low.astype(jnp.bfloat16), ones, preferred_element_type=jnp.float32)
                summed = jnp.where(target == entry + rank + number * size, summed, 0.0)
                summed = jnp.sum(summed.reshape(some * chunk, size, lanes), axis=1)
                rank_buf[pl.ds(index * some, some)] += summed.reshape(some, chunk, lanes)
            return carry

        lax.fori_loop(0, rank_buf.shape[0] // some, lay, 0)
        flat_ref[...] = rank_buf[...].reshape(flat_ref.shape).astype(flat_ref.dtype)
        for which in range(count):
            reduce.settle(which)
        for index in range(pieces):
            for target, result in ((out_sum_ref, out_result), (in_sum_ref, gate_result)):
                each = result.shape[2]
                target[:, index * each : (index + 1) * each] = result[index]


def back_kernel(
    plan,
    dims,
    lengths_ref,
    tokens_ref,
    low_ref,
    gain_ref,
    small_ref,
    flat_ref,
    branch_ref,
    signal_ref,
    slope_ref,
    signal_grad_ref,
    gate_grad_ref,
    flipped_ref,
    branch_w,
    gate_w,
    step_w_grad_ref,
    bias_grad_ref,
    decay_grad_ref,
    skip_grad_ref,
    plain_ref,
    earlier_ref,
    tokens_grad_ref,
    in_sum_ref,
    small_sum_ref,
    late_sum_ref,
    norm_ref,
    offset_buf,
    conv_buf,
    mixed_buf,
    total,
    in_stage,
    small_stage,
    late_stage,
    late_land,
    norm_own,
    norm_land,
    in_result,
    small_result,
    direct_send,
    direct_recv,
    *parts,
):
    rows = tokens_ref.shape[0]
    width = branch_ref.shape[1]
    tiles = width // lanes
    block = pl.program_id(0)
    last = in_stage.shape[0]
    count = last + 1
    reduce = Reduce(
        dims,
        [small_stage] + [in_stage.at[index] for index in range(last)],
        parts[: 5 * count],
        parts[5 * count :],
        [small_result] + [in_result.at[index] for index in range(last)],
        True,
    )
    share = small_stage.shape[4]
    half_rows = small_stage.shape[3]
    planes = small_stage.shape[1]
    owners = small_stage.shape[0] * planes

    @pl.when(block == 0)
    def _():
        Place(dims).greet(everyone=True)
        fill_offsets(lengths_ref, offset_buf, rows)

    def move_on(plan_of_moves):
        for moment, legs in plan_of_moves:

            @pl.when(block == moment)
            def _(legs=legs):
                for which, number in legs:
                    reduce.leg(which, number)

    taps = small_rows(small_ref, *plan["taps"])
    taps_count = taps.shape[0]
    zero_rows = jnp.zeros((8, lanes), jnp.float32)

    @pl.when(block < last)
    def _():
        conv_buf[pl.ds(0, rows), :] = signal_grad_ref[...] + jnp.dot(
            flat_ref[...], small_ref[:lanes, :], preferred_element_type=jnp.float32
        )
        conv_buf[pl.ds(rows, 8), :] = jnp.zeros((8, width), jnp.float32)

        def through_conv(index, at, carry):
            sums = []
            for tile in range(tiles):
                grad_conv = conv_buf[at, cut(tile)] * slope_ref[at, cut(tile)]
                conv_buf[at, cut(tile)] = grad_conv
                sums.append(carry[tile] + eight(grad_conv))
            return tuple(sums)

        shift_sums = row_loop(rows, 32, through_conv, (zero_rows,) * tiles)
        def to_branch(index, at, carry):
            longer = pl.ds(pl.multiple_of(index * 32, 32), 40)
            offsets = offset_buf[longer, :]
            result = []
            for tile in range(tiles):
                here = slice(tile * lanes, (tile + 1) * lanes)
                grads = conv_buf[longer, cut(tile)]
                branch = branch_ref[at, cut(tile)]
                summed = taps[taps_count - 1 : taps_count, here] * grads[:32]
                sums = [None] * taps_count
                sums[taps_count - 1] = carry[tile][taps_count - 1] + eight(branch * grads[:32])
                for tap in range(taps_count - 1):
                    lag = taps_count - 1 - tap
                    moved = pltpu.roll(jnp.where(offsets >= lag, grads, 0.0), 40 - lag, 0)[:32]
                    summed = summed + taps[tap : tap + 1, here] * moved
                    sums[tap] = carry[tile][tap] + eight(branch * moved)
                mixed_buf[block, at, cut(tile)] = summed.astype(mixed_buf.dtype)
                result.append(tuple(sums))
            return tuple(result)

        sums = row_loop(rows, 32, to_branch, ((zero_rows,) * taps_count,) * tiles)
        in_grad = jnp.dot(flipped_ref[...], mixed_buf[block], preferred_element_type=jnp.float32)
        in_stage[block] = in_grad.reshape(in_stage.shape[1:]).astype(in_stage.dtype)
        for index in range(last):

            @pl.when(block == index)
            def _(index=index):
                reduce.start(index + 1)

        late = [
            jnp.concatenate(
                [jnp.sum(sums[tile][tap], axis=0, keepdims=True) for tap in range(taps_count)]
                + [jnp.sum(shift_sums[tile], axis=0, keepdims=True)]
                + [jnp.zeros((8 - taps_count - 1, lanes), jnp.float32)],
                axis=0,
            )
            for tile in range(tiles)
        ]
        late = jnp.concatenate(late, axis=1)
        for piece in range(width // share):
            late_stage[block * (width // share) + piece] = late[:, piece * share : (piece + 1) * share]
        move_on(
            (
                (1, ((1, 1), (0, 1))),
                (2, ((2, 1), (1, 2), (0, 2))),
                (3, ((3, 1), (2, 2), (1, 3), (0, 3))),
            )
        )

        @pl.when(block == 0)
        def _():
            select_grad = contract(flat_ref[...], signal_ref[...], 0, 0)
            step_first, step_tall = plan["step"]
            filler = jnp.zeros((2 * half_rows - step_first - step_tall, select_grad.shape[1]), jnp.float32)
            pieces = {
                "decay": decay_grad_ref[...],
                "bias": bias_grad_ref[...],
                "skip": skip_grad_ref[...],
                "step": step_w_grad_ref[...],
            }
            first = plan["select"][1]
            rows_now = [select_grad[:first]]
            for name in ("decay", "taps", "shift", "bias", "skip", "gain"):
                tall = plan[name][1]
                rows_now.append(
                    pieces[name] if name in pieces else jnp.zeros((tall, select_grad.shape[1]), jnp.float32)
                )
                first += tall
            rows_now.append(jnp.zeros((step_first - first, select_grad.shape[1]), jnp.float32))
            rows_now.append(pieces["step"])
            if filler.shape[0]:
                rows_now.append(filler)
            everything = jnp.concatenate(rows_now, axis=0)
            for owner in range(owners):
                for side in range(2):
                    small_stage[owner // planes, owner % planes, side] = everything[
                        side * half_rows : (side + 1) * half_rows, owner * share : (owner + 1) * share
                    ].astype(small_stage.dtype)
            reduce.start(0)

    @pl.when(block >= last)
    def _():
        grad_normed_piece = contract(mixed_buf[block - last], rows_of(branch_w), 1, 1)
        grad_normed_piece += contract(gate_grad_ref[...], rows_of(gate_w), 1, 1)

        @pl.when(block == last)
        def _():
            total[...] = grad_normed_piece

        @pl.when(block > last)
        def _():
            total[...] += grad_normed_piece

        move_on(((4, ((3, 2),)), (5, ((4, 1), (2, 3))), (6, ((3, 3),)), (7, ((4, 2),))))

    @pl.when(block == pl.num_programs(0) - 1)
    def _():
        def scaled_tokens(at):
            residual = tokens_ref[at, :].astype(jnp.float32)
            return residual, lax.rsqrt(jnp.mean(residual * residual, axis=1, keepdims=True) + epsilon)

        def gain_rows(index, at, carry):
            residual, scale = scaled_tokens(at)
            return carry + eight(total[at, :] * residual * scale)

        gains = row_loop(rows, 16, gain_rows, jnp.zeros((8, total.shape[1]), jnp.float32))
        gains = jnp.sum(gains, axis=0, keepdims=True)
        place = Place(dims)
        each = gains.shape[1] // owners
        for owner in range(owners):
            late_stage[owner, taps_count + 1 : taps_count + 2, :each] = gains[
                :, owner * each : (owner + 1) * each
            ]
        late_sems = direct_send.at[0], direct_recv.at[0]
        norm_sems = direct_send.at[1], direct_recv.at[1]
        send_to_everyone(place, lambda chip: late_stage.at[chip], late_land, *late_sems)
        reduce.leg(4, 3)

        def token_rows(index, at, carry):
            residual, scale = scaled_tokens(at)
            weighted = total[at, :] * gain_ref[...]
            inner = jnp.mean(weighted * residual, axis=1, keepdims=True)
            grad_y = low_ref[at, :].astype(jnp.float32)
            result = grad_y + (scale * weighted - residual * (scale * scale * scale) * inner)
            tokens_grad_ref[at, :] = result.astype(tokens_grad_ref.dtype)
            return carry

        row_loop(rows, 16, token_rows, 0)
        more, plain = reduce.finish(0, plain_ref)
        kept = earlier_ref[...] + more
        for index in range(1, count - 1):
            kept = kept + reduce.finish(index)[0]
        late_sum = sum_of_everyone(place, late_stage[place.me], late_land, *late_sems)
        late_sum_ref[...] = late_sum
        kept = kept + folded_squares(late_sum * late_sum) * (1 - place.core).astype(jnp.float32)
        kept = kept + reduce.finish(count - 1)[0]
        norm_own[...] = jnp.stack([kept, plain])
        send_to_everyone(place, lambda chip: norm_own, norm_land, *norm_sems)
        norm_ref[...] = sum_of_everyone(place, norm_own[...], norm_land, *norm_sems)
        for index in range(count):
            reduce.settle(index)
        for index in range(last):
            in_sum_ref[:, index * width : (index + 1) * width] = in_result[index]
        small_sum_ref[...] = small_result[...]


def finish_kernel(
    plan, names, late, tokens_ref, branch_ref, gate_ref, out_ref, small_ref, late_ref, norm_ref, *outs
):
    middle = branch_ref.shape[1]
    outs[0][:, :middle] = branch_ref[...]
    outs[0][:, middle:] = gate_ref[...]
    outs[1][...] = out_ref[...]
    outs[2][...] = tokens_ref[...]
    for name, target in zip(names, outs[3 : 3 + len(names)]):
        source, (first, count) = (late_ref, late[name]) if name in late else (small_ref, plan[name])
        if len(target.shape) == 1:
            target[...] = source[first, : target.shape[0]]
        else:
            target[...] = source[first : first + count, :]
    for index in range(2):
        outs[3 + len(names) + index][0, 0] = jnp.sum(norm_ref[index])


def shape(dims, kind=jnp.float32):
    return jax.ShapeDtypeStruct(dims, kind)


def compute_call(
    kernel, name, blocks, in_specs, out_specs, out_shape, scratch, flops, operands, collective_id=None
):
    return pl.pallas_call(
        kernel,
        grid=blocks if isinstance(blocks, tuple) else (blocks,),
        in_specs=in_specs,
        out_specs=out_specs,
        out_shape=out_shape,
        scratch_shapes=scratch,
        compiler_params=pltpu.CompilerParams(
            dimension_semantics=("arbitrary",) * (len(blocks) if isinstance(blocks, tuple) else 1),
            vmem_limit_bytes=62 * 1024 * 1024,
            collective_id=collective_id,
            has_side_effects=collective_id is not None,
        ),
        cost_estimate=pl.CostEstimate(flops=flops, bytes_accessed=40 << 20, transcendentals=0),
        name=name,
    )(*operands)


class Place:
    def __init__(self, dims, swapped=False):
        depth, tall, wide = dims
        self.dims = dims
        self.core = lax.axis_index("wide")
        self.me = lax.axis_index("narrow")
        self.across = lax.rem(self.me, wide)
        self.up = lax.rem(lax.div(self.me, wide), tall)
        self.deep = lax.div(self.me, wide * tall)
        side = 1 - self.core if swapped else self.core
        turn = side if tall == wide else 0
        self.second = (1 + turn * (wide - 1), self.across + turn * (self.up - self.across), wide)
        self.third = (wide - turn * (wide - 1), self.up + turn * (self.across - self.up), tall)
        self.spans = (depth, wide, tall)
        self.other = {"wide": 1 - self.core}

    def level(self, d):
        return lax.rem(self.deep + d, self.spans[0])

    def plane(self, e, f):
        return (
            lax.rem(self.second[1] + e, self.second[2]) * self.second[0]
            + lax.rem(self.third[1] + f, self.third[2]) * self.third[0]
        )

    def plane_behind(self, e, f):
        return self.plane((self.spans[1] - e) % self.spans[1], (self.spans[2] - f) % self.spans[2])

    def at(self, d, e, f):
        return {"narrow": self.level(d) * (self.dims[1] * self.dims[2]) + self.plane(e, f)}

    def greet(self, everyone=False):
        barrier = pltpu.get_barrier_semaphore()
        peers = [self.other]
        if everyone:
            number = self.spans[0] * self.spans[1] * self.spans[2]
            for hop in range(1, number):
                chip = lax.rem(self.me + hop, number)
                peers += [{"narrow": chip}, {"wide": 1 - self.core, "narrow": chip}]
        else:
            for axis, size in enumerate(self.spans):
                for hop in range(1, size):
                    move = [0, 0, 0]
                    move[axis] = hop
                    peers.append(self.at(*move))
        for peer in peers:
            pl.semaphore_signal(barrier, inc=1, device_id=peer, device_id_type=pl.DeviceIdType.MESH)
        pl.semaphore_wait(barrier, len(peers))


def by_rows(block):
    return block[0] % 32 == 0


def half_shape(block):
    if len(block) == 3:
        return tuple(block[1:])
    return (block[0] // 2, block[1]) if by_rows(block) else (block[0], block[1] // 2)


def half(view, block, side, lead=0):
    ahead = (slice(None),) * lead
    if len(block) == 3:
        return view.at[ahead + (side,)]
    if by_rows(block):
        return view.at[ahead + (pl.ds(pl.multiple_of(side * (block[0] // 2), 16), block[0] // 2),)]
    columns = pl.ds(pl.multiple_of(side * (block[1] // 2), lanes), block[1] // 2)
    return view.at[ahead + (slice(None), columns)]


def remote(source, target, send_sem, recv_sem, device):
    return pltpu.make_async_remote_copy(
        src_ref=source,
        dst_ref=target,
        send_sem=send_sem,
        recv_sem=recv_sem,
        device_id=device,
        device_id_type=pl.DeviceIdType.MESH,
    )


class Gather:
    def __init__(self, dims, own, whole, sems, blocks=None):
        self.dims, self.own, self.whole = dims, own, whole
        self.local_sem, self.send_sem, self.recv_sem = sems
        self.lined = blocks is not None
        self.blocks = blocks or [block.shape for block in own]

    @staticmethod
    def sems(count, dims):
        copies = dims[0] + 2 * dims[1] * dims[2]
        return [pltpu.SemaphoreType.DMA((count,))] + [pltpu.SemaphoreType.DMA((count, copies))] * 2

    def line(self, which, plane, side):
        return half(self.whole[which].at[:, plane], self.blocks[which], side, 1)

    def local(self, place, which):
        block = self.blocks[which]
        if self.lined:
            return pltpu.make_async_copy(
                self.own[which], self.line(which, place.plane(0, 0), place.core), self.local_sem.at[which]
            )
        return pltpu.make_async_copy(
            half(self.own[which], block, place.core),
            half(self.whole[which].at[place.deep, place.plane(0, 0)], block, place.core),
            self.local_sem.at[which],
        )

    def copy(self, which, source, target, index, device):
        return remote(
            source, target, self.send_sem.at[which, index], self.recv_sem.at[which, index], device
        )

    def rise(self, place, which, hop):
        block = self.blocks[which]
        return self.copy(
            which,
            half(self.own[which], block, place.core),
            half(self.whole[which].at[place.deep, place.plane(0, 0)], block, place.core),
            hop,
            place.at(hop, 0, 0),
        )

    def leg_index(self, e, f):
        return self.dims[0] + e * self.dims[1] + f

    def hand_index(self, e, f):
        return self.leg_index(e, f) + self.dims[1] * self.dims[2]

    def onward(self, place, which, e, f):
        line = self.line(which, place.plane_behind(e, f), place.core)
        source = self.own[which] if self.lined and e == 0 and f == 0 else line
        if f == 0:
            for hop in range(1, place.spans[2]):
                self.copy(which, source, line, self.leg_index(e, hop), place.at(0, 0, hop)).start()
        if f == 0 and e == 0:
            for hop in range(1, place.spans[1]):
                self.copy(which, source, line, self.leg_index(hop, 0), place.at(0, hop, 0)).start()
        self.copy(which, source, line, self.hand_index(e, f), place.other).start()

    def start(self, which):
        place = Place(self.dims)
        if self.lined:
            self.onward(place, which, 0, 0)
            self.local(place, which).start()
            return
        for hop in range(1, place.spans[0]):
            self.rise(place, which, hop).start()
        self.local(place, which).start()

    def leg(self, which, number):
        place = Place(self.dims)
        if number == 1:
            self.local(place, which).wait()
            for hop in range(1, place.spans[0]):
                self.rise(place, which, hop).wait_recv()
            self.onward(place, which, 0, 0)
            return
        for e in range(place.spans[1]):
            for f in range(place.spans[2]):
                if (number == 2 and f == 0 and e > 0) or (number == 3 and f > 0):
                    line = self.line(which, place.plane_behind(e, f), place.core)
                    self.copy(which, line, line, self.leg_index(e, f), place.other).wait_recv()
                    self.onward(place, which, e, f)

    def arrive(self, which):
        place, mirror = Place(self.dims), Place(self.dims, swapped=True)
        for e in range(place.spans[1]):
            for f in range(place.spans[2]):
                line = self.line(which, mirror.plane_behind(e, f), 1 - place.core)
                self.copy(which, line, line, self.hand_index(e, f), place.other).wait_recv()

    def drain(self, which):
        place = Place(self.dims)
        if self.lined:
            self.local(place, which).wait()
        else:
            for hop in range(1, place.spans[0]):
                self.rise(place, which, hop).wait_send()
        for e in range(place.spans[1]):
            for f in range(place.spans[2]):
                line = self.line(which, place.plane_behind(e, f), place.core)
                if e > 0 or f > 0:
                    self.copy(which, line, line, self.leg_index(e, f), place.other).wait_send()
                self.copy(which, line, line, self.hand_index(e, f), place.other).wait_send()


class Rise:
    def __init__(self, dims, own, lines, sems):
        self.dims, self.own, self.lines = dims, own, lines
        self.local_sem, self.send_sem, self.recv_sem = sems

    @staticmethod
    def sems(count, dims):
        return [pltpu.SemaphoreType.DMA((count,))] + [pltpu.SemaphoreType.DMA((count, dims[0]))] * 2

    def copies(self, place, which):
        source = half(self.own[which], self.own[which].shape, place.core)
        target = self.lines[which].at[place.deep]
        local = pltpu.make_async_copy(source, target, self.local_sem.at[which])
        return local, [
            remote(
                source, target, self.send_sem.at[which, hop], self.recv_sem.at[which, hop], place.at(hop, 0, 0)
            )
            for hop in range(1, place.spans[0])
        ]

    def start(self, which):
        local, sends = self.copies(Place(self.dims), which)
        for copy in [*sends, local]:
            copy.start()

    def finish(self, which):
        local, sends = self.copies(Place(self.dims), which)
        local.wait()
        for copy in sends:
            copy.wait_recv()
            copy.wait_send()


class Reduce:
    def __init__(self, dims, grads, rooms, sems, results, resident):
        self.dims, self.grads, self.resident = dims, grads, resident
        count = len(grads)
        self.mine, self.swapped, self.third, self.second, self.first = (
            rooms[index * count : (index + 1) * count] for index in range(5)
        )
        self.loaded = None if resident else rooms[5 * count :]
        self.load_sem, self.swap_send, self.swap_recv, self.send_sem, self.recv_sem = sems[:5]
        self.last_send, self.last_recv = sems[5:]
        self.results = results

    @staticmethod
    def rooms(dims, grads, resident):
        depth, tall, wide = dims
        leads = (
            (tall, wide, depth),
            (depth, tall * wide),
            (tall - 1, wide, depth),
            (wide - 1, depth),
            (depth - 1,),
        )
        if not resident:
            leads += ((depth, tall * wide),)
        return [
            pltpu.VMEM(lead + half_shape(grad.shape[2:]), grad.dtype) for lead in leads for grad in grads
        ]

    @staticmethod
    def sems(count, dims):
        return (
            [pltpu.SemaphoreType.DMA((count,))] * 3
            + [pltpu.SemaphoreType.DMA((count, dims[0] + dims[1] + dims[2]))] * 2
            + [pltpu.SemaphoreType.DMA((count,))] * 2
        )

    def block(self, which):
        return self.grads[which].shape[2:]

    def load(self, place, which):
        return pltpu.make_async_copy(
            half(self.grads[which], self.block(which), place.core, 2),
            self.loaded[which],
            self.load_sem.at[which],
        )

    def swap(self, place, which):
        return remote(
            half(self.grads[which], self.block(which), 1 - place.core, 2),
            self.swapped[which],
            self.swap_send.at[which],
            self.swap_recv.at[which],
            place.other,
        )

    def hop(self, which, source, target, index, device):
        return remote(
            source, target, self.send_sem.at[which, index], self.recv_sem.at[which, index], device
        )

    def third_hop(self, place, which, f):
        return self.hop(which, self.mine[which].at[f], self.third[which].at[f - 1], f, place.at(0, 0, f))

    def second_hop(self, place, which, e):
        return self.hop(
            which,
            self.mine[which].at[0, e],
            self.second[which].at[e - 1],
            self.dims[1] + e,
            place.at(0, e, 0),
        )

    def first_hop(self, place, which, d):
        return self.hop(
            which,
            self.mine[which].at[0, 0, place.level(d)],
            self.first[which].at[d - 1],
            self.dims[1] + self.dims[2] + d,
            place.at(d, 0, 0),
        )

    def start(self, which):
        place = Place(self.dims)
        self.swap(place, which).start()
        if not self.resident:
            self.load(place, which).start()

    def parts(self, place, which, e, f, z):
        plane = place.plane(e, f)
        if self.resident:
            found = [half(self.grads[which].at[z, plane], self.block(which), place.core)]
        else:
            found = [self.loaded[which].at[z, plane]]
        found.append(self.swapped[which].at[z, plane])
        if f == 0:
            found += [self.third[which].at[hop - 1, e, z] for hop in range(1, place.spans[2])]
        if f == 0 and e == 0:
            found += [self.second[which].at[hop - 1, z] for hop in range(1, place.spans[1])]
        return found

    def ready(self, place, which):
        if not self.resident:
            self.load(place, which).wait()
        self.swap(place, which).wait_recv()

    def added(self, parts, store, carry):
        rows = parts[0].shape[0]
        group = min(rows, 16)

        def some(index, carry):
            at_rows = pl.ds(pl.multiple_of(index * group, group), group)
            total = parts[0][at_rows, :].astype(jnp.float32)
            for part in parts[1:]:
                total = total + part[at_rows, :].astype(jnp.float32)
            return store(at_rows, total, carry)

        return lax.fori_loop(0, rows // group, some, carry)

    def sum_into(self, place, which, e, f, z):
        target = self.mine[which].at[f, e, z]

        def keep(at_rows, total, carry):
            target[at_rows, :] = total.astype(target.dtype)
            return carry

        self.added(self.parts(place, which, e, f, z), keep, 0)

    def leg(self, which, number):
        place = Place(self.dims)
        depth, span_e, span_f = place.spans
        if number == 1:
            self.ready(place, which)
            for f in range(span_f - 1, 0, -1):
                for e in range(span_e - 1, -1, -1):
                    for z in range(depth):
                        self.sum_into(place, which, e, f, z)
                self.third_hop(place, which, f).start()
        elif number == 2:
            for f in range(1, span_f):
                self.third_hop(place, which, f).wait_recv()
            for e in range(span_e - 1, 0, -1):
                for z in range(depth):
                    self.sum_into(place, which, e, 0, z)
                self.second_hop(place, which, e).start()
        else:
            if span_e == 1:
                for f in range(1, span_f):
                    self.third_hop(place, which, f).wait_recv()
            for e in range(1, span_e):
                self.second_hop(place, which, e).wait_recv()
            for d in range(1, depth):
                self.sum_into(place, which, 0, 0, place.level(d))
                self.first_hop(place, which, d).start()

    def result(self, which, side):
        return half(self.results[which], self.block(which), side)

    def last(self, place, which, side):
        share = self.result(which, side)
        return remote(share, share, self.last_send.at[which], self.last_recv.at[which], place.other)

    def finish(self, which, marks=None):
        place = Place(self.dims)
        parts = self.parts(place, which, 0, 0, place.deep)
        for d in range(1, place.spans[0]):
            self.first_hop(place, which, d).wait_recv()
            parts.append(self.first[which].at[d - 1])
        share = self.result(which, place.core)

        def store(at_rows, total, carry):
            share[at_rows, :] = total
            kept, plain = carry
            squared = total * total
            if marks is not None:
                marked = squared * marks[place.core, at_rows, :]
                plain = plain + folded_squares(marked)
                squared = squared - marked
            return (kept + folded_squares(squared), plain)

        squares = self.added(parts, store, (jnp.zeros((8, lanes), jnp.float32),) * 2)
        self.last(place, which, place.core).start()
        return squares

    def settle(self, which):
        place = Place(self.dims)
        last = self.last(place, which, 1 - place.core)
        last.wait_recv()
        last.wait_send()
        self.swap(place, which).wait_send()
        for f in range(1, place.spans[2]):
            self.third_hop(place, which, f).wait_send()
        for e in range(1, place.spans[1]):
            self.second_hop(place, which, e).wait_send()
        for d in range(1, place.spans[0]):
            self.first_hop(place, which, d).wait_send()


def folded_squares(values):
    total = None
    if values.shape[1] < lanes:
        first = lax.broadcasted_iota(jnp.int32, (values.shape[0], lanes), 1) == 0
        values = jnp.where(first, jnp.sum(values, axis=1, keepdims=True), 0.0)
    for row in range(0, values.shape[0], 8):
        for column in range(0, values.shape[1], lanes):
            piece = values[row : row + 8, column : column + lanes]
            total = piece if total is None else total + piece
    return total


def send_to_all(place, source, landing, send_sem, recv_sem):
    number = landing.shape[0]
    for hop in range(1, number):
        target = lax.rem(place.me + hop, number)
        remote(
            source(target), landing.at[place.me], send_sem.at[hop], recv_sem.at[hop], {"narrow": target}
        ).start()


def wait_for_all(place, own, landing, send_sem, recv_sem):
    number = landing.shape[0]
    landing[place.me] = own
    for hop in range(1, number):
        came = landing.at[lax.rem(place.me + number - hop, number)]
        copy = remote(came, came, send_sem.at[hop], recv_sem.at[hop], place.other)
        copy.wait_recv()
        copy.wait_send()


def send_to_everyone(place, source, landing, send_sem, recv_sem):
    number = landing.shape[1]
    target = landing.at[place.core, place.me]

    def send(hop, carry):
        chip = lax.rem(place.me + hop, number)
        for turn in range(2):
            device = {"wide": lax.rem(place.core + turn, 2), "narrow": chip}
            remote(source(chip), target, send_sem.at[turn, hop], recv_sem.at[turn, hop], device).start()
        return carry

    lax.fori_loop(1, number, send, 0)
    remote(source(place.me), target, send_sem.at[1, 0], recv_sem.at[1, 0], place.other).start()


def sum_of_everyone(place, own, landing, send_sem, recv_sem):
    number = landing.shape[1]
    landing[place.core, place.me] = own

    def wait(turn, hop):
        came = landing.at[lax.rem(place.core + turn, 2), lax.rem(place.me + number - hop, number)]
        copy = remote(came, came, send_sem.at[turn, hop], recv_sem.at[turn, hop], place.other)
        copy.wait_recv()
        copy.wait_send()

    def wait_both(hop, carry):
        wait(0, hop)
        wait(1, hop)
        return carry

    lax.fori_loop(1, number, wait_both, 0)
    wait(1, 0)

    def add(spot, total):
        return total + landing[0, spot] + landing[1, spot]

    return lax.fori_loop(1, number, add, landing[0, 0] + landing[1, 0])


def grid_of(mesh):
    number = mesh.shape["narrow"]
    places = [getattr(device, "coords", None) for device in mesh.devices[0]]
    if all(place is not None for place in places):
        sizes = [len({place[axis] for place in places}) for axis in (2, 1, 0)]
        if sizes[0] * sizes[1] * sizes[2] == number:
            return tuple(sizes)
    side = round((number / 2) ** (1 / 3))
    return (2 * side, side, side) if 2 * side**3 == number else (number, 1, 1)


def plan_of(select_rows, state_size, tap_count, step_rows):
    plan, first = {}, 0
    for name, tall in (
        ("select", select_rows),
        ("decay", state_size),
        ("taps", tap_count),
        ("shift", 1),
        ("bias", 1),
        ("skip", 1),
        ("gain", 1),
    ):
        plan[name] = (first, tall)
        first += tall
    plan["step"] = (lanes, step_rows)
    plan["rows"] = -(-(lanes + step_rows) // 32) * 32
    return plan


def per_device(
    dims,
    tokens,
    cotangent,
    loss_mask,
    seq_lengths,
    norm_gain,
    in_proj,
    conv_weight,
    conv_bias,
    select_proj,
    step_proj,
    step_bias,
    decay_log,
    skip_scale,
    out_proj,
):
    half = jnp.bfloat16
    piece = skip_scale.shape[0]
    gain_piece = norm_gain.shape[0]
    rank, size = step_proj.shape[0], decay_log.shape[0]
    plan = plan_of(select_proj.shape[0], size, conv_weight.shape[0], rank)
    smalls = {
        "select": select_proj,
        "decay": decay_log,
        "taps": conv_weight,
        "shift": conv_bias[None],
        "bias": step_bias[None],
        "skip": skip_scale[None],
        "gain": norm_gain[None],
        "step": step_proj,
    }
    depth, planes = dims[0], dims[1] * dims[2]
    number = depth * planes
    in_rows = in_proj.shape[0]
    rows, model = tokens.shape
    inner = piece * number
    width = 4 * lanes
    blocks = inner // width
    chunks = rows // chunk
    mask_row = loss_mask[None]

    whole = pl.BlockSpec(memory_space=pltpu.VMEM)
    tall = pl.BlockSpec((rows, width), lambda b: (0, b))
    deep = pl.BlockSpec((chunks, chunk, width), lambda b: (0, 0, b))
    lead = pl.BlockSpec((rows, size, width), lambda b: (0, 0, b))
    first_w = pl.BlockSpec((model, width), lambda b: (0, b))
    second_w = pl.BlockSpec((model, width), lambda b: (0, b + blocks))
    out_w = pl.BlockSpec((width, model), lambda b: (b, 0))

    def thin(height):
        return pl.BlockSpec((height, width), lambda b: (0, b))

    def fixed(*dims_of):
        return pl.BlockSpec(dims_of, lambda b: (0,) * len(dims_of))

    scalars = pl.BlockSpec(memory_space=pltpu.SMEM)
    offset_buf = pltpu.VMEM((rows + 8, lanes), jnp.int32)
    packed = thin(plan["rows"])

    pair = (chunks, 2 * chunk, lanes)
    pair = (chunks, 2 * chunk, lanes)
    anywhere = pl.BlockSpec(memory_space=pl.ANY)
    small_half = (2, plan["rows"] // 2, piece)
    in_piece = (in_rows, width)
    shares = 2
    in_share = (in_rows, inner // shares)
    out_share = (out_proj.shape[0], model // shares)
    lines = [shape((shares, depth) + half_shape(block), half) for block in (in_share, out_share)]
    (
        branch,
        signal,
        slope,
        projected,
        flipped,
        normed,
        grad_low,
        write_pair,
        read_pair,
        small,
        gain_value,
        in_blocks,
        gate_lines,
        out_lines,
    ) = compute_call(
        functools.partial(front_kernel, plan, dims, tuple(smalls)),
        "front",
        blocks,
        [scalars, whole, whole, whole] + [whole] * len(smalls) + [whole] * 2,
        [tall, tall, tall] + [whole] * 8 + [anywhere] * 3,
        [
            shape((rows, inner)),
            shape((rows, inner), half),
            shape((rows, inner)),
            shape((rows, lanes)),
            shape((model, rows), half),
            shape((rows, model), half),
            shape((rows, model), half),
            shape(pair, half),
            shape(pair, half),
            shape((plan["rows"], inner), half),
            shape((1, model)),
            shape((blocks, depth, planes) + in_piece, half),
            *lines,
        ],
        [
            offset_buf,
            pltpu.VMEM((plan["rows"], piece), jnp.float32),
            pltpu.VMEM(small_half, half),
            pltpu.VMEM((blocks,) + in_piece, half),
            pltpu.VMEM((shares,) + in_share, half),
            pltpu.VMEM((shares,) + out_share, half),
            pltpu.VMEM((depth, planes) + small_half, half),
            pltpu.VMEM((blocks, depth, planes) + in_piece, half),
            pltpu.SemaphoreType.DMA((blocks,)),
            pltpu.VMEM((8, piece), jnp.float32),
            pltpu.VMEM((number, 8, piece), jnp.float32),
            pltpu.SemaphoreType.DMA((number,)),
            pltpu.SemaphoreType.DMA((number,)),
        ]
        + Gather.sems(1 + blocks, dims)
        + Rise.sems(2 * shares, dims),
        4 * rows * model * inner,
        (seq_lengths, tokens, cotangent, mask_row, *smalls.values(), in_proj, out_proj),
        collective_id=0,
    )
    groups = 2
    part, pieces = rows // groups, chunks // groups
    row_block = pltpu.VMEM((pieces, chunk, width), jnp.float32)
    spread_block = pltpu.VMEM((rows, size, lanes), jnp.float32)
    fold_block = pltpu.VMEM((width // lanes, chunk * chunk, lanes), jnp.float32)

    def by_group(order, *dims_of):
        middle = (0,) * (len(dims_of) - 2)
        return pl.BlockSpec(dims_of, lambda b, g: (order(g),) + middle + (b,))

    def by_token(order, *dims_of):
        return pl.BlockSpec(dims_of, lambda b, g: (order(g),) + (0,) * (len(dims_of) - 1))

    def by_channel(height):
        return pl.BlockSpec((height, width), lambda b, g: (0, b))

    def onward(g):
        return g

    def backward(g):
        return groups - 1 - g

    states, step, core, begins, gate_blocks, out_blocks = compute_call(
        functools.partial(forward_kernel, plan, dims),
        "forward",
        (blocks, groups),
        [
            scalars,
            by_token(onward, part, lanes),
            by_channel(plan["rows"]),
            by_group(onward, part, width),
            whole,
            whole,
            anywhere,
            anywhere,
        ],
        [
            by_group(onward, part, size, width),
            by_group(onward, pieces, chunk, width),
            by_group(onward, pieces, chunk, width),
            by_group(onward, 1, size, width),
            anywhere,
            anywhere,
        ],
        [
            shape((rows, size, inner)),
            shape((chunks, chunk, inner)),
            shape((chunks, chunk, inner)),
            shape((groups, size, inner)),
            shape((shares, depth, planes) + in_share, half),
            shape((shares, depth, planes) + out_share, half),
        ],
        [
            offset_buf,
            pltpu.VMEM((part, width), jnp.float32),
            row_block,
            row_block,
            spread_block,
            spread_block,
            fold_block,
            fold_block,
            pltpu.VMEM((size, width), jnp.float32),
        ]
        + Gather.sems(2 * shares, dims),
        15 * rows * inner * size,
        (seq_lengths, projected, small, signal, write_pair, read_pair, gate_lines, out_lines),
        collective_id=2,
    )
    split = in_share[1] // width
    weights = pl.BlockSpec((None, number, in_rows, width), lambda b: (b // split, 0, 0, b % split))
    per_block = width // out_share[0]
    out_pieces = pl.BlockSpec((shares, per_block) + out_share, lambda b: (0, b, 0, 0))
    branch_whole = in_blocks.reshape(blocks, number, *in_piece)
    gate_whole = gate_blocks.reshape(shares, number, *in_share)
    out_whole = out_blocks.reshape(shares, number, *out_share)
    core_grad, gate_grad, grad_skip, grad_outw, grad_in_gate, output = compute_call(
        functools.partial(middle_kernel, plan),
        "middle",
        blocks,
        [deep, packed, tall, weights, whole, out_pieces, whole, whole, whole],
        [
            deep,
            tall,
            thin(1),
            pl.BlockSpec((shares, width, out_share[1]), lambda b: (0, b, 0)),
            pl.BlockSpec((None, model, width), lambda b: (b // split, 0, b % split)),
            fixed(rows, model),
        ],
        [
            shape((chunks, chunk, inner)),
            shape((rows, inner), half),
            shape((1, inner)),
            shape((shares, inner, out_share[1]), half),
            shape((shares, model, in_share[1]), half),
            shape((rows, model), half),
        ],
        [
            pltpu.VMEM((rows, width), jnp.float32),
            pltpu.VMEM((rows, width), jnp.float32),
            pltpu.VMEM((rows, width), half),
            pltpu.VMEM((width, model), half),
            pltpu.VMEM((rows, model), jnp.float32),
        ],
        8 * rows * model * inner,
        (core, small, signal, gate_whole, grad_low, out_whole, flipped, normed, tokens),
    )
    early_grads = [
        grad_outw.reshape((shares, depth, planes) + out_share),
        grad_in_gate.reshape((shares, depth, planes) + in_share),
    ]
    early_sums = [shape(out_proj.shape), shape((in_rows, inner))]
    early_pieces = [shape((depth, planes) + block, half) for block in (in_share, out_share)] * shares
    (
        signal_grad,
        grad_stepw,
        grad_bias,
        grad_decaylog,
        flat,
        out_sum,
        in_gate_sum,
        early_squares,
    ) = compute_call(
        functools.partial(backward_kernel, plan, dims),
        "backward",
        (blocks, groups),
        [
            scalars,
            by_token(backward, part, lanes),
            by_channel(plan["rows"]),
            by_group(backward, part, width),
            whole,
            whole,
            by_group(backward, pieces, chunk, width),
            by_group(backward, pieces, chunk, width),
            by_group(backward, part, size, width),
            by_group(backward, 1, size, width),
            anywhere,
            anywhere,
        ],
        [
            by_group(backward, part, width),
            by_channel(rank),
            by_channel(1),
            by_channel(size),
            whole,
        ]
        + [whole] * 3,
        [
            shape((rows, inner)),
            shape((rank, inner)),
            shape((1, inner)),
            shape((size, inner)),
            shape((rows, lanes), half),
            *early_sums,
            shape((8, lanes)),
        ],
        [
            offset_buf,
            row_block,
            row_block,
            spread_block,
            spread_block,
            fold_block,
            fold_block,
            fold_block,
            fold_block,
            row_block,
            row_block,
            pltpu.VMEM((part, width), half),
            pltpu.VMEM((size, width), jnp.float32),
            pltpu.VMEM((chunks, chunk, lanes), jnp.float32),
            spread_block,
            spread_block,
        ]
        + [pltpu.VMEM((shares,) + block, jnp.float32) for block in (in_share, out_share)]
        + Reduce.rooms(dims, early_pieces, False)
        + Reduce.sems(2 * shares, dims),
        40 * rows * inner * size,
        (
            seq_lengths,
            projected,
            small,
            signal,
            write_pair,
            read_pair,
            step,
            core_grad,
            states,
            begins,
            *early_grads,
        ),
        collective_id=3,
    )

    plain_rows = np.zeros((plan["rows"], piece), np.float32)
    for name in ("bias", "decay", "skip"):
        first, count = plan[name]
        plain_rows[first : first + count] = 1.0
    late_grads = [shape((depth, planes) + small_half, half)]
    late_grads += [shape((depth, planes, in_rows, width), half)] * blocks
    taps_n = conv_weight.shape[0]
    late = {"taps": (0, taps_n), "shift": (taps_n, 1), "gain": (taps_n + 1, 1)}
    late_block = (8, piece)

    early_tall = pl.BlockSpec((rows, width), lambda b: (0, jnp.minimum(b, blocks - 1)))
    late_tall = pl.BlockSpec((rows, width), lambda b: (0, jnp.maximum(b - blocks, 0)))
    tokens_grad, in_branch_sum, small_sum, late_sum, norms = compute_call(
        functools.partial(back_kernel, plan, dims),
        "back",
        2 * blocks,
        [scalars, whole, whole, whole]
        + [pl.BlockSpec((plan["rows"], width), lambda b: (0, jnp.minimum(b, blocks - 1))), whole]
        + [early_tall, whole, early_tall, early_tall, late_tall, whole]
        + [
            pl.BlockSpec((None, number, in_rows, width), lambda b: (jnp.maximum(b - blocks, 0), 0, 0, 0)),
            pl.BlockSpec(
                (None, number, in_rows, width),
                lambda b: (jnp.maximum(b - blocks, 0) // split, 0, 0, jnp.maximum(b - blocks, 0) % split),
            ),
        ]
        + [whole] * 6,
        [whole] * 5,
        [
            shape((rows, model), half),
            shape((in_rows, inner)),
            shape(small_half),
            shape(late_block),
            shape((2, 8, lanes)),
        ],
        [
            offset_buf,
            pltpu.VMEM((rows + 8, width), jnp.float32),
            pltpu.VMEM((blocks, rows, width), half),
            pltpu.VMEM((rows, model), jnp.float32),
            pltpu.VMEM((blocks,) + late_grads[1].shape, half),
            pltpu.VMEM(late_grads[0].shape, late_grads[0].dtype),
            pltpu.VMEM((number,) + late_block, jnp.float32),
            pltpu.VMEM((2, number) + late_block, jnp.float32),
            pltpu.VMEM((2, 8, lanes), jnp.float32),
            pltpu.VMEM((2, number, 2, 8, lanes), jnp.float32),
            pltpu.VMEM((blocks, in_rows, width), jnp.float32),
            pltpu.VMEM(small_half, jnp.float32),
            pltpu.SemaphoreType.DMA((2, 2, number)),
            pltpu.SemaphoreType.DMA((2, 2, number)),
        ]
        + Reduce.rooms(dims, late_grads, True)
        + Reduce.sems(blocks + 1, dims),
        8 * rows * model * inner,
        (
            seq_lengths,
            tokens,
            grad_low,
            gain_value,
            small,
            flat,
            branch,
            signal,
            slope,
            signal_grad,
            gate_grad,
            flipped,
            branch_whole,
            gate_whole,
            grad_stepw,
            grad_bias,
            grad_decaylog,
            grad_skip,
            jnp.asarray(plain_rows.reshape(small_half)),
            early_squares,
        ),
        collective_id=1,
    )

    names = ("gain", "taps", "shift", "select", "step", "bias", "decay", "skip")
    own = (norm_gain, conv_weight, conv_bias, select_proj, step_proj, step_bias, decay_log, skip_scale)
    in_grad, out_grad, grad_tokens, gain_grad, *small_grads, decay_sq, plain_sq = pl.pallas_call(
        functools.partial(finish_kernel, plan, names, late),
        in_specs=[whole] * 7,
        out_specs=[whole] * (3 + len(names)) + [scalars] * 2,
        out_shape=[shape(in_proj.shape), shape(out_proj.shape), shape(tokens.shape, half)]
        + [shape(array.shape) for array in own]
        + [shape((1, 1))] * 2,
        name="finish",
    )(
        tokens_grad,
        in_branch_sum,
        in_gate_sum,
        out_sum,
        small_sum.reshape(plan["rows"], piece),
        late_sum,
        norms,
    )
    return (
        output,
        grad_tokens,
        gain_grad,
        in_grad,
        *small_grads,
        out_grad,
        decay_sq[0, 0],
        plain_sq[0, 0],
    )


def solution(mesh):
    placed = (
        P(("wide", "narrow"), None),
        P(("wide", "narrow"), None),
        P(("wide", "narrow")),
        P(("wide", "narrow"), None),
        P("narrow"),
        P("narrow", None),
        P(None, "narrow"),
        P("narrow"),
        P(None, "narrow"),
        P(None, "narrow"),
        P("narrow"),
        P(None, "narrow"),
        P("narrow"),
        P("narrow", None),
    )
    return jax.shard_map(
        functools.partial(per_device, grid_of(mesh)),
        mesh=mesh,
        in_specs=placed,
        out_specs=(
            P(("wide", "narrow"), None),
            P(("wide", "narrow"), None),
            P("narrow"),
            P("narrow", None),
            P(None, "narrow"),
            P("narrow"),
            P(None, "narrow"),
            P(None, "narrow"),
            P("narrow"),
            P(None, "narrow"),
            P("narrow"),
            P("narrow", None),
            P(),
            P(),
        ),
        check_vma=False,
    )
```

```python
import functools
import math

import jax
import jax.numpy as jnp
import numpy as np
from jax import lax
from jax.experimental import pallas as pl
from jax.experimental.pallas import tpu as pltpu
from jax.sharding import PartitionSpec as P

epsilon = 1e-05
chunk = 8
lanes = 128
log2e = math.log2(math.e)
ln2 = math.log(2.0)
far = 1e30
tiny = 1e-30


def contract(left, right, left_dim, right_dim):
    return lax.dot_general(
        left, right, (((left_dim,), (right_dim,)), ((), ())), preferred_element_type=jnp.float32
    )


def row_loop(rows, group, body, initial):
    def some(index, carry):
        return body(index, pl.ds(pl.multiple_of(index * group, group), group), carry)

    return lax.fori_loop(0, rows // group, some, initial)


def cut(tile):
    return pl.ds(tile * lanes, lanes)


def sigmoid(values):
    return 0.5 * jnp.tanh(0.5 * values) + 0.5


def softplus(values):
    small = jnp.exp(-jnp.abs(values))
    series = small * (1.0 - small * (0.5 - small * (1.0 / 3.0 - 0.25 * small)))
    return jnp.maximum(values, 0.0) + jnp.where(small < 0.03, series, jnp.log(1.0 + small))


def slope_of(step):
    return 1.0 - jnp.exp(-step)


def fill_offsets(lengths_ref, offset_buf, rows):
    place = lax.broadcasted_iota(jnp.int32, offset_buf.shape, 0)
    start = jnp.zeros(offset_buf.shape, jnp.int32)
    ahead = jnp.int32(0)
    for index in range(lengths_ref.shape[1] - 1):
        ahead = ahead + lengths_ref[0, index]
        start = jnp.where(place >= ahead, ahead, start)
    offset_buf[...] = jnp.where(place < rows, place - start, 0)


def small_rows(small_ref, first, count):
    base = first // 16 * 16
    tall = -(-(first + count - base) // 16) * 16
    return small_ref[base : base + tall, :].astype(jnp.float32)[first - base : first - base + count]


def eight(values):
    total = values[:8]
    for row in range(8, values.shape[0], 8):
        total = total + values[row : row + 8]
    return total


def conv_rows(index, at, group, tile, branch_ref, offset_buf, taps, shift):
    count = taps.shape[0]
    here = slice(tile * lanes, (tile + 1) * lanes)
    current = branch_ref[at, cut(tile)]
    before = branch_ref[pl.ds(pl.multiple_of(jnp.maximum(index * group - 8, 0), 8), 8), cut(tile)]
    both = jnp.concatenate([before, current], axis=0)
    offsets = offset_buf[at, :]
    summed = shift[:, here] + taps[count - 1 : count, here] * current
    for tap in range(count - 1):
        lag = count - 1 - tap
        read = jnp.where(offsets >= lag, pltpu.roll(both, lag, 0)[8:], 0.0)
        summed = summed + taps[tap : tap + 1, here] * read
    return summed


def rows_of(blocks):
    return as_matrix(blocks[...][None])


def as_matrix(blocks):
    columns = blocks.shape[3]
    if blocks.shape[2] % 16:
        return blocks.astype(jnp.float32).reshape(-1, columns).astype(blocks.dtype)
    return blocks.reshape(-1, columns)


def front_kernel(
    plan,
    dims,
    names,
    lengths_ref,
    tokens_ref,
    cotangent_ref,
    mask_ref,
    *refs,
):
    smalls, in_ref, out_ref, refs = refs[: len(names)], refs[len(names)], refs[len(names) + 1], refs[len(names) + 2 :]
    branch_ref, signal_ref, slope_ref, projected_ref, flipped_ref, normed_ref, low_ref = refs[:7]
    write_pair, read_pair, small_out, gain_ref, whole_ref, gate_lines, out_lines = refs[7:14]
    offset_buf, pack_buf, own_small, own_in, own_gate, own_out, land_small, land_in, store_sem = refs[14:23]
    own_gain, land_gain, gain_send, gain_recv = refs[23:27]
    rows = tokens_ref.shape[0]
    width = branch_ref.shape[1]
    block = pl.program_id(0)
    last = whole_ref.shape[0]
    shares = own_out.shape[0]
    gather = Gather(
        dims,
        [own_small] + [own_in.at[index] for index in range(last)],
        [land_small] + [land_in.at[index] for index in range(last)],
        refs[27:30],
    )
    rise = Rise(
        dims,
        [own.at[index] for index in range(shares) for own in (own_gate, own_out)],
        [lines.at[index] for index in range(shares) for lines in (gate_lines, out_lines)],
        refs[30:],
    )
    tall = pack_buf.shape[0] // 2

    def stored(index):
        return pltpu.make_async_copy(land_in.at[index], whole_ref.at[index], store_sem.at[index])

    def move_on(plan_of_moves):
        for moment, legs in plan_of_moves:

            @pl.when(block == moment)
            def _(legs=legs):
                for which, number in legs:
                    gather.leg(which, number)

    @pl.when(block == 0)
    def _():
        pack_buf[...] = jnp.zeros_like(pack_buf)
        for name, ref in zip(names, smalls):
            first, height = plan[name]
            pack_buf[first : first + height, : ref.shape[1]] = ref[...]
        own_gain[...] = jnp.zeros_like(own_gain)
        own_gain[0:1, : gain_ref.shape[1] // land_gain.shape[0]] = smalls[names.index("gain")][...]
        for side in range(2):
            own_small[side] = pack_buf[side * tall : (side + 1) * tall, :].astype(own_small.dtype)
        for index in range(last):
            own_in[index] = in_ref[:, index * width : (index + 1) * width].astype(own_in.dtype)
        place = Place(dims)
        place.greet(everyone=True)
        send_to_all(place, lambda target: own_gain, land_gain, gain_send, gain_recv)
        for index in (1, 0) + tuple(range(2, last + 1)):
            gather.start(index)
        first = last * width
        for index in range(shares):
            each = own_gate.shape[2]
            own_gate[index] = in_ref[:, first + index * each : first + (index + 1) * each].astype(own_gate.dtype)
            each = own_out.shape[2]
            own_out[index] = out_ref[:, index * each : (index + 1) * each].astype(own_out.dtype)
        fill_offsets(lengths_ref, offset_buf, rows)
        gather.leg(1, 1)
        gather.leg(0, 1)
        wait_for_all(place, own_gain[...], land_gain, gain_send, gain_recv)
        each = gain_ref.shape[1] // land_gain.shape[0]
        for owner in range(land_gain.shape[0]):
            gain_ref[:, owner * each : (owner + 1) * each] = (
                land_gain[owner, 0:1, :each].astype(jnp.bfloat16).astype(jnp.float32)
            )

        def norm(index, at, carry):
            residual = tokens_ref[at, :].astype(jnp.float32)
            scale = lax.rsqrt(jnp.mean(residual * residual, axis=1, keepdims=True) + epsilon)
            normed_ref[at, :] = (residual * scale * gain_ref[...]).astype(normed_ref.dtype)
            return carry

        row_loop(rows, 16, norm, 0)
        gather.leg(1, 2)
        gather.leg(0, 2)
        gather.leg(2, 1)
        rise.start(0)
        gather.leg(1, 3)
        gather.leg(0, 3)
        gather.leg(2, 2)
        projected_ref[...] = jnp.zeros_like(projected_ref)

    for index in range(last):

        @pl.when(block == index)
        def _(index=index):
            gather.arrive(index + 1)
            stored(index).start()

    branch_w = as_matrix(land_in[block])
    branch_ref[...] = jnp.dot(normed_ref[...], branch_w, preferred_element_type=jnp.float32)
    move_on(((0, ((3, 1), (2, 3))), (1, ((4, 2), (3, 3))), (2, ((4, 3),))))
    pl.when(block == 0)(functools.partial(rise.start, 1))

    @pl.when(block == 0)
    def _():
        gather.arrive(0)
        share = land_small.shape[4]
        for z in range(land_small.shape[0]):
            for plane in range(land_small.shape[1]):
                owner = z * land_small.shape[1] + plane
                for side in range(2):
                    small_out[side * tall : (side + 1) * tall, owner * share : (owner + 1) * share] = land_small[
                        z, plane, side
                    ]

    small_ref = small_out.at[:, pl.ds(pl.multiple_of(block * width, width), width)]
    taps = small_rows(small_ref, *plan["taps"])
    shift = small_rows(small_ref, *plan["shift"])

    def some(index, at, carry):
        for tile in range(width // lanes):
            summed = conv_rows(index, at, 32, tile, branch_ref, offset_buf, taps, shift)
            sigma = sigmoid(summed)
            active = summed * sigma
            signal_ref[at, cut(tile)] = active.astype(signal_ref.dtype)
            slope_ref[at, cut(tile)] = sigma + active * (1.0 - sigma)
        return carry

    row_loop(rows, 32, some, 0)
    move_on(((0, ((4, 1), (3, 2))),))

    @pl.when(block == 0)
    def _():
        for index in range(2, 2 * shares):
            rise.start(index)

    projected_ref[...] += contract(signal_ref[...], small_ref[:lanes, :], 1, 1)

    @pl.when(block == pl.num_programs(0) - 1)
    def _():
        high, low = high_low(projected_ref[...])
        own = own_tokens(rows)
        rank = plan["step"][1]
        size = plan["decay"][1]
        entry = lax.broadcasted_iota(jnp.int32, (lanes, lanes), 0)
        lane = lax.rem(lax.broadcasted_iota(jnp.int32, (lanes, lanes), 1), size)
        for first, pair in ((rank, write_pair), (rank + size, read_pair)):
            spread = (entry == lane + first).astype(jnp.bfloat16)
            parts = [
                (jnp.dot(part.astype(jnp.bfloat16), spread, preferred_element_type=jnp.float32) * own).reshape(
                    rows // chunk, chunk, lanes
                )
                for part in (high, low)
            ]
            pair[...] = jnp.concatenate(parts, axis=1).astype(pair.dtype)
        flipped_ref[...] = normed_ref[...].T
        down = lax.broadcasted_iota(jnp.int32, (rows, rows), 0)
        along = lax.broadcasted_iota(jnp.int32, (rows, rows), 1)
        diagonal = jnp.where(down == along, mask_ref[...].astype(jnp.float32), 0.0).astype(low_ref.dtype)
        low_ref[...] = jnp.dot(
            diagonal, cotangent_ref[...], preferred_element_type=jnp.float32
        ).astype(low_ref.dtype)
        for index in range(last + 1):
            gather.drain(index)
        for index in range(2 * shares):
            rise.finish(index)
        for index in range(last):
            stored(index).wait()


def high_low(values):
    high = values.astype(jnp.bfloat16).astype(jnp.float32)
    return high, values - high


def own_tokens(rows):
    token = lax.rem(lax.broadcasted_iota(jnp.int32, (rows, lanes), 0), chunk)
    return (token == lax.div(lax.broadcasted_iota(jnp.int32, (rows, lanes), 1), lanes // chunk)).astype(
        jnp.float32
    )


def spread_all(pairs, target):
    some = 8

    def spread(index, carry):
        rows = jnp.concatenate([pairs[index * some + number] for number in range(some)], axis=1)
        wide = contract(rows, jnp.ones((rows.shape[0], lanes), rows.dtype), 0, 0)
        target[pl.ds(index * some * chunk, some * chunk)] = wide.reshape(some * chunk, -1, lanes)
        return carry

    lax.fori_loop(0, pairs.shape[0] // some, spread, 0)


def joined(first, second, hop):
    low = lax.bitwise_and(lax.broadcasted_iota(jnp.int32, first.shape, 0), hop) == 0
    return jnp.where(low, first, second) + pltpu.roll(jnp.where(low, second, first), hop, 0)


def folded(buffer, tile):
    parts = [buffer[tile, pl.ds(row * chunk, chunk), :] for row in range(chunk)]
    hop = 1
    while len(parts) > 1:
        parts = [joined(parts[index], parts[index + 1], hop) for index in range(0, len(parts), 2)]
        hop *= 2
    return parts[0]


def forward_kernel(
    plan,
    dims,
    lengths_ref,
    projected_ref,
    small_ref,
    signal_ref,
    write_pair,
    read_pair,
    gate_lines,
    out_lines,
    states_ref,
    step_ref,
    core_ref,
    begin_ref,
    gate_whole,
    out_whole,
    offset_buf,
    pre_buf,
    decay_step,
    flows,
    write_wide,
    read_wide,
    fold_a,
    fold_b,
    held_buf,
    *sems,
):
    rows, width = pre_buf.shape
    size = plan["decay"][1]
    half_size = size // 2
    tiles = width // lanes
    chunks = rows // chunk
    rank = plan["step"][1]
    group = pl.program_id(1)
    groups = pl.num_programs(1)
    moment = pl.program_id(0) * groups + group
    moments = pl.num_programs(0) * groups
    shares = gate_whole.shape[0]
    count = 2 * shares
    gather = Gather(
        dims,
        [lines.at[index] for index in range(shares) for lines in (gate_lines, out_lines)],
        [whole.at[index] for index in range(shares) for whole in (gate_whole, out_whole)],
        sems,
        [whole.shape[3:] for _ in range(shares) for whole in (gate_whole, out_whole)],
    )

    @pl.when(moment == 0)
    def _():
        Place(dims).greet()
        for which in range(count):
            gather.start(which)
        fill_offsets(lengths_ref, offset_buf, offset_buf.shape[0] - 8)
        spread_all(write_pair, write_wide)
        spread_all(read_pair, read_wide)

    @pl.when(group == 0)
    def _():
        held_buf[...] = jnp.zeros_like(held_buf)

    begin_ref[0] = held_buf[...]
    pre_buf[...] = jnp.dot(
        projected_ref[:, :rank].astype(small_ref.dtype),
        small_ref[pl.ds(plan["step"][0], rank), :],
        preferred_element_type=jnp.float32,
    )
    bias = small_rows(small_ref, *plan["bias"])

    def before(index, at, carry):
        spot = pl.ds(pl.multiple_of(index * 4, 4), 4)
        inside = offset_buf[pl.ds(pl.multiple_of(group * rows + index * 32, 32), 32), :] > 0
        for tile in range(tiles):
            step = softplus(pre_buf[at, cut(tile)] + bias[:, tile * lanes : (tile + 1) * lanes])
            step_ref[spot, :, cut(tile)] = step.reshape(4, chunk, lanes)
            decay_step[spot, :, cut(tile)] = jnp.where(inside, step, far).reshape(4, chunk, lanes)
            flow = step * signal_ref[at, cut(tile)].astype(jnp.float32)
            flows[spot, :, cut(tile)] = flow.reshape(4, chunk, lanes)
        return carry

    row_loop(rows, 4 * chunk, before, 0)
    rates = -jnp.exp(small_rows(small_ref, *plan["decay"])) * log2e
    rates = [rates[:, tile * lanes : (tile + 1) * lanes] for tile in range(tiles)]

    def advance(index, held, fold_buf):
        held = list(held)
        for place in range(chunk):
            now = index * chunk + place
            write_now = write_wide[group * rows + now]
            read_now = read_wide[group * rows + now]
            for tile in range(tiles):
                decay = jnp.exp2(rates[tile] * decay_step[index, pl.ds(place, 1), cut(tile)])
                fresh = decay * held[tile] + write_now * flows[index, pl.ds(place, 1), cut(tile)]
                held[tile] = fresh
                states_ref[now, :, cut(tile)] = fresh
                product = read_now * fresh
                fold_buf[tile, pl.ds(place * chunk, chunk), :] = product[:half_size] + product[half_size:]
        return tuple(held)

    def forward(pair, held):
        index = 2 * pair
        held = advance(index, held, fold_a)
        for tile in range(tiles):
            core_ref[index, :, cut(tile)] = folded(fold_a, tile)
        held = advance(index + 1, held, fold_b)
        for tile in range(tiles):
            core_ref[index + 1, :, cut(tile)] = folded(fold_b, tile)
        return held

    held = tuple(held_buf[:, cut(tile)] for tile in range(tiles))
    schedule = {}
    for which in range(count):
        for number in (2, 3):
            point = ((3, 5, 7, 9), (10, 12, 13, 15))[number - 2][which]
            schedule.setdefault(point, []).append((which, number))

    def move_on(legs):
        for which, number in legs:
            gather.leg(which, number)

    for half_loop in range(2):
        for point, legs in sorted(schedule.items()):
            if point < 16 and point % 2 == half_loop:
                pl.when(moment == point // 2)(functools.partial(move_on, legs))
        held = lax.fori_loop(half_loop * chunks // 4, (half_loop + 1) * chunks // 4, forward, held)
    for tile in range(tiles):
        held_buf[:, cut(tile)] = held[tile]

    @pl.when(moment == moments - 1)
    def _():
        for which in range(count):
            gather.arrive(which)
        for which in range(count):
            gather.drain(which)


def middle_kernel(
    plan,
    core_ref,
    small_ref,
    signal_ref,
    gate_w,
    low_ref,
    out_w,
    flipped_ref,
    normed_ref,
    tokens_ref,
    core_grad_ref,
    gate_grad_ref,
    skip_grad_ref,
    out_grad_ref,
    in_grad_ref,
    output_ref,
    pre_buf,
    gate_buf,
    gated_buf,
    out_buf,
    total,
):
    rows, width = pre_buf.shape
    tiles = width // lanes
    block = pl.program_id(0)
    each = out_w.shape[3]
    for index in range(out_w.shape[0]):
        out_buf[:, index * each : (index + 1) * each] = as_matrix(out_w[index][None])
    gate_buf[...] = jnp.dot(normed_ref[...], rows_of(gate_w), preferred_element_type=jnp.float32)
    pre_buf[...] = contract(low_ref[...], out_buf[...], 1, 1)
    skip = small_rows(small_ref, *plan["skip"])

    def after(index, at, carry):
        spot = pl.ds(pl.multiple_of(index * 4, 4), 4)
        sums = []
        for tile in range(tiles):
            signal = signal_ref[at, cut(tile)].astype(jnp.float32)
            core = core_ref[spot, :, cut(tile)].reshape(4 * chunk, lanes)
            core = core + skip[:, tile * lanes : (tile + 1) * lanes] * signal
            gate = gate_buf[at, cut(tile)]
            sigma = sigmoid(gate)
            active = gate * sigma
            gated_buf[at, cut(tile)] = (core * active).astype(gated_buf.dtype)
            grad_gated = pre_buf[at, cut(tile)]
            grad_core = grad_gated * active
            core_grad_ref[spot, :, cut(tile)] = grad_core.reshape(4, chunk, lanes)
            slope = sigma + active * (1.0 - sigma)
            gate_grad_ref[at, cut(tile)] = (grad_gated * core * slope).astype(gate_grad_ref.dtype)
            sums.append(carry[tile] + eight(grad_core * signal))
        return tuple(sums)

    zero_rows = jnp.zeros((8, lanes), jnp.float32)
    skips = row_loop(rows, 4 * chunk, after, (zero_rows,) * tiles)
    for tile in range(tiles):
        skip_grad_ref[:, cut(tile)] = jnp.sum(skips[tile], axis=0, keepdims=True)
    out_grad = contract(gated_buf[...], low_ref[...], 0, 0).astype(out_grad_ref.dtype)
    for index in range(out_w.shape[0]):
        out_grad_ref[index] = out_grad[:, index * each : (index + 1) * each]
    in_grad_ref[...] = jnp.dot(
        flipped_ref[...], gate_grad_ref[...], preferred_element_type=jnp.float32
    ).astype(in_grad_ref.dtype)
    piece = jnp.dot(gated_buf[...], out_buf[...], preferred_element_type=jnp.float32)

    @pl.when(block == 0)
    def _():
        total[...] = piece

    @pl.when(block > 0)
    def _():
        total[...] += piece

    @pl.when(block == pl.num_programs(0) - 1)
    def _():
        output_ref[...] = (tokens_ref[...].astype(jnp.float32) + total[...]).astype(output_ref.dtype)


def backward_kernel(
    plan,
    dims,
    lengths_ref,
    projected_ref,
    small_ref,
    signal_ref,
    write_pair,
    read_pair,
    step_ref,
    core_grad_ref,
    states_ref,
    begin_ref,
    out_grad_ref,
    in_grad_ref,
    signal_grad_ref,
    step_w_grad_ref,
    bias_grad_ref,
    decay_grad_ref,
    flat_ref,
    out_sum_ref,
    in_sum_ref,
    square_ref,
    offset_buf,
    decay_step,
    flows,
    write_wide,
    read_wide,
    first_a,
    first_b,
    second_a,
    second_b,
    through_buf,
    scaled_buf,
    low_buf,
    incoming_buf,
    rank_buf,
    write_buf,
    read_buf,
    *parts,
):
    rows, width = low_buf.shape
    rank = plan["step"][1]
    size = plan["decay"][1]
    half_size = size // 2
    tiles = width // lanes
    chunks = rows // chunk
    block = pl.program_id(0)
    turn = pl.program_id(1)
    groups = pl.num_programs(1)
    group = groups - 1 - turn
    moment = block * groups + turn
    moments = pl.num_programs(0) * groups
    gate_result, out_result, parts = parts[0], parts[1], parts[2:]
    pieces = gate_result.shape[0]
    count = 2 * pieces

    both = ((in_grad_ref, gate_result), (out_grad_ref, out_result))
    reduce = Reduce(
        dims,
        [ref.at[index] for index in range(pieces) for ref, _ in both],
        parts[: 6 * count],
        parts[6 * count :],
        [result.at[index] for index in range(pieces) for _, result in both],
        False,
    )

    @pl.when(moment == 0)
    def _():
        Place(dims).greet()
        for which in range(count):
            reduce.start(which)
        fill_offsets(lengths_ref, offset_buf, offset_buf.shape[0] - 8)
        spread_all(write_pair, write_wide)
        spread_all(read_pair, read_wide)
        write_buf[...] = jnp.zeros_like(write_buf)
        read_buf[...] = jnp.zeros_like(read_buf)
        rank_buf[...] = jnp.zeros_like(rank_buf)

    @pl.when(turn == 0)
    def _():
        incoming_buf[...] = jnp.zeros_like(incoming_buf)
        decay_grad_ref[...] = jnp.zeros_like(decay_grad_ref)
        bias_grad_ref[...] = jnp.zeros_like(bias_grad_ref)
        step_w_grad_ref[...] = jnp.zeros_like(step_w_grad_ref)

    def before(index, at, carry):
        spot = pl.ds(pl.multiple_of(index * 4, 4), 4)
        offsets = offset_buf[pl.ds(pl.multiple_of(group * rows + index * 32, 32), 32), :]
        inside = (offsets > 0).reshape(4, chunk, lanes)
        for tile in range(tiles):
            step = step_ref[spot, :, cut(tile)]
            decay_step[spot, :, cut(tile)] = jnp.where(inside, step, far)
            signal = signal_ref[at, cut(tile)].astype(jnp.float32).reshape(4, chunk, lanes)
            flows[spot, :, cut(tile)] = step * signal
        return carry

    row_loop(rows, 4 * chunk, before, 0)
    rates = -jnp.exp(small_rows(small_ref, *plan["decay"])) * log2e
    rates = [rates[:, tile * lanes : (tile + 1) * lanes] for tile in range(tiles)]

    def retreat(index, carried, first_buf, second_buf):
        incoming, decay_sums, current = (list(tiles_of) for tiles_of in carried)
        for place in range(chunk - 1, -1, -1):
            now = index * chunk + place
            token = group * rows + now
            write_now = write_wide[token]
            read_now = read_wide[token]
            read_sum = None
            write_sum = None
            for tile in range(tiles):
                grad_now = core_grad_ref[index, pl.ds(place, 1), cut(tile)]
                if place > 0:
                    earlier = states_ref[now - 1, :, cut(tile)]
                else:
                    earlier = jnp.where(
                        index > 0, states_ref[jnp.maximum(now - 1, 0), :, cut(tile)], begin_ref[0, :, cut(tile)]
                    )
                grad_state = incoming[tile] + read_now * grad_now
                through_read = current[tile] * grad_now
                current[tile] = earlier
                through_write = grad_state * flows[index, pl.ds(place, 1), cut(tile)]
                read_sum = through_read if read_sum is None else read_sum + through_read
                write_sum = through_write if write_sum is None else write_sum + through_write
                passed = grad_state * write_now
                first_buf[tile, pl.ds(place * chunk, chunk), :] = passed[:half_size] + passed[half_size:]
                exponent = rates[tile] * decay_step[index, pl.ds(place, 1), cut(tile)]
                leaving = jnp.exp2(exponent) * grad_state
                incoming[tile] = leaving
                weighted = (leaving * earlier) * exponent
                second_buf[tile, pl.ds(place * chunk, chunk), :] = weighted[:half_size] + weighted[half_size:]
                decay_sums[tile] = decay_sums[tile] + weighted
            read_buf[token] += read_sum
            write_buf[token] += write_sum
        return (tuple(incoming), tuple(decay_sums), tuple(current))

    def backward(pair, carried):
        index = chunks - 1 - 2 * pair
        for here, first_buf, second_buf in ((index, first_a, second_a), (index - 1, first_b, second_b)):
            carried = retreat(here, carried, first_buf, second_buf)
            for tile in range(tiles):
                through_buf[here, :, cut(tile)] = folded(first_buf, tile)
                scaled_buf[here, :, cut(tile)] = folded(second_buf, tile)
        return carried

    incoming = tuple(incoming_buf[:, cut(tile)] for tile in range(tiles))
    nothing = (jnp.zeros((size, lanes), jnp.float32),) * tiles
    current = tuple(states_ref[rows - 1, :, cut(tile)] for tile in range(tiles))
    schedule = {}
    for which in range(count):
        for number in (1, 2, 3):
            point = ((2, 4, 7, 9), (5, 7, 10, 12), (7, 9, 12, 14))[number - 1][which]
            schedule.setdefault(point, []).append((which, number))

    def move_on(legs):
        for which, number in legs:
            reduce.leg(which, number)

    carried = (incoming, nothing, current)
    for half_loop in range(2):
        for point, legs in sorted(schedule.items()):
            if point % 2 == half_loop:
                pl.when(moment == point // 2)(functools.partial(move_on, legs))
        carried = lax.fori_loop(half_loop * chunks // 4, (half_loop + 1) * chunks // 4, backward, carried)
    incoming, decay_sums, _ = carried
    for tile in range(tiles):
        incoming_buf[:, cut(tile)] = incoming[tile]
        decay_grad_ref[:, cut(tile)] += decay_sums[tile] * ln2
    skip = small_rows(small_ref, *plan["skip"])

    def after(index, at, carry):
        spot = pl.ds(pl.multiple_of(index * 4, 4), 4)
        sums = []
        for tile in range(tiles):
            signal = signal_ref[at, cut(tile)].astype(jnp.float32)
            step = step_ref[spot, :, cut(tile)].reshape(4 * chunk, lanes)
            through = through_buf[spot, :, cut(tile)].reshape(4 * chunk, lanes)
            scaled = scaled_buf[spot, :, cut(tile)].reshape(4 * chunk, lanes)
            core_grad = core_grad_ref[spot, :, cut(tile)].reshape(4 * chunk, lanes)
            grad_pre = (through * signal + ln2 * scaled / jnp.maximum(step, tiny)) * slope_of(step)
            low_buf[at, cut(tile)] = grad_pre.astype(low_buf.dtype)
            signal_grad_ref[at, cut(tile)] = (
                through * step + skip[:, tile * lanes : (tile + 1) * lanes] * core_grad
            )
            sums.append(carry[tile] + eight(grad_pre))
        return tuple(sums)

    zero_rows = jnp.zeros((8, lanes), jnp.float32)
    sums = row_loop(rows, 4 * chunk, after, (zero_rows,) * tiles)
    for tile in range(tiles):
        bias_grad_ref[:, cut(tile)] += jnp.sum(sums[tile], axis=0, keepdims=True)
    step_w_grad_ref[...] += contract(
        projected_ref[:, :rank].astype(low_buf.dtype), low_buf[...], 0, 0
    )
    step_w = small_ref[pl.ds(plan["step"][0], rank), :]
    step_w = jnp.concatenate([step_w, jnp.zeros((lanes - rank, width), step_w.dtype)], axis=0)
    rank_buf[pl.ds(group * chunks, chunks)] += contract(low_buf[...], step_w, 1, 1).reshape(
        chunks, chunk, lanes
    )

    @pl.when(moment == moments - 1)
    def _():
        squares = jnp.zeros((8, lanes), jnp.float32)
        for which in range(count):
            squares = squares + reduce.finish(which)[0]
        square_ref[...] = squares
        some = 8
        entry = lax.rem(lax.broadcasted_iota(jnp.int32, (some * chunk * size, lanes), 0), size)
        target = lax.broadcasted_iota(jnp.int32, (some * chunk * size, lanes), 1)
        ones = jnp.ones((lanes, lanes), jnp.bfloat16)

        def lay(index, carry):
            lot = pl.ds(index * some * chunk, some * chunk)
            for number, buffer in enumerate((write_buf, read_buf)):
                high, low = high_low(buffer[lot].reshape(some * chunk * size, lanes))
                summed = jnp.dot(high.astype(jnp.bfloat16), ones, preferred_element_type=jnp.float32)
                summed += jnp.dot(low.astype(jnp.bfloat16), ones, preferred_element_type=jnp.float32)
                summed = jnp.where(target == entry + rank + number * size, summed, 0.0)
                summed = jnp.sum(summed.reshape(some * chunk, size, lanes), axis=1)
                rank_buf[pl.ds(index * some, some)] += summed.reshape(some, chunk, lanes)
            return carry

        lax.fori_loop(0, rank_buf.shape[0] // some, lay, 0)
        flat_ref[...] = rank_buf[...].reshape(flat_ref.shape).astype(flat_ref.dtype)
        for which in range(count):
            reduce.settle(which)
        for index in range(pieces):
            for target, result in ((out_sum_ref, out_result), (in_sum_ref, gate_result)):
                each = result.shape[2]
                target[:, index * each : (index + 1) * each] = result[index]


def back_kernel(
    plan,
    dims,
    lengths_ref,
    tokens_ref,
    low_ref,
    gain_ref,
    small_ref,
    flat_ref,
    branch_ref,
    signal_ref,
    slope_ref,
    signal_grad_ref,
    gate_grad_ref,
    flipped_ref,
    branch_w,
    gate_w,
    step_w_grad_ref,
    bias_grad_ref,
    decay_grad_ref,
    skip_grad_ref,
    plain_ref,
    earlier_ref,
    tokens_grad_ref,
    in_sum_ref,
    small_sum_ref,
    late_sum_ref,
    norm_ref,
    offset_buf,
    conv_buf,
    mixed_buf,
    total,
    in_stage,
    small_stage,
    late_stage,
    late_land,
    norm_own,
    norm_land,
    in_result,
    small_result,
    direct_send,
    direct_recv,
    *parts,
):
    rows = tokens_ref.shape[0]
    width = branch_ref.shape[1]
    tiles = width // lanes
    block = pl.program_id(0)
    last = in_stage.shape[0]
    count = last + 1
    reduce = Reduce(
        dims,
        [small_stage] + [in_stage.at[index] for index in range(last)],
        parts[: 5 * count],
        parts[5 * count :],
        [small_result] + [in_result.at[index] for index in range(last)],
        True,
    )
    share = small_stage.shape[4]
    half_rows = small_stage.shape[3]
    planes = small_stage.shape[1]
    owners = small_stage.shape[0] * planes

    @pl.when(block == 0)
    def _():
        Place(dims).greet(everyone=True)
        fill_offsets(lengths_ref, offset_buf, rows)

    def move_on(plan_of_moves):
        for moment, legs in plan_of_moves:

            @pl.when(block == moment)
            def _(legs=legs):
                for which, number in legs:
                    reduce.leg(which, number)

    taps = small_rows(small_ref, *plan["taps"])
    taps_count = taps.shape[0]
    zero_rows = jnp.zeros((8, lanes), jnp.float32)

    @pl.when(block < last)
    def _():
        conv_buf[pl.ds(0, rows), :] = signal_grad_ref[...] + jnp.dot(
            flat_ref[...], small_ref[:lanes, :], preferred_element_type=jnp.float32
        )
        conv_buf[pl.ds(rows, 8), :] = jnp.zeros((8, width), jnp.float32)

        def through_conv(index, at, carry):
            sums = []
            for tile in range(tiles):
                grad_conv = conv_buf[at, cut(tile)] * slope_ref[at, cut(tile)]
                conv_buf[at, cut(tile)] = grad_conv
                sums.append(carry[tile] + eight(grad_conv))
            return tuple(sums)

        shift_sums = row_loop(rows, 32, through_conv, (zero_rows,) * tiles)
        def to_branch(index, at, carry):
            longer = pl.ds(pl.multiple_of(index * 32, 32), 40)
            offsets = offset_buf[longer, :]
            result = []
            for tile in range(tiles):
                here = slice(tile * lanes, (tile + 1) * lanes)
                grads = conv_buf[longer, cut(tile)]
                branch = branch_ref[at, cut(tile)]
                summed = taps[taps_count - 1 : taps_count, here] * grads[:32]
                sums = [None] * taps_count
                sums[taps_count - 1] = carry[tile][taps_count - 1] + eight(branch * grads[:32])
                for tap in range(taps_count - 1):
                    lag = taps_count - 1 - tap
                    moved = pltpu.roll(jnp.where(offsets >= lag, grads, 0.0), 40 - lag, 0)[:32]
                    summed = summed + taps[tap : tap + 1, here] * moved
                    sums[tap] = carry[tile][tap] + eight(branch * moved)
                mixed_buf[block, at, cut(tile)] = summed.astype(mixed_buf.dtype)
                result.append(tuple(sums))
            return tuple(result)

        sums = row_loop(rows, 32, to_branch, ((zero_rows,) * taps_count,) * tiles)
        in_grad = jnp.dot(flipped_ref[...], mixed_buf[block], preferred_element_type=jnp.float32)
        in_stage[block] = in_grad.reshape(in_stage.shape[1:]).astype(in_stage.dtype)
        for index in range(last):

            @pl.when(block == index)
            def _(index=index):
                reduce.start(index + 1)

        late = [
            jnp.concatenate(
                [jnp.sum(sums[tile][tap], axis=0, keepdims=True) for tap in range(taps_count)]
                + [jnp.sum(shift_sums[tile], axis=0, keepdims=True)]
                + [jnp.zeros((8 - taps_count - 1, lanes), jnp.float32)],
                axis=0,
            )
            for tile in range(tiles)
        ]
        late = jnp.concatenate(late, axis=1)
        for piece in range(width // share):
            late_stage[block * (width // share) + piece] = late[:, piece * share : (piece + 1) * share]
        move_on(
            (
                (1, ((1, 1), (0, 1))),
                (2, ((2, 1), (1, 2), (0, 2))),
                (3, ((3, 1), (2, 2), (1, 3), (0, 3))),
            )
        )

        @pl.when(block == 0)
        def _():
            select_grad = contract(flat_ref[...], signal_ref[...], 0, 0)
            step_first, step_tall = plan["step"]
            filler = jnp.zeros((2 * half_rows - step_first - step_tall, select_grad.shape[1]), jnp.float32)
            pieces = {
                "decay": decay_grad_ref[...],
                "bias": bias_grad_ref[...],
                "skip": skip_grad_ref[...],
                "step": step_w_grad_ref[...],
            }
            first = plan["select"][1]
            rows_now = [select_grad[:first]]
            for name in ("decay", "taps", "shift", "bias", "skip", "gain"):
                tall = plan[name][1]
                rows_now.append(
                    pieces[name] if name in pieces else jnp.zeros((tall, select_grad.shape[1]), jnp.float32)
                )
                first += tall
            rows_now.append(jnp.zeros((step_first - first, select_grad.shape[1]), jnp.float32))
            rows_now.append(pieces["step"])
            if filler.shape[0]:
                rows_now.append(filler)
            everything = jnp.concatenate(rows_now, axis=0)
            for owner in range(owners):
                for side in range(2):
                    small_stage[owner // planes, owner % planes, side] = everything[
                        side * half_rows : (side + 1) * half_rows, owner * share : (owner + 1) * share
                    ].astype(small_stage.dtype)
            reduce.start(0)

    @pl.when(block >= last)
    def _():
        grad_normed_piece = contract(mixed_buf[block - last], rows_of(branch_w), 1, 1)
        grad_normed_piece += contract(gate_grad_ref[...], rows_of(gate_w), 1, 1)

        @pl.when(block == last)
        def _():
            total[...] = grad_normed_piece

        @pl.when(block > last)
        def _():
            total[...] += grad_normed_piece

        move_on(((4, ((3, 2),)), (5, ((4, 1), (2, 3))), (6, ((3, 3),)), (7, ((4, 2),))))

    @pl.when(block == pl.num_programs(0) - 1)
    def _():
        def scaled_tokens(at):
            residual = tokens_ref[at, :].astype(jnp.float32)
            return residual, lax.rsqrt(jnp.mean(residual * residual, axis=1, keepdims=True) + epsilon)

        def gain_rows(index, at, carry):
            residual, scale = scaled_tokens(at)
            return carry + eight(total[at, :] * residual * scale)

        gains = row_loop(rows, 16, gain_rows, jnp.zeros((8, total.shape[1]), jnp.float32))
        gains = jnp.sum(gains, axis=0, keepdims=True)
        place = Place(dims)
        each = gains.shape[1] // owners
        for owner in range(owners):
            late_stage[owner, taps_count + 1 : taps_count + 2, :each] = gains[
                :, owner * each : (owner + 1) * each
            ]
        late_sems = direct_send.at[0], direct_recv.at[0]
        norm_sems = direct_send.at[1], direct_recv.at[1]
        send_to_everyone(place, lambda chip: late_stage.at[chip], late_land, *late_sems)
        reduce.leg(4, 3)

        def token_rows(index, at, carry):
            residual, scale = scaled_tokens(at)
            weighted = total[at, :] * gain_ref[...]
            inner = jnp.mean(weighted * residual, axis=1, keepdims=True)
            grad_y = low_ref[at, :].astype(jnp.float32)
            result = grad_y + (scale * weighted - residual * (scale * scale * scale) * inner)
            tokens_grad_ref[at, :] = result.astype(tokens_grad_ref.dtype)
            return carry

        row_loop(rows, 16, token_rows, 0)
        more, plain = reduce.finish(0, plain_ref)
        kept = earlier_ref[...] + more
        for index in range(1, count - 1):
            kept = kept + reduce.finish(index)[0]
        late_sum = sum_of_everyone(place, late_stage[place.me], late_land, *late_sems)
        late_sum_ref[...] = late_sum
        kept = kept + folded_squares(late_sum * late_sum) * (1 - place.core).astype(jnp.float32)
        kept = kept + reduce.finish(count - 1)[0]
        norm_own[...] = jnp.stack([kept, plain])
        send_to_everyone(place, lambda chip: norm_own, norm_land, *norm_sems)
        norm_ref[...] = sum_of_everyone(place, norm_own[...], norm_land, *norm_sems)
        for index in range(count):
            reduce.settle(index)
        for index in range(last):
            in_sum_ref[:, index * width : (index + 1) * width] = in_result[index]
        small_sum_ref[...] = small_result[...]


def finish_kernel(
    plan, names, late, tokens_ref, branch_ref, gate_ref, out_ref, small_ref, late_ref, norm_ref, *outs
):
    middle = branch_ref.shape[1]
    outs[0][:, :middle] = branch_ref[...]
    outs[0][:, middle:] = gate_ref[...]
    outs[1][...] = out_ref[...]
    outs[2][...] = tokens_ref[...]
    for name, target in zip(names, outs[3 : 3 + len(names)]):
        source, (first, count) = (late_ref, late[name]) if name in late else (small_ref, plan[name])
        if len(target.shape) == 1:
            target[...] = source[first, : target.shape[0]]
        else:
            target[...] = source[first : first + count, :]
    for index in range(2):
        outs[3 + len(names) + index][0, 0] = jnp.sum(norm_ref[index])


def shape(dims, kind=jnp.float32):
    return jax.ShapeDtypeStruct(dims, kind)


def compute_call(
    kernel, name, blocks, in_specs, out_specs, out_shape, scratch, flops, operands, collective_id=None
):
    return pl.pallas_call(
        kernel,
        grid=blocks if isinstance(blocks, tuple) else (blocks,),
        in_specs=in_specs,
        out_specs=out_specs,
        out_shape=out_shape,
        scratch_shapes=scratch,
        compiler_params=pltpu.CompilerParams(
            dimension_semantics=("arbitrary",) * (len(blocks) if isinstance(blocks, tuple) else 1),
            vmem_limit_bytes=62 * 1024 * 1024,
            collective_id=collective_id,
            has_side_effects=collective_id is not None,
        ),
        cost_estimate=pl.CostEstimate(flops=flops, bytes_accessed=40 << 20, transcendentals=0),
        name=name,
    )(*operands)


class Place:
    def __init__(self, dims, swapped=False):
        depth, tall, wide = dims
        self.dims = dims
        self.core = lax.axis_index("wide")
        self.me = lax.axis_index("narrow")
        self.across = lax.rem(self.me, wide)
        self.up = lax.rem(lax.div(self.me, wide), tall)
        self.deep = lax.div(self.me, wide * tall)
        side = 1 - self.core if swapped else self.core
        turn = side if tall == wide else 0
        self.second = (1 + turn * (wide - 1), self.across + turn * (self.up - self.across), wide)
        self.third = (wide - turn * (wide - 1), self.up + turn * (self.across - self.up), tall)
        self.spans = (depth, wide, tall)
        self.other = {"wide": 1 - self.core}

    def level(self, d):
        return lax.rem(self.deep + d, self.spans[0])

    def plane(self, e, f):
        return (
            lax.rem(self.second[1] + e, self.second[2]) * self.second[0]
            + lax.rem(self.third[1] + f, self.third[2]) * self.third[0]
        )

    def plane_behind(self, e, f):
        return self.plane((self.spans[1] - e) % self.spans[1], (self.spans[2] - f) % self.spans[2])

    def at(self, d, e, f):
        return {"narrow": self.level(d) * (self.dims[1] * self.dims[2]) + self.plane(e, f)}

    def greet(self, everyone=False):
        barrier = pltpu.get_barrier_semaphore()
        peers = [self.other]
        if everyone:
            number = self.spans[0] * self.spans[1] * self.spans[2]
            for hop in range(1, number):
                chip = lax.rem(self.me + hop, number)
                peers += [{"narrow": chip}, {"wide": 1 - self.core, "narrow": chip}]
        else:
            for axis, size in enumerate(self.spans):
                for hop in range(1, size):
                    move = [0, 0, 0]
                    move[axis] = hop
                    peers.append(self.at(*move))
        for peer in peers:
            pl.semaphore_signal(barrier, inc=1, device_id=peer, device_id_type=pl.DeviceIdType.MESH)
        pl.semaphore_wait(barrier, len(peers))


def by_rows(block):
    return block[0] % 32 == 0


def half_shape(block):
    if len(block) == 3:
        return tuple(block[1:])
    return (block[0] // 2, block[1]) if by_rows(block) else (block[0], block[1] // 2)


def half(view, block, side, lead=0):
    ahead = (slice(None),) * lead
    if len(block) == 3:
        return view.at[ahead + (side,)]
    if by_rows(block):
        return view.at[ahead + (pl.ds(pl.multiple_of(side * (block[0] // 2), 16), block[0] // 2),)]
    columns = pl.ds(pl.multiple_of(side * (block[1] // 2), lanes), block[1] // 2)
    return view.at[ahead + (slice(None), columns)]


def remote(source, target, send_sem, recv_sem, device):
    return pltpu.make_async_remote_copy(
        src_ref=source,
        dst_ref=target,
        send_sem=send_sem,
        recv_sem=recv_sem,
        device_id=device,
        device_id_type=pl.DeviceIdType.MESH,
    )


class Gather:
    def __init__(self, dims, own, whole, sems, blocks=None):
        self.dims, self.own, self.whole = dims, own, whole
        self.local_sem, self.send_sem, self.recv_sem = sems
        self.lined = blocks is not None
        self.blocks = blocks or [block.shape for block in own]

    @staticmethod
    def sems(count, dims):
        copies = dims[0] + 2 * dims[1] * dims[2]
        return [pltpu.SemaphoreType.DMA((count,))] + [pltpu.SemaphoreType.DMA((count, copies))] * 2

    def line(self, which, plane, side):
        return half(self.whole[which].at[:, plane], self.blocks[which], side, 1)

    def local(self, place, which):
        block = self.blocks[which]
        if self.lined:
            return pltpu.make_async_copy(
                self.own[which], self.line(which, place.plane(0, 0), place.core), self.local_sem.at[which]
            )
        return pltpu.make_async_copy(
            half(self.own[which], block, place.core),
            half(self.whole[which].at[place.deep, place.plane(0, 0)], block, place.core),
            self.local_sem.at[which],
        )

    def copy(self, which, source, target, index, device):
        return remote(
            source, target, self.send_sem.at[which, index], self.recv_sem.at[which, index], device
        )

    def rise(self, place, which, hop):
        block = self.blocks[which]
        return self.copy(
            which,
            half(self.own[which], block, place.core),
            half(self.whole[which].at[place.deep, place.plane(0, 0)], block, place.core),
            hop,
            place.at(hop, 0, 0),
        )

    def leg_index(self, e, f):
        return self.dims[0] + e * self.dims[1] + f

    def hand_index(self, e, f):
        return self.leg_index(e, f) + self.dims[1] * self.dims[2]

    def onward(self, place, which, e, f):
        line = self.line(which, place.plane_behind(e, f), place.core)
        source = self.own[which] if self.lined and e == 0 and f == 0 else line
        if f == 0:
            for hop in range(1, place.spans[2]):
                self.copy(which, source, line, self.leg_index(e, hop), place.at(0, 0, hop)).start()
        if f == 0 and e == 0:
            for hop in range(1, place.spans[1]):
                self.copy(which, source, line, self.leg_index(hop, 0), place.at(0, hop, 0)).start()
        self.copy(which, source, line, self.hand_index(e, f), place.other).start()

    def start(self, which):
        place = Place(self.dims)
        if self.lined:
            self.onward(place, which, 0, 0)
            self.local(place, which).start()
            return
        for hop in range(1, place.spans[0]):
            self.rise(place, which, hop).start()
        self.local(place, which).start()

    def leg(self, which, number):
        place = Place(self.dims)
        if number == 1:
            self.local(place, which).wait()
            for hop in range(1, place.spans[0]):
                self.rise(place, which, hop).wait_recv()
            self.onward(place, which, 0, 0)
            return
        for e in range(place.spans[1]):
            for f in range(place.spans[2]):
                if (number == 2 and f == 0 and e > 0) or (number == 3 and f > 0):
                    line = self.line(which, place.plane_behind(e, f), place.core)
                    self.copy(which, line, line, self.leg_index(e, f), place.other).wait_recv()
                    self.onward(place, which, e, f)

    def arrive(self, which):
        place, mirror = Place(self.dims), Place(self.dims, swapped=True)
        for e in range(place.spans[1]):
            for f in range(place.spans[2]):
                line = self.line(which, mirror.plane_behind(e, f), 1 - place.core)
                self.copy(which, line, line, self.hand_index(e, f), place.other).wait_recv()

    def drain(self, which):
        place = Place(self.dims)
        if self.lined:
            self.local(place, which).wait()
        else:
            for hop in range(1, place.spans[0]):
                self.rise(place, which, hop).wait_send()
        for e in range(place.spans[1]):
            for f in range(place.spans[2]):
                line = self.line(which, place.plane_behind(e, f), place.core)
                if e > 0 or f > 0:
                    self.copy(which, line, line, self.leg_index(e, f), place.other).wait_send()
                self.copy(which, line, line, self.hand_index(e, f), place.other).wait_send()


class Rise:
    def __init__(self, dims, own, lines, sems):
        self.dims, self.own, self.lines = dims, own, lines
        self.local_sem, self.send_sem, self.recv_sem = sems

    @staticmethod
    def sems(count, dims):
        return [pltpu.SemaphoreType.DMA((count,))] + [pltpu.SemaphoreType.DMA((count, dims[0]))] * 2

    def copies(self, place, which):
        source = half(self.own[which], self.own[which].shape, place.core)
        target = self.lines[which].at[place.deep]
        local = pltpu.make_async_copy(source, target, self.local_sem.at[which])
        return local, [
            remote(
                source, target, self.send_sem.at[which, hop], self.recv_sem.at[which, hop], place.at(hop, 0, 0)
            )
            for hop in range(1, place.spans[0])
        ]

    def start(self, which):
        local, sends = self.copies(Place(self.dims), which)
        for copy in [*sends, local]:
            copy.start()

    def finish(self, which):
        local, sends = self.copies(Place(self.dims), which)
        local.wait()
        for copy in sends:
            copy.wait_recv()
            copy.wait_send()


class Reduce:
    def __init__(self, dims, grads, rooms, sems, results, resident):
        self.dims, self.grads, self.resident = dims, grads, resident
        count = len(grads)
        self.mine, self.swapped, self.third, self.second, self.first = (
            rooms[index * count : (index + 1) * count] for index in range(5)
        )
        self.loaded = None if resident else rooms[5 * count :]
        self.load_sem, self.swap_send, self.swap_recv, self.send_sem, self.recv_sem = sems[:5]
        self.last_send, self.last_recv = sems[5:]
        self.results = results

    @staticmethod
    def rooms(dims, grads, resident):
        depth, tall, wide = dims
        leads = (
            (tall, wide, depth),
            (depth, tall * wide),
            (tall - 1, wide, depth),
            (wide - 1, depth),
            (depth - 1,),
        )
        if not resident:
            leads += ((depth, tall * wide),)
        return [
            pltpu.VMEM(lead + half_shape(grad.shape[2:]), grad.dtype) for lead in leads for grad in grads
        ]

    @staticmethod
    def sems(count, dims):
        return (
            [pltpu.SemaphoreType.DMA((count,))] * 3
            + [pltpu.SemaphoreType.DMA((count, dims[0] + dims[1] + dims[2]))] * 2
            + [pltpu.SemaphoreType.DMA((count,))] * 2
        )

    def block(self, which):
        return self.grads[which].shape[2:]

    def load(self, place, which):
        return pltpu.make_async_copy(
            half(self.grads[which], self.block(which), place.core, 2),
            self.loaded[which],
            self.load_sem.at[which],
        )

    def swap(self, place, which):
        return remote(
            half(self.grads[which], self.block(which), 1 - place.core, 2),
            self.swapped[which],
            self.swap_send.at[which],
            self.swap_recv.at[which],
            place.other,
        )

    def hop(self, which, source, target, index, device):
        return remote(
            source, target, self.send_sem.at[which, index], self.recv_sem.at[which, index], device
        )

    def third_hop(self, place, which, f):
        return self.hop(which, self.mine[which].at[f], self.third[which].at[f - 1], f, place.at(0, 0, f))

    def second_hop(self, place, which, e):
        return self.hop(
            which,
            self.mine[which].at[0, e],
            self.second[which].at[e - 1],
            self.dims[1] + e,
            place.at(0, e, 0),
        )

    def first_hop(self, place, which, d):
        return self.hop(
            which,
            self.mine[which].at[0, 0, place.level(d)],
            self.first[which].at[d - 1],
            self.dims[1] + self.dims[2] + d,
            place.at(d, 0, 0),
        )

    def start(self, which):
        place = Place(self.dims)
        self.swap(place, which).start()
        if not self.resident:
            self.load(place, which).start()

    def parts(self, place, which, e, f, z):
        plane = place.plane(e, f)
        if self.resident:
            found = [half(self.grads[which].at[z, plane], self.block(which), place.core)]
        else:
            found = [self.loaded[which].at[z, plane]]
        found.append(self.swapped[which].at[z, plane])
        if f == 0:
            found += [self.third[which].at[hop - 1, e, z] for hop in range(1, place.spans[2])]
        if f == 0 and e == 0:
            found += [self.second[which].at[hop - 1, z] for hop in range(1, place.spans[1])]
        return found

    def ready(self, place, which):
        if not self.resident:
            self.load(place, which).wait()
        self.swap(place, which).wait_recv()

    def added(self, parts, store, carry):
        rows = parts[0].shape[0]
        group = min(rows, 16)

        def some(index, carry):
            at_rows = pl.ds(pl.multiple_of(index * group, group), group)
            total = parts[0][at_rows, :].astype(jnp.float32)
            for part in parts[1:]:
                total = total + part[at_rows, :].astype(jnp.float32)
            return store(at_rows, total, carry)

        return lax.fori_loop(0, rows // group, some, carry)

    def sum_into(self, place, which, e, f, z):
        target = self.mine[which].at[f, e, z]

        def keep(at_rows, total, carry):
            target[at_rows, :] = total.astype(target.dtype)
            return carry

        self.added(self.parts(place, which, e, f, z), keep, 0)

    def leg(self, which, number):
        place = Place(self.dims)
        depth, span_e, span_f = place.spans
        if number == 1:
            self.ready(place, which)
            for f in range(span_f - 1, 0, -1):
                for e in range(span_e - 1, -1, -1):
                    for z in range(depth):
                        self.sum_into(place, which, e, f, z)
                self.third_hop(place, which, f).start()
        elif number == 2:
            for f in range(1, span_f):
                self.third_hop(place, which, f).wait_recv()
            for e in range(span_e - 1, 0, -1):
                for z in range(depth):
                    self.sum_into(place, which, e, 0, z)
                self.second_hop(place, which, e).start()
        else:
            if span_e == 1:
                for f in range(1, span_f):
                    self.third_hop(place, which, f).wait_recv()
            for e in range(1, span_e):
                self.second_hop(place, which, e).wait_recv()
            for d in range(1, depth):
                self.sum_into(place, which, 0, 0, place.level(d))
                self.first_hop(place, which, d).start()

    def result(self, which, side):
        return half(self.results[which], self.block(which), side)

    def last(self, place, which, side):
        share = self.result(which, side)
        return remote(share, share, self.last_send.at[which], self.last_recv.at[which], place.other)

    def finish(self, which, marks=None):
        place = Place(self.dims)
        parts = self.parts(place, which, 0, 0, place.deep)
        for d in range(1, place.spans[0]):
            self.first_hop(place, which, d).wait_recv()
            parts.append(self.first[which].at[d - 1])
        share = self.result(which, place.core)

        def store(at_rows, total, carry):
            share[at_rows, :] = total
            kept, plain = carry
            squared = total * total
            if marks is not None:
                marked = squared * marks[place.core, at_rows, :]
                plain = plain + folded_squares(marked)
                squared = squared - marked
            return (kept + folded_squares(squared), plain)

        squares = self.added(parts, store, (jnp.zeros((8, lanes), jnp.float32),) * 2)
        self.last(place, which, place.core).start()
        return squares

    def settle(self, which):
        place = Place(self.dims)
        last = self.last(place, which, 1 - place.core)
        last.wait_recv()
        last.wait_send()
        self.swap(place, which).wait_send()
        for f in range(1, place.spans[2]):
            self.third_hop(place, which, f).wait_send()
        for e in range(1, place.spans[1]):
            self.second_hop(place, which, e).wait_send()
        for d in range(1, place.spans[0]):
            self.first_hop(place, which, d).wait_send()


def folded_squares(values):
    total = None
    if values.shape[1] < lanes:
        first = lax.broadcasted_iota(jnp.int32, (values.shape[0], lanes), 1) == 0
        values = jnp.where(first, jnp.sum(values, axis=1, keepdims=True), 0.0)
    for row in range(0, values.shape[0], 8):
        for column in range(0, values.shape[1], lanes):
            piece = values[row : row + 8, column : column + lanes]
            total = piece if total is None else total + piece
    return total


def send_to_all(place, source, landing, send_sem, recv_sem):
    number = landing.shape[0]
    for hop in range(1, number):
        target = lax.rem(place.me + hop, number)
        remote(
            source(target), landing.at[place.me], send_sem.at[hop], recv_sem.at[hop], {"narrow": target}
        ).start()


def wait_for_all(place, own, landing, send_sem, recv_sem):
    number = landing.shape[0]
    landing[place.me] = own
    for hop in range(1, number):
        came = landing.at[lax.rem(place.me + number - hop, number)]
        copy = remote(came, came, send_sem.at[hop], recv_sem.at[hop], place.other)
        copy.wait_recv()
        copy.wait_send()


def send_to_everyone(place, source, landing, send_sem, recv_sem):
    number = landing.shape[1]
    target = landing.at[place.core, place.me]

    def send(hop, carry):
        chip = lax.rem(place.me + hop, number)
        for turn in range(2):
            device = {"wide": lax.rem(place.core + turn, 2), "narrow": chip}
            remote(source(chip), target, send_sem.at[turn, hop], recv_sem.at[turn, hop], device).start()
        return carry

    lax.fori_loop(1, number, send, 0)
    remote(source(place.me), target, send_sem.at[1, 0], recv_sem.at[1, 0], place.other).start()


def sum_of_everyone(place, own, landing, send_sem, recv_sem):
    number = landing.shape[1]
    landing[place.core, place.me] = own

    def wait(turn, hop):
        came = landing.at[lax.rem(place.core + turn, 2), lax.rem(place.me + number - hop, number)]
        copy = remote(came, came, send_sem.at[turn, hop], recv_sem.at[turn, hop], place.other)
        copy.wait_recv()
        copy.wait_send()

    def wait_both(hop, carry):
        wait(0, hop)
        wait(1, hop)
        return carry

    lax.fori_loop(1, number, wait_both, 0)
    wait(1, 0)

    def add(spot, total):
        return total + landing[0, spot] + landing[1, spot]

    return lax.fori_loop(1, number, add, landing[0, 0] + landing[1, 0])


def grid_of(mesh):
    number = mesh.shape["narrow"]
    places = [getattr(device, "coords", None) for device in mesh.devices[0]]
    if all(place is not None for place in places):
        sizes = [len({place[axis] for place in places}) for axis in (2, 1, 0)]
        if sizes[0] * sizes[1] * sizes[2] == number:
            return tuple(sizes)
    side = round((number / 2) ** (1 / 3))
    return (2 * side, side, side) if 2 * side**3 == number else (number, 1, 1)


def plan_of(select_rows, state_size, tap_count, step_rows):
    plan, first = {}, 0
    for name, tall in (
        ("select", select_rows),
        ("decay", state_size),
        ("taps", tap_count),
        ("shift", 1),
        ("bias", 1),
        ("skip", 1),
        ("gain", 1),
    ):
        plan[name] = (first, tall)
        first += tall
    plan["step"] = (lanes, step_rows)
    plan["rows"] = -(-(lanes + step_rows) // 32) * 32
    return plan


def per_device(
    dims,
    tokens,
    cotangent,
    loss_mask,
    seq_lengths,
    norm_gain,
    in_proj,
    conv_weight,
    conv_bias,
    select_proj,
    step_proj,
    step_bias,
    decay_log,
    skip_scale,
    out_proj,
):
    half = jnp.bfloat16
    piece = skip_scale.shape[0]
    gain_piece = norm_gain.shape[0]
    rank, size = step_proj.shape[0], decay_log.shape[0]
    plan = plan_of(select_proj.shape[0], size, conv_weight.shape[0], rank)
    smalls = {
        "select": select_proj,
        "decay": decay_log,
        "taps": conv_weight,
        "shift": conv_bias[None],
        "bias": step_bias[None],
        "skip": skip_scale[None],
        "gain": norm_gain[None],
        "step": step_proj,
    }
    depth, planes = dims[0], dims[1] * dims[2]
    number = depth * planes
    in_rows = in_proj.shape[0]
    rows, model = tokens.shape
    inner = piece * number
    width = 4 * lanes
    blocks = inner // width
    chunks = rows // chunk
    mask_row = loss_mask[None]

    whole = pl.BlockSpec(memory_space=pltpu.VMEM)
    tall = pl.BlockSpec((rows, width), lambda b: (0, b))
    deep = pl.BlockSpec((chunks, chunk, width), lambda b: (0, 0, b))
    lead = pl.BlockSpec((rows, size, width), lambda b: (0, 0, b))
    first_w = pl.BlockSpec((model, width), lambda b: (0, b))
    second_w = pl.BlockSpec((model, width), lambda b: (0, b + blocks))
    out_w = pl.BlockSpec((width, model), lambda b: (b, 0))

    def thin(height):
        return pl.BlockSpec((height, width), lambda b: (0, b))

    def fixed(*dims_of):
        return pl.BlockSpec(dims_of, lambda b: (0,) * len(dims_of))

    scalars = pl.BlockSpec(memory_space=pltpu.SMEM)
    offset_buf = pltpu.VMEM((rows + 8, lanes), jnp.int32)
    packed = thin(plan["rows"])

    pair = (chunks, 2 * chunk, lanes)
    pair = (chunks, 2 * chunk, lanes)
    anywhere = pl.BlockSpec(memory_space=pl.ANY)
    small_half = (2, plan["rows"] // 2, piece)
    in_piece = (in_rows, width)
    shares = 2
    in_share = (in_rows, inner // shares)
    out_share = (out_proj.shape[0], model // shares)
    lines = [shape((shares, depth) + half_shape(block), half) for block in (in_share, out_share)]
    (
        branch,
        signal,
        slope,
        projected,
        flipped,
        normed,
        grad_low,
        write_pair,
        read_pair,
        small,
        gain_value,
        in_blocks,
        gate_lines,
        out_lines,
    ) = compute_call(
        functools.partial(front_kernel, plan, dims, tuple(smalls)),
        "front",
        blocks,
        [scalars, whole, whole, whole] + [whole] * len(smalls) + [whole] * 2,
        [tall, tall, tall] + [whole] * 8 + [anywhere] * 3,
        [
            shape((rows, inner)),
            shape((rows, inner), half),
            shape((rows, inner)),
            shape((rows, lanes)),
            shape((model, rows), half),
            shape((rows, model), half),
            shape((rows, model), half),
            shape(pair, half),
            shape(pair, half),
            shape((plan["rows"], inner), half),
            shape((1, model)),
            shape((blocks, depth, planes) + in_piece, half),
            *lines,
        ],
        [
            offset_buf,
            pltpu.VMEM((plan["rows"], piece), jnp.float32),
            pltpu.VMEM(small_half, half),
            pltpu.VMEM((blocks,) + in_piece, half),
            pltpu.VMEM((shares,) + in_share, half),
            pltpu.VMEM((shares,) + out_share, half),
            pltpu.VMEM((depth, planes) + small_half, half),
            pltpu.VMEM((blocks, depth, planes) + in_piece, half),
            pltpu.SemaphoreType.DMA((blocks,)),
            pltpu.VMEM((8, piece), jnp.float32),
            pltpu.VMEM((number, 8, piece), jnp.float32),
            pltpu.SemaphoreType.DMA((number,)),
            pltpu.SemaphoreType.DMA((number,)),
        ]
        + Gather.sems(1 + blocks, dims)
        + Rise.sems(2 * shares, dims),
        4 * rows * model * inner,
        (seq_lengths, tokens, cotangent, mask_row, *smalls.values(), in_proj, out_proj),
        collective_id=0,
    )
    groups = 2
    part, pieces = rows // groups, chunks // groups
    row_block = pltpu.VMEM((pieces, chunk, width), jnp.float32)
    spread_block = pltpu.VMEM((rows, size, lanes), jnp.float32)
    fold_block = pltpu.VMEM((width // lanes, chunk * chunk, lanes), jnp.float32)

    def by_group(order, *dims_of):
        middle = (0,) * (len(dims_of) - 2)
        return pl.BlockSpec(dims_of, lambda b, g: (order(g),) + middle + (b,))

    def by_token(order, *dims_of):
        return pl.BlockSpec(dims_of, lambda b, g: (order(g),) + (0,) * (len(dims_of) - 1))

    def by_channel(height):
        return pl.BlockSpec((height, width), lambda b, g: (0, b))

    def onward(g):
        return g

    def backward(g):
        return groups - 1 - g

    states, step, core, begins, gate_blocks, out_blocks = compute_call(
        functools.partial(forward_kernel, plan, dims),
        "forward",
        (blocks, groups),
        [
            scalars,
            by_token(onward, part, lanes),
            by_channel(plan["rows"]),
            by_group(onward, part, width),
            whole,
            whole,
            anywhere,
            anywhere,
        ],
        [
            by_group(onward, part, size, width),
            by_group(onward, pieces, chunk, width),
            by_group(onward, pieces, chunk, width),
            by_group(onward, 1, size, width),
            anywhere,
            anywhere,
        ],
        [
            shape((rows, size, inner)),
            shape((chunks, chunk, inner)),
            shape((chunks, chunk, inner)),
            shape((groups, size, inner)),
            shape((shares, depth, planes) + in_share, half),
            shape((shares, depth, planes) + out_share, half),
        ],
        [
            offset_buf,
            pltpu.VMEM((part, width), jnp.float32),
            row_block,
            row_block,
            spread_block,
            spread_block,
            fold_block,
            fold_block,
            pltpu.VMEM((size, width), jnp.float32),
        ]
        + Gather.sems(2 * shares, dims),
        15 * rows * inner * size,
        (seq_lengths, projected, small, signal, write_pair, read_pair, gate_lines, out_lines),
        collective_id=2,
    )
    split = in_share[1] // width
    weights = pl.BlockSpec((None, number, in_rows, width), lambda b: (b // split, 0, 0, b % split))
    per_block = width // out_share[0]
    out_pieces = pl.BlockSpec((shares, per_block) + out_share, lambda b: (0, b, 0, 0))
    branch_whole = in_blocks.reshape(blocks, number, *in_piece)
    gate_whole = gate_blocks.reshape(shares, number, *in_share)
    out_whole = out_blocks.reshape(shares, number, *out_share)
    core_grad, gate_grad, grad_skip, grad_outw, grad_in_gate, output = compute_call(
        functools.partial(middle_kernel, plan),
        "middle",
        blocks,
        [deep, packed, tall, weights, whole, out_pieces, whole, whole, whole],
        [
            deep,
            tall,
            thin(1),
            pl.BlockSpec((shares, width, out_share[1]), lambda b: (0, b, 0)),
            pl.BlockSpec((None, model, width), lambda b: (b // split, 0, b % split)),
            fixed(rows, model),
        ],
        [
            shape((chunks, chunk, inner)),
            shape((rows, inner), half),
            shape((1, inner)),
            shape((shares, inner, out_share[1]), half),
            shape((shares, model, in_share[1]), half),
            shape((rows, model), half),
        ],
        [
            pltpu.VMEM((rows, width), jnp.float32),
            pltpu.VMEM((rows, width), jnp.float32),
            pltpu.VMEM((rows, width), half),
            pltpu.VMEM((width, model), half),
            pltpu.VMEM((rows, model), jnp.float32),
        ],
        8 * rows * model * inner,
        (core, small, signal, gate_whole, grad_low, out_whole, flipped, normed, tokens),
    )
    early_grads = [
        grad_outw.reshape((shares, depth, planes) + out_share),
        grad_in_gate.reshape((shares, depth, planes) + in_share),
    ]
    early_sums = [shape(out_proj.shape), shape((in_rows, inner))]
    early_pieces = [shape((depth, planes) + block, half) for block in (in_share, out_share)] * shares
    (
        signal_grad,
        grad_stepw,
        grad_bias,
        grad_decaylog,
        flat,
        out_sum,
        in_gate_sum,
        early_squares,
    ) = compute_call(
        functools.partial(backward_kernel, plan, dims),
        "backward",
        (blocks, groups),
        [
            scalars,
            by_token(backward, part, lanes),
            by_channel(plan["rows"]),
            by_group(backward, part, width),
            whole,
            whole,
            by_group(backward, pieces, chunk, width),
            by_group(backward, pieces, chunk, width),
            by_group(backward, part, size, width),
            by_group(backward, 1, size, width),
            anywhere,
            anywhere,
        ],
        [
            by_group(backward, part, width),
            by_channel(rank),
            by_channel(1),
            by_channel(size),
            whole,
        ]
        + [whole] * 3,
        [
            shape((rows, inner)),
            shape((rank, inner)),
            shape((1, inner)),
            shape((size, inner)),
            shape((rows, lanes), half),
            *early_sums,
            shape((8, lanes)),
        ],
        [
            offset_buf,
            row_block,
            row_block,
            spread_block,
            spread_block,
            fold_block,
            fold_block,
            fold_block,
            fold_block,
            row_block,
            row_block,
            pltpu.VMEM((part, width), half),
            pltpu.VMEM((size, width), jnp.float32),
            pltpu.VMEM((chunks, chunk, lanes), jnp.float32),
            spread_block,
            spread_block,
        ]
        + [pltpu.VMEM((shares,) + block, jnp.float32) for block in (in_share, out_share)]
        + Reduce.rooms(dims, early_pieces, False)
        + Reduce.sems(2 * shares, dims),
        40 * rows * inner * size,
        (
            seq_lengths,
            projected,
            small,
            signal,
            write_pair,
            read_pair,
            step,
            core_grad,
            states,
            begins,
            *early_grads,
        ),
        collective_id=3,
    )

    plain_rows = np.zeros((plan["rows"], piece), np.float32)
    for name in ("bias", "decay", "skip"):
        first, count = plan[name]
        plain_rows[first : first + count] = 1.0
    late_grads = [shape((depth, planes) + small_half, half)]
    late_grads += [shape((depth, planes, in_rows, width), half)] * blocks
    taps_n = conv_weight.shape[0]
    late = {"taps": (0, taps_n), "shift": (taps_n, 1), "gain": (taps_n + 1, 1)}
    late_block = (8, piece)

    early_tall = pl.BlockSpec((rows, width), lambda b: (0, jnp.minimum(b, blocks - 1)))
    late_tall = pl.BlockSpec((rows, width), lambda b: (0, jnp.maximum(b - blocks, 0)))
    tokens_grad, in_branch_sum, small_sum, late_sum, norms = compute_call(
        functools.partial(back_kernel, plan, dims),
        "back",
        2 * blocks,
        [scalars, whole, whole, whole]
        + [pl.BlockSpec((plan["rows"], width), lambda b: (0, jnp.minimum(b, blocks - 1))), whole]
        + [early_tall, whole, early_tall, early_tall, late_tall, whole]
        + [
            pl.BlockSpec((None, number, in_rows, width), lambda b: (jnp.maximum(b - blocks, 0), 0, 0, 0)),
            pl.BlockSpec(
                (None, number, in_rows, width),
                lambda b: (jnp.maximum(b - blocks, 0) // split, 0, 0, jnp.maximum(b - blocks, 0) % split),
            ),
        ]
        + [whole] * 6,
        [whole] * 5,
        [
            shape((rows, model), half),
            shape((in_rows, inner)),
            shape(small_half),
            shape(late_block),
            shape((2, 8, lanes)),
        ],
        [
            offset_buf,
            pltpu.VMEM((rows + 8, width), jnp.float32),
            pltpu.VMEM((blocks, rows, width), half),
            pltpu.VMEM((rows, model), jnp.float32),
            pltpu.VMEM((blocks,) + late_grads[1].shape, half),
            pltpu.VMEM(late_grads[0].shape, late_grads[0].dtype),
            pltpu.VMEM((number,) + late_block, jnp.float32),
            pltpu.VMEM((2, number) + late_block, jnp.float32),
            pltpu.VMEM((2, 8, lanes), jnp.float32),
            pltpu.VMEM((2, number, 2, 8, lanes), jnp.float32),
            pltpu.VMEM((blocks, in_rows, width), jnp.float32),
            pltpu.VMEM(small_half, jnp.float32),
            pltpu.SemaphoreType.DMA((2, 2, number)),
            pltpu.SemaphoreType.DMA((2, 2, number)),
        ]
        + Reduce.rooms(dims, late_grads, True)
        + Reduce.sems(blocks + 1, dims),
        8 * rows * model * inner,
        (
            seq_lengths,
            tokens,
            grad_low,
            gain_value,
            small,
            flat,
            branch,
            signal,
            slope,
            signal_grad,
            gate_grad,
            flipped,
            branch_whole,
            gate_whole,
            grad_stepw,
            grad_bias,
            grad_decaylog,
            grad_skip,
            jnp.asarray(plain_rows.reshape(small_half)),
            early_squares,
        ),
        collective_id=1,
    )

    names = ("gain", "taps", "shift", "select", "step", "bias", "decay", "skip")
    own = (norm_gain, conv_weight, conv_bias, select_proj, step_proj, step_bias, decay_log, skip_scale)
    in_grad, out_grad, grad_tokens, gain_grad, *small_grads, decay_sq, plain_sq = pl.pallas_call(
        functools.partial(finish_kernel, plan, names, late),
        in_specs=[whole] * 7,
        out_specs=[whole] * (3 + len(names)) + [scalars] * 2,
        out_shape=[shape(in_proj.shape), shape(out_proj.shape), shape(tokens.shape, half)]
        + [shape(array.shape) for array in own]
        + [shape((1, 1))] * 2,
        name="finish",
    )(
        tokens_grad,
        in_branch_sum,
        in_gate_sum,
        out_sum,
        small_sum.reshape(plan["rows"], piece),
        late_sum,
        norms,
    )
    return (
        output,
        grad_tokens,
        gain_grad,
        in_grad,
        *small_grads,
        out_grad,
        decay_sq[0, 0],
        plain_sq[0, 0],
    )


def solution(mesh):
    placed = (
        P(("wide", "narrow"), None),
        P(("wide", "narrow"), None),
        P(("wide", "narrow")),
        P(("wide", "narrow"), None),
        P("narrow"),
        P("narrow", None),
        P(None, "narrow"),
        P("narrow"),
        P(None, "narrow"),
        P(None, "narrow"),
        P("narrow"),
        P(None, "narrow"),
        P("narrow"),
        P("narrow", None),
    )
    return jax.shard_map(
        functools.partial(per_device, grid_of(mesh)),
        mesh=mesh,
        in_specs=placed,
        out_specs=(
            P(("wide", "narrow"), None),
            P(("wide", "narrow"), None),
            P("narrow"),
            P("narrow", None),
            P(None, "narrow"),
            P("narrow"),
            P(None, "narrow"),
            P(None, "narrow"),
            P("narrow"),
            P(None, "narrow"),
            P("narrow"),
            P("narrow", None),
            P(),
            P(),
        ),
        check_vma=False,
    )
```
